32 devices in a mesh: rep: 4 (over y, x), shard: 8 (over z, core).
Axes of the slice: x: 2, y: 2, z: 4, core: 2. Of those that a mesh axis runs over, the one named last changes fastest.
Arguments:
- tokens: bfloat16 [224, 144, 768], P(('rep', 'shard')), may hold values from -6 to 6
- out_grad: bfloat16 [224, 144, 768], P(('rep', 'shard')), may hold values from -6 to 6
- window_count: int32 [32], P(('rep', 'shard')), may hold values from 1 to 7, as said below
- qkv_weight: float32 [768, 2304], P('shard'), may hold values from -0.21875 to 0.21875
- qkv_first: float32 [768, 2304], P('shard')
- qkv_second: float32 [768, 2304], P('shard'), as said below
- output_weight: float32 [768, 768], P('shard'), may hold values from -0.875 to 0.875
- output_first: float32 [768, 768], P('shard'), may hold values from -320 to 320
- output_second: float32 [768, 768], P('shard'), may hold values from 1935.36 to 7741.44
- up_weight: float32 [768, 3072], P('shard'), may hold values from -0.21875 to 0.21875
- up_first: float32 [768, 3072], P('shard'), may hold values from -256 to 256
- up_second: float32 [768, 3072], P('shard'), may hold values from 1064.448 to 4193.28
- down_weight: float32 [3072, 768], P('shard'), may hold values from -0.109375 to 0.109375
- down_first: float32 [3072, 768], P('shard'), may hold values from -448 to 448
- down_second: float32 [3072, 768], P('shard'), may hold values from 3548.16 to 13870.08
- vectors: float32 [12, 768], P(None, 'shard')
- vector_first: float32 [12, 768], P(None, 'shard')
- vector_second: float32 [12, 768], P(None, 'shard'), as said below
- bias_table: float32 [536, 24], P('shard'), may hold values from -4 to 4
- table_first: float32 [536, 24], P('shard'), may hold values from -320 to 320
- table_second: float32 [536, 24], P('shard'), may hold values from 1935.36 to 7741.44
Outputs:
- layer_out: bfloat16 [224, 144, 768], P(('rep', 'shard'))
- input_grad: float32 [224, 144, 768], P(('rep', 'shard'))
- qkv_new: float32 [768, 2304], P('shard')
- qkv_moment: float32 [768, 2304], P('shard')
- qkv_square: float32 [768, 2304], P('shard')
- qkv_copy: bfloat16 [768, 2304], P('shard')
- output_new: float32 [768, 768], P('shard')
- output_moment: float32 [768, 768], P('shard')
- output_square: float32 [768, 768], P('shard')
- output_copy: bfloat16 [768, 768], P('shard')
- up_new: float32 [768, 3072], P('shard')
- up_moment: float32 [768, 3072], P('shard')
- up_square: float32 [768, 3072], P('shard')
- up_copy: bfloat16 [768, 3072], P('shard')
- down_new: float32 [3072, 768], P('shard')
- down_moment: float32 [3072, 768], P('shard')
- down_square: float32 [3072, 768], P('shard')
- down_copy: bfloat16 [3072, 768], P('shard')
- vector_new: float32 [12, 768], P(None, 'shard')
- vector_moment: float32 [12, 768], P(None, 'shard')
- vector_square: float32 [12, 768], P(None, 'shard')
- table_new: float32 [536, 24], P('shard')
- table_moment: float32 [536, 24], P('shard')
- table_square: float32 [536, 24], P('shard')
The draws below stay inside these ranges and needn't reach their ends.
Inputs may be any that keep to these rules, and one draw needn't show every extreme that they name: `window_count`: some device holds 7 windows and some other holds 1 in every draw; a device's live windows are its first slots. `qkv_second`: Positive. `vector_second`: Positive.
All inputs are finite; a program needn't handle non-finite values.
Results may differ from the reference program's by a relative error of at most 0.012.
The reference program's roundings to bfloat16 on the way count: a program that leaves them out, or rounds other values in their place, can miss the bound.
Values may be sent and summed in bfloat16 or wider, within the bound.
A program may use at most 256 MiB of HBM per device.

```python
import math
import jax
import jax.numpy as jnp
import numpy as np
from jax import lax

C = 768
HEADS = 24
MLP = 3072
WIN = 12
WIN_DEV = 7
STEP = 5
HEAD_DIM = 32
TOK_WIN = 144
WINDOWS = 224
TOKENS = 32256
TAB_ROWS = 536


def draw_window_count(key, part):
    key = jax.random.fold_in(key, 7)
    key_counts, key_places = jax.random.split(key)
    device_total = WINDOWS // WIN_DEV
    counts = jax.random.randint(key_counts, (device_total,), 1, WIN_DEV + 1)
    places = jax.random.permutation(key_places, device_total)
    counts = counts.at[places[0]].set(WIN_DEV)
    counts = counts.at[places[1]].set(1)
    return counts.astype(jnp.int32)


def draw_vectors(key, part):
    key = jax.random.fold_in(key, 11)
    key_bias, key_gain = jax.random.split(key)
    row_total = 8 + MLP // C
    biases = 0.3 * jax.random.normal(key_bias, (row_total, C), jnp.float32)
    gain_rows = jax.random.uniform(key_gain, (row_total, C), jnp.float32, 0.5, 1.5)
    row_number = jnp.arange(row_total)[:, None]
    is_gain = (row_number == 0) | (row_number == 5)
    return jnp.where(is_gain, gain_rows, biases).astype(jnp.float32)


def qkv_scale():
    column = jnp.arange(3 * C)[None, :]
    return jnp.where(column < 2 * C, 0.35, 3.3) * jnp.sqrt(jnp.float32(TOKENS))


def vector_scale():
    head_rows = jnp.array([3.3, 3.3, 0.35, 3.3, 0.8, 0.5, 0.5, 0.75], jnp.float32)
    tail_rows = jnp.full((MLP // C,), 0.26, jnp.float32)
    return jnp.concatenate([head_rows, tail_rows])[:, None] * jnp.sqrt(jnp.float32(TOKENS))


def second_from(key, scale, shape):
    spread = jax.random.uniform(key, shape, jnp.float32, 0.0, jnp.log(4.0))
    return (0.67 * scale * scale * jnp.exp(spread)).astype(jnp.float32)


def draw_qkv_first(key, part):
    key = jax.random.fold_in(key, 13)
    values = jax.random.truncated_normal(key, -6.0, 6.0, (C, 3 * C), jnp.float32)
    return (values * qkv_scale()).astype(jnp.float32)


def draw_qkv_second(key, part):
    key = jax.random.fold_in(key, 17)
    return second_from(key, qkv_scale(), (C, 3 * C))


def draw_vector_first(key, part):
    key = jax.random.fold_in(key, 19)
    values = jax.random.truncated_normal(key, -6.0, 6.0, (8 + MLP // C, C), jnp.float32)
    return (values * vector_scale()).astype(jnp.float32)


def draw_vector_second(key, part):
    key = jax.random.fold_in(key, 23)
    return second_from(key, vector_scale(), (8 + MLP // C, C))


def level_of(own_key, dims, shards, smallest, top_value):
    def one(axis_at, parts):
        heights = jax.random.uniform(jax.random.fold_in(jax.random.fold_in(own_key, 6), axis_at), (parts,), jnp.float32, smallest / len(shards), top_value / len(shards))
        return jnp.repeat(jnp.exp(heights), dims[axis_at] // parts).reshape((-1,) + (1,) * (len(dims) - axis_at - 1))

    factor_of = one(*shards[0])
    for cut in shards[1:]:
        factor_of = factor_of * one(*cut)
    return factor_of


def gaussian(rng, dims, width, bound, cuts=(), kind=jnp.bfloat16):
    values = width * jax.random.normal(rng, dims, jnp.float32)
    if cuts:
        values = values * level_of(rng, dims, cuts, -0.22, 0.18)
    return jnp.clip(values, -bound, bound).astype(kind)


def setup_inputs(seed: int = 0) -> dict:
    keys = jax.random.split(jax.random.key(seed), 22)
    return {
        "tokens": gaussian(keys[0], (WINDOWS, TOK_WIN, C), 1.0, 6.0, ((0, 32),)),
        "out_grad": gaussian(keys[1], (WINDOWS, TOK_WIN, C), 1.0, 6.0, ((0, 32),)),
        "window_count": draw_window_count(jax.random.fold_in(keys[21], 71), 0),
        "qkv_weight": gaussian(keys[3], (C, 3 * C), C ** -0.5, 0.21875, ((0, 8),), jnp.float32),
        "qkv_first": draw_qkv_first(jax.random.fold_in(keys[21], 71), 0),
        "qkv_second": draw_qkv_second(jax.random.fold_in(keys[21], 71), 0),
        "output_weight": gaussian(keys[6], (C, C), (C // 16) ** -0.5, 0.875, ((0, 8),), jnp.float32),
        "output_first": gaussian(keys[7], (C, C), (0.3 * TOKENS ** 0.5), 320.0, ((0, 8),), jnp.float32),
        "output_second": jnp.clip(jnp.exp(math.log(7741.44) - 1.3862944 * jax.random.uniform(keys[8], (C, C), jnp.float32) ** level_of(keys[8], (C, C), ((0, 8),), -0.2, 0.2)), 1935.36, 7741.44),
        "up_weight": gaussian(keys[9], (C, MLP), C ** -0.5, 0.21875, ((0, 8),), jnp.float32),
        "up_first": gaussian(keys[10], (C, MLP), (0.22 * TOKENS ** 0.5), 256.0, ((0, 8),), jnp.float32),
        "up_second": jnp.clip(jnp.exp(math.log(4193.28) - 1.37102684 * jax.random.uniform(keys[11], (C, MLP), jnp.float32) ** level_of(keys[11], (C, MLP), ((0, 8),), -0.2, 0.2)), 1064.448, 4193.28),
        "down_weight": gaussian(keys[12], (MLP, C), MLP ** -0.5, 0.109375, ((0, 8),), jnp.float32),
        "down_first": gaussian(keys[13], (MLP, C), (0.4 * TOKENS ** 0.5), 448.0, ((0, 8),), jnp.float32),
        "down_second": jnp.clip(jnp.exp(math.log(13870.08) - 1.3633049 * jax.random.uniform(keys[14], (MLP, C), jnp.float32) ** level_of(keys[14], (MLP, C), ((0, 8),), -0.2, 0.2)), 3548.16, 13870.08),
        "vectors": draw_vectors(jax.random.fold_in(keys[21], 71), 0),
        "vector_first": draw_vector_first(jax.random.fold_in(keys[21], 71), 0),
        "vector_second": draw_vector_second(jax.random.fold_in(keys[21], 71), 0),
        "bias_table": gaussian(keys[18], (TAB_ROWS, HEADS), 1.0, 4.0, ((0, 8),), jnp.float32),
        "table_first": gaussian(keys[19], (TAB_ROWS, HEADS), (0.3 * TOKENS ** 0.5), 320.0, ((0, 8),), jnp.float32),
        "table_second": jnp.clip(jnp.exp(math.log(7741.44) - 1.3862944 * jax.random.uniform(keys[20], (TAB_ROWS, HEADS), jnp.float32) ** level_of(keys[20], (TAB_ROWS, HEADS), ((0, 8),), -0.2, 0.2)), 1935.36, 7741.44),
    }


beta_one = 0.5
beta_two = 0.6
weight_decay = 0.05
adam_eps = 1e-08
norm_eps = 1e-05
step_rates = (0.04, 0.15, 0.04, 0.02, 0.2, 1.0)

@jax.custom_vjp
def low(v):
    return lax.optimization_barrier(v.astype(jnp.bfloat16)).astype(jnp.float32)

@jax.custom_vjp
def low_back(v):
    return v

def low_keep(v):
    return (low(v), None)

def low_pass(kept, grad):
    return (grad,)

def back_keep(v):
    return (v, None)

def back_low(kept, grad):
    return (low(grad),)
low.defvjp(low_keep, low_pass)
low_back.defvjp(back_keep, back_low)

def relative_index(window_side):
    coords = np.arange(window_side * window_side)
    row_of = coords // window_side
    col_of = coords % window_side
    delta_row = row_of[:, None] - row_of[None, :] + window_side - 1
    delta_col = col_of[:, None] - col_of[None, :] + window_side - 1
    return (delta_row * (2 * window_side - 1) + delta_col).reshape(-1).astype(np.int32)

def layer_norm(values, norm_gain, norm_shift):
    center = values - lax.optimization_barrier(jnp.mean(values, -1, keepdims=True))
    spread = lax.optimization_barrier(jnp.mean(center * center, -1, keepdims=True))
    return center * lax.rsqrt(spread + norm_eps) * norm_gain + norm_shift

def soft_max(scores):
    shifted = scores - lax.optimization_barrier(jnp.max(scores, -1, keepdims=True))
    expon = jnp.exp(shifted)
    return expon / lax.optimization_barrier(jnp.sum(expon, -1, keepdims=True))

def forward(params, inputs, live_mask):
    highest = lax.Precision.HIGHEST
    w_qkv, w_output, w_up, w_down, vec_full, table_full = [low(member) for member in params]
    windows = inputs.shape[0]
    tok_win = inputs.shape[1]
    head_shape = (windows, tok_win, HEADS, HEAD_DIM)
    score_scale = HEAD_DIM ** (-0.5)
    normed = low(layer_norm(inputs, vec_full[0], vec_full[1]))
    qkv_bias = jnp.concatenate([vec_full[2], jnp.zeros_like(vec_full[2]), vec_full[3]])
    project = low_back(jnp.einsum('wtc,cf->wtf', normed, w_qkv, precision=highest) + qkv_bias)
    query_heads = low(project[..., :C] * score_scale).reshape(head_shape)
    key_heads = low(project[..., C:2 * C]).reshape(head_shape)
    value_heads = low(project[..., 2 * C:]).reshape(head_shape)
    position = table_full[relative_index(WIN)].T.reshape(HEADS, tok_win, tok_win)
    scores = jnp.einsum('wihd,wjhd->whij', query_heads, key_heads, precision=highest) + position[None]
    scores = low_back(scores)
    probs = low(soft_max(scores))
    attended = jnp.einsum('whij,wjhd->wihd', probs, value_heads, precision=highest).reshape(windows, tok_win, C)
    attended = low_back(low(attended))
    branch = low_back(jnp.einsum('wtc,cd->wtd', attended, w_output, precision=highest) + vec_full[4])
    middle = inputs + branch
    normed_two = low(layer_norm(middle, vec_full[5], vec_full[6]))
    hidden = low_back(jnp.einsum('wtc,cf->wtf', normed_two, w_up, precision=highest) + vec_full[8:].reshape(-1))
    active = low(jax.nn.gelu(hidden, approximate=True))
    result = middle + jnp.einsum('wtf,fc->wtc', active, w_down, precision=highest) + vec_full[7]
    return live_mask[:, None, None] * result

def adamw(weight, moment, second, gradient, step_rate):
    moment_new = beta_one * moment + (1.0 - beta_one) * gradient
    second_new = beta_two * second + (1.0 - beta_two) * gradient * gradient
    update = moment_new / (1.0 - beta_one ** STEP) / (jnp.sqrt(second_new / (1.0 - beta_two ** STEP)) + adam_eps)
    weight_new = weight * (1.0 - step_rate * weight_decay) - step_rate * update
    return (weight_new, moment_new, second_new)

def reference(tokens, out_grad, window_count, qkv_weight, qkv_first, qkv_second, output_weight, output_first, output_second, up_weight, up_first, up_second, down_weight, down_first, down_second, vectors, vector_first, vector_second, bias_table, table_first, table_second):
    params = (qkv_weight, output_weight, up_weight, down_weight, vectors, bias_table)
    block_total = WINDOWS // WIN_DEV
    block_tokens = tokens.reshape(block_total, WIN_DEV, TOK_WIN, C)
    block_grads = out_grad.reshape(block_total, WIN_DEV, TOK_WIN, C)

    def accumulate(totals, pieces):
        stretch_tokens, stretch_grads, block_count = pieces
        live_mask = (jnp.arange(WIN_DEV) < block_count).astype(jnp.float32)

        def apply_layer(weights_in, inputs):
            return forward(weights_in, inputs, live_mask)
        result, pullback = jax.vjp(apply_layer, params, stretch_tokens.astype(jnp.float32))
        gradients, in_grad = pullback(stretch_grads.astype(jnp.float32))
        totals = jax.tree.map(jnp.add, totals, gradients)
        return (totals, (result.astype(jnp.bfloat16), in_grad))
    start_totals = jax.tree.map(jnp.zeros_like, params)
    totals, outputs = lax.scan(accumulate, start_totals, (block_tokens, block_grads, window_count))
    layer_out = outputs[0].reshape(WINDOWS, TOK_WIN, C)
    input_grad = outputs[1].reshape(WINDOWS, TOK_WIN, C)
    qkv_state = adamw(qkv_weight, qkv_first, qkv_second, totals[0], step_rates[0])
    output_state = adamw(output_weight, output_first, output_second, totals[1], step_rates[1])
    up_state = adamw(up_weight, up_first, up_second, totals[2], step_rates[2])
    down_state = adamw(down_weight, down_first, down_second, totals[3], step_rates[3])
    vector_state = adamw(vectors, vector_first, vector_second, totals[4], step_rates[4])
    table_state = adamw(bias_table, table_first, table_second, totals[5], step_rates[5])
    return (layer_out, input_grad, qkv_state[0], qkv_state[1], qkv_state[2], qkv_state[0].astype(jnp.bfloat16), output_state[0], output_state[1], output_state[2], output_state[0].astype(jnp.bfloat16), up_state[0], up_state[1], up_state[2], up_state[0].astype(jnp.bfloat16), down_state[0], down_state[1], down_state[2], down_state[0].astype(jnp.bfloat16), vector_state[0], vector_state[1], vector_state[2], table_state[0], table_state[1], table_state[2])
```

```python
import functools
import math

import jax
import jax.numpy as jnp
import numpy as np
from jax import lax
from jax.experimental import pallas as pl
from jax.experimental.pallas import tpu as pltpu
from jax.sharding import PartitionSpec as P

C = 768
HEADS = 24
MLP = 3072
WIN = 12
STEP = 5
HEAD_DIM = 32
SPAN = 2 * WIN - 1
TOK = WIN * WIN
ROWS = 1024
GROUPS = 3
GCOLS = 256
GHEADS = 8
PACK = GHEADS * TOK
TAB_LANES = 640
LINE = 384
MIB = 1 << 20

beta_one = 0.5
beta_two = 0.6
weight_decay = 0.05
adam_eps = 1e-08
norm_eps = 1e-05
step_rates = (0.04, 0.15, 0.04, 0.02, 0.2, 1.0)
low = jnp.bfloat16
full = jnp.float32
NT = (((1,), (1,)), ((), ()))


def dot(a, b):
    return jnp.dot(a, b, preferred_element_type=full)


def dot_nt(a, b):
    return lax.dot_general(a, b, NT, preferred_element_type=full)


def line_matrix():
    out = np.zeros((TAB_LANES, LINE), np.float32)
    col = np.arange(SPAN * WIN)
    out[(col // WIN) * SPAN + col % WIN + WIN - 1, col] = 1.0
    return out


def head_masks():
    lane = np.arange(GCOLS) // HEAD_DIM
    one = (lane[None, :] == np.arange(GHEADS)[:, None]).astype(np.float32)
    return np.broadcast_to(one[:, None, :], (GHEADS, 16, GCOLS))


def norm_parts(z):
    mean = jnp.sum(z, -1, keepdims=True) * (1.0 / C)
    center = z - mean
    spread = jnp.sum(center * center, -1, keepdims=True) * (1.0 / C)
    scale = lax.rsqrt(spread + norm_eps)
    return center * scale, scale


def norm_back(xhat, scale, dn, gain):
    g = dn * gain
    m1 = jnp.sum(g, -1, keepdims=True) * (1.0 / C)
    m2 = jnp.sum(g * xhat, -1, keepdims=True) * (1.0 / C)
    return scale * (g - m1 - xhat * m2)


def diag(x, mask_ref):
    head = x[0:128].reshape(8, 16, GCOLS)
    tail = x[128:144]
    parts = []
    for h in range(GHEADS):
        parts.append((head * mask_ref[h][None]).reshape(128, GCOLS))
    for h in range(GHEADS):
        parts.append(tail * mask_ref[h])
    return jnp.concatenate(parts, 0)


def undiag(xt, m, mask_ref):
    main = []
    for h in range(0, GHEADS, 2):
        r = dot(xt[h * HEAD_DIM : (h + 2) * HEAD_DIM], m[:, h * 128 : (h + 2) * 128])
        main.append(r[0:HEAD_DIM, 0:128])
        main.append(r[HEAD_DIM : 2 * HEAD_DIM, 128:256])
    main = jnp.concatenate(main, 0)
    rest = dot(xt, m[:, GHEADS * 128 :])
    rest_t = rest.T.reshape(GHEADS, 16, GCOLS)
    keep = mask_ref[...].astype(full)
    return jnp.concatenate([main.T, jnp.sum(rest_t * keep, 0)], 0)


def build_bias(tab, line_ref, tmp_ref, bias_ref):
    def column(cj, carry):
        shifted = pltpu.roll(tab, cj, 1)
        line = dot(shifted.astype(low), line_ref[...])
        for rj in range(WIN):
            cut = (WIN - 1 - rj) * WIN
            part = pltpu.roll(line, LINE - cut, 1) if cut else line
            row = pl.multiple_of((rj * WIN + cj) * HEADS, 8)
            tmp_ref[0, pl.ds(row, HEADS), :] = part[:, 0:128]
            tmp_ref[1, pl.ds(row, HEADS), :] = part[:, 128:256]
        return carry

    lax.fori_loop(0, WIN, column, 0)
    lane = lax.broadcasted_iota(jnp.int32, (TOK, 128), 1)
    for g in range(GROUPS):
        rest = jnp.zeros((TOK, 128), full)
        for h in range(GHEADS):
            at = pl.ds(g * GHEADS + h, TOK, stride=HEADS)
            bias_ref[g, :, h * 128 : (h + 1) * 128] = tmp_ref[0, at, :]
            piece = tmp_ref[1, at, :]
            piece = pltpu.roll(piece, 16 * h, 1) if h else piece
            rest = jnp.where((lane >= 16 * h) & (lane < 16 * h + 16), piece, rest)
        bias_ref[g, :, GHEADS * 128 :] = rest


def table_grad(line_ref, tmp_ref, bias_ref):
    lane = lax.broadcasted_iota(jnp.int32, (TOK, 128), 1)
    for g in range(GROUPS):
        rest = bias_ref[g, :, GHEADS * 128 :]
        for h in range(GHEADS):
            at = pl.ds(g * GHEADS + h, TOK, stride=HEADS)
            tmp_ref[0, at, :] = bias_ref[g, :, h * 128 : (h + 1) * 128]
            piece = pltpu.roll(rest, 128 - 16 * h, 1) if h else rest
            tmp_ref[1, at, :] = jnp.where(lane < 16, piece, 0.0)

    def column(cj, total):
        line = jnp.zeros((HEADS, LINE), full)
        for rj in range(WIN):
            cut = (WIN - 1 - rj) * WIN
            row = pl.multiple_of((rj * WIN + cj) * HEADS, 8)
            part = jnp.concatenate([tmp_ref[0, pl.ds(row, HEADS), :], tmp_ref[1, pl.ds(row, HEADS), :], jnp.zeros((HEADS, 128), full)], 1)
            line = line + (pltpu.roll(part, cut, 1) if cut else part)
        high = line.astype(low)
        rest = (line - high.astype(full)).astype(low)
        spread = dot_nt(high, line_ref[...]) + dot_nt(rest, line_ref[...])
        return total + pltpu.roll(spread, TAB_LANES - cj, 1)

    return lax.fori_loop(0, WIN, column, jnp.zeros((HEADS, TAB_LANES), full))


def transpose_rows(src_ref, dst_ref):
    def block(i, carry):
        at = pl.multiple_of(i * 128, 128)
        dst_ref[:, pl.ds(at, 128)] = src_ref[pl.ds(at, 128), :].T
        return carry

    lax.fori_loop(0, ROWS // 128, block, 0)


def window_rows(w):
    return pl.ds(pl.multiple_of(w * TOK, 16), TOK)


def zero_tail(ref, windows):
    at = windows * TOK
    ref[at:ROWS, :] = jnp.zeros((ROWS - at, ref.shape[1]), ref.dtype)


def attention_forward(windows, x_ref, vec_ref, tab_ref, line_ref, mask_ref, wq_ref, wp_ref,
                      qkv_ref, pt_ref, o_ref, x1_ref, n1t_ref, n1_ref, bias_ref, tmp_ref):
    build_bias(tab_ref[...], line_ref, tmp_ref, bias_ref)
    zero_tail(n1_ref, windows)
    zero_tail(o_ref, windows)

    def first_norm(w, carry):
        xhat, _ = norm_parts(x_ref[window_rows(w), :].astype(full))
        n1_ref[window_rows(w), :] = (xhat * vec_ref[0:1, :] + vec_ref[1:2, :]).astype(low)
        return carry

    lax.fori_loop(0, windows, first_norm, 0)
    transpose_rows(n1_ref, n1t_ref)

    def group(g, carry):
        cols = pl.ds(pl.multiple_of(g * GCOLS, GCOLS), GCOLS)
        n1 = n1_ref[...]
        qkv_ref[g] = ((dot(n1, wq_ref[g]) + vec_ref[2:3, cols]) * (HEAD_DIM**-0.5)).astype(low)
        qkv_ref[GROUPS + g] = dot(n1, wq_ref[GROUPS + g]).astype(low)
        qkv_ref[2 * GROUPS + g] = (dot(n1, wq_ref[2 * GROUPS + g]) + vec_ref[3:4, cols]).astype(low)

        def window(w, inner):
            rows = window_rows(w)
            q = qkv_ref[g, rows, :]
            k = qkv_ref[GROUPS + g, rows, :]
            v = qkv_ref[2 * GROUPS + g, rows, :]
            s = dot_nt(k, diag(q, mask_ref)) + bias_ref[g]
            e = jnp.exp(s - jnp.max(s, 0, keepdims=True))
            p = (e * (1.0 / jnp.sum(e, 0, keepdims=True))).astype(low)
            pt_ref[g, w] = p
            o_ref[rows, cols] = undiag(v.T, p, mask_ref).astype(low)
            return inner

        lax.fori_loop(0, windows, window, 0)
        return carry

    lax.fori_loop(0, GROUPS, group, 0)

    def output(w, carry):
        rows = window_rows(w)
        branch = dot(o_ref[rows, :], wp_ref[...]) + vec_ref[4:5, :]
        x1_ref[rows, :] = x_ref[rows, :].astype(full) + branch
        return carry

    lax.fori_loop(0, windows, output, 0)


def gelu_both(h):
    c = math.sqrt(2.0 / math.pi)
    square = h * h
    t = jnp.tanh(h * (c + (c * 0.044715) * square))
    half = 0.5 + 0.5 * t
    slope = half + (0.5 * h) * (1.0 - t * t) * (c + (3.0 * c * 0.044715) * square)
    return h * half, slope


def feed_forward(windows, tile, x1_ref, dy_ref, live_ref, vec_ref, bu_ref, up_ref, down_ref, wp_ref, o_ref,
                 out_ref, dx1_ref, do_ref, gup_ref, gdown_ref, gout_ref, sums_ref, bsum_ref,
                 n2_ref, n2t_ref, dy2_ref, dyt_ref, y_ref, dn_ref):
    zero_tail(n2_ref, windows)
    zero_tail(dy2_ref, windows)

    def second_norm(w, carry):
        rows = window_rows(w)
        xhat, _ = norm_parts(x1_ref[rows, :])
        n2_ref[rows, :] = (xhat * vec_ref[5:6, :] + vec_ref[6:7, :]).astype(low)
        dy2_ref[rows, :] = (dy_ref[rows, :].astype(full) * live_ref[w]).astype(low)
        return carry

    lax.fori_loop(0, windows, second_norm, 0)
    transpose_rows(n2_ref, n2t_ref)
    transpose_rows(dy2_ref, dyt_ref)
    y_ref[...] = jnp.zeros_like(y_ref)
    dn_ref[...] = jnp.zeros_like(dn_ref)

    def step(i, carry):
        up = up_ref[i]
        down = down_ref[i]
        h = dot(n2_ref[...], up) + bu_ref[i]
        da = dot_nt(dy2_ref[...], down)
        act, slope = gelu_both(h)
        a = act.astype(low)
        dh = (da * slope).astype(low)
        bsum_ref[i] = jnp.sum(dh.astype(full), 0, keepdims=True)
        y_ref[...] += dot(a, down)
        dn_ref[...] += dot_nt(dh, up)
        gdown_ref[i] = dot(dyt_ref[...], a).astype(gdown_ref.dtype)
        gup_ref[i] = dot(n2t_ref[...], dh).astype(gup_ref.dtype)
        return carry

    lax.fori_loop(0, MLP // tile, step, 0)
    sums_ref[...] = jnp.zeros_like(sums_ref)
    zero_tail(dx1_ref, windows)

    def finish(w, carry):
        rows = window_rows(w)
        x1 = x1_ref[rows, :]
        out_ref[rows, :] = ((x1 + y_ref[rows, :] + vec_ref[7:8, :]) * live_ref[w]).astype(low)
        xhat, scale = norm_parts(x1)
        dn = dn_ref[rows, :]
        dy = dy2_ref[rows, :].astype(full)
        dx1 = dy + norm_back(xhat, scale, dn, vec_ref[5:6, :])
        dx1_ref[rows, :] = dx1
        dr = dx1.astype(low)
        n2_ref[rows, :] = dr
        do_ref[rows, :] = dot_nt(dr, wp_ref[...]).astype(low)
        sums_ref[4:5, :] += jnp.sum(dr.astype(full), 0, keepdims=True)
        sums_ref[5:6, :] += jnp.sum(dn * xhat, 0, keepdims=True)
        sums_ref[6:7, :] += jnp.sum(dn, 0, keepdims=True)
        sums_ref[7:8, :] += jnp.sum(dy, 0, keepdims=True)
        return carry

    lax.fori_loop(0, windows, finish, 0)
    transpose_rows(o_ref, dyt_ref)
    for g in range(GROUPS):
        at = pl.ds(g * GCOLS, GCOLS)
        gout_ref[:, at] = dot(dyt_ref[...], n2_ref[:, at]).astype(gout_ref.dtype)


def attention_backward(windows, x_ref, vec_ref, line_ref, mask_ref, wq_ref, qkv_ref, pt_ref, do_ref, dx1_ref, n1t_ref, sums_in_ref,
                       gq_ref, gtab_ref, sums_ref, grad_ref, bias_ref, tmp_ref, dproj_ref, dn_ref):
    bias_ref[...] = jnp.zeros_like(bias_ref)
    dn_ref[...] = jnp.zeros_like(dn_ref)
    sums_ref[...] = sums_in_ref[...]
    for part in range(3):
        dproj_ref[part, windows * TOK :, :] = jnp.zeros((ROWS - windows * TOK, GCOLS), low)

    def group(g, carry):
        cols = pl.ds(pl.multiple_of(g * GCOLS, GCOLS), GCOLS)

        def window(w, inner):
            rows = window_rows(w)
            q = qkv_ref[g, rows, :]
            k = qkv_ref[GROUPS + g, rows, :]
            v = qkv_ref[2 * GROUPS + g, rows, :]
            p = pt_ref[g, w]
            do = diag(do_ref[rows, cols], mask_ref)
            dp = dot_nt(v, do)
            dv = dot(p, do)
            pf = p.astype(full)
            ds = (pf * (dp - jnp.sum(pf * dp, 0, keepdims=True))).astype(low)
            bias_ref[g] += ds.astype(full)
            dk = dot(ds, diag(q, mask_ref))
            dq = undiag(k.T, ds, mask_ref) * (HEAD_DIM**-0.5)
            dq = dq.astype(low)
            dv = dv.astype(low)
            dproj_ref[0, rows, :] = dq
            dproj_ref[1, rows, :] = dk.astype(low)
            dproj_ref[2, rows, :] = dv
            sums_ref[2:3, cols] += jnp.sum(dq.astype(full), 0, keepdims=True)
            sums_ref[3:4, cols] += jnp.sum(dv.astype(full), 0, keepdims=True)
            return inner

        lax.fori_loop(0, windows, window, 0)
        for part in range(3):
            d = dproj_ref[part]
            gq_ref[part * GROUPS + g] = dot(n1t_ref[...], d).astype(gq_ref.dtype)
            dn_ref[...] += dot_nt(d, wq_ref[part * GROUPS + g])
        return carry

    lax.fori_loop(0, GROUPS, group, 0)

    def finish(w, carry):
        rows = window_rows(w)
        xhat, scale = norm_parts(x_ref[rows, :].astype(full))
        dn = dn_ref[rows, :]
        grad_ref[rows, :] = dx1_ref[rows, :] + norm_back(xhat, scale, dn, vec_ref[0:1, :])
        sums_ref[0:1, :] += jnp.sum(dn * xhat, 0, keepdims=True)
        sums_ref[1:2, :] += jnp.sum(dn, 0, keepdims=True)
        return carry

    lax.fori_loop(0, windows, finish, 0)
    gtab_ref[...] = table_grad(line_ref, tmp_ref, bias_ref)


def shape(dims, kind):
    return jax.ShapeDtypeStruct(dims, kind)


def vmem_call(body, outs, scratch, args, name, limit=60):
    spec = pl.BlockSpec(memory_space=pltpu.VMEM)
    return pl.pallas_call(
        body,
        out_shape=outs,
        in_specs=[pl.BlockSpec(memory_space=pltpu.SMEM) if a.dtype == full and a.ndim == 1 else spec for a in args],
        out_specs=[spec] * len(outs),
        scratch_shapes=scratch,
        compiler_params=pltpu.CompilerParams(vmem_limit_bytes=limit * MIB),
        name=name,
    )(*args)


def local_step(tokens, out_grad, count, wq, wp, up, down, vec, tab, bu, tile, grad_kind):
    windows = tokens.shape[0]
    n = MLP // tile
    rows = windows * TOK
    x = tokens.reshape(rows, C)
    dy = out_grad.reshape(rows, C)
    live = (jnp.arange(windows) < count).astype(full)
    line = jnp.asarray(line_matrix(), low)
    masks = jnp.asarray(head_masks(), low)
    V = pltpu.VMEM
    qkv, pt, o, x1, n1t = vmem_call(
        functools.partial(attention_forward, windows),
        [shape((9, ROWS, GCOLS), low), shape((GROUPS, windows, TOK, PACK), low), shape((ROWS, C), low), shape((rows, C), full), shape((C, ROWS), low)],
        [V((ROWS, C), low), V((GROUPS, TOK, PACK), full), V((2, TOK * HEADS, 128), full)],
        (x, vec, tab, line, masks, wq, wp), "attention_forward")
    out, dx1, do, gup, gdown, gout, sums, bsum = vmem_call(
        functools.partial(feed_forward, windows, tile),
        [shape((rows, C), low), shape((ROWS, C), full), shape((rows, C), low), shape((n, C, tile), grad_kind), shape((n, C, tile), grad_kind),
         shape((C, C), grad_kind), shape((8, C), full), shape((n, 1, tile), full)],
        [V((ROWS, C), low), V((C, ROWS), low), V((ROWS, C), low), V((C, ROWS), low), V((ROWS, C), full), V((ROWS, C), full)],
        (x1, dy, live, vec, bu, up, down, wp, o), "feed_forward")
    gq, gtab, sums, grad = vmem_call(
        functools.partial(attention_backward, windows),
        [shape((9, C, GCOLS), grad_kind), shape((HEADS, TAB_LANES), full), shape((8, C), full), shape((rows, C), full)],
        [V((GROUPS, TOK, PACK), full), V((2, TOK * HEADS, 128), full), V((3, ROWS, GCOLS), low), V((ROWS, C), full)],
        (x, vec, line, masks, wq, qkv, pt, do, dx1, n1t, sums), "attention_backward")
    return (out.reshape(tokens.shape), grad.reshape(tokens.shape), gq, gout, gup, gdown, sums, bsum, gtab)


def adamw(weight, moment, second, gradient, step_rate):
    moment_new = beta_one * moment + (1.0 - beta_one) * gradient
    second_new = beta_two * second + (1.0 - beta_two) * gradient * gradient
    update = (
        moment_new
        / (1.0 - beta_one**STEP)
        / (jnp.sqrt(second_new / (1.0 - beta_two**STEP)) + adam_eps)
    )
    weight_new = weight * (1.0 - step_rate * weight_decay) - step_rate * update
    return (weight_new, moment_new, second_new)


def shards(
    tokens, out_grad, window_count,
    qkv_weight, qkv_first, qkv_second,
    output_weight, output_first, output_second,
    up_weight, up_first, up_second,
    down_weight, down_first, down_second,
    vectors, vector_first, vector_second,
    bias_table, table_first, table_second,
):
    tile = 512
    n = MLP // tile
    gather = functools.partial(lax.all_gather, axis_name="shard", tiled=True)
    wq = gather(qkv_weight.astype(low), axis=0).reshape(C, 9, GCOLS).transpose(1, 0, 2)
    wp = gather(output_weight.astype(low), axis=0)
    up = gather(up_weight.astype(low), axis=0).reshape(C, n, tile).transpose(1, 0, 2)
    down = gather(down_weight.astype(low), axis=0).reshape(n, tile, C)
    vec = gather(vectors.astype(low), axis=1).astype(full)
    tab = gather(bias_table.astype(low), axis=0).astype(full)
    table_rows = tab.shape[0]
    bu = vec[8:].reshape(n, 1, tile)
    vec = jnp.pad(vec, ((0, 4), (0, 0)))
    tab = jnp.pad(tab.T, ((0, 0), (0, TAB_LANES - table_rows)))
    out, grad, gq, gout, gup, gdown, sums, bsum, gtab = local_step(
        tokens, out_grad, window_count[0], wq, wp, up, down, vec, tab, bu, tile, full)
    gq = gq.transpose(1, 0, 2).reshape(C, 3 * C)
    gup = gup.transpose(1, 0, 2).reshape(C, MLP)
    gdown = gdown.transpose(0, 2, 1).reshape(MLP, C)
    gvec = jnp.concatenate([sums, bsum.reshape(-1, C)], 0)
    gtab = gtab.T[:table_rows]
    scatter = functools.partial(lax.psum_scatter, axis_name="shard", tiled=True)
    totals = lax.psum(
        (scatter(gq, scatter_dimension=0), scatter(gout, scatter_dimension=0), scatter(gup, scatter_dimension=0),
         scatter(gdown, scatter_dimension=0), scatter(gvec, scatter_dimension=1), scatter(gtab, scatter_dimension=0)), "rep")
    qkv_state = adamw(qkv_weight, qkv_first, qkv_second, totals[0], step_rates[0])
    output_state = adamw(output_weight, output_first, output_second, totals[1], step_rates[1])
    up_state = adamw(up_weight, up_first, up_second, totals[2], step_rates[2])
    down_state = adamw(down_weight, down_first, down_second, totals[3], step_rates[3])
    vector_state = adamw(vectors, vector_first, vector_second, totals[4], step_rates[4])
    table_state = adamw(bias_table, table_first, table_second, totals[5], step_rates[5])
    return (
        out, grad,
        *qkv_state, qkv_state[0].astype(low),
        *output_state, output_state[0].astype(low),
        *up_state, up_state[0].astype(low),
        *down_state, down_state[0].astype(low),
        *vector_state,
        *table_state,
    )


def solution(mesh):
    wins = P(("rep", "shard"), None, None)
    rows = P("shard", None)
    cols = P(None, "shard")
    return jax.shard_map(
        shards,
        mesh=mesh,
        in_specs=(wins, wins, P(("rep", "shard"))) + (rows,) * 12 + (cols,) * 3 + (rows,) * 3,
        out_specs=(wins, wins) + (rows,) * 16 + (cols,) * 3 + (rows,) * 3,
        check_vma=False,
    )
```

```python
import functools
import math

import jax
import jax.numpy as jnp
import numpy as np
from jax import lax
from jax.experimental import pallas as pl
from jax.experimental.pallas import tpu as pltpu
from jax.sharding import PartitionSpec as P

C = 768
HEADS = 24
MLP = 3072
WIN = 12
STEP = 5
HEAD_DIM = 32
SPAN = 2 * WIN - 1
TOK = WIN * WIN
TAB_ROWS = 536
ROWS = 1024
GROUPS = 3
GCOLS = 256
GHEADS = 8
PACK = GHEADS * TOK
TAB_LANES = 640
TILES = 3
TILE = MLP // TILES
SUB = 512
LINE = 384
MIB = 1 << 20

beta_one = 0.5
beta_two = 0.6
weight_decay = 0.05
adam_eps = 1e-08
norm_eps = 1e-05
step_rates = (0.04, 0.15, 0.04, 0.02, 0.2, 1.0)
low = jnp.bfloat16
full = jnp.float32
NT = (((1,), (1,)), ((), ()))


def dot(a, b):
    return jnp.dot(a, b, preferred_element_type=full)


def dot_nt(a, b):
    return lax.dot_general(a, b, NT, preferred_element_type=full)


def line_matrix():
    out = np.zeros((TAB_LANES, LINE), np.float32)
    col = np.arange(SPAN * WIN)
    out[(col // WIN) * SPAN + col % WIN + WIN - 1, col] = 1.0
    return out


def head_masks():
    lane = np.arange(GCOLS) // HEAD_DIM
    one = (lane[None, :] == np.arange(GHEADS)[:, None]).astype(np.float32)
    return np.broadcast_to(one[:, None, :], (GHEADS, 16, GCOLS))


def norm_parts(z):
    mean = jnp.sum(z, -1, keepdims=True) * (1.0 / C)
    center = z - mean
    spread = jnp.sum(center * center, -1, keepdims=True) * (1.0 / C)
    scale = lax.rsqrt(spread + norm_eps)
    return center * scale, scale


def norm_back(xhat, scale, dn, gain):
    g = dn * gain
    m1 = jnp.sum(g, -1, keepdims=True) * (1.0 / C)
    m2 = jnp.sum(g * xhat, -1, keepdims=True) * (1.0 / C)
    return scale * (g - m1 - xhat * m2)


def diag(x, mask_ref):
    head = x[0:128].reshape(8, 16, GCOLS)
    tail = x[128:144]
    parts = []
    for h in range(GHEADS):
        parts.append((head * mask_ref[h][None]).reshape(128, GCOLS))
    for h in range(GHEADS):
        parts.append(tail * mask_ref[h])
    return jnp.concatenate(parts, 0)


def undiag(xt, m, mask_ref):
    main = []
    for h in range(0, GHEADS, 2):
        r = dot(xt[h * HEAD_DIM : (h + 2) * HEAD_DIM], m[:, h * 128 : (h + 2) * 128])
        main.append(r[0:HEAD_DIM, 0:128])
        main.append(r[HEAD_DIM : 2 * HEAD_DIM, 128:256])
    main = jnp.concatenate(main, 0)
    rest = dot(xt, m[:, GHEADS * 128 :])
    rest_t = rest.T.reshape(GHEADS, 16, GCOLS)
    keep = mask_ref[...].astype(full)
    return jnp.concatenate([main.T, jnp.sum(rest_t * keep, 0)], 0)


def flat(x):
    return x.reshape(x.shape[0] * x.shape[1], x.shape[2])


def blocks(x, owners):
    return x.reshape(owners, x.shape[0] // owners, x.shape[1])


def hidden_place(t, s):
    at = (MLP // GHEADS) * s + 128 * t
    return 8 + at // C, at % C


def unpack_small(small_ref, vec_ref):
    owners = small_ref.shape[0]
    width = C // owners
    count = TAB_ROWS // owners
    vec = jnp.zeros((16, C), full)
    tab = jnp.zeros((HEADS, TAB_LANES), full)
    lane = lax.broadcasted_iota(jnp.int32, (16, 128), 1)
    lane_tab = lax.broadcasted_iota(jnp.int32, (HEADS, 128), 1)
    for s in range(owners):
        piece = small_ref[s].astype(full)
        part = jnp.where(lane < width, piece[0:16], 0.0)
        part = jnp.concatenate([part, jnp.zeros((16, C - 128), full)], 1)
        vec = vec + (pltpu.roll(part, width * s, 1) if s else part)
        part = jnp.where(lane_tab < count, piece[16 : 16 + HEADS], 0.0)
        part = jnp.concatenate([part, jnp.zeros((HEADS, TAB_LANES - 128), full)], 1)
        tab = tab + (pltpu.roll(part, count * s, 1) if s else part)
    vec_ref[...] = vec
    return tab


def pack_small(vec, tab, out_ref):
    owners = out_ref.shape[0]
    width = C // owners
    count = TAB_ROWS // owners
    for s in range(owners):
        out_ref[s, 0:16, :] = (pltpu.roll(vec, C - width * s, 1) if s else vec)[:, 0:128]
        out_ref[s, 16:40, :] = (pltpu.roll(tab, TAB_LANES - count * s, 1) if s else tab)[:, 0:128]


def build_bias(tab, line_ref, tmp_ref, bias_ref):
    def column(cj, carry):
        shifted = pltpu.roll(tab, cj, 1)
        line = dot(shifted.astype(low), line_ref[...])
        for rj in range(WIN):
            cut = (WIN - 1 - rj) * WIN
            part = pltpu.roll(line, LINE - cut, 1) if cut else line
            row = pl.multiple_of((rj * WIN + cj) * HEADS, 8)
            tmp_ref[0, pl.ds(row, HEADS), :] = part[:, 0:128]
            tmp_ref[1, pl.ds(row, HEADS), :] = part[:, 128:256]
        return carry

    lax.fori_loop(0, WIN, column, 0)
    lane = lax.broadcasted_iota(jnp.int32, (TOK, 128), 1)
    for g in range(GROUPS):
        rest = jnp.zeros((TOK, 128), full)
        for h in range(GHEADS):
            at = pl.ds(g * GHEADS + h, TOK, stride=HEADS)
            bias_ref[g, :, h * 128 : (h + 1) * 128] = tmp_ref[0, at, :]
            piece = tmp_ref[1, at, :]
            piece = pltpu.roll(piece, 16 * h, 1) if h else piece
            rest = jnp.where((lane >= 16 * h) & (lane < 16 * h + 16), piece, rest)
        bias_ref[g, :, GHEADS * 128 :] = rest


def table_grad(line_ref, tmp_ref, bias_ref):
    lane = lax.broadcasted_iota(jnp.int32, (TOK, 128), 1)
    for g in range(GROUPS):
        rest = bias_ref[g, :, GHEADS * 128 :]
        for h in range(GHEADS):
            at = pl.ds(g * GHEADS + h, TOK, stride=HEADS)
            tmp_ref[0, at, :] = bias_ref[g, :, h * 128 : (h + 1) * 128]
            piece = pltpu.roll(rest, 128 - 16 * h, 1) if h else rest
            tmp_ref[1, at, :] = jnp.where(lane < 16, piece, 0.0)

    def column(cj, total):
        line = jnp.zeros((HEADS, LINE), full)
        for rj in range(WIN):
            cut = (WIN - 1 - rj) * WIN
            row = pl.multiple_of((rj * WIN + cj) * HEADS, 8)
            part = jnp.concatenate([tmp_ref[0, pl.ds(row, HEADS), :], tmp_ref[1, pl.ds(row, HEADS), :], jnp.zeros((HEADS, 128), full)], 1)
            line = line + (pltpu.roll(part, cut, 1) if cut else part)
        high = line.astype(low)
        rest = (line - high.astype(full)).astype(low)
        spread = dot_nt(high, line_ref[...]) + dot_nt(rest, line_ref[...])
        return total + pltpu.roll(spread, TAB_LANES - cj, 1)

    return lax.fori_loop(0, WIN, column, jnp.zeros((HEADS, TAB_LANES), full))


def transpose_rows(src_ref, dst_ref):
    def block(i, carry):
        at = pl.multiple_of(i * 128, 128)
        dst_ref[:, pl.ds(at, 128)] = src_ref[pl.ds(at, 128), :].T
        return carry

    lax.fori_loop(0, ROWS // 128, block, 0)


def window_rows(w):
    return pl.ds(pl.multiple_of(w * TOK, 16), TOK)


def zero_tail(ref, windows):
    at = windows * TOK
    ref[at:ROWS, :] = jnp.zeros((ROWS - at, ref.shape[1]), ref.dtype)


def attention_forward(windows, x_ref, small_ref, line_ref, mask_ref, wq_ref, wp_ref,
                      qkv_ref, pt_ref, o_ref, x1_ref, n1t_ref, vec_ref, n1_ref, bias_ref, tmp_ref):
    tab = unpack_small(small_ref, vec_ref)
    build_bias(tab, line_ref, tmp_ref, bias_ref)
    zero_tail(n1_ref, windows)
    zero_tail(o_ref, windows)

    def first_norm(w, carry):
        xhat, _ = norm_parts(x_ref[window_rows(w), :].astype(full))
        n1_ref[window_rows(w), :] = (xhat * vec_ref[0:1, :] + vec_ref[1:2, :]).astype(low)
        return carry

    lax.fori_loop(0, windows, first_norm, 0)
    transpose_rows(n1_ref, n1t_ref)

    def group(g, carry):
        cols = pl.ds(pl.multiple_of(g * GCOLS, GCOLS), GCOLS)
        n1 = n1_ref[...]
        qkv_ref[g] = ((dot(n1, flat(wq_ref[g, 0])) + vec_ref[2:3, cols]) * (HEAD_DIM**-0.5)).astype(low)
        qkv_ref[GROUPS + g] = dot(n1, flat(wq_ref[g, 1])).astype(low)
        qkv_ref[2 * GROUPS + g] = (dot(n1, flat(wq_ref[g, 2])) + vec_ref[3:4, cols]).astype(low)

        def window(w, inner):
            rows = window_rows(w)
            q = qkv_ref[g, rows, :]
            k = qkv_ref[GROUPS + g, rows, :]
            v = qkv_ref[2 * GROUPS + g, rows, :]
            s = dot_nt(k, diag(q, mask_ref)) + bias_ref[g]
            e = jnp.exp(s - jnp.max(s, 0, keepdims=True))
            p = (e * (1.0 / jnp.sum(e, 0, keepdims=True))).astype(low)
            pt_ref[g, w] = p
            o_ref[rows, cols] = undiag(v.T, p, mask_ref).astype(low)
            return inner

        lax.fori_loop(0, windows, window, 0)
        return carry

    lax.fori_loop(0, GROUPS, group, 0)

    def output(w, carry):
        rows = window_rows(w)
        branch = dot(o_ref[rows, :], flat(wp_ref[...])) + vec_ref[4:5, :]
        x1_ref[rows, :] = x_ref[rows, :].astype(full) + branch
        return carry

    lax.fori_loop(0, windows, output, 0)


def gelu_both(h):
    c = math.sqrt(2.0 / math.pi)
    square = h * h
    t = jnp.tanh(h * (c + (c * 0.044715) * square))
    half = 0.5 + 0.5 * t
    slope = half + (0.5 * h) * (1.0 - t * t) * (c + (3.0 * c * 0.044715) * square)
    return h * half, slope


def feed_forward(windows, x1_ref, dy_ref, live_ref, vec_ref, up_ref, down_ref, wp_ref, o_ref,
                 out_ref, dx1_ref, do_ref, gup_ref, gdown_ref, gout_ref, sums_ref,
                 n2_ref, n2t_ref, dy2_ref, dyt_ref, y_ref, dn_ref, bu_ref, bsum_ref):
    zero_tail(n2_ref, windows)
    zero_tail(dy2_ref, windows)

    def second_norm(w, carry):
        rows = window_rows(w)
        xhat, _ = norm_parts(x1_ref[rows, :])
        n2_ref[rows, :] = (xhat * vec_ref[5:6, :] + vec_ref[6:7, :]).astype(low)
        dy2_ref[rows, :] = (dy_ref[rows, :].astype(full) * live_ref[w]).astype(low)
        return carry

    lax.fori_loop(0, windows, second_norm, 0)
    transpose_rows(n2_ref, n2t_ref)
    transpose_rows(dy2_ref, dyt_ref)
    y_ref[...] = jnp.zeros_like(y_ref)
    dn_ref[...] = jnp.zeros_like(dn_ref)
    owners = gup_ref.shape[1]
    for t in range(TILES):
        for s in range(TILE // 128):
            row, at = hidden_place(t, s)
            bu_ref[t, :, s * 128 : (s + 1) * 128] = vec_ref[row : row + 1, at : at + 128]

    def step(t, carry):
        for part in range(TILE // SUB):
            cols = slice(part * SUB, (part + 1) * SUB)
            up = flat(up_ref[t, :, :, cols])
            down = flat(down_ref[t, part * SUB // 128 : (part + 1) * SUB // 128])
            h = dot(n2_ref[...], up) + bu_ref[t, :, cols]
            da = dot_nt(dy2_ref[...], down)
            act, slope = gelu_both(h)
            a = act.astype(low)
            dh = (da * slope).astype(low)
            bsum_ref[t, :, cols] = jnp.sum(dh.astype(full), 0, keepdims=True)
            y_ref[...] += dot(a, down)
            dn_ref[...] += dot_nt(dh, up)
            gd = dot(dyt_ref[...], a).astype(low)
            for b in range(SUB // 128):
                gdown_ref[t, part * SUB // 128 + b] = gd[:, b * 128 : (b + 1) * 128]
            gup_ref[t, :, :, cols] = blocks(dot(n2t_ref[...], dh).astype(low), owners)
        return carry

    lax.fori_loop(0, TILES, step, 0)
    sums_ref[...] = jnp.zeros_like(sums_ref)
    for t in range(TILES):
        for s in range(TILE // 128):
            row, at = hidden_place(t, s)
            sums_ref[row : row + 1, at : at + 128] = bsum_ref[t, :, s * 128 : (s + 1) * 128]
    zero_tail(dx1_ref, windows)

    def finish(w, carry):
        rows = window_rows(w)
        x1 = x1_ref[rows, :]
        out_ref[rows, :] = ((x1 + y_ref[rows, :] + vec_ref[7:8, :]) * live_ref[w]).astype(low)
        xhat, scale = norm_parts(x1)
        dn = dn_ref[rows, :]
        dy = dy2_ref[rows, :].astype(full)
        dx1 = dy + norm_back(xhat, scale, dn, vec_ref[5:6, :])
        dx1_ref[rows, :] = dx1
        dr = dx1.astype(low)
        n2_ref[rows, :] = dr
        do_ref[rows, :] = dot_nt(dr, flat(wp_ref[...])).astype(low)
        sums_ref[4:5, :] += jnp.sum(dr.astype(full), 0, keepdims=True)
        sums_ref[5:6, :] += jnp.sum(dn * xhat, 0, keepdims=True)
        sums_ref[6:7, :] += jnp.sum(dn, 0, keepdims=True)
        sums_ref[7:8, :] += jnp.sum(dy, 0, keepdims=True)
        return carry

    lax.fori_loop(0, windows, finish, 0)
    transpose_rows(o_ref, dyt_ref)
    for g in range(GROUPS):
        at = pl.ds(g * GCOLS, GCOLS)
        gout_ref[:, :, at] = blocks(dot(dyt_ref[...], n2_ref[:, at]).astype(low), gout_ref.shape[0])


def attention_backward(windows, x_ref, vec_ref, line_ref, mask_ref, wq_ref, qkv_ref, pt_ref, do_ref, dx1_ref, n1t_ref, sums_in_ref,
                       gq_ref, gsmall_ref, grad_ref, sums_ref, bias_ref, tmp_ref, dproj_ref, dn_ref):
    bias_ref[...] = jnp.zeros_like(bias_ref)
    dn_ref[...] = jnp.zeros_like(dn_ref)
    sums_ref[...] = sums_in_ref[...]
    for part in range(3):
        dproj_ref[part, windows * TOK :, :] = jnp.zeros((ROWS - windows * TOK, GCOLS), low)

    def group(g, carry):
        cols = pl.ds(pl.multiple_of(g * GCOLS, GCOLS), GCOLS)

        def window(w, inner):
            rows = window_rows(w)
            q = qkv_ref[g, rows, :]
            k = qkv_ref[GROUPS + g, rows, :]
            v = qkv_ref[2 * GROUPS + g, rows, :]
            p = pt_ref[g, w]
            do = diag(do_ref[rows, cols], mask_ref)
            dp = dot_nt(v, do)
            dv = dot(p, do)
            pf = p.astype(full)
            ds = (pf * (dp - jnp.sum(pf * dp, 0, keepdims=True))).astype(low)
            bias_ref[g] += ds.astype(full)
            dk = dot(ds, diag(q, mask_ref))
            dq = undiag(k.T, ds, mask_ref) * (HEAD_DIM**-0.5)
            dq = dq.astype(low)
            dv = dv.astype(low)
            dproj_ref[0, rows, :] = dq
            dproj_ref[1, rows, :] = dk.astype(low)
            dproj_ref[2, rows, :] = dv
            sums_ref[2:3, cols] += jnp.sum(dq.astype(full), 0, keepdims=True)
            sums_ref[3:4, cols] += jnp.sum(dv.astype(full), 0, keepdims=True)
            return inner

        lax.fori_loop(0, windows, window, 0)
        for part in range(3):
            d = dproj_ref[part]
            gq_ref[g, part] = blocks(dot(n1t_ref[...], d).astype(low), gq_ref.shape[2])
            dn_ref[...] += dot_nt(d, flat(wq_ref[g, part]))
        return carry

    lax.fori_loop(0, GROUPS, group, 0)

    def finish(w, carry):
        rows = window_rows(w)
        xhat, scale = norm_parts(x_ref[rows, :].astype(full))
        dn = dn_ref[rows, :]
        grad_ref[rows, :] = dx1_ref[rows, :] + norm_back(xhat, scale, dn, vec_ref[0:1, :])
        sums_ref[0:1, :] += jnp.sum(dn * xhat, 0, keepdims=True)
        sums_ref[1:2, :] += jnp.sum(dn, 0, keepdims=True)
        return carry

    lax.fori_loop(0, windows, finish, 0)
    pack_small(sums_ref[...], table_grad(line_ref, tmp_ref, bias_ref), gsmall_ref)


MESH = pl.DeviceIdType.MESH
REPS = 4
OWNERS = 8
LINKS = OWNERS // 2


class Spot:
    def __init__(self):
        self.rep = lax.axis_index("rep")
        shard = lax.axis_index("shard")
        self.z = shard // 2
        self.core = shard % 2
        self.shard = shard

    def sibling(self):
        return (self.rep, self.z * 2 + (1 - self.core))

    def along_z(self, step):
        return (self.rep, ((self.z + step) % LINKS) * 2 + self.core)

    def along_rep(self, step):
        return ((self.rep + step) % REPS, self.shard)


def greet(spot):
    barrier = pltpu.get_barrier_semaphore()
    peers = [(spot.rep, (spot.shard + i) % OWNERS) for i in range(1, OWNERS)] + [spot.along_rep(i) for i in range(1, REPS)]
    for peer in peers:
        pl.semaphore_signal(barrier, inc=1, device_id=peer, device_id_type=MESH)
    pl.semaphore_wait(barrier, len(peers))


def send(src, dst, send_sem, recv_sem, peer):
    copy = pltpu.make_async_remote_copy(src_ref=src, dst_ref=dst, send_sem=send_sem, recv_sem=recv_sem, device_id=peer, device_id_type=MESH)
    copy.start()
    return copy


def cutter(rows, cols):
    down = 2 if rows % 32 == 0 and cols % 256 == 0 else (4 if rows % 64 == 0 else 1)
    across = REPS // down
    tall, wide = rows // down, cols // across

    def cut(ref, index):
        lead = (slice(None),) * (len(ref.shape) - 2)
        top = pl.multiple_of((index // across) * tall, 16) if down > 1 else 0
        left = pl.multiple_of((index % across) * wide, 128) if across > 1 else 0
        return ref.at[lead + (pl.ds(top, tall), pl.ds(left, wide))]

    return cut, tall, wide


class Gather:
    SEMS = 2 * ((LINKS - 1) + (LINKS - 1) * (REPS - 1) + LINKS)

    def __init__(self, spot, src, place, sems):
        self.spot, self.src, self.place = spot, src, place
        self.cut = cutter(*src.shape[-2:])[0]
        self.sems = sems
        self.sent = []

    def sem(self, side, kind, i, j=0):
        base = (0, LINKS - 1, (LINKS - 1) * REPS)[kind]
        return self.sems.at[side * (self.SEMS // 2) + base + i * ((REPS - 1) if kind == 1 else 1) + j]

    def owner(self, step, core):
        return ((self.spot.z - step + LINKS) % LINKS) * 2 + core

    def start(self):
        spot = self.spot
        mine = self.place(spot.shard)
        for i in range(1, LINKS):
            self.sent.append(send(self.cut(self.src, spot.rep), self.cut(mine, spot.rep), self.sem(0, 0, i - 1), self.sem(1, 0, i - 1), spot.along_z(i)))
        self.sent.append(send(self.src, mine, self.sem(0, 2, 0), self.sem(1, 2, 0), spot.sibling()))

    def across(self):
        spot = self.spot
        for i in range(1, LINKS):
            block = self.cut(self.place(self.owner(i, spot.core)), spot.rep)
            self.got(block, self.sem(1, 0, i - 1))
            for j in range(1, REPS):
                self.sent.append(send(block, block, self.sem(0, 1, i - 1, j - 1), self.sem(1, 1, i - 1, j - 1), spot.along_rep(j)))

    def beside(self):
        spot = self.spot
        for i in range(1, LINKS):
            block = self.place(self.owner(i, spot.core))
            for j in range(1, REPS):
                self.got(self.cut(block, (spot.rep - j + REPS) % REPS), self.sem(1, 1, i - 1, j - 1))
            self.sent.append(send(block, block, self.sem(0, 2, i), self.sem(1, 2, i), spot.sibling()))

    def finish(self):
        for i in range(LINKS):
            self.got(self.place(self.owner(i, 1 - self.spot.core)), self.sem(1, 2, i))

    def got(self, ref, sem):
        pltpu.make_async_copy(ref, ref, sem).wait()

    def close(self):
        for copy in self.sent:
            copy.wait_send()


class Reduce:
    SEMS = 2 * (1 + 2 * (REPS - 1) + (LINKS - 1)) + 2 * (LINKS - 1)

    def __init__(self, spot, place, out, beside, parts, sums, links, sems):
        self.spot, self.place, self.out = spot, place, out
        self.beside_ref, self.parts, self.sums, self.links = beside, parts, sums, links
        self.cut, self.tall, self.wide = cutter(*out.shape[-2:])
        self.sems = sems
        self.sent = []

    def sem(self, side, kind, i):
        base = (0, LINKS, LINKS + REPS - 1, LINKS + 2 * (REPS - 1))[kind]
        return self.sems.at[side * (self.SEMS // 2) + base + i]

    def got(self, ref, sem):
        pltpu.make_async_copy(ref, ref, sem).wait()

    def start(self):
        spot = self.spot
        for z in range(LINKS):
            self.sent.append(send(self.place(z * 2 + (1 - spot.core)), self.beside_ref.at[z], self.sem(0, 0, z), self.sem(1, 0, z), spot.sibling()))

    def across(self):
        spot = self.spot
        for z in range(LINKS):
            half = self.beside_ref.at[z]
            self.got(half, self.sem(1, 0, z))
            half[...] = (half[...].astype(full) + self.place(z * 2 + spot.core)[...].astype(full)).astype(low)
        for j in range(1, REPS):
            to = (spot.rep + j) % REPS
            self.sent.append(send(self.cut(self.beside_ref, to), self.parts.at[j - 1], self.sem(0, 1, j - 1), self.sem(1, 1, j - 1), spot.along_rep(j)))

    def along(self):
        spot = self.spot
        for j in range(1, REPS):
            self.got(self.parts.at[j - 1], self.sem(1, 1, j - 1))
        own = self.cut(self.beside_ref, spot.rep)
        for z in range(LINKS):
            total = own[z].astype(full)
            for j in range(1, REPS):
                total = total + self.parts[j - 1, z].astype(full)
            self.sums[z] = total.astype(low)
        for i in range(1, LINKS):
            self.sent.append(send(self.sums.at[(spot.z + i) % LINKS], self.links.at[i - 1], self.sem(0, 3, i - 1), self.sem(1, 3, i - 1), spot.along_z(i)))

    def spread(self):
        spot = self.spot
        for i in range(1, LINKS):
            self.got(self.links.at[i - 1], self.sem(1, 3, i - 1))
        total = self.sums[spot.z].astype(full)
        for i in range(1, LINKS):
            total = total + self.links[i - 1].astype(full)
        mine = self.cut(self.out, spot.rep)
        mine[...] = total.astype(low)
        for j in range(1, REPS):
            self.sent.append(send(mine, mine, self.sem(0, 2, j - 1), self.sem(1, 2, j - 1), spot.along_rep(j)))

    def finish(self):
        for j in range(1, REPS):
            self.got(self.cut(self.out, (self.spot.rep - j + REPS) % REPS), self.sem(1, 2, j - 1))

    def close(self):
        for copy in self.sent:
            copy.wait_send()


class ReduceSmall:
    SEMS = 2 * (LINKS + (LINKS - 1) + (REPS - 1))

    def __init__(self, spot, terms, out, beside, links, parts, sems):
        self.spot, self.terms, self.out, self.beside_ref, self.links, self.parts = spot, terms, out, beside, links, parts
        self.sems = sems
        self.sent = []

    def sem(self, side, kind, i):
        return self.sems.at[side * (self.SEMS // 2) + (0, LINKS, 2 * LINKS - 1)[kind] + i]

    def got(self, ref, sem):
        pltpu.make_async_copy(ref, ref, sem).wait()

    def start(self):
        spot = self.spot
        for z in range(LINKS):
            self.sent.append(send(self.terms.at[z * 2 + (1 - spot.core)], self.beside_ref.at[z], self.sem(0, 0, z), self.sem(1, 0, z), spot.sibling()))

    def across(self):
        spot = self.spot
        for z in range(LINKS):
            self.got(self.beside_ref.at[z], self.sem(1, 0, z))
            self.beside_ref[z] = self.beside_ref[z] + self.terms[z * 2 + spot.core]
        for i in range(1, LINKS):
            self.sent.append(send(self.beside_ref.at[(spot.z + i) % LINKS], self.links.at[i - 1], self.sem(0, 1, i - 1), self.sem(1, 1, i - 1), spot.along_z(i)))

    def along(self):
        spot = self.spot
        for i in range(1, LINKS):
            self.got(self.links.at[i - 1], self.sem(1, 1, i - 1))
        total = self.beside_ref[spot.z]
        for i in range(1, LINKS):
            total = total + self.links[i - 1]
        self.parts[spot.rep] = total
        mine = self.parts.at[spot.rep]
        for j in range(1, REPS):
            self.sent.append(send(mine, mine, self.sem(0, 2, j - 1), self.sem(1, 2, j - 1), spot.along_rep(j)))

    def spread(self):
        for j in range(1, REPS):
            self.got(self.parts.at[(self.spot.rep - j + REPS) % REPS], self.sem(1, 2, j - 1))
        total = self.parts[0]
        for j in range(1, REPS):
            total = total + self.parts[j]
        self.out[...] = total

    def finish(self):
        pass

    def close(self):
        for copy in self.sent:
            copy.wait_send()


def shape(dims, kind):
    return jax.ShapeDtypeStruct(dims, kind)


def vmem_call(body, outs, scratch, args, name, limit=60, **params):
    spec = pl.BlockSpec(memory_space=pltpu.VMEM)
    return pl.pallas_call(
        body,
        out_shape=outs,
        in_specs=[pl.BlockSpec(memory_space=pltpu.SMEM) if a.dtype == full and a.ndim == 1 else spec for a in args],
        out_specs=[spec] * len(outs),
        scratch_shapes=scratch,
        compiler_params=pltpu.CompilerParams(vmem_limit_bytes=limit * MIB, **params),
        name=name,
    )(*args)


def gather_weights(q_ref, p_ref, u_ref, d_ref, s_ref, wq_ref, wp_ref, up_ref, down_ref, small_ref, sems, local, small_sems):
    spot = Spot()
    greet(spot)
    mine = spot.shard
    own = []
    for src, dst in ((q_ref, wq_ref.at[:, :, mine]), (p_ref, wp_ref.at[mine]), (u_ref, up_ref.at[:, mine]), (d_ref, down_ref.at[:, mine]), (s_ref, small_ref.at[mine])):
        own.append(pltpu.make_async_copy(src, dst, local.at[len(own)]))
        own[-1].start()
    small = []
    for i in range(1, OWNERS):
        to = (spot.shard + i) % OWNERS
        small.append(send(s_ref, small_ref.at[mine], small_sems.at[i], small_sems.at[OWNERS + i], (spot.rep, to)))
    chunks = [(q_ref.at[g], lambda s, g=g: wq_ref.at[g, :, s]) for g in range(GROUPS)]
    chunks.append((p_ref, lambda s: wp_ref.at[s]))
    for t in range(TILES):
        chunks.append((u_ref.at[t], lambda s, t=t: up_ref.at[t, s]))
        chunks.append((d_ref.at[t], lambda s, t=t: down_ref.at[t, s]))
    jobs = [Gather(spot, src, place, sems.at[i]) for i, (src, place) in enumerate(chunks)]
    for job in jobs:
        job.start()
    for tick in range(len(jobs) + 2):
        if tick >= 2:
            jobs[tick - 2].finish()
        if 1 <= tick <= len(jobs):
            jobs[tick - 1].beside()
        if tick < len(jobs):
            jobs[tick].across()
    for i in range(1, OWNERS):
        at = small_ref.at[(spot.shard - i + OWNERS) % OWNERS]
        pltpu.make_async_copy(at, at, small_sems.at[OWNERS + i]).wait()
    for copy in small:
        copy.wait_send()
    for copy in own:
        copy.wait()
    for job in jobs:
        job.close()


def reduce_gradients(gq_ref, gp_ref, gu_ref, gd_ref, gs_ref, q_ref, p_ref, u_ref, d_ref, s_ref, *scratch):
    spot = Spot()
    greet(spot)
    jobs = []
    sems = scratch[-2]
    views = []
    for t in range(TILES):
        views.append((lambda s, t=t: gd_ref.at[t, s], d_ref.at[t]))
        views.append((lambda s, t=t: gu_ref.at[t, s], u_ref.at[t]))
    views.append((lambda s: gp_ref.at[s], p_ref))
    for g in range(GROUPS):
        views.append((lambda s, g=g: gq_ref.at[g, :, s], q_ref.at[g]))
    for i, (place, out) in enumerate(views):
        jobs.append(Reduce(spot, place, out, *scratch[4 * i : 4 * i + 4], sems.at[i]))
    jobs.append(ReduceSmall(spot, gs_ref, s_ref, *scratch[-5:-2], scratch[-1]))
    for job in jobs:
        job.start()
    count = len(jobs)
    for tick in range(count + 3):
        for delay, name in ((3, "finish"), (2, "spread"), (1, "along"), (0, "across")):
            if 0 <= tick - delay < count:
                getattr(jobs[tick - delay], name)()
    for job in jobs:
        job.close()


def reduce_scratch():
    out = []
    for lead, rows, cols in [((), C, 128), ((), C // OWNERS, TILE)] * TILES + [((), C // OWNERS, C)] + [((3,), C // OWNERS, GCOLS)] * GROUPS:
        _, tall, wide = cutter(rows, cols)
        V = pltpu.VMEM
        out += [V((LINKS, *lead, rows, cols), low), V((REPS - 1, LINKS, *lead, tall, wide), low), V((LINKS, *lead, tall, wide), low), V((LINKS - 1, *lead, tall, wide), low)]
    out += [pltpu.VMEM((LINKS, 40, 128), full), pltpu.VMEM((LINKS - 1, 40, 128), full), pltpu.VMEM((REPS, 40, 128), full)]
    return out


def adamw(weight, moment, second, gradient, step_rate):
    moment_new = beta_one * moment + (1.0 - beta_one) * gradient
    second_new = beta_two * second + (1.0 - beta_two) * gradient * gradient
    update = (
        moment_new
        / (1.0 - beta_one**STEP)
        / (jnp.sqrt(second_new / (1.0 - beta_two**STEP)) + adam_eps)
    )
    weight_new = weight * (1.0 - step_rate * weight_decay) - step_rate * update
    return (weight_new, moment_new, second_new)


def local_step(tokens, out_grad, window_count, small, wq, wp, up, down):
    windows = tokens.shape[0]
    rows = windows * TOK
    owned = C // OWNERS
    V = pltpu.VMEM
    x = tokens.reshape(rows, C)
    dy = out_grad.reshape(rows, C)
    live = (jnp.arange(windows) < window_count[0]).astype(full)
    line = jnp.asarray(line_matrix(), low)
    masks = jnp.asarray(head_masks(), low)
    qkv, pt, o, x1, n1t, vec = vmem_call(
        functools.partial(attention_forward, windows),
        [shape((9, ROWS, GCOLS), low), shape((GROUPS, windows, TOK, PACK), low), shape((ROWS, C), low), shape((rows, C), full), shape((C, ROWS), low),
         shape((16, C), full)],
        [V((ROWS, C), low), V((GROUPS, TOK, PACK), full), V((2, TOK * HEADS, 128), full)],
        (x, small, line, masks, wq, wp), "attention_forward")
    out, dx1, do, gup, gdown, gout, sums = vmem_call(
        functools.partial(feed_forward, windows),
        [shape((rows, C), low), shape((ROWS, C), full), shape((rows, C), low), shape((TILES, OWNERS, owned, TILE), low),
         shape((TILES, OWNERS, C, 128), low), shape((OWNERS, owned, C), low), shape((16, C), full)],
        [V((ROWS, C), low), V((C, ROWS), low), V((ROWS, C), low), V((C, ROWS), low), V((ROWS, C), full), V((ROWS, C), full),
         V((TILES, 1, TILE), full), V((TILES, 1, TILE), full)],
        (x1, dy, live, vec, up, down, wp, o), "feed_forward")
    gq, gsmall, grad = vmem_call(
        functools.partial(attention_backward, windows),
        [shape((GROUPS, 3, OWNERS, owned, GCOLS), low), shape((OWNERS, 40, 128), full), shape((rows, C), full)],
        [V((16, C), full), V((GROUPS, TOK, PACK), full), V((2, TOK * HEADS, 128), full), V((3, ROWS, GCOLS), low), V((ROWS, C), full)],
        (x, vec, line, masks, wq, qkv, pt, do, dx1, n1t, sums), "attention_backward")
    return out.reshape(tokens.shape), grad.reshape(tokens.shape), gq, gout, gup, gdown, gsmall


def shards(
    tokens, out_grad, window_count,
    qkv_weight, qkv_first, qkv_second,
    output_weight, output_first, output_second,
    up_weight, up_first, up_second,
    down_weight, down_first, down_second,
    vectors, vector_first, vector_second,
    bias_table, table_first, table_second,
):
    owned = C // OWNERS
    D = pltpu.SemaphoreType.DMA
    q = qkv_weight.astype(low).reshape(owned, 3, GROUPS, GCOLS).transpose(2, 1, 0, 3)
    u = up_weight.astype(low).reshape(owned, OWNERS, TILES, 128).transpose(2, 0, 1, 3).reshape(TILES, owned, TILE)
    d = down_weight.astype(low).reshape(TILES, 128, C)
    width, count = vectors.shape[1], bias_table.shape[0]
    small = jnp.concatenate([jnp.pad(vectors.astype(low), ((0, 4), (0, 128 - width))), jnp.pad(bias_table.astype(low).T, ((0, 8), (0, 128 - count)))], 0)
    anyspec = pl.BlockSpec(memory_space=pl.ANY)
    wq, wp, up, down, small = pl.pallas_call(
        gather_weights,
        out_shape=[shape((GROUPS, 3, OWNERS, owned, GCOLS), low), shape((OWNERS, owned, C), low), shape((TILES, OWNERS, owned, TILE), low),
                   shape((TILES, OWNERS, 128, C), low), shape((OWNERS, 48, 128), low)],
        in_specs=[anyspec] * 5, out_specs=[anyspec] * 5,
        scratch_shapes=[D((10, Gather.SEMS)), D((5,)), D((2 * OWNERS,))],
        compiler_params=pltpu.CompilerParams(collective_id=0, has_side_effects=True, vmem_limit_bytes=16 * MIB),
        name="gather_weights",
    )(q, output_weight.astype(low), u, d, small)

    out, grad, gq, gout, gup, gdown, gsmall = local_step(tokens, out_grad, window_count, small, wq, wp, up, down)
    gq, gp, gu, gd, gs = vmem_call(
        reduce_gradients,
        [shape((GROUPS, 3, owned, GCOLS), low), shape((owned, C), low), shape((TILES, owned, TILE), low), shape((TILES, C, 128), low), shape((40, 128), full)],
        reduce_scratch() + [D((10, Reduce.SEMS)), D((ReduceSmall.SEMS,))],
        (gq, gout, gup, gdown, gsmall), "reduce_gradients", collective_id=1, has_side_effects=True)
    gq = gq.astype(full).transpose(2, 1, 0, 3).reshape(owned, 3 * C)
    gu = gu.astype(full).reshape(TILES, owned, OWNERS, 128).transpose(1, 2, 0, 3).reshape(owned, MLP)
    gd = gd.astype(full).transpose(0, 2, 1).reshape(TILES * 128, C)
    qkv_state = adamw(qkv_weight, qkv_first, qkv_second, gq, step_rates[0])
    output_state = adamw(output_weight, output_first, output_second, gp.astype(full), step_rates[1])
    up_state = adamw(up_weight, up_first, up_second, gu, step_rates[2])
    down_state = adamw(down_weight, down_first, down_second, gd, step_rates[3])
    vector_state = adamw(vectors, vector_first, vector_second, gs[:12, :width], step_rates[4])
    table_state = adamw(bias_table, table_first, table_second, gs[16:40, :count].T, step_rates[5])
    return (
        out, grad,
        *qkv_state, qkv_state[0].astype(low),
        *output_state, output_state[0].astype(low),
        *up_state, up_state[0].astype(low),
        *down_state, down_state[0].astype(low),
        *vector_state,
        *table_state,
    )


def shards_general(
    tokens, out_grad, window_count,
    qkv_weight, qkv_first, qkv_second,
    output_weight, output_first, output_second,
    up_weight, up_first, up_second,
    down_weight, down_first, down_second,
    vectors, vector_first, vector_second,
    bias_table, table_first, table_second,
):
    gather = functools.partial(lax.all_gather, axis_name="shard", tiled=True)
    scatter = functools.partial(lax.psum_scatter, axis_name="shard", tiled=True)
    owned = C // OWNERS
    wq = gather(qkv_weight.astype(low), axis=0).reshape(OWNERS, owned, 3, GROUPS, GCOLS).transpose(3, 2, 0, 1, 4)
    wp = gather(output_weight.astype(low), axis=0).reshape(OWNERS, owned, C)
    up = gather(up_weight.astype(low), axis=0).reshape(OWNERS, owned, OWNERS, TILES, 128).transpose(3, 0, 1, 2, 4)
    up = up.reshape(TILES, OWNERS, owned, TILE)
    down = gather(down_weight.astype(low), axis=0).reshape(OWNERS, TILES, 128, C).transpose(1, 0, 2, 3)
    vec = gather(vectors.astype(low), axis=1)
    tab = gather(bias_table.astype(low), axis=0)
    table_rows = tab.shape[0]
    count = TAB_ROWS // OWNERS
    vec = vec.reshape(12, OWNERS, owned).transpose(1, 0, 2)
    tab = tab[:TAB_ROWS].reshape(OWNERS, count, HEADS).transpose(0, 2, 1)
    small = jnp.concatenate([jnp.pad(vec, ((0, 0), (0, 4), (0, 128 - owned))), jnp.pad(tab, ((0, 0), (0, 8), (0, 128 - count)))], 1)
    out, grad, gq, gp, gu, gd, gs = local_step(tokens, out_grad, window_count, small, wq, wp, up, down)
    gq = gq.astype(full).transpose(2, 3, 1, 0, 4).reshape(C, 3 * C)
    gu = gu.astype(full).reshape(TILES, C, OWNERS, 128).transpose(1, 2, 0, 3).reshape(C, MLP)
    gd = gd.astype(full).transpose(1, 0, 3, 2).reshape(MLP, C)
    gv = gs[:, :12, :owned].transpose(1, 0, 2).reshape(12, C)
    gb = gs[:, 16:40, :count].transpose(0, 2, 1).reshape(TAB_ROWS, HEADS)
    gb = jnp.pad(gb, ((0, table_rows - TAB_ROWS), (0, 0)))
    totals = lax.psum(
        (scatter(gq, scatter_dimension=0), scatter(gp.astype(full).reshape(C, C), scatter_dimension=0), scatter(gu, scatter_dimension=0),
         scatter(gd, scatter_dimension=0), scatter(gv, scatter_dimension=1), scatter(gb, scatter_dimension=0)), "rep")
    states = (
        (qkv_weight, qkv_first, qkv_second), (output_weight, output_first, output_second), (up_weight, up_first, up_second),
        (down_weight, down_first, down_second), (vectors, vector_first, vector_second), (bias_table, table_first, table_second))
    results = [out, grad]
    for i, (state, total, rate) in enumerate(zip(states, totals, step_rates)):
        new = adamw(*state, total, rate)
        results += [*new, new[0].astype(low)] if i < 4 else [*new]
    return tuple(results)


def solution(mesh):
    wins = P(("rep", "shard"), None, None)
    rows = P("shard", None)
    cols = P(None, "shard")
    fits = mesh.shape["rep"] == REPS and mesh.shape["shard"] == OWNERS
    return jax.shard_map(
        shards if fits else shards_general,
        mesh=mesh,
        in_specs=(wins, wins, P(("rep", "shard"))) + (rows,) * 12 + (cols,) * 3 + (rows,) * 3,
        out_specs=(wins, wins) + (rows,) * 16 + (cols,) * 3 + (rows,) * 3,
        check_vma=False,
    )
```

```python
import functools
import math

import jax
import jax.numpy as jnp
import numpy as np
from jax import lax
from jax.experimental import pallas as pl
from jax.experimental.pallas import tpu as pltpu
from jax.sharding import PartitionSpec as P

C = 768
HEADS = 24
MLP = 3072
WIN = 12
STEP = 5
HEAD_DIM = 32
SPAN = 2 * WIN - 1
TOK = WIN * WIN
TAB_ROWS = 536
ROWS = 1024
GROUPS = 3
GCOLS = 256
GHEADS = 8
PACK = GHEADS * TOK
TAB_LANES = 640
TILES = 3
TILE = MLP // TILES
SUB = 512
LINE = 384
MIB = 1 << 20

beta_one = 0.5
beta_two = 0.6
weight_decay = 0.05
adam_eps = 1e-08
norm_eps = 1e-05
step_rates = (0.04, 0.15, 0.04, 0.02, 0.2, 1.0)
low = jnp.bfloat16
full = jnp.float32
NT = (((1,), (1,)), ((), ()))


def dot(a, b):
    return jnp.dot(a, b, preferred_element_type=full)


def dot_nt(a, b):
    return lax.dot_general(a, b, NT, preferred_element_type=full)


def line_matrix():
    out = np.zeros((TAB_LANES, LINE), np.float32)
    col = np.arange(SPAN * WIN)
    out[(col // WIN) * SPAN + col % WIN + WIN - 1, col] = 1.0
    return out


def head_masks():
    lane = np.arange(GCOLS) // HEAD_DIM
    one = (lane[None, :] == np.arange(GHEADS)[:, None]).astype(np.float32)
    return np.broadcast_to(one[:, None, :], (GHEADS, 16, GCOLS))


def norm_parts(z):
    mean = jnp.sum(z, -1, keepdims=True) * (1.0 / C)
    center = z - mean
    spread = jnp.sum(center * center, -1, keepdims=True) * (1.0 / C)
    scale = lax.rsqrt(spread + norm_eps)
    return center * scale, scale


def norm_back(xhat, scale, dn, gain):
    g = dn * gain
    m1 = jnp.sum(g, -1, keepdims=True) * (1.0 / C)
    m2 = jnp.sum(g * xhat, -1, keepdims=True) * (1.0 / C)
    return scale * (g - m1 - xhat * m2)


def diag(x, mask_ref):
    head = x[0:128].reshape(8, 16, GCOLS)
    tail = x[128:144]
    parts = []
    for h in range(GHEADS):
        parts.append((head * mask_ref[h][None]).reshape(128, GCOLS))
    for h in range(GHEADS):
        parts.append(tail * mask_ref[h])
    return jnp.concatenate(parts, 0)


def undiag(xt, m, mask_ref):
    main = []
    for h in range(0, GHEADS, 2):
        r = dot(xt[h * HEAD_DIM : (h + 2) * HEAD_DIM], m[:, h * 128 : (h + 2) * 128])
        main.append(r[0:HEAD_DIM, 0:128])
        main.append(r[HEAD_DIM : 2 * HEAD_DIM, 128:256])
    main = jnp.concatenate(main, 0)
    rest = dot(xt, m[:, GHEADS * 128 :])
    rest_t = rest.T.reshape(GHEADS, 16, GCOLS)
    keep = mask_ref[...].astype(full)
    return jnp.concatenate([main.T, jnp.sum(rest_t * keep, 0)], 0)


def flat(x):
    return x.reshape(x.shape[0] * x.shape[1], x.shape[2])


def blocks(x, owners):
    return x.reshape(owners, x.shape[0] // owners, x.shape[1])


def hidden_place(t, s):
    at = (MLP // GHEADS) * s + 128 * t
    return 8 + at // C, at % C


def unpack_small(small_ref, vec_ref):
    owners = small_ref.shape[0]
    width = C // owners
    count = TAB_ROWS // owners
    vec = jnp.zeros((16, C), full)
    tab = jnp.zeros((HEADS, TAB_LANES), full)
    lane = lax.broadcasted_iota(jnp.int32, (16, 128), 1)
    lane_tab = lax.broadcasted_iota(jnp.int32, (HEADS, 128), 1)
    for s in range(owners):
        piece = small_ref[s].astype(full)
        part = jnp.where(lane < width, piece[0:16], 0.0)
        part = jnp.concatenate([part, jnp.zeros((16, C - 128), full)], 1)
        vec = vec + (pltpu.roll(part, width * s, 1) if s else part)
        part = jnp.where(lane_tab < count, piece[16 : 16 + HEADS], 0.0)
        part = jnp.concatenate([part, jnp.zeros((HEADS, TAB_LANES - 128), full)], 1)
        tab = tab + (pltpu.roll(part, count * s, 1) if s else part)
    vec_ref[...] = vec
    return tab


def pack_small(vec, tab, out_ref):
    owners = out_ref.shape[0]
    width = C // owners
    count = TAB_ROWS // owners
    for s in range(owners):
        out_ref[s, 0:16, :] = (pltpu.roll(vec, C - width * s, 1) if s else vec)[:, 0:128]
        out_ref[s, 16:40, :] = (pltpu.roll(tab, TAB_LANES - count * s, 1) if s else tab)[:, 0:128]


def build_bias(tab, line_ref, tmp_ref, bias_ref):
    def column(cj, carry):
        shifted = pltpu.roll(tab, cj, 1)
        line = dot(shifted.astype(low), line_ref[...])
        for rj in range(WIN):
            cut = (WIN - 1 - rj) * WIN
            part = pltpu.roll(line, LINE - cut, 1) if cut else line
            row = pl.multiple_of((rj * WIN + cj) * HEADS, 8)
            tmp_ref[0, pl.ds(row, HEADS), :] = part[:, 0:128]
            tmp_ref[1, pl.ds(row, HEADS), :] = part[:, 128:256]
        return carry

    lax.fori_loop(0, WIN, column, 0)
    lane = lax.broadcasted_iota(jnp.int32, (TOK, 128), 1)
    for g in range(GROUPS):
        rest = jnp.zeros((TOK, 128), full)
        for h in range(GHEADS):
            at = pl.ds(g * GHEADS + h, TOK, stride=HEADS)
            bias_ref[g, :, h * 128 : (h + 1) * 128] = tmp_ref[0, at, :]
            piece = tmp_ref[1, at, :]
            piece = pltpu.roll(piece, 16 * h, 1) if h else piece
            rest = jnp.where((lane >= 16 * h) & (lane < 16 * h + 16), piece, rest)
        bias_ref[g, :, GHEADS * 128 :] = rest


def table_grad(line_ref, tmp_ref, bias_ref):
    lane = lax.broadcasted_iota(jnp.int32, (TOK, 128), 1)
    for g in range(GROUPS):
        rest = bias_ref[g, :, GHEADS * 128 :]
        for h in range(GHEADS):
            at = pl.ds(g * GHEADS + h, TOK, stride=HEADS)
            tmp_ref[0, at, :] = bias_ref[g, :, h * 128 : (h + 1) * 128]
            piece = pltpu.roll(rest, 128 - 16 * h, 1) if h else rest
            tmp_ref[1, at, :] = jnp.where(lane < 16, piece, 0.0)

    def column(cj, total):
        line = jnp.zeros((HEADS, LINE), full)
        for rj in range(WIN):
            cut = (WIN - 1 - rj) * WIN
            row = pl.multiple_of((rj * WIN + cj) * HEADS, 8)
            part = jnp.concatenate([tmp_ref[0, pl.ds(row, HEADS), :], tmp_ref[1, pl.ds(row, HEADS), :], jnp.zeros((HEADS, 128), full)], 1)
            line = line + (pltpu.roll(part, cut, 1) if cut else part)
        high = line.astype(low)
        rest = (line - high.astype(full)).astype(low)
        spread = dot_nt(high, line_ref[...]) + dot_nt(rest, line_ref[...])
        return total + pltpu.roll(spread, TAB_LANES - cj, 1)

    return lax.fori_loop(0, WIN, column, jnp.zeros((HEADS, TAB_LANES), full))


def transpose_rows(src_ref, dst_ref):
    def block(i, carry):
        at = pl.multiple_of(i * 128, 128)
        dst_ref[:, pl.ds(at, 128)] = src_ref[pl.ds(at, 128), :].T
        return carry

    lax.fori_loop(0, ROWS // 128, block, 0)


def window_rows(w):
    return pl.ds(pl.multiple_of(w * TOK, 16), TOK)


def zero_tail(ref, windows):
    at = windows * TOK
    ref[at:ROWS, :] = jnp.zeros((ROWS - at, ref.shape[1]), ref.dtype)


def attention_forward(windows, x_ref, small_ref, line_ref, mask_ref, wq_ref, wp_ref,
                      qkv_ref, pt_ref, o_ref, x1_ref, n1t_ref, vec_ref, n1_ref, bias_ref, tmp_ref):
    tab = unpack_small(small_ref, vec_ref)
    build_bias(tab, line_ref, tmp_ref, bias_ref)
    zero_tail(n1_ref, windows)
    zero_tail(o_ref, windows)

    def first_norm(w, carry):
        xhat, _ = norm_parts(x_ref[window_rows(w), :].astype(full))
        n1_ref[window_rows(w), :] = (xhat * vec_ref[0:1, :] + vec_ref[1:2, :]).astype(low)
        return carry

    lax.fori_loop(0, windows, first_norm, 0)
    transpose_rows(n1_ref, n1t_ref)

    def group(g, carry):
        cols = pl.ds(pl.multiple_of(g * GCOLS, GCOLS), GCOLS)
        n1 = n1_ref[...]
        qkv_ref[g] = ((dot(n1, flat(wq_ref[g, 0])) + vec_ref[2:3, cols]) * (HEAD_DIM**-0.5)).astype(low)
        qkv_ref[GROUPS + g] = dot(n1, flat(wq_ref[g, 1])).astype(low)
        qkv_ref[2 * GROUPS + g] = (dot(n1, flat(wq_ref[g, 2])) + vec_ref[3:4, cols]).astype(low)

        def window(w, inner):
            rows = window_rows(w)
            q = qkv_ref[g, rows, :]
            k = qkv_ref[GROUPS + g, rows, :]
            v = qkv_ref[2 * GROUPS + g, rows, :]
            s = dot_nt(k, diag(q, mask_ref)) + bias_ref[g]
            e = jnp.exp(s - jnp.max(s, 0, keepdims=True))
            p = (e * (1.0 / jnp.sum(e, 0, keepdims=True))).astype(low)
            pt_ref[g, w] = p
            o_ref[rows, cols] = undiag(v.T, p, mask_ref).astype(low)
            return inner

        lax.fori_loop(0, windows, window, 0)
        return carry

    lax.fori_loop(0, GROUPS, group, 0)

    def output(w, carry):
        rows = window_rows(w)
        branch = dot(o_ref[rows, :], flat(wp_ref[...])) + vec_ref[4:5, :]
        x1_ref[rows, :] = x_ref[rows, :].astype(full) + branch
        return carry

    lax.fori_loop(0, windows, output, 0)


def gelu_both(h):
    c = math.sqrt(2.0 / math.pi)
    square = h * h
    t = jnp.tanh(h * (c + (c * 0.044715) * square))
    half = 0.5 + 0.5 * t
    slope = half + (0.5 * h) * (1.0 - t * t) * (c + (3.0 * c * 0.044715) * square)
    return h * half, slope


def feed_forward(windows, x1_ref, dy_ref, live_ref, vec_ref, up_ref, down_ref, wp_ref, o_ref,
                 out_ref, dx1_ref, do_ref, gup_ref, gdown_ref, gout_ref, sums_ref,
                 n2_ref, n2t_ref, dy2_ref, dyt_ref, y_ref, dn_ref, bu_ref, bsum_ref):
    zero_tail(n2_ref, windows)
    zero_tail(dy2_ref, windows)

    def second_norm(w, carry):
        rows = window_rows(w)
        xhat, _ = norm_parts(x1_ref[rows, :])
        n2_ref[rows, :] = (xhat * vec_ref[5:6, :] + vec_ref[6:7, :]).astype(low)
        dy2_ref[rows, :] = (dy_ref[rows, :].astype(full) * live_ref[w]).astype(low)
        return carry

    lax.fori_loop(0, windows, second_norm, 0)
    transpose_rows(n2_ref, n2t_ref)
    transpose_rows(dy2_ref, dyt_ref)
    y_ref[...] = jnp.zeros_like(y_ref)
    dn_ref[...] = jnp.zeros_like(dn_ref)
    owners = gup_ref.shape[1]
    for t in range(TILES):
        for s in range(TILE // 128):
            row, at = hidden_place(t, s)
            bu_ref[t, :, s * 128 : (s + 1) * 128] = vec_ref[row : row + 1, at : at + 128]

    def step(t, carry):
        for part in range(TILE // SUB):
            cols = slice(part * SUB, (part + 1) * SUB)
            up = flat(up_ref[t, :, :, cols])
            down = flat(down_ref[t, part * SUB // 128 : (part + 1) * SUB // 128])
            h = dot(n2_ref[...], up) + bu_ref[t, :, cols]
            da = dot_nt(dy2_ref[...], down)
            act, slope = gelu_both(h)
            a = act.astype(low)
            dh = (da * slope).astype(low)
            bsum_ref[t, :, cols] = jnp.sum(dh.astype(full), 0, keepdims=True)
            y_ref[...] += dot(a, down)
            dn_ref[...] += dot_nt(dh, up)
            gd = dot(dyt_ref[...], a).astype(low)
            for b in range(SUB // 128):
                gdown_ref[t, part * SUB // 128 + b] = gd[:, b * 128 : (b + 1) * 128]
            gup_ref[t, :, :, cols] = blocks(dot(n2t_ref[...], dh).astype(low), owners)
        return carry

    lax.fori_loop(0, TILES, step, 0)
    sums_ref[...] = jnp.zeros_like(sums_ref)
    for t in range(TILES):
        for s in range(TILE // 128):
            row, at = hidden_place(t, s)
            sums_ref[row : row + 1, at : at + 128] = bsum_ref[t, :, s * 128 : (s + 1) * 128]
    zero_tail(dx1_ref, windows)

    def finish(w, carry):
        rows = window_rows(w)
        x1 = x1_ref[rows, :]
        out_ref[rows, :] = ((x1 + y_ref[rows, :] + vec_ref[7:8, :]) * live_ref[w]).astype(low)
        xhat, scale = norm_parts(x1)
        dn = dn_ref[rows, :]
        dy = dy2_ref[rows, :].astype(full)
        dx1 = dy + norm_back(xhat, scale, dn, vec_ref[5:6, :])
        dx1_ref[rows, :] = dx1
        dr = dx1.astype(low)
        n2_ref[rows, :] = dr
        do_ref[rows, :] = dot_nt(dr, flat(wp_ref[...])).astype(low)
        sums_ref[4:5, :] += jnp.sum(dr.astype(full), 0, keepdims=True)
        sums_ref[5:6, :] += jnp.sum(dn * xhat, 0, keepdims=True)
        sums_ref[6:7, :] += jnp.sum(dn, 0, keepdims=True)
        sums_ref[7:8, :] += jnp.sum(dy, 0, keepdims=True)
        return carry

    lax.fori_loop(0, windows, finish, 0)
    transpose_rows(o_ref, dyt_ref)
    for g in range(GROUPS):
        at = pl.ds(g * GCOLS, GCOLS)
        gout_ref[:, :, at] = blocks(dot(dyt_ref[...], n2_ref[:, at]).astype(low), gout_ref.shape[0])


def attention_backward(windows, x_ref, vec_ref, line_ref, mask_ref, wq_ref, qkv_ref, pt_ref, do_ref, dx1_ref, n1t_ref, sums_in_ref,
                       gq_ref, gsmall_ref, grad_ref, sums_ref, bias_ref, tmp_ref, dproj_ref, dn_ref):
    bias_ref[...] = jnp.zeros_like(bias_ref)
    dn_ref[...] = jnp.zeros_like(dn_ref)
    sums_ref[...] = sums_in_ref[...]
    for part in range(3):
        dproj_ref[part, windows * TOK :, :] = jnp.zeros((ROWS - windows * TOK, GCOLS), low)

    def group(g, carry):
        cols = pl.ds(pl.multiple_of(g * GCOLS, GCOLS), GCOLS)

        def window(w, inner):
            rows = window_rows(w)
            q = qkv_ref[g, rows, :]
            k = qkv_ref[GROUPS + g, rows, :]
            v = qkv_ref[2 * GROUPS + g, rows, :]
            p = pt_ref[g, w]
            do = diag(do_ref[rows, cols], mask_ref)
            dp = dot_nt(v, do)
            dv = dot(p, do)
            pf = p.astype(full)
            ds = (pf * (dp - jnp.sum(pf * dp, 0, keepdims=True))).astype(low)
            bias_ref[g] += ds.astype(full)
            dk = dot(ds, diag(q, mask_ref))
            dq = undiag(k.T, ds, mask_ref) * (HEAD_DIM**-0.5)
            dq = dq.astype(low)
            dv = dv.astype(low)
            dproj_ref[0, rows, :] = dq
            dproj_ref[1, rows, :] = dk.astype(low)
            dproj_ref[2, rows, :] = dv
            sums_ref[2:3, cols] += jnp.sum(dq.astype(full), 0, keepdims=True)
            sums_ref[3:4, cols] += jnp.sum(dv.astype(full), 0, keepdims=True)
            return inner

        lax.fori_loop(0, windows, window, 0)
        for part in range(3):
            d = dproj_ref[part]
            gq_ref[g, part] = blocks(dot(n1t_ref[...], d).astype(low), gq_ref.shape[2])
            dn_ref[...] += dot_nt(d, flat(wq_ref[g, part]))
        return carry

    lax.fori_loop(0, GROUPS, group, 0)

    def finish(w, carry):
        rows = window_rows(w)
        xhat, scale = norm_parts(x_ref[rows, :].astype(full))
        dn = dn_ref[rows, :]
        grad_ref[rows, :] = dx1_ref[rows, :] + norm_back(xhat, scale, dn, vec_ref[0:1, :])
        sums_ref[0:1, :] += jnp.sum(dn * xhat, 0, keepdims=True)
        sums_ref[1:2, :] += jnp.sum(dn, 0, keepdims=True)
        return carry

    lax.fori_loop(0, windows, finish, 0)
    pack_small(sums_ref[...], table_grad(line_ref, tmp_ref, bias_ref), gsmall_ref)


MESH = pl.DeviceIdType.MESH
REPS = 4
OWNERS = 8
LINKS = OWNERS // 2


class Spot:
    def __init__(self):
        self.rep = lax.axis_index("rep")
        self.shard = lax.axis_index("shard")
        self.z = self.shard // 2
        self.core = self.shard % 2

    def sibling(self):
        return (self.rep, self.z * 2 + (1 - self.core))

    def along_z(self, step):
        return (self.rep, ((self.z + step) % LINKS) * 2 + self.core)

    def turned(self, axis):
        x, y = self.rep % 2, self.rep // 2
        return y * 2 + (1 - x) if axis == 0 else (1 - y) * 2 + x

    def beside(self, axis):
        return (self.turned(axis), self.shard)


def greet(spot):
    barrier = pltpu.get_barrier_semaphore()
    peers = [(spot.rep, (spot.shard + i) % OWNERS) for i in range(1, OWNERS)]
    peers += [((spot.rep + i) % REPS, spot.shard) for i in range(1, REPS)]
    for peer in peers:
        pl.semaphore_signal(barrier, inc=1, device_id=peer, device_id_type=MESH)
    return barrier, len(peers)


def send(src, dst, send_sem, recv_sem, peer):
    pltpu.make_async_remote_copy(src_ref=src, dst_ref=dst, send_sem=send_sem, recv_sem=recv_sem, device_id=peer, device_id_type=MESH).start()


def await_bytes(ref, sem):
    pltpu.make_async_copy(ref, ref, sem).wait()


def quarter(ref, rep):
    rows, cols = ref.shape[-2:]
    lead = (slice(None),) * (len(ref.shape) - 2)
    top = pl.multiple_of((rep // 2) * (rows // 2), 16)
    left = pl.multiple_of((rep % 2) * (cols // 2), 128)
    return ref.at[lead + (pl.ds(top, rows // 2), pl.ds(left, cols // 2))]


def half(ref, rep, axis):
    rows, cols = ref.shape[-2:]
    lead = (slice(None),) * (len(ref.shape) - 2)
    if axis == 0:
        left = pl.multiple_of((rep % 2) * (cols // 2), 128)
        return ref.at[lead + (slice(None), pl.ds(left, cols // 2))]
    top = pl.multiple_of((rep // 2) * (rows // 2), 16)
    return ref.at[lead + (pl.ds(top, rows // 2), slice(None))]


class Gather:
    KINDS = (LINKS - 1, LINKS - 1, LINKS - 1, LINKS - 1, LINKS)
    SEMS = 2 * sum(KINDS)

    def __init__(self, spot, place, axis, sems):
        self.spot, self.place, self.axis, self.sems = spot, place, axis, sems

    def sem(self, side, kind, i):
        return self.sems.at[side * (self.SEMS // 2) + sum(self.KINDS[:kind]) + i]

    def block(self, step):
        return self.place(((self.spot.z - step + LINKS) % LINKS) * 2 + self.spot.core)

    def other(self, step):
        return self.place(((self.spot.z - step + LINKS) % LINKS) * 2 + 1 - self.spot.core)

    def start(self):
        spot = self.spot
        mine = self.block(0)
        for i in range(1, LINKS):
            piece = quarter(mine, spot.rep)
            send(piece, piece, self.sem(0, 0, i - 1), self.sem(1, 0, i - 1), spot.along_z(i))
        send(mine, mine, self.sem(0, 4, 0), self.sem(1, 4, 0), spot.sibling())

    def across(self):
        spot = self.spot
        for i in range(1, LINKS):
            piece = quarter(self.block(i), spot.rep)
            await_bytes(piece, self.sem(1, 0, i - 1))
            for axis in (self.axis, 1 - self.axis):
                send(piece, piece, self.sem(0, 1 + axis, i - 1), self.sem(1, 1 + axis, i - 1), spot.beside(axis))

    def relay(self):
        spot = self.spot
        for i in range(1, LINKS):
            piece = quarter(self.block(i), spot.turned(self.axis))
            await_bytes(piece, self.sem(1, 1 + self.axis, i - 1))
            send(piece, piece, self.sem(0, 3, i - 1), self.sem(1, 3, i - 1), spot.beside(1 - self.axis))

    def beside(self):
        spot = self.spot
        for i in range(1, LINKS):
            block = self.block(i)
            piece = quarter(block, spot.rep)
            await_bytes(piece, self.sem(1, 2 - self.axis, i - 1))
            await_bytes(piece, self.sem(1, 3, i - 1))
            send(block, block, self.sem(0, 4, i), self.sem(1, 4, i), spot.sibling())

    def finish(self):
        for i in range(LINKS):
            await_bytes(self.other(i), self.sem(1, 4, i))

    def close(self):
        piece = quarter(self.block(0), self.spot.rep)
        for kind in range(4):
            for i in range(1, LINKS):
                await_bytes(piece, self.sem(0, kind, i - 1))
        for i in range(LINKS):
            await_bytes(self.block(i), self.sem(0, 4, i))


class Reduce:
    KINDS = (LINKS, 1, 1, LINKS - 1, REPS - 1)
    SEMS = 2 * sum(KINDS)
    STAGES = ("first", "second", "along", "spread", "finish")

    def __init__(self, spot, place, out, core_sum, halves, quarters, links, axis, sems):
        self.spot, self.place, self.out, self.axis, self.sems = spot, place, out, axis, sems
        self.core_sum, self.halves, self.quarters, self.links = core_sum, halves, quarters, links

    def sem(self, side, kind, i):
        return self.sems.at[side * (self.SEMS // 2) + sum(self.KINDS[:kind]) + i]

    def start(self):
        spot = self.spot
        for z in range(LINKS):
            send(self.place(z * 2 + (1 - spot.core)), self.core_sum.at[z], self.sem(0, 0, z), self.sem(1, 0, z), spot.sibling())

    def first(self):
        spot = self.spot
        for z in range(LINKS):
            total = self.core_sum.at[z]
            await_bytes(total, self.sem(1, 0, z))
            total[...] = (total[...].astype(full) + self.place(z * 2 + spot.core)[...].astype(full)).astype(low)
        theirs = half(self.core_sum, spot.turned(self.axis), self.axis)
        send(theirs, self.halves, self.sem(0, 1, 0), self.sem(1, 1, 0), spot.beside(self.axis))

    def second(self):
        spot = self.spot
        await_bytes(self.halves, self.sem(1, 1, 0))
        mine = half(self.core_sum, spot.rep, self.axis)
        self.halves[...] = (self.halves[...].astype(full) + mine[...].astype(full)).astype(low)
        theirs = half(self.halves, spot.turned(1 - self.axis), 1 - self.axis)
        send(theirs, self.quarters, self.sem(0, 2, 0), self.sem(1, 2, 0), spot.beside(1 - self.axis))

    def along(self):
        spot = self.spot
        await_bytes(self.quarters, self.sem(1, 2, 0))
        mine = half(self.halves, spot.rep, 1 - self.axis)
        self.quarters[...] = (self.quarters[...].astype(full) + mine[...].astype(full)).astype(low)
        for i in range(1, LINKS):
            send(self.quarters.at[(spot.z + i) % LINKS], self.links.at[i - 1], self.sem(0, 3, i - 1), self.sem(1, 3, i - 1), spot.along_z(i))

    def spread(self):
        spot = self.spot
        total = self.quarters[spot.z].astype(full)
        for i in range(1, LINKS):
            await_bytes(self.links.at[i - 1], self.sem(1, 3, i - 1))
            total = total + self.links[i - 1].astype(full)
        mine = quarter(self.out, spot.rep)
        mine[...] = total.astype(low)
        for j in range(1, REPS):
            send(mine, mine, self.sem(0, 4, j - 1), self.sem(1, 4, j - 1), ((spot.rep + j) % REPS, spot.shard))

    def finish(self):
        for j in range(1, REPS):
            await_bytes(quarter(self.out, (self.spot.rep - j + REPS) % REPS), self.sem(1, 4, j - 1))

    def close(self):
        for z in range(LINKS):
            await_bytes(self.core_sum.at[z], self.sem(0, 0, z))
        await_bytes(self.halves, self.sem(0, 1, 0))
        await_bytes(self.quarters, self.sem(0, 2, 0))
        for i in range(1, LINKS):
            await_bytes(self.links.at[i - 1], self.sem(0, 3, i - 1))
        for j in range(1, REPS):
            await_bytes(quarter(self.out, self.spot.rep), self.sem(0, 4, j - 1))


class ReduceSmall:
    KINDS = (LINKS, LINKS - 1, REPS - 1)
    SEMS = 2 * sum(KINDS)
    STAGES = ("first", "second", "along")

    def __init__(self, spot, terms, out, core_sum, links, parts, sems):
        self.spot, self.terms, self.out, self.core_sum, self.links, self.parts, self.sems = spot, terms, out, core_sum, links, parts, sems

    sem = Reduce.sem

    def start(self):
        spot = self.spot
        for z in range(LINKS):
            send(self.terms.at[z * 2 + (1 - spot.core)], self.core_sum.at[z], self.sem(0, 0, z), self.sem(1, 0, z), spot.sibling())

    def first(self):
        spot = self.spot
        for z in range(LINKS):
            await_bytes(self.core_sum.at[z], self.sem(1, 0, z))
            self.core_sum[z] = self.core_sum[z] + self.terms[z * 2 + spot.core]
        for i in range(1, LINKS):
            send(self.core_sum.at[(spot.z + i) % LINKS], self.links.at[i - 1], self.sem(0, 1, i - 1), self.sem(1, 1, i - 1), spot.along_z(i))

    def second(self):
        spot = self.spot
        total = self.core_sum[spot.z]
        for i in range(1, LINKS):
            await_bytes(self.links.at[i - 1], self.sem(1, 1, i - 1))
            total = total + self.links[i - 1]
        self.parts[spot.rep] = total
        mine = self.parts.at[spot.rep]
        for j in range(1, REPS):
            send(mine, mine, self.sem(0, 2, j - 1), self.sem(1, 2, j - 1), ((spot.rep + j) % REPS, spot.shard))

    def along(self):
        for j in range(1, REPS):
            await_bytes(self.parts.at[(self.spot.rep - j + REPS) % REPS], self.sem(1, 2, j - 1))
        total = self.parts[0]
        for j in range(1, REPS):
            total = total + self.parts[j]
        self.out[...] = total

    def close(self):
        for z in range(LINKS):
            await_bytes(self.core_sum.at[z], self.sem(0, 0, z))
        for i in range(1, LINKS):
            await_bytes(self.links.at[i - 1], self.sem(0, 1, i - 1))
        for j in range(1, REPS):
            await_bytes(self.parts.at[self.spot.rep], self.sem(0, 2, j - 1))


OWNED = C // OWNERS
SLOTS = TILES + 1
CHUNKS = 2 * TILES + 1 + GROUPS


def chunk_shapes():
    out = []
    for _ in range(TILES):
        out += [(128, C), (OWNED, TILE)]
    return out + [(OWNED, C)] + [(3, OWNED, GCOLS)] * GROUPS


def reduce_scratch():
    out = []
    for i, dims in enumerate(chunk_shapes()):
        *lead, rows, cols = dims
        near = (rows, cols // 2) if i % 2 == 0 else (rows // 2, cols)
        out.append(pltpu.VMEM((LINKS, *dims), low))
        out.append(pltpu.VMEM((LINKS, *lead, *near), low))
        out.append(pltpu.VMEM((LINKS, *lead, rows // 2, cols // 2), low))
        out.append(pltpu.VMEM((LINKS - 1, *lead, rows // 2, cols // 2), low))
    out += [pltpu.VMEM((LINKS, 40, 128), full), pltpu.VMEM((LINKS - 1, 40, 128), full), pltpu.VMEM((REPS, 40, 128), full)]
    return out


def layer_kernel(windows, x_hbm, dy_hbm, live_ref, q32, p32, u32, d32, vec_in, tab_in, line_ref, mask_ref,
                 out_hbm, grad_hbm, gq_out, gp_out, gu_out, gd_out, gs_out, qkv_hbm, pt_hbm, n1t_hbm, *scratch):
    wq, wp, up, down, small, o_ref, x1_ref, vec_ref, sums_ref, terms_ref = scratch[:10]
    gather_sems, reduce_sems, small_sems, small_reduce_sems, local = scratch[-5:]
    reduce_refs = scratch[10:-5]
    spot = Spot()
    rows_all = windows * TOK
    mine = spot.shard
    V = pltpu.VMEM

    gathers = {}
    for i, (name, place) in enumerate(
        [(f"q{g}", lambda s, g=g: wq.at[g, :, s]) for g in range(GROUPS)]
        + [("p", lambda s: wp.at[s])]
        + [item for t in range(TILES) for item in ((f"u{t}", lambda s, t=t: up.at[t, s]), (f"d{t}", lambda s, t=t: down.at[t, s]))]
    ):
        gathers[name] = Gather(spot, place, i % 2, gather_sems.at[i])
    reduces = {}
    targets = []
    for t in range(TILES):
        slot = (t + SLOTS - 1) % SLOTS
        targets.append((f"d{t}", lambda s, slot=slot: down.at[slot, s], gd_out.at[t]))
        targets.append((f"u{t}", lambda s, slot=slot: up.at[slot, s], gu_out.at[t]))
    targets.append(("p", lambda s: wp.at[s], gp_out))
    for g in range(GROUPS):
        targets.append((f"q{g}", lambda s, g=g: wq.at[g, :, s], gq_out.at[g]))
    for i, (name, place, out) in enumerate(targets):
        reduces[name] = Reduce(spot, place, out, *reduce_refs[4 * i : 4 * i + 4], i % 2, reduce_sems.at[i])
    reduces["s"] = ReduceSmall(spot, terms_ref, gs_out, *reduce_refs[-3:], small_reduce_sems)

    def at(kind, names, stage):
        for name in names.split():
            getattr((gathers if kind == "g" else reduces)[name], stage)()

    barrier, peers = greet(spot)

    def cast(q_v, p_v, u_v, d_v):
        loads = [pltpu.make_async_copy(a, b, local.at[i]) for i, (a, b) in enumerate(((q32, q_v), (p32, p_v), (u32, u_v), (d32, d_v)))]
        for load in loads:
            load.start()
        small[mine] = jnp.zeros((48, 128), low)
        pad = jnp.zeros((16, 128), full)
        vec_ref[:, 0:128] = pad
        vec_ref[0:12, 0:OWNED] = vec_in[...]
        small[mine, 0:16, :] = vec_ref[:, 0:128].astype(low)
        x1_ref[0:128, 0:128] = jnp.zeros((128, 128), full)
        x1_ref[0 : tab_in.shape[0], 0:HEADS] = tab_in[...]
        small[mine, 16:48, :] = x1_ref[0:128, 0:128].T[0:32].astype(low)
        loads[0].wait()
        for g in range(GROUPS):
            for part in range(3):
                wq[g, part, mine] = q_v[:, part * C + g * GCOLS : part * C + (g + 1) * GCOLS].astype(low)
        pl.semaphore_wait(barrier, peers)
        for i in range(1, OWNERS):
            send(small.at[mine], small.at[mine], small_sems.at[i], small_sems.at[OWNERS + i], (spot.rep, (mine + i) % OWNERS))
        at("g", "q0 q1 q2", "start")
        loads[1].wait()
        wp[mine] = p_v[...].astype(low)
        at("g", "p", "start")
        loads[2].wait()
        loads[3].wait()
        for t in range(TILES):
            for s in range(OWNERS):
                src = (MLP // OWNERS) * s + 128 * t
                up[t, mine, :, s * 128 : (s + 1) * 128] = u_v[:, src : src + 128].astype(low)
            down[t, mine] = d_v[t * 128 : (t + 1) * 128, :].astype(low)
            at("g", f"u{t} d{t}", "start")

    pl.run_scoped(cast, V((OWNED, 3 * C), full), V((OWNED, C), full), V((OWNED, MLP), full), V((TILES * 128, C), full))

    def forward(x_ref, n1_ref, n1t_ref, qkv_ref, pt_ref, bias_ref):
        load = pltpu.make_async_copy(x_hbm, x_ref, local.at[0])
        load.start()
        zero_tail(n1_ref, windows)
        zero_tail(o_ref, windows)
        for i in range(1, OWNERS):
            await_bytes(small.at[(mine - i + OWNERS) % OWNERS], small_sems.at[OWNERS + i])
        tab = unpack_small(small, vec_ref)
        at("g", "q0", "across")
        load.wait()

        def first_norm(w, carry):
            xhat, _ = norm_parts(x_ref[window_rows(w), :].astype(full))
            n1_ref[window_rows(w), :] = (xhat * vec_ref[0:1, :] + vec_ref[1:2, :]).astype(low)
            return carry

        lax.fori_loop(0, windows, first_norm, 0)
        at("g", "q0", "relay")
        at("g", "q1", "across")
        transpose_rows(n1_ref, n1t_ref)
        save = pltpu.make_async_copy(n1t_ref, n1t_hbm, local.at[1])
        save.start()
        at("g", "q0", "beside")
        at("g", "q1", "relay")
        at("g", "q2", "across")
        pl.run_scoped(functools.partial(build_bias, tab, line_ref, bias_ref=bias_ref), V((2, TOK * HEADS, 128), full))
        at("g", "q1", "beside")
        at("g", "q2", "relay")
        at("g", "p", "across")
        at("g", "q0", "finish")
        hooks = {
            (0, 1): [("p", "relay"), ("q2", "beside")],
            (0, 2): [("u0", "across"), ("p", "beside")],
            (0, 4): [("d0", "across"), ("u0", "relay")],
            (0, 6): [("d0", "relay"), ("q1", "finish")],
            (1, 1): [("u0", "beside"), ("u1", "across")],
            (1, 3): [("d0", "beside"), ("d1", "across"), ("u1", "relay")],
            (1, 6): [("d1", "relay"), ("q2", "finish")],
            (2, 2): [("u2", "across"), ("u1", "beside")],
            (2, 4): [("d2", "across"), ("d1", "beside")],
            (2, 6): [("u2", "relay"), ("p", "finish")],
        }
        for g in range(GROUPS):
            cols = slice(g * GCOLS, (g + 1) * GCOLS)
            held = qkv_ref.at[g % 2]
            if g >= 2:
                pltpu.make_async_copy(held, qkv_hbm.at[g - 2], local.at[2 + g % 2]).wait()
            n1 = n1_ref[...]
            held[0] = ((dot(n1, flat(wq[g, 0])) + vec_ref[2:3, cols]) * (HEAD_DIM**-0.5)).astype(low)
            held[1] = dot(n1, flat(wq[g, 1])).astype(low)
            held[2] = (dot(n1, flat(wq[g, 2])) + vec_ref[3:4, cols]).astype(low)
            pltpu.make_async_copy(held, qkv_hbm.at[g], local.at[2 + g % 2]).start()

            def window(w, carry, g=g, cols=cols, held=held):
                for (hg, hw), steps in hooks.items():
                    if hg == g:

                        @pl.when(w == hw)
                        def _(steps=steps):
                            for name, stage in steps:
                                at("g", name, stage)

                rows = window_rows(w)
                n = g * windows + w
                slot = n % 2
                s = dot_nt(held[1, rows, :], diag(held[0, rows, :], mask_ref)) + bias_ref[g]
                e = jnp.exp(s - jnp.max(s, 0, keepdims=True))
                p = (e * (1.0 / jnp.sum(e, 0, keepdims=True))).astype(low)
                keep = pltpu.make_async_copy(pt_ref.at[slot], pt_hbm.at[n], local.at[4 + slot])

                @pl.when(n >= 2)
                def _():
                    keep.wait()

                pt_ref[slot] = p
                keep.start()
                o_ref[rows, cols] = undiag(held[2, rows, :].T, p, mask_ref).astype(low)
                return carry

            lax.fori_loop(0, windows, window, 0)

        def output(w, carry):
            rows = window_rows(w)
            x1_ref[rows, :] = x_ref[rows, :].astype(full) + (dot(o_ref[rows, :], flat(wp[...])) + vec_ref[4:5, :])
            return carry

        lax.fori_loop(0, windows, output, 0)
        save.wait()
        for g in (GROUPS - 2, GROUPS - 1):
            pltpu.make_async_copy(qkv_ref.at[g % 2], qkv_hbm.at[g], local.at[2 + g % 2]).wait()
        for slot in range(2):
            pltpu.make_async_copy(pt_ref.at[slot], pt_hbm.at[0], local.at[4 + slot]).wait()

    pl.run_scoped(forward, V((rows_all, C), low), V((ROWS, C), low), V((C, ROWS), low), V((2, 3, ROWS, GCOLS), low), V((2, TOK, PACK), low),
                  V((GROUPS, TOK, PACK), full))

    def middle(n2_ref, n2t_ref, dy_ref, dyt_ref, y_ref, dn_ref, bu_ref, bsum_ref):
        load = pltpu.make_async_copy(dy_hbm, dy_ref.at[0:rows_all], local.at[0])
        load.start()
        zero_tail(n2_ref, windows)
        zero_tail(dy_ref, windows)
        at("g", "d2", "relay")
        load.wait()

        def second_norm(w, carry):
            rows = window_rows(w)
            xhat, _ = norm_parts(x1_ref[rows, :])
            n2_ref[rows, :] = (xhat * vec_ref[5:6, :] + vec_ref[6:7, :]).astype(low)
            dy_ref[rows, :] = (dy_ref[rows, :].astype(full) * live_ref[w]).astype(low)
            return carry

        lax.fori_loop(0, windows, second_norm, 0)
        transpose_rows(n2_ref, n2t_ref)
        transpose_rows(dy_ref, dyt_ref)
        y_ref[...] = jnp.zeros_like(y_ref)
        dn_ref[...] = jnp.zeros_like(dn_ref)
        for t in range(TILES):
            for s in range(TILE // 128):
                row, left = hidden_place(t, s)
                bu_ref[t, :, s * 128 : (s + 1) * 128] = vec_ref[row : row + 1, left : left + 128]
        at("g", "u0 d0", "finish")
        halves = TILE // SUB
        before = {
            1: [("g", "u2", "beside")],
            2: [("g", "d2", "beside"), ("g", "u1 d1", "finish"), ("g", "u0 d0", "close"), ("r", "d0 u0", "start")],
            3: [("r", "d0 u0", "first")],
            4: [("g", "u2 d2", "finish"), ("g", "u1 d1", "close"), ("r", "d1 u1", "start"), ("r", "d0 u0", "second")],
            5: [("r", "d1 u1", "first"), ("r", "d0 u0", "along")],
        }

        def step(i, carry):
            for k, steps in before.items():

                @pl.when(i == k)
                def _(steps=steps):
                    for item in steps:
                        at(*item)

            t, part = i // halves, i % halves
            cols = pl.ds(pl.multiple_of(part * SUB, SUB), SUB)
            wide = SUB // 128
            slot = (t + SLOTS - 1) % SLOTS
            u = flat(up[t, :, :, cols])
            d = flat(down[t, pl.ds(part * wide, wide)])
            h = dot(n2_ref[...], u) + bu_ref[t, :, cols]
            da = dot_nt(dy_ref[...], d)
            act, slope = gelu_both(h)
            a = act.astype(low)
            dh = (da * slope).astype(low)
            bsum_ref[t, :, cols] = jnp.sum(dh.astype(full), 0, keepdims=True)
            y_ref[...] += dot(a, d)
            dn_ref[...] += dot_nt(dh, u)
            gd = dot(dyt_ref[...], a).astype(low)
            down[slot, pl.ds(part * wide, wide)] = blocks(gd.T, wide)
            up[slot, :, :, cols] = blocks(dot(n2t_ref[...], dh).astype(low), OWNERS)
            return carry

        lax.fori_loop(0, TILES * halves, step, 0)
        at("r", "d2 u2", "start")
        at("r", "d1 u1", "second")
        sums_ref[...] = jnp.zeros_like(sums_ref)
        for t in range(TILES):
            for s in range(TILE // 128):
                row, left = hidden_place(t, s)
                sums_ref[row : row + 1, left : left + 128] = bsum_ref[t, :, s * 128 : (s + 1) * 128]
        transpose_rows(o_ref, dyt_ref)
        at("r", "d0 u0", "spread")
        at("r", "d2 u2", "first")

        def finish(w, carry):
            rows = window_rows(w)
            x1 = x1_ref[rows, :]
            xhat, scale = norm_parts(x1)
            dn = dn_ref[rows, :]
            dy = dy_ref[rows, :].astype(full)
            dx1 = dy + norm_back(xhat, scale, dn, vec_ref[5:6, :])
            dr = dx1.astype(low)
            sums_ref[4:5, :] += jnp.sum(dr.astype(full), 0, keepdims=True)
            sums_ref[5:6, :] += jnp.sum(dn * xhat, 0, keepdims=True)
            sums_ref[6:7, :] += jnp.sum(dn, 0, keepdims=True)
            sums_ref[7:8, :] += jnp.sum(dy, 0, keepdims=True)
            dy_ref[rows, :] = ((x1 + y_ref[rows, :] + vec_ref[7:8, :]) * live_ref[w]).astype(low)
            x1_ref[rows, :] = dx1
            n2_ref[rows, :] = dr
            o_ref[rows, :] = dot_nt(dr, flat(wp[...])).astype(low)
            return carry

        lax.fori_loop(0, windows, finish, 0)
        save = pltpu.make_async_copy(dy_ref.at[0:rows_all], out_hbm, local.at[0])
        save.start()
        at("r", "d1 u1", "along")
        at("g", "p", "close")
        for g in range(GROUPS):
            cols = slice(g * GCOLS, (g + 1) * GCOLS)
            wp[:, :, cols] = blocks(dot(dyt_ref[...], n2_ref[:, cols]).astype(low), OWNERS)
        at("r", "p", "start")
        at("r", "d2 u2", "second")
        save.wait()

    pl.run_scoped(middle, V((ROWS, C), low), V((C, ROWS), low), V((ROWS, C), low), V((C, ROWS), low), V((ROWS, C), full), V((ROWS, C), full),
                  V((TILES, 1, TILE), full), V((TILES, 1, TILE), full))

    def backward(x_ref, n1t_ref, qkv_ref, pt_ref, dproj_ref, dn_ref, bias_ref):
        loads = [pltpu.make_async_copy(x_hbm, x_ref, local.at[0]), pltpu.make_async_copy(n1t_hbm, n1t_ref, local.at[1])]
        fetch = [pltpu.make_async_copy(qkv_hbm.at[g], qkv_ref.at[g % 2], local.at[2 + g % 2]) for g in range(GROUPS)]
        fetch[0].start()
        pltpu.make_async_copy(pt_hbm.at[0], pt_ref.at[0], local.at[4]).start()
        fetch[1].start()
        for load in loads:
            load.start()
        bias_ref[...] = jnp.zeros_like(bias_ref)
        dn_ref[...] = jnp.zeros_like(dn_ref)
        for part in range(3):
            dproj_ref[part, rows_all:, :] = jnp.zeros((ROWS - rows_all, GCOLS), low)
        hooks = {
            (0, 1): [("d1 u1", "spread"), ("p", "first")],
            (0, 3): [("d2 u2", "along"), ("p", "second")],
            (0, 5): [("d0 u0", "finish"), ("p", "along")],
            (1, 0): [("d2 u2", "spread")],
            (1, 1): [("q0", "first"), ("p", "spread")],
            (1, 3): [("q0", "second"), ("d1 u1", "finish")],
            (1, 5): [("q0", "along")],
            (2, 1): [("q1", "first"), ("q0", "spread")],
            (2, 3): [("q1", "second"), ("d2 u2", "finish")],
            (2, 5): [("q1", "along"), ("p", "finish")],
        }
        for g in range(GROUPS):
            cols = slice(g * GCOLS, (g + 1) * GCOLS)
            held = qkv_ref.at[g % 2]
            fetch[g].wait()

            def window(w, carry, g=g, cols=cols, held=held):
                for (hg, hw), steps in hooks.items():
                    if hg == g:

                        @pl.when(w == hw)
                        def _(steps=steps):
                            for names, stage in steps:
                                at("r", names, stage)

                rows = window_rows(w)
                n = g * windows + w
                slot = n % 2

                @pl.when(n + 1 < GROUPS * windows)
                def _():
                    pltpu.make_async_copy(pt_hbm.at[n + 1], pt_ref.at[1 - slot], local.at[5 - slot]).start()

                pltpu.make_async_copy(pt_hbm.at[n], pt_ref.at[slot], local.at[4 + slot]).wait()
                q = held[0, rows, :]
                k = held[1, rows, :]
                v = held[2, rows, :]
                p = pt_ref[slot]
                do = diag(o_ref[rows, cols], mask_ref)
                dp = dot_nt(v, do)
                dv = dot(p, do).astype(low)
                pf = p.astype(full)
                ds = (pf * (dp - jnp.sum(pf * dp, 0, keepdims=True))).astype(low)
                bias_ref[g] += ds.astype(full)
                dproj_ref[1, rows, :] = dot(ds, diag(q, mask_ref)).astype(low)
                dq = (undiag(k.T, ds, mask_ref) * (HEAD_DIM**-0.5)).astype(low)
                dproj_ref[0, rows, :] = dq
                dproj_ref[2, rows, :] = dv
                sums_ref[2:3, cols] += jnp.sum(dq.astype(full), 0, keepdims=True)
                sums_ref[3:4, cols] += jnp.sum(dv.astype(full), 0, keepdims=True)
                return carry

            lax.fori_loop(0, windows, window, 0)
            if g + 2 < GROUPS:
                fetch[g + 2].start()
            if g == 0:
                for load in loads:
                    load.wait()
            at("g", f"q{g}", "close")
            for part in range(3):
                d = dproj_ref[part]
                dn_ref[...] += dot_nt(d, flat(wq[g, part]))
                wq[g, part] = blocks(dot(n1t_ref[...], d).astype(low), OWNERS)
            at("r", f"q{g}", "start")

        def last_norm(grad_ref):
            def finish(w, carry):
                rows = window_rows(w)
                slot = w % 2
                xhat, scale = norm_parts(x_ref[rows, :].astype(full))
                dn = dn_ref[rows, :]
                save = pltpu.make_async_copy(grad_ref.at[slot], grad_hbm.at[rows], local.at[4 + slot])

                @pl.when(w >= 2)
                def _():
                    save.wait()

                grad_ref[slot] = x1_ref[rows, :] + norm_back(xhat, scale, dn, vec_ref[0:1, :])
                save.start()
                sums_ref[0:1, :] += jnp.sum(dn * xhat, 0, keepdims=True)
                sums_ref[1:2, :] += jnp.sum(dn, 0, keepdims=True)
                return carry

            lax.fori_loop(0, windows, finish, 0)
            for slot in range(2):
                pltpu.make_async_copy(grad_ref.at[slot], grad_hbm.at[pl.ds(0, TOK)], local.at[4 + slot]).wait()

        pl.run_scoped(last_norm, V((2, TOK, C), full))
        at("r", "q2", "first")
        at("r", "q1", "spread")

        def table(tmp_ref):
            pack_small(sums_ref[...], table_grad(line_ref, tmp_ref, bias_ref), terms_ref)

        pl.run_scoped(table, V((2, TOK * HEADS, 128), full))
        at("r", "q2", "second")
        at("r", "s", "start")
        at("r", "q0", "finish")
        at("r", "s", "first")
        at("r", "q2", "along")
        at("r", "s", "second")
        at("r", "q1", "finish")
        at("r", "s", "along")
        at("r", "q2", "spread")
        at("r", "q2", "finish")

    pl.run_scoped(backward, V((rows_all, C), low), V((C, ROWS), low), V((2, 3, ROWS, GCOLS), low), V((2, TOK, PACK), low), V((3, ROWS, GCOLS), low),
                  V((ROWS, C), full), V((GROUPS, TOK, PACK), full))
    at("g", "u2 d2", "close")
    for i in range(1, OWNERS):
        await_bytes(small.at[mine], small_sems.at[i])
    for job in reduces.values():
        job.close()


def shape(dims, kind):
    return jax.ShapeDtypeStruct(dims, kind)


def adamw(weight, moment, second, gradient, step_rate):
    moment_new = beta_one * moment + (1.0 - beta_one) * gradient
    second_new = beta_two * second + (1.0 - beta_two) * gradient * gradient
    update = (
        moment_new
        / (1.0 - beta_one**STEP)
        / (jnp.sqrt(second_new / (1.0 - beta_two**STEP)) + adam_eps)
    )
    weight_new = weight * (1.0 - step_rate * weight_decay) - step_rate * update
    return (weight_new, moment_new, second_new)


def update_kernel(*refs):
    gq, gp, gu, gd, gs = refs[:5]
    ins = [refs[5 + 3 * i : 8 + 3 * i] for i in range(6)]
    outs = [refs[23 + 4 * i : 27 + 4 * i] for i in range(4)] + [refs[39:42], refs[42:45]]

    def piece(which, place, gradient):
        new = adamw(*(ref[place] for ref in ins[which]), gradient, step_rates[which])
        for ref, value in zip(outs[which], new):
            ref[place] = value
        if which < 4:
            outs[which][3][place] = new[0].astype(low)

    for part in range(3):
        for g in range(GROUPS):
            left = part * C + g * GCOLS
            piece(0, (slice(None), slice(left, left + GCOLS)), gq[g, part].astype(full))
    piece(1, (slice(None), slice(None)), gp[...].astype(full))
    for t in range(TILES):
        for s in range(OWNERS):
            left = (MLP // OWNERS) * s + 128 * t
            piece(2, (slice(None), slice(left, left + 128)), gu[t, :, s * 128 : (s + 1) * 128].astype(full))
    piece(3, (slice(None), slice(None)), gd[0].astype(full))

    @pl.when(pl.program_id(0) == 0)
    def _():
        every = (slice(None), slice(None))
        piece(4, every, gs[0:12, 0:OWNED])
        turned = jnp.concatenate([gs[16:40, :], jnp.zeros((104, 128), full)], 0).T
        piece(5, every, turned[0 : ins[5][0].shape[0], 0:HEADS])


def update(gq, gp, gu, gd, gs, states):
    steps = OWNED // 16

    def rows_of(array):
        tall = array.shape[0] // steps
        return pl.BlockSpec((tall, array.shape[1]), lambda i: (i, 0))

    def whole(array):
        return pl.BlockSpec(array.shape, lambda i: (0, 0))

    per_tile = 128 * TILES // steps
    specs = [
        pl.BlockSpec((GROUPS, 3, 16, GCOLS), lambda i: (0, 0, i, 0)),
        pl.BlockSpec((16, C), lambda i: (i, 0)),
        pl.BlockSpec((TILES, 16, TILE), lambda i: (0, i, 0)),
        pl.BlockSpec((1, per_tile, C), lambda i: (i // (128 // per_tile), i % (128 // per_tile), 0)),
        whole(gs),
    ]
    out_shapes, out_specs = [], []
    for i, group in enumerate(states):
        for array in group:
            specs.append(rows_of(array) if i < 4 else whole(array))
            out_shapes.append(shape(array.shape, full))
            out_specs.append(specs[-1])
        if i < 4:
            out_shapes.append(shape(group[0].shape, low))
            out_specs.append(rows_of(group[0]))
    return pl.pallas_call(
        update_kernel,
        grid=(steps,),
        in_specs=specs,
        out_specs=out_specs,
        out_shape=out_shapes,
        compiler_params=pltpu.CompilerParams(vmem_limit_bytes=40 * MIB),
        name="update",
    )(gq, gp, gu, gd, gs, *[array for group in states for array in group])


def shards(
    tokens, out_grad, window_count,
    qkv_weight, qkv_first, qkv_second,
    output_weight, output_first, output_second,
    up_weight, up_first, up_second,
    down_weight, down_first, down_second,
    vectors, vector_first, vector_second,
    bias_table, table_first, table_second,
):
    windows = tokens.shape[0]
    rows = windows * TOK
    V = pltpu.VMEM
    D = pltpu.SemaphoreType.DMA
    live = (jnp.arange(windows) < window_count[0]).astype(full)
    hbm = pl.BlockSpec(memory_space=pl.ANY)
    vmem = pl.BlockSpec(memory_space=pltpu.VMEM)
    result = pl.pallas_call(
        functools.partial(layer_kernel, windows),
        out_shape=[
            shape((rows, C), low), shape((rows, C), full),
            shape((GROUPS, 3, OWNED, GCOLS), low), shape((OWNED, C), low), shape((TILES, OWNED, TILE), low), shape((TILES, 128, C), low),
            shape((40, 128), full),
            shape((GROUPS, 3, ROWS, GCOLS), low), shape((GROUPS * windows, TOK, PACK), low), shape((C, ROWS), low)],
        in_specs=[hbm, hbm, pl.BlockSpec(memory_space=pltpu.SMEM)] + [hbm] * 4 + [vmem] * 4,
        out_specs=[hbm, hbm] + [vmem] * 5 + [hbm] * 3,
        scratch_shapes=[
            V((GROUPS, 3, OWNERS, OWNED, GCOLS), low), V((OWNERS, OWNED, C), low), V((SLOTS, OWNERS, OWNED, TILE), low),
            V((SLOTS, OWNERS, 128, C), low), V((OWNERS, 48, 128), low), V((ROWS, C), low), V((rows, C), full), V((16, C), full), V((16, C), full),
            V((OWNERS, 40, 128), full)]
        + reduce_scratch()
        + [D((CHUNKS, Gather.SEMS)), D((CHUNKS, Reduce.SEMS)), D((2 * OWNERS,)), D((ReduceSmall.SEMS,)), D((6,))],
        compiler_params=pltpu.CompilerParams(vmem_limit_bytes=63 * MIB, collective_id=0, has_side_effects=True),
        name="layer",
    )(tokens.reshape(rows, C), out_grad.reshape(rows, C), live, qkv_weight, output_weight, up_weight, down_weight, vectors, bias_table,
      jnp.asarray(line_matrix(), low), jnp.asarray(head_masks(), low))
    out, grad, gq, gp, gu, gd, gs = result[:7]
    new = update(gq, gp, gu, gd, gs, (
        (qkv_weight, qkv_first, qkv_second), (output_weight, output_first, output_second), (up_weight, up_first, up_second),
        (down_weight, down_first, down_second), (vectors, vector_first, vector_second), (bias_table, table_first, table_second)))
    return (out.reshape(tokens.shape), grad.reshape(tokens.shape), *new)


def vmem_call(body, outs, scratch, args, name, limit=60, **params):
    spec = pl.BlockSpec(memory_space=pltpu.VMEM)
    return pl.pallas_call(
        body,
        out_shape=outs,
        in_specs=[pl.BlockSpec(memory_space=pltpu.SMEM) if a.dtype == full and a.ndim == 1 else spec for a in args],
        out_specs=[spec] * len(outs),
        scratch_shapes=scratch,
        compiler_params=pltpu.CompilerParams(vmem_limit_bytes=limit * MIB, **params),
        name=name,
    )(*args)


def local_step(tokens, out_grad, window_count, small, wq, wp, up, down):
    windows = tokens.shape[0]
    rows = windows * TOK
    owned = C // OWNERS
    V = pltpu.VMEM
    x = tokens.reshape(rows, C)
    dy = out_grad.reshape(rows, C)
    live = (jnp.arange(windows) < window_count[0]).astype(full)
    line = jnp.asarray(line_matrix(), low)
    masks = jnp.asarray(head_masks(), low)
    qkv, pt, o, x1, n1t, vec = vmem_call(
        functools.partial(attention_forward, windows),
        [shape((9, ROWS, GCOLS), low), shape((GROUPS, windows, TOK, PACK), low), shape((ROWS, C), low), shape((rows, C), full), shape((C, ROWS), low),
         shape((16, C), full)],
        [V((ROWS, C), low), V((GROUPS, TOK, PACK), full), V((2, TOK * HEADS, 128), full)],
        (x, small, line, masks, wq, wp), "attention_forward")
    out, dx1, do, gup, gdown, gout, sums = vmem_call(
        functools.partial(feed_forward, windows),
        [shape((rows, C), low), shape((ROWS, C), full), shape((rows, C), low), shape((TILES, OWNERS, owned, TILE), low),
         shape((TILES, OWNERS, C, 128), low), shape((OWNERS, owned, C), low), shape((16, C), full)],
        [V((ROWS, C), low), V((C, ROWS), low), V((ROWS, C), low), V((C, ROWS), low), V((ROWS, C), full), V((ROWS, C), full),
         V((TILES, 1, TILE), full), V((TILES, 1, TILE), full)],
        (x1, dy, live, vec, up, down, wp, o), "feed_forward")
    gq, gsmall, grad = vmem_call(
        functools.partial(attention_backward, windows),
        [shape((GROUPS, 3, OWNERS, owned, GCOLS), low), shape((OWNERS, 40, 128), full), shape((rows, C), full)],
        [V((16, C), full), V((GROUPS, TOK, PACK), full), V((2, TOK * HEADS, 128), full), V((3, ROWS, GCOLS), low), V((ROWS, C), full)],
        (x, vec, line, masks, wq, qkv, pt, do, dx1, n1t, sums), "attention_backward")
    return out.reshape(tokens.shape), grad.reshape(tokens.shape), gq, gout, gup, gdown, gsmall


def shards_general(
    tokens, out_grad, window_count,
    qkv_weight, qkv_first, qkv_second,
    output_weight, output_first, output_second,
    up_weight, up_first, up_second,
    down_weight, down_first, down_second,
    vectors, vector_first, vector_second,
    bias_table, table_first, table_second,
):
    gather = functools.partial(lax.all_gather, axis_name="shard", tiled=True)
    scatter = functools.partial(lax.psum_scatter, axis_name="shard", tiled=True)
    owned = C // OWNERS
    wq = gather(qkv_weight.astype(low), axis=0).reshape(OWNERS, owned, 3, GROUPS, GCOLS).transpose(3, 2, 0, 1, 4)
    wp = gather(output_weight.astype(low), axis=0).reshape(OWNERS, owned, C)
    up = gather(up_weight.astype(low), axis=0).reshape(OWNERS, owned, OWNERS, TILES, 128).transpose(3, 0, 1, 2, 4)
    up = up.reshape(TILES, OWNERS, owned, TILE)
    down = gather(down_weight.astype(low), axis=0).reshape(OWNERS, TILES, 128, C).transpose(1, 0, 2, 3)
    vec = gather(vectors.astype(low), axis=1)
    tab = gather(bias_table.astype(low), axis=0)
    table_rows = tab.shape[0]
    count = TAB_ROWS // OWNERS
    vec = vec.reshape(12, OWNERS, owned).transpose(1, 0, 2)
    tab = tab[:TAB_ROWS].reshape(OWNERS, count, HEADS).transpose(0, 2, 1)
    small = jnp.concatenate([jnp.pad(vec, ((0, 0), (0, 4), (0, 128 - owned))), jnp.pad(tab, ((0, 0), (0, 8), (0, 128 - count)))], 1)
    out, grad, gq, gp, gu, gd, gs = local_step(tokens, out_grad, window_count, small, wq, wp, up, down)
    gq = gq.astype(full).transpose(2, 3, 1, 0, 4).reshape(C, 3 * C)
    gu = gu.astype(full).reshape(TILES, C, OWNERS, 128).transpose(1, 2, 0, 3).reshape(C, MLP)
    gd = gd.astype(full).transpose(1, 0, 3, 2).reshape(MLP, C)
    gv = gs[:, :12, :owned].transpose(1, 0, 2).reshape(12, C)
    gb = gs[:, 16:40, :count].transpose(0, 2, 1).reshape(TAB_ROWS, HEADS)
    gb = jnp.pad(gb, ((0, table_rows - TAB_ROWS), (0, 0)))
    totals = lax.psum(
        (scatter(gq, scatter_dimension=0), scatter(gp.astype(full).reshape(C, C), scatter_dimension=0), scatter(gu, scatter_dimension=0),
         scatter(gd, scatter_dimension=0), scatter(gv, scatter_dimension=1), scatter(gb, scatter_dimension=0)), "rep")
    states = (
        (qkv_weight, qkv_first, qkv_second), (output_weight, output_first, output_second), (up_weight, up_first, up_second),
        (down_weight, down_first, down_second), (vectors, vector_first, vector_second), (bias_table, table_first, table_second))
    results = [out, grad]
    for i, (state, total, rate) in enumerate(zip(states, totals, step_rates)):
        new = adamw(*state, total, rate)
        results += [*new, new[0].astype(low)] if i < 4 else [*new]
    return tuple(results)


def solution(mesh):
    wins = P(("rep", "shard"), None, None)
    rows = P("shard", None)
    cols = P(None, "shard")
    fits = mesh.shape["rep"] == REPS and mesh.shape["shard"] == OWNERS
    return jax.shard_map(
        shards if fits else shards_general,
        mesh=mesh,
        in_specs=(wins, wins, P(("rep", "shard"))) + (rows,) * 12 + (cols,) * 3 + (rows,) * 3,
        out_specs=(wins, wins) + (rows,) * 16 + (cols,) * 3 + (rows,) * 3,
        check_vma=False,
    )
```

```python
import functools
import math

import jax
import jax.numpy as jnp
import numpy as np
from jax import lax
from jax.experimental import pallas as pl
from jax.experimental.pallas import tpu as pltpu
from jax.sharding import PartitionSpec as P

C = 768
HEADS = 24
MLP = 3072
WIN = 12
STEP = 5
HEAD_DIM = 32
SPAN = 2 * WIN - 1
TOK = WIN * WIN
TAB_ROWS = 536
ROWS = 1024
GROUPS = 3
GCOLS = 256
GHEADS = 8
PACK = GHEADS * TOK
TAB_LANES = 640
TILES = 3
TILE = MLP // TILES
SUB = 512
LINE = 384
MIB = 1 << 20

beta_one = 0.5
beta_two = 0.6
weight_decay = 0.05
adam_eps = 1e-08
norm_eps = 1e-05
step_rates = (0.04, 0.15, 0.04, 0.02, 0.2, 1.0)
low = jnp.bfloat16
full = jnp.float32
NT = (((1,), (1,)), ((), ()))


def dot(a, b):
    return jnp.dot(a, b, preferred_element_type=full)


def dot_nt(a, b):
    return lax.dot_general(a, b, NT, preferred_element_type=full)


def line_matrix():
    out = np.zeros((TAB_LANES, LINE), np.float32)
    col = np.arange(SPAN * WIN)
    out[(col // WIN) * SPAN + col % WIN + WIN - 1, col] = 1.0
    return out


def head_masks():
    lane = np.arange(GCOLS) // HEAD_DIM
    one = (lane[None, :] == np.arange(GHEADS)[:, None]).astype(np.float32)
    return np.broadcast_to(one[:, None, :], (GHEADS, 16, GCOLS))


def norm_parts(z):
    mean = jnp.sum(z, -1, keepdims=True) * (1.0 / C)
    center = z - mean
    spread = jnp.sum(center * center, -1, keepdims=True) * (1.0 / C)
    scale = lax.rsqrt(spread + norm_eps)
    return center * scale, scale


def norm_back(xhat, scale, dn, gain):
    g = dn * gain
    m1 = jnp.sum(g, -1, keepdims=True) * (1.0 / C)
    m2 = jnp.sum(g * xhat, -1, keepdims=True) * (1.0 / C)
    return scale * (g - m1 - xhat * m2)


def diag(x, mask_ref):
    head = x[0:128].reshape(8, 16, GCOLS)
    tail = x[128:144]
    parts = []
    for h in range(GHEADS):
        parts.append((head * mask_ref[h][None]).reshape(128, GCOLS))
    for h in range(GHEADS):
        parts.append(tail * mask_ref[h])
    return jnp.concatenate(parts, 0)


def undiag(xt, m, mask_ref):
    main = []
    for h in range(0, GHEADS, 2):
        r = dot(xt[h * HEAD_DIM : (h + 2) * HEAD_DIM], m[:, h * 128 : (h + 2) * 128])
        main.append(r[0:HEAD_DIM, 0:128])
        main.append(r[HEAD_DIM : 2 * HEAD_DIM, 128:256])
    main = jnp.concatenate(main, 0)
    rest = dot(xt, m[:, GHEADS * 128 :])
    rest_t = rest.T.reshape(GHEADS, 16, GCOLS)
    keep = mask_ref[...].astype(full)
    return jnp.concatenate([main.T, jnp.sum(rest_t * keep, 0)], 0)


def flat(x):
    return x.reshape(x.shape[0] * x.shape[1], x.shape[2])


def blocks(x, owners):
    return x.reshape(owners, x.shape[0] // owners, x.shape[1])


def hidden_place(t, s):
    at = (MLP // GHEADS) * s + 128 * t
    return 8 + at // C, at % C


def unpack_small(small_ref, vec_ref):
    owners = small_ref.shape[0]
    width = C // owners
    count = TAB_ROWS // owners
    vec = jnp.zeros((16, C), full)
    tab = jnp.zeros((HEADS, TAB_LANES), full)
    lane = lax.broadcasted_iota(jnp.int32, (16, 128), 1)
    lane_tab = lax.broadcasted_iota(jnp.int32, (HEADS, 128), 1)
    for s in range(owners):
        piece = small_ref[s].astype(full)
        part = jnp.where(lane < width, piece[0:16], 0.0)
        part = jnp.concatenate([part, jnp.zeros((16, C - 128), full)], 1)
        vec = vec + (pltpu.roll(part, width * s, 1) if s else part)
        part = jnp.where(lane_tab < count, piece[16 : 16 + HEADS], 0.0)
        part = jnp.concatenate([part, jnp.zeros((HEADS, TAB_LANES - 128), full)], 1)
        tab = tab + (pltpu.roll(part, count * s, 1) if s else part)
    vec_ref[...] = vec
    return tab


def pack_small(vec, tab, out_ref):
    owners = out_ref.shape[0]
    width = C // owners
    count = TAB_ROWS // owners
    for s in range(owners):
        out_ref[s, 0:16, :] = (pltpu.roll(vec, C - width * s, 1) if s else vec)[:, 0:128]
        out_ref[s, 16:40, :] = (pltpu.roll(tab, TAB_LANES - count * s, 1) if s else tab)[:, 0:128]


def spread_table(tab, line_ref, tmp_ref):
    def column(cj, carry):
        shifted = pltpu.roll(tab, cj, 1)
        line = dot(shifted.astype(low), line_ref[...])
        for rj in range(WIN):
            cut = (WIN - 1 - rj) * WIN
            part = pltpu.roll(line, LINE - cut, 1) if cut else line
            row = pl.multiple_of((rj * WIN + cj) * HEADS, 8)
            tmp_ref[0, pl.ds(row, HEADS), :] = part[:, 0:128]
            tmp_ref[1, pl.ds(row, HEADS), :] = part[:, 128:256]
        return carry

    lax.fori_loop(0, WIN, column, 0)


def place_bias(tmp_ref, bias_ref):
    lane = lax.broadcasted_iota(jnp.int32, (TOK, 128), 1)
    for g in range(GROUPS):
        rest = jnp.zeros((TOK, 128), full)
        for h in range(GHEADS):
            at = pl.ds(g * GHEADS + h, TOK, stride=HEADS)
            bias_ref[g, :, h * 128 : (h + 1) * 128] = tmp_ref[0, at, :]
            piece = tmp_ref[1, at, :]
            piece = pltpu.roll(piece, 16 * h, 1) if h else piece
            rest = jnp.where((lane >= 16 * h) & (lane < 16 * h + 16), piece, rest)
        bias_ref[g, :, GHEADS * 128 :] = rest


def table_grad(line_ref, tmp_ref, bias_ref):
    lane = lax.broadcasted_iota(jnp.int32, (TOK, 128), 1)
    for g in range(GROUPS):
        rest = bias_ref[g, :, GHEADS * 128 :]
        for h in range(GHEADS):
            at = pl.ds(g * GHEADS + h, TOK, stride=HEADS)
            tmp_ref[0, at, :] = bias_ref[g, :, h * 128 : (h + 1) * 128]
            piece = pltpu.roll(rest, 128 - 16 * h, 1) if h else rest
            tmp_ref[1, at, :] = jnp.where(lane < 16, piece, 0.0)

    def column(cj, total):
        line = jnp.zeros((HEADS, LINE), full)
        for rj in range(WIN):
            cut = (WIN - 1 - rj) * WIN
            row = pl.multiple_of((rj * WIN + cj) * HEADS, 8)
            part = jnp.concatenate([tmp_ref[0, pl.ds(row, HEADS), :], tmp_ref[1, pl.ds(row, HEADS), :], jnp.zeros((HEADS, 128), full)], 1)
            line = line + (pltpu.roll(part, cut, 1) if cut else part)
        high = line.astype(low)
        rest = (line - high.astype(full)).astype(low)
        spread = dot_nt(high, line_ref[...]) + dot_nt(rest, line_ref[...])
        return total + pltpu.roll(spread, TAB_LANES - cj, 1)

    return lax.fori_loop(0, WIN, column, jnp.zeros((HEADS, TAB_LANES), full))


def transpose_rows(src_ref, dst_ref):
    def block(i, carry):
        at = pl.multiple_of(i * 128, 128)
        dst_ref[:, pl.ds(at, 128)] = src_ref[pl.ds(at, 128), :].T
        return carry

    lax.fori_loop(0, ROWS // 128, block, 0)


def window_rows(w):
    return pl.ds(pl.multiple_of(w * TOK, 16), TOK)


def zero_tail(ref, windows):
    at = windows * TOK
    ref[at:ROWS, :] = jnp.zeros((ROWS - at, ref.shape[1]), ref.dtype)


def attention_forward(windows, x_ref, small_ref, line_ref, mask_ref, wq_ref, wp_ref,
                      qkv_ref, pt_ref, o_ref, x1_ref, n1t_ref, vec_ref, n1_ref, bias_ref, tmp_ref):
    tab = unpack_small(small_ref, vec_ref)
    spread_table(tab, line_ref, tmp_ref)
    place_bias(tmp_ref, bias_ref)
    zero_tail(n1_ref, windows)
    zero_tail(o_ref, windows)

    def first_norm(w, carry):
        xhat, _ = norm_parts(x_ref[window_rows(w), :].astype(full))
        n1_ref[window_rows(w), :] = (xhat * vec_ref[0:1, :] + vec_ref[1:2, :]).astype(low)
        return carry

    lax.fori_loop(0, windows, first_norm, 0)
    transpose_rows(n1_ref, n1t_ref)

    def group(g, carry):
        cols = pl.ds(pl.multiple_of(g * GCOLS, GCOLS), GCOLS)
        n1 = n1_ref[...]
        qkv_ref[g] = ((dot(n1, flat(wq_ref[g, 0])) + vec_ref[2:3, cols]) * (HEAD_DIM**-0.5)).astype(low)
        qkv_ref[GROUPS + g] = dot(n1, flat(wq_ref[g, 1])).astype(low)
        qkv_ref[2 * GROUPS + g] = (dot(n1, flat(wq_ref[g, 2])) + vec_ref[3:4, cols]).astype(low)

        def window(w, inner):
            rows = window_rows(w)
            q = qkv_ref[g, rows, :]
            k = qkv_ref[GROUPS + g, rows, :]
            v = qkv_ref[2 * GROUPS + g, rows, :]
            s = dot_nt(k, diag(q, mask_ref)) + bias_ref[g]
            e = jnp.exp(s - jnp.max(s, 0, keepdims=True))
            p = (e * (1.0 / jnp.sum(e, 0, keepdims=True))).astype(low)
            pt_ref[g, w] = p
            o_ref[rows, cols] = undiag(v.T, p, mask_ref).astype(low)
            return inner

        lax.fori_loop(0, windows, window, 0)
        return carry

    lax.fori_loop(0, GROUPS, group, 0)

    def output(w, carry):
        rows = window_rows(w)
        branch = dot(o_ref[rows, :], flat(wp_ref[...])) + vec_ref[4:5, :]
        x1_ref[rows, :] = x_ref[rows, :].astype(full) + branch
        return carry

    lax.fori_loop(0, windows, output, 0)


def gelu_both(h):
    c = math.sqrt(2.0 / math.pi)
    square = h * h
    t = jnp.tanh(h * (c + (c * 0.044715) * square))
    half = 0.5 + 0.5 * t
    slope = half + (0.5 * h) * (1.0 - t * t) * (c + (3.0 * c * 0.044715) * square)
    return h * half, slope


def feed_forward(windows, x1_ref, dy_ref, live_ref, vec_ref, up_ref, down_ref, wp_ref, o_ref,
                 out_ref, dx1_ref, do_ref, gup_ref, gdown_ref, gout_ref, sums_ref,
                 n2_ref, n2t_ref, dy2_ref, dyt_ref, y_ref, dn_ref, bu_ref, bsum_ref):
    zero_tail(n2_ref, windows)
    zero_tail(dy2_ref, windows)

    def second_norm(w, carry):
        rows = window_rows(w)
        xhat, _ = norm_parts(x1_ref[rows, :])
        n2_ref[rows, :] = (xhat * vec_ref[5:6, :] + vec_ref[6:7, :]).astype(low)
        dy2_ref[rows, :] = (dy_ref[rows, :].astype(full) * live_ref[w]).astype(low)
        return carry

    lax.fori_loop(0, windows, second_norm, 0)
    transpose_rows(n2_ref, n2t_ref)
    transpose_rows(dy2_ref, dyt_ref)
    y_ref[...] = jnp.zeros_like(y_ref)
    dn_ref[...] = jnp.zeros_like(dn_ref)
    owners = gup_ref.shape[1]
    for t in range(TILES):
        for s in range(TILE // 128):
            row, at = hidden_place(t, s)
            bu_ref[t, :, s * 128 : (s + 1) * 128] = vec_ref[row : row + 1, at : at + 128]

    def step(t, carry):
        for part in range(TILE // SUB):
            cols = slice(part * SUB, (part + 1) * SUB)
            up = flat(up_ref[t, :, :, cols])
            down = flat(down_ref[t, part * SUB // 128 : (part + 1) * SUB // 128])
            h = dot(n2_ref[...], up) + bu_ref[t, :, cols]
            da = dot_nt(dy2_ref[...], down)
            act, slope = gelu_both(h)
            a = act.astype(low)
            dh = (da * slope).astype(low)
            bsum_ref[t, :, cols] = jnp.sum(dh.astype(full), 0, keepdims=True)
            y_ref[...] += dot(a, down)
            dn_ref[...] += dot_nt(dh, up)
            gd = dot(dyt_ref[...], a).astype(low)
            for b in range(SUB // 128):
                gdown_ref[t, part * SUB // 128 + b] = gd[:, b * 128 : (b + 1) * 128]
            gup_ref[t, :, :, cols] = blocks(dot(n2t_ref[...], dh).astype(low), owners)
        return carry

    lax.fori_loop(0, TILES, step, 0)
    sums_ref[...] = jnp.zeros_like(sums_ref)
    for t in range(TILES):
        for s in range(TILE // 128):
            row, at = hidden_place(t, s)
            sums_ref[row : row + 1, at : at + 128] = bsum_ref[t, :, s * 128 : (s + 1) * 128]
    zero_tail(dx1_ref, windows)

    def finish(w, carry):
        rows = window_rows(w)
        x1 = x1_ref[rows, :]
        out_ref[rows, :] = ((x1 + y_ref[rows, :] + vec_ref[7:8, :]) * live_ref[w]).astype(low)
        xhat, scale = norm_parts(x1)
        dn = dn_ref[rows, :]
        dy = dy2_ref[rows, :].astype(full)
        dx1 = dy + norm_back(xhat, scale, dn, vec_ref[5:6, :])
        dx1_ref[rows, :] = dx1
        dr = dx1.astype(low)
        n2_ref[rows, :] = dr
        do_ref[rows, :] = dot_nt(dr, flat(wp_ref[...])).astype(low)
        sums_ref[4:5, :] += jnp.sum(dr.astype(full), 0, keepdims=True)
        sums_ref[5:6, :] += jnp.sum(dn * xhat, 0, keepdims=True)
        sums_ref[6:7, :] += jnp.sum(dn, 0, keepdims=True)
        sums_ref[7:8, :] += jnp.sum(dy, 0, keepdims=True)
        return carry

    lax.fori_loop(0, windows, finish, 0)
    transpose_rows(o_ref, dyt_ref)
    for g in range(GROUPS):
        at = pl.ds(g * GCOLS, GCOLS)
        gout_ref[:, :, at] = blocks(dot(dyt_ref[...], n2_ref[:, at]).astype(low), gout_ref.shape[0])


def attention_backward(windows, x_ref, vec_ref, line_ref, mask_ref, wq_ref, qkv_ref, pt_ref, do_ref, dx1_ref, n1t_ref, sums_in_ref,
                       gq_ref, gsmall_ref, grad_ref, sums_ref, bias_ref, tmp_ref, dproj_ref, dn_ref):
    bias_ref[...] = jnp.zeros_like(bias_ref)
    dn_ref[...] = jnp.zeros_like(dn_ref)
    sums_ref[...] = sums_in_ref[...]
    for part in range(3):
        dproj_ref[part, windows * TOK :, :] = jnp.zeros((ROWS - windows * TOK, GCOLS), low)

    def group(g, carry):
        cols = pl.ds(pl.multiple_of(g * GCOLS, GCOLS), GCOLS)

        def window(w, inner):
            rows = window_rows(w)
            q = qkv_ref[g, rows, :]
            k = qkv_ref[GROUPS + g, rows, :]
            v = qkv_ref[2 * GROUPS + g, rows, :]
            p = pt_ref[g, w]
            do = diag(do_ref[rows, cols], mask_ref)
            dp = dot_nt(v, do)
            dv = dot(p, do)
            pf = p.astype(full)
            ds = (pf * (dp - jnp.sum(pf * dp, 0, keepdims=True))).astype(low)
            bias_ref[g] += ds.astype(full)
            dk = dot(ds, diag(q, mask_ref))
            dq = undiag(k.T, ds, mask_ref) * (HEAD_DIM**-0.5)
            dq = dq.astype(low)
            dv = dv.astype(low)
            dproj_ref[0, rows, :] = dq
            dproj_ref[1, rows, :] = dk.astype(low)
            dproj_ref[2, rows, :] = dv
            sums_ref[2:3, cols] += jnp.sum(dq.astype(full), 0, keepdims=True)
            sums_ref[3:4, cols] += jnp.sum(dv.astype(full), 0, keepdims=True)
            return inner

        lax.fori_loop(0, windows, window, 0)
        for part in range(3):
            d = dproj_ref[part]
            gq_ref[g, part] = blocks(dot(n1t_ref[...], d).astype(low), gq_ref.shape[2])
            dn_ref[...] += dot_nt(d, flat(wq_ref[g, part]))
        return carry

    lax.fori_loop(0, GROUPS, group, 0)

    def finish(w, carry):
        rows = window_rows(w)
        xhat, scale = norm_parts(x_ref[rows, :].astype(full))
        dn = dn_ref[rows, :]
        grad_ref[rows, :] = dx1_ref[rows, :] + norm_back(xhat, scale, dn, vec_ref[0:1, :])
        sums_ref[0:1, :] += jnp.sum(dn * xhat, 0, keepdims=True)
        sums_ref[1:2, :] += jnp.sum(dn, 0, keepdims=True)
        return carry

    lax.fori_loop(0, windows, finish, 0)
    pack_small(sums_ref[...], table_grad(line_ref, tmp_ref, bias_ref), gsmall_ref)


MESH = pl.DeviceIdType.MESH
REPS = 4
OWNERS = 8
LINKS = OWNERS // 2


class Spot:
    def __init__(self):
        self.rep = lax.axis_index("rep")
        self.shard = lax.axis_index("shard")
        self.z = self.shard // 2
        self.core = self.shard % 2

    def sibling(self):
        return (self.rep, self.z * 2 + (1 - self.core))

    def along_z(self, step):
        return (self.rep, ((self.z + step) % LINKS) * 2 + self.core)

    def turned(self, axis):
        x, y = self.rep % 2, self.rep // 2
        return y * 2 + (1 - x) if axis == 0 else (1 - y) * 2 + x

    def beside(self, axis):
        return (self.turned(axis), self.shard)


def greet(spot):
    barrier = pltpu.get_barrier_semaphore()
    peers = [(spot.rep, (spot.shard + i) % OWNERS) for i in range(1, OWNERS)]
    peers += [((spot.rep + i) % REPS, spot.shard) for i in range(1, REPS)]
    for peer in peers:
        pl.semaphore_signal(barrier, inc=1, device_id=peer, device_id_type=MESH)
    return barrier, len(peers)


def send(src, dst, send_sem, recv_sem, peer):
    pltpu.make_async_remote_copy(src_ref=src, dst_ref=dst, send_sem=send_sem, recv_sem=recv_sem, device_id=peer, device_id_type=MESH).start()


def await_bytes(ref, sem):
    pltpu.make_async_copy(ref, ref, sem).wait()


def quarter(ref, rep):
    rows, cols = ref.shape[-2:]
    lead = (slice(None),) * (len(ref.shape) - 2)
    top = pl.multiple_of((rep // 2) * (rows // 2), 16)
    left = pl.multiple_of((rep % 2) * (cols // 2), 128)
    return ref.at[lead + (pl.ds(top, rows // 2), pl.ds(left, cols // 2))]


def half(ref, rep, axis):
    rows, cols = ref.shape[-2:]
    lead = (slice(None),) * (len(ref.shape) - 2)
    if axis == 0:
        left = pl.multiple_of((rep % 2) * (cols // 2), 128)
        return ref.at[lead + (slice(None), pl.ds(left, cols // 2))]
    top = pl.multiple_of((rep // 2) * (rows // 2), 16)
    return ref.at[lead + (pl.ds(top, rows // 2), slice(None))]


class Gather:
    KINDS = (LINKS - 1, LINKS - 1, LINKS - 1, LINKS - 1, LINKS)
    SEMS = 2 * sum(KINDS)
    STAGES = ("start", "across", "relay", "beside", "finish")

    def __init__(self, spot, place, axis, sems):
        self.spot, self.place, self.axis, self.sems = spot, place, axis, sems

    def sem(self, side, kind, i):
        return self.sems.at[side * (self.SEMS // 2) + sum(self.KINDS[:kind]) + i]

    def block(self, step):
        return self.place(((self.spot.z - step + LINKS) % LINKS) * 2 + self.spot.core)

    def other(self, step):
        return self.place(((self.spot.z - step + LINKS) % LINKS) * 2 + 1 - self.spot.core)

    def start(self):
        spot = self.spot
        mine = self.block(0)
        for i in range(1, LINKS):
            piece = quarter(mine, spot.rep)
            send(piece, piece, self.sem(0, 0, i - 1), self.sem(1, 0, i - 1), spot.along_z(i))
        send(mine, mine, self.sem(0, 4, 0), self.sem(1, 4, 0), spot.sibling())

    def across(self):
        spot = self.spot
        for i in range(1, LINKS):
            piece = quarter(self.block(i), spot.rep)
            await_bytes(piece, self.sem(1, 0, i - 1))
            for axis in (self.axis, 1 - self.axis):
                send(piece, piece, self.sem(0, 1 + axis, i - 1), self.sem(1, 1 + axis, i - 1), spot.beside(axis))

    def relay(self):
        spot = self.spot
        for i in range(1, LINKS):
            piece = quarter(self.block(i), spot.turned(self.axis))
            await_bytes(piece, self.sem(1, 1 + self.axis, i - 1))
            send(piece, piece, self.sem(0, 3, i - 1), self.sem(1, 3, i - 1), spot.beside(1 - self.axis))

    def beside(self):
        spot = self.spot
        for i in range(1, LINKS):
            block = self.block(i)
            piece = quarter(block, spot.rep)
            await_bytes(piece, self.sem(1, 2 - self.axis, i - 1))
            await_bytes(piece, self.sem(1, 3, i - 1))
            send(block, block, self.sem(0, 4, i), self.sem(1, 4, i), spot.sibling())

    def finish(self):
        for i in range(LINKS):
            await_bytes(self.other(i), self.sem(1, 4, i))

    def close(self):
        piece = quarter(self.block(0), self.spot.rep)
        for kind in range(4):
            for i in range(1, LINKS):
                await_bytes(piece, self.sem(0, kind, i - 1))
        for i in range(LINKS):
            await_bytes(self.block(i), self.sem(0, 4, i))


class Reduce:
    KINDS = (LINKS, 1, 1, LINKS - 1, REPS - 1)
    SEMS = 2 * sum(KINDS)
    STAGES = ("start", "first", "second", "along", "spread", "finish")

    def __init__(self, spot, place, out, core_sum, halves, quarters, links, axis, sems):
        self.spot, self.place, self.out, self.axis, self.sems = spot, place, out, axis, sems
        self.core_sum, self.halves, self.quarters, self.links = core_sum, halves, quarters, links

    def sem(self, side, kind, i):
        return self.sems.at[side * (self.SEMS // 2) + sum(self.KINDS[:kind]) + i]

    def start(self):
        spot = self.spot
        for z in range(LINKS):
            send(self.place(z * 2 + (1 - spot.core)), self.core_sum.at[z], self.sem(0, 0, z), self.sem(1, 0, z), spot.sibling())

    def first(self):
        spot = self.spot
        for z in range(LINKS):
            total = self.core_sum.at[z]
            await_bytes(total, self.sem(1, 0, z))
            total[...] = (total[...].astype(full) + self.place(z * 2 + spot.core)[...].astype(full)).astype(low)
        theirs = half(self.core_sum, spot.turned(self.axis), self.axis)
        send(theirs, self.halves, self.sem(0, 1, 0), self.sem(1, 1, 0), spot.beside(self.axis))

    def second(self):
        spot = self.spot
        await_bytes(self.halves, self.sem(1, 1, 0))
        mine = half(self.core_sum, spot.rep, self.axis)
        self.halves[...] = (self.halves[...].astype(full) + mine[...].astype(full)).astype(low)
        theirs = half(self.halves, spot.turned(1 - self.axis), 1 - self.axis)
        send(theirs, self.quarters, self.sem(0, 2, 0), self.sem(1, 2, 0), spot.beside(1 - self.axis))

    def along(self):
        spot = self.spot
        await_bytes(self.quarters, self.sem(1, 2, 0))
        mine = half(self.halves, spot.rep, 1 - self.axis)
        self.quarters[...] = (self.quarters[...].astype(full) + mine[...].astype(full)).astype(low)
        for i in range(1, LINKS):
            send(self.quarters.at[(spot.z + i) % LINKS], self.links.at[i - 1], self.sem(0, 3, i - 1), self.sem(1, 3, i - 1), spot.along_z(i))

    def spread(self):
        spot = self.spot
        total = self.quarters[spot.z].astype(full)
        for i in range(1, LINKS):
            await_bytes(self.links.at[i - 1], self.sem(1, 3, i - 1))
            total = total + self.links[i - 1].astype(full)
        mine = quarter(self.out, spot.rep)
        mine[...] = total.astype(low)
        for j in range(1, REPS):
            send(mine, mine, self.sem(0, 4, j - 1), self.sem(1, 4, j - 1), ((spot.rep + j) % REPS, spot.shard))

    def finish(self):
        for j in range(1, REPS):
            await_bytes(quarter(self.out, (self.spot.rep - j + REPS) % REPS), self.sem(1, 4, j - 1))

    def close(self):
        for z in range(LINKS):
            await_bytes(self.core_sum.at[z], self.sem(0, 0, z))
        await_bytes(self.halves, self.sem(0, 1, 0))
        await_bytes(self.quarters, self.sem(0, 2, 0))
        for i in range(1, LINKS):
            await_bytes(self.links.at[i - 1], self.sem(0, 3, i - 1))
        for j in range(1, REPS):
            await_bytes(quarter(self.out, self.spot.rep), self.sem(0, 4, j - 1))


class ReduceSmall:
    KINDS = (LINKS, LINKS - 1, REPS - 1)
    SEMS = 2 * sum(KINDS)
    STAGES = ("start", "first", "second", "along")

    def __init__(self, spot, terms, out, core_sum, links, parts, sems):
        self.spot, self.terms, self.out, self.core_sum, self.links, self.parts, self.sems = spot, terms, out, core_sum, links, parts, sems

    sem = Reduce.sem

    def start(self):
        spot = self.spot
        for z in range(LINKS):
            send(self.terms.at[z * 2 + (1 - spot.core)], self.core_sum.at[z], self.sem(0, 0, z), self.sem(1, 0, z), spot.sibling())

    def first(self):
        spot = self.spot
        for z in range(LINKS):
            await_bytes(self.core_sum.at[z], self.sem(1, 0, z))
            self.core_sum[z] = self.core_sum[z] + self.terms[z * 2 + spot.core]
        for i in range(1, LINKS):
            send(self.core_sum.at[(spot.z + i) % LINKS], self.links.at[i - 1], self.sem(0, 1, i - 1), self.sem(1, 1, i - 1), spot.along_z(i))

    def second(self):
        spot = self.spot
        total = self.core_sum[spot.z]
        for i in range(1, LINKS):
            await_bytes(self.links.at[i - 1], self.sem(1, 1, i - 1))
            total = total + self.links[i - 1]
        self.parts[spot.rep] = total
        mine = self.parts.at[spot.rep]
        for j in range(1, REPS):
            send(mine, mine, self.sem(0, 2, j - 1), self.sem(1, 2, j - 1), ((spot.rep + j) % REPS, spot.shard))

    def along(self):
        for j in range(1, REPS):
            await_bytes(self.parts.at[(self.spot.rep - j + REPS) % REPS], self.sem(1, 2, j - 1))
        total = self.parts[0]
        for j in range(1, REPS):
            total = total + self.parts[j]
        self.out[...] = total

    def close(self):
        for z in range(LINKS):
            await_bytes(self.core_sum.at[z], self.sem(0, 0, z))
        for i in range(1, LINKS):
            await_bytes(self.links.at[i - 1], self.sem(0, 1, i - 1))
        for j in range(1, REPS):
            await_bytes(self.parts.at[self.spot.rep], self.sem(0, 2, j - 1))


OWNED = C // OWNERS
SLOTS = TILES + 1
GATHERS = 2 * TILES + 1 + GROUPS
REDUCES = 2 * TILES + 1 + (GROUPS - 1) + 3
W_Q0, W_Q1, W_Q2, W_P, W_U0, W_D0, W_U1, W_D1, W_U2, W_D2 = W_ALL = range(10)
G_D0, G_U0, G_D1, G_U1, G_D2, G_U2, G_P, G_Q0, G_Q1, G_Q2, G_K2, G_V2, G_S = G_ALL = range(10, 23)
W_Q, W_U, W_D = (W_Q0, W_Q1, W_Q2), (W_U0, W_U1, W_U2), (W_D0, W_D1, W_D2)
G_D, G_U, G_Q, G_LAST = (G_D0, G_D1, G_D2), (G_U0, G_U1, G_U2), (G_Q0, G_Q1), (G_Q2, G_K2, G_V2)
START, ACROSS, RELAY, BESIDE, ARRIVED = range(5)
FIRST, SECOND, ALONG, SPREAD, SUMMED = range(1, 6)
BEFORE = {
    0: ((W_Q2, START), (W_P, START),),
    2: ((W_Q0, ACROSS), (W_U0, START),),
    4: ((W_Q0, RELAY), (W_Q1, ACROSS), (W_D0, START),),
}
FORWARD = {
    0: ((W_Q2, ACROSS), (W_Q1, RELAY), (W_U1, START), (W_P, ACROSS), (W_D1, START),),
    4: ((W_U0, ACROSS), (W_U2, START), (W_Q1, BESIDE),),
    6: ((W_Q2, RELAY), (W_P, RELAY),),
    7: ((W_D0, ACROSS), (W_D2, START),),
    9: ((W_Q2, BESIDE), (W_U0, RELAY),),
    11: ((W_P, BESIDE),),
    12: ((W_U1, ACROSS), (W_D0, RELAY),),
    14: ((W_U0, BESIDE),),
    15: ((W_D1, ACROSS),),
    18: ((W_U2, ACROSS),),
    19: ((W_U1, RELAY), (W_D0, BESIDE),),
}
MIDDLE = {
    0: ((W_D2, ACROSS), (W_D1, RELAY),),
    1: ((W_U2, RELAY),),
    2: ((W_U1, BESIDE),),
}
TILE_STEP = {
    1: ((W_D1, BESIDE), (W_U2, BESIDE), (W_D2, RELAY),),
    2: ((W_D2, BESIDE),),
    3: ((G_D0, FIRST), (G_U0, FIRST),),
    5: ((G_D0, SECOND), (G_U0, SECOND), (G_D1, FIRST), (G_U1, FIRST),),
}
AFTER_TILES = {
    0: ((G_D0, ALONG), (G_U0, ALONG),),
    2: ((G_D2, FIRST),),
    3: ((G_D0, SPREAD), (G_D1, SECOND), (G_U1, SECOND), (G_U2, FIRST),),
}
BACKWARD = {
    2: ((G_U0, SPREAD), (G_P, FIRST),),
    4: ((G_D1, ALONG),),
    5: ((G_D2, SECOND),),
    6: ((G_D0, SUMMED),),
    7: ((G_U1, ALONG),),
    8: ((G_D1, SPREAD), (G_U2, SECOND),),
    9: ((G_U0, SUMMED), (G_Q0, FIRST),),
    12: ((G_U1, SPREAD), (G_D2, ALONG),),
    13: ((G_P, SECOND),),
    14: ((G_D1, SUMMED),),
    15: ((G_Q0, SECOND),),
    16: ((G_D2, SPREAD), (G_U2, ALONG), (G_Q1, FIRST),),
    17: ((G_U1, SUMMED),),
    18: ((G_P, ALONG),),
    20: ((G_D2, SUMMED), (G_U2, SPREAD),),
}
LAST_STEPS = {
    0: ((G_Q0, ALONG), (G_P, SPREAD), (G_Q2, FIRST),),
    1: ((G_K2, FIRST), (G_V2, FIRST),),
    2: ((G_Q1, SECOND),),
    3: ((G_Q0, SPREAD), (G_U2, SUMMED), (G_Q2, SECOND),),
}


def chunk_shapes():
    out = []
    for _ in range(TILES):
        out += [(128, C), (OWNED, TILE)]
    return out + [(OWNED, C)] + [(3, OWNED, GCOLS)] * (GROUPS - 1) + [(OWNED, GCOLS)] * 3


def reduce_scratch():
    out = []
    for i, dims in enumerate(chunk_shapes()):
        *lead, rows, cols = dims
        near = (rows, cols // 2) if i % 2 == 0 else (rows // 2, cols)
        out.append(pltpu.VMEM((LINKS, *dims), low))
        out.append(pltpu.VMEM((LINKS, *lead, *near), low))
        out.append(pltpu.VMEM((LINKS, *lead, rows // 2, cols // 2), low))
        out.append(pltpu.VMEM((LINKS - 1, *lead, rows // 2, cols // 2), low))
    out += [pltpu.VMEM((LINKS, 40, 128), full), pltpu.VMEM((LINKS - 1, 40, 128), full), pltpu.VMEM((REPS, 40, 128), full)]
    return out


def layer_kernel(windows, x_hbm, dy_hbm, live_ref, q32, p32, u32, d32, vec_in, tab_in, line_ref, mask_ref,
                 out_hbm, grad_hbm, gq_out, gp_out, gu_out, gd_out, gs_out, qkv_hbm, pt_hbm, n1t_hbm, *scratch):
    wq, wp, up, down, small, o_ref, x1_ref, vec_ref, sums_ref, terms_ref = scratch[:10]
    gather_sems, reduce_sems, small_sems, small_reduce_sems, local = scratch[-5:]
    reduce_refs = scratch[10:-5]
    spot = Spot()
    rows_all = windows * TOK
    mine = spot.shard
    V = pltpu.VMEM

    jobs = {}
    places = [(W_Q[g], lambda s, g=g: wq.at[g, :, s]) for g in range(GROUPS)] + [(W_P, lambda s: wp.at[s])]
    for t in range(TILES):
        places += [(W_U[t], lambda s, t=t: up.at[t, s]), (W_D[t], lambda s, t=t: down.at[t, s])]
    for i, (name, place) in enumerate(places):
        jobs[name] = Gather(spot, place, i % 2, gather_sems.at[i])
    places = []
    for t in range(TILES):
        slot = (t + SLOTS - 1) % SLOTS
        places.append((G_D[t], lambda s, slot=slot: down.at[slot, s], gd_out.at[t]))
        places.append((G_U[t], lambda s, slot=slot: up.at[slot, s], gu_out.at[t]))
    places.append((G_P, lambda s: wp.at[s], gp_out))
    for g in range(GROUPS - 1):
        places.append((G_Q[g], lambda s, g=g: wq.at[g, :, s], gq_out.at[g]))
    for part in range(3):
        places.append((G_LAST[part], lambda s, part=part: wq.at[GROUPS - 1, part, s], gq_out.at[GROUPS - 1, part]))
    for i, (name, place, out) in enumerate(places):
        jobs[name] = Reduce(spot, place, out, *reduce_refs[4 * i : 4 * i + 4], i % 2, reduce_sems.at[i])
    jobs[G_S] = ReduceSmall(spot, terms_ref, gs_out, *reduce_refs[-3:], small_reduce_sems)

    done = {}

    def run(name, upto):
        for stage in range(done.get(name, 0), upto + 1):
            getattr(jobs[name], jobs[name].STAGES[stage])()
        done[name] = max(done.get(name, 0), upto + 1)

    def hook(table, place):
        for item in table.get(place, ()):
            run(*item)

    def hook_window(table, g, w):
        for at in range(windows):
            place = g * windows + at
            if place in table:

                @pl.when(w == at)
                def _(place=place):
                    hook(table, place)

    barrier, peers = greet(spot)

    def cast(q_v, p_v, u_v, d_v):
        loads = [pltpu.make_async_copy(a, b, local.at[i]) for i, (a, b) in enumerate(((q32, q_v), (p32, p_v), (u32, u_v), (d32, d_v)))]
        for load in loads:
            load.start()
        small[mine] = jnp.zeros((48, 128), low)
        pad = jnp.zeros((16, 128), full)
        vec_ref[:, 0:128] = pad
        vec_ref[0:12, 0:OWNED] = vec_in[...]
        small[mine, 0:16, :] = vec_ref[:, 0:128].astype(low)
        x1_ref[0:32, 0:128] = jnp.zeros((32, 128), full)
        x1_ref[0:HEADS, 0 : tab_in.shape[1]] = tab_in[...]
        small[mine, 16:48, :] = x1_ref[0:32, 0:128].astype(low)
        loads[0].wait()
        for g in range(GROUPS):
            for part in range(3):
                wq[g, part, mine] = q_v[:, part * C + g * GCOLS : part * C + (g + 1) * GCOLS].astype(low)
        pl.semaphore_wait(barrier, peers)
        for i in range(1, OWNERS):
            send(small.at[mine], small.at[mine], small_sems.at[i], small_sems.at[OWNERS + i], (spot.rep, (mine + i) % OWNERS))
        run(W_Q0, START)
        run(W_Q1, START)
        loads[1].wait()
        wp[mine] = p_v[...].astype(low)
        loads[2].wait()
        loads[3].wait()
        for t in range(TILES):
            for s in range(OWNERS):
                src = (MLP // OWNERS) * s + 128 * t
                up[t, mine, :, s * 128 : (s + 1) * 128] = u_v[:, src : src + 128].astype(low)
            down[t, mine] = d_v[t * 128 : (t + 1) * 128, :].astype(low)

    pl.run_scoped(cast, V((OWNED, 3 * C), full), V((OWNED, C), full), V((OWNED, MLP), full), V((TILES * 128, C), full))

    def forward(x_ref, n1_ref, n1t_ref, qkv_ref, pt_ref, bias_ref):
        load = pltpu.make_async_copy(x_hbm, x_ref, local.at[0])
        load.start()
        zero_tail(n1_ref, windows)
        zero_tail(o_ref, windows)
        for i in range(1, OWNERS):
            await_bytes(small.at[(mine - i + OWNERS) % OWNERS], small_sems.at[OWNERS + i])
        tab = unpack_small(small, vec_ref)
        hook(BEFORE, 0)
        load.wait()
        hook(BEFORE, 1)

        def first_norm(w, carry):
            xhat, _ = norm_parts(x_ref[window_rows(w), :].astype(full))
            n1_ref[window_rows(w), :] = (xhat * vec_ref[0:1, :] + vec_ref[1:2, :]).astype(low)
            return carry

        lax.fori_loop(0, windows, first_norm, 0)
        hook(BEFORE, 2)
        transpose_rows(n1_ref, n1t_ref)
        save = pltpu.make_async_copy(n1t_ref, n1t_hbm, local.at[1])
        save.start()
        hook(BEFORE, 3)

        def bias(tmp_ref):
            spread_table(tab, line_ref, tmp_ref)
            hook(BEFORE, 4)
            place_bias(tmp_ref, bias_ref)

        pl.run_scoped(bias, V((2, TOK * HEADS, 128), full))
        for g in range(GROUPS):
            cols = slice(g * GCOLS, (g + 1) * GCOLS)
            held = qkv_ref.at[g % 2]
            if g >= 2:
                pltpu.make_async_copy(held, qkv_hbm.at[g - 2], local.at[2 + g % 2]).wait()
            run(W_Q[g], ARRIVED)
            n1 = n1_ref[...]
            held[0] = ((dot(n1, flat(wq[g, 0])) + vec_ref[2:3, cols]) * (HEAD_DIM**-0.5)).astype(low)
            held[1] = dot(n1, flat(wq[g, 1])).astype(low)
            held[2] = (dot(n1, flat(wq[g, 2])) + vec_ref[3:4, cols]).astype(low)
            pltpu.make_async_copy(held, qkv_hbm.at[g], local.at[2 + g % 2]).start()

            def window(w, carry, g=g, cols=cols, held=held):
                hook_window(FORWARD, g, w)
                rows = window_rows(w)
                n = g * windows + w
                slot = n % 2
                s = dot_nt(held[1, rows, :], diag(held[0, rows, :], mask_ref)) + bias_ref[g]
                e = jnp.exp(s - jnp.max(s, 0, keepdims=True))
                p = (e * (1.0 / jnp.sum(e, 0, keepdims=True))).astype(low)
                keep = pltpu.make_async_copy(pt_ref.at[slot], pt_hbm.at[n], local.at[4 + slot])

                @pl.when(n >= 2)
                def _():
                    keep.wait()

                pt_ref[slot] = p
                keep.start()
                o_ref[rows, cols] = undiag(held[2, rows, :].T, p, mask_ref).astype(low)
                return carry

            lax.fori_loop(0, windows, window, 0)

        run(W_P, ARRIVED)

        def output(w, carry):
            rows = window_rows(w)
            x1_ref[rows, :] = x_ref[rows, :].astype(full) + (dot(o_ref[rows, :], flat(wp[...])) + vec_ref[4:5, :])
            return carry

        lax.fori_loop(0, windows, output, 0)
        save.wait()
        for g in (GROUPS - 2, GROUPS - 1):
            pltpu.make_async_copy(qkv_ref.at[g % 2], qkv_hbm.at[g], local.at[2 + g % 2]).wait()
        for slot in range(2):
            pltpu.make_async_copy(pt_ref.at[slot], pt_hbm.at[0], local.at[4 + slot]).wait()

    pl.run_scoped(forward, V((rows_all, C), low), V((ROWS, C), low), V((C, ROWS), low), V((2, 3, ROWS, GCOLS), low), V((2, TOK, PACK), low),
                  V((GROUPS, TOK, PACK), full))

    def middle(n2_ref, n2t_ref, dy_ref, dyt_ref, y_ref, dn_ref, bu_ref, bsum_ref):
        load = pltpu.make_async_copy(dy_hbm, dy_ref.at[0:rows_all], local.at[0])
        load.start()
        zero_tail(n2_ref, windows)
        zero_tail(dy_ref, windows)
        hook(MIDDLE, 0)
        load.wait()

        def second_norm(w, carry):
            rows = window_rows(w)
            xhat, _ = norm_parts(x1_ref[rows, :])
            n2_ref[rows, :] = (xhat * vec_ref[5:6, :] + vec_ref[6:7, :]).astype(low)
            dy_ref[rows, :] = (dy_ref[rows, :].astype(full) * live_ref[w]).astype(low)
            return carry

        lax.fori_loop(0, windows, second_norm, 0)
        transpose_rows(n2_ref, n2t_ref)
        hook(MIDDLE, 1)
        transpose_rows(dy_ref, dyt_ref)
        y_ref[...] = jnp.zeros_like(y_ref)
        dn_ref[...] = jnp.zeros_like(dn_ref)
        for t in range(TILES):
            for s in range(TILE // 128):
                row, left = hidden_place(t, s)
                bu_ref[t, :, s * 128 : (s + 1) * 128] = vec_ref[row : row + 1, left : left + 128]
        hook(MIDDLE, 2)
        run(W_U0, ARRIVED)
        run(W_D0, ARRIVED)
        halves = TILE // SUB

        def step(i, carry):
            for k in range(1, TILES * halves):

                @pl.when(i == k)
                def _(k=k):
                    if k % halves == 0:
                        t = k // halves
                        for name in (W_U[t], W_D[t]):
                            run(name, ARRIVED)
                        for name in (W_U[t - 1], W_D[t - 1]):
                            jobs[name].close()
                        for name in (G_D[t - 1], G_U[t - 1]):
                            run(name, START)
                    hook(TILE_STEP, k)

            t, part = i // halves, i % halves
            cols = pl.ds(pl.multiple_of(part * SUB, SUB), SUB)
            wide = SUB // 128
            slot = (t + SLOTS - 1) % SLOTS
            u = flat(up[t, :, :, cols])
            d = flat(down[t, pl.ds(part * wide, wide)])
            h = dot(n2_ref[...], u) + bu_ref[t, :, cols]
            da = dot_nt(dy_ref[...], d)
            act, slope = gelu_both(h)
            a = act.astype(low)
            dh = (da * slope).astype(low)
            bsum_ref[t, :, cols] = jnp.sum(dh.astype(full), 0, keepdims=True)
            y_ref[...] += dot(a, d)
            dn_ref[...] += dot_nt(dh, u)
            gd = dot(dyt_ref[...], a).astype(low)
            down[slot, pl.ds(part * wide, wide)] = blocks(gd.T, wide)
            up[slot, :, :, cols] = blocks(dot(n2t_ref[...], dh).astype(low), OWNERS)
            return carry

        lax.fori_loop(0, TILES * halves, step, 0)
        run(G_D[-1], START)
        run(G_U[-1], START)
        hook(AFTER_TILES, 0)
        sums_ref[...] = jnp.zeros_like(sums_ref)
        for t in range(TILES):
            for s in range(TILE // 128):
                row, left = hidden_place(t, s)
                sums_ref[row : row + 1, left : left + 128] = bsum_ref[t, :, s * 128 : (s + 1) * 128]
        transpose_rows(o_ref, dyt_ref)
        hook(AFTER_TILES, 1)

        def finish(w, carry):
            rows = window_rows(w)
            x1 = x1_ref[rows, :]
            xhat, scale = norm_parts(x1)
            dn = dn_ref[rows, :]
            dy = dy_ref[rows, :].astype(full)
            dx1 = dy + norm_back(xhat, scale, dn, vec_ref[5:6, :])
            dr = dx1.astype(low)
            sums_ref[4:5, :] += jnp.sum(dr.astype(full), 0, keepdims=True)
            sums_ref[5:6, :] += jnp.sum(dn * xhat, 0, keepdims=True)
            sums_ref[6:7, :] += jnp.sum(dn, 0, keepdims=True)
            sums_ref[7:8, :] += jnp.sum(dy, 0, keepdims=True)
            dy_ref[rows, :] = ((x1 + y_ref[rows, :] + vec_ref[7:8, :]) * live_ref[w]).astype(low)
            x1_ref[rows, :] = dx1
            n2_ref[rows, :] = dr
            o_ref[rows, :] = dot_nt(dr, flat(wp[...])).astype(low)
            return carry

        lax.fori_loop(0, windows, finish, 0)
        save = pltpu.make_async_copy(dy_ref.at[0:rows_all], out_hbm, local.at[0])
        save.start()
        hook(AFTER_TILES, 2)
        jobs[W_P].close()
        for g in range(GROUPS):
            cols = slice(g * GCOLS, (g + 1) * GCOLS)
            wp[:, :, cols] = blocks(dot(dyt_ref[...], n2_ref[:, cols]).astype(low), OWNERS)
        run(G_P, START)
        hook(AFTER_TILES, 3)
        save.wait()

    pl.run_scoped(middle, V((ROWS, C), low), V((C, ROWS), low), V((ROWS, C), low), V((C, ROWS), low), V((ROWS, C), full), V((ROWS, C), full),
                  V((TILES, 1, TILE), full), V((TILES, 1, TILE), full))

    def backward(x_ref, n1t_ref, qkv_ref, pt_ref, dproj_ref, dn_ref, bias_ref):
        loads = [pltpu.make_async_copy(x_hbm, x_ref, local.at[0]), pltpu.make_async_copy(n1t_hbm, n1t_ref, local.at[1])]
        fetch = [pltpu.make_async_copy(qkv_hbm.at[g], qkv_ref.at[g % 2], local.at[2 + g % 2]) for g in range(GROUPS)]
        fetch[0].start()
        pltpu.make_async_copy(pt_hbm.at[0], pt_ref.at[0], local.at[4]).start()
        fetch[1].start()
        for load in loads:
            load.start()
        bias_ref[...] = jnp.zeros_like(bias_ref)
        dn_ref[...] = jnp.zeros_like(dn_ref)
        for part in range(3):
            dproj_ref[part, rows_all:, :] = jnp.zeros((ROWS - rows_all, GCOLS), low)
        for g in range(GROUPS):
            cols = slice(g * GCOLS, (g + 1) * GCOLS)
            held = qkv_ref.at[g % 2]
            fetch[g].wait()

            def window(w, carry, g=g, cols=cols, held=held):
                hook_window(BACKWARD, g, w)
                rows = window_rows(w)
                n = g * windows + w
                slot = n % 2

                @pl.when(n + 1 < GROUPS * windows)
                def _():
                    pltpu.make_async_copy(pt_hbm.at[n + 1], pt_ref.at[1 - slot], local.at[5 - slot]).start()

                pltpu.make_async_copy(pt_hbm.at[n], pt_ref.at[slot], local.at[4 + slot]).wait()
                q = held[0, rows, :]
                k = held[1, rows, :]
                v = held[2, rows, :]
                p = pt_ref[slot]
                do = diag(o_ref[rows, cols], mask_ref)
                dp = dot_nt(v, do)
                dv = dot(p, do).astype(low)
                pf = p.astype(full)
                ds = (pf * (dp - jnp.sum(pf * dp, 0, keepdims=True))).astype(low)
                bias_ref[g] += ds.astype(full)
                dproj_ref[1, rows, :] = dot(ds, diag(q, mask_ref)).astype(low)
                dq = (undiag(k.T, ds, mask_ref) * (HEAD_DIM**-0.5)).astype(low)
                dproj_ref[0, rows, :] = dq
                dproj_ref[2, rows, :] = dv
                sums_ref[2:3, cols] += jnp.sum(dq.astype(full), 0, keepdims=True)
                sums_ref[3:4, cols] += jnp.sum(dv.astype(full), 0, keepdims=True)
                return carry

            lax.fori_loop(0, windows, window, 0)
            if g + 2 < GROUPS:
                fetch[g + 2].start()
            if g == 0:
                for load in loads:
                    load.wait()
            jobs[W_Q[g]].close()
            for part in range(3):
                d = dproj_ref[part]
                dn_ref[...] += dot_nt(d, flat(wq[g, part]))
                wq[g, part] = blocks(dot(n1t_ref[...], d).astype(low), OWNERS)
                if g == GROUPS - 1:
                    run(G_LAST[part], START)
            if g < GROUPS - 1:
                run(G_Q[g], START)
        hook(LAST_STEPS, 0)

        def last_norm(grad_ref):
            def finish(w, carry):
                rows = window_rows(w)
                slot = w % 2
                xhat, scale = norm_parts(x_ref[rows, :].astype(full))
                dn = dn_ref[rows, :]
                save = pltpu.make_async_copy(grad_ref.at[slot], grad_hbm.at[rows], local.at[4 + slot])

                @pl.when(w >= 2)
                def _():
                    save.wait()

                grad_ref[slot] = x1_ref[rows, :] + norm_back(xhat, scale, dn, vec_ref[0:1, :])
                save.start()
                sums_ref[0:1, :] += jnp.sum(dn * xhat, 0, keepdims=True)
                sums_ref[1:2, :] += jnp.sum(dn, 0, keepdims=True)
                return carry

            lax.fori_loop(0, windows, finish, 0)
            hook(LAST_STEPS, 1)
            for slot in range(2):
                pltpu.make_async_copy(grad_ref.at[slot], grad_hbm.at[pl.ds(0, TOK)], local.at[4 + slot]).wait()

        pl.run_scoped(last_norm, V((2, TOK, C), full))
        hook(LAST_STEPS, 2)

        def table(tmp_ref):
            pack_small(sums_ref[...], table_grad(line_ref, tmp_ref, bias_ref), terms_ref)

        pl.run_scoped(table, V((2, TOK * HEADS, 128), full))
        run(G_S, START)
        hook(LAST_STEPS, 3)
        for stage in range(len(Reduce.STAGES)):
            for name in G_ALL:
                if stage < len(jobs[name].STAGES):
                    run(name, stage)

    pl.run_scoped(backward, V((rows_all, C), low), V((C, ROWS), low), V((2, 3, ROWS, GCOLS), low), V((2, TOK, PACK), low), V((3, ROWS, GCOLS), low),
                  V((ROWS, C), full), V((GROUPS, TOK, PACK), full))
    jobs[W_U[-1]].close()
    jobs[W_D[-1]].close()
    for i in range(1, OWNERS):
        await_bytes(small.at[mine], small_sems.at[i])
    for name in G_ALL:
        jobs[name].close()


def shape(dims, kind):
    return jax.ShapeDtypeStruct(dims, kind)


def adamw(weight, moment, second, gradient, step_rate):
    moment_new = beta_one * moment + (1.0 - beta_one) * gradient
    second_new = beta_two * second + (1.0 - beta_two) * gradient * gradient
    update = (
        moment_new
        / (1.0 - beta_one**STEP)
        / (jnp.sqrt(second_new / (1.0 - beta_two**STEP)) + adam_eps)
    )
    weight_new = weight * (1.0 - step_rate * weight_decay) - step_rate * update
    return (weight_new, moment_new, second_new)


def update_kernel(*refs):
    gq, gp, gu, gd, gs = refs[:5]
    ins = [refs[5 + 3 * i : 8 + 3 * i] for i in range(6)]
    outs = [refs[23 + 4 * i : 27 + 4 * i] for i in range(4)] + [refs[39:42], refs[42:45]]

    def piece(which, place, gradient):
        new = adamw(*(ref[place] for ref in ins[which]), gradient, step_rates[which])
        for ref, value in zip(outs[which], new):
            ref[place] = value
        if which < 4:
            outs[which][3][place] = new[0].astype(low)

    for part in range(3):
        for g in range(GROUPS):
            left = part * C + g * GCOLS
            piece(0, (slice(None), slice(left, left + GCOLS)), gq[g, part].astype(full))
    piece(1, (slice(None), slice(None)), gp[...].astype(full))
    for t in range(TILES):
        for s in range(OWNERS):
            left = (MLP // OWNERS) * s + 128 * t
            piece(2, (slice(None), slice(left, left + 128)), gu[t, :, s * 128 : (s + 1) * 128].astype(full))
    piece(3, (slice(None), slice(None)), gd[0].astype(full))

    @pl.when(pl.program_id(0) == 0)
    def _():
        every = (slice(None), slice(None))
        piece(4, every, gs[0:12, 0:OWNED])
        piece(5, every, gs[16:40, 0 : ins[5][0].shape[1]])


def update(gq, gp, gu, gd, gs, states):
    steps = OWNED // 16

    def rows_of(array):
        tall = array.shape[0] // steps
        return pl.BlockSpec((tall, array.shape[1]), lambda i: (i, 0))

    def whole(array):
        return pl.BlockSpec(array.shape, lambda i: (0, 0))

    per_tile = 128 * TILES // steps
    specs = [
        pl.BlockSpec((GROUPS, 3, 16, GCOLS), lambda i: (0, 0, i, 0)),
        pl.BlockSpec((16, C), lambda i: (i, 0)),
        pl.BlockSpec((TILES, 16, TILE), lambda i: (0, i, 0)),
        pl.BlockSpec((1, per_tile, C), lambda i: (i // (128 // per_tile), i % (128 // per_tile), 0)),
        whole(gs),
    ]
    out_shapes, out_specs = [], []
    for i, group in enumerate(states):
        for array in group:
            specs.append(rows_of(array) if i < 4 else whole(array))
            out_shapes.append(shape(array.shape, full))
            out_specs.append(specs[-1])
        if i < 4:
            out_shapes.append(shape(group[0].shape, low))
            out_specs.append(rows_of(group[0]))
    return pl.pallas_call(
        update_kernel,
        grid=(steps,),
        in_specs=specs,
        out_specs=out_specs,
        out_shape=out_shapes,
        compiler_params=pltpu.CompilerParams(vmem_limit_bytes=63 * MIB),
        name="update",
    )(gq, gp, gu, gd, gs, *[array for group in states for array in group])


def shards(
    tokens, out_grad, window_count,
    qkv_weight, qkv_first, qkv_second,
    output_weight, output_first, output_second,
    up_weight, up_first, up_second,
    down_weight, down_first, down_second,
    vectors, vector_first, vector_second,
    bias_table, table_first, table_second,
):
    windows = tokens.shape[0]
    rows = windows * TOK
    V = pltpu.VMEM
    D = pltpu.SemaphoreType.DMA
    live = (jnp.arange(windows) < window_count[0]).astype(full)
    hbm = pl.BlockSpec(memory_space=pl.ANY)
    vmem = pl.BlockSpec(memory_space=pltpu.VMEM)
    result = pl.pallas_call(
        functools.partial(layer_kernel, windows),
        out_shape=[
            shape((rows, C), low), shape((rows, C), full),
            shape((GROUPS, 3, OWNED, GCOLS), low), shape((OWNED, C), low), shape((TILES, OWNED, TILE), low), shape((TILES, 128, C), low),
            shape((40, 128), full),
            shape((GROUPS, 3, ROWS, GCOLS), low), shape((GROUPS * windows, TOK, PACK), low), shape((C, ROWS), low)],
        in_specs=[hbm, hbm, pl.BlockSpec(memory_space=pltpu.SMEM)] + [hbm] * 4 + [vmem] * 4,
        out_specs=[hbm, hbm] + [vmem] * 5 + [hbm] * 3,
        scratch_shapes=[
            V((GROUPS, 3, OWNERS, OWNED, GCOLS), low), V((OWNERS, OWNED, C), low), V((SLOTS, OWNERS, OWNED, TILE), low),
            V((SLOTS, OWNERS, 128, C), low), V((OWNERS, 48, 128), low), V((ROWS, C), low), V((rows, C), full), V((16, C), full), V((16, C), full),
            V((OWNERS, 40, 128), full)]
        + reduce_scratch()
        + [D((GATHERS, Gather.SEMS)), D((REDUCES, Reduce.SEMS)), D((2 * OWNERS,)), D((ReduceSmall.SEMS,)), D((6,))],
        compiler_params=pltpu.CompilerParams(vmem_limit_bytes=63 * MIB, collective_id=0, has_side_effects=True),
        name="layer",
    )(tokens.reshape(rows, C), out_grad.reshape(rows, C), live, qkv_weight, output_weight, up_weight, down_weight, vectors, bias_table.T,
      jnp.asarray(line_matrix(), low), jnp.asarray(head_masks(), low))
    out, grad, gq, gp, gu, gd, gs = result[:7]
    new = update(gq, gp, gu, gd, gs, (
        (qkv_weight, qkv_first, qkv_second), (output_weight, output_first, output_second), (up_weight, up_first, up_second),
        (down_weight, down_first, down_second), (vectors, vector_first, vector_second), (bias_table.T, table_first.T, table_second.T)))
    return (out.reshape(tokens.shape), grad.reshape(tokens.shape), *new[:-3], *(array.T for array in new[-3:]))


def vmem_call(body, outs, scratch, args, name, limit=60, **params):
    spec = pl.BlockSpec(memory_space=pltpu.VMEM)
    return pl.pallas_call(
        body,
        out_shape=outs,
        in_specs=[pl.BlockSpec(memory_space=pltpu.SMEM) if a.dtype == full and a.ndim == 1 else spec for a in args],
        out_specs=[spec] * len(outs),
        scratch_shapes=scratch,
        compiler_params=pltpu.CompilerParams(vmem_limit_bytes=limit * MIB, **params),
        name=name,
    )(*args)


def local_step(tokens, out_grad, window_count, small, wq, wp, up, down):
    windows = tokens.shape[0]
    rows = windows * TOK
    owned = C // OWNERS
    V = pltpu.VMEM
    x = tokens.reshape(rows, C)
    dy = out_grad.reshape(rows, C)
    live = (jnp.arange(windows) < window_count[0]).astype(full)
    line = jnp.asarray(line_matrix(), low)
    masks = jnp.asarray(head_masks(), low)
    qkv, pt, o, x1, n1t, vec = vmem_call(
        functools.partial(attention_forward, windows),
        [shape((9, ROWS, GCOLS), low), shape((GROUPS, windows, TOK, PACK), low), shape((ROWS, C), low), shape((rows, C), full), shape((C, ROWS), low),
         shape((16, C), full)],
        [V((ROWS, C), low), V((GROUPS, TOK, PACK), full), V((2, TOK * HEADS, 128), full)],
        (x, small, line, masks, wq, wp), "attention_forward")
    out, dx1, do, gup, gdown, gout, sums = vmem_call(
        functools.partial(feed_forward, windows),
        [shape((rows, C), low), shape((ROWS, C), full), shape((rows, C), low), shape((TILES, OWNERS, owned, TILE), low),
         shape((TILES, OWNERS, C, 128), low), shape((OWNERS, owned, C), low), shape((16, C), full)],
        [V((ROWS, C), low), V((C, ROWS), low), V((ROWS, C), low), V((C, ROWS), low), V((ROWS, C), full), V((ROWS, C), full),
         V((TILES, 1, TILE), full), V((TILES, 1, TILE), full)],
        (x1, dy, live, vec, up, down, wp, o), "feed_forward")
    gq, gsmall, grad = vmem_call(
        functools.partial(attention_backward, windows),
        [shape((GROUPS, 3, OWNERS, owned, GCOLS), low), shape((OWNERS, 40, 128), full), shape((rows, C), full)],
        [V((16, C), full), V((GROUPS, TOK, PACK), full), V((2, TOK * HEADS, 128), full), V((3, ROWS, GCOLS), low), V((ROWS, C), full)],
        (x, vec, line, masks, wq, qkv, pt, do, dx1, n1t, sums), "attention_backward")
    return out.reshape(tokens.shape), grad.reshape(tokens.shape), gq, gout, gup, gdown, gsmall


def shards_general(
    tokens, out_grad, window_count,
    qkv_weight, qkv_first, qkv_second,
    output_weight, output_first, output_second,
    up_weight, up_first, up_second,
    down_weight, down_first, down_second,
    vectors, vector_first, vector_second,
    bias_table, table_first, table_second,
):
    gather = functools.partial(lax.all_gather, axis_name="shard", tiled=True)
    scatter = functools.partial(lax.psum_scatter, axis_name="shard", tiled=True)
    owned = C // OWNERS
    wq = gather(qkv_weight.astype(low), axis=0).reshape(OWNERS, owned, 3, GROUPS, GCOLS).transpose(3, 2, 0, 1, 4)
    wp = gather(output_weight.astype(low), axis=0).reshape(OWNERS, owned, C)
    up = gather(up_weight.astype(low), axis=0).reshape(OWNERS, owned, OWNERS, TILES, 128).transpose(3, 0, 1, 2, 4)
    up = up.reshape(TILES, OWNERS, owned, TILE)
    down = gather(down_weight.astype(low), axis=0).reshape(OWNERS, TILES, 128, C).transpose(1, 0, 2, 3)
    vec = gather(vectors.astype(low), axis=1)
    tab = gather(bias_table.astype(low), axis=0)
    table_rows = tab.shape[0]
    count = TAB_ROWS // OWNERS
    vec = vec.reshape(12, OWNERS, owned).transpose(1, 0, 2)
    tab = tab[:TAB_ROWS].reshape(OWNERS, count, HEADS).transpose(0, 2, 1)
    small = jnp.concatenate([jnp.pad(vec, ((0, 0), (0, 4), (0, 128 - owned))), jnp.pad(tab, ((0, 0), (0, 8), (0, 128 - count)))], 1)
    out, grad, gq, gp, gu, gd, gs = local_step(tokens, out_grad, window_count, small, wq, wp, up, down)
    gq = gq.astype(full).transpose(2, 3, 1, 0, 4).reshape(C, 3 * C)
    gu = gu.astype(full).reshape(TILES, C, OWNERS, 128).transpose(1, 2, 0, 3).reshape(C, MLP)
    gd = gd.astype(full).transpose(1, 0, 3, 2).reshape(MLP, C)
    gv = gs[:, :12, :owned].transpose(1, 0, 2).reshape(12, C)
    gb = gs[:, 16:40, :count].transpose(0, 2, 1).reshape(TAB_ROWS, HEADS)
    gb = jnp.pad(gb, ((0, table_rows - TAB_ROWS), (0, 0)))
    totals = lax.psum(
        (scatter(gq, scatter_dimension=0), scatter(gp.astype(full).reshape(C, C), scatter_dimension=0), scatter(gu, scatter_dimension=0),
         scatter(gd, scatter_dimension=0), scatter(gv, scatter_dimension=1), scatter(gb, scatter_dimension=0)), "rep")
    states = (
        (qkv_weight, qkv_first, qkv_second), (output_weight, output_first, output_second), (up_weight, up_first, up_second),
        (down_weight, down_first, down_second), (vectors, vector_first, vector_second), (bias_table, table_first, table_second))
    results = [out, grad]
    for i, (state, total, rate) in enumerate(zip(states, totals, step_rates)):
        new = adamw(*state, total, rate)
        results += [*new, new[0].astype(low)] if i < 4 else [*new]
    return tuple(results)


def solution(mesh):
    wins = P(("rep", "shard"), None, None)
    rows = P("shard", None)
    cols = P(None, "shard")
    fits = mesh.shape["rep"] == REPS and mesh.shape["shard"] == OWNERS
    return jax.shard_map(
        shards if fits else shards_general,
        mesh=mesh,
        in_specs=(wins, wins, P(("rep", "shard"))) + (rows,) * 12 + (cols,) * 3 + (rows,) * 3,
        out_specs=(wins, wins) + (rows,) * 16 + (cols,) * 3 + (rows,) * 3,
        check_vma=False,
    )
```

```python
import functools
import math

import jax
import jax.numpy as jnp
import numpy as np
from jax import lax
from jax.experimental import pallas as pl
from jax.experimental.pallas import tpu as pltpu
from jax.sharding import PartitionSpec as P

C = 768
HEADS = 24
MLP = 3072
WIN = 12
STEP = 5
HEAD_DIM = 32
SPAN = 2 * WIN - 1
TOK = WIN * WIN
TAB_ROWS = 536
ROWS = 1024
GROUPS = 3
GCOLS = 256
GHEADS = 8
PACK = GHEADS * TOK
TAB_LANES = 640
TILES = 3
TILE = MLP // TILES
SUB = 512
LINE = 384
MIB = 1 << 20

beta_one = 0.5
beta_two = 0.6
weight_decay = 0.05
adam_eps = 1e-08
norm_eps = 1e-05
step_rates = (0.04, 0.15, 0.04, 0.02, 0.2, 1.0)
low = jnp.bfloat16
full = jnp.float32
NT = (((1,), (1,)), ((), ()))


def dot(a, b):
    return jnp.dot(a, b, preferred_element_type=full)


def dot_nt(a, b):
    return lax.dot_general(a, b, NT, preferred_element_type=full)


def line_matrix():
    out = np.zeros((TAB_LANES, LINE), np.float32)
    col = np.arange(SPAN * WIN)
    out[(col // WIN) * SPAN + col % WIN + WIN - 1, col] = 1.0
    return out


def head_masks():
    lane = np.arange(GCOLS) // HEAD_DIM
    one = (lane[None, :] == np.arange(GHEADS)[:, None]).astype(np.float32)
    return np.broadcast_to(one[:, None, :], (GHEADS, 16, GCOLS))


def norm_parts(z):
    mean = jnp.sum(z, -1, keepdims=True) * (1.0 / C)
    center = z - mean
    spread = jnp.sum(center * center, -1, keepdims=True) * (1.0 / C)
    scale = lax.rsqrt(spread + norm_eps)
    return center * scale, scale


def norm_back(xhat, scale, dn, gain):
    g = dn * gain
    m1 = jnp.sum(g, -1, keepdims=True) * (1.0 / C)
    m2 = jnp.sum(g * xhat, -1, keepdims=True) * (1.0 / C)
    return scale * (g - m1 - xhat * m2)


def diag(x, mask_ref):
    head = x[0:128].reshape(8, 16, GCOLS)
    tail = x[128:144]
    parts = []
    for h in range(GHEADS):
        parts.append((head * mask_ref[h][None]).reshape(128, GCOLS))
    for h in range(GHEADS):
        parts.append(tail * mask_ref[h])
    return jnp.concatenate(parts, 0)


def undiag(xt, m, mask_ref):
    main = []
    for h in range(0, GHEADS, 2):
        r = dot(xt[h * HEAD_DIM : (h + 2) * HEAD_DIM], m[:, h * 128 : (h + 2) * 128])
        main.append(r[0:HEAD_DIM, 0:128])
        main.append(r[HEAD_DIM : 2 * HEAD_DIM, 128:256])
    main = jnp.concatenate(main, 0)
    rest = dot(xt, m[:, GHEADS * 128 :])
    rest_t = rest.T.reshape(GHEADS, 16, GCOLS)
    keep = mask_ref[...].astype(full)
    return jnp.concatenate([main.T, jnp.sum(rest_t * keep, 0)], 0)


def flat(x):
    return x.reshape(x.shape[0] * x.shape[1], x.shape[2])


def blocks(x, owners):
    return x.reshape(owners, x.shape[0] // owners, x.shape[1])


def hidden_place(t, s):
    at = (MLP // GHEADS) * s + 128 * t
    return 8 + at // C, at % C


def unpack_small(small_ref, vec_ref):
    owners = small_ref.shape[0]
    width = C // owners
    count = TAB_ROWS // owners
    vec = jnp.zeros((16, C), full)
    tab = jnp.zeros((HEADS, TAB_LANES), full)
    lane = lax.broadcasted_iota(jnp.int32, (16, 128), 1)
    lane_tab = lax.broadcasted_iota(jnp.int32, (HEADS, 128), 1)
    for s in range(owners):
        piece = small_ref[s].astype(full)
        part = jnp.where(lane < width, piece[0:16], 0.0)
        part = jnp.concatenate([part, jnp.zeros((16, C - 128), full)], 1)
        vec = vec + (pltpu.roll(part, width * s, 1) if s else part)
        part = jnp.where(lane_tab < count, piece[16 : 16 + HEADS], 0.0)
        part = jnp.concatenate([part, jnp.zeros((HEADS, TAB_LANES - 128), full)], 1)
        tab = tab + (pltpu.roll(part, count * s, 1) if s else part)
    vec_ref[...] = vec
    return tab


def pack_small(vec, tab, out_ref):
    owners = out_ref.shape[0]
    width = C // owners
    count = TAB_ROWS // owners
    for s in range(owners):
        out_ref[s, 0:16, :] = (pltpu.roll(vec, C - width * s, 1) if s else vec)[:, 0:128]
        out_ref[s, 16:40, :] = (pltpu.roll(tab, TAB_LANES - count * s, 1) if s else tab)[:, 0:128]


def spread_table(tab, line_ref, tmp_ref):
    def column(cj, carry):
        shifted = pltpu.roll(tab, cj, 1)
        line = dot(shifted.astype(low), line_ref[...])
        for rj in range(WIN):
            cut = (WIN - 1 - rj) * WIN
            part = pltpu.roll(line, LINE - cut, 1) if cut else line
            row = pl.multiple_of((rj * WIN + cj) * HEADS, 8)
            tmp_ref[0, pl.ds(row, HEADS), :] = part[:, 0:128]
            tmp_ref[1, pl.ds(row, HEADS), :] = part[:, 128:256]
        return carry

    lax.fori_loop(0, WIN, column, 0)


def place_bias(tmp_ref, bias_ref):
    lane = lax.broadcasted_iota(jnp.int32, (TOK, 128), 1)
    for g in range(GROUPS):
        rest = jnp.zeros((TOK, 128), full)
        for h in range(GHEADS):
            at = pl.ds(g * GHEADS + h, TOK, stride=HEADS)
            bias_ref[g, :, h * 128 : (h + 1) * 128] = tmp_ref[0, at, :]
            piece = tmp_ref[1, at, :]
            piece = pltpu.roll(piece, 16 * h, 1) if h else piece
            rest = jnp.where((lane >= 16 * h) & (lane < 16 * h + 16), piece, rest)
        bias_ref[g, :, GHEADS * 128 :] = rest


def table_grad(line_ref, tmp_ref, bias_ref):
    lane = lax.broadcasted_iota(jnp.int32, (TOK, 128), 1)
    for g in range(GROUPS):
        rest = bias_ref[g, :, GHEADS * 128 :]
        for h in range(GHEADS):
            at = pl.ds(g * GHEADS + h, TOK, stride=HEADS)
            tmp_ref[0, at, :] = bias_ref[g, :, h * 128 : (h + 1) * 128]
            piece = pltpu.roll(rest, 128 - 16 * h, 1) if h else rest
            tmp_ref[1, at, :] = jnp.where(lane < 16, piece, 0.0)

    def column(cj, total):
        line = jnp.zeros((HEADS, LINE), full)
        for rj in range(WIN):
            cut = (WIN - 1 - rj) * WIN
            row = pl.multiple_of((rj * WIN + cj) * HEADS, 8)
            part = jnp.concatenate([tmp_ref[0, pl.ds(row, HEADS), :], tmp_ref[1, pl.ds(row, HEADS), :], jnp.zeros((HEADS, 128), full)], 1)
            line = line + (pltpu.roll(part, cut, 1) if cut else part)
        high = line.astype(low)
        rest = (line - high.astype(full)).astype(low)
        spread = dot_nt(high, line_ref[...]) + dot_nt(rest, line_ref[...])
        return total + pltpu.roll(spread, TAB_LANES - cj, 1)

    return lax.fori_loop(0, WIN, column, jnp.zeros((HEADS, TAB_LANES), full))


def transpose_rows(src_ref, dst_ref):
    def block(i, carry):
        at = pl.multiple_of(i * 128, 128)
        dst_ref[:, pl.ds(at, 128)] = src_ref[pl.ds(at, 128), :].T
        return carry

    lax.fori_loop(0, ROWS // 128, block, 0)


def window_rows(w):
    return pl.ds(pl.multiple_of(w * TOK, 16), TOK)


def zero_tail(ref, windows):
    at = windows * TOK
    ref[at:ROWS, :] = jnp.zeros((ROWS - at, ref.shape[1]), ref.dtype)


def attention_forward(windows, x_ref, small_ref, line_ref, mask_ref, wq_ref, wp_ref,
                      qkv_ref, pt_ref, o_ref, x1_ref, n1t_ref, vec_ref, n1_ref, bias_ref, tmp_ref):
    tab = unpack_small(small_ref, vec_ref)
    spread_table(tab, line_ref, tmp_ref)
    place_bias(tmp_ref, bias_ref)
    zero_tail(n1_ref, windows)
    zero_tail(o_ref, windows)

    def first_norm(w, carry):
        xhat, _ = norm_parts(x_ref[window_rows(w), :].astype(full))
        n1_ref[window_rows(w), :] = (xhat * vec_ref[0:1, :] + vec_ref[1:2, :]).astype(low)
        return carry

    lax.fori_loop(0, windows, first_norm, 0)
    transpose_rows(n1_ref, n1t_ref)

    def group(g, carry):
        cols = pl.ds(pl.multiple_of(g * GCOLS, GCOLS), GCOLS)
        n1 = n1_ref[...]
        qkv_ref[g] = ((dot(n1, flat(wq_ref[g, 0])) + vec_ref[2:3, cols]) * (HEAD_DIM**-0.5)).astype(low)
        qkv_ref[GROUPS + g] = dot(n1, flat(wq_ref[g, 1])).astype(low)
        qkv_ref[2 * GROUPS + g] = (dot(n1, flat(wq_ref[g, 2])) + vec_ref[3:4, cols]).astype(low)

        def window(w, inner):
            rows = window_rows(w)
            q = qkv_ref[g, rows, :]
            k = qkv_ref[GROUPS + g, rows, :]
            v = qkv_ref[2 * GROUPS + g, rows, :]
            s = dot_nt(k, diag(q, mask_ref)) + bias_ref[g]
            e = jnp.exp(s - jnp.max(s, 0, keepdims=True))
            p = (e * (1.0 / jnp.sum(e, 0, keepdims=True))).astype(low)
            pt_ref[g, w] = p
            o_ref[rows, cols] = undiag(v.T, p, mask_ref).astype(low)
            return inner

        lax.fori_loop(0, windows, window, 0)
        return carry

    lax.fori_loop(0, GROUPS, group, 0)

    def output(w, carry):
        rows = window_rows(w)
        branch = dot(o_ref[rows, :], flat(wp_ref[...])) + vec_ref[4:5, :]
        x1_ref[rows, :] = x_ref[rows, :].astype(full) + branch
        return carry

    lax.fori_loop(0, windows, output, 0)


def gelu_both(h):
    c = math.sqrt(2.0 / math.pi)
    square = h * h
    t = jnp.tanh(h * (c + (c * 0.044715) * square))
    half = 0.5 + 0.5 * t
    slope = half + (0.5 * h) * (1.0 - t * t) * (c + (3.0 * c * 0.044715) * square)
    return h * half, slope


def feed_forward(windows, x1_ref, dy_ref, live_ref, vec_ref, up_ref, down_ref, wp_ref, o_ref,
                 out_ref, dx1_ref, do_ref, gup_ref, gdown_ref, gout_ref, sums_ref,
                 n2_ref, n2t_ref, dy2_ref, dyt_ref, y_ref, dn_ref, bu_ref, bsum_ref):
    zero_tail(n2_ref, windows)
    zero_tail(dy2_ref, windows)

    def second_norm(w, carry):
        rows = window_rows(w)
        xhat, _ = norm_parts(x1_ref[rows, :])
        n2_ref[rows, :] = (xhat * vec_ref[5:6, :] + vec_ref[6:7, :]).astype(low)
        dy2_ref[rows, :] = (dy_ref[rows, :].astype(full) * live_ref[w]).astype(low)
        return carry

    lax.fori_loop(0, windows, second_norm, 0)
    transpose_rows(n2_ref, n2t_ref)
    transpose_rows(dy2_ref, dyt_ref)
    y_ref[...] = jnp.zeros_like(y_ref)
    dn_ref[...] = jnp.zeros_like(dn_ref)
    owners = gup_ref.shape[1]
    for t in range(TILES):
        for s in range(TILE // 128):
            row, at = hidden_place(t, s)
            bu_ref[t, :, s * 128 : (s + 1) * 128] = vec_ref[row : row + 1, at : at + 128]

    def step(t, carry):
        for part in range(TILE // SUB):
            cols = slice(part * SUB, (part + 1) * SUB)
            up = flat(up_ref[t, :, :, cols])
            down = flat(down_ref[t, part * SUB // 128 : (part + 1) * SUB // 128])
            h = dot(n2_ref[...], up) + bu_ref[t, :, cols]
            da = dot_nt(dy2_ref[...], down)
            act, slope = gelu_both(h)
            a = act.astype(low)
            dh = (da * slope).astype(low)
            bsum_ref[t, :, cols] = jnp.sum(dh.astype(full), 0, keepdims=True)
            y_ref[...] += dot(a, down)
            dn_ref[...] += dot_nt(dh, up)
            gd = dot(dyt_ref[...], a).astype(low)
            for b in range(SUB // 128):
                gdown_ref[t, part * SUB // 128 + b] = gd[:, b * 128 : (b + 1) * 128]
            gup_ref[t, :, :, cols] = blocks(dot(n2t_ref[...], dh).astype(low), owners)
        return carry

    lax.fori_loop(0, TILES, step, 0)
    sums_ref[...] = jnp.zeros_like(sums_ref)
    for t in range(TILES):
        for s in range(TILE // 128):
            row, at = hidden_place(t, s)
            sums_ref[row : row + 1, at : at + 128] = bsum_ref[t, :, s * 128 : (s + 1) * 128]
    zero_tail(dx1_ref, windows)

    def finish(w, carry):
        rows = window_rows(w)
        x1 = x1_ref[rows, :]
        out_ref[rows, :] = ((x1 + y_ref[rows, :] + vec_ref[7:8, :]) * live_ref[w]).astype(low)
        xhat, scale = norm_parts(x1)
        dn = dn_ref[rows, :]
        dy = dy2_ref[rows, :].astype(full)
        dx1 = dy + norm_back(xhat, scale, dn, vec_ref[5:6, :])
        dx1_ref[rows, :] = dx1
        dr = dx1.astype(low)
        n2_ref[rows, :] = dr
        do_ref[rows, :] = dot_nt(dr, flat(wp_ref[...])).astype(low)
        sums_ref[4:5, :] += jnp.sum(dr.astype(full), 0, keepdims=True)
        sums_ref[5:6, :] += jnp.sum(dn * xhat, 0, keepdims=True)
        sums_ref[6:7, :] += jnp.sum(dn, 0, keepdims=True)
        sums_ref[7:8, :] += jnp.sum(dy, 0, keepdims=True)
        return carry

    lax.fori_loop(0, windows, finish, 0)
    transpose_rows(o_ref, dyt_ref)
    for g in range(GROUPS):
        at = pl.ds(g * GCOLS, GCOLS)
        gout_ref[:, :, at] = blocks(dot(dyt_ref[...], n2_ref[:, at]).astype(low), gout_ref.shape[0])


def attention_backward(windows, x_ref, vec_ref, line_ref, mask_ref, wq_ref, qkv_ref, pt_ref, do_ref, dx1_ref, n1t_ref, sums_in_ref,
                       gq_ref, gsmall_ref, grad_ref, sums_ref, bias_ref, tmp_ref, dproj_ref, dn_ref):
    bias_ref[...] = jnp.zeros_like(bias_ref)
    dn_ref[...] = jnp.zeros_like(dn_ref)
    sums_ref[...] = sums_in_ref[...]
    for part in range(3):
        dproj_ref[part, windows * TOK :, :] = jnp.zeros((ROWS - windows * TOK, GCOLS), low)

    def group(g, carry):
        cols = pl.ds(pl.multiple_of(g * GCOLS, GCOLS), GCOLS)

        def window(w, inner):
            rows = window_rows(w)
            q = qkv_ref[g, rows, :]
            k = qkv_ref[GROUPS + g, rows, :]
            v = qkv_ref[2 * GROUPS + g, rows, :]
            p = pt_ref[g, w]
            do = diag(do_ref[rows, cols], mask_ref)
            dp = dot_nt(v, do)
            dv = dot(p, do)
            pf = p.astype(full)
            ds = (pf * (dp - jnp.sum(pf * dp, 0, keepdims=True))).astype(low)
            bias_ref[g] += ds.astype(full)
            dk = dot(ds, diag(q, mask_ref))
            dq = undiag(k.T, ds, mask_ref) * (HEAD_DIM**-0.5)
            dq = dq.astype(low)
            dv = dv.astype(low)
            dproj_ref[0, rows, :] = dq
            dproj_ref[1, rows, :] = dk.astype(low)
            dproj_ref[2, rows, :] = dv
            sums_ref[2:3, cols] += jnp.sum(dq.astype(full), 0, keepdims=True)
            sums_ref[3:4, cols] += jnp.sum(dv.astype(full), 0, keepdims=True)
            return inner

        lax.fori_loop(0, windows, window, 0)
        for part in range(3):
            d = dproj_ref[part]
            gq_ref[g, part] = blocks(dot(n1t_ref[...], d).astype(low), gq_ref.shape[2])
            dn_ref[...] += dot_nt(d, flat(wq_ref[g, part]))
        return carry

    lax.fori_loop(0, GROUPS, group, 0)

    def finish(w, carry):
        rows = window_rows(w)
        xhat, scale = norm_parts(x_ref[rows, :].astype(full))
        dn = dn_ref[rows, :]
        grad_ref[rows, :] = dx1_ref[rows, :] + norm_back(xhat, scale, dn, vec_ref[0:1, :])
        sums_ref[0:1, :] += jnp.sum(dn * xhat, 0, keepdims=True)
        sums_ref[1:2, :] += jnp.sum(dn, 0, keepdims=True)
        return carry

    lax.fori_loop(0, windows, finish, 0)
    pack_small(sums_ref[...], table_grad(line_ref, tmp_ref, bias_ref), gsmall_ref)


MESH = pl.DeviceIdType.MESH
REPS = 4
OWNERS = 8
LINKS = OWNERS // 2


class Spot:
    def __init__(self):
        self.rep = lax.axis_index("rep")
        self.shard = lax.axis_index("shard")
        self.z = self.shard // 2
        self.core = self.shard % 2

    def sibling(self):
        return (self.rep, self.z * 2 + (1 - self.core))

    def along_z(self, step):
        return (self.rep, ((self.z + step) % LINKS) * 2 + self.core)

    def turned(self, axis):
        x, y = self.rep % 2, self.rep // 2
        return y * 2 + (1 - x) if axis == 0 else (1 - y) * 2 + x

    def beside(self, axis):
        return (self.turned(axis), self.shard)


def greet(spot):
    barrier = pltpu.get_barrier_semaphore()
    peers = [(spot.rep, (spot.shard + i) % OWNERS) for i in range(1, OWNERS)]
    peers += [((spot.rep + i) % REPS, spot.shard) for i in range(1, REPS)]
    for peer in peers:
        pl.semaphore_signal(barrier, inc=1, device_id=peer, device_id_type=MESH)
    return barrier, len(peers)


def send(src, dst, send_sem, recv_sem, peer):
    pltpu.make_async_remote_copy(src_ref=src, dst_ref=dst, send_sem=send_sem, recv_sem=recv_sem, device_id=peer, device_id_type=MESH).start()


def await_bytes(ref, sem):
    pltpu.make_async_copy(ref, ref, sem).wait()


def quarter(ref, rep):
    rows, cols = ref.shape[-2:]
    lead = (slice(None),) * (len(ref.shape) - 2)
    top = pl.multiple_of((rep // 2) * (rows // 2), 16)
    left = pl.multiple_of((rep % 2) * (cols // 2), 128)
    return ref.at[lead + (pl.ds(top, rows // 2), pl.ds(left, cols // 2))]


def half(ref, rep, axis):
    rows, cols = ref.shape[-2:]
    lead = (slice(None),) * (len(ref.shape) - 2)
    if axis == 0:
        left = pl.multiple_of((rep % 2) * (cols // 2), 128)
        return ref.at[lead + (slice(None), pl.ds(left, cols // 2))]
    top = pl.multiple_of((rep // 2) * (rows // 2), 16)
    return ref.at[lead + (pl.ds(top, rows // 2), slice(None))]


class Gather:
    KINDS = (LINKS - 1, LINKS - 1, LINKS - 1, LINKS - 1, LINKS)
    SEMS = 2 * sum(KINDS)
    STAGES = ("start", "across", "relay", "beside", "finish")

    def __init__(self, spot, place, axis, sems):
        self.spot, self.place, self.axis, self.sems = spot, place, axis, sems

    def sem(self, side, kind, i):
        return self.sems.at[side * (self.SEMS // 2) + sum(self.KINDS[:kind]) + i]

    def block(self, step):
        return self.place(((self.spot.z - step + LINKS) % LINKS) * 2 + self.spot.core)

    def other(self, step):
        return self.place(((self.spot.z - step + LINKS) % LINKS) * 2 + 1 - self.spot.core)

    def start(self):
        spot = self.spot
        mine = self.block(0)
        for i in range(1, LINKS):
            piece = quarter(mine, spot.rep)
            send(piece, piece, self.sem(0, 0, i - 1), self.sem(1, 0, i - 1), spot.along_z(i))
        send(mine, mine, self.sem(0, 4, 0), self.sem(1, 4, 0), spot.sibling())

    def across(self):
        spot = self.spot
        for i in range(1, LINKS):
            piece = quarter(self.block(i), spot.rep)
            await_bytes(piece, self.sem(1, 0, i - 1))
            for axis in (self.axis, 1 - self.axis):
                send(piece, piece, self.sem(0, 1 + axis, i - 1), self.sem(1, 1 + axis, i - 1), spot.beside(axis))

    def relay(self):
        spot = self.spot
        for i in range(1, LINKS):
            piece = quarter(self.block(i), spot.turned(self.axis))
            await_bytes(piece, self.sem(1, 1 + self.axis, i - 1))
            send(piece, piece, self.sem(0, 3, i - 1), self.sem(1, 3, i - 1), spot.beside(1 - self.axis))

    def beside(self):
        spot = self.spot
        for i in range(1, LINKS):
            block = self.block(i)
            piece = quarter(block, spot.rep)
            await_bytes(piece, self.sem(1, 2 - self.axis, i - 1))
            await_bytes(piece, self.sem(1, 3, i - 1))
            send(block, block, self.sem(0, 4, i), self.sem(1, 4, i), spot.sibling())

    def finish(self):
        for i in range(LINKS):
            await_bytes(self.other(i), self.sem(1, 4, i))

    def close(self):
        piece = quarter(self.block(0), self.spot.rep)
        for kind in range(4):
            for i in range(1, LINKS):
                await_bytes(piece, self.sem(0, kind, i - 1))
        for i in range(LINKS):
            await_bytes(self.block(i), self.sem(0, 4, i))


class Reduce:
    KINDS = (LINKS, 1, 1, LINKS - 1, REPS - 1)
    SEMS = 2 * sum(KINDS)
    STAGES = ("start", "first", "second", "along", "spread", "finish")

    def __init__(self, spot, place, out, core_sum, halves, quarters, links, axis, sems):
        self.spot, self.place, self.out, self.axis, self.sems = spot, place, out, axis, sems
        self.core_sum, self.halves, self.quarters, self.links = core_sum, halves, quarters, links

    def sem(self, side, kind, i):
        return self.sems.at[side * (self.SEMS // 2) + sum(self.KINDS[:kind]) + i]

    def start(self):
        spot = self.spot
        for z in range(LINKS):
            send(self.place(z * 2 + (1 - spot.core)), self.core_sum.at[z], self.sem(0, 0, z), self.sem(1, 0, z), spot.sibling())

    def first(self):
        spot = self.spot
        for z in range(LINKS):
            total = self.core_sum.at[z]
            await_bytes(total, self.sem(1, 0, z))
            total[...] = (total[...].astype(full) + self.place(z * 2 + spot.core)[...].astype(full)).astype(low)
        theirs = half(self.core_sum, spot.turned(self.axis), self.axis)
        send(theirs, self.halves, self.sem(0, 1, 0), self.sem(1, 1, 0), spot.beside(self.axis))

    def second(self):
        spot = self.spot
        await_bytes(self.halves, self.sem(1, 1, 0))
        mine = half(self.core_sum, spot.rep, self.axis)
        self.halves[...] = (self.halves[...].astype(full) + mine[...].astype(full)).astype(low)
        theirs = half(self.halves, spot.turned(1 - self.axis), 1 - self.axis)
        send(theirs, self.quarters, self.sem(0, 2, 0), self.sem(1, 2, 0), spot.beside(1 - self.axis))

    def along(self):
        spot = self.spot
        await_bytes(self.quarters, self.sem(1, 2, 0))
        mine = half(self.halves, spot.rep, 1 - self.axis)
        self.quarters[...] = (self.quarters[...].astype(full) + mine[...].astype(full)).astype(low)
        for i in range(1, LINKS):
            send(self.quarters.at[(spot.z + i) % LINKS], self.links.at[i - 1], self.sem(0, 3, i - 1), self.sem(1, 3, i - 1), spot.along_z(i))

    def spread(self):
        spot = self.spot
        total = self.quarters[spot.z].astype(full)
        for i in range(1, LINKS):
            await_bytes(self.links.at[i - 1], self.sem(1, 3, i - 1))
            total = total + self.links[i - 1].astype(full)
        mine = quarter(self.out, spot.rep)
        mine[...] = total.astype(low)
        for j in range(1, REPS):
            send(mine, mine, self.sem(0, 4, j - 1), self.sem(1, 4, j - 1), ((spot.rep + j) % REPS, spot.shard))

    def finish(self):
        for j in range(1, REPS):
            await_bytes(quarter(self.out, (self.spot.rep - j + REPS) % REPS), self.sem(1, 4, j - 1))

    def close(self):
        for z in range(LINKS):
            await_bytes(self.core_sum.at[z], self.sem(0, 0, z))
        await_bytes(self.halves, self.sem(0, 1, 0))
        await_bytes(self.quarters, self.sem(0, 2, 0))
        for i in range(1, LINKS):
            await_bytes(self.links.at[i - 1], self.sem(0, 3, i - 1))
        for j in range(1, REPS):
            await_bytes(quarter(self.out, self.spot.rep), self.sem(0, 4, j - 1))


class ReduceSmall:
    KINDS = (LINKS, LINKS - 1, REPS - 1)
    SEMS = 2 * sum(KINDS)
    STAGES = ("start", "first", "second", "along")

    def __init__(self, spot, terms, out, core_sum, links, parts, sems):
        self.spot, self.terms, self.out, self.core_sum, self.links, self.parts, self.sems = spot, terms, out, core_sum, links, parts, sems

    sem = Reduce.sem

    def start(self):
        spot = self.spot
        for z in range(LINKS):
            send(self.terms.at[z * 2 + (1 - spot.core)], self.core_sum.at[z], self.sem(0, 0, z), self.sem(1, 0, z), spot.sibling())

    def first(self):
        spot = self.spot
        for z in range(LINKS):
            await_bytes(self.core_sum.at[z], self.sem(1, 0, z))
            self.core_sum[z] = self.core_sum[z] + self.terms[z * 2 + spot.core]
        for i in range(1, LINKS):
            send(self.core_sum.at[(spot.z + i) % LINKS], self.links.at[i - 1], self.sem(0, 1, i - 1), self.sem(1, 1, i - 1), spot.along_z(i))

    def second(self):
        spot = self.spot
        total = self.core_sum[spot.z]
        for i in range(1, LINKS):
            await_bytes(self.links.at[i - 1], self.sem(1, 1, i - 1))
            total = total + self.links[i - 1]
        self.parts[spot.rep] = total
        mine = self.parts.at[spot.rep]
        for j in range(1, REPS):
            send(mine, mine, self.sem(0, 2, j - 1), self.sem(1, 2, j - 1), ((spot.rep + j) % REPS, spot.shard))

    def along(self):
        for j in range(1, REPS):
            await_bytes(self.parts.at[(self.spot.rep - j + REPS) % REPS], self.sem(1, 2, j - 1))
        total = self.parts[0]
        for j in range(1, REPS):
            total = total + self.parts[j]
        self.out[...] = total

    def close(self):
        for z in range(LINKS):
            await_bytes(self.core_sum.at[z], self.sem(0, 0, z))
        for i in range(1, LINKS):
            await_bytes(self.links.at[i - 1], self.sem(0, 1, i - 1))
        for j in range(1, REPS):
            await_bytes(self.parts.at[self.spot.rep], self.sem(0, 2, j - 1))


OWNED = C // OWNERS
SLOTS = TILES + 1
GATHERS = 2 * TILES + 1 + GROUPS
REDUCES = 2 * TILES + 1 + (GROUPS - 1) + 3
W_Q0, W_Q1, W_Q2, W_P, W_U0, W_D0, W_U1, W_D1, W_U2, W_D2 = W_ALL = range(10)
G_D0, G_U0, G_D1, G_U1, G_D2, G_U2, G_P, G_Q0, G_Q1, G_Q2, G_K2, G_V2, G_S = G_ALL = range(10, 23)
W_Q, W_U, W_D = (W_Q0, W_Q1, W_Q2), (W_U0, W_U1, W_U2), (W_D0, W_D1, W_D2)
G_D, G_U, G_Q, G_LAST = (G_D0, G_D1, G_D2), (G_U0, G_U1, G_U2), (G_Q0, G_Q1), (G_Q2, G_K2, G_V2)
START, ACROSS, RELAY, BESIDE, ARRIVED = range(5)
FIRST, SECOND, ALONG, SPREAD, SUMMED = range(1, 6)
BEFORE = {
    0: ((W_Q2, START), (W_P, START),),
    2: ((W_Q0, ACROSS), (W_U0, START),),
    4: ((W_Q0, RELAY), (W_Q1, ACROSS), (W_D0, START),),
}
FORWARD = {
    0: ((W_Q2, ACROSS), (W_Q1, RELAY), (W_U1, START), (W_P, ACROSS), (W_D1, START),),
    4: ((W_U0, ACROSS), (W_U2, START), (W_Q1, BESIDE),),
    6: ((W_Q2, RELAY), (W_P, RELAY),),
    7: ((W_D0, ACROSS), (W_D2, START),),
    9: ((W_Q2, BESIDE), (W_U0, RELAY),),
    11: ((W_P, BESIDE),),
    12: ((W_U1, ACROSS), (W_D0, RELAY),),
    14: ((W_U0, BESIDE),),
    15: ((W_D1, ACROSS),),
    18: ((W_U2, ACROSS),),
    19: ((W_U1, RELAY), (W_D0, BESIDE),),
}
MIDDLE = {
    0: ((W_D2, ACROSS), (W_D1, RELAY),),
    1: ((W_U2, RELAY),),
    2: ((W_U1, BESIDE),),
}
TILE_STEP = {
    1: ((W_D1, BESIDE), (W_U2, BESIDE), (W_D2, RELAY),),
    2: ((W_D2, BESIDE),),
    3: ((G_D0, FIRST), (G_U0, FIRST),),
    5: ((G_D0, SECOND), (G_U0, SECOND), (G_D1, FIRST), (G_U1, FIRST),),
}
AFTER_TILES = {
    0: ((G_D0, ALONG), (G_U0, ALONG),),
    2: ((G_D2, FIRST),),
    3: ((G_D0, SPREAD), (G_D1, SECOND), (G_U1, SECOND), (G_U2, FIRST),),
}
BACKWARD = {
    2: ((G_U0, SPREAD), (G_P, FIRST),),
    4: ((G_D1, ALONG),),
    5: ((G_D2, SECOND),),
    6: ((G_D0, SUMMED),),
    7: ((G_U1, ALONG),),
    8: ((G_D1, SPREAD), (G_U2, SECOND),),
    9: ((G_U0, SUMMED), (G_Q0, FIRST),),
    12: ((G_U1, SPREAD), (G_D2, ALONG),),
    13: ((G_P, SECOND),),
    14: ((G_D1, SUMMED),),
    15: ((G_Q0, SECOND),),
    16: ((G_D2, SPREAD), (G_U2, ALONG), (G_Q1, FIRST),),
    17: ((G_U1, SUMMED),),
    18: ((G_P, ALONG),),
    20: ((G_D2, SUMMED), (G_U2, SPREAD),),
}
LAST_STEPS = {
    0: ((G_Q0, ALONG), (G_P, SPREAD), (G_Q2, FIRST),),
    1: ((G_K2, FIRST), (G_V2, FIRST),),
    2: ((G_Q1, SECOND),),
    3: ((G_Q0, SPREAD), (G_U2, SUMMED), (G_Q2, SECOND),),
}


def chunk_shapes():
    out = []
    for _ in range(TILES):
        out += [(128, C), (OWNED, TILE)]
    return out + [(OWNED, C)] + [(3, OWNED, GCOLS)] * (GROUPS - 1) + [(OWNED, GCOLS)] * 3


def reduce_scratch():
    out = []
    for i, dims in enumerate(chunk_shapes()):
        *lead, rows, cols = dims
        near = (rows, cols // 2) if i % 2 == 0 else (rows // 2, cols)
        out.append(pltpu.VMEM((LINKS, *dims), low))
        out.append(pltpu.VMEM((LINKS, *lead, *near), low))
        out.append(pltpu.VMEM((LINKS, *lead, rows // 2, cols // 2), low))
        out.append(pltpu.VMEM((LINKS - 1, *lead, rows // 2, cols // 2), low))
    out += [pltpu.VMEM((LINKS, 40, 128), full), pltpu.VMEM((LINKS - 1, 40, 128), full), pltpu.VMEM((REPS, 40, 128), full)]
    return out


def layer_kernel(windows, x_hbm, dy_hbm, count_ref, q32, p32, u32, d32, vec_in, tab_in, line_ref, mask_ref,
                 out_hbm, grad_hbm, gq_out, gp_out, gu_out, gd_out, gs_out, qkv_hbm, pt_hbm, n1t_hbm, *scratch):
    wq, wp, up, down, small, o_ref, x1_ref, vec_ref, sums_ref, terms_ref = scratch[:10]
    gather_sems, reduce_sems, small_sems, small_reduce_sems, local = scratch[-5:]
    reduce_refs = scratch[10:-5]
    spot = Spot()
    rows_all = windows * TOK

    def live(w):
        return (w < count_ref[0]).astype(full)

    mine = spot.shard
    V = pltpu.VMEM

    jobs = {}
    places = [(W_Q[g], lambda s, g=g: wq.at[g, :, s]) for g in range(GROUPS)] + [(W_P, lambda s: wp.at[s])]
    for t in range(TILES):
        places += [(W_U[t], lambda s, t=t: up.at[t, s]), (W_D[t], lambda s, t=t: down.at[t, s])]
    for i, (name, place) in enumerate(places):
        jobs[name] = Gather(spot, place, i % 2, gather_sems.at[i])
    places = []
    for t in range(TILES):
        slot = (t + SLOTS - 1) % SLOTS
        places.append((G_D[t], lambda s, slot=slot: down.at[slot, s], gd_out.at[t]))
        places.append((G_U[t], lambda s, slot=slot: up.at[slot, s], gu_out.at[t]))
    places.append((G_P, lambda s: wp.at[s], gp_out))
    for g in range(GROUPS - 1):
        places.append((G_Q[g], lambda s, g=g: wq.at[g, :, s], gq_out.at[g]))
    for part in range(3):
        places.append((G_LAST[part], lambda s, part=part: wq.at[GROUPS - 1, part, s], gq_out.at[GROUPS - 1, part]))
    for i, (name, place, out) in enumerate(places):
        jobs[name] = Reduce(spot, place, out, *reduce_refs[4 * i : 4 * i + 4], i % 2, reduce_sems.at[i])
    jobs[G_S] = ReduceSmall(spot, terms_ref, gs_out, *reduce_refs[-3:], small_reduce_sems)

    done = {}

    def run(name, upto):
        for stage in range(done.get(name, 0), upto + 1):
            getattr(jobs[name], jobs[name].STAGES[stage])()
        done[name] = max(done.get(name, 0), upto + 1)

    def hook(table, place):
        for item in table.get(place, ()):
            run(*item)

    barrier, peers = greet(spot)

    def cast(q_v, p_v, u_v, d_v):
        loads = [pltpu.make_async_copy(a, b, local.at[i]) for i, (a, b) in enumerate(((q32, q_v), (p32, p_v), (u32, u_v), (d32, d_v)))]
        for load in loads:
            load.start()
        small[mine] = jnp.zeros((48, 128), low)
        pad = jnp.zeros((16, 128), full)
        vec_ref[:, 0:128] = pad
        vec_ref[0:12, 0:OWNED] = vec_in[...]
        small[mine, 0:16, :] = vec_ref[:, 0:128].astype(low)
        x1_ref[0:32, 0:128] = jnp.zeros((32, 128), full)
        x1_ref[0:HEADS, 0 : tab_in.shape[1]] = tab_in[...]
        small[mine, 16:48, :] = x1_ref[0:32, 0:128].astype(low)
        loads[0].wait()
        for g in range(GROUPS):
            for part in range(3):
                wq[g, part, mine] = q_v[:, part * C + g * GCOLS : part * C + (g + 1) * GCOLS].astype(low)
        pl.semaphore_wait(barrier, peers)
        for i in range(1, OWNERS):
            send(small.at[mine], small.at[mine], small_sems.at[i], small_sems.at[OWNERS + i], (spot.rep, (mine + i) % OWNERS))
        run(W_Q0, START)
        run(W_Q1, START)
        loads[1].wait()
        wp[mine] = p_v[...].astype(low)
        loads[2].wait()
        loads[3].wait()
        for t in range(TILES):
            for s in range(OWNERS):
                src = (MLP // OWNERS) * s + 128 * t
                up[t, mine, :, s * 128 : (s + 1) * 128] = u_v[:, src : src + 128].astype(low)
            down[t, mine] = d_v[t * 128 : (t + 1) * 128, :].astype(low)

    pl.run_scoped(cast, V((OWNED, 3 * C), full), V((OWNED, C), full), V((OWNED, MLP), full), V((TILES * 128, C), full))

    def forward(x_ref, n1_ref, n1t_ref, qkv_ref, pt_ref, bias_ref):
        load = pltpu.make_async_copy(x_hbm, x_ref, local.at[0])
        load.start()
        zero_tail(n1_ref, windows)
        zero_tail(o_ref, windows)
        for i in range(1, OWNERS):
            await_bytes(small.at[(mine - i + OWNERS) % OWNERS], small_sems.at[OWNERS + i])
        tab = unpack_small(small, vec_ref)
        hook(BEFORE, 0)
        load.wait()
        hook(BEFORE, 1)

        def first_norm(w, carry):
            xhat, _ = norm_parts(x_ref[window_rows(w), :].astype(full))
            n1_ref[window_rows(w), :] = (xhat * vec_ref[0:1, :] + vec_ref[1:2, :]).astype(low)
            return carry

        lax.fori_loop(0, windows, first_norm, 0)
        hook(BEFORE, 2)
        transpose_rows(n1_ref, n1t_ref)
        save = pltpu.make_async_copy(n1t_ref, n1t_hbm, local.at[1])
        save.start()
        hook(BEFORE, 3)

        def bias(tmp_ref):
            spread_table(tab, line_ref, tmp_ref)
            hook(BEFORE, 4)
            place_bias(tmp_ref, bias_ref)

        pl.run_scoped(bias, V((2, TOK * HEADS, 128), full))
        for g in range(GROUPS):
            cols = slice(g * GCOLS, (g + 1) * GCOLS)
            held = qkv_ref.at[g % 2]
            if g >= 2:
                pltpu.make_async_copy(held, qkv_hbm.at[g - 2], local.at[2 + g % 2]).wait()
            run(W_Q[g], ARRIVED)
            n1 = n1_ref[...]
            held[0] = ((dot(n1, flat(wq[g, 0])) + vec_ref[2:3, cols]) * (HEAD_DIM**-0.5)).astype(low)
            held[1] = dot(n1, flat(wq[g, 1])).astype(low)
            held[2] = (dot(n1, flat(wq[g, 2])) + vec_ref[3:4, cols]).astype(low)
            pltpu.make_async_copy(held, qkv_hbm.at[g], local.at[2 + g % 2]).start()

            for w in range(windows):
                n = g * windows + w
                hook(FORWARD, n)
                rows = slice(w * TOK, (w + 1) * TOK)
                slot = n % 2
                s = dot_nt(held[1, rows, :], diag(held[0, rows, :], mask_ref)) + bias_ref[g]
                e = jnp.exp(s - jnp.max(s, 0, keepdims=True))
                p = (e * (1.0 / jnp.sum(e, 0, keepdims=True))).astype(low)
                keep = pltpu.make_async_copy(pt_ref.at[slot], pt_hbm.at[n], local.at[4 + slot])
                if n >= 2:
                    keep.wait()
                pt_ref[slot] = p
                keep.start()
                o_ref[rows, cols] = undiag(held[2, rows, :].T, p, mask_ref).astype(low)

        run(W_P, ARRIVED)

        def output(w, carry):
            rows = window_rows(w)
            x1_ref[rows, :] = x_ref[rows, :].astype(full) + (dot(o_ref[rows, :], flat(wp[...])) + vec_ref[4:5, :])
            return carry

        lax.fori_loop(0, windows, output, 0)
        save.wait()
        for g in (GROUPS - 2, GROUPS - 1):
            pltpu.make_async_copy(qkv_ref.at[g % 2], qkv_hbm.at[g], local.at[2 + g % 2]).wait()
        for slot in range(2):
            pltpu.make_async_copy(pt_ref.at[slot], pt_hbm.at[0], local.at[4 + slot]).wait()

    pl.run_scoped(forward, V((rows_all, C), low), V((ROWS, C), low), V((C, ROWS), low), V((2, 3, ROWS, GCOLS), low), V((2, TOK, PACK), low),
                  V((GROUPS, TOK, PACK), full))

    def middle(n2_ref, n2t_ref, dy_ref, dyt_ref, y_ref, dn_ref, bu_ref, bsum_ref):
        load = pltpu.make_async_copy(dy_hbm, dy_ref.at[0:rows_all], local.at[0])
        load.start()
        zero_tail(n2_ref, windows)
        zero_tail(dy_ref, windows)
        hook(MIDDLE, 0)
        load.wait()

        def second_norm(w, carry):
            rows = window_rows(w)
            xhat, _ = norm_parts(x1_ref[rows, :])
            n2_ref[rows, :] = (xhat * vec_ref[5:6, :] + vec_ref[6:7, :]).astype(low)
            dy_ref[rows, :] = (dy_ref[rows, :].astype(full) * live(w)).astype(low)
            return carry

        lax.fori_loop(0, windows, second_norm, 0)
        transpose_rows(n2_ref, n2t_ref)
        hook(MIDDLE, 1)
        transpose_rows(dy_ref, dyt_ref)
        y_ref[...] = jnp.zeros_like(y_ref)
        dn_ref[...] = jnp.zeros_like(dn_ref)
        for t in range(TILES):
            for s in range(TILE // 128):
                row, left = hidden_place(t, s)
                bu_ref[t, :, s * 128 : (s + 1) * 128] = vec_ref[row : row + 1, left : left + 128]
        hook(MIDDLE, 2)
        run(W_U0, ARRIVED)
        run(W_D0, ARRIVED)
        halves = TILE // SUB

        def step(i, carry):
            for k in range(1, TILES * halves):

                @pl.when(i == k)
                def _(k=k):
                    if k % halves == 0:
                        t = k // halves
                        for name in (W_U[t], W_D[t]):
                            run(name, ARRIVED)
                        for name in (W_U[t - 1], W_D[t - 1]):
                            jobs[name].close()
                        for name in (G_D[t - 1], G_U[t - 1]):
                            run(name, START)
                    hook(TILE_STEP, k)

            t, part = i // halves, i % halves
            cols = pl.ds(pl.multiple_of(part * SUB, SUB), SUB)
            wide = SUB // 128
            slot = (t + SLOTS - 1) % SLOTS
            u = flat(up[t, :, :, cols])
            d = flat(down[t, pl.ds(part * wide, wide)])
            h = dot(n2_ref[...], u) + bu_ref[t, :, cols]
            da = dot_nt(dy_ref[...], d)
            act, slope = gelu_both(h)
            a = act.astype(low)
            dh = (da * slope).astype(low)
            bsum_ref[t, :, cols] = jnp.sum(dh.astype(full), 0, keepdims=True)
            y_ref[...] += dot(a, d)
            dn_ref[...] += dot_nt(dh, u)
            gd = dot(dyt_ref[...], a).astype(low)
            down[slot, pl.ds(part * wide, wide)] = blocks(gd.T, wide)
            up[slot, :, :, cols] = blocks(dot(n2t_ref[...], dh).astype(low), OWNERS)
            return carry

        lax.fori_loop(0, TILES * halves, step, 0)
        run(G_D[-1], START)
        run(G_U[-1], START)
        hook(AFTER_TILES, 0)
        sums_ref[...] = jnp.zeros_like(sums_ref)
        for t in range(TILES):
            for s in range(TILE // 128):
                row, left = hidden_place(t, s)
                sums_ref[row : row + 1, left : left + 128] = bsum_ref[t, :, s * 128 : (s + 1) * 128]
        transpose_rows(o_ref, dyt_ref)
        hook(AFTER_TILES, 1)

        def finish(w, carry):
            rows = window_rows(w)
            x1 = x1_ref[rows, :]
            xhat, scale = norm_parts(x1)
            dn = dn_ref[rows, :]
            dy = dy_ref[rows, :].astype(full)
            dx1 = dy + norm_back(xhat, scale, dn, vec_ref[5:6, :])
            dr = dx1.astype(low)
            sums_ref[4:5, :] += jnp.sum(dr.astype(full), 0, keepdims=True)
            sums_ref[5:6, :] += jnp.sum(dn * xhat, 0, keepdims=True)
            sums_ref[6:7, :] += jnp.sum(dn, 0, keepdims=True)
            sums_ref[7:8, :] += jnp.sum(dy, 0, keepdims=True)
            dy_ref[rows, :] = ((x1 + y_ref[rows, :] + vec_ref[7:8, :]) * live(w)).astype(low)
            x1_ref[rows, :] = dx1
            n2_ref[rows, :] = dr
            o_ref[rows, :] = dot_nt(dr, flat(wp[...])).astype(low)
            return carry

        lax.fori_loop(0, windows, finish, 0)
        save = pltpu.make_async_copy(dy_ref.at[0:rows_all], out_hbm, local.at[0])
        save.start()
        hook(AFTER_TILES, 2)
        jobs[W_P].close()
        for g in range(GROUPS):
            cols = slice(g * GCOLS, (g + 1) * GCOLS)
            wp[:, :, cols] = blocks(dot(dyt_ref[...], n2_ref[:, cols]).astype(low), OWNERS)
        run(G_P, START)
        hook(AFTER_TILES, 3)
        save.wait()

    pl.run_scoped(middle, V((ROWS, C), low), V((C, ROWS), low), V((ROWS, C), low), V((C, ROWS), low), V((ROWS, C), full), V((ROWS, C), full),
                  V((TILES, 1, TILE), full), V((TILES, 1, TILE), full))

    def backward(x_ref, n1t_ref, qkv_ref, pt_ref, dproj_ref, dn_ref, bias_ref):
        loads = [pltpu.make_async_copy(x_hbm, x_ref, local.at[0]), pltpu.make_async_copy(n1t_hbm, n1t_ref, local.at[1])]
        fetch = [pltpu.make_async_copy(qkv_hbm.at[g], qkv_ref.at[g % 2], local.at[2 + g % 2]) for g in range(GROUPS)]
        fetch[0].start()
        pltpu.make_async_copy(pt_hbm.at[0], pt_ref.at[0], local.at[4]).start()
        fetch[1].start()
        for load in loads:
            load.start()
        bias_ref[...] = jnp.zeros_like(bias_ref)
        dn_ref[...] = jnp.zeros_like(dn_ref)
        for part in range(3):
            dproj_ref[part, rows_all:, :] = jnp.zeros((ROWS - rows_all, GCOLS), low)
        for g in range(GROUPS):
            cols = slice(g * GCOLS, (g + 1) * GCOLS)
            held = qkv_ref.at[g % 2]
            fetch[g].wait()

            for w in range(windows):
                n = g * windows + w
                hook(BACKWARD, n)
                rows = slice(w * TOK, (w + 1) * TOK)
                slot = n % 2
                if n + 1 < GROUPS * windows:
                    pltpu.make_async_copy(pt_hbm.at[n + 1], pt_ref.at[1 - slot], local.at[5 - slot]).start()
                pltpu.make_async_copy(pt_hbm.at[n], pt_ref.at[slot], local.at[4 + slot]).wait()
                q = held[0, rows, :]
                k = held[1, rows, :]
                v = held[2, rows, :]
                p = pt_ref[slot]
                do = diag(o_ref[rows, cols], mask_ref)
                dp = dot_nt(v, do)
                dv = dot(p, do).astype(low)
                pf = p.astype(full)
                ds = (pf * (dp - jnp.sum(pf * dp, 0, keepdims=True))).astype(low)
                bias_ref[g] += ds.astype(full)
                dproj_ref[1, rows, :] = dot(ds, diag(q, mask_ref)).astype(low)
                dq = (undiag(k.T, ds, mask_ref) * (HEAD_DIM**-0.5)).astype(low)
                dproj_ref[0, rows, :] = dq
                dproj_ref[2, rows, :] = dv
                sums_ref[2:3, cols] += jnp.sum(dq.astype(full), 0, keepdims=True)
                sums_ref[3:4, cols] += jnp.sum(dv.astype(full), 0, keepdims=True)
            if g + 2 < GROUPS:
                fetch[g + 2].start()
            if g == 0:
                for load in loads:
                    load.wait()
            jobs[W_Q[g]].close()
            for part in range(3):
                d = dproj_ref[part]
                dn_ref[...] += dot_nt(d, flat(wq[g, part]))
                wq[g, part] = blocks(dot(n1t_ref[...], d).astype(low), OWNERS)
                if g == GROUPS - 1:
                    run(G_LAST[part], START)
            if g < GROUPS - 1:
                run(G_Q[g], START)
        hook(LAST_STEPS, 0)

        def last_norm(grad_ref):
            def finish(w, carry):
                rows = window_rows(w)
                slot = w % 2
                xhat, scale = norm_parts(x_ref[rows, :].astype(full))
                dn = dn_ref[rows, :]
                save = pltpu.make_async_copy(grad_ref.at[slot], grad_hbm.at[rows], local.at[4 + slot])

                @pl.when(w >= 2)
                def _():
                    save.wait()

                grad_ref[slot] = x1_ref[rows, :] + norm_back(xhat, scale, dn, vec_ref[0:1, :])
                save.start()
                sums_ref[0:1, :] += jnp.sum(dn * xhat, 0, keepdims=True)
                sums_ref[1:2, :] += jnp.sum(dn, 0, keepdims=True)
                return carry

            lax.fori_loop(0, windows, finish, 0)
            hook(LAST_STEPS, 1)
            for slot in range(2):
                pltpu.make_async_copy(grad_ref.at[slot], grad_hbm.at[pl.ds(0, TOK)], local.at[4 + slot]).wait()

        pl.run_scoped(last_norm, V((2, TOK, C), full))
        hook(LAST_STEPS, 2)

        def table(tmp_ref):
            pack_small(sums_ref[...], table_grad(line_ref, tmp_ref, bias_ref), terms_ref)

        pl.run_scoped(table, V((2, TOK * HEADS, 128), full))
        run(G_S, START)
        hook(LAST_STEPS, 3)
        for stage in range(len(Reduce.STAGES)):
            for name in G_ALL:
                if stage < len(jobs[name].STAGES):
                    run(name, stage)

    pl.run_scoped(backward, V((rows_all, C), low), V((C, ROWS), low), V((2, 3, ROWS, GCOLS), low), V((2, TOK, PACK), low), V((3, ROWS, GCOLS), low),
                  V((ROWS, C), full), V((GROUPS, TOK, PACK), full))
    jobs[W_U[-1]].close()
    jobs[W_D[-1]].close()
    for i in range(1, OWNERS):
        await_bytes(small.at[mine], small_sems.at[i])
    for name in G_ALL:
        jobs[name].close()


def shape(dims, kind):
    return jax.ShapeDtypeStruct(dims, kind)


def adamw(weight, moment, second, gradient, step_rate):
    moment_new = beta_one * moment + (1.0 - beta_one) * gradient
    second_new = beta_two * second + (1.0 - beta_two) * gradient * gradient
    update = moment_new * (1.0 / (1.0 - beta_one**STEP)) / (jnp.sqrt(second_new * (1.0 / (1.0 - beta_two**STEP))) + adam_eps)
    weight_new = weight * (1.0 - step_rate * weight_decay) - step_rate * update
    return (weight_new, moment_new, second_new)


def update_kernel(*refs):
    gq, gp, gu, gd, gs = refs[:5]
    ins = [refs[5 + 3 * i : 8 + 3 * i] for i in range(6)]
    outs = [refs[25 + 4 * i : 29 + 4 * i] for i in range(4)] + [refs[41:44], refs[44:47]]
    results = [pltpu.make_async_copy(refs[23 + i], refs[47 + i], refs[49].at[i]) for i in range(2)]

    @pl.when(pl.program_id(0) == 0)
    def _():
        for copy in results:
            copy.start()

    def piece(which, place, gradient):
        new = adamw(*(ref[place] for ref in ins[which]), gradient, step_rates[which])
        for ref, value in zip(outs[which], new):
            ref[place] = value
        if which < 4:
            outs[which][3][place] = new[0].astype(low)

    for part in range(3):
        for g in range(GROUPS):
            left = part * C + g * GCOLS
            piece(0, (slice(None), slice(left, left + GCOLS)), gq[g, part].astype(full))
    piece(1, (slice(None), slice(None)), gp[...].astype(full))
    for t in range(TILES):
        for s in range(OWNERS):
            left = (MLP // OWNERS) * s + 128 * t
            piece(2, (slice(None), slice(left, left + 128)), gu[t, :, s * 128 : (s + 1) * 128].astype(full))
    piece(3, (slice(None), slice(None)), gd[0].astype(full))

    @pl.when(pl.program_id(0) == 0)
    def _():
        every = (slice(None), slice(None))
        piece(4, every, gs[0:12, 0:OWNED])
        piece(5, every, gs[16:40, 0 : ins[5][0].shape[1]])

    @pl.when(pl.program_id(0) == pl.num_programs(0) - 1)
    def _():
        for copy in results:
            copy.wait()


def update(gq, gp, gu, gd, gs, states, results):
    steps = OWNED // 16

    def rows_of(array):
        tall = array.shape[0] // steps
        return pl.BlockSpec((tall, array.shape[1]), lambda i: (i, 0))

    def whole(array):
        return pl.BlockSpec(array.shape, lambda i: (0, 0))

    per_tile = 128 * TILES // steps
    specs = [
        pl.BlockSpec((GROUPS, 3, 16, GCOLS), lambda i: (0, 0, i, 0)),
        pl.BlockSpec((16, C), lambda i: (i, 0)),
        pl.BlockSpec((TILES, 16, TILE), lambda i: (0, i, 0)),
        pl.BlockSpec((1, per_tile, C), lambda i: (i // (128 // per_tile), i % (128 // per_tile), 0)),
        whole(gs),
    ]
    out_shapes, out_specs = [], []
    for i, group in enumerate(states):
        for array in group:
            specs.append(rows_of(array) if i < 4 else whole(array))
            out_shapes.append(shape(array.shape, full))
            out_specs.append(specs[-1])
        if i < 4:
            out_shapes.append(shape(group[0].shape, low))
            out_specs.append(rows_of(group[0]))
    hbm = pl.BlockSpec(memory_space=pl.ANY)
    for array in results:
        specs.append(hbm)
        out_shapes.append(shape(array.shape, array.dtype))
        out_specs.append(hbm)
    return pl.pallas_call(
        update_kernel,
        grid=(steps,),
        in_specs=specs,
        out_specs=out_specs,
        out_shape=out_shapes,
        scratch_shapes=[pltpu.SemaphoreType.DMA((2,))],
        compiler_params=pltpu.CompilerParams(vmem_limit_bytes=63 * MIB),
        name="update",
    )(gq, gp, gu, gd, gs, *[array for group in states for array in group], *results)


def shards(
    tokens, out_grad, window_count,
    qkv_weight, qkv_first, qkv_second,
    output_weight, output_first, output_second,
    up_weight, up_first, up_second,
    down_weight, down_first, down_second,
    vectors, vector_first, vector_second,
    bias_table, table_first, table_second,
):
    windows = tokens.shape[0]
    rows = windows * TOK
    V = pltpu.VMEM
    D = pltpu.SemaphoreType.DMA
    hbm = pl.BlockSpec(memory_space=pl.ANY)
    vmem = pl.BlockSpec(memory_space=pltpu.VMEM)
    result = pl.pallas_call(
        functools.partial(layer_kernel, windows),
        out_shape=[
            shape((rows, C), low), shape((rows, C), full),
            shape((GROUPS, 3, OWNED, GCOLS), low), shape((OWNED, C), low), shape((TILES, OWNED, TILE), low), shape((TILES, 128, C), low),
            shape((40, 128), full),
            shape((GROUPS, 3, ROWS, GCOLS), low), shape((GROUPS * windows, TOK, PACK), low), shape((C, ROWS), low)],
        in_specs=[hbm, hbm, pl.BlockSpec(memory_space=pltpu.SMEM)] + [hbm] * 4 + [vmem] * 4,
        out_specs=[hbm, hbm] + [vmem] * 5 + [hbm] * 3,
        scratch_shapes=[
            V((GROUPS, 3, OWNERS, OWNED, GCOLS), low), V((OWNERS, OWNED, C), low), V((SLOTS, OWNERS, OWNED, TILE), low),
            V((SLOTS, OWNERS, 128, C), low), V((OWNERS, 48, 128), low), V((ROWS, C), low), V((rows, C), full), V((16, C), full), V((16, C), full),
            V((OWNERS, 40, 128), full)]
        + reduce_scratch()
        + [D((GATHERS, Gather.SEMS)), D((REDUCES, Reduce.SEMS)), D((2 * OWNERS,)), D((ReduceSmall.SEMS,)), D((6,))],
        compiler_params=pltpu.CompilerParams(vmem_limit_bytes=63 * MIB, collective_id=0, has_side_effects=True),
        name="layer",
    )(tokens.reshape(rows, C), out_grad.reshape(rows, C), window_count, qkv_weight, output_weight, up_weight, down_weight, vectors, bias_table.T,
      jnp.asarray(line_matrix(), low), jnp.asarray(head_masks(), low))
    out, grad, gq, gp, gu, gd, gs = result[:7]
    new = update(gq, gp, gu, gd, gs, (
        (qkv_weight, qkv_first, qkv_second), (output_weight, output_first, output_second), (up_weight, up_first, up_second),
        (down_weight, down_first, down_second), (vectors, vector_first, vector_second), (bias_table.T, table_first.T, table_second.T)), (out, grad))
    *new, out, grad = new
    return (out.reshape(tokens.shape), grad.reshape(tokens.shape), *new[:-3], *(array.T for array in new[-3:]))


def vmem_call(body, outs, scratch, args, name, limit=60, **params):
    spec = pl.BlockSpec(memory_space=pltpu.VMEM)
    return pl.pallas_call(
        body,
        out_shape=outs,
        in_specs=[pl.BlockSpec(memory_space=pltpu.SMEM) if a.dtype == full and a.ndim == 1 else spec for a in args],
        out_specs=[spec] * len(outs),
        scratch_shapes=scratch,
        compiler_params=pltpu.CompilerParams(vmem_limit_bytes=limit * MIB, **params),
        name=name,
    )(*args)


def local_step(tokens, out_grad, window_count, small, wq, wp, up, down):
    windows = tokens.shape[0]
    rows = windows * TOK
    owned = C // OWNERS
    V = pltpu.VMEM
    x = tokens.reshape(rows, C)
    dy = out_grad.reshape(rows, C)
    live = (jnp.arange(windows) < window_count[0]).astype(full)
    line = jnp.asarray(line_matrix(), low)
    masks = jnp.asarray(head_masks(), low)
    qkv, pt, o, x1, n1t, vec = vmem_call(
        functools.partial(attention_forward, windows),
        [shape((9, ROWS, GCOLS), low), shape((GROUPS, windows, TOK, PACK), low), shape((ROWS, C), low), shape((rows, C), full), shape((C, ROWS), low),
         shape((16, C), full)],
        [V((ROWS, C), low), V((GROUPS, TOK, PACK), full), V((2, TOK * HEADS, 128), full)],
        (x, small, line, masks, wq, wp), "attention_forward")
    out, dx1, do, gup, gdown, gout, sums = vmem_call(
        functools.partial(feed_forward, windows),
        [shape((rows, C), low), shape((ROWS, C), full), shape((rows, C), low), shape((TILES, OWNERS, owned, TILE), low),
         shape((TILES, OWNERS, C, 128), low), shape((OWNERS, owned, C), low), shape((16, C), full)],
        [V((ROWS, C), low), V((C, ROWS), low), V((ROWS, C), low), V((C, ROWS), low), V((ROWS, C), full), V((ROWS, C), full),
         V((TILES, 1, TILE), full), V((TILES, 1, TILE), full)],
        (x1, dy, live, vec, up, down, wp, o), "feed_forward")
    gq, gsmall, grad = vmem_call(
        functools.partial(attention_backward, windows),
        [shape((GROUPS, 3, OWNERS, owned, GCOLS), low), shape((OWNERS, 40, 128), full), shape((rows, C), full)],
        [V((16, C), full), V((GROUPS, TOK, PACK), full), V((2, TOK * HEADS, 128), full), V((3, ROWS, GCOLS), low), V((ROWS, C), full)],
        (x, vec, line, masks, wq, qkv, pt, do, dx1, n1t, sums), "attention_backward")
    return out.reshape(tokens.shape), grad.reshape(tokens.shape), gq, gout, gup, gdown, gsmall


def shards_general(
    tokens, out_grad, window_count,
    qkv_weight, qkv_first, qkv_second,
    output_weight, output_first, output_second,
    up_weight, up_first, up_second,
    down_weight, down_first, down_second,
    vectors, vector_first, vector_second,
    bias_table, table_first, table_second,
):
    gather = functools.partial(lax.all_gather, axis_name="shard", tiled=True)
    scatter = functools.partial(lax.psum_scatter, axis_name="shard", tiled=True)
    owned = C // OWNERS
    wq = gather(qkv_weight.astype(low), axis=0).reshape(OWNERS, owned, 3, GROUPS, GCOLS).transpose(3, 2, 0, 1, 4)
    wp = gather(output_weight.astype(low), axis=0).reshape(OWNERS, owned, C)
    up = gather(up_weight.astype(low), axis=0).reshape(OWNERS, owned, OWNERS, TILES, 128).transpose(3, 0, 1, 2, 4)
    up = up.reshape(TILES, OWNERS, owned, TILE)
    down = gather(down_weight.astype(low), axis=0).reshape(OWNERS, TILES, 128, C).transpose(1, 0, 2, 3)
    vec = gather(vectors.astype(low), axis=1)
    tab = gather(bias_table.astype(low), axis=0)
    table_rows = tab.shape[0]
    count = TAB_ROWS // OWNERS
    vec = vec.reshape(12, OWNERS, owned).transpose(1, 0, 2)
    tab = tab[:TAB_ROWS].reshape(OWNERS, count, HEADS).transpose(0, 2, 1)
    small = jnp.concatenate([jnp.pad(vec, ((0, 0), (0, 4), (0, 128 - owned))), jnp.pad(tab, ((0, 0), (0, 8), (0, 128 - count)))], 1)
    out, grad, gq, gp, gu, gd, gs = local_step(tokens, out_grad, window_count, small, wq, wp, up, down)
    gq = gq.astype(full).transpose(2, 3, 1, 0, 4).reshape(C, 3 * C)
    gu = gu.astype(full).reshape(TILES, C, OWNERS, 128).transpose(1, 2, 0, 3).reshape(C, MLP)
    gd = gd.astype(full).transpose(1, 0, 3, 2).reshape(MLP, C)
    gv = gs[:, :12, :owned].transpose(1, 0, 2).reshape(12, C)
    gb = gs[:, 16:40, :count].transpose(0, 2, 1).reshape(TAB_ROWS, HEADS)
    gb = jnp.pad(gb, ((0, table_rows - TAB_ROWS), (0, 0)))
    totals = lax.psum(
        (scatter(gq, scatter_dimension=0), scatter(gp.astype(full).reshape(C, C), scatter_dimension=0), scatter(gu, scatter_dimension=0),
         scatter(gd, scatter_dimension=0), scatter(gv, scatter_dimension=1), scatter(gb, scatter_dimension=0)), "rep")
    states = (
        (qkv_weight, qkv_first, qkv_second), (output_weight, output_first, output_second), (up_weight, up_first, up_second),
        (down_weight, down_first, down_second), (vectors, vector_first, vector_second), (bias_table, table_first, table_second))
    results = [out, grad]
    for i, (state, total, rate) in enumerate(zip(states, totals, step_rates)):
        new = adamw(*state, total, rate)
        results += [*new, new[0].astype(low)] if i < 4 else [*new]
    return tuple(results)


def solution(mesh):
    wins = P(("rep", "shard"), None, None)
    rows = P("shard", None)
    cols = P(None, "shard")
    fits = mesh.shape["rep"] == REPS and mesh.shape["shard"] == OWNERS
    return jax.shard_map(
        shards if fits else shards_general,
        mesh=mesh,
        in_specs=(wins, wins, P(("rep", "shard"))) + (rows,) * 12 + (cols,) * 3 + (rows,) * 3,
        out_specs=(wins, wins) + (rows,) * 16 + (cols,) * 3 + (rows,) * 3,
        check_vma=False,
    )
```

```python
import functools
import math

import jax
import jax.numpy as jnp
import numpy as np
from jax import lax
from jax.experimental import pallas as pl
from jax.experimental.pallas import tpu as pltpu
from jax.sharding import PartitionSpec as P

C = 768
HEADS = 24
MLP = 3072
WIN = 12
STEP = 5
HEAD_DIM = 32
SPAN = 2 * WIN - 1
TOK = WIN * WIN
TAB_ROWS = 536
ROWS = 1024
GROUPS = 3
GCOLS = 256
GHEADS = 8
PACK = GHEADS * TOK
TAB_LANES = 640
TILES = 3
TILE = MLP // TILES
SUB = 512
LINE = 384
MIB = 1 << 20

beta_one = 0.5
beta_two = 0.6
weight_decay = 0.05
adam_eps = 1e-08
norm_eps = 1e-05
step_rates = (0.04, 0.15, 0.04, 0.02, 0.2, 1.0)
low = jnp.bfloat16
full = jnp.float32
NT = (((1,), (1,)), ((), ()))


def dot(a, b):
    return jnp.dot(a, b, preferred_element_type=full)


def dot_nt(a, b):
    return lax.dot_general(a, b, NT, preferred_element_type=full)


def line_matrix():
    out = np.zeros((TAB_LANES, LINE), np.float32)
    col = np.arange(SPAN * WIN)
    out[(col // WIN) * SPAN + col % WIN + WIN - 1, col] = 1.0
    return out


def head_masks():
    lane = np.arange(GCOLS) // HEAD_DIM
    one = (lane[None, :] == np.arange(GHEADS)[:, None]).astype(np.float32)
    return np.broadcast_to(one[:, None, :], (GHEADS, 16, GCOLS))


def norm_parts(z):
    mean = jnp.sum(z, -1, keepdims=True) * (1.0 / C)
    center = z - mean
    spread = jnp.sum(center * center, -1, keepdims=True) * (1.0 / C)
    scale = lax.rsqrt(spread + norm_eps)
    return center * scale, scale


def norm_back(xhat, scale, dn, gain):
    g = dn * gain
    m1 = jnp.sum(g, -1, keepdims=True) * (1.0 / C)
    m2 = jnp.sum(g * xhat, -1, keepdims=True) * (1.0 / C)
    return scale * (g - m1 - xhat * m2)


def diag(x, mask_ref):
    head = x[0:128].reshape(8, 16, GCOLS)
    tail = x[128:144]
    parts = []
    for h in range(GHEADS):
        parts.append((head * mask_ref[h][None]).reshape(128, GCOLS))
    for h in range(GHEADS):
        parts.append(tail * mask_ref[h])
    return jnp.concatenate(parts, 0)


def undiag(xt, m, mask_ref):
    main = []
    for h in range(0, GHEADS, 2):
        r = dot(xt[h * HEAD_DIM : (h + 2) * HEAD_DIM], m[:, h * 128 : (h + 2) * 128])
        main.append(r[0:HEAD_DIM, 0:128])
        main.append(r[HEAD_DIM : 2 * HEAD_DIM, 128:256])
    main = jnp.concatenate(main, 0)
    rest = dot(xt, m[:, GHEADS * 128 :])
    rest_t = rest.T.reshape(GHEADS, 16, GCOLS)
    keep = mask_ref[...].astype(full)
    return jnp.concatenate([main.T, jnp.sum(rest_t * keep, 0)], 0)


def flat(x):
    return x.reshape(x.shape[0] * x.shape[1], x.shape[2])


def blocks(x, owners):
    return x.reshape(owners, x.shape[0] // owners, x.shape[1])


def hidden_place(t, s):
    at = (MLP // GHEADS) * s + 128 * t
    return 8 + at // C, at % C


def unpack_small(small_ref, vec_ref):
    owners = small_ref.shape[0]
    width = C // owners
    count = TAB_ROWS // owners
    vec = jnp.zeros((16, C), full)
    tab = jnp.zeros((HEADS, TAB_LANES), full)
    lane = lax.broadcasted_iota(jnp.int32, (16, 128), 1)
    lane_tab = lax.broadcasted_iota(jnp.int32, (HEADS, 128), 1)
    for s in range(owners):
        piece = small_ref[s].astype(full)
        part = jnp.where(lane < width, piece[0:16], 0.0)
        part = jnp.concatenate([part, jnp.zeros((16, C - 128), full)], 1)
        vec = vec + (pltpu.roll(part, width * s, 1) if s else part)
        part = jnp.where(lane_tab < count, piece[16 : 16 + HEADS], 0.0)
        part = jnp.concatenate([part, jnp.zeros((HEADS, TAB_LANES - 128), full)], 1)
        tab = tab + (pltpu.roll(part, count * s, 1) if s else part)
    vec_ref[...] = vec
    return tab


def pack_small(vec, tab, out_ref):
    owners = out_ref.shape[0]
    width = C // owners
    count = TAB_ROWS // owners
    for s in range(owners):
        out_ref[s, 0:16, :] = (pltpu.roll(vec, C - width * s, 1) if s else vec)[:, 0:128]
        out_ref[s, 16:40, :] = (pltpu.roll(tab, TAB_LANES - count * s, 1) if s else tab)[:, 0:128]


def spread_table(tab, line_ref, tmp_ref):
    def column(cj, carry):
        shifted = pltpu.roll(tab, cj, 1)
        line = dot(shifted.astype(low), line_ref[...])
        for rj in range(WIN):
            cut = (WIN - 1 - rj) * WIN
            part = pltpu.roll(line, LINE - cut, 1) if cut else line
            row = pl.multiple_of((rj * WIN + cj) * HEADS, 8)
            tmp_ref[0, pl.ds(row, HEADS), :] = part[:, 0:128]
            tmp_ref[1, pl.ds(row, HEADS), :] = part[:, 128:256]
        return carry

    lax.fori_loop(0, WIN, column, 0)


def place_bias(tmp_ref, bias_ref):
    lane = lax.broadcasted_iota(jnp.int32, (TOK, 128), 1)
    for g in range(GROUPS):
        rest = jnp.zeros((TOK, 128), full)
        for h in range(GHEADS):
            at = pl.ds(g * GHEADS + h, TOK, stride=HEADS)
            bias_ref[g, :, h * 128 : (h + 1) * 128] = tmp_ref[0, at, :]
            piece = tmp_ref[1, at, :]
            piece = pltpu.roll(piece, 16 * h, 1) if h else piece
            rest = jnp.where((lane >= 16 * h) & (lane < 16 * h + 16), piece, rest)
        bias_ref[g, :, GHEADS * 128 :] = rest


def table_grad(line_ref, tmp_ref, bias_ref):
    lane = lax.broadcasted_iota(jnp.int32, (TOK, 128), 1)
    for g in range(GROUPS):
        rest = bias_ref[g, :, GHEADS * 128 :]
        for h in range(GHEADS):
            at = pl.ds(g * GHEADS + h, TOK, stride=HEADS)
            tmp_ref[0, at, :] = bias_ref[g, :, h * 128 : (h + 1) * 128]
            piece = pltpu.roll(rest, 128 - 16 * h, 1) if h else rest
            tmp_ref[1, at, :] = jnp.where(lane < 16, piece, 0.0)

    def column(cj, total):
        line = jnp.zeros((HEADS, LINE), full)
        for rj in range(WIN):
            cut = (WIN - 1 - rj) * WIN
            row = pl.multiple_of((rj * WIN + cj) * HEADS, 8)
            part = jnp.concatenate([tmp_ref[0, pl.ds(row, HEADS), :], tmp_ref[1, pl.ds(row, HEADS), :], jnp.zeros((HEADS, 128), full)], 1)
            line = line + (pltpu.roll(part, cut, 1) if cut else part)
        high = line.astype(low)
        rest = (line - high.astype(full)).astype(low)
        spread = dot_nt(high, line_ref[...]) + dot_nt(rest, line_ref[...])
        return total + pltpu.roll(spread, TAB_LANES - cj, 1)

    return lax.fori_loop(0, WIN, column, jnp.zeros((HEADS, TAB_LANES), full))


def transpose_rows(src_ref, dst_ref):
    def block(i, carry):
        at = pl.multiple_of(i * 128, 128)
        dst_ref[:, pl.ds(at, 128)] = src_ref[pl.ds(at, 128), :].T
        return carry

    lax.fori_loop(0, ROWS // 128, block, 0)


def window_rows(w):
    return pl.ds(pl.multiple_of(w * TOK, 16), TOK)


def zero_tail(ref, windows):
    at = windows * TOK
    ref[at:ROWS, :] = jnp.zeros((ROWS - at, ref.shape[1]), ref.dtype)


def attention_forward(windows, x_ref, small_ref, line_ref, mask_ref, wq_ref, wp_ref,
                      qkv_ref, pt_ref, o_ref, x1_ref, n1t_ref, vec_ref, n1_ref, bias_ref, tmp_ref):
    tab = unpack_small(small_ref, vec_ref)
    spread_table(tab, line_ref, tmp_ref)
    place_bias(tmp_ref, bias_ref)
    zero_tail(n1_ref, windows)
    zero_tail(o_ref, windows)

    def first_norm(w, carry):
        xhat, _ = norm_parts(x_ref[window_rows(w), :].astype(full))
        n1_ref[window_rows(w), :] = (xhat * vec_ref[0:1, :] + vec_ref[1:2, :]).astype(low)
        return carry

    lax.fori_loop(0, windows, first_norm, 0)
    transpose_rows(n1_ref, n1t_ref)

    def group(g, carry):
        cols = pl.ds(pl.multiple_of(g * GCOLS, GCOLS), GCOLS)
        n1 = n1_ref[...]
        qkv_ref[g] = ((dot(n1, flat(wq_ref[g, 0])) + vec_ref[2:3, cols]) * (HEAD_DIM**-0.5)).astype(low)
        qkv_ref[GROUPS + g] = dot(n1, flat(wq_ref[g, 1])).astype(low)
        qkv_ref[2 * GROUPS + g] = (dot(n1, flat(wq_ref[g, 2])) + vec_ref[3:4, cols]).astype(low)

        def window(w, inner):
            rows = window_rows(w)
            q = qkv_ref[g, rows, :]
            k = qkv_ref[GROUPS + g, rows, :]
            v = qkv_ref[2 * GROUPS + g, rows, :]
            s = dot_nt(k, diag(q, mask_ref)) + bias_ref[g]
            e = jnp.exp(s - jnp.max(s, 0, keepdims=True))
            p = (e * (1.0 / jnp.sum(e, 0, keepdims=True))).astype(low)
            pt_ref[g, w] = p
            o_ref[rows, cols] = undiag(v.T, p, mask_ref).astype(low)
            return inner

        lax.fori_loop(0, windows, window, 0)
        return carry

    lax.fori_loop(0, GROUPS, group, 0)

    def output(w, carry):
        rows = window_rows(w)
        branch = dot(o_ref[rows, :], flat(wp_ref[...])) + vec_ref[4:5, :]
        x1_ref[rows, :] = x_ref[rows, :].astype(full) + branch
        return carry

    lax.fori_loop(0, windows, output, 0)


def gelu_both(h):
    c = math.sqrt(2.0 / math.pi)
    square = h * h
    t = jnp.tanh(h * (c + (c * 0.044715) * square))
    half = 0.5 + 0.5 * t
    slope = half + (0.5 * h) * (1.0 - t * t) * (c + (3.0 * c * 0.044715) * square)
    return h * half, slope


def feed_forward(windows, x1_ref, dy_ref, live_ref, vec_ref, up_ref, down_ref, wp_ref, o_ref,
                 out_ref, dx1_ref, do_ref, gup_ref, gdown_ref, gout_ref, sums_ref,
                 n2_ref, n2t_ref, dy2_ref, dyt_ref, y_ref, dn_ref, bu_ref, bsum_ref):
    zero_tail(n2_ref, windows)
    zero_tail(dy2_ref, windows)

    def second_norm(w, carry):
        rows = window_rows(w)
        xhat, _ = norm_parts(x1_ref[rows, :])
        n2_ref[rows, :] = (xhat * vec_ref[5:6, :] + vec_ref[6:7, :]).astype(low)
        dy2_ref[rows, :] = (dy_ref[rows, :].astype(full) * live_ref[w]).astype(low)
        return carry

    lax.fori_loop(0, windows, second_norm, 0)
    transpose_rows(n2_ref, n2t_ref)
    transpose_rows(dy2_ref, dyt_ref)
    y_ref[...] = jnp.zeros_like(y_ref)
    dn_ref[...] = jnp.zeros_like(dn_ref)
    owners = gup_ref.shape[1]
    for t in range(TILES):
        for s in range(TILE // 128):
            row, at = hidden_place(t, s)
            bu_ref[t, :, s * 128 : (s + 1) * 128] = vec_ref[row : row + 1, at : at + 128]

    def step(t, carry):
        for part in range(TILE // SUB):
            cols = slice(part * SUB, (part + 1) * SUB)
            up = flat(up_ref[t, :, :, cols])
            down = flat(down_ref[t, part * SUB // 128 : (part + 1) * SUB // 128])
            h = dot(n2_ref[...], up) + bu_ref[t, :, cols]
            da = dot_nt(dy2_ref[...], down)
            act, slope = gelu_both(h)
            a = act.astype(low)
            dh = (da * slope).astype(low)
            bsum_ref[t, :, cols] = jnp.sum(dh.astype(full), 0, keepdims=True)
            y_ref[...] += dot(a, down)
            dn_ref[...] += dot_nt(dh, up)
            gd = dot(dyt_ref[...], a).astype(low)
            for b in range(SUB // 128):
                gdown_ref[t, part * SUB // 128 + b] = gd[:, b * 128 : (b + 1) * 128]
            gup_ref[t, :, :, cols] = blocks(dot(n2t_ref[...], dh).astype(low), owners)
        return carry

    lax.fori_loop(0, TILES, step, 0)
    sums_ref[...] = jnp.zeros_like(sums_ref)
    for t in range(TILES):
        for s in range(TILE // 128):
            row, at = hidden_place(t, s)
            sums_ref[row : row + 1, at : at + 128] = bsum_ref[t, :, s * 128 : (s + 1) * 128]
    zero_tail(dx1_ref, windows)

    def finish(w, carry):
        rows = window_rows(w)
        x1 = x1_ref[rows, :]
        out_ref[rows, :] = ((x1 + y_ref[rows, :] + vec_ref[7:8, :]) * live_ref[w]).astype(low)
        xhat, scale = norm_parts(x1)
        dn = dn_ref[rows, :]
        dy = dy2_ref[rows, :].astype(full)
        dx1 = dy + norm_back(xhat, scale, dn, vec_ref[5:6, :])
        dx1_ref[rows, :] = dx1
        dr = dx1.astype(low)
        n2_ref[rows, :] = dr
        do_ref[rows, :] = dot_nt(dr, flat(wp_ref[...])).astype(low)
        sums_ref[4:5, :] += jnp.sum(dr.astype(full), 0, keepdims=True)
        sums_ref[5:6, :] += jnp.sum(dn * xhat, 0, keepdims=True)
        sums_ref[6:7, :] += jnp.sum(dn, 0, keepdims=True)
        sums_ref[7:8, :] += jnp.sum(dy, 0, keepdims=True)
        return carry

    lax.fori_loop(0, windows, finish, 0)
    transpose_rows(o_ref, dyt_ref)
    for g in range(GROUPS):
        at = pl.ds(g * GCOLS, GCOLS)
        gout_ref[:, :, at] = blocks(dot(dyt_ref[...], n2_ref[:, at]).astype(low), gout_ref.shape[0])


def attention_backward(windows, x_ref, vec_ref, line_ref, mask_ref, wq_ref, qkv_ref, pt_ref, do_ref, dx1_ref, n1t_ref, sums_in_ref,
                       gq_ref, gsmall_ref, grad_ref, sums_ref, bias_ref, tmp_ref, dproj_ref, dn_ref):
    bias_ref[...] = jnp.zeros_like(bias_ref)
    dn_ref[...] = jnp.zeros_like(dn_ref)
    sums_ref[...] = sums_in_ref[...]
    for part in range(3):
        dproj_ref[part, windows * TOK :, :] = jnp.zeros((ROWS - windows * TOK, GCOLS), low)

    def group(g, carry):
        cols = pl.ds(pl.multiple_of(g * GCOLS, GCOLS), GCOLS)

        def window(w, inner):
            rows = window_rows(w)
            q = qkv_ref[g, rows, :]
            k = qkv_ref[GROUPS + g, rows, :]
            v = qkv_ref[2 * GROUPS + g, rows, :]
            p = pt_ref[g, w]
            do = diag(do_ref[rows, cols], mask_ref)
            dp = dot_nt(v, do)
            dv = dot(p, do)
            pf = p.astype(full)
            ds = (pf * (dp - jnp.sum(pf * dp, 0, keepdims=True))).astype(low)
            bias_ref[g] += ds.astype(full)
            dk = dot(ds, diag(q, mask_ref))
            dq = undiag(k.T, ds, mask_ref) * (HEAD_DIM**-0.5)
            dq = dq.astype(low)
            dv = dv.astype(low)
            dproj_ref[0, rows, :] = dq
            dproj_ref[1, rows, :] = dk.astype(low)
            dproj_ref[2, rows, :] = dv
            sums_ref[2:3, cols] += jnp.sum(dq.astype(full), 0, keepdims=True)
            sums_ref[3:4, cols] += jnp.sum(dv.astype(full), 0, keepdims=True)
            return inner

        lax.fori_loop(0, windows, window, 0)
        for part in range(3):
            d = dproj_ref[part]
            gq_ref[g, part] = blocks(dot(n1t_ref[...], d).astype(low), gq_ref.shape[2])
            dn_ref[...] += dot_nt(d, flat(wq_ref[g, part]))
        return carry

    lax.fori_loop(0, GROUPS, group, 0)

    def finish(w, carry):
        rows = window_rows(w)
        xhat, scale = norm_parts(x_ref[rows, :].astype(full))
        dn = dn_ref[rows, :]
        grad_ref[rows, :] = dx1_ref[rows, :] + norm_back(xhat, scale, dn, vec_ref[0:1, :])
        sums_ref[0:1, :] += jnp.sum(dn * xhat, 0, keepdims=True)
        sums_ref[1:2, :] += jnp.sum(dn, 0, keepdims=True)
        return carry

    lax.fori_loop(0, windows, finish, 0)
    pack_small(sums_ref[...], table_grad(line_ref, tmp_ref, bias_ref), gsmall_ref)


MESH = pl.DeviceIdType.MESH
REPS = 4
OWNERS = 8
LINKS = OWNERS // 2


class Spot:
    def __init__(self):
        self.rep = lax.axis_index("rep")
        self.shard = lax.axis_index("shard")
        self.z = self.shard // 2
        self.core = self.shard % 2

    def sibling(self):
        return (self.rep, self.z * 2 + (1 - self.core))

    def along_z(self, step):
        return (self.rep, ((self.z + step) % LINKS) * 2 + self.core)

    def turned(self, axis):
        x, y = self.rep % 2, self.rep // 2
        return y * 2 + (1 - x) if axis == 0 else (1 - y) * 2 + x

    def beside(self, axis):
        return (self.turned(axis), self.shard)


def greet(spot):
    barrier = pltpu.get_barrier_semaphore()
    peers = [(spot.rep, (spot.shard + i) % OWNERS) for i in range(1, OWNERS)]
    peers += [((spot.rep + i) % REPS, spot.shard) for i in range(1, REPS)]
    for peer in peers:
        pl.semaphore_signal(barrier, inc=1, device_id=peer, device_id_type=MESH)
    return barrier, len(peers)


def send(src, dst, send_sem, recv_sem, peer):
    pltpu.make_async_remote_copy(src_ref=src, dst_ref=dst, send_sem=send_sem, recv_sem=recv_sem, device_id=peer, device_id_type=MESH).start()


def await_bytes(ref, sem):
    pltpu.make_async_copy(ref, ref, sem).wait()


def quarter(ref, rep):
    rows, cols = ref.shape[-2:]
    lead = (slice(None),) * (len(ref.shape) - 2)
    top = pl.multiple_of((rep // 2) * (rows // 2), 16)
    left = pl.multiple_of((rep % 2) * (cols // 2), 128)
    return ref.at[lead + (pl.ds(top, rows // 2), pl.ds(left, cols // 2))]


def half(ref, rep, axis):
    rows, cols = ref.shape[-2:]
    lead = (slice(None),) * (len(ref.shape) - 2)
    if axis == 0:
        left = pl.multiple_of((rep % 2) * (cols // 2), 128)
        return ref.at[lead + (slice(None), pl.ds(left, cols // 2))]
    top = pl.multiple_of((rep // 2) * (rows // 2), 16)
    return ref.at[lead + (pl.ds(top, rows // 2), slice(None))]


class Gather:
    KINDS = (LINKS - 1, LINKS - 1, LINKS - 1, LINKS - 1, LINKS)
    SEMS = 2 * sum(KINDS)
    STAGES = ("start", "across", "relay", "beside", "finish")

    def __init__(self, spot, place, axis, sems):
        self.spot, self.place, self.axis, self.sems = spot, place, axis, sems

    def sem(self, side, kind, i):
        return self.sems.at[side * (self.SEMS // 2) + sum(self.KINDS[:kind]) + i]

    def block(self, step):
        return self.place(((self.spot.z - step + LINKS) % LINKS) * 2 + self.spot.core)

    def other(self, step):
        return self.place(((self.spot.z - step + LINKS) % LINKS) * 2 + 1 - self.spot.core)

    def start(self):
        spot = self.spot
        mine = self.block(0)
        for i in range(1, LINKS):
            piece = quarter(mine, spot.rep)
            send(piece, piece, self.sem(0, 0, i - 1), self.sem(1, 0, i - 1), spot.along_z(i))
        send(mine, mine, self.sem(0, 4, 0), self.sem(1, 4, 0), spot.sibling())

    def across(self):
        spot = self.spot
        for i in range(1, LINKS):
            piece = quarter(self.block(i), spot.rep)
            await_bytes(piece, self.sem(1, 0, i - 1))
            for axis in (self.axis, 1 - self.axis):
                send(piece, piece, self.sem(0, 1 + axis, i - 1), self.sem(1, 1 + axis, i - 1), spot.beside(axis))

    def relay(self):
        spot = self.spot
        for i in range(1, LINKS):
            piece = quarter(self.block(i), spot.turned(self.axis))
            await_bytes(piece, self.sem(1, 1 + self.axis, i - 1))
            send(piece, piece, self.sem(0, 3, i - 1), self.sem(1, 3, i - 1), spot.beside(1 - self.axis))

    def beside(self):
        spot = self.spot
        for i in range(1, LINKS):
            block = self.block(i)
            piece = quarter(block, spot.rep)
            await_bytes(piece, self.sem(1, 2 - self.axis, i - 1))
            await_bytes(piece, self.sem(1, 3, i - 1))
            send(block, block, self.sem(0, 4, i), self.sem(1, 4, i), spot.sibling())

    def finish(self):
        for i in range(LINKS):
            await_bytes(self.other(i), self.sem(1, 4, i))

    def close(self):
        piece = quarter(self.block(0), self.spot.rep)
        for kind in range(4):
            for i in range(1, LINKS):
                await_bytes(piece, self.sem(0, kind, i - 1))
        for i in range(LINKS):
            await_bytes(self.block(i), self.sem(0, 4, i))


class Reduce:
    KINDS = (LINKS, 1, 1, LINKS - 1, REPS - 1)
    SEMS = 2 * sum(KINDS)
    STAGES = ("start", "first", "second", "along", "spread", "finish")

    def __init__(self, spot, place, out, core_sum, halves, quarters, links, axis, sems):
        self.spot, self.place, self.out, self.axis, self.sems = spot, place, out, axis, sems
        self.core_sum, self.halves, self.quarters, self.links = core_sum, halves, quarters, links

    def sem(self, side, kind, i):
        return self.sems.at[side * (self.SEMS // 2) + sum(self.KINDS[:kind]) + i]

    def start(self):
        spot = self.spot
        for z in range(LINKS):
            send(self.place(z * 2 + (1 - spot.core)), self.core_sum.at[z], self.sem(0, 0, z), self.sem(1, 0, z), spot.sibling())

    def first(self):
        spot = self.spot
        for z in range(LINKS):
            total = self.core_sum.at[z]
            await_bytes(total, self.sem(1, 0, z))
            total[...] = (total[...].astype(full) + self.place(z * 2 + spot.core)[...].astype(full)).astype(low)
        theirs = half(self.core_sum, spot.turned(self.axis), self.axis)
        send(theirs, self.halves, self.sem(0, 1, 0), self.sem(1, 1, 0), spot.beside(self.axis))

    def second(self):
        spot = self.spot
        await_bytes(self.halves, self.sem(1, 1, 0))
        mine = half(self.core_sum, spot.rep, self.axis)
        self.halves[...] = (self.halves[...].astype(full) + mine[...].astype(full)).astype(low)
        theirs = half(self.halves, spot.turned(1 - self.axis), 1 - self.axis)
        send(theirs, self.quarters, self.sem(0, 2, 0), self.sem(1, 2, 0), spot.beside(1 - self.axis))

    def along(self):
        spot = self.spot
        await_bytes(self.quarters, self.sem(1, 2, 0))
        mine = half(self.halves, spot.rep, 1 - self.axis)
        self.quarters[...] = (self.quarters[...].astype(full) + mine[...].astype(full)).astype(low)
        for i in range(1, LINKS):
            send(self.quarters.at[(spot.z + i) % LINKS], self.links.at[i - 1], self.sem(0, 3, i - 1), self.sem(1, 3, i - 1), spot.along_z(i))

    def spread(self):
        spot = self.spot
        total = self.quarters[spot.z].astype(full)
        for i in range(1, LINKS):
            await_bytes(self.links.at[i - 1], self.sem(1, 3, i - 1))
            total = total + self.links[i - 1].astype(full)
        mine = quarter(self.out, spot.rep)
        mine[...] = total.astype(low)
        for j in range(1, REPS):
            send(mine, mine, self.sem(0, 4, j - 1), self.sem(1, 4, j - 1), ((spot.rep + j) % REPS, spot.shard))

    def finish(self):
        for j in range(1, REPS):
            await_bytes(quarter(self.out, (self.spot.rep - j + REPS) % REPS), self.sem(1, 4, j - 1))

    def close(self):
        for z in range(LINKS):
            await_bytes(self.core_sum.at[z], self.sem(0, 0, z))
        await_bytes(self.halves, self.sem(0, 1, 0))
        await_bytes(self.quarters, self.sem(0, 2, 0))
        for i in range(1, LINKS):
            await_bytes(self.links.at[i - 1], self.sem(0, 3, i - 1))
        for j in range(1, REPS):
            await_bytes(quarter(self.out, self.spot.rep), self.sem(0, 4, j - 1))


class ReduceSmall:
    KINDS = (LINKS, LINKS - 1, REPS - 1)
    SEMS = 2 * sum(KINDS)
    STAGES = ("start", "first", "second", "along")

    def __init__(self, spot, terms, out, core_sum, links, parts, sems):
        self.spot, self.terms, self.out, self.core_sum, self.links, self.parts, self.sems = spot, terms, out, core_sum, links, parts, sems

    sem = Reduce.sem

    def start(self):
        spot = self.spot
        for z in range(LINKS):
            send(self.terms.at[z * 2 + (1 - spot.core)], self.core_sum.at[z], self.sem(0, 0, z), self.sem(1, 0, z), spot.sibling())

    def first(self):
        spot = self.spot
        for z in range(LINKS):
            await_bytes(self.core_sum.at[z], self.sem(1, 0, z))
            self.core_sum[z] = self.core_sum[z] + self.terms[z * 2 + spot.core]
        for i in range(1, LINKS):
            send(self.core_sum.at[(spot.z + i) % LINKS], self.links.at[i - 1], self.sem(0, 1, i - 1), self.sem(1, 1, i - 1), spot.along_z(i))

    def second(self):
        spot = self.spot
        total = self.core_sum[spot.z]
        for i in range(1, LINKS):
            await_bytes(self.links.at[i - 1], self.sem(1, 1, i - 1))
            total = total + self.links[i - 1]
        self.parts[spot.rep] = total
        mine = self.parts.at[spot.rep]
        for j in range(1, REPS):
            send(mine, mine, self.sem(0, 2, j - 1), self.sem(1, 2, j - 1), ((spot.rep + j) % REPS, spot.shard))

    def along(self):
        for j in range(1, REPS):
            await_bytes(self.parts.at[(self.spot.rep - j + REPS) % REPS], self.sem(1, 2, j - 1))
        total = self.parts[0]
        for j in range(1, REPS):
            total = total + self.parts[j]
        self.out[...] = total

    def close(self):
        for z in range(LINKS):
            await_bytes(self.core_sum.at[z], self.sem(0, 0, z))
        for i in range(1, LINKS):
            await_bytes(self.links.at[i - 1], self.sem(0, 1, i - 1))
        for j in range(1, REPS):
            await_bytes(self.parts.at[self.spot.rep], self.sem(0, 2, j - 1))


OWNED = C // OWNERS
SLOTS = TILES + 1
GATHERS = 2 * TILES + 1 + GROUPS
REDUCES = 2 * TILES + 1 + (GROUPS - 1) + 3
W_Q0, W_Q1, W_Q2, W_P, W_U0, W_D0, W_U1, W_D1, W_U2, W_D2 = W_ALL = range(10)
G_D0, G_U0, G_D1, G_U1, G_D2, G_U2, G_P, G_Q0, G_Q1, G_Q2, G_K2, G_V2, G_S = G_ALL = range(10, 23)
W_Q, W_U, W_D = (W_Q0, W_Q1, W_Q2), (W_U0, W_U1, W_U2), (W_D0, W_D1, W_D2)
G_D, G_U, G_Q, G_LAST = (G_D0, G_D1, G_D2), (G_U0, G_U1, G_U2), (G_Q0, G_Q1), (G_Q2, G_K2, G_V2)
START, ACROSS, RELAY, BESIDE, ARRIVED = range(5)
FIRST, SECOND, ALONG, SPREAD, SUMMED = range(1, 6)
BEFORE = {
    3: ((W_Q0, ACROSS), (W_Q1, ACROSS), (W_Q2, START), (W_P, START),),
}
FORWARD = {
    0: ((W_Q1, RELAY), (W_Q2, ACROSS), (W_U0, START),),
    1: ((W_P, ACROSS), (W_D0, START),),
    7: ((W_Q2, RELAY), (W_P, RELAY), (W_U0, ACROSS), (W_U1, START),),
    9: ((W_D0, ACROSS), (W_D1, START),),
    14: ((W_P, BESIDE), (W_U0, RELAY), (W_D0, RELAY), (W_U1, ACROSS), (W_U2, START),),
    17: ((W_D1, ACROSS), (W_D2, START),),
}
MIDDLE = {
    0: ((W_U2, ACROSS),),
    1: ((W_U0, BESIDE), (W_D0, BESIDE), (W_U1, RELAY),),
    2: ((W_D1, RELAY), (W_D2, ACROSS),),
}
TILE_STEP = {
    0: ((W_U2, RELAY),),
    1: ((W_U1, BESIDE), (W_D1, BESIDE),),
    2: ((W_U2, BESIDE), (W_D2, RELAY),),
    3: ((W_D2, BESIDE),),
    4: ((G_D0, FIRST), (G_U0, FIRST),),
    5: ((G_D1, FIRST), (G_U1, FIRST),),
}
AFTER_TILES = {
    1: ((G_D0, SECOND), (G_U0, SECOND),),
    3: ((G_D2, FIRST), (G_U2, FIRST),),
}
BACKWARD = {
    4: ((G_D0, ALONG), (G_U0, ALONG),),
    5: ((G_D1, SECOND), (G_U1, SECOND),),
    7: ((G_P, FIRST),),
    8: ((G_D2, SECOND),),
    10: ((G_D0, SPREAD), (G_D1, ALONG), (G_U1, ALONG), (G_Q0, FIRST),),
    11: ((G_U2, SECOND),),
    14: ((G_D0, SUMMED), (G_U0, SPREAD), (G_D2, ALONG),),
    15: ((G_D1, SPREAD),),
    16: ((G_U1, SPREAD),),
    17: ((G_Q1, FIRST), (G_P, SECOND),),
    19: ((G_U0, SUMMED),),
}
LAST_STEPS = {
    0: ((G_D1, SUMMED), (G_U1, SUMMED), (G_D2, SPREAD), (G_U2, ALONG), (G_Q0, SECOND), (G_Q2, FIRST), (G_P, ALONG),),
    1: ((G_V2, FIRST),),
    2: ((G_K2, FIRST),),
    3: ((G_D2, SUMMED),),
}


def chunk_shapes():
    out = []
    for _ in range(TILES):
        out += [(128, C), (OWNED, TILE)]
    return out + [(OWNED, C)] + [(3, OWNED, GCOLS)] * (GROUPS - 1) + [(OWNED, GCOLS)] * 3


def reduce_scratch():
    out = []
    for i, dims in enumerate(chunk_shapes()):
        *lead, rows, cols = dims
        near = (rows, cols // 2) if i % 2 == 0 else (rows // 2, cols)
        out.append(pltpu.VMEM((LINKS, *dims), low))
        out.append(pltpu.VMEM((LINKS, *lead, *near), low))
        out.append(pltpu.VMEM((LINKS, *lead, rows // 2, cols // 2), low))
        out.append(pltpu.VMEM((LINKS - 1, *lead, rows // 2, cols // 2), low))
    out += [pltpu.VMEM((LINKS, 40, 128), full), pltpu.VMEM((LINKS - 1, 40, 128), full), pltpu.VMEM((REPS, 40, 128), full)]
    return out


def layer_kernel(windows, x_hbm, dy_hbm, count_ref, q32, p32, u32, d32, vec_in, tab_in, line_ref, mask_ref,
                 out_hbm, grad_hbm, gq_out, gp_out, gu_out, gd_out, gs_out, qkv_hbm, pt_hbm, n1t_hbm, *scratch):
    wq, wp, up, down, small, o_ref, x1_ref, vec_ref, sums_ref, terms_ref = scratch[:10]
    gather_sems, reduce_sems, small_sems, small_reduce_sems, local = scratch[-5:]
    reduce_refs = scratch[10:-5]
    spot = Spot()
    rows_all = windows * TOK

    def live(w):
        return (w < count_ref[0]).astype(full)

    mine = spot.shard
    V = pltpu.VMEM

    jobs = {}
    places = [(W_Q[g], lambda s, g=g: wq.at[g, :, s]) for g in range(GROUPS)] + [(W_P, lambda s: wp.at[s])]
    for t in range(TILES):
        places += [(W_U[t], lambda s, t=t: up.at[t, s]), (W_D[t], lambda s, t=t: down.at[t, s])]
    for i, (name, place) in enumerate(places):
        jobs[name] = Gather(spot, place, i % 2, gather_sems.at[i])
    places = []
    for t in range(TILES):
        slot = (t + SLOTS - 1) % SLOTS
        places.append((G_D[t], lambda s, slot=slot: down.at[slot, s], gd_out.at[t]))
        places.append((G_U[t], lambda s, slot=slot: up.at[slot, s], gu_out.at[t]))
    places.append((G_P, lambda s: wp.at[s], gp_out))
    for g in range(GROUPS - 1):
        places.append((G_Q[g], lambda s, g=g: wq.at[g, :, s], gq_out.at[g]))
    for part in range(3):
        places.append((G_LAST[part], lambda s, part=part: wq.at[GROUPS - 1, part, s], gq_out.at[GROUPS - 1, part]))
    for i, (name, place, out) in enumerate(places):
        jobs[name] = Reduce(spot, place, out, *reduce_refs[4 * i : 4 * i + 4], i % 2, reduce_sems.at[i])
    jobs[G_S] = ReduceSmall(spot, terms_ref, gs_out, *reduce_refs[-3:], small_reduce_sems)

    done = {}

    def run(name, upto):
        for stage in range(done.get(name, 0), upto + 1):
            getattr(jobs[name], jobs[name].STAGES[stage])()
        done[name] = max(done.get(name, 0), upto + 1)

    def hook(table, place):
        for item in table.get(place, ()):
            run(*item)

    def hook_window(table, g, w):
        for at in range(windows):
            place = g * windows + at
            if place in table:

                @pl.when(w == at)
                def _(place=place):
                    hook(table, place)

    barrier, peers = greet(spot)

    def cast(q_v, p_v, u_v, d_v):
        loads = [pltpu.make_async_copy(a, b, local.at[i]) for i, (a, b) in enumerate(((q32, q_v), (p32, p_v), (u32, u_v), (d32, d_v)))]
        for load in loads:
            load.start()
        small[mine] = jnp.zeros((48, 128), low)
        pad = jnp.zeros((16, 128), full)
        vec_ref[:, 0:128] = pad
        vec_ref[0:12, 0:OWNED] = vec_in[...]
        small[mine, 0:16, :] = vec_ref[:, 0:128].astype(low)
        x1_ref[0:32, 0:128] = jnp.zeros((32, 128), full)
        x1_ref[0:HEADS, 0 : tab_in.shape[1]] = tab_in[...]
        small[mine, 16:48, :] = x1_ref[0:32, 0:128].astype(low)
        loads[0].wait()
        for g in range(GROUPS):
            for part in range(3):
                wq[g, part, mine] = q_v[:, part * C + g * GCOLS : part * C + (g + 1) * GCOLS].astype(low)
        pl.semaphore_wait(barrier, peers)
        for i in range(1, OWNERS):
            send(small.at[mine], small.at[mine], small_sems.at[i], small_sems.at[OWNERS + i], (spot.rep, (mine + i) % OWNERS))
        run(W_Q0, START)
        run(W_Q1, START)
        loads[1].wait()
        wp[mine] = p_v[...].astype(low)
        loads[2].wait()
        loads[3].wait()
        for t in range(TILES):
            for s in range(OWNERS):
                src = (MLP // OWNERS) * s + 128 * t
                up[t, mine, :, s * 128 : (s + 1) * 128] = u_v[:, src : src + 128].astype(low)
            down[t, mine] = d_v[t * 128 : (t + 1) * 128, :].astype(low)

    pl.run_scoped(cast, V((OWNED, 3 * C), full), V((OWNED, C), full), V((OWNED, MLP), full), V((TILES * 128, C), full))

    def forward(x_ref, n1_ref, n1t_ref, qkv_ref, pt_ref, bias_ref):
        load = pltpu.make_async_copy(x_hbm, x_ref, local.at[0])
        load.start()
        zero_tail(n1_ref, windows)
        zero_tail(o_ref, windows)
        for i in range(1, OWNERS):
            await_bytes(small.at[(mine - i + OWNERS) % OWNERS], small_sems.at[OWNERS + i])
        tab = unpack_small(small, vec_ref)
        hook(BEFORE, 0)
        load.wait()
        hook(BEFORE, 1)

        def first_norm(w, carry):
            xhat, _ = norm_parts(x_ref[window_rows(w), :].astype(full))
            n1_ref[window_rows(w), :] = (xhat * vec_ref[0:1, :] + vec_ref[1:2, :]).astype(low)
            return carry

        lax.fori_loop(0, windows, first_norm, 0)
        hook(BEFORE, 2)
        transpose_rows(n1_ref, n1t_ref)
        save = pltpu.make_async_copy(n1t_ref, n1t_hbm, local.at[1])
        save.start()
        hook(BEFORE, 3)

        def bias(tmp_ref):
            spread_table(tab, line_ref, tmp_ref)
            hook(BEFORE, 4)
            place_bias(tmp_ref, bias_ref)

        pl.run_scoped(bias, V((2, TOK * HEADS, 128), full))
        for g in range(GROUPS):
            cols = slice(g * GCOLS, (g + 1) * GCOLS)
            held = qkv_ref.at[g % 2]
            if g >= 2:
                pltpu.make_async_copy(held, qkv_hbm.at[g - 2], local.at[2 + g % 2]).wait()
            run(W_Q[g], ARRIVED)
            n1 = n1_ref[...]
            held[0] = ((dot(n1, flat(wq[g, 0])) + vec_ref[2:3, cols]) * (HEAD_DIM**-0.5)).astype(low)
            held[1] = dot(n1, flat(wq[g, 1])).astype(low)
            held[2] = (dot(n1, flat(wq[g, 2])) + vec_ref[3:4, cols]).astype(low)
            pltpu.make_async_copy(held, qkv_hbm.at[g], local.at[2 + g % 2]).start()

            def window(w, carry, g=g, cols=cols, held=held):
                hook_window(FORWARD, g, w)
                rows = window_rows(w)
                n = g * windows + w
                slot = n % 2
                s = dot_nt(held[1, rows, :], diag(held[0, rows, :], mask_ref)) + bias_ref[g]
                e = jnp.exp(s - jnp.max(s, 0, keepdims=True))
                p = (e * (1.0 / jnp.sum(e, 0, keepdims=True))).astype(low)
                keep = pltpu.make_async_copy(pt_ref.at[slot], pt_hbm.at[n], local.at[4 + slot])

                @pl.when(n >= 2)
                def _():
                    keep.wait()

                pt_ref[slot] = p
                keep.start()
                o_ref[rows, cols] = undiag(held[2, rows, :].T, p, mask_ref).astype(low)
                return carry

            lax.fori_loop(0, windows, window, 0)

        run(W_P, ARRIVED)

        def output(w, carry):
            rows = window_rows(w)
            x1_ref[rows, :] = x_ref[rows, :].astype(full) + (dot(o_ref[rows, :], flat(wp[...])) + vec_ref[4:5, :])
            return carry

        lax.fori_loop(0, windows, output, 0)
        save.wait()
        for g in (GROUPS - 2, GROUPS - 1):
            pltpu.make_async_copy(qkv_ref.at[g % 2], qkv_hbm.at[g], local.at[2 + g % 2]).wait()
        for slot in range(2):
            pltpu.make_async_copy(pt_ref.at[slot], pt_hbm.at[0], local.at[4 + slot]).wait()

    pl.run_scoped(forward, V((rows_all, C), low), V((ROWS, C), low), V((C, ROWS), low), V((2, 3, ROWS, GCOLS), low), V((2, TOK, PACK), low),
                  V((GROUPS, TOK, PACK), full))

    def middle(n2_ref, n2t_ref, dy_ref, dyt_ref, y_ref, dn_ref, bu_ref, bsum_ref):
        load = pltpu.make_async_copy(dy_hbm, dy_ref.at[0:rows_all], local.at[0])
        load.start()
        zero_tail(n2_ref, windows)
        zero_tail(dy_ref, windows)
        hook(MIDDLE, 0)
        load.wait()

        def second_norm(w, carry):
            rows = window_rows(w)
            xhat, _ = norm_parts(x1_ref[rows, :])
            n2_ref[rows, :] = (xhat * vec_ref[5:6, :] + vec_ref[6:7, :]).astype(low)
            dy_ref[rows, :] = (dy_ref[rows, :].astype(full) * live(w)).astype(low)
            return carry

        lax.fori_loop(0, windows, second_norm, 0)
        transpose_rows(n2_ref, n2t_ref)
        hook(MIDDLE, 1)
        transpose_rows(dy_ref, dyt_ref)
        y_ref[...] = jnp.zeros_like(y_ref)
        dn_ref[...] = jnp.zeros_like(dn_ref)
        for t in range(TILES):
            for s in range(TILE // 128):
                row, left = hidden_place(t, s)
                bu_ref[t, :, s * 128 : (s + 1) * 128] = vec_ref[row : row + 1, left : left + 128]
        hook(MIDDLE, 2)
        run(W_U0, ARRIVED)
        run(W_D0, ARRIVED)
        hook(TILE_STEP, 0)
        halves = TILE // SUB

        def step(i, carry):
            for k in range(1, TILES * halves):

                @pl.when(i == k)
                def _(k=k):
                    if k % halves == 0:
                        t = k // halves
                        for name in (W_U[t], W_D[t]):
                            run(name, ARRIVED)
                        for name in (W_U[t - 1], W_D[t - 1]):
                            jobs[name].close()
                        for name in (G_D[t - 1], G_U[t - 1]):
                            run(name, START)
                    hook(TILE_STEP, k)

            t, part = i // halves, i % halves
            cols = pl.ds(pl.multiple_of(part * SUB, SUB), SUB)
            wide = SUB // 128
            slot = (t + SLOTS - 1) % SLOTS
            u = flat(up[t, :, :, cols])
            d = flat(down[t, pl.ds(part * wide, wide)])
            h = dot(n2_ref[...], u) + bu_ref[t, :, cols]
            da = dot_nt(dy_ref[...], d)
            act, slope = gelu_both(h)
            a = act.astype(low)
            dh = (da * slope).astype(low)
            bsum_ref[t, :, cols] = jnp.sum(dh.astype(full), 0, keepdims=True)
            y_ref[...] += dot(a, d)
            dn_ref[...] += dot_nt(dh, u)
            gd = dot(dyt_ref[...], a).astype(low)
            down[slot, pl.ds(part * wide, wide)] = blocks(gd.T, wide)
            up[slot, :, :, cols] = blocks(dot(n2t_ref[...], dh).astype(low), OWNERS)
            return carry

        lax.fori_loop(0, TILES * halves, step, 0)
        run(G_D[-1], START)
        run(G_U[-1], START)
        hook(AFTER_TILES, 0)
        sums_ref[...] = jnp.zeros_like(sums_ref)
        for t in range(TILES):
            for s in range(TILE // 128):
                row, left = hidden_place(t, s)
                sums_ref[row : row + 1, left : left + 128] = bsum_ref[t, :, s * 128 : (s + 1) * 128]
        transpose_rows(o_ref, dyt_ref)
        hook(AFTER_TILES, 1)

        def finish(w, carry):
            rows = window_rows(w)
            x1 = x1_ref[rows, :]
            xhat, scale = norm_parts(x1)
            dn = dn_ref[rows, :]
            dy = dy_ref[rows, :].astype(full)
            dx1 = dy + norm_back(xhat, scale, dn, vec_ref[5:6, :])
            dr = dx1.astype(low)
            sums_ref[4:5, :] += jnp.sum(dr.astype(full), 0, keepdims=True)
            sums_ref[5:6, :] += jnp.sum(dn * xhat, 0, keepdims=True)
            sums_ref[6:7, :] += jnp.sum(dn, 0, keepdims=True)
            sums_ref[7:8, :] += jnp.sum(dy, 0, keepdims=True)
            dy_ref[rows, :] = ((x1 + y_ref[rows, :] + vec_ref[7:8, :]) * live(w)).astype(low)
            x1_ref[rows, :] = dx1
            n2_ref[rows, :] = dr
            o_ref[rows, :] = dot_nt(dr, flat(wp[...])).astype(low)
            return carry

        lax.fori_loop(0, windows, finish, 0)
        save = pltpu.make_async_copy(dy_ref.at[0:rows_all], out_hbm, local.at[0])
        save.start()
        hook(AFTER_TILES, 2)
        jobs[W_P].close()
        for g in range(GROUPS):
            cols = slice(g * GCOLS, (g + 1) * GCOLS)
            wp[:, :, cols] = blocks(dot(dyt_ref[...], n2_ref[:, cols]).astype(low), OWNERS)
        run(G_P, START)
        hook(AFTER_TILES, 3)
        save.wait()

    pl.run_scoped(middle, V((ROWS, C), low), V((C, ROWS), low), V((ROWS, C), low), V((C, ROWS), low), V((ROWS, C), full), V((ROWS, C), full),
                  V((TILES, 1, TILE), full), V((TILES, 1, TILE), full))

    def backward(x_ref, n1t_ref, qkv_ref, pt_ref, dproj_ref, dn_ref, bias_ref):
        loads = [pltpu.make_async_copy(x_hbm, x_ref, local.at[0]), pltpu.make_async_copy(n1t_hbm, n1t_ref, local.at[1])]
        fetch = [pltpu.make_async_copy(qkv_hbm.at[g], qkv_ref.at[g % 2], local.at[2 + g % 2]) for g in range(GROUPS)]
        fetch[0].start()
        pltpu.make_async_copy(pt_hbm.at[0], pt_ref.at[0], local.at[4]).start()
        fetch[1].start()
        for load in loads:
            load.start()
        bias_ref[...] = jnp.zeros_like(bias_ref)
        dn_ref[...] = jnp.zeros_like(dn_ref)
        for part in range(3):
            dproj_ref[part, rows_all:, :] = jnp.zeros((ROWS - rows_all, GCOLS), low)
        for g in range(GROUPS):
            cols = slice(g * GCOLS, (g + 1) * GCOLS)
            held = qkv_ref.at[g % 2]
            fetch[g].wait()

            def window(w, carry, g=g, cols=cols, held=held):
                hook_window(BACKWARD, g, w)
                rows = window_rows(w)
                n = g * windows + w
                slot = n % 2

                @pl.when(n + 1 < GROUPS * windows)
                def _():
                    pltpu.make_async_copy(pt_hbm.at[n + 1], pt_ref.at[1 - slot], local.at[5 - slot]).start()

                pltpu.make_async_copy(pt_hbm.at[n], pt_ref.at[slot], local.at[4 + slot]).wait()
                q = held[0, rows, :]
                k = held[1, rows, :]
                v = held[2, rows, :]
                p = pt_ref[slot]
                do = diag(o_ref[rows, cols], mask_ref)
                dp = dot_nt(v, do)
                dv = dot(p, do).astype(low)
                pf = p.astype(full)
                ds = (pf * (dp - jnp.sum(pf * dp, 0, keepdims=True))).astype(low)
                bias_ref[g] += ds.astype(full)
                dproj_ref[1, rows, :] = dot(ds, diag(q, mask_ref)).astype(low)
                dq = (undiag(k.T, ds, mask_ref) * (HEAD_DIM**-0.5)).astype(low)
                dproj_ref[0, rows, :] = dq
                dproj_ref[2, rows, :] = dv
                sums_ref[2:3, cols] += jnp.sum(dq.astype(full), 0, keepdims=True)
                sums_ref[3:4, cols] += jnp.sum(dv.astype(full), 0, keepdims=True)
                return carry

            lax.fori_loop(0, windows, window, 0)
            if g + 2 < GROUPS:
                fetch[g + 2].start()
            if g == 0:
                for load in loads:
                    load.wait()
            jobs[W_Q[g]].close()
            for part in range(3):
                d = dproj_ref[part]
                dn_ref[...] += dot_nt(d, flat(wq[g, part]))
                wq[g, part] = blocks(dot(n1t_ref[...], d).astype(low), OWNERS)
                if g == GROUPS - 1:
                    run(G_LAST[part], START)
            if g < GROUPS - 1:
                run(G_Q[g], START)
        hook(LAST_STEPS, 0)

        def last_norm(grad_ref):
            def finish(w, carry):
                rows = window_rows(w)
                slot = w % 2
                xhat, scale = norm_parts(x_ref[rows, :].astype(full))
                dn = dn_ref[rows, :]
                save = pltpu.make_async_copy(grad_ref.at[slot], grad_hbm.at[rows], local.at[4 + slot])

                @pl.when(w >= 2)
                def _():
                    save.wait()

                grad_ref[slot] = x1_ref[rows, :] + norm_back(xhat, scale, dn, vec_ref[0:1, :])
                save.start()
                sums_ref[0:1, :] += jnp.sum(dn * xhat, 0, keepdims=True)
                sums_ref[1:2, :] += jnp.sum(dn, 0, keepdims=True)
                return carry

            lax.fori_loop(0, windows, finish, 0)
            hook(LAST_STEPS, 1)
            for slot in range(2):
                pltpu.make_async_copy(grad_ref.at[slot], grad_hbm.at[pl.ds(0, TOK)], local.at[4 + slot]).wait()

        pl.run_scoped(last_norm, V((2, TOK, C), full))
        hook(LAST_STEPS, 2)

        def table(tmp_ref):
            pack_small(sums_ref[...], table_grad(line_ref, tmp_ref, bias_ref), terms_ref)

        pl.run_scoped(table, V((2, TOK * HEADS, 128), full))
        run(G_S, START)
        hook(LAST_STEPS, 3)
        for stage in range(len(Reduce.STAGES)):
            for name in G_ALL:
                if stage < len(jobs[name].STAGES):
                    run(name, stage)

    pl.run_scoped(backward, V((rows_all, C), low), V((C, ROWS), low), V((2, 3, ROWS, GCOLS), low), V((2, TOK, PACK), low), V((3, ROWS, GCOLS), low),
                  V((ROWS, C), full), V((GROUPS, TOK, PACK), full))
    jobs[W_U[-1]].close()
    jobs[W_D[-1]].close()
    for i in range(1, OWNERS):
        await_bytes(small.at[mine], small_sems.at[i])
    for name in G_ALL:
        jobs[name].close()


def shape(dims, kind):
    return jax.ShapeDtypeStruct(dims, kind)


def adamw(weight, moment, second, gradient, step_rate):
    moment_new = beta_one * moment + (1.0 - beta_one) * gradient
    second_new = beta_two * second + (1.0 - beta_two) * gradient * gradient
    update = moment_new * (1.0 / (1.0 - beta_one**STEP)) / (jnp.sqrt(second_new * (1.0 / (1.0 - beta_two**STEP))) + adam_eps)
    weight_new = weight * (1.0 - step_rate * weight_decay) - step_rate * update
    return (weight_new, moment_new, second_new)


def update_kernel(*refs):
    gq, gp, gu, gd, gs = refs[:5]
    ins = [refs[5 + 3 * i : 8 + 3 * i] for i in range(6)]
    outs = [refs[25 + 4 * i : 29 + 4 * i] for i in range(4)] + [refs[41:44], refs[44:47]]
    for i in range(2):
        refs[47 + i][...] = refs[23 + i][...]

    def piece(which, place, gradient):
        new = adamw(*(ref[place] for ref in ins[which]), gradient, step_rates[which])
        for ref, value in zip(outs[which], new):
            ref[place] = value
        if which < 4:
            outs[which][3][place] = new[0].astype(low)

    for part in range(3):
        for g in range(GROUPS):
            left = part * C + g * GCOLS
            piece(0, (slice(None), slice(left, left + GCOLS)), gq[g, part].astype(full))
    piece(1, (slice(None), slice(None)), gp[...].astype(full))
    for t in range(TILES):
        for s in range(OWNERS):
            left = (MLP // OWNERS) * s + 128 * t
            piece(2, (slice(None), slice(left, left + 128)), gu[t, :, s * 128 : (s + 1) * 128].astype(full))
    piece(3, (slice(None), slice(None)), gd[0].astype(full))

    @pl.when(pl.program_id(0) == 0)
    def _():
        every = (slice(None), slice(None))
        piece(4, every, gs[0:12, 0:OWNED])
        piece(5, every, gs[16:40, 0 : ins[5][0].shape[1]])


def update(gq, gp, gu, gd, gs, states, results):
    steps = OWNED // 16

    def rows_of(array):
        tall = array.shape[0] // steps
        return pl.BlockSpec((tall, array.shape[1]), lambda i: (i, 0))

    def whole(array):
        return pl.BlockSpec(array.shape, lambda i: (0, 0))

    per_tile = 128 * TILES // steps
    specs = [
        pl.BlockSpec((GROUPS, 3, 16, GCOLS), lambda i: (0, 0, i, 0)),
        pl.BlockSpec((16, C), lambda i: (i, 0)),
        pl.BlockSpec((TILES, 16, TILE), lambda i: (0, i, 0)),
        pl.BlockSpec((1, per_tile, C), lambda i: (i // (128 // per_tile), i % (128 // per_tile), 0)),
        whole(gs),
    ]
    out_shapes, out_specs = [], []
    for i, group in enumerate(states):
        for array in group:
            specs.append(rows_of(array) if i < 4 else whole(array))
            out_shapes.append(shape(array.shape, full))
            out_specs.append(specs[-1])
        if i < 4:
            out_shapes.append(shape(group[0].shape, low))
            out_specs.append(rows_of(group[0]))
    results = [array.reshape(steps, -1, C) for array in results]
    for array in results:
        specs.append(pl.BlockSpec((1, *array.shape[1:]), lambda i: (i, 0, 0)))
        out_shapes.append(shape(array.shape, array.dtype))
        out_specs.append(specs[-1])
    return pl.pallas_call(
        update_kernel,
        grid=(steps,),
        in_specs=specs,
        out_specs=out_specs,
        out_shape=out_shapes,
        compiler_params=pltpu.CompilerParams(vmem_limit_bytes=63 * MIB),
        name="update",
    )(gq, gp, gu, gd, gs, *[array for group in states for array in group], *results)


def shards(
    tokens, out_grad, window_count,
    qkv_weight, qkv_first, qkv_second,
    output_weight, output_first, output_second,
    up_weight, up_first, up_second,
    down_weight, down_first, down_second,
    vectors, vector_first, vector_second,
    bias_table, table_first, table_second,
):
    windows = tokens.shape[0]
    rows = windows * TOK
    V = pltpu.VMEM
    D = pltpu.SemaphoreType.DMA
    hbm = pl.BlockSpec(memory_space=pl.ANY)
    vmem = pl.BlockSpec(memory_space=pltpu.VMEM)
    result = pl.pallas_call(
        functools.partial(layer_kernel, windows),
        out_shape=[
            shape((rows, C), low), shape((rows, C), full),
            shape((GROUPS, 3, OWNED, GCOLS), low), shape((OWNED, C), low), shape((TILES, OWNED, TILE), low), shape((TILES, 128, C), low),
            shape((40, 128), full),
            shape((GROUPS, 3, ROWS, GCOLS), low), shape((GROUPS * windows, TOK, PACK), low), shape((C, ROWS), low)],
        in_specs=[hbm, hbm, pl.BlockSpec(memory_space=pltpu.SMEM)] + [hbm] * 4 + [vmem] * 4,
        out_specs=[hbm, hbm] + [vmem] * 5 + [hbm] * 3,
        scratch_shapes=[
            V((GROUPS, 3, OWNERS, OWNED, GCOLS), low), V((OWNERS, OWNED, C), low), V((SLOTS, OWNERS, OWNED, TILE), low),
            V((SLOTS, OWNERS, 128, C), low), V((OWNERS, 48, 128), low), V((ROWS, C), low), V((rows, C), full), V((16, C), full), V((16, C), full),
            V((OWNERS, 40, 128), full)]
        + reduce_scratch()
        + [D((GATHERS, Gather.SEMS)), D((REDUCES, Reduce.SEMS)), D((2 * OWNERS,)), D((ReduceSmall.SEMS,)), D((6,))],
        compiler_params=pltpu.CompilerParams(vmem_limit_bytes=63 * MIB, collective_id=0, has_side_effects=True),
        name="layer",
    )(tokens.reshape(rows, C), out_grad.reshape(rows, C), window_count, qkv_weight, output_weight, up_weight, down_weight, vectors, bias_table.T,
      jnp.asarray(line_matrix(), low), jnp.asarray(head_masks(), low))
    out, grad, gq, gp, gu, gd, gs = result[:7]
    new = update(gq, gp, gu, gd, gs, (
        (qkv_weight, qkv_first, qkv_second), (output_weight, output_first, output_second), (up_weight, up_first, up_second),
        (down_weight, down_first, down_second), (vectors, vector_first, vector_second), (bias_table.T, table_first.T, table_second.T)), (out, grad))
    *new, out, grad = new
    return (out.reshape(tokens.shape), grad.reshape(tokens.shape), *new[:-3], *(array.T for array in new[-3:]))


def vmem_call(body, outs, scratch, args, name, limit=60, **params):
    spec = pl.BlockSpec(memory_space=pltpu.VMEM)
    return pl.pallas_call(
        body,
        out_shape=outs,
        in_specs=[pl.BlockSpec(memory_space=pltpu.SMEM) if a.dtype == full and a.ndim == 1 else spec for a in args],
        out_specs=[spec] * len(outs),
        scratch_shapes=scratch,
        compiler_params=pltpu.CompilerParams(vmem_limit_bytes=limit * MIB, **params),
        name=name,
    )(*args)


def local_step(tokens, out_grad, window_count, small, wq, wp, up, down):
    windows = tokens.shape[0]
    rows = windows * TOK
    owned = C // OWNERS
    V = pltpu.VMEM
    x = tokens.reshape(rows, C)
    dy = out_grad.reshape(rows, C)
    live = (jnp.arange(windows) < window_count[0]).astype(full)
    line = jnp.asarray(line_matrix(), low)
    masks = jnp.asarray(head_masks(), low)
    qkv, pt, o, x1, n1t, vec = vmem_call(
        functools.partial(attention_forward, windows),
        [shape((9, ROWS, GCOLS), low), shape((GROUPS, windows, TOK, PACK), low), shape((ROWS, C), low), shape((rows, C), full), shape((C, ROWS), low),
         shape((16, C), full)],
        [V((ROWS, C), low), V((GROUPS, TOK, PACK), full), V((2, TOK * HEADS, 128), full)],
        (x, small, line, masks, wq, wp), "attention_forward")
    out, dx1, do, gup, gdown, gout, sums = vmem_call(
        functools.partial(feed_forward, windows),
        [shape((rows, C), low), shape((ROWS, C), full), shape((rows, C), low), shape((TILES, OWNERS, owned, TILE), low),
         shape((TILES, OWNERS, C, 128), low), shape((OWNERS, owned, C), low), shape((16, C), full)],
        [V((ROWS, C), low), V((C, ROWS), low), V((ROWS, C), low), V((C, ROWS), low), V((ROWS, C), full), V((ROWS, C), full),
         V((TILES, 1, TILE), full), V((TILES, 1, TILE), full)],
        (x1, dy, live, vec, up, down, wp, o), "feed_forward")
    gq, gsmall, grad = vmem_call(
        functools.partial(attention_backward, windows),
        [shape((GROUPS, 3, OWNERS, owned, GCOLS), low), shape((OWNERS, 40, 128), full), shape((rows, C), full)],
        [V((16, C), full), V((GROUPS, TOK, PACK), full), V((2, TOK * HEADS, 128), full), V((3, ROWS, GCOLS), low), V((ROWS, C), full)],
        (x, vec, line, masks, wq, qkv, pt, do, dx1, n1t, sums), "attention_backward")
    return out.reshape(tokens.shape), grad.reshape(tokens.shape), gq, gout, gup, gdown, gsmall


def shards_general(
    tokens, out_grad, window_count,
    qkv_weight, qkv_first, qkv_second,
    output_weight, output_first, output_second,
    up_weight, up_first, up_second,
    down_weight, down_first, down_second,
    vectors, vector_first, vector_second,
    bias_table, table_first, table_second,
):
    gather = functools.partial(lax.all_gather, axis_name="shard", tiled=True)
    scatter = functools.partial(lax.psum_scatter, axis_name="shard", tiled=True)
    owned = C // OWNERS
    wq = gather(qkv_weight.astype(low), axis=0).reshape(OWNERS, owned, 3, GROUPS, GCOLS).transpose(3, 2, 0, 1, 4)
    wp = gather(output_weight.astype(low), axis=0).reshape(OWNERS, owned, C)
    up = gather(up_weight.astype(low), axis=0).reshape(OWNERS, owned, OWNERS, TILES, 128).transpose(3, 0, 1, 2, 4)
    up = up.reshape(TILES, OWNERS, owned, TILE)
    down = gather(down_weight.astype(low), axis=0).reshape(OWNERS, TILES, 128, C).transpose(1, 0, 2, 3)
    vec = gather(vectors.astype(low), axis=1)
    tab = gather(bias_table.astype(low), axis=0)
    table_rows = tab.shape[0]
    count = TAB_ROWS // OWNERS
    vec = vec.reshape(12, OWNERS, owned).transpose(1, 0, 2)
    tab = tab[:TAB_ROWS].reshape(OWNERS, count, HEADS).transpose(0, 2, 1)
    small = jnp.concatenate([jnp.pad(vec, ((0, 0), (0, 4), (0, 128 - owned))), jnp.pad(tab, ((0, 0), (0, 8), (0, 128 - count)))], 1)
    out, grad, gq, gp, gu, gd, gs = local_step(tokens, out_grad, window_count, small, wq, wp, up, down)
    gq = gq.astype(full).transpose(2, 3, 1, 0, 4).reshape(C, 3 * C)
    gu = gu.astype(full).reshape(TILES, C, OWNERS, 128).transpose(1, 2, 0, 3).reshape(C, MLP)
    gd = gd.astype(full).transpose(1, 0, 3, 2).reshape(MLP, C)
    gv = gs[:, :12, :owned].transpose(1, 0, 2).reshape(12, C)
    gb = gs[:, 16:40, :count].transpose(0, 2, 1).reshape(TAB_ROWS, HEADS)
    gb = jnp.pad(gb, ((0, table_rows - TAB_ROWS), (0, 0)))
    totals = lax.psum(
        (scatter(gq, scatter_dimension=0), scatter(gp.astype(full).reshape(C, C), scatter_dimension=0), scatter(gu, scatter_dimension=0),
         scatter(gd, scatter_dimension=0), scatter(gv, scatter_dimension=1), scatter(gb, scatter_dimension=0)), "rep")
    states = (
        (qkv_weight, qkv_first, qkv_second), (output_weight, output_first, output_second), (up_weight, up_first, up_second),
        (down_weight, down_first, down_second), (vectors, vector_first, vector_second), (bias_table, table_first, table_second))
    results = [out, grad]
    for i, (state, total, rate) in enumerate(zip(states, totals, step_rates)):
        new = adamw(*state, total, rate)
        results += [*new, new[0].astype(low)] if i < 4 else [*new]
    return tuple(results)


def solution(mesh):
    wins = P(("rep", "shard"), None, None)
    rows = P("shard", None)
    cols = P(None, "shard")
    fits = mesh.shape["rep"] == REPS and mesh.shape["shard"] == OWNERS
    return jax.shard_map(
        shards if fits else shards_general,
        mesh=mesh,
        in_specs=(wins, wins, P(("rep", "shard"))) + (rows,) * 12 + (cols,) * 3 + (rows,) * 3,
        out_specs=(wins, wins) + (rows,) * 16 + (cols,) * 3 + (rows,) * 3,
        check_vma=False,
    )
```

```python
import functools
import math

import jax
import jax.numpy as jnp
import numpy as np
from jax import lax
from jax.experimental import pallas as pl
from jax.experimental.pallas import tpu as pltpu
from jax.sharding import PartitionSpec as P

C = 768
HEADS = 24
MLP = 3072
WIN = 12
STEP = 5
HEAD_DIM = 32
SPAN = 2 * WIN - 1
TOK = WIN * WIN
TAB_ROWS = 536
ROWS = 1024
GROUPS = 3
GCOLS = 256
GHEADS = 8
PACK = GHEADS * TOK
TAB_LANES = 640
TILES = 3
TILE = MLP // TILES
SUB = 512
LINE = 384
MIB = 1 << 20

beta_one = 0.5
beta_two = 0.6
weight_decay = 0.05
adam_eps = 1e-08
norm_eps = 1e-05
step_rates = (0.04, 0.15, 0.04, 0.02, 0.2, 1.0)
low = jnp.bfloat16
full = jnp.float32
NT = (((1,), (1,)), ((), ()))


def dot(a, b):
    return jnp.dot(a, b, preferred_element_type=full)


def dot_nt(a, b):
    return lax.dot_general(a, b, NT, preferred_element_type=full)


def line_matrix():
    out = np.zeros((TAB_LANES, LINE), np.float32)
    col = np.arange(SPAN * WIN)
    out[(col // WIN) * SPAN + col % WIN + WIN - 1, col] = 1.0
    return out


def head_masks():
    lane = np.arange(GCOLS) // HEAD_DIM
    one = (lane[None, :] == np.arange(GHEADS)[:, None]).astype(np.float32)
    return np.broadcast_to(one[:, None, :], (GHEADS, 16, GCOLS))


def norm_parts(z):
    mean = jnp.sum(z, -1, keepdims=True) * (1.0 / C)
    center = z - mean
    spread = jnp.sum(center * center, -1, keepdims=True) * (1.0 / C)
    scale = lax.rsqrt(spread + norm_eps)
    return center * scale, scale


def norm_back(xhat, scale, dn, gain):
    g = dn * gain
    m1 = jnp.sum(g, -1, keepdims=True) * (1.0 / C)
    m2 = jnp.sum(g * xhat, -1, keepdims=True) * (1.0 / C)
    return scale * (g - m1 - xhat * m2)


def diag(x, mask_ref):
    head = x[0:128].reshape(8, 16, GCOLS)
    tail = x[128:144]
    parts = []
    for h in range(GHEADS):
        parts.append((head * mask_ref[h][None]).reshape(128, GCOLS))
    for h in range(GHEADS):
        parts.append(tail * mask_ref[h])
    return jnp.concatenate(parts, 0)


def undiag(xt, m, mask_ref):
    main = []
    for h in range(0, GHEADS, 2):
        r = dot(xt[h * HEAD_DIM : (h + 2) * HEAD_DIM], m[:, h * 128 : (h + 2) * 128])
        main.append(r[0:HEAD_DIM, 0:128])
        main.append(r[HEAD_DIM : 2 * HEAD_DIM, 128:256])
    main = jnp.concatenate(main, 0)
    rest = dot(xt, m[:, GHEADS * 128 :])
    rest_t = rest.T.reshape(GHEADS, 16, GCOLS)
    keep = mask_ref[...].astype(full)
    return jnp.concatenate([main.T, jnp.sum(rest_t * keep, 0)], 0)


def flat(x):
    return x.reshape(x.shape[0] * x.shape[1], x.shape[2])


def blocks(x, owners):
    return x.reshape(owners, x.shape[0] // owners, x.shape[1])


def hidden_place(t, s):
    at = (MLP // GHEADS) * s + 128 * t
    return 8 + at // C, at % C


def unpack_small(small_ref, vec_ref):
    owners = small_ref.shape[0]
    width = C // owners
    count = TAB_ROWS // owners
    vec = jnp.zeros((16, C), full)
    tab = jnp.zeros((HEADS, TAB_LANES), full)
    lane = lax.broadcasted_iota(jnp.int32, (16, 128), 1)
    lane_tab = lax.broadcasted_iota(jnp.int32, (HEADS, 128), 1)
    for s in range(owners):
        piece = small_ref[s].astype(full)
        part = jnp.where(lane < width, piece[0:16], 0.0)
        part = jnp.concatenate([part, jnp.zeros((16, C - 128), full)], 1)
        vec = vec + (pltpu.roll(part, width * s, 1) if s else part)
        part = jnp.where(lane_tab < count, piece[16 : 16 + HEADS], 0.0)
        part = jnp.concatenate([part, jnp.zeros((HEADS, TAB_LANES - 128), full)], 1)
        tab = tab + (pltpu.roll(part, count * s, 1) if s else part)
    vec_ref[...] = vec
    return tab


def pack_small(vec, tab, out_ref):
    owners = out_ref.shape[0]
    width = C // owners
    count = TAB_ROWS // owners
    for s in range(owners):
        out_ref[s, 0:16, :] = (pltpu.roll(vec, C - width * s, 1) if s else vec)[:, 0:128]
        out_ref[s, 16:40, :] = (pltpu.roll(tab, TAB_LANES - count * s, 1) if s else tab)[:, 0:128]


def spread_table(tab, line_ref, tmp_ref):
    def column(cj, carry):
        shifted = pltpu.roll(tab, cj, 1)
        line = dot(shifted.astype(low), line_ref[...])
        for rj in range(WIN):
            cut = (WIN - 1 - rj) * WIN
            part = pltpu.roll(line, LINE - cut, 1) if cut else line
            row = pl.multiple_of((rj * WIN + cj) * HEADS, 8)
            tmp_ref[0, pl.ds(row, HEADS), :] = part[:, 0:128]
            tmp_ref[1, pl.ds(row, HEADS), :] = part[:, 128:256]
        return carry

    lax.fori_loop(0, WIN, column, 0)


def place_bias(tmp_ref, bias_ref):
    lane = lax.broadcasted_iota(jnp.int32, (TOK, 128), 1)
    for g in range(GROUPS):
        rest = jnp.zeros((TOK, 128), full)
        for h in range(GHEADS):
            at = pl.ds(g * GHEADS + h, TOK, stride=HEADS)
            bias_ref[g, :, h * 128 : (h + 1) * 128] = tmp_ref[0, at, :]
            piece = tmp_ref[1, at, :]
            piece = pltpu.roll(piece, 16 * h, 1) if h else piece
            rest = jnp.where((lane >= 16 * h) & (lane < 16 * h + 16), piece, rest)
        bias_ref[g, :, GHEADS * 128 :] = rest


def table_grad(line_ref, tmp_ref, bias_ref):
    lane = lax.broadcasted_iota(jnp.int32, (TOK, 128), 1)
    for g in range(GROUPS):
        rest = bias_ref[g, :, GHEADS * 128 :]
        for h in range(GHEADS):
            at = pl.ds(g * GHEADS + h, TOK, stride=HEADS)
            tmp_ref[0, at, :] = bias_ref[g, :, h * 128 : (h + 1) * 128]
            piece = pltpu.roll(rest, 128 - 16 * h, 1) if h else rest
            tmp_ref[1, at, :] = jnp.where(lane < 16, piece, 0.0)

    def column(cj, total):
        line = jnp.zeros((HEADS, LINE), full)
        for rj in range(WIN):
            cut = (WIN - 1 - rj) * WIN
            row = pl.multiple_of((rj * WIN + cj) * HEADS, 8)
            part = jnp.concatenate([tmp_ref[0, pl.ds(row, HEADS), :], tmp_ref[1, pl.ds(row, HEADS), :], jnp.zeros((HEADS, 128), full)], 1)
            line = line + (pltpu.roll(part, cut, 1) if cut else part)
        high = line.astype(low)
        rest = (line - high.astype(full)).astype(low)
        spread = dot_nt(high, line_ref[...]) + dot_nt(rest, line_ref[...])
        return total + pltpu.roll(spread, TAB_LANES - cj, 1)

    return lax.fori_loop(0, WIN, column, jnp.zeros((HEADS, TAB_LANES), full))


def transpose_rows(src_ref, dst_ref):
    def block(i, carry):
        at = pl.multiple_of(i * 128, 128)
        dst_ref[0 : src_ref.shape[1], pl.ds(at, 128)] = src_ref[pl.ds(at, 128), :].T
        return carry

    lax.fori_loop(0, ROWS // 128, block, 0)


def window_rows(w):
    return slice(w * TOK, (w + 1) * TOK) if isinstance(w, int) else pl.ds(pl.multiple_of(w * TOK, 16), TOK)


def zero_tail(ref, windows):
    at = windows * TOK
    ref[at:ROWS, :] = jnp.zeros((ROWS - at, ref.shape[1]), ref.dtype)


def attention_forward(windows, x_ref, small_ref, line_ref, mask_ref, wq_ref, wp_ref,
                      qkv_ref, pt_ref, o_ref, x1_ref, n1t_ref, vec_ref, n1_ref, bias_ref, tmp_ref):
    tab = unpack_small(small_ref, vec_ref)
    spread_table(tab, line_ref, tmp_ref)
    place_bias(tmp_ref, bias_ref)
    zero_tail(n1_ref, windows)
    zero_tail(o_ref, windows)

    def first_norm(w, carry):
        xhat, _ = norm_parts(x_ref[window_rows(w), :].astype(full))
        n1_ref[window_rows(w), :] = (xhat * vec_ref[0:1, :] + vec_ref[1:2, :]).astype(low)
        return carry

    lax.fori_loop(0, windows, first_norm, 0)
    transpose_rows(n1_ref, n1t_ref)

    def group(g, carry):
        cols = pl.ds(pl.multiple_of(g * GCOLS, GCOLS), GCOLS)
        n1 = n1_ref[...]
        qkv_ref[g] = ((dot(n1, flat(wq_ref[g, 0])) + vec_ref[2:3, cols]) * (HEAD_DIM**-0.5)).astype(low)
        qkv_ref[GROUPS + g] = dot(n1, flat(wq_ref[g, 1])).astype(low)
        qkv_ref[2 * GROUPS + g] = (dot(n1, flat(wq_ref[g, 2])) + vec_ref[3:4, cols]).astype(low)

        def window(w, inner):
            rows = window_rows(w)
            q = qkv_ref[g, rows, :]
            k = qkv_ref[GROUPS + g, rows, :]
            v = qkv_ref[2 * GROUPS + g, rows, :]
            s = dot_nt(k, diag(q, mask_ref)) + bias_ref[g]
            e = jnp.exp(s - jnp.max(s, 0, keepdims=True))
            p = (e * (1.0 / jnp.sum(e, 0, keepdims=True))).astype(low)
            pt_ref[g, w] = p
            o_ref[rows, cols] = undiag(v.T, p, mask_ref).astype(low)
            return inner

        lax.fori_loop(0, windows, window, 0)
        return carry

    lax.fori_loop(0, GROUPS, group, 0)

    def output(w, carry):
        rows = window_rows(w)
        branch = dot(o_ref[rows, :], flat(wp_ref[...])) + vec_ref[4:5, :]
        x1_ref[rows, :] = x_ref[rows, :].astype(full) + branch
        return carry

    lax.fori_loop(0, windows, output, 0)


def gelu_both(h):
    c = math.sqrt(2.0 / math.pi)
    square = h * h
    t = jnp.tanh(h * (c + (c * 0.044715) * square))
    half = 0.5 + 0.5 * t
    act = h * half
    return act, half + act * (1.0 - half) * (2.0 * c + (6.0 * c * 0.044715) * square)


def feed_forward(windows, x1_ref, dy_ref, live_ref, vec_ref, up_ref, down_ref, wp_ref, o_ref,
                 out_ref, dx1_ref, do_ref, gup_ref, gdown_ref, gout_ref, sums_ref,
                 n2_ref, n2t_ref, dy2_ref, dyt_ref, y_ref, dn_ref, bu_ref, bsum_ref):
    zero_tail(n2_ref, windows)
    zero_tail(dy2_ref, windows)

    def second_norm(w, carry):
        rows = window_rows(w)
        xhat, _ = norm_parts(x1_ref[rows, :])
        n2_ref[rows, :] = (xhat * vec_ref[5:6, :] + vec_ref[6:7, :]).astype(low)
        dy2_ref[rows, :] = (dy_ref[rows, :].astype(full) * live_ref[w]).astype(low)
        return carry

    lax.fori_loop(0, windows, second_norm, 0)
    transpose_rows(n2_ref, n2t_ref)
    transpose_rows(dy2_ref, dyt_ref)
    y_ref[...] = jnp.zeros_like(y_ref)
    dn_ref[...] = jnp.zeros_like(dn_ref)
    owners = gup_ref.shape[1]
    for t in range(TILES):
        for s in range(TILE // 128):
            row, at = hidden_place(t, s)
            bu_ref[t, :, s * 128 : (s + 1) * 128] = vec_ref[row : row + 1, at : at + 128]

    def step(t, carry):
        for part in range(TILE // SUB):
            cols = slice(part * SUB, (part + 1) * SUB)
            up = flat(up_ref[t, :, :, cols])
            down = flat(down_ref[t, part * SUB // 128 : (part + 1) * SUB // 128])
            h = dot(n2_ref[...], up) + bu_ref[t, :, cols]
            da = dot_nt(dy2_ref[...], down)
            act, slope = gelu_both(h)
            a = act.astype(low)
            dh = (da * slope).astype(low)
            bsum_ref[t, :, cols] = jnp.sum(dh.astype(full), 0, keepdims=True)
            y_ref[...] += dot(a, down)
            dn_ref[...] += dot_nt(dh, up)
            gd = dot(dyt_ref[...], a).astype(low)
            for b in range(SUB // 128):
                gdown_ref[t, part * SUB // 128 + b] = gd[:, b * 128 : (b + 1) * 128]
            gup_ref[t, :, :, cols] = blocks(dot(n2t_ref[...], dh).astype(low), owners)
        return carry

    lax.fori_loop(0, TILES, step, 0)
    sums_ref[...] = jnp.zeros_like(sums_ref)
    for t in range(TILES):
        for s in range(TILE // 128):
            row, at = hidden_place(t, s)
            sums_ref[row : row + 1, at : at + 128] = bsum_ref[t, :, s * 128 : (s + 1) * 128]
    zero_tail(dx1_ref, windows)

    def finish(w, carry):
        rows = window_rows(w)
        x1 = x1_ref[rows, :]
        out_ref[rows, :] = ((x1 + y_ref[rows, :] + vec_ref[7:8, :]) * live_ref[w]).astype(low)
        xhat, scale = norm_parts(x1)
        dn = dn_ref[rows, :]
        dy = dy2_ref[rows, :].astype(full)
        dx1 = dy + norm_back(xhat, scale, dn, vec_ref[5:6, :])
        dx1_ref[rows, :] = dx1
        dr = dx1.astype(low)
        n2_ref[rows, :] = dr
        do_ref[rows, :] = dot_nt(dr, flat(wp_ref[...])).astype(low)
        sums_ref[4:5, :] += jnp.sum(dr.astype(full), 0, keepdims=True)
        sums_ref[5:6, :] += jnp.sum(dn * xhat, 0, keepdims=True)
        sums_ref[6:7, :] += jnp.sum(dn, 0, keepdims=True)
        sums_ref[7:8, :] += jnp.sum(dy, 0, keepdims=True)
        return carry

    lax.fori_loop(0, windows, finish, 0)
    transpose_rows(o_ref, dyt_ref)
    for g in range(GROUPS):
        at = pl.ds(g * GCOLS, GCOLS)
        gout_ref[:, :, at] = blocks(dot(dyt_ref[...], n2_ref[:, at]).astype(low), gout_ref.shape[0])


def attention_backward(windows, x_ref, vec_ref, line_ref, mask_ref, wq_ref, qkv_ref, pt_ref, do_ref, dx1_ref, n1t_ref, sums_in_ref,
                       gq_ref, gsmall_ref, grad_ref, sums_ref, bias_ref, tmp_ref, dproj_ref, dn_ref):
    bias_ref[...] = jnp.zeros_like(bias_ref)
    dn_ref[...] = jnp.zeros_like(dn_ref)
    sums_ref[...] = sums_in_ref[...]
    for part in range(3):
        dproj_ref[part, windows * TOK :, :] = jnp.zeros((ROWS - windows * TOK, GCOLS), low)

    def group(g, carry):
        cols = pl.ds(pl.multiple_of(g * GCOLS, GCOLS), GCOLS)

        def window(w, inner):
            rows = window_rows(w)
            q = qkv_ref[g, rows, :]
            k = qkv_ref[GROUPS + g, rows, :]
            v = qkv_ref[2 * GROUPS + g, rows, :]
            p = pt_ref[g, w]
            do = diag(do_ref[rows, cols], mask_ref)
            dp = dot_nt(v, do)
            dv = dot(p, do)
            pf = p.astype(full)
            ds = (pf * (dp - jnp.sum(pf * dp, 0, keepdims=True))).astype(low)
            bias_ref[g] += ds.astype(full)
            dk = dot(ds, diag(q, mask_ref))
            dq = undiag(k.T, ds, mask_ref) * (HEAD_DIM**-0.5)
            dq = dq.astype(low)
            dv = dv.astype(low)
            dproj_ref[0, rows, :] = dq
            dproj_ref[1, rows, :] = dk.astype(low)
            dproj_ref[2, rows, :] = dv
            sums_ref[2:3, cols] += jnp.sum(dq.astype(full), 0, keepdims=True)
            sums_ref[3:4, cols] += jnp.sum(dv.astype(full), 0, keepdims=True)
            return inner

        lax.fori_loop(0, windows, window, 0)
        for part in range(3):
            d = dproj_ref[part]
            gq_ref[g, part] = blocks(dot(n1t_ref[...], d).astype(low), gq_ref.shape[2])
            dn_ref[...] += dot_nt(d, flat(wq_ref[g, part]))
        return carry

    lax.fori_loop(0, GROUPS, group, 0)

    def finish(w, carry):
        rows = window_rows(w)
        xhat, scale = norm_parts(x_ref[rows, :].astype(full))
        dn = dn_ref[rows, :]
        grad_ref[rows, :] = dx1_ref[rows, :] + norm_back(xhat, scale, dn, vec_ref[0:1, :])
        sums_ref[0:1, :] += jnp.sum(dn * xhat, 0, keepdims=True)
        sums_ref[1:2, :] += jnp.sum(dn, 0, keepdims=True)
        return carry

    lax.fori_loop(0, windows, finish, 0)
    pack_small(sums_ref[...], table_grad(line_ref, tmp_ref, bias_ref), gsmall_ref)


MESH = pl.DeviceIdType.MESH
REPS = 4
OWNERS = 8
LINKS = OWNERS // 2


class Spot:
    def __init__(self):
        self.rep = lax.axis_index("rep")
        self.shard = lax.axis_index("shard")
        self.z = self.shard // 2
        self.core = self.shard % 2

    def sibling(self):
        return (self.rep, self.z * 2 + (1 - self.core))

    def along_z(self, step):
        return (self.rep, ((self.z + step) % LINKS) * 2 + self.core)

    def turned(self, axis):
        x, y = self.rep % 2, self.rep // 2
        return y * 2 + (1 - x) if axis == 0 else (1 - y) * 2 + x

    def beside(self, axis):
        return (self.turned(axis), self.shard)


def greet(spot):
    barrier = pltpu.get_barrier_semaphore()
    peers = [(spot.rep, (spot.shard + i) % OWNERS) for i in range(1, OWNERS)]
    peers += [((spot.rep + i) % REPS, spot.shard) for i in range(1, REPS)]
    for peer in peers:
        pl.semaphore_signal(barrier, inc=1, device_id=peer, device_id_type=MESH)
    return barrier, len(peers)


def send(src, dst, send_sem, recv_sem, peer):
    pltpu.make_async_remote_copy(src_ref=src, dst_ref=dst, send_sem=send_sem, recv_sem=recv_sem, device_id=peer, device_id_type=MESH).start()


def await_bytes(ref, sem):
    pltpu.make_async_copy(ref, ref, sem).wait()


def quarter(ref, rep):
    rows, cols = ref.shape[-2:]
    lead = (slice(None),) * (len(ref.shape) - 2)
    top = pl.multiple_of((rep // 2) * (rows // 2), 16)
    left = pl.multiple_of((rep % 2) * (cols // 2), 128)
    return ref.at[lead + (pl.ds(top, rows // 2), pl.ds(left, cols // 2))]


def half(ref, rep, axis):
    rows, cols = ref.shape[-2:]
    lead = (slice(None),) * (len(ref.shape) - 2)
    if axis == 0:
        left = pl.multiple_of((rep % 2) * (cols // 2), 128)
        return ref.at[lead + (slice(None), pl.ds(left, cols // 2))]
    top = pl.multiple_of((rep // 2) * (rows // 2), 16)
    return ref.at[lead + (pl.ds(top, rows // 2), slice(None))]


class Gather:
    KINDS = (LINKS - 1, LINKS - 1, LINKS - 1, LINKS - 1, LINKS)
    SEMS = 2 * sum(KINDS)
    STAGES = ("start", "across", "relay", "beside", "finish")

    def __init__(self, spot, place, axis, sems):
        self.spot, self.place, self.axis, self.sems = spot, place, axis, sems

    def sem(self, side, kind, i):
        return self.sems.at[side * (self.SEMS // 2) + sum(self.KINDS[:kind]) + i]

    def block(self, step):
        return self.place(((self.spot.z - step + LINKS) % LINKS) * 2 + self.spot.core)

    def other(self, step):
        return self.place(((self.spot.z - step + LINKS) % LINKS) * 2 + 1 - self.spot.core)

    def start(self):
        spot = self.spot
        mine = self.block(0)
        for i in range(1, LINKS):
            piece = quarter(mine, spot.rep)
            send(piece, piece, self.sem(0, 0, i - 1), self.sem(1, 0, i - 1), spot.along_z(i))
        send(mine, mine, self.sem(0, 4, 0), self.sem(1, 4, 0), spot.sibling())

    def across(self):
        spot = self.spot
        for i in range(1, LINKS):
            piece = quarter(self.block(i), spot.rep)
            await_bytes(piece, self.sem(1, 0, i - 1))
            for axis in (self.axis, 1 - self.axis):
                send(piece, piece, self.sem(0, 1 + axis, i - 1), self.sem(1, 1 + axis, i - 1), spot.beside(axis))

    def relay(self):
        spot = self.spot
        for i in range(1, LINKS):
            piece = quarter(self.block(i), spot.turned(self.axis))
            await_bytes(piece, self.sem(1, 1 + self.axis, i - 1))
            send(piece, piece, self.sem(0, 3, i - 1), self.sem(1, 3, i - 1), spot.beside(1 - self.axis))

    def beside(self):
        spot = self.spot
        for i in range(1, LINKS):
            block = self.block(i)
            piece = quarter(block, spot.rep)
            await_bytes(piece, self.sem(1, 2 - self.axis, i - 1))
            await_bytes(piece, self.sem(1, 3, i - 1))
            send(block, block, self.sem(0, 4, i), self.sem(1, 4, i), spot.sibling())

    def finish(self):
        for i in range(LINKS):
            await_bytes(self.other(i), self.sem(1, 4, i))

    def close(self):
        piece = quarter(self.block(0), self.spot.rep)
        for kind in range(4):
            for i in range(1, LINKS):
                await_bytes(piece, self.sem(0, kind, i - 1))
        for i in range(LINKS):
            await_bytes(self.block(i), self.sem(0, 4, i))


class Reduce:
    KINDS = (LINKS, 1, 1, LINKS - 1, REPS - 1)
    SEMS = 2 * sum(KINDS)
    STAGES = ("start", "first", "second", "along", "spread", "finish")

    def __init__(self, spot, place, out, core_sum, halves, quarters, links, axis, sems):
        self.spot, self.place, self.out, self.axis, self.sems = spot, place, out, axis, sems
        self.core_sum, self.halves, self.quarters, self.links = core_sum, halves, quarters, links

    def sem(self, side, kind, i):
        return self.sems.at[side * (self.SEMS // 2) + sum(self.KINDS[:kind]) + i]

    def start(self):
        spot = self.spot
        for z in range(LINKS):
            send(self.place(z * 2 + (1 - spot.core)), self.core_sum.at[z], self.sem(0, 0, z), self.sem(1, 0, z), spot.sibling())

    def first(self):
        spot = self.spot
        for z in range(LINKS):
            total = self.core_sum.at[z]
            await_bytes(total, self.sem(1, 0, z))
            total[...] = (total[...].astype(full) + self.place(z * 2 + spot.core)[...].astype(full)).astype(low)
        theirs = half(self.core_sum, spot.turned(self.axis), self.axis)
        send(theirs, self.halves, self.sem(0, 1, 0), self.sem(1, 1, 0), spot.beside(self.axis))

    def second(self):
        spot = self.spot
        await_bytes(self.halves, self.sem(1, 1, 0))
        mine = half(self.core_sum, spot.rep, self.axis)
        self.halves[...] = (self.halves[...].astype(full) + mine[...].astype(full)).astype(low)
        theirs = half(self.halves, spot.turned(1 - self.axis), 1 - self.axis)
        send(theirs, self.quarters, self.sem(0, 2, 0), self.sem(1, 2, 0), spot.beside(1 - self.axis))

    def along(self):
        spot = self.spot
        await_bytes(self.quarters, self.sem(1, 2, 0))
        mine = half(self.halves, spot.rep, 1 - self.axis)
        self.quarters[...] = (self.quarters[...].astype(full) + mine[...].astype(full)).astype(low)
        for i in range(1, LINKS):
            send(self.quarters.at[(spot.z + i) % LINKS], self.links.at[i - 1], self.sem(0, 3, i - 1), self.sem(1, 3, i - 1), spot.along_z(i))

    def spread(self):
        spot = self.spot
        total = self.quarters[spot.z].astype(full)
        for i in range(1, LINKS):
            await_bytes(self.links.at[i - 1], self.sem(1, 3, i - 1))
            total = total + self.links[i - 1].astype(full)
        mine = quarter(self.out, spot.rep)
        mine[...] = total.astype(low)
        for j in range(1, REPS):
            send(mine, mine, self.sem(0, 4, j - 1), self.sem(1, 4, j - 1), ((spot.rep + j) % REPS, spot.shard))

    def finish(self):
        for j in range(1, REPS):
            await_bytes(quarter(self.out, (self.spot.rep - j + REPS) % REPS), self.sem(1, 4, j - 1))

    def close(self):
        for z in range(LINKS):
            await_bytes(self.core_sum.at[z], self.sem(0, 0, z))
        await_bytes(self.halves, self.sem(0, 1, 0))
        await_bytes(self.quarters, self.sem(0, 2, 0))
        for i in range(1, LINKS):
            await_bytes(self.links.at[i - 1], self.sem(0, 3, i - 1))
        for j in range(1, REPS):
            await_bytes(quarter(self.out, self.spot.rep), self.sem(0, 4, j - 1))


class ReduceSmall:
    KINDS = (LINKS, LINKS - 1, REPS - 1)
    SEMS = 2 * sum(KINDS)
    STAGES = ("start", "first", "second", "along")

    def __init__(self, spot, terms, out, core_sum, links, parts, sems):
        self.spot, self.terms, self.out, self.core_sum, self.links, self.parts, self.sems = spot, terms, out, core_sum, links, parts, sems

    sem = Reduce.sem

    def start(self):
        spot = self.spot
        for z in range(LINKS):
            send(self.terms.at[z * 2 + (1 - spot.core)], self.core_sum.at[z], self.sem(0, 0, z), self.sem(1, 0, z), spot.sibling())

    def first(self):
        spot = self.spot
        for z in range(LINKS):
            await_bytes(self.core_sum.at[z], self.sem(1, 0, z))
            self.core_sum[z] = self.core_sum[z] + self.terms[z * 2 + spot.core]
        for i in range(1, LINKS):
            send(self.core_sum.at[(spot.z + i) % LINKS], self.links.at[i - 1], self.sem(0, 1, i - 1), self.sem(1, 1, i - 1), spot.along_z(i))

    def second(self):
        spot = self.spot
        total = self.core_sum[spot.z]
        for i in range(1, LINKS):
            await_bytes(self.links.at[i - 1], self.sem(1, 1, i - 1))
            total = total + self.links[i - 1]
        self.parts[spot.rep] = total
        mine = self.parts.at[spot.rep]
        for j in range(1, REPS):
            send(mine, mine, self.sem(0, 2, j - 1), self.sem(1, 2, j - 1), ((spot.rep + j) % REPS, spot.shard))

    def along(self):
        for j in range(1, REPS):
            await_bytes(self.parts.at[(self.spot.rep - j + REPS) % REPS], self.sem(1, 2, j - 1))
        total = self.parts[0]
        for j in range(1, REPS):
            total = total + self.parts[j]
        self.out[...] = total

    def close(self):
        for z in range(LINKS):
            await_bytes(self.core_sum.at[z], self.sem(0, 0, z))
        for i in range(1, LINKS):
            await_bytes(self.links.at[i - 1], self.sem(0, 1, i - 1))
        for j in range(1, REPS):
            await_bytes(self.parts.at[self.spot.rep], self.sem(0, 2, j - 1))


OWNED = C // OWNERS
SLOTS = TILES + 1
GATHERS = 2 * TILES + 1 + GROUPS
REDUCES = 2 * TILES + 1 + (GROUPS - 1) + 3
W_Q0, W_Q1, W_Q2, W_P, W_U0, W_D0, W_U1, W_D1, W_U2, W_D2 = W_ALL = range(10)
G_D0, G_U0, G_D1, G_U1, G_D2, G_U2, G_P, G_Q0, G_Q1, G_Q2, G_K2, G_V2, G_S = G_ALL = range(10, 23)
W_Q, W_U, W_D = (W_Q0, W_Q1, W_Q2), (W_U0, W_U1, W_U2), (W_D0, W_D1, W_D2)
G_D, G_U, G_Q, G_LAST = (G_D0, G_D1, G_D2), (G_U0, G_U1, G_U2), (G_Q0, G_Q1), (G_Q2, G_K2, G_V2)
START, ACROSS, RELAY, BESIDE, ARRIVED = range(5)
FIRST, SECOND, ALONG, SPREAD, SUMMED = range(1, 6)
BEFORE = {
    3: ((W_Q0, ACROSS), (W_Q1, ACROSS), (W_Q2, START), (W_P, START),),
}
FORWARD = {
    0: ((W_Q1, RELAY), (W_Q2, ACROSS), (W_P, ACROSS), (W_U0, START), (W_D0, START),),
    7: ((W_Q2, RELAY), (W_P, RELAY), (W_U0, ACROSS), (W_U1, START),),
    8: ((W_D0, ACROSS), (W_D1, START),),
    14: ((W_P, BESIDE), (W_U0, RELAY), (W_D0, RELAY), (W_U1, ACROSS), (W_U2, START),),
    16: ((W_D1, ACROSS), (W_D2, START),),
}
MIDDLE = {
    2: ((W_U0, BESIDE), (W_D0, BESIDE), (W_U1, RELAY), (W_U2, ACROSS), (W_D1, RELAY),),
}
TILE_STEP = {
    0: ((W_D2, ACROSS),),
    1: ((W_U1, BESIDE), (W_U2, RELAY), (W_D1, BESIDE),),
    2: ((W_D2, RELAY), (W_U2, BESIDE),),
    3: ((W_D2, BESIDE),),
    4: ((G_D0, FIRST), (G_U0, FIRST),),
}
AFTER_TILES = {
    0: ((G_D0, SECOND), (G_U0, SECOND), (G_D1, FIRST), (G_U1, FIRST),),
}
BACKWARD = {
    1: ((G_D2, FIRST), (G_U2, FIRST), (G_D0, ALONG),),
    2: ((G_U0, ALONG),),
    7: ((G_U1, SECOND),),
    8: ((G_D1, SECOND),),
    10: ((G_D0, SPREAD),),
    12: ((G_U0, SPREAD),),
    14: ((G_U2, SECOND), (G_Q0, FIRST), (G_D0, SUMMED),),
    15: ((G_P, FIRST),),
    16: ((G_U0, SUMMED),),
    17: ((G_D2, SECOND),),
    19: ((G_D1, ALONG), (G_U1, ALONG),),
}
LAST_STEPS = {
    0: ((G_Q1, FIRST), (G_Q2, FIRST), (G_U2, ALONG),),
    1: ((G_V2, FIRST),),
    2: ((G_D2, ALONG), (G_K2, FIRST),),
    3: ((G_P, SECOND), (G_Q0, SECOND),),
}


def chunk_shapes():
    out = []
    for _ in range(TILES):
        out += [(128, C), (OWNED, TILE)]
    return out + [(OWNED, C)] + [(3, OWNED, GCOLS)] * (GROUPS - 1) + [(OWNED, GCOLS)] * 3


def reduce_scratch():
    out = []
    for i, dims in enumerate(chunk_shapes()):
        *lead, rows, cols = dims
        near = (rows, cols // 2) if i % 2 == 0 else (rows // 2, cols)
        out.append(pltpu.VMEM((LINKS, *dims), low))
        out.append(pltpu.VMEM((LINKS, *lead, *near), low))
        out.append(pltpu.VMEM((LINKS, *lead, rows // 2, cols // 2), low))
        out.append(pltpu.VMEM((LINKS - 1, *lead, rows // 2, cols // 2), low))
    out += [pltpu.VMEM((LINKS, 40, 128), full), pltpu.VMEM((LINKS - 1, 40, 128), full), pltpu.VMEM((REPS, 40, 128), full)]
    return out


def layer_kernel(windows, x_hbm, dy_hbm, count_ref, q32, p32, u32, d32, vec_in, tab_in, line_ref, mask_ref,
                 out_hbm, grad_hbm, gq_out, gp_out, gu_out, gd_out, gs_out, qkv_hbm, pt_hbm, n1t_hbm, *scratch):
    wq, wp, up, down, small, o_ref, x1_ref, vec_ref, sums_ref, terms_ref = scratch[:10]
    gather_sems, reduce_sems, small_sems, small_reduce_sems, local = scratch[-5:]
    reduce_refs = scratch[10:-5]
    spot = Spot()
    rows_all = windows * TOK

    def live(w):
        return (w < count_ref[0]).astype(full)

    mine = spot.shard
    V = pltpu.VMEM

    jobs = {}
    places = [(W_Q[g], lambda s, g=g: wq.at[g, :, s]) for g in range(GROUPS)] + [(W_P, lambda s: wp.at[s])]
    for t in range(TILES):
        places += [(W_U[t], lambda s, t=t: up.at[t, s]), (W_D[t], lambda s, t=t: down.at[t, s])]
    for i, (name, place) in enumerate(places):
        jobs[name] = Gather(spot, place, i % 2, gather_sems.at[i])
    places = []
    for t in range(TILES):
        slot = (t + SLOTS - 1) % SLOTS
        places.append((G_D[t], lambda s, slot=slot: down.at[slot, s], gd_out.at[t]))
        places.append((G_U[t], lambda s, slot=slot: up.at[slot, s], gu_out.at[t]))
    places.append((G_P, lambda s: wp.at[s], gp_out))
    for g in range(GROUPS - 1):
        places.append((G_Q[g], lambda s, g=g: wq.at[g, :, s], gq_out.at[g]))
    for part in range(3):
        places.append((G_LAST[part], lambda s, part=part: wq.at[GROUPS - 1, part, s], gq_out.at[GROUPS - 1, part]))
    for i, (name, place, out) in enumerate(places):
        jobs[name] = Reduce(spot, place, out, *reduce_refs[4 * i : 4 * i + 4], i % 2, reduce_sems.at[i])
    jobs[G_S] = ReduceSmall(spot, terms_ref, gs_out, *reduce_refs[-3:], small_reduce_sems)

    done = {}

    def run(name, upto):
        for stage in range(done.get(name, 0), upto + 1):
            getattr(jobs[name], jobs[name].STAGES[stage])()
        done[name] = max(done.get(name, 0), upto + 1)

    def hook(table, place):
        for item in table.get(place, ()):
            run(*item)

    def when(condition, act):
        if isinstance(condition, bool):
            if condition:
                act()
        else:
            pl.when(condition)(act)

    def hook_window(table, g, w):
        for at in range(windows):
            place = g * windows + at
            if place in table:
                when(w == at, functools.partial(hook, table, place))

    def sweep(window):
        window(0, True, False)

        def inner(w, carry):
            window(w, False, False)
            return carry

        lax.fori_loop(1, windows - 1, inner, 0)
        window(windows - 1, False, True)

    barrier, peers = greet(spot)

    def cast(q_v, p_v, u_v, d_v):
        loads = [pltpu.make_async_copy(a, b, local.at[i]) for i, (a, b) in enumerate(((q32, q_v), (p32, p_v), (u32, u_v), (d32, d_v)))]
        for load in loads:
            load.start()
        small[mine] = jnp.zeros((48, 128), low)
        pad = jnp.zeros((16, 128), full)
        vec_ref[:, 0:128] = pad
        vec_ref[0:12, 0:OWNED] = vec_in[...]
        small[mine, 0:16, :] = vec_ref[:, 0:128].astype(low)
        x1_ref[0:32, 0:128] = jnp.zeros((32, 128), full)
        x1_ref[0:HEADS, 0 : tab_in.shape[1]] = tab_in[...]
        small[mine, 16:48, :] = x1_ref[0:32, 0:128].astype(low)
        loads[0].wait()
        for g in range(GROUPS):
            for part in range(3):
                wq[g, part, mine] = q_v[:, part * C + g * GCOLS : part * C + (g + 1) * GCOLS].astype(low)
        pl.semaphore_wait(barrier, peers)
        for i in range(1, OWNERS):
            send(small.at[mine], small.at[mine], small_sems.at[i], small_sems.at[OWNERS + i], (spot.rep, (mine + i) % OWNERS))
        run(W_Q0, START)
        run(W_Q1, START)
        loads[1].wait()
        wp[mine] = p_v[...].astype(low)
        loads[2].wait()
        loads[3].wait()
        for t in range(TILES):
            for s in range(OWNERS):
                src = (MLP // OWNERS) * s + 128 * t
                up[t, mine, :, s * 128 : (s + 1) * 128] = u_v[:, src : src + 128].astype(low)
            down[t, mine] = d_v[t * 128 : (t + 1) * 128, :].astype(low)

    pl.run_scoped(cast, V((OWNED, 3 * C), full), V((OWNED, C), full), V((OWNED, MLP), full), V((TILES * 128, C), full))

    def forward(x_ref, n1_ref, n1t_ref, qkv_ref, pt_ref, bias_ref, s_ref):
        load = pltpu.make_async_copy(x_hbm, x_ref, local.at[0])
        load.start()
        zero_tail(n1_ref, windows)
        zero_tail(o_ref, windows)
        for i in range(1, OWNERS):
            await_bytes(small.at[(mine - i + OWNERS) % OWNERS], small_sems.at[OWNERS + i])
        tab = unpack_small(small, vec_ref)
        hook(BEFORE, 0)
        load.wait()
        hook(BEFORE, 1)

        def first_norm(w, carry):
            xhat, _ = norm_parts(x_ref[window_rows(w), :].astype(full))
            n1_ref[window_rows(w), :] = (xhat * vec_ref[0:1, :] + vec_ref[1:2, :]).astype(low)
            return carry

        lax.fori_loop(0, windows, first_norm, 0)
        hook(BEFORE, 2)
        transpose_rows(n1_ref, n1t_ref)
        save = pltpu.make_async_copy(n1t_ref, n1t_hbm, local.at[1])
        save.start()
        hook(BEFORE, 3)

        def bias(tmp_ref):
            spread_table(tab, line_ref, tmp_ref)
            hook(BEFORE, 4)
            place_bias(tmp_ref, bias_ref)

        pl.run_scoped(bias, V((2, TOK * HEADS, 128), full))
        for g in range(GROUPS):
            cols = slice(g * GCOLS, (g + 1) * GCOLS)
            held = qkv_ref.at[g % 2]
            if g >= 2:
                pltpu.make_async_copy(held, qkv_hbm.at[g - 2], local.at[2 + g % 2]).wait()
            run(W_Q[g], ARRIVED)
            n1 = n1_ref[...]
            held[0] = ((dot(n1, flat(wq[g, 0])) + vec_ref[2:3, cols]) * (HEAD_DIM**-0.5)).astype(low)
            held[1] = dot(n1, flat(wq[g, 1])).astype(low)
            held[2] = (dot(n1, flat(wq[g, 2])) + vec_ref[3:4, cols]).astype(low)
            pltpu.make_async_copy(held, qkv_hbm.at[g], local.at[2 + g % 2]).start()

            def scores(w, held=held, g=g):
                rows = window_rows(w)
                s_ref[w % 2] = dot_nt(held[1, rows, :], diag(held[0, rows, :], mask_ref)) + bias_ref[g]

            def attend(w, held=held, g=g, cols=cols):
                rows = window_rows(w)
                o_ref[rows, cols] = undiag(held[2, rows, :].T, pt_ref[(g * windows + w) % 2], mask_ref).astype(low)

            def window(w, first, last, g=g):
                n = g * windows + w
                slot = n % 2
                hook_window(FORWARD, g, w)
                keep = pltpu.make_async_copy(pt_ref.at[slot], pt_hbm.at[n], local.at[4 + slot])
                if g or not first:
                    when(n >= 2, keep.wait)
                if not last:
                    scores(w + 1)
                s = s_ref[w % 2]
                e = jnp.exp(s - jnp.max(s, 0, keepdims=True))
                pt_ref[slot] = (e * (1.0 / jnp.sum(e, 0, keepdims=True))).astype(low)
                if not first:
                    attend(w - 1)
                keep.start()

            scores(0)
            sweep(window)
            attend(windows - 1)

        run(W_P, ARRIVED)

        def output(w, carry):
            rows = window_rows(w)
            x1_ref[rows, :] = x_ref[rows, :].astype(full) + (dot(o_ref[rows, :], flat(wp[...])) + vec_ref[4:5, :])
            return carry

        lax.fori_loop(0, windows, output, 0)
        save.wait()
        for g in (GROUPS - 2, GROUPS - 1):
            pltpu.make_async_copy(qkv_ref.at[g % 2], qkv_hbm.at[g], local.at[2 + g % 2]).wait()
        for slot in range(2):
            pltpu.make_async_copy(pt_ref.at[slot], pt_hbm.at[0], local.at[4 + slot]).wait()

    pl.run_scoped(forward, V((rows_all, C), low), V((ROWS, C), low), V((C, ROWS), low), V((2, 3, ROWS, GCOLS), low), V((2, TOK, PACK), low),
                  V((GROUPS, TOK, PACK), full), V((2, TOK, PACK), full))

    def middle(n2_ref, n2t_ref, dy_ref, dyt_ref, y_ref, dn_ref, bu_ref, bsum_ref, a_ref, dh_ref):
        load = pltpu.make_async_copy(dy_hbm, dy_ref.at[0:rows_all], local.at[0])
        load.start()
        zero_tail(n2_ref, windows)
        zero_tail(dy_ref, windows)
        hook(MIDDLE, 0)
        load.wait()

        def second_norm(w, carry):
            rows = window_rows(w)
            xhat, _ = norm_parts(x1_ref[rows, :])
            n2_ref[rows, :] = (xhat * vec_ref[5:6, :] + vec_ref[6:7, :]).astype(low)
            dy_ref[rows, :] = (dy_ref[rows, :].astype(full) * live(w)).astype(low)
            return carry

        lax.fori_loop(0, windows, second_norm, 0)
        transpose_rows(n2_ref, n2t_ref)
        hook(MIDDLE, 1)
        transpose_rows(dy_ref, dyt_ref)
        y_ref[...] = jnp.zeros_like(y_ref)
        dn_ref[...] = jnp.zeros_like(dn_ref)
        for t in range(TILES):
            for s in range(TILE // 128):
                row, left = hidden_place(t, s)
                bu_ref[t, :, s * 128 : (s + 1) * 128] = vec_ref[row : row + 1, left : left + 128]
        hook(MIDDLE, 2)
        run(W_U0, ARRIVED)
        run(W_D0, ARRIVED)
        halves = TILE // SUB
        steps = TILES * halves
        wide = SUB // 128
        n2t_ref[C:, :] = jnp.ones((16, ROWS), low)

        def weights(i):
            t, part = i // halves, i % halves
            cols = pl.ds(part * SUB, SUB) if isinstance(i, int) else pl.ds(pl.multiple_of(part * SUB, SUB), SUB)
            return t, part, cols, flat(up[t, :, :, cols]), flat(down[t, pl.ds(part * wide, wide)])

        def hidden(i):
            t, _, cols, u, d = weights(i)
            return dot(n2_ref[...], u) + bu_ref[t, :, cols], dot_nt(dy_ref[...], d)

        def activate(i, h, da, rows):
            act, slope = gelu_both(h[rows])
            a_ref[i % 2, rows] = act.astype(low)
            dh_ref[i % 2, rows] = (da[rows] * slope).astype(low)

        def products(i):
            t, part, cols, u, d = weights(i)
            slot = (t + SLOTS - 1) % SLOTS
            y_ref[...] += dot(a_ref[i % 2], d)
            yield
            dn_ref[...] += dot_nt(dh_ref[i % 2], u)
            yield
            down[slot, pl.ds(part * wide, wide)] = blocks(dot(dyt_ref[...], a_ref[i % 2]).astype(low).T, wide)
            yield
            gu = dot(n2t_ref[...], dh_ref[i % 2])
            up[slot, :, :, cols] = blocks(gu[0:C].astype(low), OWNERS)
            bsum_ref[t, :, cols] = gu[C : C + 1]
            yield

        quarters = [slice(k * ROWS // 4, (k + 1) * ROWS // 4) for k in range(4)]
        hook(TILE_STEP, 0)
        h, da = hidden(0)
        for rows in quarters:
            activate(0, h, da, rows)

        def step(i, carry):
            for k in range(1, steps):

                @pl.when(i == k)
                def _(k=k):
                    if k % halves == 0:
                        for name in (W_U[k // halves], W_D[k // halves]):
                            run(name, ARRIVED)
                    if k % halves == 1 and k > halves:
                        t = k // halves - 1
                        for name in (W_U[t], W_D[t]):
                            jobs[name].close()
                        for name in (G_D[t], G_U[t]):
                            run(name, START)
                    hook(TILE_STEP, k)

            h, da = hidden(i)
            before = products(i - 1)
            for rows in quarters:
                next(before)
                activate(i, h, da, rows)
            return carry

        lax.fori_loop(1, steps, step, 0)
        hook(TILE_STEP, steps)
        for _ in products(steps - 1):
            pass
        run(G_D[-1], START)
        run(G_U[-1], START)
        hook(AFTER_TILES, 0)
        sums_ref[...] = jnp.zeros_like(sums_ref)
        for t in range(TILES):
            for s in range(TILE // 128):
                row, left = hidden_place(t, s)
                sums_ref[row : row + 1, left : left + 128] = bsum_ref[t, :, s * 128 : (s + 1) * 128]
        transpose_rows(o_ref, dyt_ref)
        hook(AFTER_TILES, 1)

        def finish(w, carry):
            rows = window_rows(w)
            x1 = x1_ref[rows, :]
            xhat, scale = norm_parts(x1)
            dn = dn_ref[rows, :]
            dy = dy_ref[rows, :].astype(full)
            dx1 = dy + norm_back(xhat, scale, dn, vec_ref[5:6, :])
            dr = dx1.astype(low)
            sums_ref[4:5, :] += jnp.sum(dr.astype(full), 0, keepdims=True)
            sums_ref[5:6, :] += jnp.sum(dn * xhat, 0, keepdims=True)
            sums_ref[6:7, :] += jnp.sum(dn, 0, keepdims=True)
            sums_ref[7:8, :] += jnp.sum(dy, 0, keepdims=True)
            dy_ref[rows, :] = ((x1 + y_ref[rows, :] + vec_ref[7:8, :]) * live(w)).astype(low)
            x1_ref[rows, :] = dx1
            n2_ref[rows, :] = dr
            o_ref[rows, :] = dot_nt(dr, flat(wp[...])).astype(low)
            return carry

        lax.fori_loop(0, windows, finish, 0)
        save = pltpu.make_async_copy(dy_ref.at[0:rows_all], out_hbm, local.at[0])
        save.start()
        hook(AFTER_TILES, 2)
        jobs[W_P].close()
        for g in range(GROUPS):
            cols = slice(g * GCOLS, (g + 1) * GCOLS)
            wp[:, :, cols] = blocks(dot(dyt_ref[...], n2_ref[:, cols]).astype(low), OWNERS)
        run(G_P, START)
        hook(AFTER_TILES, 3)
        save.wait()

    pl.run_scoped(middle, V((ROWS, C), low), V((C + 16, ROWS), low), V((ROWS, C), low), V((C, ROWS), low), V((ROWS, C), full), V((ROWS, C), full),
                  V((TILES, 1, TILE), full), V((TILES, 1, TILE), full), V((2, ROWS, SUB), low), V((2, ROWS, SUB), low))

    def backward(x_ref, n1t_ref, qkv_ref, pt_ref, dproj_ref, dn_ref, bias_ref, dp_ref, ds_ref):
        loads = [pltpu.make_async_copy(x_hbm, x_ref, local.at[0]), pltpu.make_async_copy(n1t_hbm, n1t_ref, local.at[1])]
        fetch = [pltpu.make_async_copy(qkv_hbm.at[g], qkv_ref.at[g % 2], local.at[2 + g % 2]) for g in range(GROUPS)]
        fetch[0].start()
        probs = [pltpu.make_async_copy(pt_hbm.at[n], pt_ref.at[n], local.at[4 + n]) for n in range(2)]
        for load in probs:
            load.start()
        fetch[1].start()
        for load in loads:
            load.start()
        bias_ref[...] = jnp.zeros_like(bias_ref)
        dn_ref[...] = jnp.zeros_like(dn_ref)
        for part in range(3):
            dproj_ref[part, rows_all:, :] = jnp.zeros((ROWS - rows_all, GCOLS), low)
        for g in range(GROUPS):
            cols = slice(g * GCOLS, (g + 1) * GCOLS)
            held = qkv_ref.at[g % 2]
            fetch[g].wait()

            def terms(w, g=g, cols=cols, held=held):
                rows = window_rows(w)
                do = diag(o_ref[rows, cols], mask_ref)
                dp_ref[w % 2] = dot_nt(held[2, rows, :], do)
                dv = dot(pt_ref[(g * windows + w) % 3], do).astype(low)
                dproj_ref[2, rows, :] = dv
                sums_ref[3:4, cols] += jnp.sum(dv.astype(full), 0, keepdims=True)

            def products(w, cols=cols, held=held):
                rows = window_rows(w)
                ds = ds_ref[w % 2]
                dproj_ref[1, rows, :] = dot(ds, diag(held[0, rows, :], mask_ref)).astype(low)
                dq = (undiag(held[1, rows, :].T, ds, mask_ref) * (HEAD_DIM**-0.5)).astype(low)
                dproj_ref[0, rows, :] = dq
                sums_ref[2:3, cols] += jnp.sum(dq.astype(full), 0, keepdims=True)

            def window(w, first, last, g=g):
                n = g * windows + w
                hook_window(BACKWARD, g, w)

                def fetch_next():
                    pltpu.make_async_copy(pt_hbm.at[n + 2], pt_ref.at[(n + 2) % 3], local.at[4 + (n + 2) % 3]).start()

                when(n + 2 < GROUPS * windows, fetch_next)
                if not last:
                    pltpu.make_async_copy(pt_hbm.at[n + 1], pt_ref.at[(n + 1) % 3], local.at[4 + (n + 1) % 3]).wait()
                    terms(w + 1)
                pf = pt_ref[n % 3].astype(full)
                dp = dp_ref[w % 2]
                ds = (pf * (dp - jnp.sum(pf * dp, 0, keepdims=True))).astype(low)
                ds_ref[w % 2] = ds
                bias_ref[g] += ds.astype(full)
                if not first:
                    products(w - 1)

            pltpu.make_async_copy(pt_hbm.at[g * windows], pt_ref.at[g * windows % 3], local.at[4 + g * windows % 3]).wait()
            terms(0)
            sweep(window)
            products(windows - 1)
            if g + 2 < GROUPS:
                fetch[g + 2].start()
            if g == 0:
                for load in loads:
                    load.wait()
            jobs[W_Q[g]].close()
            for part in range(3):
                d = dproj_ref[part]
                dn_ref[...] += dot_nt(d, flat(wq[g, part]))
                wq[g, part] = blocks(dot(n1t_ref[...], d).astype(low), OWNERS)
                if g == GROUPS - 1:
                    run(G_LAST[part], START)
            if g < GROUPS - 1:
                run(G_Q[g], START)
        hook(LAST_STEPS, 0)

        def last_norm(grad_ref):
            def finish(w, carry):
                rows = window_rows(w)
                slot = w % 2
                xhat, scale = norm_parts(x_ref[rows, :].astype(full))
                dn = dn_ref[rows, :]
                save = pltpu.make_async_copy(grad_ref.at[slot], grad_hbm.at[rows], local.at[4 + slot])

                @pl.when(w >= 2)
                def _():
                    save.wait()

                grad_ref[slot] = x1_ref[rows, :] + norm_back(xhat, scale, dn, vec_ref[0:1, :])
                save.start()
                sums_ref[0:1, :] += jnp.sum(dn * xhat, 0, keepdims=True)
                sums_ref[1:2, :] += jnp.sum(dn, 0, keepdims=True)
                return carry

            lax.fori_loop(0, windows, finish, 0)
            hook(LAST_STEPS, 1)
            for slot in range(2):
                pltpu.make_async_copy(grad_ref.at[slot], grad_hbm.at[pl.ds(0, TOK)], local.at[4 + slot]).wait()

        pl.run_scoped(last_norm, V((2, TOK, C), full))
        hook(LAST_STEPS, 2)

        def table(tmp_ref):
            pack_small(sums_ref[...], table_grad(line_ref, tmp_ref, bias_ref), terms_ref)

        pl.run_scoped(table, V((2, TOK * HEADS, 128), full))
        run(G_S, START)
        hook(LAST_STEPS, 3)
        for stage in range(len(Reduce.STAGES)):
            for name in G_ALL:
                if stage < len(jobs[name].STAGES):
                    run(name, stage)

    pl.run_scoped(backward, V((rows_all, C), low), V((C, ROWS), low), V((2, 3, ROWS, GCOLS), low), V((3, TOK, PACK), low), V((3, ROWS, GCOLS), low),
                  V((ROWS, C), full), V((GROUPS, TOK, PACK), full), V((2, TOK, PACK), full), V((2, TOK, PACK), low))
    jobs[W_U[-1]].close()
    jobs[W_D[-1]].close()
    for i in range(1, OWNERS):
        await_bytes(small.at[mine], small_sems.at[i])
    for name in G_ALL:
        jobs[name].close()


def shape(dims, kind):
    return jax.ShapeDtypeStruct(dims, kind)


def adamw(weight, moment, second, gradient, step_rate):
    moment_new = beta_one * moment + (1.0 - beta_one) * gradient
    second_new = beta_two * second + (1.0 - beta_two) * gradient * gradient
    update = moment_new * (1.0 / (1.0 - beta_one**STEP)) / (jnp.sqrt(second_new * (1.0 / (1.0 - beta_two**STEP))) + adam_eps)
    weight_new = weight * (1.0 - step_rate * weight_decay) - step_rate * update
    return (weight_new, moment_new, second_new)


def update_kernel(*refs):
    gq, gp, gu, gd, gs = refs[:5]
    ins = [refs[5 + 3 * i : 8 + 3 * i] for i in range(6)]
    outs = [refs[25 + 4 * i : 29 + 4 * i] for i in range(4)] + [refs[41:44], refs[44:47]]
    for i in range(2):
        refs[47 + i][...] = refs[23 + i][...]

    def piece(which, place, gradient):
        new = adamw(*(ref[place] for ref in ins[which]), gradient, step_rates[which])
        for ref, value in zip(outs[which], new):
            ref[place] = value
        if which < 4:
            outs[which][3][place] = new[0].astype(low)

    for part in range(3):
        for g in range(GROUPS):
            left = part * C + g * GCOLS
            piece(0, (slice(None), slice(left, left + GCOLS)), gq[g, part].astype(full))
    piece(1, (slice(None), slice(None)), gp[...].astype(full))
    for t in range(TILES):
        for s in range(OWNERS):
            left = (MLP // OWNERS) * s + 128 * t
            piece(2, (slice(None), slice(left, left + 128)), gu[t, :, s * 128 : (s + 1) * 128].astype(full))
    piece(3, (slice(None), slice(None)), gd[0].astype(full))

    @pl.when(pl.program_id(0) == 0)
    def _():
        every = (slice(None), slice(None))
        piece(4, every, gs[0:12, 0:OWNED])
        piece(5, every, gs[16:40, 0 : ins[5][0].shape[1]])


def update(gq, gp, gu, gd, gs, states, results):
    steps = OWNED // 16

    def rows_of(array):
        tall = array.shape[0] // steps
        return pl.BlockSpec((tall, array.shape[1]), lambda i: (i, 0))

    def whole(array):
        return pl.BlockSpec(array.shape, lambda i: (0, 0))

    per_tile = 128 * TILES // steps
    specs = [
        pl.BlockSpec((GROUPS, 3, 16, GCOLS), lambda i: (0, 0, i, 0)),
        pl.BlockSpec((16, C), lambda i: (i, 0)),
        pl.BlockSpec((TILES, 16, TILE), lambda i: (0, i, 0)),
        pl.BlockSpec((1, per_tile, C), lambda i: (i // (128 // per_tile), i % (128 // per_tile), 0)),
        whole(gs),
    ]
    out_shapes, out_specs = [], []
    for i, group in enumerate(states):
        for array in group:
            specs.append(rows_of(array) if i < 4 else whole(array))
            out_shapes.append(shape(array.shape, full))
            out_specs.append(specs[-1])
        if i < 4:
            out_shapes.append(shape(group[0].shape, low))
            out_specs.append(rows_of(group[0]))
    results = [array.reshape(steps, -1, C) for array in results]
    for array in results:
        specs.append(pl.BlockSpec((1, *array.shape[1:]), lambda i: (i, 0, 0)))
        out_shapes.append(shape(array.shape, array.dtype))
        out_specs.append(specs[-1])
    return pl.pallas_call(
        update_kernel,
        grid=(steps,),
        in_specs=specs,
        out_specs=out_specs,
        out_shape=out_shapes,
        compiler_params=pltpu.CompilerParams(vmem_limit_bytes=63 * MIB),
        name="update",
    )(gq, gp, gu, gd, gs, *[array for group in states for array in group], *results)


def shards(
    tokens, out_grad, window_count,
    qkv_weight, qkv_first, qkv_second,
    output_weight, output_first, output_second,
    up_weight, up_first, up_second,
    down_weight, down_first, down_second,
    vectors, vector_first, vector_second,
    bias_table, table_first, table_second,
):
    windows = tokens.shape[0]
    rows = windows * TOK
    V = pltpu.VMEM
    D = pltpu.SemaphoreType.DMA
    hbm = pl.BlockSpec(memory_space=pl.ANY)
    vmem = pl.BlockSpec(memory_space=pltpu.VMEM)
    result = pl.pallas_call(
        functools.partial(layer_kernel, windows),
        out_shape=[
            shape((rows, C), low), shape((rows, C), full),
            shape((GROUPS, 3, OWNED, GCOLS), low), shape((OWNED, C), low), shape((TILES, OWNED, TILE), low), shape((TILES, 128, C), low),
            shape((40, 128), full),
            shape((GROUPS, 3, ROWS, GCOLS), low), shape((GROUPS * windows, TOK, PACK), low), shape((C, ROWS), low)],
        in_specs=[hbm, hbm, pl.BlockSpec(memory_space=pltpu.SMEM)] + [hbm] * 4 + [vmem] * 4,
        out_specs=[hbm, hbm] + [vmem] * 5 + [hbm] * 3,
        scratch_shapes=[
            V((GROUPS, 3, OWNERS, OWNED, GCOLS), low), V((OWNERS, OWNED, C), low), V((SLOTS, OWNERS, OWNED, TILE), low),
            V((SLOTS, OWNERS, 128, C), low), V((OWNERS, 48, 128), low), V((ROWS, C), low), V((rows, C), full), V((16, C), full), V((16, C), full),
            V((OWNERS, 40, 128), full)]
        + reduce_scratch()
        + [D((GATHERS, Gather.SEMS)), D((REDUCES, Reduce.SEMS)), D((2 * OWNERS,)), D((ReduceSmall.SEMS,)), D((7,))],
        compiler_params=pltpu.CompilerParams(vmem_limit_bytes=63 * MIB, collective_id=0, has_side_effects=True),
        name="layer",
    )(tokens.reshape(rows, C), out_grad.reshape(rows, C), window_count, qkv_weight, output_weight, up_weight, down_weight, vectors, bias_table.T,
      jnp.asarray(line_matrix(), low), jnp.asarray(head_masks(), low))
    out, grad, gq, gp, gu, gd, gs = result[:7]
    new = update(gq, gp, gu, gd, gs, (
        (qkv_weight, qkv_first, qkv_second), (output_weight, output_first, output_second), (up_weight, up_first, up_second),
        (down_weight, down_first, down_second), (vectors, vector_first, vector_second), (bias_table.T, table_first.T, table_second.T)), (out, grad))
    *new, out, grad = new
    return (out.reshape(tokens.shape), grad.reshape(tokens.shape), *new[:-3], *(array.T for array in new[-3:]))


def vmem_call(body, outs, scratch, args, name, limit=60, **params):
    spec = pl.BlockSpec(memory_space=pltpu.VMEM)
    return pl.pallas_call(
        body,
        out_shape=outs,
        in_specs=[pl.BlockSpec(memory_space=pltpu.SMEM) if a.dtype == full and a.ndim == 1 else spec for a in args],
        out_specs=[spec] * len(outs),
        scratch_shapes=scratch,
        compiler_params=pltpu.CompilerParams(vmem_limit_bytes=limit * MIB, **params),
        name=name,
    )(*args)


def local_step(tokens, out_grad, window_count, small, wq, wp, up, down):
    windows = tokens.shape[0]
    rows = windows * TOK
    owned = C // OWNERS
    V = pltpu.VMEM
    x = tokens.reshape(rows, C)
    dy = out_grad.reshape(rows, C)
    live = (jnp.arange(windows) < window_count[0]).astype(full)
    line = jnp.asarray(line_matrix(), low)
    masks = jnp.asarray(head_masks(), low)
    qkv, pt, o, x1, n1t, vec = vmem_call(
        functools.partial(attention_forward, windows),
        [shape((9, ROWS, GCOLS), low), shape((GROUPS, windows, TOK, PACK), low), shape((ROWS, C), low), shape((rows, C), full), shape((C, ROWS), low),
         shape((16, C), full)],
        [V((ROWS, C), low), V((GROUPS, TOK, PACK), full), V((2, TOK * HEADS, 128), full)],
        (x, small, line, masks, wq, wp), "attention_forward")
    out, dx1, do, gup, gdown, gout, sums = vmem_call(
        functools.partial(feed_forward, windows),
        [shape((rows, C), low), shape((ROWS, C), full), shape((rows, C), low), shape((TILES, OWNERS, owned, TILE), low),
         shape((TILES, OWNERS, C, 128), low), shape((OWNERS, owned, C), low), shape((16, C), full)],
        [V((ROWS, C), low), V((C, ROWS), low), V((ROWS, C), low), V((C, ROWS), low), V((ROWS, C), full), V((ROWS, C), full),
         V((TILES, 1, TILE), full), V((TILES, 1, TILE), full)],
        (x1, dy, live, vec, up, down, wp, o), "feed_forward")
    gq, gsmall, grad = vmem_call(
        functools.partial(attention_backward, windows),
        [shape((GROUPS, 3, OWNERS, owned, GCOLS), low), shape((OWNERS, 40, 128), full), shape((rows, C), full)],
        [V((16, C), full), V((GROUPS, TOK, PACK), full), V((2, TOK * HEADS, 128), full), V((3, ROWS, GCOLS), low), V((ROWS, C), full)],
        (x, vec, line, masks, wq, qkv, pt, do, dx1, n1t, sums), "attention_backward")
    return out.reshape(tokens.shape), grad.reshape(tokens.shape), gq, gout, gup, gdown, gsmall


def shards_general(
    tokens, out_grad, window_count,
    qkv_weight, qkv_first, qkv_second,
    output_weight, output_first, output_second,
    up_weight, up_first, up_second,
    down_weight, down_first, down_second,
    vectors, vector_first, vector_second,
    bias_table, table_first, table_second,
):
    gather = functools.partial(lax.all_gather, axis_name="shard", tiled=True)
    scatter = functools.partial(lax.psum_scatter, axis_name="shard", tiled=True)
    owned = C // OWNERS
    wq = gather(qkv_weight.astype(low), axis=0).reshape(OWNERS, owned, 3, GROUPS, GCOLS).transpose(3, 2, 0, 1, 4)
    wp = gather(output_weight.astype(low), axis=0).reshape(OWNERS, owned, C)
    up = gather(up_weight.astype(low), axis=0).reshape(OWNERS, owned, OWNERS, TILES, 128).transpose(3, 0, 1, 2, 4)
    up = up.reshape(TILES, OWNERS, owned, TILE)
    down = gather(down_weight.astype(low), axis=0).reshape(OWNERS, TILES, 128, C).transpose(1, 0, 2, 3)
    vec = gather(vectors.astype(low), axis=1)
    tab = gather(bias_table.astype(low), axis=0)
    table_rows = tab.shape[0]
    count = TAB_ROWS // OWNERS
    vec = vec.reshape(12, OWNERS, owned).transpose(1, 0, 2)
    tab = tab[:TAB_ROWS].reshape(OWNERS, count, HEADS).transpose(0, 2, 1)
    small = jnp.concatenate([jnp.pad(vec, ((0, 0), (0, 4), (0, 128 - owned))), jnp.pad(tab, ((0, 0), (0, 8), (0, 128 - count)))], 1)
    out, grad, gq, gp, gu, gd, gs = local_step(tokens, out_grad, window_count, small, wq, wp, up, down)
    gq = gq.astype(full).transpose(2, 3, 1, 0, 4).reshape(C, 3 * C)
    gu = gu.astype(full).reshape(TILES, C, OWNERS, 128).transpose(1, 2, 0, 3).reshape(C, MLP)
    gd = gd.astype(full).transpose(1, 0, 3, 2).reshape(MLP, C)
    gv = gs[:, :12, :owned].transpose(1, 0, 2).reshape(12, C)
    gb = gs[:, 16:40, :count].transpose(0, 2, 1).reshape(TAB_ROWS, HEADS)
    gb = jnp.pad(gb, ((0, table_rows - TAB_ROWS), (0, 0)))
    totals = lax.psum(
        (scatter(gq, scatter_dimension=0), scatter(gp.astype(full).reshape(C, C), scatter_dimension=0), scatter(gu, scatter_dimension=0),
         scatter(gd, scatter_dimension=0), scatter(gv, scatter_dimension=1), scatter(gb, scatter_dimension=0)), "rep")
    states = (
        (qkv_weight, qkv_first, qkv_second), (output_weight, output_first, output_second), (up_weight, up_first, up_second),
        (down_weight, down_first, down_second), (vectors, vector_first, vector_second), (bias_table, table_first, table_second))
    results = [out, grad]
    for i, (state, total, rate) in enumerate(zip(states, totals, step_rates)):
        new = adamw(*state, total, rate)
        results += [*new, new[0].astype(low)] if i < 4 else [*new]
    return tuple(results)


def solution(mesh):
    wins = P(("rep", "shard"), None, None)
    rows = P("shard", None)
    cols = P(None, "shard")
    fits = mesh.shape["rep"] == REPS and mesh.shape["shard"] == OWNERS
    return jax.shard_map(
        shards if fits else shards_general,
        mesh=mesh,
        in_specs=(wins, wins, P(("rep", "shard"))) + (rows,) * 12 + (cols,) * 3 + (rows,) * 3,
        out_specs=(wins, wins) + (rows,) * 16 + (cols,) * 3 + (rows,) * 3,
        check_vma=False,
    )
```

```python
import functools
import math

import jax
import jax.numpy as jnp
import numpy as np
from jax import lax
from jax.experimental import pallas as pl
from jax.experimental.pallas import tpu as pltpu
from jax.sharding import PartitionSpec as P

C = 768
HEADS = 24
MLP = 3072
WIN = 12
STEP = 5
HEAD_DIM = 32
SPAN = 2 * WIN - 1
TOK = WIN * WIN
TAB_ROWS = 536
ROWS = 1024
GROUPS = 3
GCOLS = 256
GHEADS = 8
PACK = GHEADS * TOK
TAB_LANES = 640
TILES = 3
TILE = MLP // TILES
SUB = 512
LINE = 384
MIB = 1 << 20

beta_one = 0.5
beta_two = 0.6
weight_decay = 0.05
adam_eps = 1e-08
norm_eps = 1e-05
step_rates = (0.04, 0.15, 0.04, 0.02, 0.2, 1.0)
low = jnp.bfloat16
full = jnp.float32
NT = (((1,), (1,)), ((), ()))


def dot(a, b):
    return jnp.dot(a, b, preferred_element_type=full)


def dot_nt(a, b):
    return lax.dot_general(a, b, NT, preferred_element_type=full)


def line_matrix():
    out = np.zeros((TAB_LANES, LINE), np.float32)
    col = np.arange(SPAN * WIN)
    out[(col // WIN) * SPAN + col % WIN + WIN - 1, col] = 1.0
    return out


def head_masks():
    lane = np.arange(GCOLS) // HEAD_DIM
    one = (lane[None, :] == np.arange(GHEADS)[:, None]).astype(np.float32)
    return np.broadcast_to(one[:, None, :], (GHEADS, 16, GCOLS))


def norm_parts(z):
    mean = jnp.sum(z, -1, keepdims=True) * (1.0 / C)
    center = z - mean
    spread = jnp.sum(center * center, -1, keepdims=True) * (1.0 / C)
    scale = lax.rsqrt(spread + norm_eps)
    return center * scale, scale


def norm_back(xhat, scale, dn, gain):
    g = dn * gain
    m1 = jnp.sum(g, -1, keepdims=True) * (1.0 / C)
    m2 = jnp.sum(g * xhat, -1, keepdims=True) * (1.0 / C)
    return scale * (g - m1 - xhat * m2)


def diag(x, mask_ref):
    head = x[0:128].reshape(8, 16, GCOLS)
    tail = x[128:144]
    parts = []
    for h in range(GHEADS):
        parts.append((head * mask_ref[h][None]).reshape(128, GCOLS))
    for h in range(GHEADS):
        parts.append(tail * mask_ref[h])
    return jnp.concatenate(parts, 0)


def undiag(xt, m, mask_ref):
    main = []
    for h in range(0, GHEADS, 2):
        r = dot(xt[h * HEAD_DIM : (h + 2) * HEAD_DIM], m[:, h * 128 : (h + 2) * 128])
        main.append(r[0:HEAD_DIM, 0:128])
        main.append(r[HEAD_DIM : 2 * HEAD_DIM, 128:256])
    main = jnp.concatenate(main, 0)
    rest = dot(xt, m[:, GHEADS * 128 :])
    rest_t = rest.T.reshape(GHEADS, 16, GCOLS)
    keep = mask_ref[...].astype(full)
    return jnp.concatenate([main.T, jnp.sum(rest_t * keep, 0)], 0)


def flat(x):
    return x.reshape(x.shape[0] * x.shape[1], x.shape[2])


def blocks(x, owners):
    return x.reshape(owners, x.shape[0] // owners, x.shape[1])


def hidden_place(t, s):
    at = (MLP // GHEADS) * s + 128 * t
    return 8 + at // C, at % C


def unpack_small(small_ref, vec_ref):
    owners = small_ref.shape[0]
    width = C // owners
    count = TAB_ROWS // owners
    vec = jnp.zeros((16, C), full)
    tab = jnp.zeros((HEADS, TAB_LANES), full)
    lane = lax.broadcasted_iota(jnp.int32, (16, 128), 1)
    lane_tab = lax.broadcasted_iota(jnp.int32, (HEADS, 128), 1)
    for s in range(owners):
        piece = small_ref[s].astype(full)
        part = jnp.where(lane < width, piece[0:16], 0.0)
        part = jnp.concatenate([part, jnp.zeros((16, C - 128), full)], 1)
        vec = vec + (pltpu.roll(part, width * s, 1) if s else part)
        part = jnp.where(lane_tab < count, piece[16 : 16 + HEADS], 0.0)
        part = jnp.concatenate([part, jnp.zeros((HEADS, TAB_LANES - 128), full)], 1)
        tab = tab + (pltpu.roll(part, count * s, 1) if s else part)
    vec_ref[...] = vec
    return tab


def pack_small(vec, tab, out_ref):
    owners = out_ref.shape[0]
    width = C // owners
    count = TAB_ROWS // owners
    for s in range(owners):
        out_ref[s, 0:16, :] = (pltpu.roll(vec, C - width * s, 1) if s else vec)[:, 0:128]
        out_ref[s, 16:40, :] = (pltpu.roll(tab, TAB_LANES - count * s, 1) if s else tab)[:, 0:128]


def spread_table(tab, line_ref, tmp_ref):
    def column(cj, carry):
        shifted = pltpu.roll(tab, cj, 1)
        line = dot(shifted.astype(low), line_ref[...])
        for rj in range(WIN):
            cut = (WIN - 1 - rj) * WIN
            part = pltpu.roll(line, LINE - cut, 1) if cut else line
            row = pl.multiple_of((rj * WIN + cj) * HEADS, 8)
            tmp_ref[0, pl.ds(row, HEADS), :] = part[:, 0:128]
            tmp_ref[1, pl.ds(row, HEADS), :] = part[:, 128:256]
        return carry

    lax.fori_loop(0, WIN, column, 0)


def place_bias(tmp_ref, bias_ref):
    lane = lax.broadcasted_iota(jnp.int32, (TOK, 128), 1)
    for g in range(GROUPS):
        rest = jnp.zeros((TOK, 128), full)
        for h in range(GHEADS):
            at = pl.ds(g * GHEADS + h, TOK, stride=HEADS)
            bias_ref[g, :, h * 128 : (h + 1) * 128] = tmp_ref[0, at, :]
            piece = tmp_ref[1, at, :]
            piece = pltpu.roll(piece, 16 * h, 1) if h else piece
            rest = jnp.where((lane >= 16 * h) & (lane < 16 * h + 16), piece, rest)
        bias_ref[g, :, GHEADS * 128 :] = rest


def table_grad(line_ref, tmp_ref, bias_ref):
    lane = lax.broadcasted_iota(jnp.int32, (TOK, 128), 1)
    for g in range(GROUPS):
        rest = bias_ref[g, :, GHEADS * 128 :]
        for h in range(GHEADS):
            at = pl.ds(g * GHEADS + h, TOK, stride=HEADS)
            tmp_ref[0, at, :] = bias_ref[g, :, h * 128 : (h + 1) * 128]
            piece = pltpu.roll(rest, 128 - 16 * h, 1) if h else rest
            tmp_ref[1, at, :] = jnp.where(lane < 16, piece, 0.0)

    def column(cj, total):
        line = jnp.zeros((HEADS, LINE), full)
        for rj in range(WIN):
            cut = (WIN - 1 - rj) * WIN
            row = pl.multiple_of((rj * WIN + cj) * HEADS, 8)
            part = jnp.concatenate([tmp_ref[0, pl.ds(row, HEADS), :], tmp_ref[1, pl.ds(row, HEADS), :], jnp.zeros((HEADS, 128), full)], 1)
            line = line + (pltpu.roll(part, cut, 1) if cut else part)
        high = line.astype(low)
        rest = (line - high.astype(full)).astype(low)
        spread = dot_nt(high, line_ref[...]) + dot_nt(rest, line_ref[...])
        return total + pltpu.roll(spread, TAB_LANES - cj, 1)

    return lax.fori_loop(0, WIN, column, jnp.zeros((HEADS, TAB_LANES), full))


def transpose_rows(src_ref, dst_ref):
    def block(i, carry):
        at = pl.multiple_of(i * 128, 128)
        dst_ref[0 : src_ref.shape[1], pl.ds(at, 128)] = src_ref[pl.ds(at, 128), :].T
        return carry

    lax.fori_loop(0, ROWS // 128, block, 0)


def window_rows(w):
    return slice(w * TOK, (w + 1) * TOK) if isinstance(w, int) else pl.ds(pl.multiple_of(w * TOK, 16), TOK)


def zero_tail(ref, windows):
    at = windows * TOK
    ref[at:ROWS, :] = jnp.zeros((ROWS - at, ref.shape[1]), ref.dtype)


CHUNK = 16


def pair_diag(x, pair, mask_ref):
    lanes = slice((pair // 2) * 128, (pair // 2 + 1) * 128)
    part = x[0:128, lanes].reshape(8, 16, 128)
    return jnp.concatenate([(part * mask_ref[h, :, lanes][None]).reshape(128, 128) for h in (2 * pair, 2 * pair + 1)], 0)


def rest_diag(x, mask_ref):
    return jnp.concatenate([x[128:144] * mask_ref[h] for h in range(GHEADS)], 0)


def pair_values(xt, pair, m):
    r = dot(xt[pair * 64 : (pair + 1) * 64], m)
    return [r[0:HEAD_DIM, 0:128], r[HEAD_DIM : 2 * HEAD_DIM, 128:256]]


def join_values(main, rest, mask_ref):
    rest_t = rest.T.reshape(GHEADS, 16, GCOLS)
    keep = mask_ref[...].astype(full)
    return jnp.concatenate([jnp.concatenate(main, 0).T, jnp.sum(rest_t * keep, 0)], 0)


def half_of(x, pair):
    return x[:, (pair // 2) * 128 : (pair // 2 + 1) * 128]


def by_rows(windows, body):
    def window(w, carry):
        for k in range(TOK // CHUNK):
            body(w, pl.ds(pl.multiple_of(w * TOK + k * CHUNK, CHUNK), CHUNK))
        return carry

    lax.fori_loop(0, windows, window, 0)


def fold(x):
    return x[0:8] + x[8:16]


def attention_forward(windows, x_ref, small_ref, line_ref, mask_ref, wq_ref, wp_ref,
                      qkv_ref, pt_ref, o_ref, x1_ref, n1t_ref, vec_ref, n1_ref, bias_ref, tmp_ref):
    tab = unpack_small(small_ref, vec_ref)
    spread_table(tab, line_ref, tmp_ref)
    place_bias(tmp_ref, bias_ref)
    zero_tail(n1_ref, windows)
    zero_tail(o_ref, windows)

    def first_norm(w, carry):
        xhat, _ = norm_parts(x_ref[window_rows(w), :].astype(full))
        n1_ref[window_rows(w), :] = (xhat * vec_ref[0:1, :] + vec_ref[1:2, :]).astype(low)
        return carry

    lax.fori_loop(0, windows, first_norm, 0)
    transpose_rows(n1_ref, n1t_ref)

    def group(g, carry):
        cols = pl.ds(pl.multiple_of(g * GCOLS, GCOLS), GCOLS)
        n1 = n1_ref[...]
        qkv_ref[g] = ((dot(n1, flat(wq_ref[g, 0])) + vec_ref[2:3, cols]) * (HEAD_DIM**-0.5)).astype(low)
        qkv_ref[GROUPS + g] = dot(n1, flat(wq_ref[g, 1])).astype(low)
        qkv_ref[2 * GROUPS + g] = (dot(n1, flat(wq_ref[g, 2])) + vec_ref[3:4, cols]).astype(low)

        def window(w, inner):
            rows = window_rows(w)
            q = qkv_ref[g, rows, :]
            k = qkv_ref[GROUPS + g, rows, :]
            v = qkv_ref[2 * GROUPS + g, rows, :]
            s = dot_nt(k, diag(q, mask_ref)) + bias_ref[g]
            e = jnp.exp(s - jnp.max(s, 0, keepdims=True))
            p = (e * (1.0 / jnp.sum(e, 0, keepdims=True))).astype(low)
            pt_ref[g, w] = p
            o_ref[rows, cols] = undiag(v.T, p, mask_ref).astype(low)
            return inner

        lax.fori_loop(0, windows, window, 0)
        return carry

    lax.fori_loop(0, GROUPS, group, 0)

    def output(w, carry):
        rows = window_rows(w)
        branch = dot(o_ref[rows, :], flat(wp_ref[...])) + vec_ref[4:5, :]
        x1_ref[rows, :] = x_ref[rows, :].astype(full) + branch
        return carry

    lax.fori_loop(0, windows, output, 0)


def gelu_both(h):
    c = math.sqrt(2.0 / math.pi)
    square = h * h
    t = jnp.tanh(h * (c + (c * 0.044715) * square))
    half = 0.5 + 0.5 * t
    act = h * half
    return act, half + act * (1.0 - half) * (2.0 * c + (6.0 * c * 0.044715) * square)


def feed_forward(windows, x1_ref, dy_ref, live_ref, vec_ref, up_ref, down_ref, wp_ref, o_ref,
                 out_ref, dx1_ref, do_ref, gup_ref, gdown_ref, gout_ref, sums_ref,
                 n2_ref, n2t_ref, dy2_ref, dyt_ref, y_ref, dn_ref, bu_ref, bsum_ref):
    zero_tail(n2_ref, windows)
    zero_tail(dy2_ref, windows)

    def second_norm(w, carry):
        rows = window_rows(w)
        xhat, _ = norm_parts(x1_ref[rows, :])
        n2_ref[rows, :] = (xhat * vec_ref[5:6, :] + vec_ref[6:7, :]).astype(low)
        dy2_ref[rows, :] = (dy_ref[rows, :].astype(full) * live_ref[w]).astype(low)
        return carry

    lax.fori_loop(0, windows, second_norm, 0)
    transpose_rows(n2_ref, n2t_ref)
    transpose_rows(dy2_ref, dyt_ref)
    y_ref[...] = jnp.zeros_like(y_ref)
    dn_ref[...] = jnp.zeros_like(dn_ref)
    owners = gup_ref.shape[1]
    for t in range(TILES):
        for s in range(TILE // 128):
            row, at = hidden_place(t, s)
            bu_ref[t, :, s * 128 : (s + 1) * 128] = vec_ref[row : row + 1, at : at + 128]

    def step(t, carry):
        for part in range(TILE // SUB):
            cols = slice(part * SUB, (part + 1) * SUB)
            up = flat(up_ref[t, :, :, cols])
            down = flat(down_ref[t, part * SUB // 128 : (part + 1) * SUB // 128])
            h = dot(n2_ref[...], up) + bu_ref[t, :, cols]
            da = dot_nt(dy2_ref[...], down)
            act, slope = gelu_both(h)
            a = act.astype(low)
            dh = (da * slope).astype(low)
            bsum_ref[t, :, cols] = jnp.sum(dh.astype(full), 0, keepdims=True)
            y_ref[...] += dot(a, down)
            dn_ref[...] += dot_nt(dh, up)
            gd = dot(dyt_ref[...], a).astype(low)
            for b in range(SUB // 128):
                gdown_ref[t, part * SUB // 128 + b] = gd[:, b * 128 : (b + 1) * 128]
            gup_ref[t, :, :, cols] = blocks(dot(n2t_ref[...], dh).astype(low), owners)
        return carry

    lax.fori_loop(0, TILES, step, 0)
    sums_ref[...] = jnp.zeros_like(sums_ref)
    for t in range(TILES):
        for s in range(TILE // 128):
            row, at = hidden_place(t, s)
            sums_ref[row : row + 1, at : at + 128] = bsum_ref[t, :, s * 128 : (s + 1) * 128]
    zero_tail(dx1_ref, windows)

    def finish(w, carry):
        rows = window_rows(w)
        x1 = x1_ref[rows, :]
        out_ref[rows, :] = ((x1 + y_ref[rows, :] + vec_ref[7:8, :]) * live_ref[w]).astype(low)
        xhat, scale = norm_parts(x1)
        dn = dn_ref[rows, :]
        dy = dy2_ref[rows, :].astype(full)
        dx1 = dy + norm_back(xhat, scale, dn, vec_ref[5:6, :])
        dx1_ref[rows, :] = dx1
        dr = dx1.astype(low)
        n2_ref[rows, :] = dr
        do_ref[rows, :] = dot_nt(dr, flat(wp_ref[...])).astype(low)
        sums_ref[4:5, :] += jnp.sum(dr.astype(full), 0, keepdims=True)
        sums_ref[5:6, :] += jnp.sum(dn * xhat, 0, keepdims=True)
        sums_ref[6:7, :] += jnp.sum(dn, 0, keepdims=True)
        sums_ref[7:8, :] += jnp.sum(dy, 0, keepdims=True)
        return carry

    lax.fori_loop(0, windows, finish, 0)
    transpose_rows(o_ref, dyt_ref)
    for g in range(GROUPS):
        at = pl.ds(g * GCOLS, GCOLS)
        gout_ref[:, :, at] = blocks(dot(dyt_ref[...], n2_ref[:, at]).astype(low), gout_ref.shape[0])


def attention_backward(windows, x_ref, vec_ref, line_ref, mask_ref, wq_ref, qkv_ref, pt_ref, do_ref, dx1_ref, n1t_ref, sums_in_ref,
                       gq_ref, gsmall_ref, grad_ref, sums_ref, bias_ref, tmp_ref, dproj_ref, dn_ref):
    bias_ref[...] = jnp.zeros_like(bias_ref)
    dn_ref[...] = jnp.zeros_like(dn_ref)
    sums_ref[...] = sums_in_ref[...]
    for part in range(3):
        dproj_ref[part, windows * TOK :, :] = jnp.zeros((ROWS - windows * TOK, GCOLS), low)

    def group(g, carry):
        cols = pl.ds(pl.multiple_of(g * GCOLS, GCOLS), GCOLS)

        def window(w, inner):
            rows = window_rows(w)
            q = qkv_ref[g, rows, :]
            k = qkv_ref[GROUPS + g, rows, :]
            v = qkv_ref[2 * GROUPS + g, rows, :]
            p = pt_ref[g, w]
            do = diag(do_ref[rows, cols], mask_ref)
            dp = dot_nt(v, do)
            dv = dot(p, do)
            pf = p.astype(full)
            ds = (pf * (dp - jnp.sum(pf * dp, 0, keepdims=True))).astype(low)
            bias_ref[g] += ds.astype(full)
            dk = dot(ds, diag(q, mask_ref))
            dq = undiag(k.T, ds, mask_ref) * (HEAD_DIM**-0.5)
            dq = dq.astype(low)
            dv = dv.astype(low)
            dproj_ref[0, rows, :] = dq
            dproj_ref[1, rows, :] = dk.astype(low)
            dproj_ref[2, rows, :] = dv
            sums_ref[2:3, cols] += jnp.sum(dq.astype(full), 0, keepdims=True)
            sums_ref[3:4, cols] += jnp.sum(dv.astype(full), 0, keepdims=True)
            return inner

        lax.fori_loop(0, windows, window, 0)
        for part in range(3):
            d = dproj_ref[part]
            gq_ref[g, part] = blocks(dot(n1t_ref[...], d).astype(low), gq_ref.shape[2])
            dn_ref[...] += dot_nt(d, flat(wq_ref[g, part]))
        return carry

    lax.fori_loop(0, GROUPS, group, 0)

    def finish(w, carry):
        rows = window_rows(w)
        xhat, scale = norm_parts(x_ref[rows, :].astype(full))
        dn = dn_ref[rows, :]
        grad_ref[rows, :] = dx1_ref[rows, :] + norm_back(xhat, scale, dn, vec_ref[0:1, :])
        sums_ref[0:1, :] += jnp.sum(dn * xhat, 0, keepdims=True)
        sums_ref[1:2, :] += jnp.sum(dn, 0, keepdims=True)
        return carry

    lax.fori_loop(0, windows, finish, 0)
    pack_small(sums_ref[...], table_grad(line_ref, tmp_ref, bias_ref), gsmall_ref)


MESH = pl.DeviceIdType.MESH
REPS = 4
OWNERS = 8
LINKS = OWNERS // 2


class Spot:
    def __init__(self):
        self.rep = lax.axis_index("rep")
        self.shard = lax.axis_index("shard")
        self.z = self.shard // 2
        self.core = self.shard % 2

    def sibling(self):
        return (self.rep, self.z * 2 + (1 - self.core))

    def along_z(self, step):
        return (self.rep, ((self.z + step) % LINKS) * 2 + self.core)

    def turned(self, axis):
        x, y = self.rep % 2, self.rep // 2
        return y * 2 + (1 - x) if axis == 0 else (1 - y) * 2 + x

    def beside(self, axis):
        return (self.turned(axis), self.shard)


def greet(spot):
    barrier = pltpu.get_barrier_semaphore()
    peers = [(spot.rep, (spot.shard + i) % OWNERS) for i in range(1, OWNERS)]
    peers += [((spot.rep + i) % REPS, spot.shard) for i in range(1, REPS)]
    for peer in peers:
        pl.semaphore_signal(barrier, inc=1, device_id=peer, device_id_type=MESH)
    return barrier, len(peers)


def send(src, dst, send_sem, recv_sem, peer):
    pltpu.make_async_remote_copy(src_ref=src, dst_ref=dst, send_sem=send_sem, recv_sem=recv_sem, device_id=peer, device_id_type=MESH).start()


def await_bytes(ref, sem):
    pltpu.make_async_copy(ref, ref, sem).wait()


def quarter(ref, rep):
    rows, cols = ref.shape[-2:]
    lead = (slice(None),) * (len(ref.shape) - 2)
    top = pl.multiple_of((rep // 2) * (rows // 2), 16)
    left = pl.multiple_of((rep % 2) * (cols // 2), 128)
    return ref.at[lead + (pl.ds(top, rows // 2), pl.ds(left, cols // 2))]


def half(ref, rep, axis):
    rows, cols = ref.shape[-2:]
    lead = (slice(None),) * (len(ref.shape) - 2)
    if axis == 0:
        left = pl.multiple_of((rep % 2) * (cols // 2), 128)
        return ref.at[lead + (slice(None), pl.ds(left, cols // 2))]
    top = pl.multiple_of((rep // 2) * (rows // 2), 16)
    return ref.at[lead + (pl.ds(top, rows // 2), slice(None))]


class Gather:
    KINDS = (LINKS - 1, LINKS - 1, LINKS - 1, LINKS - 1, LINKS)
    SEMS = 2 * sum(KINDS)
    STAGES = ("start", "across", "relay", "beside", "finish")

    def __init__(self, spot, place, axis, sems):
        self.spot, self.place, self.axis, self.sems = spot, place, axis, sems

    def sem(self, side, kind, i):
        return self.sems.at[side * (self.SEMS // 2) + sum(self.KINDS[:kind]) + i]

    def block(self, step):
        return self.place(((self.spot.z - step + LINKS) % LINKS) * 2 + self.spot.core)

    def other(self, step):
        return self.place(((self.spot.z - step + LINKS) % LINKS) * 2 + 1 - self.spot.core)

    def start(self):
        spot = self.spot
        mine = self.block(0)
        for i in range(1, LINKS):
            piece = quarter(mine, spot.rep)
            send(piece, piece, self.sem(0, 0, i - 1), self.sem(1, 0, i - 1), spot.along_z(i))
        send(mine, mine, self.sem(0, 4, 0), self.sem(1, 4, 0), spot.sibling())

    def across(self):
        spot = self.spot
        for i in range(1, LINKS):
            piece = quarter(self.block(i), spot.rep)
            await_bytes(piece, self.sem(1, 0, i - 1))
            for axis in (self.axis, 1 - self.axis):
                send(piece, piece, self.sem(0, 1 + axis, i - 1), self.sem(1, 1 + axis, i - 1), spot.beside(axis))

    def relay(self):
        spot = self.spot
        for i in range(1, LINKS):
            piece = quarter(self.block(i), spot.turned(self.axis))
            await_bytes(piece, self.sem(1, 1 + self.axis, i - 1))
            send(piece, piece, self.sem(0, 3, i - 1), self.sem(1, 3, i - 1), spot.beside(1 - self.axis))

    def beside(self):
        spot = self.spot
        for i in range(1, LINKS):
            block = self.block(i)
            piece = quarter(block, spot.rep)
            await_bytes(piece, self.sem(1, 2 - self.axis, i - 1))
            await_bytes(piece, self.sem(1, 3, i - 1))
            send(block, block, self.sem(0, 4, i), self.sem(1, 4, i), spot.sibling())

    def finish(self):
        for i in range(LINKS):
            await_bytes(self.other(i), self.sem(1, 4, i))

    def close(self):
        piece = quarter(self.block(0), self.spot.rep)
        for kind in range(4):
            for i in range(1, LINKS):
                await_bytes(piece, self.sem(0, kind, i - 1))
        for i in range(LINKS):
            await_bytes(self.block(i), self.sem(0, 4, i))


class Reduce:
    KINDS = (LINKS, 1, 1, LINKS - 1, REPS - 1)
    SEMS = 2 * sum(KINDS)
    STAGES = ("start", "first", "second", "along", "spread", "finish")

    def __init__(self, spot, place, out, core_sum, halves, quarters, links, axis, sems):
        self.spot, self.place, self.out, self.axis, self.sems = spot, place, out, axis, sems
        self.core_sum, self.halves, self.quarters, self.links = core_sum, halves, quarters, links

    def sem(self, side, kind, i):
        return self.sems.at[side * (self.SEMS // 2) + sum(self.KINDS[:kind]) + i]

    def start(self):
        spot = self.spot
        for z in range(LINKS):
            send(self.place(z * 2 + (1 - spot.core)), self.core_sum.at[z], self.sem(0, 0, z), self.sem(1, 0, z), spot.sibling())

    def first(self):
        spot = self.spot
        for z in range(LINKS):
            total = self.core_sum.at[z]
            await_bytes(total, self.sem(1, 0, z))
            total[...] = (total[...].astype(full) + self.place(z * 2 + spot.core)[...].astype(full)).astype(low)
        theirs = half(self.core_sum, spot.turned(self.axis), self.axis)
        send(theirs, self.halves, self.sem(0, 1, 0), self.sem(1, 1, 0), spot.beside(self.axis))

    def second(self):
        spot = self.spot
        await_bytes(self.halves, self.sem(1, 1, 0))
        mine = half(self.core_sum, spot.rep, self.axis)
        self.halves[...] = (self.halves[...].astype(full) + mine[...].astype(full)).astype(low)
        theirs = half(self.halves, spot.turned(1 - self.axis), 1 - self.axis)
        send(theirs, self.quarters, self.sem(0, 2, 0), self.sem(1, 2, 0), spot.beside(1 - self.axis))

    def along(self):
        spot = self.spot
        await_bytes(self.quarters, self.sem(1, 2, 0))
        mine = half(self.halves, spot.rep, 1 - self.axis)
        self.quarters[...] = (self.quarters[...].astype(full) + mine[...].astype(full)).astype(low)
        for i in range(1, LINKS):
            send(self.quarters.at[(spot.z + i) % LINKS], self.links.at[i - 1], self.sem(0, 3, i - 1), self.sem(1, 3, i - 1), spot.along_z(i))

    def spread(self):
        spot = self.spot
        total = self.quarters[spot.z].astype(full)
        for i in range(1, LINKS):
            await_bytes(self.links.at[i - 1], self.sem(1, 3, i - 1))
            total = total + self.links[i - 1].astype(full)
        mine = quarter(self.out, spot.rep)
        mine[...] = total.astype(low)
        for j in range(1, REPS):
            send(mine, mine, self.sem(0, 4, j - 1), self.sem(1, 4, j - 1), ((spot.rep + j) % REPS, spot.shard))

    def finish(self):
        for j in range(1, REPS):
            await_bytes(quarter(self.out, (self.spot.rep - j + REPS) % REPS), self.sem(1, 4, j - 1))

    def close(self):
        for z in range(LINKS):
            await_bytes(self.core_sum.at[z], self.sem(0, 0, z))
        await_bytes(self.halves, self.sem(0, 1, 0))
        await_bytes(self.quarters, self.sem(0, 2, 0))
        for i in range(1, LINKS):
            await_bytes(self.links.at[i - 1], self.sem(0, 3, i - 1))
        for j in range(1, REPS):
            await_bytes(quarter(self.out, self.spot.rep), self.sem(0, 4, j - 1))


class ReduceSmall:
    KINDS = (LINKS, LINKS - 1, REPS - 1)
    SEMS = 2 * sum(KINDS)
    STAGES = ("start", "first", "second", "along")

    def __init__(self, spot, terms, out, core_sum, links, parts, sems):
        self.spot, self.terms, self.out, self.core_sum, self.links, self.parts, self.sems = spot, terms, out, core_sum, links, parts, sems

    sem = Reduce.sem

    def start(self):
        spot = self.spot
        for z in range(LINKS):
            send(self.terms.at[z * 2 + (1 - spot.core)], self.core_sum.at[z], self.sem(0, 0, z), self.sem(1, 0, z), spot.sibling())

    def first(self):
        spot = self.spot
        for z in range(LINKS):
            await_bytes(self.core_sum.at[z], self.sem(1, 0, z))
            self.core_sum[z] = self.core_sum[z] + self.terms[z * 2 + spot.core]
        for i in range(1, LINKS):
            send(self.core_sum.at[(spot.z + i) % LINKS], self.links.at[i - 1], self.sem(0, 1, i - 1), self.sem(1, 1, i - 1), spot.along_z(i))

    def second(self):
        spot = self.spot
        total = self.core_sum[spot.z]
        for i in range(1, LINKS):
            await_bytes(self.links.at[i - 1], self.sem(1, 1, i - 1))
            total = total + self.links[i - 1]
        self.parts[spot.rep] = total
        mine = self.parts.at[spot.rep]
        for j in range(1, REPS):
            send(mine, mine, self.sem(0, 2, j - 1), self.sem(1, 2, j - 1), ((spot.rep + j) % REPS, spot.shard))

    def along(self):
        for j in range(1, REPS):
            await_bytes(self.parts.at[(self.spot.rep - j + REPS) % REPS], self.sem(1, 2, j - 1))
        total = self.parts[0]
        for j in range(1, REPS):
            total = total + self.parts[j]
        self.out[...] = total

    def close(self):
        for z in range(LINKS):
            await_bytes(self.core_sum.at[z], self.sem(0, 0, z))
        for i in range(1, LINKS):
            await_bytes(self.links.at[i - 1], self.sem(0, 1, i - 1))
        for j in range(1, REPS):
            await_bytes(self.parts.at[self.spot.rep], self.sem(0, 2, j - 1))


OWNED = C // OWNERS
SLOTS = TILES + 1
GATHERS = 2 * TILES + 1 + GROUPS
REDUCES = 2 * TILES + 1 + (GROUPS - 1) + 3
W_Q0, W_Q1, W_Q2, W_P, W_U0, W_D0, W_U1, W_D1, W_U2, W_D2 = W_ALL = range(10)
G_D0, G_U0, G_D1, G_U1, G_D2, G_U2, G_P, G_Q0, G_Q1, G_Q2, G_K2, G_V2, G_S = G_ALL = range(10, 23)
W_Q, W_U, W_D = (W_Q0, W_Q1, W_Q2), (W_U0, W_U1, W_U2), (W_D0, W_D1, W_D2)
G_D, G_U, G_Q, G_LAST = (G_D0, G_D1, G_D2), (G_U0, G_U1, G_U2), (G_Q0, G_Q1), (G_Q2, G_K2, G_V2)
START, ACROSS, RELAY, BESIDE, ARRIVED = range(5)
FIRST, SECOND, ALONG, SPREAD, SUMMED = range(1, 6)
BEFORE = {
    3: ((W_Q0, ACROSS), (W_Q1, ACROSS), (W_Q2, START), (W_P, START),),
}
FORWARD = {
    0: ((W_Q1, RELAY), (W_Q2, ACROSS), (W_U0, START),),
    1: ((W_P, ACROSS), (W_D0, START),),
    7: ((W_Q2, RELAY), (W_P, RELAY), (W_U0, ACROSS), (W_U1, START),),
    9: ((W_D0, ACROSS), (W_D1, START),),
    14: ((W_P, BESIDE), (W_U0, RELAY), (W_D0, RELAY), (W_U1, ACROSS), (W_U2, START),),
    18: ((W_D1, ACROSS), (W_D2, START),),
}
MIDDLE = {
    1: ((W_U0, BESIDE), (W_U2, ACROSS), (W_D0, BESIDE),),
    2: ((W_U1, RELAY), (W_D1, RELAY),),
}
TILE_STEP = {
    0: ((W_D2, ACROSS),),
    1: ((W_U1, BESIDE), (W_D1, BESIDE), (W_U2, RELAY),),
    2: ((W_U2, BESIDE), (W_D2, RELAY),),
    3: ((W_D2, BESIDE),),
    4: ((G_D0, FIRST), (G_U0, FIRST),),
}
AFTER_TILES = {
    0: ((G_D0, SECOND), (G_U0, SECOND), (G_D1, FIRST), (G_U1, FIRST),),
}
BACKWARD = {
    2: ((G_D0, ALONG), (G_D2, FIRST), (G_U2, FIRST), (G_U0, ALONG),),
    7: ((G_D0, SPREAD),),
    8: ((G_D1, SECOND), (G_U1, SECOND),),
    12: ((G_D0, SUMMED), (G_U0, SPREAD),),
    14: ((G_U2, SECOND), (G_Q0, FIRST),),
    15: ((G_U0, SUMMED), (G_P, FIRST),),
    16: ((G_D1, ALONG), (G_D2, SECOND), (G_U1, ALONG),),
    20: ((G_Q1, FIRST),),
}
LAST_STEPS = {
    0: ((G_U2, ALONG), (G_Q2, FIRST),),
    1: ((G_D2, ALONG), (G_Q0, SECOND), (G_V2, FIRST),),
    3: ((G_D1, SPREAD), (G_P, SECOND),),
}


def chunk_shapes():
    out = []
    for _ in range(TILES):
        out += [(128, C), (OWNED, TILE)]
    return out + [(OWNED, C)] + [(3, OWNED, GCOLS)] * (GROUPS - 1) + [(OWNED, GCOLS)] * 3


def reduce_scratch():
    out = []
    for i, dims in enumerate(chunk_shapes()):
        *lead, rows, cols = dims
        near = (rows, cols // 2) if i % 2 == 0 else (rows // 2, cols)
        out.append(pltpu.VMEM((LINKS, *dims), low))
        out.append(pltpu.VMEM((LINKS, *lead, *near), low))
        out.append(pltpu.VMEM((LINKS, *lead, rows // 2, cols // 2), low))
        out.append(pltpu.VMEM((LINKS - 1, *lead, rows // 2, cols // 2), low))
    out += [pltpu.VMEM((LINKS, 40, 128), full), pltpu.VMEM((LINKS - 1, 40, 128), full), pltpu.VMEM((REPS, 40, 128), full)]
    return out


def layer_kernel(windows, x_hbm, dy_hbm, count_ref, q32, p32, u32, d32, vec_in, tab_in, line_ref, mask_ref,
                 out_hbm, grad_hbm, gq_out, gp_out, gu_out, gd_out, gs_out, qkv_hbm, pt_hbm, n1t_hbm, *scratch):
    wq, wp, up, down, small, o_ref, x1_ref, vec_ref, sums_ref, terms_ref = scratch[:10]
    gather_sems, reduce_sems, small_sems, small_reduce_sems, local = scratch[-5:]
    reduce_refs = scratch[10:-5]
    spot = Spot()
    rows_all = windows * TOK

    def live(w):
        return (w < count_ref[0]).astype(full)

    mine = spot.shard
    V = pltpu.VMEM

    jobs = {}
    places = [(W_Q[g], lambda s, g=g: wq.at[g, :, s]) for g in range(GROUPS)] + [(W_P, lambda s: wp.at[s])]
    for t in range(TILES):
        places += [(W_U[t], lambda s, t=t: up.at[t, s]), (W_D[t], lambda s, t=t: down.at[t, s])]
    for i, (name, place) in enumerate(places):
        jobs[name] = Gather(spot, place, i % 2, gather_sems.at[i])
    places = []
    for t in range(TILES):
        slot = (t + SLOTS - 1) % SLOTS
        places.append((G_D[t], lambda s, slot=slot: down.at[slot, s], gd_out.at[t]))
        places.append((G_U[t], lambda s, slot=slot: up.at[slot, s], gu_out.at[t]))
    places.append((G_P, lambda s: wp.at[s], gp_out))
    for g in range(GROUPS - 1):
        places.append((G_Q[g], lambda s, g=g: wq.at[g, :, s], gq_out.at[g]))
    for part in range(3):
        places.append((G_LAST[part], lambda s, part=part: wq.at[GROUPS - 1, part, s], gq_out.at[GROUPS - 1, part]))
    for i, (name, place, out) in enumerate(places):
        jobs[name] = Reduce(spot, place, out, *reduce_refs[4 * i : 4 * i + 4], i % 2, reduce_sems.at[i])
    jobs[G_S] = ReduceSmall(spot, terms_ref, gs_out, *reduce_refs[-3:], small_reduce_sems)

    done = {}

    def run(name, upto):
        for stage in range(done.get(name, 0), upto + 1):
            getattr(jobs[name], jobs[name].STAGES[stage])()
        done[name] = max(done.get(name, 0), upto + 1)

    def hook(table, place):
        for item in table.get(place, ()):
            run(*item)

    def hook_window(table, g, w):
        for at in range(windows):
            place = g * windows + at
            if place in table:

                @pl.when(w == at)
                def _(place=place):
                    hook(table, place)

    barrier, peers = greet(spot)

    def cast(q_v, p_v, u_v, d_v):
        loads = [pltpu.make_async_copy(a, b, local.at[i]) for i, (a, b) in enumerate(((q32, q_v), (p32, p_v), (u32, u_v), (d32, d_v)))]
        for load in loads:
            load.start()
        small[mine] = jnp.zeros((48, 128), low)
        pad = jnp.zeros((16, 128), full)
        vec_ref[:, 0:128] = pad
        vec_ref[0:12, 0:OWNED] = vec_in[...]
        small[mine, 0:16, :] = vec_ref[:, 0:128].astype(low)
        x1_ref[0:32, 0:128] = jnp.zeros((32, 128), full)
        x1_ref[0:HEADS, 0 : tab_in.shape[1]] = tab_in[...]
        small[mine, 16:48, :] = x1_ref[0:32, 0:128].astype(low)
        loads[0].wait()
        for g in range(GROUPS):
            for part in range(3):
                wq[g, part, mine] = q_v[:, part * C + g * GCOLS : part * C + (g + 1) * GCOLS].astype(low)
        pl.semaphore_wait(barrier, peers)
        for i in range(1, OWNERS):
            send(small.at[mine], small.at[mine], small_sems.at[i], small_sems.at[OWNERS + i], (spot.rep, (mine + i) % OWNERS))
        run(W_Q0, START)
        run(W_Q1, START)
        loads[1].wait()
        wp[mine] = p_v[...].astype(low)
        loads[2].wait()
        loads[3].wait()
        for t in range(TILES):
            for s in range(OWNERS):
                src = (MLP // OWNERS) * s + 128 * t
                up[t, mine, :, s * 128 : (s + 1) * 128] = u_v[:, src : src + 128].astype(low)
            down[t, mine] = d_v[t * 128 : (t + 1) * 128, :].astype(low)

    pl.run_scoped(cast, V((OWNED, 3 * C), full), V((OWNED, C), full), V((OWNED, MLP), full), V((TILES * 128, C), full))

    def forward(x_ref, n1_ref, n1t_ref, qkv_ref, pt_ref, bias_ref):
        load = pltpu.make_async_copy(x_hbm, x_ref, local.at[0])
        load.start()
        zero_tail(n1_ref, windows)
        zero_tail(o_ref, windows)
        for i in range(1, OWNERS):
            await_bytes(small.at[(mine - i + OWNERS) % OWNERS], small_sems.at[OWNERS + i])
        tab = unpack_small(small, vec_ref)
        hook(BEFORE, 0)
        load.wait()
        hook(BEFORE, 1)

        def first_norm(w, rows):
            xhat, _ = norm_parts(x_ref[rows, :].astype(full))
            n1_ref[rows, :] = (xhat * vec_ref[0:1, :] + vec_ref[1:2, :]).astype(low)

        by_rows(windows, first_norm)
        hook(BEFORE, 2)
        transpose_rows(n1_ref, n1t_ref)
        save = pltpu.make_async_copy(n1t_ref, n1t_hbm, local.at[1])
        save.start()
        hook(BEFORE, 3)

        def bias(tmp_ref):
            spread_table(tab, line_ref, tmp_ref)
            hook(BEFORE, 4)
            place_bias(tmp_ref, bias_ref)

        pl.run_scoped(bias, V((2, TOK * HEADS, 128), full))
        for g in range(GROUPS):
            cols = slice(g * GCOLS, (g + 1) * GCOLS)
            held = qkv_ref.at[g % 2]
            if g >= 2:
                pltpu.make_async_copy(held, qkv_hbm.at[g - 2], local.at[2 + g % 2]).wait()
            run(W_Q[g], ARRIVED)
            n1 = n1_ref[...]
            held[0] = ((dot(n1, flat(wq[g, 0])) + vec_ref[2:3, cols]) * (HEAD_DIM**-0.5)).astype(low)
            held[1] = dot(n1, flat(wq[g, 1])).astype(low)
            held[2] = (dot(n1, flat(wq[g, 2])) + vec_ref[3:4, cols]).astype(low)
            pltpu.make_async_copy(held, qkv_hbm.at[g], local.at[2 + g % 2]).start()

            def window(w, carry, g=g, cols=cols, held=held):
                hook_window(FORWARD, g, w)
                rows = window_rows(w)
                n = g * windows + w
                slot = n % 2
                keep = pltpu.make_async_copy(pt_ref.at[slot], pt_hbm.at[n], local.at[4 + slot])

                @pl.when(n >= 2)
                def _():
                    keep.wait()

                q = held[0, rows, :]
                k = held[1, rows, :]
                vt = held[2, rows, :].T

                def soft(s, lanes):
                    s = s + bias_ref[g, :, lanes]
                    e = jnp.exp(s - jnp.max(s, 0, keepdims=True))
                    p = (e * (1.0 / jnp.sum(e, 0, keepdims=True))).astype(low)
                    pt_ref[slot, :, lanes] = p
                    return p

                main = []
                for pair in range(GHEADS // 2):
                    lanes = slice(pair * 256, (pair + 1) * 256)
                    main += pair_values(vt, pair, soft(dot_nt(half_of(k, pair), pair_diag(q, pair, mask_ref)), lanes))
                lanes = slice(GHEADS * 128, PACK)
                rest = dot(vt, soft(dot_nt(k, rest_diag(q, mask_ref)), lanes))
                keep.start()
                o_ref[rows, cols] = join_values(main, rest, mask_ref).astype(low)
                return carry

            lax.fori_loop(0, windows, window, 0)

        run(W_P, ARRIVED)

        def output(w, carry):
            rows = window_rows(w)
            x1_ref[rows, :] = x_ref[rows, :].astype(full) + (dot(o_ref[rows, :], flat(wp[...])) + vec_ref[4:5, :])
            return carry

        lax.fori_loop(0, windows, output, 0)
        save.wait()
        for g in (GROUPS - 2, GROUPS - 1):
            pltpu.make_async_copy(qkv_ref.at[g % 2], qkv_hbm.at[g], local.at[2 + g % 2]).wait()
        for slot in range(2):
            pltpu.make_async_copy(pt_ref.at[slot], pt_hbm.at[0], local.at[4 + slot]).wait()

    pl.run_scoped(forward, V((rows_all, C), low), V((ROWS, C), low), V((C, ROWS), low), V((2, 3, ROWS, GCOLS), low), V((2, TOK, PACK), low),
                  V((GROUPS, TOK, PACK), full))

    def middle(n2_ref, n2t_ref, dy_ref, dyt_ref, y_ref, dn_ref, bu_ref, bsum_ref, h_ref, da_ref, a_ref, dh_ref, part_ref):
        load = pltpu.make_async_copy(dy_hbm, dy_ref.at[0:rows_all], local.at[0])
        load.start()
        zero_tail(n2_ref, windows)
        zero_tail(dy_ref, windows)
        hook(MIDDLE, 0)
        load.wait()

        def second_norm(w, rows):
            xhat, _ = norm_parts(x1_ref[rows, :])
            n2_ref[rows, :] = (xhat * vec_ref[5:6, :] + vec_ref[6:7, :]).astype(low)
            dy_ref[rows, :] = (dy_ref[rows, :].astype(full) * live(w)).astype(low)

        by_rows(windows, second_norm)
        transpose_rows(n2_ref, n2t_ref)
        hook(MIDDLE, 1)
        transpose_rows(dy_ref, dyt_ref)
        n2t_ref[C:, :] = jnp.ones((16, ROWS), low)
        y_ref[...] = jnp.zeros_like(y_ref)
        dn_ref[...] = jnp.zeros_like(dn_ref)
        for t in range(TILES):
            for s in range(TILE // 128):
                row, left = hidden_place(t, s)
                bu_ref[t, :, s * 128 : (s + 1) * 128] = vec_ref[row : row + 1, left : left + 128]
        hook(MIDDLE, 2)
        run(W_U0, ARRIVED)
        run(W_D0, ARRIVED)
        hook(TILE_STEP, 0)
        halves = TILE // SUB

        def step(i, carry):
            for k in range(1, TILES * halves):

                @pl.when(i == k)
                def _(k=k):
                    if k % halves == 0:
                        t = k // halves
                        for name in (W_U[t], W_D[t]):
                            run(name, ARRIVED)
                        for name in (W_U[t - 1], W_D[t - 1]):
                            jobs[name].close()
                        for name in (G_D[t - 1], G_U[t - 1]):
                            run(name, START)
                    hook(TILE_STEP, k)

            t, part = i // halves, i % halves
            cols = pl.ds(pl.multiple_of(part * SUB, SUB), SUB)
            wide = SUB // 128
            slot = (t + SLOTS - 1) % SLOTS
            u = flat(up[t, :, :, cols])
            d = flat(down[t, pl.ds(part * wide, wide)])
            h_ref[...] = dot(n2_ref[...], u)
            da_ref[...] = dot_nt(dy_ref[...], d)
            bias = bu_ref[t, :, cols]
            for k in range(ROWS // CHUNK):
                rows = slice(k * CHUNK, (k + 1) * CHUNK)
                act, slope = gelu_both(h_ref[rows] + bias)
                a_ref[rows] = act.astype(low)
                dh_ref[rows] = (da_ref[rows] * slope).astype(low)
            a = a_ref[...]
            dh = dh_ref[...]
            y_ref[...] += dot(a, d)
            dn_ref[...] += dot_nt(dh, u)
            gd = dot(dyt_ref[...], a).astype(low)
            down[slot, pl.ds(part * wide, wide)] = blocks(gd.T, wide)
            gu = dot(n2t_ref[...], dh)
            up[slot, :, :, cols] = blocks(gu[0:C].astype(low), OWNERS)
            bsum_ref[t, :, cols] = gu[C : C + 1]
            return carry

        lax.fori_loop(0, TILES * halves, step, 0)
        run(G_D[-1], START)
        run(G_U[-1], START)
        hook(AFTER_TILES, 0)
        sums_ref[...] = jnp.zeros_like(sums_ref)
        for t in range(TILES):
            for s in range(TILE // 128):
                row, left = hidden_place(t, s)
                sums_ref[row : row + 1, left : left + 128] = bsum_ref[t, :, s * 128 : (s + 1) * 128]
        transpose_rows(o_ref, dyt_ref)
        hook(AFTER_TILES, 1)

        part_ref[...] = jnp.zeros_like(part_ref)

        def finish(w, rows):
            x1 = x1_ref[rows, :]
            xhat, scale = norm_parts(x1)
            dn = dn_ref[rows, :]
            dy = dy_ref[rows, :].astype(full)
            dx1 = dy + norm_back(xhat, scale, dn, vec_ref[5:6, :])
            dr = dx1.astype(low)
            part_ref[0] += fold(dr.astype(full))
            part_ref[1] += fold(dn * xhat)
            part_ref[2] += fold(dn)
            part_ref[3] += fold(dy)
            dy_ref[rows, :] = ((x1 + y_ref[rows, :] + vec_ref[7:8, :]) * live(w)).astype(low)
            x1_ref[rows, :] = dx1
            n2_ref[rows, :] = dr

        by_rows(windows, finish)
        sums_ref[4:8, :] = jnp.sum(part_ref[...], 1)

        def project(w, carry):
            rows = window_rows(w)
            o_ref[rows, :] = dot_nt(n2_ref[rows, :], flat(wp[...])).astype(low)
            return carry

        lax.fori_loop(0, windows, project, 0)
        save = pltpu.make_async_copy(dy_ref.at[0:rows_all], out_hbm, local.at[0])
        save.start()
        hook(AFTER_TILES, 2)
        jobs[W_P].close()
        for g in range(GROUPS):
            cols = slice(g * GCOLS, (g + 1) * GCOLS)
            wp[:, :, cols] = blocks(dot(dyt_ref[...], n2_ref[:, cols]).astype(low), OWNERS)
        run(G_P, START)
        hook(AFTER_TILES, 3)
        save.wait()

    pl.run_scoped(middle, V((ROWS, C), low), V((C + 16, ROWS), low), V((ROWS, C), low), V((C, ROWS), low), V((ROWS, C), full), V((ROWS, C), full),
                  V((TILES, 1, TILE), full), V((TILES, 1, TILE), full), V((ROWS, SUB), full), V((ROWS, SUB), full), V((ROWS, SUB), low), V((ROWS, SUB), low),
                  V((4, 8, C), full))

    def backward(x_ref, n1t_ref, qkv_ref, pt_ref, dproj_ref, dn_ref, bias_ref):
        loads = [pltpu.make_async_copy(x_hbm, x_ref, local.at[0]), pltpu.make_async_copy(n1t_hbm, n1t_ref, local.at[1])]
        fetch = [pltpu.make_async_copy(qkv_hbm.at[g], qkv_ref.at[g % 2], local.at[2 + g % 2]) for g in range(GROUPS)]
        fetch[0].start()
        pltpu.make_async_copy(pt_hbm.at[0], pt_ref.at[0], local.at[4]).start()
        fetch[1].start()
        for load in loads:
            load.start()
        bias_ref[...] = jnp.zeros_like(bias_ref)
        dn_ref[...] = jnp.zeros_like(dn_ref)
        for part in range(3):
            dproj_ref[part, rows_all:, :] = jnp.zeros((ROWS - rows_all, GCOLS), low)
        for g in range(GROUPS):
            cols = slice(g * GCOLS, (g + 1) * GCOLS)
            held = qkv_ref.at[g % 2]
            fetch[g].wait()

            def window(w, carry, g=g, cols=cols, held=held):
                hook_window(BACKWARD, g, w)
                rows = window_rows(w)
                n = g * windows + w
                slot = n % 2

                @pl.when(n + 1 < GROUPS * windows)
                def _():
                    pltpu.make_async_copy(pt_hbm.at[n + 1], pt_ref.at[1 - slot], local.at[5 - slot]).start()

                pltpu.make_async_copy(pt_hbm.at[n], pt_ref.at[slot], local.at[4 + slot]).wait()
                q = held[0, rows, :]
                k = held[1, rows, :]
                v = held[2, rows, :]
                kt = k.T
                do = o_ref[rows, cols]

                def back(dp, lanes):
                    p = pt_ref[slot, :, lanes]
                    pf = p.astype(full)
                    ds = (pf * (dp - jnp.sum(pf * dp, 0, keepdims=True))).astype(low)
                    bias_ref[g, :, lanes] += ds.astype(full)
                    return p, ds

                main, dv, dk = [], [], []
                for pair in range(GHEADS // 2):
                    lanes = slice(pair * 256, (pair + 1) * 256)
                    wide = pair_diag(do, pair, mask_ref)
                    p, ds = back(dot_nt(half_of(v, pair), wide), lanes)
                    main += pair_values(kt, pair, ds)
                    dv.append(dot(p, wide))
                    dk.append(dot(ds, pair_diag(q, pair, mask_ref)))
                wide = rest_diag(do, mask_ref)
                p, ds = back(dot_nt(v, wide), slice(GHEADS * 128, PACK))
                dv = (jnp.concatenate([dv[0] + dv[1], dv[2] + dv[3]], 1) + dot(p, wide)).astype(low)
                dk = jnp.concatenate([dk[0] + dk[1], dk[2] + dk[3]], 1) + dot(ds, rest_diag(q, mask_ref))
                dq = (join_values(main, dot(kt, ds), mask_ref) * (HEAD_DIM**-0.5)).astype(low)
                dproj_ref[0, rows, :] = dq
                dproj_ref[1, rows, :] = dk.astype(low)
                dproj_ref[2, rows, :] = dv
                sums_ref[2:3, cols] += jnp.sum(dq.astype(full), 0, keepdims=True)
                sums_ref[3:4, cols] += jnp.sum(dv.astype(full), 0, keepdims=True)
                return carry

            lax.fori_loop(0, windows, window, 0)
            if g + 2 < GROUPS:
                fetch[g + 2].start()
            if g == 0:
                for load in loads:
                    load.wait()
            jobs[W_Q[g]].close()
            for part in range(3):
                d = dproj_ref[part]
                dn_ref[...] += dot_nt(d, flat(wq[g, part]))
                wq[g, part] = blocks(dot(n1t_ref[...], d).astype(low), OWNERS)
                if g == GROUPS - 1:
                    run(G_LAST[part], START)
            if g < GROUPS - 1:
                run(G_Q[g], START)
        hook(LAST_STEPS, 0)

        def last_norm(grad_ref, part_ref):
            part_ref[...] = jnp.zeros_like(part_ref)

            def finish(w, carry):
                slot = w % 2
                save = pltpu.make_async_copy(grad_ref.at[slot], grad_hbm.at[window_rows(w)], local.at[4 + slot])

                @pl.when(w >= 2)
                def _():
                    save.wait()

                for k in range(TOK // CHUNK):
                    rows = pl.ds(pl.multiple_of(w * TOK + k * CHUNK, CHUNK), CHUNK)
                    xhat, scale = norm_parts(x_ref[rows, :].astype(full))
                    dn = dn_ref[rows, :]
                    grad_ref[slot, k * CHUNK : (k + 1) * CHUNK] = x1_ref[rows, :] + norm_back(xhat, scale, dn, vec_ref[0:1, :])
                    part_ref[0] += fold(dn * xhat)
                    part_ref[1] += fold(dn)
                save.start()
                return carry

            lax.fori_loop(0, windows, finish, 0)
            sums_ref[0:2, :] = jnp.sum(part_ref[...], 1)
            hook(LAST_STEPS, 1)
            for slot in range(2):
                pltpu.make_async_copy(grad_ref.at[slot], grad_hbm.at[pl.ds(0, TOK)], local.at[4 + slot]).wait()

        pl.run_scoped(last_norm, V((2, TOK, C), full), V((2, 8, C), full))
        hook(LAST_STEPS, 2)

        def table(tmp_ref):
            pack_small(sums_ref[...], table_grad(line_ref, tmp_ref, bias_ref), terms_ref)

        pl.run_scoped(table, V((2, TOK * HEADS, 128), full))
        run(G_S, START)
        hook(LAST_STEPS, 3)
        for stage in range(len(Reduce.STAGES)):
            for name in G_ALL:
                if stage < len(jobs[name].STAGES):
                    run(name, stage)

    pl.run_scoped(backward, V((rows_all, C), low), V((C, ROWS), low), V((2, 3, ROWS, GCOLS), low), V((2, TOK, PACK), low), V((3, ROWS, GCOLS), low),
                  V((ROWS, C), full), V((GROUPS, TOK, PACK), full))
    jobs[W_U[-1]].close()
    jobs[W_D[-1]].close()
    for i in range(1, OWNERS):
        await_bytes(small.at[mine], small_sems.at[i])
    for name in G_ALL:
        jobs[name].close()


def shape(dims, kind):
    return jax.ShapeDtypeStruct(dims, kind)


def adamw(weight, moment, second, gradient, step_rate):
    moment_new = beta_one * moment + (1.0 - beta_one) * gradient
    second_new = beta_two * second + (1.0 - beta_two) * gradient * gradient
    update = moment_new * (1.0 / (1.0 - beta_one**STEP)) / (jnp.sqrt(second_new * (1.0 / (1.0 - beta_two**STEP))) + adam_eps)
    weight_new = weight * (1.0 - step_rate * weight_decay) - step_rate * update
    return (weight_new, moment_new, second_new)


def update_kernel(*refs):
    gq, gp, gu, gd, gs = refs[:5]
    ins = [refs[5 + 3 * i : 8 + 3 * i] for i in range(6)]
    outs = [refs[25 + 4 * i : 29 + 4 * i] for i in range(4)] + [refs[41:44], refs[44:47]]
    for i in range(2):
        refs[47 + i][...] = refs[23 + i][...]

    def piece(which, place, gradient):
        new = adamw(*(ref[place] for ref in ins[which]), gradient, step_rates[which])
        for ref, value in zip(outs[which], new):
            ref[place] = value
        if which < 4:
            outs[which][3][place] = new[0].astype(low)

    for part in range(3):
        for g in range(GROUPS):
            left = part * C + g * GCOLS
            piece(0, (slice(None), slice(left, left + GCOLS)), gq[g, part].astype(full))
    piece(1, (slice(None), slice(None)), gp[...].astype(full))
    for t in range(TILES):
        for s in range(OWNERS):
            left = (MLP // OWNERS) * s + 128 * t
            piece(2, (slice(None), slice(left, left + 128)), gu[t, :, s * 128 : (s + 1) * 128].astype(full))
    piece(3, (slice(None), slice(None)), gd[0].astype(full))

    @pl.when(pl.program_id(0) == 0)
    def _():
        every = (slice(None), slice(None))
        piece(4, every, gs[0:12, 0:OWNED])
        piece(5, every, gs[16:40, 0 : ins[5][0].shape[1]])


def update(gq, gp, gu, gd, gs, states, results):
    steps = OWNED // 16

    def rows_of(array):
        tall = array.shape[0] // steps
        return pl.BlockSpec((tall, array.shape[1]), lambda i: (i, 0))

    def whole(array):
        return pl.BlockSpec(array.shape, lambda i: (0, 0))

    per_tile = 128 * TILES // steps
    specs = [
        pl.BlockSpec((GROUPS, 3, 16, GCOLS), lambda i: (0, 0, i, 0)),
        pl.BlockSpec((16, C), lambda i: (i, 0)),
        pl.BlockSpec((TILES, 16, TILE), lambda i: (0, i, 0)),
        pl.BlockSpec((1, per_tile, C), lambda i: (i // (128 // per_tile), i % (128 // per_tile), 0)),
        whole(gs),
    ]
    out_shapes, out_specs = [], []
    for i, group in enumerate(states):
        for array in group:
            specs.append(rows_of(array) if i < 4 else whole(array))
            out_shapes.append(shape(array.shape, full))
            out_specs.append(specs[-1])
        if i < 4:
            out_shapes.append(shape(group[0].shape, low))
            out_specs.append(rows_of(group[0]))
    results = [array.reshape(steps, -1, C) for array in results]
    for array in results:
        specs.append(pl.BlockSpec((1, *array.shape[1:]), lambda i: (i, 0, 0)))
        out_shapes.append(shape(array.shape, array.dtype))
        out_specs.append(specs[-1])
    return pl.pallas_call(
        update_kernel,
        grid=(steps,),
        in_specs=specs,
        out_specs=out_specs,
        out_shape=out_shapes,
        compiler_params=pltpu.CompilerParams(vmem_limit_bytes=63 * MIB),
        name="update",
    )(gq, gp, gu, gd, gs, *[array for group in states for array in group], *results)


def shards(
    tokens, out_grad, window_count,
    qkv_weight, qkv_first, qkv_second,
    output_weight, output_first, output_second,
    up_weight, up_first, up_second,
    down_weight, down_first, down_second,
    vectors, vector_first, vector_second,
    bias_table, table_first, table_second,
):
    windows = tokens.shape[0]
    rows = windows * TOK
    V = pltpu.VMEM
    D = pltpu.SemaphoreType.DMA
    hbm = pl.BlockSpec(memory_space=pl.ANY)
    vmem = pl.BlockSpec(memory_space=pltpu.VMEM)
    result = pl.pallas_call(
        functools.partial(layer_kernel, windows),
        out_shape=[
            shape((rows, C), low), shape((rows, C), full),
            shape((GROUPS, 3, OWNED, GCOLS), low), shape((OWNED, C), low), shape((TILES, OWNED, TILE), low), shape((TILES, 128, C), low),
            shape((40, 128), full),
            shape((GROUPS, 3, ROWS, GCOLS), low), shape((GROUPS * windows, TOK, PACK), low), shape((C, ROWS), low)],
        in_specs=[hbm, hbm, pl.BlockSpec(memory_space=pltpu.SMEM)] + [hbm] * 4 + [vmem] * 4,
        out_specs=[hbm, hbm] + [vmem] * 5 + [hbm] * 3,
        scratch_shapes=[
            V((GROUPS, 3, OWNERS, OWNED, GCOLS), low), V((OWNERS, OWNED, C), low), V((SLOTS, OWNERS, OWNED, TILE), low),
            V((SLOTS, OWNERS, 128, C), low), V((OWNERS, 48, 128), low), V((ROWS, C), low), V((rows, C), full), V((16, C), full), V((16, C), full),
            V((OWNERS, 40, 128), full)]
        + reduce_scratch()
        + [D((GATHERS, Gather.SEMS)), D((REDUCES, Reduce.SEMS)), D((2 * OWNERS,)), D((ReduceSmall.SEMS,)), D((6,))],
        compiler_params=pltpu.CompilerParams(vmem_limit_bytes=63 * MIB, collective_id=0, has_side_effects=True),
        name="layer",
    )(tokens.reshape(rows, C), out_grad.reshape(rows, C), window_count, qkv_weight, output_weight, up_weight, down_weight, vectors, bias_table.T,
      jnp.asarray(line_matrix(), low), jnp.asarray(head_masks(), low))
    out, grad, gq, gp, gu, gd, gs = result[:7]
    new = update(gq, gp, gu, gd, gs, (
        (qkv_weight, qkv_first, qkv_second), (output_weight, output_first, output_second), (up_weight, up_first, up_second),
        (down_weight, down_first, down_second), (vectors, vector_first, vector_second), (bias_table.T, table_first.T, table_second.T)), (out, grad))
    *new, out, grad = new
    return (out.reshape(tokens.shape), grad.reshape(tokens.shape), *new[:-3], *(array.T for array in new[-3:]))


def vmem_call(body, outs, scratch, args, name, limit=60, **params):
    spec = pl.BlockSpec(memory_space=pltpu.VMEM)
    return pl.pallas_call(
        body,
        out_shape=outs,
        in_specs=[pl.BlockSpec(memory_space=pltpu.SMEM) if a.dtype == full and a.ndim == 1 else spec for a in args],
        out_specs=[spec] * len(outs),
        scratch_shapes=scratch,
        compiler_params=pltpu.CompilerParams(vmem_limit_bytes=limit * MIB, **params),
        name=name,
    )(*args)


def local_step(tokens, out_grad, window_count, small, wq, wp, up, down):
    windows = tokens.shape[0]
    rows = windows * TOK
    owned = C // OWNERS
    V = pltpu.VMEM
    x = tokens.reshape(rows, C)
    dy = out_grad.reshape(rows, C)
    live = (jnp.arange(windows) < window_count[0]).astype(full)
    line = jnp.asarray(line_matrix(), low)
    masks = jnp.asarray(head_masks(), low)
    qkv, pt, o, x1, n1t, vec = vmem_call(
        functools.partial(attention_forward, windows),
        [shape((9, ROWS, GCOLS), low), shape((GROUPS, windows, TOK, PACK), low), shape((ROWS, C), low), shape((rows, C), full), shape((C, ROWS), low),
         shape((16, C), full)],
        [V((ROWS, C), low), V((GROUPS, TOK, PACK), full), V((2, TOK * HEADS, 128), full)],
        (x, small, line, masks, wq, wp), "attention_forward")
    out, dx1, do, gup, gdown, gout, sums = vmem_call(
        functools.partial(feed_forward, windows),
        [shape((rows, C), low), shape((ROWS, C), full), shape((rows, C), low), shape((TILES, OWNERS, owned, TILE), low),
         shape((TILES, OWNERS, C, 128), low), shape((OWNERS, owned, C), low), shape((16, C), full)],
        [V((ROWS, C), low), V((C, ROWS), low), V((ROWS, C), low), V((C, ROWS), low), V((ROWS, C), full), V((ROWS, C), full),
         V((TILES, 1, TILE), full), V((TILES, 1, TILE), full)],
        (x1, dy, live, vec, up, down, wp, o), "feed_forward")
    gq, gsmall, grad = vmem_call(
        functools.partial(attention_backward, windows),
        [shape((GROUPS, 3, OWNERS, owned, GCOLS), low), shape((OWNERS, 40, 128), full), shape((rows, C), full)],
        [V((16, C), full), V((GROUPS, TOK, PACK), full), V((2, TOK * HEADS, 128), full), V((3, ROWS, GCOLS), low), V((ROWS, C), full)],
        (x, vec, line, masks, wq, qkv, pt, do, dx1, n1t, sums), "attention_backward")
    return out.reshape(tokens.shape), grad.reshape(tokens.shape), gq, gout, gup, gdown, gsmall


def shards_general(
    tokens, out_grad, window_count,
    qkv_weight, qkv_first, qkv_second,
    output_weight, output_first, output_second,
    up_weight, up_first, up_second,
    down_weight, down_first, down_second,
    vectors, vector_first, vector_second,
    bias_table, table_first, table_second,
):
    gather = functools.partial(lax.all_gather, axis_name="shard", tiled=True)
    scatter = functools.partial(lax.psum_scatter, axis_name="shard", tiled=True)
    owned = C // OWNERS
    wq = gather(qkv_weight.astype(low), axis=0).reshape(OWNERS, owned, 3, GROUPS, GCOLS).transpose(3, 2, 0, 1, 4)
    wp = gather(output_weight.astype(low), axis=0).reshape(OWNERS, owned, C)
    up = gather(up_weight.astype(low), axis=0).reshape(OWNERS, owned, OWNERS, TILES, 128).transpose(3, 0, 1, 2, 4)
    up = up.reshape(TILES, OWNERS, owned, TILE)
    down = gather(down_weight.astype(low), axis=0).reshape(OWNERS, TILES, 128, C).transpose(1, 0, 2, 3)
    vec = gather(vectors.astype(low), axis=1)
    tab = gather(bias_table.astype(low), axis=0)
    table_rows = tab.shape[0]
    count = TAB_ROWS // OWNERS
    vec = vec.reshape(12, OWNERS, owned).transpose(1, 0, 2)
    tab = tab[:TAB_ROWS].reshape(OWNERS, count, HEADS).transpose(0, 2, 1)
    small = jnp.concatenate([jnp.pad(vec, ((0, 0), (0, 4), (0, 128 - owned))), jnp.pad(tab, ((0, 0), (0, 8), (0, 128 - count)))], 1)
    out, grad, gq, gp, gu, gd, gs = local_step(tokens, out_grad, window_count, small, wq, wp, up, down)
    gq = gq.astype(full).transpose(2, 3, 1, 0, 4).reshape(C, 3 * C)
    gu = gu.astype(full).reshape(TILES, C, OWNERS, 128).transpose(1, 2, 0, 3).reshape(C, MLP)
    gd = gd.astype(full).transpose(1, 0, 3, 2).reshape(MLP, C)
    gv = gs[:, :12, :owned].transpose(1, 0, 2).reshape(12, C)
    gb = gs[:, 16:40, :count].transpose(0, 2, 1).reshape(TAB_ROWS, HEADS)
    gb = jnp.pad(gb, ((0, table_rows - TAB_ROWS), (0, 0)))
    totals = lax.psum(
        (scatter(gq, scatter_dimension=0), scatter(gp.astype(full).reshape(C, C), scatter_dimension=0), scatter(gu, scatter_dimension=0),
         scatter(gd, scatter_dimension=0), scatter(gv, scatter_dimension=1), scatter(gb, scatter_dimension=0)), "rep")
    states = (
        (qkv_weight, qkv_first, qkv_second), (output_weight, output_first, output_second), (up_weight, up_first, up_second),
        (down_weight, down_first, down_second), (vectors, vector_first, vector_second), (bias_table, table_first, table_second))
    results = [out, grad]
    for i, (state, total, rate) in enumerate(zip(states, totals, step_rates)):
        new = adamw(*state, total, rate)
        results += [*new, new[0].astype(low)] if i < 4 else [*new]
    return tuple(results)


def solution(mesh):
    wins = P(("rep", "shard"), None, None)
    rows = P("shard", None)
    cols = P(None, "shard")
    fits = mesh.shape["rep"] == REPS and mesh.shape["shard"] == OWNERS
    return jax.shard_map(
        shards if fits else shards_general,
        mesh=mesh,
        in_specs=(wins, wins, P(("rep", "shard"))) + (rows,) * 12 + (cols,) * 3 + (rows,) * 3,
        out_specs=(wins, wins) + (rows,) * 16 + (cols,) * 3 + (rows,) * 3,
        check_vma=False,
    )
```

```python
import functools
import math

import jax
import jax.numpy as jnp
import numpy as np
from jax import lax
from jax.experimental import pallas as pl
from jax.experimental.pallas import tpu as pltpu
from jax.sharding import PartitionSpec as P

C = 768
HEADS = 24
MLP = 3072
WIN = 12
STEP = 5
HEAD_DIM = 32
SPAN = 2 * WIN - 1
TOK = WIN * WIN
TAB_ROWS = 536
ROWS = 1024
GROUPS = 3
GCOLS = 256
GHEADS = 8
PACK = GHEADS * TOK
TAB_LANES = 640
TILES = 3
TILE = MLP // TILES
SUB = 512
LINE = 384
MIB = 1 << 20

beta_one = 0.5
beta_two = 0.6
weight_decay = 0.05
adam_eps = 1e-08
norm_eps = 1e-05
step_rates = (0.04, 0.15, 0.04, 0.02, 0.2, 1.0)
low = jnp.bfloat16
full = jnp.float32
NT = (((1,), (1,)), ((), ()))


def dot(a, b):
    return jnp.dot(a, b, preferred_element_type=full)


def dot_nt(a, b):
    return lax.dot_general(a, b, NT, preferred_element_type=full)


def line_matrix():
    out = np.zeros((TAB_LANES, LINE), np.float32)
    col = np.arange(SPAN * WIN)
    out[(col // WIN) * SPAN + col % WIN + WIN - 1, col] = 1.0
    return out


def head_masks():
    lane = np.arange(GCOLS) // HEAD_DIM
    one = (lane[None, :] == np.arange(GHEADS)[:, None]).astype(np.float32)
    return np.broadcast_to(one[:, None, :], (GHEADS, 16, GCOLS))


def norm_parts(z):
    mean = jnp.sum(z, -1, keepdims=True) * (1.0 / C)
    center = z - mean
    spread = jnp.sum(center * center, -1, keepdims=True) * (1.0 / C)
    scale = lax.rsqrt(spread + norm_eps)
    return center * scale, scale


def norm_back(xhat, scale, dn, gain):
    g = dn * gain
    m1 = jnp.sum(g, -1, keepdims=True) * (1.0 / C)
    m2 = jnp.sum(g * xhat, -1, keepdims=True) * (1.0 / C)
    return scale * (g - m1 - xhat * m2)


def diag(x, mask_ref):
    head = x[0:128].reshape(8, 16, GCOLS)
    tail = x[128:144]
    parts = []
    for h in range(GHEADS):
        parts.append((head * mask_ref[h][None]).reshape(128, GCOLS))
    for h in range(GHEADS):
        parts.append(tail * mask_ref[h])
    return jnp.concatenate(parts, 0)


def undiag(xt, m, mask_ref):
    main = []
    for h in range(0, GHEADS, 2):
        r = dot(xt[h * HEAD_DIM : (h + 2) * HEAD_DIM], m[:, h * 128 : (h + 2) * 128])
        main.append(r[0:HEAD_DIM, 0:128])
        main.append(r[HEAD_DIM : 2 * HEAD_DIM, 128:256])
    main = jnp.concatenate(main, 0)
    rest = dot(xt, m[:, GHEADS * 128 :])
    rest_t = rest.T.reshape(GHEADS, 16, GCOLS)
    keep = mask_ref[...].astype(full)
    return jnp.concatenate([main.T, jnp.sum(rest_t * keep, 0)], 0)


def flat(x):
    return x.reshape(x.shape[0] * x.shape[1], x.shape[2])


def blocks(x, owners):
    return x.reshape(owners, x.shape[0] // owners, x.shape[1])


def hidden_place(t, s):
    at = (MLP // GHEADS) * s + 128 * t
    return 8 + at // C, at % C


def unpack_small(small_ref, vec_ref):
    owners = small_ref.shape[0]
    width = C // owners
    count = TAB_ROWS // owners
    vec = jnp.zeros((16, C), full)
    tab = jnp.zeros((HEADS, TAB_LANES), full)
    lane = lax.broadcasted_iota(jnp.int32, (16, 128), 1)
    lane_tab = lax.broadcasted_iota(jnp.int32, (HEADS, 128), 1)
    for s in range(owners):
        piece = small_ref[s].astype(full)
        part = jnp.where(lane < width, piece[0:16], 0.0)
        part = jnp.concatenate([part, jnp.zeros((16, C - 128), full)], 1)
        vec = vec + (pltpu.roll(part, width * s, 1) if s else part)
        part = jnp.where(lane_tab < count, piece[16 : 16 + HEADS], 0.0)
        part = jnp.concatenate([part, jnp.zeros((HEADS, TAB_LANES - 128), full)], 1)
        tab = tab + (pltpu.roll(part, count * s, 1) if s else part)
    vec_ref[...] = vec
    return tab


def pack_small(vec, tab, out_ref):
    owners = out_ref.shape[0]
    width = C // owners
    count = TAB_ROWS // owners
    for s in range(owners):
        out_ref[s, 0:16, :] = (pltpu.roll(vec, C - width * s, 1) if s else vec)[:, 0:128]
        out_ref[s, 16:40, :] = (pltpu.roll(tab, TAB_LANES - count * s, 1) if s else tab)[:, 0:128]


def spread_table(tab, line_ref, tmp_ref):
    def column(cj, carry):
        shifted = pltpu.roll(tab, cj, 1)
        line = dot(shifted.astype(low), line_ref[...])
        for rj in range(WIN):
            cut = (WIN - 1 - rj) * WIN
            part = pltpu.roll(line, LINE - cut, 1) if cut else line
            row = pl.multiple_of((rj * WIN + cj) * HEADS, 8)
            tmp_ref[0, pl.ds(row, HEADS), :] = part[:, 0:128]
            tmp_ref[1, pl.ds(row, HEADS), :] = part[:, 128:256]
        return carry

    lax.fori_loop(0, WIN, column, 0)


def place_bias(tmp_ref, bias_ref):
    lane = lax.broadcasted_iota(jnp.int32, (TOK, 128), 1)
    for g in range(GROUPS):
        rest = jnp.zeros((TOK, 128), full)
        for h in range(GHEADS):
            at = pl.ds(g * GHEADS + h, TOK, stride=HEADS)
            bias_ref[g, :, h * 128 : (h + 1) * 128] = tmp_ref[0, at, :]
            piece = tmp_ref[1, at, :]
            piece = pltpu.roll(piece, 16 * h, 1) if h else piece
            rest = jnp.where((lane >= 16 * h) & (lane < 16 * h + 16), piece, rest)
        bias_ref[g, :, GHEADS * 128 :] = rest


def table_grad(line_ref, tmp_ref, bias_ref):
    lane = lax.broadcasted_iota(jnp.int32, (TOK, 128), 1)
    for g in range(GROUPS):
        rest = bias_ref[g, :, GHEADS * 128 :]
        for h in range(GHEADS):
            at = pl.ds(g * GHEADS + h, TOK, stride=HEADS)
            tmp_ref[0, at, :] = bias_ref[g, :, h * 128 : (h + 1) * 128]
            piece = pltpu.roll(rest, 128 - 16 * h, 1) if h else rest
            tmp_ref[1, at, :] = jnp.where(lane < 16, piece, 0.0)

    def column(cj, total):
        line = jnp.zeros((HEADS, LINE), full)
        for rj in range(WIN):
            cut = (WIN - 1 - rj) * WIN
            row = pl.multiple_of((rj * WIN + cj) * HEADS, 8)
            part = jnp.concatenate([tmp_ref[0, pl.ds(row, HEADS), :], tmp_ref[1, pl.ds(row, HEADS), :], jnp.zeros((HEADS, 128), full)], 1)
            line = line + (pltpu.roll(part, cut, 1) if cut else part)
        high = line.astype(low)
        rest = (line - high.astype(full)).astype(low)
        spread = dot_nt(high, line_ref[...]) + dot_nt(rest, line_ref[...])
        return total + pltpu.roll(spread, TAB_LANES - cj, 1)

    return lax.fori_loop(0, WIN, column, jnp.zeros((HEADS, TAB_LANES), full))


def transpose_rows(src_ref, dst_ref):
    def block(i, carry):
        at = pl.multiple_of(i * 128, 128)
        dst_ref[0 : src_ref.shape[1], pl.ds(at, 128)] = src_ref[pl.ds(at, 128), :].T
        return carry

    lax.fori_loop(0, ROWS // 128, block, 0)


def window_rows(w):
    return slice(w * TOK, (w + 1) * TOK) if isinstance(w, int) else pl.ds(pl.multiple_of(w * TOK, 16), TOK)


def zero_tail(ref, windows):
    at = windows * TOK
    ref[at:ROWS, :] = jnp.zeros((ROWS - at, ref.shape[1]), ref.dtype)


def half_diag(x, half, mask_ref):
    lanes = slice(half * 128, (half + 1) * 128)
    part = x[0:128, lanes].reshape(8, 16, 128)
    heads = range(half * GHEADS // 2, (half + 1) * GHEADS // 2)
    return jnp.concatenate([(part * mask_ref[h, :, lanes][None]).reshape(128, 128) for h in heads], 0)


def rest_diag(x, mask_ref):
    return jnp.concatenate([x[128:144] * mask_ref[h] for h in range(GHEADS)], 0)


def split_diag(x, mask_ref):
    return half_diag(x, 0, mask_ref), half_diag(x, 1, mask_ref), rest_diag(x, mask_ref)


def against_heads(x, split):
    first, second, rest = split
    return jnp.concatenate([dot_nt(x[:, 0:128], first), dot_nt(x[:, 128:256], second), dot_nt(x, rest)], 1)


def over_queries(m, split):
    first, second, rest = split
    return jnp.concatenate([dot(m[:, 0:512], first), dot(m[:, 512:1024], second)], 1) + dot(m[:, 1024:], rest)


def attention_forward(windows, x_ref, small_ref, line_ref, mask_ref, wq_ref, wp_ref,
                      qkv_ref, pt_ref, o_ref, x1_ref, n1t_ref, vec_ref, n1_ref, bias_ref, tmp_ref):
    tab = unpack_small(small_ref, vec_ref)
    spread_table(tab, line_ref, tmp_ref)
    place_bias(tmp_ref, bias_ref)
    zero_tail(n1_ref, windows)
    zero_tail(o_ref, windows)

    def first_norm(w, carry):
        xhat, _ = norm_parts(x_ref[window_rows(w), :].astype(full))
        n1_ref[window_rows(w), :] = (xhat * vec_ref[0:1, :] + vec_ref[1:2, :]).astype(low)
        return carry

    lax.fori_loop(0, windows, first_norm, 0)
    transpose_rows(n1_ref, n1t_ref)

    def group(g, carry):
        cols = pl.ds(pl.multiple_of(g * GCOLS, GCOLS), GCOLS)
        n1 = n1_ref[...]
        qkv_ref[g] = ((dot(n1, flat(wq_ref[g, 0])) + vec_ref[2:3, cols]) * (HEAD_DIM**-0.5)).astype(low)
        qkv_ref[GROUPS + g] = dot(n1, flat(wq_ref[g, 1])).astype(low)
        qkv_ref[2 * GROUPS + g] = (dot(n1, flat(wq_ref[g, 2])) + vec_ref[3:4, cols]).astype(low)

        def window(w, inner):
            rows = window_rows(w)
            q = qkv_ref[g, rows, :]
            k = qkv_ref[GROUPS + g, rows, :]
            v = qkv_ref[2 * GROUPS + g, rows, :]
            s = dot_nt(k, diag(q, mask_ref)) + bias_ref[g]
            e = jnp.exp(s - jnp.max(s, 0, keepdims=True))
            p = (e * (1.0 / jnp.sum(e, 0, keepdims=True))).astype(low)
            pt_ref[g, w] = p
            o_ref[rows, cols] = undiag(v.T, p, mask_ref).astype(low)
            return inner

        lax.fori_loop(0, windows, window, 0)
        return carry

    lax.fori_loop(0, GROUPS, group, 0)

    def output(w, carry):
        rows = window_rows(w)
        branch = dot(o_ref[rows, :], flat(wp_ref[...])) + vec_ref[4:5, :]
        x1_ref[rows, :] = x_ref[rows, :].astype(full) + branch
        return carry

    lax.fori_loop(0, windows, output, 0)


def gelu_both(h):
    c = math.sqrt(2.0 / math.pi)
    square = h * h
    t = jnp.tanh(h * (c + (c * 0.044715) * square))
    half = 0.5 + 0.5 * t
    act = h * half
    return act, half + act * (1.0 - half) * (2.0 * c + (6.0 * c * 0.044715) * square)


def feed_forward(windows, x1_ref, dy_ref, live_ref, vec_ref, up_ref, down_ref, wp_ref, o_ref,
                 out_ref, dx1_ref, do_ref, gup_ref, gdown_ref, gout_ref, sums_ref,
                 n2_ref, n2t_ref, dy2_ref, dyt_ref, y_ref, dn_ref, bu_ref, bsum_ref):
    zero_tail(n2_ref, windows)
    zero_tail(dy2_ref, windows)

    def second_norm(w, carry):
        rows = window_rows(w)
        xhat, _ = norm_parts(x1_ref[rows, :])
        n2_ref[rows, :] = (xhat * vec_ref[5:6, :] + vec_ref[6:7, :]).astype(low)
        dy2_ref[rows, :] = (dy_ref[rows, :].astype(full) * live_ref[w]).astype(low)
        return carry

    lax.fori_loop(0, windows, second_norm, 0)
    transpose_rows(n2_ref, n2t_ref)
    transpose_rows(dy2_ref, dyt_ref)
    y_ref[...] = jnp.zeros_like(y_ref)
    dn_ref[...] = jnp.zeros_like(dn_ref)
    owners = gup_ref.shape[1]
    for t in range(TILES):
        for s in range(TILE // 128):
            row, at = hidden_place(t, s)
            bu_ref[t, :, s * 128 : (s + 1) * 128] = vec_ref[row : row + 1, at : at + 128]

    def step(t, carry):
        for part in range(TILE // SUB):
            cols = slice(part * SUB, (part + 1) * SUB)
            up = flat(up_ref[t, :, :, cols])
            down = flat(down_ref[t, part * SUB // 128 : (part + 1) * SUB // 128])
            h = dot(n2_ref[...], up) + bu_ref[t, :, cols]
            da = dot_nt(dy2_ref[...], down)
            act, slope = gelu_both(h)
            a = act.astype(low)
            dh = (da * slope).astype(low)
            bsum_ref[t, :, cols] = jnp.sum(dh.astype(full), 0, keepdims=True)
            y_ref[...] += dot(a, down)
            dn_ref[...] += dot_nt(dh, up)
            gd = dot(dyt_ref[...], a).astype(low)
            for b in range(SUB // 128):
                gdown_ref[t, part * SUB // 128 + b] = gd[:, b * 128 : (b + 1) * 128]
            gup_ref[t, :, :, cols] = blocks(dot(n2t_ref[...], dh).astype(low), owners)
        return carry

    lax.fori_loop(0, TILES, step, 0)
    sums_ref[...] = jnp.zeros_like(sums_ref)
    for t in range(TILES):
        for s in range(TILE // 128):
            row, at = hidden_place(t, s)
            sums_ref[row : row + 1, at : at + 128] = bsum_ref[t, :, s * 128 : (s + 1) * 128]
    zero_tail(dx1_ref, windows)

    def finish(w, carry):
        rows = window_rows(w)
        x1 = x1_ref[rows, :]
        out_ref[rows, :] = ((x1 + y_ref[rows, :] + vec_ref[7:8, :]) * live_ref[w]).astype(low)
        xhat, scale = norm_parts(x1)
        dn = dn_ref[rows, :]
        dy = dy2_ref[rows, :].astype(full)
        dx1 = dy + norm_back(xhat, scale, dn, vec_ref[5:6, :])
        dx1_ref[rows, :] = dx1
        dr = dx1.astype(low)
        n2_ref[rows, :] = dr
        do_ref[rows, :] = dot_nt(dr, flat(wp_ref[...])).astype(low)
        sums_ref[4:5, :] += jnp.sum(dr.astype(full), 0, keepdims=True)
        sums_ref[5:6, :] += jnp.sum(dn * xhat, 0, keepdims=True)
        sums_ref[6:7, :] += jnp.sum(dn, 0, keepdims=True)
        sums_ref[7:8, :] += jnp.sum(dy, 0, keepdims=True)
        return carry

    lax.fori_loop(0, windows, finish, 0)
    transpose_rows(o_ref, dyt_ref)
    for g in range(GROUPS):
        at = pl.ds(g * GCOLS, GCOLS)
        gout_ref[:, :, at] = blocks(dot(dyt_ref[...], n2_ref[:, at]).astype(low), gout_ref.shape[0])


def attention_backward(windows, x_ref, vec_ref, line_ref, mask_ref, wq_ref, qkv_ref, pt_ref, do_ref, dx1_ref, n1t_ref, sums_in_ref,
                       gq_ref, gsmall_ref, grad_ref, sums_ref, bias_ref, tmp_ref, dproj_ref, dn_ref):
    bias_ref[...] = jnp.zeros_like(bias_ref)
    dn_ref[...] = jnp.zeros_like(dn_ref)
    sums_ref[...] = sums_in_ref[...]
    for part in range(3):
        dproj_ref[part, windows * TOK :, :] = jnp.zeros((ROWS - windows * TOK, GCOLS), low)

    def group(g, carry):
        cols = pl.ds(pl.multiple_of(g * GCOLS, GCOLS), GCOLS)

        def window(w, inner):
            rows = window_rows(w)
            q = qkv_ref[g, rows, :]
            k = qkv_ref[GROUPS + g, rows, :]
            v = qkv_ref[2 * GROUPS + g, rows, :]
            p = pt_ref[g, w]
            do = diag(do_ref[rows, cols], mask_ref)
            dp = dot_nt(v, do)
            dv = dot(p, do)
            pf = p.astype(full)
            ds = (pf * (dp - jnp.sum(pf * dp, 0, keepdims=True))).astype(low)
            bias_ref[g] += ds.astype(full)
            dk = dot(ds, diag(q, mask_ref))
            dq = undiag(k.T, ds, mask_ref) * (HEAD_DIM**-0.5)
            dq = dq.astype(low)
            dv = dv.astype(low)
            dproj_ref[0, rows, :] = dq
            dproj_ref[1, rows, :] = dk.astype(low)
            dproj_ref[2, rows, :] = dv
            sums_ref[2:3, cols] += jnp.sum(dq.astype(full), 0, keepdims=True)
            sums_ref[3:4, cols] += jnp.sum(dv.astype(full), 0, keepdims=True)
            return inner

        lax.fori_loop(0, windows, window, 0)
        for part in range(3):
            d = dproj_ref[part]
            gq_ref[g, part] = blocks(dot(n1t_ref[...], d).astype(low), gq_ref.shape[2])
            dn_ref[...] += dot_nt(d, flat(wq_ref[g, part]))
        return carry

    lax.fori_loop(0, GROUPS, group, 0)

    def finish(w, carry):
        rows = window_rows(w)
        xhat, scale = norm_parts(x_ref[rows, :].astype(full))
        dn = dn_ref[rows, :]
        grad_ref[rows, :] = dx1_ref[rows, :] + norm_back(xhat, scale, dn, vec_ref[0:1, :])
        sums_ref[0:1, :] += jnp.sum(dn * xhat, 0, keepdims=True)
        sums_ref[1:2, :] += jnp.sum(dn, 0, keepdims=True)
        return carry

    lax.fori_loop(0, windows, finish, 0)
    pack_small(sums_ref[...], table_grad(line_ref, tmp_ref, bias_ref), gsmall_ref)


MESH = pl.DeviceIdType.MESH
REPS = 4
OWNERS = 8
LINKS = OWNERS // 2


class Spot:
    def __init__(self):
        self.rep = lax.axis_index("rep")
        self.shard = lax.axis_index("shard")
        self.z = self.shard // 2
        self.core = self.shard % 2

    def sibling(self):
        return (self.rep, self.z * 2 + (1 - self.core))

    def along_z(self, step):
        return (self.rep, ((self.z + step) % LINKS) * 2 + self.core)

    def turned(self, axis):
        x, y = self.rep % 2, self.rep // 2
        return y * 2 + (1 - x) if axis == 0 else (1 - y) * 2 + x

    def beside(self, axis):
        return (self.turned(axis), self.shard)

    def across(self):
        return (REPS - 1 - self.rep, self.shard)


def greet(spot):
    barrier = pltpu.get_barrier_semaphore()
    peers = [(spot.rep, (spot.shard + i) % OWNERS) for i in range(1, OWNERS)]
    peers += [((spot.rep + i) % REPS, spot.shard) for i in range(1, REPS)]
    for peer in peers:
        pl.semaphore_signal(barrier, inc=1, device_id=peer, device_id_type=MESH)
    return barrier, len(peers)


def send(src, dst, send_sem, recv_sem, peer):
    pltpu.make_async_remote_copy(src_ref=src, dst_ref=dst, send_sem=send_sem, recv_sem=recv_sem, device_id=peer, device_id_type=MESH).start()


def await_bytes(ref, sem):
    pltpu.make_async_copy(ref, ref, sem).wait()


def quarter(ref, rep):
    rows, cols = ref.shape[-2:]
    lead = (slice(None),) * (len(ref.shape) - 2)
    top = pl.multiple_of((rep // 2) * (rows // 2), 16)
    left = pl.multiple_of((rep % 2) * (cols // 2), 128)
    return ref.at[lead + (pl.ds(top, rows // 2), pl.ds(left, cols // 2))]


def half(ref, rep, axis):
    rows, cols = ref.shape[-2:]
    lead = (slice(None),) * (len(ref.shape) - 2)
    if axis == 0:
        left = pl.multiple_of((rep % 2) * (cols // 2), 128)
        return ref.at[lead + (slice(None), pl.ds(left, cols // 2))]
    top = pl.multiple_of((rep // 2) * (rows // 2), 16)
    return ref.at[lead + (pl.ds(top, rows // 2), slice(None))]


class Gather:
    KINDS = (LINKS - 1, LINKS - 1, LINKS - 1, LINKS - 1, LINKS)
    SEMS = 2 * sum(KINDS)
    STAGES = ("start", "across", "relay", "beside", "finish")

    def __init__(self, spot, place, axis, sems, direct=False):
        self.spot, self.place, self.axis, self.sems, self.direct = spot, place, axis, sems, direct

    def sem(self, side, kind, i):
        return self.sems.at[side * (self.SEMS // 2) + sum(self.KINDS[:kind]) + i]

    def block(self, step):
        return self.place(((self.spot.z - step + LINKS) % LINKS) * 2 + self.spot.core)

    def other(self, step):
        return self.place(((self.spot.z - step + LINKS) % LINKS) * 2 + 1 - self.spot.core)

    def start(self):
        spot = self.spot
        mine = self.block(0)
        for i in range(1, LINKS):
            piece = quarter(mine, spot.rep)
            send(piece, piece, self.sem(0, 0, i - 1), self.sem(1, 0, i - 1), spot.along_z(i))
        send(mine, mine, self.sem(0, 4, 0), self.sem(1, 4, 0), spot.sibling())

    def across(self):
        spot = self.spot
        for i in range(1, LINKS):
            piece = quarter(self.block(i), spot.rep)
            await_bytes(piece, self.sem(1, 0, i - 1))
            for axis in (self.axis, 1 - self.axis):
                send(piece, piece, self.sem(0, 1 + axis, i - 1), self.sem(1, 1 + axis, i - 1), spot.beside(axis))
            if self.direct:
                send(piece, piece, self.sem(0, 3, i - 1), self.sem(1, 3, i - 1), spot.across())

    def relay(self):
        spot = self.spot
        if self.direct:
            return
        for i in range(1, LINKS):
            piece = quarter(self.block(i), spot.turned(self.axis))
            await_bytes(piece, self.sem(1, 1 + self.axis, i - 1))
            send(piece, piece, self.sem(0, 3, i - 1), self.sem(1, 3, i - 1), spot.beside(1 - self.axis))

    def beside(self):
        spot = self.spot
        for i in range(1, LINKS):
            block = self.block(i)
            piece = quarter(block, spot.rep)
            if self.direct:
                await_bytes(piece, self.sem(1, 1 + self.axis, i - 1))
            await_bytes(piece, self.sem(1, 2 - self.axis, i - 1))
            await_bytes(piece, self.sem(1, 3, i - 1))
            send(block, block, self.sem(0, 4, i), self.sem(1, 4, i), spot.sibling())

    def finish(self):
        for i in range(LINKS):
            await_bytes(self.other(i), self.sem(1, 4, i))

    def close(self):
        piece = quarter(self.block(0), self.spot.rep)
        for kind in range(4):
            for i in range(1, LINKS):
                await_bytes(piece, self.sem(0, kind, i - 1))
        for i in range(LINKS):
            await_bytes(self.block(i), self.sem(0, 4, i))


class Reduce:
    KINDS = (LINKS, 1, 1, LINKS - 1, REPS - 1)
    SEMS = 2 * sum(KINDS)
    STAGES = ("start", "first", "second", "along", "spread", "finish")

    def __init__(self, spot, place, out, core_sum, halves, quarters, links, axis, sems):
        self.spot, self.place, self.out, self.axis, self.sems = spot, place, out, axis, sems
        self.core_sum, self.halves, self.quarters, self.links = core_sum, halves, quarters, links

    def sem(self, side, kind, i):
        return self.sems.at[side * (self.SEMS // 2) + sum(self.KINDS[:kind]) + i]

    def start(self):
        spot = self.spot
        for z in range(LINKS):
            send(self.place(z * 2 + (1 - spot.core)), self.core_sum.at[z], self.sem(0, 0, z), self.sem(1, 0, z), spot.sibling())

    def first(self):
        spot = self.spot
        for z in range(LINKS):
            total = self.core_sum.at[z]
            await_bytes(total, self.sem(1, 0, z))
            total[...] = (total[...].astype(full) + self.place(z * 2 + spot.core)[...].astype(full)).astype(low)
        theirs = half(self.core_sum, spot.turned(self.axis), self.axis)
        send(theirs, self.halves, self.sem(0, 1, 0), self.sem(1, 1, 0), spot.beside(self.axis))

    def second(self):
        spot = self.spot
        await_bytes(self.halves, self.sem(1, 1, 0))
        mine = half(self.core_sum, spot.rep, self.axis)
        self.halves[...] = (self.halves[...].astype(full) + mine[...].astype(full)).astype(low)
        theirs = half(self.halves, spot.turned(1 - self.axis), 1 - self.axis)
        send(theirs, self.quarters, self.sem(0, 2, 0), self.sem(1, 2, 0), spot.beside(1 - self.axis))

    def along(self):
        spot = self.spot
        await_bytes(self.quarters, self.sem(1, 2, 0))
        mine = half(self.halves, spot.rep, 1 - self.axis)
        self.quarters[...] = (self.quarters[...].astype(full) + mine[...].astype(full)).astype(low)
        for i in range(1, LINKS):
            send(self.quarters.at[(spot.z + i) % LINKS], self.links.at[i - 1], self.sem(0, 3, i - 1), self.sem(1, 3, i - 1), spot.along_z(i))

    def spread(self):
        spot = self.spot
        total = self.quarters[spot.z].astype(full)
        for i in range(1, LINKS):
            await_bytes(self.links.at[i - 1], self.sem(1, 3, i - 1))
            total = total + self.links[i - 1].astype(full)
        mine = quarter(self.out, spot.rep)
        mine[...] = total.astype(low)
        for j in range(1, REPS):
            send(mine, mine, self.sem(0, 4, j - 1), self.sem(1, 4, j - 1), ((spot.rep + j) % REPS, spot.shard))

    def finish(self):
        for j in range(1, REPS):
            await_bytes(quarter(self.out, (self.spot.rep - j + REPS) % REPS), self.sem(1, 4, j - 1))

    def close(self):
        for z in range(LINKS):
            await_bytes(self.core_sum.at[z], self.sem(0, 0, z))
        await_bytes(self.halves, self.sem(0, 1, 0))
        await_bytes(self.quarters, self.sem(0, 2, 0))
        for i in range(1, LINKS):
            await_bytes(self.links.at[i - 1], self.sem(0, 3, i - 1))
        for j in range(1, REPS):
            await_bytes(quarter(self.out, self.spot.rep), self.sem(0, 4, j - 1))


class ReduceDirect(Reduce):
    KINDS = (LINKS, REPS - 1, 0, LINKS - 1, REPS - 1)
    SEMS = 2 * sum(KINDS)

    def peers(self):
        spot = self.spot
        return (spot.turned(0), spot.turned(1), REPS - 1 - spot.rep)

    def first(self):
        spot = self.spot
        for z in range(LINKS):
            total = self.core_sum.at[z]
            await_bytes(total, self.sem(1, 0, z))
            total[...] = (total[...].astype(full) + self.place(z * 2 + spot.core)[...].astype(full)).astype(low)
        for j, rep in enumerate(self.peers()):
            send(quarter(self.core_sum, rep), self.halves.at[j], self.sem(0, 1, j), self.sem(1, 1, j), (rep, spot.shard))

    def second(self):
        pass

    def along(self):
        spot = self.spot
        total = quarter(self.core_sum, spot.rep)[...].astype(full)
        for j in range(REPS - 1):
            await_bytes(self.halves.at[j], self.sem(1, 1, j))
            total = total + self.halves[j].astype(full)
        self.quarters[...] = total.astype(low)
        for i in range(1, LINKS):
            send(self.quarters.at[(spot.z + i) % LINKS], self.links.at[i - 1], self.sem(0, 3, i - 1), self.sem(1, 3, i - 1), spot.along_z(i))

    def close(self):
        for z in range(LINKS):
            await_bytes(self.core_sum.at[z], self.sem(0, 0, z))
        for j in range(REPS - 1):
            await_bytes(self.halves.at[j], self.sem(0, 1, j))
        for i in range(1, LINKS):
            await_bytes(self.links.at[i - 1], self.sem(0, 3, i - 1))
        for j in range(1, REPS):
            await_bytes(quarter(self.out, self.spot.rep), self.sem(0, 4, j - 1))


class ReduceSmall:
    KINDS = (LINKS, LINKS - 1, REPS - 1)
    SEMS = 2 * sum(KINDS)
    STAGES = ("start", "first", "second", "along")

    def __init__(self, spot, terms, out, core_sum, links, parts, sems):
        self.spot, self.terms, self.out, self.core_sum, self.links, self.parts, self.sems = spot, terms, out, core_sum, links, parts, sems

    sem = Reduce.sem

    def start(self):
        spot = self.spot
        for z in range(LINKS):
            send(self.terms.at[z * 2 + (1 - spot.core)], self.core_sum.at[z], self.sem(0, 0, z), self.sem(1, 0, z), spot.sibling())

    def first(self):
        spot = self.spot
        for z in range(LINKS):
            await_bytes(self.core_sum.at[z], self.sem(1, 0, z))
            self.core_sum[z] = self.core_sum[z] + self.terms[z * 2 + spot.core]
        for i in range(1, LINKS):
            send(self.core_sum.at[(spot.z + i) % LINKS], self.links.at[i - 1], self.sem(0, 1, i - 1), self.sem(1, 1, i - 1), spot.along_z(i))

    def second(self):
        spot = self.spot
        total = self.core_sum[spot.z]
        for i in range(1, LINKS):
            await_bytes(self.links.at[i - 1], self.sem(1, 1, i - 1))
            total = total + self.links[i - 1]
        self.parts[spot.rep] = total
        mine = self.parts.at[spot.rep]
        for j in range(1, REPS):
            send(mine, mine, self.sem(0, 2, j - 1), self.sem(1, 2, j - 1), ((spot.rep + j) % REPS, spot.shard))

    def along(self):
        for j in range(1, REPS):
            await_bytes(self.parts.at[(self.spot.rep - j + REPS) % REPS], self.sem(1, 2, j - 1))
        total = self.parts[0]
        for j in range(1, REPS):
            total = total + self.parts[j]
        self.out[...] = total

    def close(self):
        for z in range(LINKS):
            await_bytes(self.core_sum.at[z], self.sem(0, 0, z))
        for i in range(1, LINKS):
            await_bytes(self.links.at[i - 1], self.sem(0, 1, i - 1))
        for j in range(1, REPS):
            await_bytes(self.parts.at[self.spot.rep], self.sem(0, 2, j - 1))


OWNED = C // OWNERS
SLOTS = TILES + 1
GATHERS = 2 * TILES + 1 + GROUPS
REDUCES = 2 * TILES + 1 + (GROUPS - 1) + 3
W_Q0, W_Q1, W_Q2, W_P, W_U0, W_D0, W_U1, W_D1, W_U2, W_D2 = W_ALL = range(10)
G_D0, G_U0, G_D1, G_U1, G_D2, G_U2, G_P, G_Q0, G_Q1, G_Q2, G_K2, G_V2, G_S = G_ALL = range(10, 23)
W_Q, W_U, W_D = (W_Q0, W_Q1, W_Q2), (W_U0, W_U1, W_U2), (W_D0, W_D1, W_D2)
G_D, G_U, G_Q, G_LAST = (G_D0, G_D1, G_D2), (G_U0, G_U1, G_U2), (G_Q0, G_Q1), (G_Q2, G_K2, G_V2)
START, ACROSS, RELAY, BESIDE, ARRIVED = range(5)
FIRST, SECOND, ALONG, SPREAD, SUMMED = range(1, 6)
BEFORE = {
    2: ((W_P, START),),
    3: ((W_Q0, ACROSS), (W_Q2, START),),
    4: ((W_Q1, ACROSS),),
    5: ((W_P, ACROSS), (W_D0, START),),
}
FORWARD = {
    0: ((W_Q0, RELAY), (W_Q1, RELAY), (W_U0, START),),
    2: ((W_Q2, ACROSS),),
    3: ((W_U1, START),),
    4: ((W_Q0, BESIDE),),
    5: ((W_Q1, BESIDE), (W_Q2, RELAY), (W_P, RELAY),),
    7: ((W_U0, ACROSS),),
    8: ((W_P, BESIDE),),
    10: ((W_Q2, BESIDE), (W_D1, START),),
    12: ((W_D0, ACROSS),),
    14: ((W_U0, RELAY), (W_U1, ACROSS), (W_U2, START),),
    16: ((W_D0, RELAY),),
    17: ((W_D1, ACROSS), (W_D2, START),),
}
MIDDLE = {
    1: ((W_U0, BESIDE), (W_U2, ACROSS),),
    2: ((W_D0, BESIDE), (W_U1, RELAY),),
}
TILE_STEP = {
    0: ((W_D1, RELAY), (W_U2, RELAY),),
    1: ((W_U1, BESIDE), (W_D1, BESIDE), (W_D2, ACROSS),),
    2: ((W_U2, BESIDE), (W_D2, RELAY),),
    3: ((W_D2, BESIDE),),
    4: ((G_D0, FIRST), (G_U0, FIRST),),
    5: ((G_D1, FIRST), (G_U1, FIRST),),
}
AFTER_TILES = {
    1: ((G_D0, SECOND),),
    2: ((G_U0, SECOND),),
    3: ((G_D2, FIRST), (G_U2, FIRST),),
}
BACKWARD = {
    1: ((G_D1, SECOND),),
    4: ((G_D0, ALONG), (G_U0, ALONG),),
    5: ((G_U1, SECOND),),
    7: ((G_P, FIRST),),
    9: ((G_D2, SECOND),),
    10: ((G_D1, ALONG), (G_Q0, FIRST),),
    11: ((G_U1, ALONG), (G_U2, SECOND),),
    14: ((G_D0, SPREAD), (G_D1, SPREAD),),
    15: ((G_U0, SPREAD), (G_U1, SPREAD), (G_D2, ALONG),),
    16: ((G_Q1, FIRST),),
    17: ((G_U2, ALONG),),
    18: ((G_P, SECOND),),
}
LAST_STEPS = {
    0: ((G_D1, SUMMED), (G_U1, SUMMED),),
    1: ((G_K2, FIRST),),
    2: ((G_V2, FIRST),),
    3: ((G_P, ALONG), (G_Q0, SECOND), (G_V2, SECOND),),
}


def chunk_shapes():
    out = []
    for _ in range(TILES):
        out += [(128, C), (OWNED, TILE)]
    return out + [(OWNED, C)] + [(3, OWNED, GCOLS)] * (GROUPS - 1) + [(OWNED, GCOLS)] * 3


def reduce_scratch():
    out = []
    for i, dims in enumerate(chunk_shapes()):
        *lead, rows, cols = dims
        near = (rows, cols // 2) if i % 2 == 0 else (rows // 2, cols)
        near = (LINKS, *lead, *near) if i < REDUCES - 3 else (REPS - 1, LINKS, *lead, rows // 2, cols // 2)
        out.append(pltpu.VMEM((LINKS, *dims), low))
        out.append(pltpu.VMEM(near, low))
        out.append(pltpu.VMEM((LINKS, *lead, rows // 2, cols // 2), low))
        out.append(pltpu.VMEM((LINKS - 1, *lead, rows // 2, cols // 2), low))
    out += [pltpu.VMEM((LINKS, 40, 128), full), pltpu.VMEM((LINKS - 1, 40, 128), full), pltpu.VMEM((REPS, 40, 128), full)]
    return out


def layer_kernel(windows, x_hbm, dy_hbm, count_ref, q32, p32, u32, d32, vec_in, tab_in, line_ref, mask_ref,
                 out_hbm, grad_hbm, gq_out, gp_out, gu_out, gd_out, gs_out, qkv_hbm, pt_hbm, n1t_hbm, *scratch):
    wq, wp, up, down, small, o_ref, x1_ref, vec_ref, sums_ref, terms_ref = scratch[:10]
    gather_sems, reduce_sems, small_sems, small_reduce_sems, local = scratch[-5:]
    reduce_refs = scratch[10:-5]
    spot = Spot()
    rows_all = windows * TOK

    def live(w):
        return (w < count_ref[0]).astype(full)

    mine = spot.shard
    V = pltpu.VMEM

    jobs = {}
    places = [(W_Q[g], lambda s, g=g: wq.at[g, :, s]) for g in range(GROUPS)] + [(W_P, lambda s: wp.at[s])]
    for t in range(TILES):
        places += [(W_U[t], lambda s, t=t: up.at[t, s]), (W_D[t], lambda s, t=t: down.at[t, s])]
    for i, (name, place) in enumerate(places):
        jobs[name] = Gather(spot, place, i % 2, gather_sems.at[i], direct=name == W_Q0)
    places = []
    for t in range(TILES):
        slot = (t + SLOTS - 1) % SLOTS
        places.append((G_D[t], lambda s, slot=slot: down.at[slot, s], gd_out.at[t]))
        places.append((G_U[t], lambda s, slot=slot: up.at[slot, s], gu_out.at[t]))
    places.append((G_P, lambda s: wp.at[s], gp_out))
    for g in range(GROUPS - 1):
        places.append((G_Q[g], lambda s, g=g: wq.at[g, :, s], gq_out.at[g]))
    for part in range(3):
        places.append((G_LAST[part], lambda s, part=part: wq.at[GROUPS - 1, part, s], gq_out.at[GROUPS - 1, part]))
    for i, (name, place, out) in enumerate(places):
        kind = ReduceDirect if name in G_LAST else Reduce
        jobs[name] = kind(spot, place, out, *reduce_refs[4 * i : 4 * i + 4], i % 2, reduce_sems.at[i])
    jobs[G_S] = ReduceSmall(spot, terms_ref, gs_out, *reduce_refs[-3:], small_reduce_sems)

    done = {}

    def run(name, upto):
        for stage in range(done.get(name, 0), upto + 1):
            getattr(jobs[name], jobs[name].STAGES[stage])()
        done[name] = max(done.get(name, 0), upto + 1)

    def hook(table, place):
        for item in table.get(place, ()):
            run(*item)

    def hook_window(table, g, w):
        for at in range(windows):
            place = g * windows + at
            if place in table:

                @pl.when(w == at)
                def _(place=place):
                    hook(table, place)

    barrier, peers = greet(spot)

    def cast(q_v, p_v, u_v, d_v):
        loads = [pltpu.make_async_copy(a, b, local.at[i]) for i, (a, b) in enumerate(((q32, q_v), (p32, p_v), (u32, u_v), (d32, d_v)))]
        for load in loads:
            load.start()
        small[mine] = jnp.zeros((48, 128), low)
        pad = jnp.zeros((16, 128), full)
        vec_ref[:, 0:128] = pad
        vec_ref[0:12, 0:OWNED] = vec_in[...]
        small[mine, 0:16, :] = vec_ref[:, 0:128].astype(low)
        x1_ref[0:32, 0:128] = jnp.zeros((32, 128), full)
        x1_ref[0:HEADS, 0 : tab_in.shape[1]] = tab_in[...]
        small[mine, 16:48, :] = x1_ref[0:32, 0:128].astype(low)
        loads[0].wait()
        for g in range(GROUPS):
            for part in range(3):
                wq[g, part, mine] = q_v[:, part * C + g * GCOLS : part * C + (g + 1) * GCOLS].astype(low)
        pl.semaphore_wait(barrier, peers)
        for i in range(1, OWNERS):
            send(small.at[mine], small.at[mine], small_sems.at[i], small_sems.at[OWNERS + i], (spot.rep, (mine + i) % OWNERS))
        run(W_Q0, START)
        run(W_Q1, START)
        loads[1].wait()
        wp[mine] = p_v[...].astype(low)
        loads[2].wait()
        loads[3].wait()
        for t in range(TILES):
            for s in range(OWNERS):
                src = (MLP // OWNERS) * s + 128 * t
                up[t, mine, :, s * 128 : (s + 1) * 128] = u_v[:, src : src + 128].astype(low)
            down[t, mine] = d_v[t * 128 : (t + 1) * 128, :].astype(low)

    pl.run_scoped(cast, V((OWNED, 3 * C), full), V((OWNED, C), full), V((OWNED, MLP), full), V((TILES * 128, C), full))

    def forward(dy_ref, dyt_ref, x_ref, n1_ref, n1t_ref, qkv_ref, pt_ref, bias_ref):
        load = pltpu.make_async_copy(x_hbm, x_ref, local.at[0])
        load.start()
        load_dy = pltpu.make_async_copy(dy_hbm, dy_ref.at[0:rows_all], local.at[2])
        load_dy.start()
        zero_tail(n1_ref, windows)
        zero_tail(dy_ref, windows)
        zero_tail(o_ref, windows)
        for i in range(1, OWNERS):
            await_bytes(small.at[(mine - i + OWNERS) % OWNERS], small_sems.at[OWNERS + i])
        tab = unpack_small(small, vec_ref)
        hook(BEFORE, 0)
        load.wait()
        hook(BEFORE, 1)

        def first_norm(w, carry):
            xhat, _ = norm_parts(x_ref[window_rows(w), :].astype(full))
            n1_ref[window_rows(w), :] = (xhat * vec_ref[0:1, :] + vec_ref[1:2, :]).astype(low)
            return carry

        lax.fori_loop(0, windows, first_norm, 0)
        hook(BEFORE, 2)
        transpose_rows(n1_ref, n1t_ref)
        save = pltpu.make_async_copy(n1t_ref, n1t_hbm, local.at[1])
        save.start()
        hook(BEFORE, 3)
        load_dy.wait()

        def keep_live(w, carry):
            dy_ref[window_rows(w), :] = (dy_ref[window_rows(w), :].astype(full) * live(w)).astype(low)
            return carry

        lax.fori_loop(0, windows, keep_live, 0)
        transpose_rows(dy_ref, dyt_ref)
        hook(BEFORE, 4)

        def bias(tmp_ref):
            spread_table(tab, line_ref, tmp_ref)
            hook(BEFORE, 5)
            place_bias(tmp_ref, bias_ref)

        pl.run_scoped(bias, V((2, TOK * HEADS, 128), full))
        for g in range(GROUPS):
            cols = slice(g * GCOLS, (g + 1) * GCOLS)
            held = qkv_ref.at[g % 2]
            if g >= 2:
                pltpu.make_async_copy(held, qkv_hbm.at[g - 2], local.at[2 + g % 2]).wait()
            run(W_Q[g], ARRIVED)
            n1 = n1_ref[...]
            held[0] = ((dot(n1, flat(wq[g, 0])) + vec_ref[2:3, cols]) * (HEAD_DIM**-0.5)).astype(low)
            held[1] = dot(n1, flat(wq[g, 1])).astype(low)
            held[2] = (dot(n1, flat(wq[g, 2])) + vec_ref[3:4, cols]).astype(low)
            pltpu.make_async_copy(held, qkv_hbm.at[g], local.at[2 + g % 2]).start()

            def window(w, carry, g=g, cols=cols, held=held):
                hook_window(FORWARD, g, w)
                rows = window_rows(w)
                n = g * windows + w
                slot = n % 2
                s = against_heads(held[1, rows, :], split_diag(held[0, rows, :], mask_ref)) + bias_ref[g]
                e = jnp.exp(s - jnp.max(s, 0, keepdims=True))
                p = (e * (1.0 / jnp.sum(e, 0, keepdims=True))).astype(low)
                keep = pltpu.make_async_copy(pt_ref.at[slot], pt_hbm.at[n], local.at[4 + slot])

                @pl.when(n >= 2)
                def _():
                    keep.wait()

                pt_ref[slot] = p
                keep.start()
                o_ref[rows, cols] = undiag(held[2, rows, :].T, p, mask_ref).astype(low)
                return carry

            lax.fori_loop(0, windows, window, 0)

        run(W_P, ARRIVED)

        def output(w, carry):
            rows = window_rows(w)
            x1_ref[rows, :] = x_ref[rows, :].astype(full) + (dot(o_ref[rows, :], flat(wp[...])) + vec_ref[4:5, :])
            return carry

        lax.fori_loop(0, windows, output, 0)
        save.wait()
        for g in (GROUPS - 2, GROUPS - 1):
            pltpu.make_async_copy(qkv_ref.at[g % 2], qkv_hbm.at[g], local.at[2 + g % 2]).wait()
        for slot in range(2):
            pltpu.make_async_copy(pt_ref.at[slot], pt_hbm.at[0], local.at[4 + slot]).wait()

    def middle(dy_ref, dyt_ref, n2_ref, n2t_ref, y_ref, dn_ref, bu_ref, bsum_ref):
        zero_tail(n2_ref, windows)
        hook(MIDDLE, 0)

        def second_norm(w, carry):
            rows = window_rows(w)
            xhat, _ = norm_parts(x1_ref[rows, :])
            n2_ref[rows, :] = (xhat * vec_ref[5:6, :] + vec_ref[6:7, :]).astype(low)
            return carry

        lax.fori_loop(0, windows, second_norm, 0)
        transpose_rows(n2_ref, n2t_ref)
        hook(MIDDLE, 1)
        n2t_ref[C:, :] = jnp.ones((16, ROWS), low)
        y_ref[...] = jnp.zeros_like(y_ref)
        dn_ref[...] = jnp.zeros_like(dn_ref)
        for t in range(TILES):
            for s in range(TILE // 128):
                row, left = hidden_place(t, s)
                bu_ref[t, :, s * 128 : (s + 1) * 128] = vec_ref[row : row + 1, left : left + 128]
        hook(MIDDLE, 2)
        run(W_U0, ARRIVED)
        run(W_D0, ARRIVED)
        hook(TILE_STEP, 0)
        halves = TILE // SUB

        def step(i, carry):
            for k in range(1, TILES * halves):

                @pl.when(i == k)
                def _(k=k):
                    if k % halves == 0:
                        t = k // halves
                        for name in (W_U[t], W_D[t]):
                            run(name, ARRIVED)
                        for name in (W_U[t - 1], W_D[t - 1]):
                            jobs[name].close()
                        for name in (G_D[t - 1], G_U[t - 1]):
                            run(name, START)
                    hook(TILE_STEP, k)

            t, part = i // halves, i % halves
            cols = pl.ds(pl.multiple_of(part * SUB, SUB), SUB)
            wide = SUB // 128
            slot = (t + SLOTS - 1) % SLOTS
            u = flat(up[t, :, :, cols])
            d = flat(down[t, pl.ds(part * wide, wide)])
            h = dot(n2_ref[...], u) + bu_ref[t, :, cols]
            da = dot_nt(dy_ref[...], d)
            act, slope = gelu_both(h)
            a = act.astype(low)
            dh = (da * slope).astype(low)
            y_ref[...] += dot(a, d)
            dn_ref[...] += dot_nt(dh, u)
            gd = dot(dyt_ref[...], a).astype(low)
            down[slot, pl.ds(part * wide, wide)] = blocks(gd.T, wide)
            gu = dot(n2t_ref[...], dh)
            up[slot, :, :, cols] = blocks(gu[0:C].astype(low), OWNERS)
            bsum_ref[t, :, cols] = gu[C : C + 1]
            return carry

        lax.fori_loop(0, TILES * halves, step, 0)
        run(G_D[-1], START)
        run(G_U[-1], START)
        hook(AFTER_TILES, 0)
        sums_ref[...] = jnp.zeros_like(sums_ref)
        for t in range(TILES):
            for s in range(TILE // 128):
                row, left = hidden_place(t, s)
                sums_ref[row : row + 1, left : left + 128] = bsum_ref[t, :, s * 128 : (s + 1) * 128]
        transpose_rows(o_ref, dyt_ref)
        hook(AFTER_TILES, 1)

        def finish(w, carry):
            rows = window_rows(w)
            x1 = x1_ref[rows, :]
            xhat, scale = norm_parts(x1)
            dn = dn_ref[rows, :]
            dy = dy_ref[rows, :].astype(full)
            dx1 = dy + norm_back(xhat, scale, dn, vec_ref[5:6, :])
            dr = dx1.astype(low)
            sums_ref[4:5, :] += jnp.sum(dr.astype(full), 0, keepdims=True)
            sums_ref[5:6, :] += jnp.sum(dn * xhat, 0, keepdims=True)
            sums_ref[6:7, :] += jnp.sum(dn, 0, keepdims=True)
            sums_ref[7:8, :] += jnp.sum(dy, 0, keepdims=True)
            dy_ref[rows, :] = ((x1 + y_ref[rows, :] + vec_ref[7:8, :]) * live(w)).astype(low)
            x1_ref[rows, :] = dx1
            n2_ref[rows, :] = dr
            o_ref[rows, :] = dot_nt(dr, flat(wp[...])).astype(low)
            return carry

        lax.fori_loop(0, windows, finish, 0)
        save = pltpu.make_async_copy(dy_ref.at[0:rows_all], out_hbm, local.at[0])
        save.start()
        hook(AFTER_TILES, 2)
        jobs[W_P].close()
        for g in range(GROUPS):
            cols = slice(g * GCOLS, (g + 1) * GCOLS)
            wp[:, :, cols] = blocks(dot(dyt_ref[...], n2_ref[:, cols]).astype(low), OWNERS)
        run(G_P, START)
        hook(AFTER_TILES, 3)
        save.wait()

    def both(dy_ref, dyt_ref):
        pl.run_scoped(functools.partial(forward, dy_ref, dyt_ref), V((rows_all, C), low), V((ROWS, C), low), V((C, ROWS), low),
                      V((2, 3, ROWS, GCOLS), low), V((2, TOK, PACK), low), V((GROUPS, TOK, PACK), full))
        pl.run_scoped(functools.partial(middle, dy_ref, dyt_ref), V((ROWS, C), low), V((C + 16, ROWS), low), V((ROWS, C), full), V((ROWS, C), full),
                      V((TILES, 1, TILE), full), V((TILES, 1, TILE), full))

    pl.run_scoped(both, V((ROWS, C), low), V((C, ROWS), low))

    def backward(x_ref, n1t_ref, qkv_ref, pt_ref, dproj_ref, dn_ref, bias_ref):
        loads = [pltpu.make_async_copy(x_hbm, x_ref, local.at[0]), pltpu.make_async_copy(n1t_hbm, n1t_ref, local.at[1])]
        fetch = [pltpu.make_async_copy(qkv_hbm.at[g], qkv_ref.at[g % 2], local.at[2 + g % 2]) for g in range(GROUPS)]
        fetch[0].start()
        pltpu.make_async_copy(pt_hbm.at[0], pt_ref.at[0], local.at[4]).start()
        fetch[1].start()
        for load in loads:
            load.start()
        bias_ref[...] = jnp.zeros_like(bias_ref)
        dn_ref[...] = jnp.zeros_like(dn_ref)
        for part in range(3):
            dproj_ref[part, rows_all:, :] = jnp.zeros((ROWS - rows_all, GCOLS), low)
        for g in range(GROUPS):
            cols = slice(g * GCOLS, (g + 1) * GCOLS)
            held = qkv_ref.at[g % 2]
            fetch[g].wait()

            def window(w, carry, g=g, cols=cols, held=held):
                hook_window(BACKWARD, g, w)
                rows = window_rows(w)
                n = g * windows + w
                slot = n % 2

                @pl.when(n + 1 < GROUPS * windows)
                def _():
                    pltpu.make_async_copy(pt_hbm.at[n + 1], pt_ref.at[1 - slot], local.at[5 - slot]).start()

                pltpu.make_async_copy(pt_hbm.at[n], pt_ref.at[slot], local.at[4 + slot]).wait()
                q = held[0, rows, :]
                k = held[1, rows, :]
                v = held[2, rows, :]
                p = pt_ref[slot]
                do = split_diag(o_ref[rows, cols], mask_ref)
                dp = against_heads(v, do)
                dv = over_queries(p, do).astype(low)
                pf = p.astype(full)
                ds = (pf * (dp - jnp.sum(pf * dp, 0, keepdims=True))).astype(low)
                bias_ref[g] += ds.astype(full)
                dproj_ref[1, rows, :] = over_queries(ds, split_diag(q, mask_ref)).astype(low)
                dq = (undiag(k.T, ds, mask_ref) * (HEAD_DIM**-0.5)).astype(low)
                dproj_ref[0, rows, :] = dq
                dproj_ref[2, rows, :] = dv
                sums_ref[2:3, cols] += jnp.sum(dq.astype(full), 0, keepdims=True)
                sums_ref[3:4, cols] += jnp.sum(dv.astype(full), 0, keepdims=True)
                return carry

            lax.fori_loop(0, windows, window, 0)
            if g + 2 < GROUPS:
                fetch[g + 2].start()
            if g == 0:
                for load in loads:
                    load.wait()
            jobs[W_Q[g]].close()
            for part in range(3):
                d = dproj_ref[part]
                dn_ref[...] += dot_nt(d, flat(wq[g, part]))
                wq[g, part] = blocks(dot(n1t_ref[...], d).astype(low), OWNERS)
                if g == GROUPS - 1:
                    run(G_LAST[part], START)
            if g < GROUPS - 1:
                run(G_Q[g], START)
        hook(LAST_STEPS, 0)

        def last_norm(grad_ref):
            def finish(w, carry):
                rows = window_rows(w)
                slot = w % 2
                xhat, scale = norm_parts(x_ref[rows, :].astype(full))
                dn = dn_ref[rows, :]
                save = pltpu.make_async_copy(grad_ref.at[slot], grad_hbm.at[rows], local.at[4 + slot])

                @pl.when(w >= 2)
                def _():
                    save.wait()

                grad_ref[slot] = x1_ref[rows, :] + norm_back(xhat, scale, dn, vec_ref[0:1, :])
                save.start()
                sums_ref[0:1, :] += jnp.sum(dn * xhat, 0, keepdims=True)
                sums_ref[1:2, :] += jnp.sum(dn, 0, keepdims=True)
                return carry

            lax.fori_loop(0, windows, finish, 0)
            hook(LAST_STEPS, 1)
            for slot in range(2):
                pltpu.make_async_copy(grad_ref.at[slot], grad_hbm.at[pl.ds(0, TOK)], local.at[4 + slot]).wait()

        pl.run_scoped(last_norm, V((2, TOK, C), full))
        hook(LAST_STEPS, 2)

        def table(tmp_ref):
            pack_small(sums_ref[...], table_grad(line_ref, tmp_ref, bias_ref), terms_ref)

        pl.run_scoped(table, V((2, TOK * HEADS, 128), full))
        run(G_S, START)
        hook(LAST_STEPS, 3)
        for stage in range(len(Reduce.STAGES)):
            for name in G_ALL:
                if stage < len(jobs[name].STAGES):
                    run(name, stage)

    pl.run_scoped(backward, V((rows_all, C), low), V((C, ROWS), low), V((2, 3, ROWS, GCOLS), low), V((2, TOK, PACK), low), V((3, ROWS, GCOLS), low),
                  V((ROWS, C), full), V((GROUPS, TOK, PACK), full))
    jobs[W_U[-1]].close()
    jobs[W_D[-1]].close()
    for i in range(1, OWNERS):
        await_bytes(small.at[mine], small_sems.at[i])
    for name in G_ALL:
        jobs[name].close()


def shape(dims, kind):
    return jax.ShapeDtypeStruct(dims, kind)


def adamw(weight, moment, second, gradient, step_rate):
    moment_new = beta_one * moment + (1.0 - beta_one) * gradient
    second_new = beta_two * second + (1.0 - beta_two) * gradient * gradient
    update = moment_new * (1.0 / (1.0 - beta_one**STEP)) / (jnp.sqrt(second_new * (1.0 / (1.0 - beta_two**STEP))) + adam_eps)
    weight_new = weight * (1.0 - step_rate * weight_decay) - step_rate * update
    return (weight_new, moment_new, second_new)


def update_kernel(*refs):
    gq, gp, gu, gd, gs = refs[:5]
    ins = [refs[5 + 3 * i : 8 + 3 * i] for i in range(6)]
    outs = [refs[25 + 4 * i : 29 + 4 * i] for i in range(4)] + [refs[41:44], refs[44:47]]
    for i in range(2):
        refs[47 + i][...] = refs[23 + i][...]

    def piece(which, place, gradient):
        new = adamw(*(ref[place] for ref in ins[which]), gradient, step_rates[which])
        for ref, value in zip(outs[which], new):
            ref[place] = value
        if which < 4:
            outs[which][3][place] = new[0].astype(low)

    for part in range(3):
        for g in range(GROUPS):
            left = part * C + g * GCOLS
            piece(0, (slice(None), slice(left, left + GCOLS)), gq[g, part].astype(full))
    piece(1, (slice(None), slice(None)), gp[...].astype(full))
    for t in range(TILES):
        for s in range(OWNERS):
            left = (MLP // OWNERS) * s + 128 * t
            piece(2, (slice(None), slice(left, left + 128)), gu[t, :, s * 128 : (s + 1) * 128].astype(full))
    piece(3, (slice(None), slice(None)), gd[0].astype(full))

    @pl.when(pl.program_id(0) == 0)
    def _():
        every = (slice(None), slice(None))
        piece(4, every, gs[0:12, 0:OWNED])
        piece(5, every, gs[16:40, 0 : ins[5][0].shape[1]])


def update(gq, gp, gu, gd, gs, states, results):
    steps = OWNED // 16

    def rows_of(array):
        tall = array.shape[0] // steps
        return pl.BlockSpec((tall, array.shape[1]), lambda i: (i, 0))

    def whole(array):
        return pl.BlockSpec(array.shape, lambda i: (0, 0))

    per_tile = 128 * TILES // steps
    specs = [
        pl.BlockSpec((GROUPS, 3, 16, GCOLS), lambda i: (0, 0, i, 0)),
        pl.BlockSpec((16, C), lambda i: (i, 0)),
        pl.BlockSpec((TILES, 16, TILE), lambda i: (0, i, 0)),
        pl.BlockSpec((1, per_tile, C), lambda i: (i // (128 // per_tile), i % (128 // per_tile), 0)),
        whole(gs),
    ]
    out_shapes, out_specs = [], []
    for i, group in enumerate(states):
        for array in group:
            specs.append(rows_of(array) if i < 4 else whole(array))
            out_shapes.append(shape(array.shape, full))
            out_specs.append(specs[-1])
        if i < 4:
            out_shapes.append(shape(group[0].shape, low))
            out_specs.append(rows_of(group[0]))
    results = [array.reshape(steps, -1, C) for array in results]
    for array in results:
        specs.append(pl.BlockSpec((1, *array.shape[1:]), lambda i: (i, 0, 0)))
        out_shapes.append(shape(array.shape, array.dtype))
        out_specs.append(specs[-1])
    return pl.pallas_call(
        update_kernel,
        grid=(steps,),
        in_specs=specs,
        out_specs=out_specs,
        out_shape=out_shapes,
        compiler_params=pltpu.CompilerParams(vmem_limit_bytes=63 * MIB),
        name="update",
    )(gq, gp, gu, gd, gs, *[array for group in states for array in group], *results)


def shards(
    tokens, out_grad, window_count,
    qkv_weight, qkv_first, qkv_second,
    output_weight, output_first, output_second,
    up_weight, up_first, up_second,
    down_weight, down_first, down_second,
    vectors, vector_first, vector_second,
    bias_table, table_first, table_second,
):
    windows = tokens.shape[0]
    rows = windows * TOK
    V = pltpu.VMEM
    D = pltpu.SemaphoreType.DMA
    hbm = pl.BlockSpec(memory_space=pl.ANY)
    vmem = pl.BlockSpec(memory_space=pltpu.VMEM)
    result = pl.pallas_call(
        functools.partial(layer_kernel, windows),
        out_shape=[
            shape((rows, C), low), shape((rows, C), full),
            shape((GROUPS, 3, OWNED, GCOLS), low), shape((OWNED, C), low), shape((TILES, OWNED, TILE), low), shape((TILES, 128, C), low),
            shape((40, 128), full),
            shape((GROUPS, 3, ROWS, GCOLS), low), shape((GROUPS * windows, TOK, PACK), low), shape((C, ROWS), low)],
        in_specs=[hbm, hbm, pl.BlockSpec(memory_space=pltpu.SMEM)] + [hbm] * 4 + [vmem] * 4,
        out_specs=[hbm, hbm] + [vmem] * 5 + [hbm] * 3,
        scratch_shapes=[
            V((GROUPS, 3, OWNERS, OWNED, GCOLS), low), V((OWNERS, OWNED, C), low), V((SLOTS, OWNERS, OWNED, TILE), low),
            V((SLOTS, OWNERS, 128, C), low), V((OWNERS, 48, 128), low), V((ROWS, C), low), V((rows, C), full), V((16, C), full), V((16, C), full),
            V((OWNERS, 40, 128), full)]
        + reduce_scratch()
        + [D((GATHERS, Gather.SEMS)), D((REDUCES, ReduceDirect.SEMS)), D((2 * OWNERS,)), D((ReduceSmall.SEMS,)), D((6,))],
        compiler_params=pltpu.CompilerParams(vmem_limit_bytes=63 * MIB, collective_id=0, has_side_effects=True),
        name="layer",
    )(tokens.reshape(rows, C), out_grad.reshape(rows, C), window_count, qkv_weight, output_weight, up_weight, down_weight, vectors, bias_table.T,
      jnp.asarray(line_matrix(), low), jnp.asarray(head_masks(), low))
    out, grad, gq, gp, gu, gd, gs = result[:7]
    new = update(gq, gp, gu, gd, gs, (
        (qkv_weight, qkv_first, qkv_second), (output_weight, output_first, output_second), (up_weight, up_first, up_second),
        (down_weight, down_first, down_second), (vectors, vector_first, vector_second), (bias_table.T, table_first.T, table_second.T)), (out, grad))
    *new, out, grad = new
    return (out.reshape(tokens.shape), grad.reshape(tokens.shape), *new[:-3], *(array.T for array in new[-3:]))


def vmem_call(body, outs, scratch, args, name, limit=60, **params):
    spec = pl.BlockSpec(memory_space=pltpu.VMEM)
    return pl.pallas_call(
        body,
        out_shape=outs,
        in_specs=[pl.BlockSpec(memory_space=pltpu.SMEM) if a.dtype == full and a.ndim == 1 else spec for a in args],
        out_specs=[spec] * len(outs),
        scratch_shapes=scratch,
        compiler_params=pltpu.CompilerParams(vmem_limit_bytes=limit * MIB, **params),
        name=name,
    )(*args)


def local_step(tokens, out_grad, window_count, small, wq, wp, up, down):
    windows = tokens.shape[0]
    rows = windows * TOK
    owned = C // OWNERS
    V = pltpu.VMEM
    x = tokens.reshape(rows, C)
    dy = out_grad.reshape(rows, C)
    live = (jnp.arange(windows) < window_count[0]).astype(full)
    line = jnp.asarray(line_matrix(), low)
    masks = jnp.asarray(head_masks(), low)
    qkv, pt, o, x1, n1t, vec = vmem_call(
        functools.partial(attention_forward, windows),
        [shape((9, ROWS, GCOLS), low), shape((GROUPS, windows, TOK, PACK), low), shape((ROWS, C), low), shape((rows, C), full), shape((C, ROWS), low),
         shape((16, C), full)],
        [V((ROWS, C), low), V((GROUPS, TOK, PACK), full), V((2, TOK * HEADS, 128), full)],
        (x, small, line, masks, wq, wp), "attention_forward")
    out, dx1, do, gup, gdown, gout, sums = vmem_call(
        functools.partial(feed_forward, windows),
        [shape((rows, C), low), shape((ROWS, C), full), shape((rows, C), low), shape((TILES, OWNERS, owned, TILE), low),
         shape((TILES, OWNERS, C, 128), low), shape((OWNERS, owned, C), low), shape((16, C), full)],
        [V((ROWS, C), low), V((C, ROWS), low), V((ROWS, C), low), V((C, ROWS), low), V((ROWS, C), full), V((ROWS, C), full),
         V((TILES, 1, TILE), full), V((TILES, 1, TILE), full)],
        (x1, dy, live, vec, up, down, wp, o), "feed_forward")
    gq, gsmall, grad = vmem_call(
        functools.partial(attention_backward, windows),
        [shape((GROUPS, 3, OWNERS, owned, GCOLS), low), shape((OWNERS, 40, 128), full), shape((rows, C), full)],
        [V((16, C), full), V((GROUPS, TOK, PACK), full), V((2, TOK * HEADS, 128), full), V((3, ROWS, GCOLS), low), V((ROWS, C), full)],
        (x, vec, line, masks, wq, qkv, pt, do, dx1, n1t, sums), "attention_backward")
    return out.reshape(tokens.shape), grad.reshape(tokens.shape), gq, gout, gup, gdown, gsmall


def shards_general(
    tokens, out_grad, window_count,
    qkv_weight, qkv_first, qkv_second,
    output_weight, output_first, output_second,
    up_weight, up_first, up_second,
    down_weight, down_first, down_second,
    vectors, vector_first, vector_second,
    bias_table, table_first, table_second,
):
    gather = functools.partial(lax.all_gather, axis_name="shard", tiled=True)
    scatter = functools.partial(lax.psum_scatter, axis_name="shard", tiled=True)
    owned = C // OWNERS
    wq = gather(qkv_weight.astype(low), axis=0).reshape(OWNERS, owned, 3, GROUPS, GCOLS).transpose(3, 2, 0, 1, 4)
    wp = gather(output_weight.astype(low), axis=0).reshape(OWNERS, owned, C)
    up = gather(up_weight.astype(low), axis=0).reshape(OWNERS, owned, OWNERS, TILES, 128).transpose(3, 0, 1, 2, 4)
    up = up.reshape(TILES, OWNERS, owned, TILE)
    down = gather(down_weight.astype(low), axis=0).reshape(OWNERS, TILES, 128, C).transpose(1, 0, 2, 3)
    vec = gather(vectors.astype(low), axis=1)
    tab = gather(bias_table.astype(low), axis=0)
    table_rows = tab.shape[0]
    count = TAB_ROWS // OWNERS
    vec = vec.reshape(12, OWNERS, owned).transpose(1, 0, 2)
    tab = tab[:TAB_ROWS].reshape(OWNERS, count, HEADS).transpose(0, 2, 1)
    small = jnp.concatenate([jnp.pad(vec, ((0, 0), (0, 4), (0, 128 - owned))), jnp.pad(tab, ((0, 0), (0, 8), (0, 128 - count)))], 1)
    out, grad, gq, gp, gu, gd, gs = local_step(tokens, out_grad, window_count, small, wq, wp, up, down)
    gq = gq.astype(full).transpose(2, 3, 1, 0, 4).reshape(C, 3 * C)
    gu = gu.astype(full).reshape(TILES, C, OWNERS, 128).transpose(1, 2, 0, 3).reshape(C, MLP)
    gd = gd.astype(full).transpose(1, 0, 3, 2).reshape(MLP, C)
    gv = gs[:, :12, :owned].transpose(1, 0, 2).reshape(12, C)
    gb = gs[:, 16:40, :count].transpose(0, 2, 1).reshape(TAB_ROWS, HEADS)
    gb = jnp.pad(gb, ((0, table_rows - TAB_ROWS), (0, 0)))
    totals = lax.psum(
        (scatter(gq, scatter_dimension=0), scatter(gp.astype(full).reshape(C, C), scatter_dimension=0), scatter(gu, scatter_dimension=0),
         scatter(gd, scatter_dimension=0), scatter(gv, scatter_dimension=1), scatter(gb, scatter_dimension=0)), "rep")
    states = (
        (qkv_weight, qkv_first, qkv_second), (output_weight, output_first, output_second), (up_weight, up_first, up_second),
        (down_weight, down_first, down_second), (vectors, vector_first, vector_second), (bias_table, table_first, table_second))
    results = [out, grad]
    for i, (state, total, rate) in enumerate(zip(states, totals, step_rates)):
        new = adamw(*state, total, rate)
        results += [*new, new[0].astype(low)] if i < 4 else [*new]
    return tuple(results)


def solution(mesh):
    wins = P(("rep", "shard"), None, None)
    rows = P("shard", None)
    cols = P(None, "shard")
    fits = mesh.shape["rep"] == REPS and mesh.shape["shard"] == OWNERS
    return jax.shard_map(
        shards if fits else shards_general,
        mesh=mesh,
        in_specs=(wins, wins, P(("rep", "shard"))) + (rows,) * 12 + (cols,) * 3 + (rows,) * 3,
        out_specs=(wins, wins) + (rows,) * 16 + (cols,) * 3 + (rows,) * 3,
        check_vma=False,
    )
```

```python
import functools
import math

import jax
import jax.numpy as jnp
import numpy as np
from jax import lax
from jax.experimental import pallas as pl
from jax.experimental.pallas import tpu as pltpu
from jax.sharding import PartitionSpec as P

C = 768
HEADS = 24
MLP = 3072
WIN = 12
STEP = 5
HEAD_DIM = 32
SPAN = 2 * WIN - 1
TOK = WIN * WIN
TAB_ROWS = 536
ROWS = 1024
GROUPS = 3
GCOLS = 256
GHEADS = 8
PACK = GHEADS * TOK
TAB_LANES = 640
TILES = 3
TILE = MLP // TILES
SUB = 512
LINE = 384
MIB = 1 << 20

beta_one = 0.5
beta_two = 0.6
weight_decay = 0.05
adam_eps = 1e-08
norm_eps = 1e-05
step_rates = (0.04, 0.15, 0.04, 0.02, 0.2, 1.0)
low = jnp.bfloat16
full = jnp.float32
NT = (((1,), (1,)), ((), ()))


def dot(a, b):
    return jnp.dot(a, b, preferred_element_type=full)


def dot_nt(a, b):
    return lax.dot_general(a, b, NT, preferred_element_type=full)


def line_matrix():
    out = np.zeros((TAB_LANES, LINE), np.float32)
    col = np.arange(SPAN * WIN)
    out[(col // WIN) * SPAN + col % WIN + WIN - 1, col] = 1.0
    return out


def head_masks():
    lane = np.arange(GCOLS) // HEAD_DIM
    one = (lane[None, :] == np.arange(GHEADS)[:, None]).astype(np.float32)
    return np.broadcast_to(one[:, None, :], (GHEADS, 16, GCOLS))


def norm_parts(z):
    mean = jnp.sum(z, -1, keepdims=True) * (1.0 / C)
    center = z - mean
    spread = jnp.sum(center * center, -1, keepdims=True) * (1.0 / C)
    scale = lax.rsqrt(spread + norm_eps)
    return center * scale, scale


def norm_back(xhat, scale, dn, gain):
    g = dn * gain
    m1 = jnp.sum(g, -1, keepdims=True) * (1.0 / C)
    m2 = jnp.sum(g * xhat, -1, keepdims=True) * (1.0 / C)
    return scale * (g - m1 - xhat * m2)


def diag(x, mask_ref):
    head = x[0:128].reshape(8, 16, GCOLS)
    tail = x[128:144]
    parts = []
    for h in range(GHEADS):
        parts.append((head * mask_ref[h][None]).reshape(128, GCOLS))
    for h in range(GHEADS):
        parts.append(tail * mask_ref[h])
    return jnp.concatenate(parts, 0)


def undiag(xt, m, mask_ref):
    main = []
    for h in range(0, GHEADS, 2):
        r = dot(xt[h * HEAD_DIM : (h + 2) * HEAD_DIM], m[:, h * 128 : (h + 2) * 128])
        main.append(r[0:HEAD_DIM, 0:128])
        main.append(r[HEAD_DIM : 2 * HEAD_DIM, 128:256])
    main = jnp.concatenate(main, 0)
    rest = dot(xt, m[:, GHEADS * 128 :])
    rest_t = rest.T.reshape(GHEADS, 16, GCOLS)
    keep = mask_ref[...].astype(full)
    return jnp.concatenate([main.T, jnp.sum(rest_t * keep, 0)], 0)


def flat(x):
    return x.reshape(x.shape[0] * x.shape[1], x.shape[2])


def blocks(x, owners):
    return x.reshape(owners, x.shape[0] // owners, x.shape[1])


def hidden_place(t, s):
    at = (MLP // GHEADS) * s + 128 * t
    return 8 + at // C, at % C


def unpack_small(small_ref, vec_ref):
    owners = small_ref.shape[0]
    width = C // owners
    count = TAB_ROWS // owners
    vec = jnp.zeros((16, C), full)
    tab = jnp.zeros((HEADS, TAB_LANES), full)
    lane = lax.broadcasted_iota(jnp.int32, (16, 128), 1)
    lane_tab = lax.broadcasted_iota(jnp.int32, (HEADS, 128), 1)
    for s in range(owners):
        piece = small_ref[s].astype(full)
        part = jnp.where(lane < width, piece[0:16], 0.0)
        part = jnp.concatenate([part, jnp.zeros((16, C - 128), full)], 1)
        vec = vec + (pltpu.roll(part, width * s, 1) if s else part)
        part = jnp.where(lane_tab < count, piece[16 : 16 + HEADS], 0.0)
        part = jnp.concatenate([part, jnp.zeros((HEADS, TAB_LANES - 128), full)], 1)
        tab = tab + (pltpu.roll(part, count * s, 1) if s else part)
    vec_ref[...] = vec
    return tab


def pack_small(vec, tab, out_ref):
    owners = out_ref.shape[0]
    width = C // owners
    count = TAB_ROWS // owners
    for s in range(owners):
        out_ref[s, 0:16, :] = (pltpu.roll(vec, C - width * s, 1) if s else vec)[:, 0:128]
        out_ref[s, 16:40, :] = (pltpu.roll(tab, TAB_LANES - count * s, 1) if s else tab)[:, 0:128]


def spread_table(tab, line_ref, tmp_ref):
    def column(cj, carry):
        shifted = pltpu.roll(tab, cj, 1)
        line = dot(shifted.astype(low), line_ref[...])
        for rj in range(WIN):
            cut = (WIN - 1 - rj) * WIN
            part = pltpu.roll(line, LINE - cut, 1) if cut else line
            row = pl.multiple_of((rj * WIN + cj) * HEADS, 8)
            tmp_ref[0, pl.ds(row, HEADS), :] = part[:, 0:128]
            tmp_ref[1, pl.ds(row, HEADS), :] = part[:, 128:256]
        return carry

    lax.fori_loop(0, WIN, column, 0)


def place_bias(tmp_ref, bias_ref):
    lane = lax.broadcasted_iota(jnp.int32, (TOK, 128), 1)
    for g in range(GROUPS):
        rest = jnp.zeros((TOK, 128), full)
        for h in range(GHEADS):
            at = pl.ds(g * GHEADS + h, TOK, stride=HEADS)
            bias_ref[g, :, h * 128 : (h + 1) * 128] = tmp_ref[0, at, :]
            piece = tmp_ref[1, at, :]
            piece = pltpu.roll(piece, 16 * h, 1) if h else piece
            rest = jnp.where((lane >= 16 * h) & (lane < 16 * h + 16), piece, rest)
        bias_ref[g, :, GHEADS * 128 :] = rest


def table_grad(line_ref, tmp_ref, bias_ref):
    lane = lax.broadcasted_iota(jnp.int32, (TOK, 128), 1)
    for g in range(GROUPS):
        rest = bias_ref[g, :, GHEADS * 128 :]
        for h in range(GHEADS):
            at = pl.ds(g * GHEADS + h, TOK, stride=HEADS)
            tmp_ref[0, at, :] = bias_ref[g, :, h * 128 : (h + 1) * 128]
            piece = pltpu.roll(rest, 128 - 16 * h, 1) if h else rest
            tmp_ref[1, at, :] = jnp.where(lane < 16, piece, 0.0)

    def column(cj, total):
        line = jnp.zeros((HEADS, LINE), full)
        for rj in range(WIN):
            cut = (WIN - 1 - rj) * WIN
            row = pl.multiple_of((rj * WIN + cj) * HEADS, 8)
            part = jnp.concatenate([tmp_ref[0, pl.ds(row, HEADS), :], tmp_ref[1, pl.ds(row, HEADS), :], jnp.zeros((HEADS, 128), full)], 1)
            line = line + (pltpu.roll(part, cut, 1) if cut else part)
        high = line.astype(low)
        rest = (line - high.astype(full)).astype(low)
        spread = dot_nt(high, line_ref[...]) + dot_nt(rest, line_ref[...])
        return total + pltpu.roll(spread, TAB_LANES - cj, 1)

    return lax.fori_loop(0, WIN, column, jnp.zeros((HEADS, TAB_LANES), full))


def transpose_rows(src_ref, dst_ref):
    def block(i, carry):
        at = pl.multiple_of(i * 128, 128)
        dst_ref[0 : src_ref.shape[1], pl.ds(at, 128)] = src_ref[pl.ds(at, 128), :].T
        return carry

    lax.fori_loop(0, ROWS // 128, block, 0)


def window_rows(w):
    return slice(w * TOK, (w + 1) * TOK) if isinstance(w, int) else pl.ds(pl.multiple_of(w * TOK, 16), TOK)


def zero_tail(ref, windows):
    at = windows * TOK
    ref[at:ROWS, :] = jnp.zeros((ROWS - at, ref.shape[1]), ref.dtype)


def half_diag(x, half, mask_ref):
    lanes = slice(half * 128, (half + 1) * 128)
    part = x[0:128, lanes].reshape(8, 16, 128)
    heads = range(half * GHEADS // 2, (half + 1) * GHEADS // 2)
    return jnp.concatenate([(part * mask_ref[h, :, lanes][None]).reshape(128, 128) for h in heads], 0)


def rest_diag(x, mask_ref):
    return jnp.concatenate([x[128:144] * mask_ref[h] for h in range(GHEADS)], 0)


def split_diag(x, mask_ref):
    return half_diag(x, 0, mask_ref), half_diag(x, 1, mask_ref), rest_diag(x, mask_ref)


def against_heads(x, split):
    first, second, rest = split
    return jnp.concatenate([dot_nt(x[:, 0:128], first), dot_nt(x[:, 128:256], second), dot_nt(x, rest)], 1)


def over_queries(m, split):
    first, second, rest = split
    return jnp.concatenate([dot(m[:, 0:512], first), dot(m[:, 512:1024], second)], 1) + dot(m[:, 1024:], rest)


def attention_forward(windows, x_ref, small_ref, line_ref, mask_ref, wq_ref, wp_ref,
                      qkv_ref, pt_ref, o_ref, x1_ref, n1t_ref, vec_ref, n1_ref, bias_ref, tmp_ref):
    tab = unpack_small(small_ref, vec_ref)
    spread_table(tab, line_ref, tmp_ref)
    place_bias(tmp_ref, bias_ref)
    zero_tail(n1_ref, windows)
    zero_tail(o_ref, windows)

    def first_norm(w, carry):
        xhat, _ = norm_parts(x_ref[window_rows(w), :].astype(full))
        n1_ref[window_rows(w), :] = (xhat * vec_ref[0:1, :] + vec_ref[1:2, :]).astype(low)
        return carry

    lax.fori_loop(0, windows, first_norm, 0)
    transpose_rows(n1_ref, n1t_ref)

    def group(g, carry):
        cols = pl.ds(pl.multiple_of(g * GCOLS, GCOLS), GCOLS)
        n1 = n1_ref[...]
        qkv_ref[g] = ((dot(n1, flat(wq_ref[g, 0])) + vec_ref[2:3, cols]) * (HEAD_DIM**-0.5)).astype(low)
        qkv_ref[GROUPS + g] = dot(n1, flat(wq_ref[g, 1])).astype(low)
        qkv_ref[2 * GROUPS + g] = (dot(n1, flat(wq_ref[g, 2])) + vec_ref[3:4, cols]).astype(low)

        def window(w, inner):
            rows = window_rows(w)
            q = qkv_ref[g, rows, :]
            k = qkv_ref[GROUPS + g, rows, :]
            v = qkv_ref[2 * GROUPS + g, rows, :]
            s = dot_nt(k, diag(q, mask_ref)) + bias_ref[g]
            e = jnp.exp(s - jnp.max(s, 0, keepdims=True))
            p = (e * (1.0 / jnp.sum(e, 0, keepdims=True))).astype(low)
            pt_ref[g, w] = p
            o_ref[rows, cols] = undiag(v.T, p, mask_ref).astype(low)
            return inner

        lax.fori_loop(0, windows, window, 0)
        return carry

    lax.fori_loop(0, GROUPS, group, 0)

    def output(w, carry):
        rows = window_rows(w)
        branch = dot(o_ref[rows, :], flat(wp_ref[...])) + vec_ref[4:5, :]
        x1_ref[rows, :] = x_ref[rows, :].astype(full) + branch
        return carry

    lax.fori_loop(0, windows, output, 0)


def gelu_both(h):
    c = math.sqrt(2.0 / math.pi)
    square = h * h
    t = jnp.tanh(h * (c + (c * 0.044715) * square))
    half = 0.5 + 0.5 * t
    act = h * half
    return act, half + act * (1.0 - half) * (2.0 * c + (6.0 * c * 0.044715) * square)


def feed_forward(windows, x1_ref, dy_ref, live_ref, vec_ref, up_ref, down_ref, wp_ref, o_ref,
                 out_ref, dx1_ref, do_ref, gup_ref, gdown_ref, gout_ref, sums_ref,
                 n2_ref, n2t_ref, dy2_ref, dyt_ref, y_ref, dn_ref, bu_ref, bsum_ref):
    zero_tail(n2_ref, windows)
    zero_tail(dy2_ref, windows)

    def second_norm(w, carry):
        rows = window_rows(w)
        xhat, _ = norm_parts(x1_ref[rows, :])
        n2_ref[rows, :] = (xhat * vec_ref[5:6, :] + vec_ref[6:7, :]).astype(low)
        dy2_ref[rows, :] = (dy_ref[rows, :].astype(full) * live_ref[w]).astype(low)
        return carry

    lax.fori_loop(0, windows, second_norm, 0)
    transpose_rows(n2_ref, n2t_ref)
    transpose_rows(dy2_ref, dyt_ref)
    y_ref[...] = jnp.zeros_like(y_ref)
    dn_ref[...] = jnp.zeros_like(dn_ref)
    owners = gup_ref.shape[1]
    for t in range(TILES):
        for s in range(TILE // 128):
            row, at = hidden_place(t, s)
            bu_ref[t, :, s * 128 : (s + 1) * 128] = vec_ref[row : row + 1, at : at + 128]

    def step(t, carry):
        for part in range(TILE // SUB):
            cols = slice(part * SUB, (part + 1) * SUB)
            up = flat(up_ref[t, :, :, cols])
            down = flat(down_ref[t, part * SUB // 128 : (part + 1) * SUB // 128])
            h = dot(n2_ref[...], up) + bu_ref[t, :, cols]
            da = dot_nt(dy2_ref[...], down)
            act, slope = gelu_both(h)
            a = act.astype(low)
            dh = (da * slope).astype(low)
            bsum_ref[t, :, cols] = jnp.sum(dh.astype(full), 0, keepdims=True)
            y_ref[...] += dot(a, down)
            dn_ref[...] += dot_nt(dh, up)
            gd = dot(dyt_ref[...], a).astype(low)
            for b in range(SUB // 128):
                gdown_ref[t, part * SUB // 128 + b] = gd[:, b * 128 : (b + 1) * 128]
            gup_ref[t, :, :, cols] = blocks(dot(n2t_ref[...], dh).astype(low), owners)
        return carry

    lax.fori_loop(0, TILES, step, 0)
    sums_ref[...] = jnp.zeros_like(sums_ref)
    for t in range(TILES):
        for s in range(TILE // 128):
            row, at = hidden_place(t, s)
            sums_ref[row : row + 1, at : at + 128] = bsum_ref[t, :, s * 128 : (s + 1) * 128]
    zero_tail(dx1_ref, windows)

    def finish(w, carry):
        rows = window_rows(w)
        x1 = x1_ref[rows, :]
        out_ref[rows, :] = ((x1 + y_ref[rows, :] + vec_ref[7:8, :]) * live_ref[w]).astype(low)
        xhat, scale = norm_parts(x1)
        dn = dn_ref[rows, :]
        dy = dy2_ref[rows, :].astype(full)
        dx1 = dy + norm_back(xhat, scale, dn, vec_ref[5:6, :])
        dx1_ref[rows, :] = dx1
        dr = dx1.astype(low)
        n2_ref[rows, :] = dr
        do_ref[rows, :] = dot_nt(dr, flat(wp_ref[...])).astype(low)
        sums_ref[4:5, :] += jnp.sum(dr.astype(full), 0, keepdims=True)
        sums_ref[5:6, :] += jnp.sum(dn * xhat, 0, keepdims=True)
        sums_ref[6:7, :] += jnp.sum(dn, 0, keepdims=True)
        sums_ref[7:8, :] += jnp.sum(dy, 0, keepdims=True)
        return carry

    lax.fori_loop(0, windows, finish, 0)
    transpose_rows(o_ref, dyt_ref)
    for g in range(GROUPS):
        at = pl.ds(g * GCOLS, GCOLS)
        gout_ref[:, :, at] = blocks(dot(dyt_ref[...], n2_ref[:, at]).astype(low), gout_ref.shape[0])


def attention_backward(windows, x_ref, vec_ref, line_ref, mask_ref, wq_ref, qkv_ref, pt_ref, do_ref, dx1_ref, n1t_ref, sums_in_ref,
                       gq_ref, gsmall_ref, grad_ref, sums_ref, bias_ref, tmp_ref, dproj_ref, dn_ref):
    bias_ref[...] = jnp.zeros_like(bias_ref)
    dn_ref[...] = jnp.zeros_like(dn_ref)
    sums_ref[...] = sums_in_ref[...]
    for part in range(3):
        dproj_ref[part, windows * TOK :, :] = jnp.zeros((ROWS - windows * TOK, GCOLS), low)

    def group(g, carry):
        cols = pl.ds(pl.multiple_of(g * GCOLS, GCOLS), GCOLS)

        def window(w, inner):
            rows = window_rows(w)
            q = qkv_ref[g, rows, :]
            k = qkv_ref[GROUPS + g, rows, :]
            v = qkv_ref[2 * GROUPS + g, rows, :]
            p = pt_ref[g, w]
            do = diag(do_ref[rows, cols], mask_ref)
            dp = dot_nt(v, do)
            dv = dot(p, do)
            pf = p.astype(full)
            ds = (pf * (dp - jnp.sum(pf * dp, 0, keepdims=True))).astype(low)
            bias_ref[g] += ds.astype(full)
            dk = dot(ds, diag(q, mask_ref))
            dq = undiag(k.T, ds, mask_ref) * (HEAD_DIM**-0.5)
            dq = dq.astype(low)
            dv = dv.astype(low)
            dproj_ref[0, rows, :] = dq
            dproj_ref[1, rows, :] = dk.astype(low)
            dproj_ref[2, rows, :] = dv
            sums_ref[2:3, cols] += jnp.sum(dq.astype(full), 0, keepdims=True)
            sums_ref[3:4, cols] += jnp.sum(dv.astype(full), 0, keepdims=True)
            return inner

        lax.fori_loop(0, windows, window, 0)
        for part in range(3):
            d = dproj_ref[part]
            gq_ref[g, part] = blocks(dot(n1t_ref[...], d).astype(low), gq_ref.shape[2])
            dn_ref[...] += dot_nt(d, flat(wq_ref[g, part]))
        return carry

    lax.fori_loop(0, GROUPS, group, 0)

    def finish(w, carry):
        rows = window_rows(w)
        xhat, scale = norm_parts(x_ref[rows, :].astype(full))
        dn = dn_ref[rows, :]
        grad_ref[rows, :] = dx1_ref[rows, :] + norm_back(xhat, scale, dn, vec_ref[0:1, :])
        sums_ref[0:1, :] += jnp.sum(dn * xhat, 0, keepdims=True)
        sums_ref[1:2, :] += jnp.sum(dn, 0, keepdims=True)
        return carry

    lax.fori_loop(0, windows, finish, 0)
    pack_small(sums_ref[...], table_grad(line_ref, tmp_ref, bias_ref), gsmall_ref)


MESH = pl.DeviceIdType.MESH
REPS = 4
OWNERS = 8
LINKS = OWNERS // 2


class Spot:
    def __init__(self):
        self.rep = lax.axis_index("rep")
        self.shard = lax.axis_index("shard")
        self.z = self.shard // 2
        self.core = self.shard % 2

    def sibling(self):
        return (self.rep, self.z * 2 + (1 - self.core))

    def along_z(self, step):
        return (self.rep, ((self.z + step) % LINKS) * 2 + self.core)

    def turned(self, axis):
        x, y = self.rep % 2, self.rep // 2
        return y * 2 + (1 - x) if axis == 0 else (1 - y) * 2 + x

    def beside(self, axis):
        return (self.turned(axis), self.shard)

    def across(self):
        return (REPS - 1 - self.rep, self.shard)


def greet(spot):
    barrier = pltpu.get_barrier_semaphore()
    peers = [(spot.rep, (spot.shard + i) % OWNERS) for i in range(1, OWNERS)]
    peers += [((spot.rep + i) % REPS, spot.shard) for i in range(1, REPS)]
    for peer in peers:
        pl.semaphore_signal(barrier, inc=1, device_id=peer, device_id_type=MESH)
    return barrier, len(peers)


def send(src, dst, send_sem, recv_sem, peer):
    pltpu.make_async_remote_copy(src_ref=src, dst_ref=dst, send_sem=send_sem, recv_sem=recv_sem, device_id=peer, device_id_type=MESH).start()


def await_bytes(ref, sem):
    pltpu.make_async_copy(ref, ref, sem).wait()


def quarter(ref, rep):
    rows, cols = ref.shape[-2:]
    lead = (slice(None),) * (len(ref.shape) - 2)
    top = pl.multiple_of((rep // 2) * (rows // 2), 16)
    left = pl.multiple_of((rep % 2) * (cols // 2), 128)
    return ref.at[lead + (pl.ds(top, rows // 2), pl.ds(left, cols // 2))]


def half(ref, rep, axis):
    rows, cols = ref.shape[-2:]
    lead = (slice(None),) * (len(ref.shape) - 2)
    if axis == 0:
        left = pl.multiple_of((rep % 2) * (cols // 2), 128)
        return ref.at[lead + (slice(None), pl.ds(left, cols // 2))]
    top = pl.multiple_of((rep // 2) * (rows // 2), 16)
    return ref.at[lead + (pl.ds(top, rows // 2), slice(None))]


class Gather:
    KINDS = (LINKS - 1, LINKS - 1, LINKS - 1, LINKS - 1, LINKS)
    SEMS = 2 * sum(KINDS)
    STAGES = ("start", "across", "relay", "beside", "finish")

    def __init__(self, spot, place, axis, sems, direct=False):
        self.spot, self.place, self.axis, self.sems, self.direct = spot, place, axis, sems, direct

    def sem(self, side, kind, i):
        return self.sems.at[side * (self.SEMS // 2) + sum(self.KINDS[:kind]) + i]

    def block(self, step):
        return self.place(((self.spot.z - step + LINKS) % LINKS) * 2 + self.spot.core)

    def other(self, step):
        return self.place(((self.spot.z - step + LINKS) % LINKS) * 2 + 1 - self.spot.core)

    def start(self):
        spot = self.spot
        mine = self.block(0)
        for i in range(1, LINKS):
            piece = quarter(mine, spot.rep)
            send(piece, piece, self.sem(0, 0, i - 1), self.sem(1, 0, i - 1), spot.along_z(i))
        send(mine, mine, self.sem(0, 4, 0), self.sem(1, 4, 0), spot.sibling())

    def across(self):
        spot = self.spot
        for i in range(1, LINKS):
            piece = quarter(self.block(i), spot.rep)
            await_bytes(piece, self.sem(1, 0, i - 1))
            for axis in (self.axis, 1 - self.axis):
                send(piece, piece, self.sem(0, 1 + axis, i - 1), self.sem(1, 1 + axis, i - 1), spot.beside(axis))
            if self.direct:
                send(piece, piece, self.sem(0, 3, i - 1), self.sem(1, 3, i - 1), spot.across())

    def relay(self):
        spot = self.spot
        if self.direct:
            return
        for i in range(1, LINKS):
            piece = quarter(self.block(i), spot.turned(self.axis))
            await_bytes(piece, self.sem(1, 1 + self.axis, i - 1))
            send(piece, piece, self.sem(0, 3, i - 1), self.sem(1, 3, i - 1), spot.beside(1 - self.axis))

    def beside(self):
        spot = self.spot
        for i in range(1, LINKS):
            block = self.block(i)
            piece = quarter(block, spot.rep)
            if self.direct:
                await_bytes(piece, self.sem(1, 1 + self.axis, i - 1))
            await_bytes(piece, self.sem(1, 2 - self.axis, i - 1))
            await_bytes(piece, self.sem(1, 3, i - 1))
            send(block, block, self.sem(0, 4, i), self.sem(1, 4, i), spot.sibling())

    def finish(self):
        for i in range(LINKS):
            await_bytes(self.other(i), self.sem(1, 4, i))

    def close(self):
        piece = quarter(self.block(0), self.spot.rep)
        for kind in range(4):
            for i in range(1, LINKS):
                await_bytes(piece, self.sem(0, kind, i - 1))
        for i in range(LINKS):
            await_bytes(self.block(i), self.sem(0, 4, i))


class Reduce:
    KINDS = (LINKS, 1, 1, LINKS - 1, REPS - 1)
    SEMS = 2 * sum(KINDS)
    STAGES = ("start", "first", "second", "along", "spread", "finish")

    def __init__(self, spot, place, out, core_sum, halves, quarters, links, axis, sems):
        self.spot, self.place, self.out, self.axis, self.sems = spot, place, out, axis, sems
        self.core_sum, self.halves, self.quarters, self.links = core_sum, halves, quarters, links

    def sem(self, side, kind, i):
        return self.sems.at[side * (self.SEMS // 2) + sum(self.KINDS[:kind]) + i]

    def start(self):
        spot = self.spot
        for z in range(LINKS):
            send(self.place(z * 2 + (1 - spot.core)), self.core_sum.at[z], self.sem(0, 0, z), self.sem(1, 0, z), spot.sibling())

    def first(self):
        spot = self.spot
        for z in range(LINKS):
            total = self.core_sum.at[z]
            await_bytes(total, self.sem(1, 0, z))
            total[...] = (total[...].astype(full) + self.place(z * 2 + spot.core)[...].astype(full)).astype(low)
        theirs = half(self.core_sum, spot.turned(self.axis), self.axis)
        send(theirs, self.halves, self.sem(0, 1, 0), self.sem(1, 1, 0), spot.beside(self.axis))

    def second(self):
        spot = self.spot
        await_bytes(self.halves, self.sem(1, 1, 0))
        mine = half(self.core_sum, spot.rep, self.axis)
        self.halves[...] = (self.halves[...].astype(full) + mine[...].astype(full)).astype(low)
        theirs = half(self.halves, spot.turned(1 - self.axis), 1 - self.axis)
        send(theirs, self.quarters, self.sem(0, 2, 0), self.sem(1, 2, 0), spot.beside(1 - self.axis))

    def along(self):
        spot = self.spot
        await_bytes(self.quarters, self.sem(1, 2, 0))
        mine = half(self.halves, spot.rep, 1 - self.axis)
        self.quarters[...] = (self.quarters[...].astype(full) + mine[...].astype(full)).astype(low)
        for i in range(1, LINKS):
            send(self.quarters.at[(spot.z + i) % LINKS], self.links.at[i - 1], self.sem(0, 3, i - 1), self.sem(1, 3, i - 1), spot.along_z(i))

    def spread(self):
        spot = self.spot
        total = self.quarters[spot.z].astype(full)
        for i in range(1, LINKS):
            await_bytes(self.links.at[i - 1], self.sem(1, 3, i - 1))
            total = total + self.links[i - 1].astype(full)
        mine = quarter(self.out, spot.rep)
        mine[...] = total.astype(low)
        for j in range(1, REPS):
            send(mine, mine, self.sem(0, 4, j - 1), self.sem(1, 4, j - 1), ((spot.rep + j) % REPS, spot.shard))

    def finish(self):
        for j in range(1, REPS):
            await_bytes(quarter(self.out, (self.spot.rep - j + REPS) % REPS), self.sem(1, 4, j - 1))

    def close(self):
        for z in range(LINKS):
            await_bytes(self.core_sum.at[z], self.sem(0, 0, z))
        await_bytes(self.halves, self.sem(0, 1, 0))
        await_bytes(self.quarters, self.sem(0, 2, 0))
        for i in range(1, LINKS):
            await_bytes(self.links.at[i - 1], self.sem(0, 3, i - 1))
        for j in range(1, REPS):
            await_bytes(quarter(self.out, self.spot.rep), self.sem(0, 4, j - 1))


class ReduceDirect(Reduce):
    KINDS = (LINKS, REPS - 1, 0, LINKS - 1, REPS - 1)
    SEMS = 2 * sum(KINDS)

    def peers(self):
        spot = self.spot
        return (spot.turned(0), spot.turned(1), REPS - 1 - spot.rep)

    def first(self):
        spot = self.spot
        for z in range(LINKS):
            total = self.core_sum.at[z]
            await_bytes(total, self.sem(1, 0, z))
            total[...] = (total[...].astype(full) + self.place(z * 2 + spot.core)[...].astype(full)).astype(low)
        for j, rep in enumerate(self.peers()):
            send(quarter(self.core_sum, rep), self.halves.at[j], self.sem(0, 1, j), self.sem(1, 1, j), (rep, spot.shard))

    def second(self):
        pass

    def along(self):
        spot = self.spot
        total = quarter(self.core_sum, spot.rep)[...].astype(full)
        for j in range(REPS - 1):
            await_bytes(self.halves.at[j], self.sem(1, 1, j))
            total = total + self.halves[j].astype(full)
        self.quarters[...] = total.astype(low)
        for i in range(1, LINKS):
            send(self.quarters.at[(spot.z + i) % LINKS], self.links.at[i - 1], self.sem(0, 3, i - 1), self.sem(1, 3, i - 1), spot.along_z(i))

    def close(self):
        for z in range(LINKS):
            await_bytes(self.core_sum.at[z], self.sem(0, 0, z))
        for j in range(REPS - 1):
            await_bytes(self.halves.at[j], self.sem(0, 1, j))
        for i in range(1, LINKS):
            await_bytes(self.links.at[i - 1], self.sem(0, 3, i - 1))
        for j in range(1, REPS):
            await_bytes(quarter(self.out, self.spot.rep), self.sem(0, 4, j - 1))


class ReduceSmall:
    KINDS = (LINKS, LINKS - 1, REPS - 1)
    SEMS = 2 * sum(KINDS)
    STAGES = ("start", "first", "second", "along")

    def __init__(self, spot, terms, out, core_sum, links, parts, sems):
        self.spot, self.terms, self.out, self.core_sum, self.links, self.parts, self.sems = spot, terms, out, core_sum, links, parts, sems

    sem = Reduce.sem

    def start(self):
        spot = self.spot
        for z in range(LINKS):
            send(self.terms.at[z * 2 + (1 - spot.core)], self.core_sum.at[z], self.sem(0, 0, z), self.sem(1, 0, z), spot.sibling())

    def first(self):
        spot = self.spot
        for z in range(LINKS):
            await_bytes(self.core_sum.at[z], self.sem(1, 0, z))
            self.core_sum[z] = self.core_sum[z] + self.terms[z * 2 + spot.core]
        for i in range(1, LINKS):
            send(self.core_sum.at[(spot.z + i) % LINKS], self.links.at[i - 1], self.sem(0, 1, i - 1), self.sem(1, 1, i - 1), spot.along_z(i))

    def second(self):
        spot = self.spot
        total = self.core_sum[spot.z]
        for i in range(1, LINKS):
            await_bytes(self.links.at[i - 1], self.sem(1, 1, i - 1))
            total = total + self.links[i - 1]
        self.parts[spot.rep] = total
        mine = self.parts.at[spot.rep]
        for j in range(1, REPS):
            send(mine, mine, self.sem(0, 2, j - 1), self.sem(1, 2, j - 1), ((spot.rep + j) % REPS, spot.shard))

    def along(self):
        for j in range(1, REPS):
            await_bytes(self.parts.at[(self.spot.rep - j + REPS) % REPS], self.sem(1, 2, j - 1))
        total = self.parts[0]
        for j in range(1, REPS):
            total = total + self.parts[j]
        self.out[...] = total

    def close(self):
        for z in range(LINKS):
            await_bytes(self.core_sum.at[z], self.sem(0, 0, z))
        for i in range(1, LINKS):
            await_bytes(self.links.at[i - 1], self.sem(0, 1, i - 1))
        for j in range(1, REPS):
            await_bytes(self.parts.at[self.spot.rep], self.sem(0, 2, j - 1))


OWNED = C // OWNERS
SLOTS = TILES + 1
GATHERS = 2 * TILES + 1 + GROUPS
REDUCES = 2 * TILES + 1 + (GROUPS - 1) + 3
W_Q0, W_Q1, W_Q2, W_P, W_U0, W_D0, W_U1, W_D1, W_U2, W_D2 = W_ALL = range(10)
G_D0, G_U0, G_D1, G_U1, G_D2, G_U2, G_P, G_Q0, G_Q1, G_Q2, G_K2, G_V2, G_S = G_ALL = range(10, 23)
W_Q, W_U, W_D = (W_Q0, W_Q1, W_Q2), (W_U0, W_U1, W_U2), (W_D0, W_D1, W_D2)
G_D, G_U, G_Q, G_LAST = (G_D0, G_D1, G_D2), (G_U0, G_U1, G_U2), (G_Q0, G_Q1), (G_Q2, G_K2, G_V2)
START, ACROSS, RELAY, BESIDE, ARRIVED = range(5)
FIRST, SECOND, ALONG, SPREAD, SUMMED = range(1, 6)
BEFORE = {
    2: ((W_Q0, ACROSS), (W_P, START),),
    3: ((W_Q2, START),),
    4: ((W_Q0, RELAY), (W_U0, START),),
    5: ((W_Q0, BESIDE), (W_Q1, ACROSS),),
}
FORWARD = {
    0: ((W_Q1, RELAY), (W_Q2, ACROSS), (W_P, ACROSS), (W_D0, START), (W_U1, START),),
    2: ((W_D1, START),),
    4: ((W_Q1, BESIDE),),
    5: ((W_U0, ACROSS),),
    6: ((W_Q2, RELAY),),
    7: ((W_P, RELAY),),
    8: ((W_D0, ACROSS),),
    11: ((W_Q2, BESIDE), (W_U0, RELAY),),
    12: ((W_U1, ACROSS),),
    14: ((W_D0, RELAY), (W_U2, START), (W_D2, START),),
    16: ((W_D1, ACROSS),),
    17: ((W_P, BESIDE), (W_U0, BESIDE),),
    18: ((W_U1, RELAY),),
}
MIDDLE = {
    0: ((W_D0, BESIDE), (W_U2, ACROSS),),
    1: ((W_D1, RELAY),),
    2: ((W_U1, BESIDE), (W_D2, ACROSS),),
}
TILE_STEP = {
    1: ((W_D1, BESIDE), (W_U2, RELAY), (W_D2, RELAY),),
    2: ((W_U2, BESIDE), (W_D2, BESIDE),),
    3: ((G_D0, FIRST), (G_U0, FIRST),),
    5: ((G_D0, SECOND), (G_U0, SECOND), (G_D1, FIRST), (G_U1, FIRST),),
}
AFTER_TILES = {
    0: ((G_D0, ALONG), (G_U0, ALONG),),
    2: ((G_D2, FIRST), (G_U2, FIRST),),
    3: ((G_U1, SECOND),),
}
BACKWARD = {
    2: ((G_D0, SPREAD), (G_U0, SPREAD),),
    3: ((G_D1, SECOND), (G_P, FIRST),),
    7: ((G_D2, SECOND),),
    8: ((G_U2, SECOND),),
    9: ((G_U1, ALONG),),
    10: ((G_Q0, FIRST),),
    11: ((G_U0, SUMMED), (G_D1, ALONG),),
    12: ((G_D0, SUMMED),),
    14: ((G_D2, ALONG), (G_P, SECOND),),
    16: ((G_U1, SPREAD), (G_Q0, SECOND),),
    17: ((G_D1, SPREAD), (G_U2, ALONG), (G_Q1, FIRST),),
    20: ((G_D2, SPREAD), (G_P, ALONG),),
}
LAST_STEPS = {
    0: ((G_Q2, FIRST), (G_Q2, SECOND), (G_K2, FIRST),),
    1: ((G_U2, SPREAD), (G_P, SPREAD), (G_Q0, ALONG), (G_V2, FIRST),),
    2: ((G_D1, SUMMED),),
    3: ((G_U1, SUMMED), (G_Q0, SPREAD), (G_Q1, SECOND), (G_K2, SECOND), (G_V2, SECOND),),
}


def chunk_shapes():
    out = []
    for _ in range(TILES):
        out += [(128, C), (OWNED, TILE)]
    return out + [(OWNED, C)] + [(3, OWNED, GCOLS)] * (GROUPS - 1) + [(OWNED, GCOLS)] * 3


def reduce_scratch():
    out = []
    for i, dims in enumerate(chunk_shapes()):
        *lead, rows, cols = dims
        near = (rows, cols // 2) if i % 2 == 0 else (rows // 2, cols)
        near = (LINKS, *lead, *near) if i < REDUCES - 3 else (REPS - 1, LINKS, *lead, rows // 2, cols // 2)
        out.append(pltpu.VMEM((LINKS, *dims), low))
        out.append(pltpu.VMEM(near, low))
        out.append(pltpu.VMEM((LINKS, *lead, rows // 2, cols // 2), low))
        out.append(pltpu.VMEM((LINKS - 1, *lead, rows // 2, cols // 2), low))
    out += [pltpu.VMEM((LINKS, 40, 128), full), pltpu.VMEM((LINKS - 1, 40, 128), full), pltpu.VMEM((REPS, 40, 128), full)]
    return out


def layer_kernel(windows, x_hbm, dy_hbm, count_ref, q32, p32, u32, d32, vec_in, tab_in, line_ref, mask_ref,
                 out_hbm, grad_hbm, gq_out, gp_out, gu_out, gd_out, gs_out, qkv_hbm, pt_hbm, n1t_hbm, *scratch):
    wq, wp, up, down, small, o_ref, x1_ref, vec_ref, sums_ref, terms_ref = scratch[:10]
    gather_sems, reduce_sems, small_sems, small_reduce_sems, local = scratch[-5:]
    reduce_refs = scratch[10:-5]
    spot = Spot()
    rows_all = windows * TOK

    def live(w):
        return (w < count_ref[0]).astype(full)

    mine = spot.shard
    V = pltpu.VMEM

    jobs = {}
    places = [(W_Q[g], lambda s, g=g: wq.at[g, :, s]) for g in range(GROUPS)] + [(W_P, lambda s: wp.at[s])]
    for t in range(TILES):
        places += [(W_U[t], lambda s, t=t: up.at[t, s]), (W_D[t], lambda s, t=t: down.at[t, s])]
    for i, (name, place) in enumerate(places):
        jobs[name] = Gather(spot, place, i % 2, gather_sems.at[i], direct=name == W_Q0)
    places = []
    for t in range(TILES):
        slot = (t + SLOTS - 1) % SLOTS
        places.append((G_D[t], lambda s, slot=slot: down.at[slot, s], gd_out.at[t]))
        places.append((G_U[t], lambda s, slot=slot: up.at[slot, s], gu_out.at[t]))
    places.append((G_P, lambda s: wp.at[s], gp_out))
    for g in range(GROUPS - 1):
        places.append((G_Q[g], lambda s, g=g: wq.at[g, :, s], gq_out.at[g]))
    for part in range(3):
        places.append((G_LAST[part], lambda s, part=part: up.at[TILES - 1, s, :, pl.ds(part * GCOLS, GCOLS)], gq_out.at[GROUPS - 1, part]))
    for i, (name, place, out) in enumerate(places):
        kind = ReduceDirect if name in G_LAST else Reduce
        jobs[name] = kind(spot, place, out, *reduce_refs[4 * i : 4 * i + 4], i % 2, reduce_sems.at[i])
    jobs[G_S] = ReduceSmall(spot, terms_ref, gs_out, *reduce_refs[-3:], small_reduce_sems)

    done = {}

    def run(name, upto):
        for stage in range(done.get(name, 0), upto + 1):
            getattr(jobs[name], jobs[name].STAGES[stage])()
        done[name] = max(done.get(name, 0), upto + 1)

    def hook(table, place):
        for item in table.get(place, ()):
            run(*item)

    def hook_window(table, g, w):
        for at in range(windows):
            place = g * windows + at
            if place in table:

                @pl.when(w == at)
                def _(place=place):
                    hook(table, place)

    barrier, peers = greet(spot)

    def cast(q_v, p_v, u_v, d_v):
        loads = [pltpu.make_async_copy(a, b, local.at[i]) for i, (a, b) in enumerate(((q32, q_v), (p32, p_v), (u32, u_v), (d32, d_v)))]
        for load in loads:
            load.start()
        small[mine] = jnp.zeros((48, 128), low)
        pad = jnp.zeros((16, 128), full)
        vec_ref[:, 0:128] = pad
        vec_ref[0:12, 0:OWNED] = vec_in[...]
        small[mine, 0:16, :] = vec_ref[:, 0:128].astype(low)
        x1_ref[0:32, 0:128] = jnp.zeros((32, 128), full)
        x1_ref[0:HEADS, 0 : tab_in.shape[1]] = tab_in[...]
        small[mine, 16:48, :] = x1_ref[0:32, 0:128].astype(low)
        loads[0].wait()
        for g in range(GROUPS):
            for part in range(3):
                wq[g, part, mine] = q_v[:, part * C + g * GCOLS : part * C + (g + 1) * GCOLS].astype(low)
        pl.semaphore_wait(barrier, peers)
        for i in range(1, OWNERS):
            send(small.at[mine], small.at[mine], small_sems.at[i], small_sems.at[OWNERS + i], (spot.rep, (mine + i) % OWNERS))
        run(W_Q0, START)
        run(W_Q1, START)
        loads[1].wait()
        wp[mine] = p_v[...].astype(low)
        loads[2].wait()
        loads[3].wait()
        for t in range(TILES):
            for s in range(OWNERS):
                src = (MLP // OWNERS) * s + 128 * t
                up[t, mine, :, s * 128 : (s + 1) * 128] = u_v[:, src : src + 128].astype(low)
            down[t, mine] = d_v[t * 128 : (t + 1) * 128, :].astype(low)

    pl.run_scoped(cast, V((OWNED, 3 * C), full), V((OWNED, C), full), V((OWNED, MLP), full), V((TILES * 128, C), full))

    def forward(dy_ref, dyt_ref, x_ref, n1_ref, n1t_ref, qkv_ref, pt_ref, bias_ref):
        load = pltpu.make_async_copy(x_hbm, x_ref, local.at[0])
        load.start()
        load_dy = pltpu.make_async_copy(dy_hbm, dy_ref.at[0:rows_all], local.at[2])
        load_dy.start()
        zero_tail(n1_ref, windows)
        zero_tail(dy_ref, windows)
        zero_tail(o_ref, windows)
        for i in range(1, OWNERS):
            await_bytes(small.at[(mine - i + OWNERS) % OWNERS], small_sems.at[OWNERS + i])
        tab = unpack_small(small, vec_ref)
        hook(BEFORE, 0)
        load.wait()
        hook(BEFORE, 1)

        def first_norm(w, carry):
            xhat, _ = norm_parts(x_ref[window_rows(w), :].astype(full))
            n1_ref[window_rows(w), :] = (xhat * vec_ref[0:1, :] + vec_ref[1:2, :]).astype(low)
            return carry

        lax.fori_loop(0, windows, first_norm, 0)
        hook(BEFORE, 2)
        transpose_rows(n1_ref, n1t_ref)
        save = pltpu.make_async_copy(n1t_ref, n1t_hbm, local.at[1])
        save.start()
        hook(BEFORE, 3)
        load_dy.wait()

        def keep_live(w, carry):
            dy_ref[window_rows(w), :] = (dy_ref[window_rows(w), :].astype(full) * live(w)).astype(low)
            return carry

        lax.fori_loop(0, windows, keep_live, 0)
        transpose_rows(dy_ref, dyt_ref)
        hook(BEFORE, 4)

        def bias(tmp_ref):
            spread_table(tab, line_ref, tmp_ref)
            hook(BEFORE, 5)
            place_bias(tmp_ref, bias_ref)

        pl.run_scoped(bias, V((2, TOK * HEADS, 128), full))
        for g in range(GROUPS):
            cols = slice(g * GCOLS, (g + 1) * GCOLS)
            held = qkv_ref.at[g % 2]
            if g >= 2:
                pltpu.make_async_copy(held, qkv_hbm.at[g - 2], local.at[2 + g % 2]).wait()
            run(W_Q[g], ARRIVED)
            n1 = n1_ref[...]
            held[0] = ((dot(n1, flat(wq[g, 0])) + vec_ref[2:3, cols]) * (HEAD_DIM**-0.5)).astype(low)
            held[1] = dot(n1, flat(wq[g, 1])).astype(low)
            held[2] = (dot(n1, flat(wq[g, 2])) + vec_ref[3:4, cols]).astype(low)
            pltpu.make_async_copy(held, qkv_hbm.at[g], local.at[2 + g % 2]).start()

            def window(w, carry, g=g, cols=cols, held=held):
                hook_window(FORWARD, g, w)
                rows = window_rows(w)
                n = g * windows + w
                slot = n % 2
                s = against_heads(held[1, rows, :], split_diag(held[0, rows, :], mask_ref)) + bias_ref[g]
                e = jnp.exp(s - jnp.max(s, 0, keepdims=True))
                p = (e * (1.0 / jnp.sum(e, 0, keepdims=True))).astype(low)
                keep = pltpu.make_async_copy(pt_ref.at[slot], pt_hbm.at[n], local.at[4 + slot])

                @pl.when(n >= 2)
                def _():
                    keep.wait()

                pt_ref[slot] = p
                keep.start()
                o_ref[rows, cols] = undiag(held[2, rows, :].T, p, mask_ref).astype(low)
                return carry

            lax.fori_loop(0, windows, window, 0)

        run(W_P, ARRIVED)

        x1_ref[...] = x_ref[...].astype(full) + (dot(o_ref[0:rows_all], flat(wp[...])) + vec_ref[4:5, :])
        save.wait()
        for g in (GROUPS - 2, GROUPS - 1):
            pltpu.make_async_copy(qkv_ref.at[g % 2], qkv_hbm.at[g], local.at[2 + g % 2]).wait()
        for slot in range(2):
            pltpu.make_async_copy(pt_ref.at[slot], pt_hbm.at[0], local.at[4 + slot]).wait()

    def middle(dy_ref, dyt_ref, n2_ref, n2t_ref, y_ref, dn_ref, bu_ref, bsum_ref):
        zero_tail(n2_ref, windows)
        hook(MIDDLE, 0)

        def second_norm(w, carry):
            rows = window_rows(w)
            xhat, _ = norm_parts(x1_ref[rows, :])
            n2_ref[rows, :] = (xhat * vec_ref[5:6, :] + vec_ref[6:7, :]).astype(low)
            return carry

        lax.fori_loop(0, windows, second_norm, 0)
        transpose_rows(n2_ref, n2t_ref)
        hook(MIDDLE, 1)
        n2t_ref[C:, :] = jnp.ones((16, ROWS), low)
        y_ref[...] = jnp.zeros_like(y_ref)
        dn_ref[...] = jnp.zeros_like(dn_ref)
        for t in range(TILES):
            for s in range(TILE // 128):
                row, left = hidden_place(t, s)
                bu_ref[t, :, s * 128 : (s + 1) * 128] = vec_ref[row : row + 1, left : left + 128]
        hook(MIDDLE, 2)
        run(W_U0, ARRIVED)
        run(W_D0, ARRIVED)
        hook(TILE_STEP, 0)
        halves = TILE // SUB

        def step(i, carry):
            for k in range(1, TILES * halves):

                @pl.when(i == k)
                def _(k=k):
                    if k % halves == 0:
                        t = k // halves
                        for name in (W_U[t], W_D[t]):
                            run(name, ARRIVED)
                        for name in (W_U[t - 1], W_D[t - 1]):
                            jobs[name].close()
                        for name in (G_D[t - 1], G_U[t - 1]):
                            run(name, START)
                    hook(TILE_STEP, k)

            t, part = i // halves, i % halves
            cols = pl.ds(pl.multiple_of(part * SUB, SUB), SUB)
            wide = SUB // 128
            slot = (t + SLOTS - 1) % SLOTS
            u = flat(up[t, :, :, cols])
            d = flat(down[t, pl.ds(part * wide, wide)])
            h = dot(n2_ref[...], u) + bu_ref[t, :, cols]
            da = dot_nt(dy_ref[...], d)
            act, slope = gelu_both(h)
            a = act.astype(low)
            dh = (da * slope).astype(low)
            y_ref[...] += dot(a, d)
            dn_ref[...] += dot_nt(dh, u)
            gd = dot(dyt_ref[...], a).astype(low)
            down[slot, pl.ds(part * wide, wide)] = blocks(gd.T, wide)
            gu = dot(n2t_ref[...], dh)
            up[slot, :, :, cols] = blocks(gu[0:C].astype(low), OWNERS)
            bsum_ref[t, :, cols] = gu[C : C + 1]
            return carry

        lax.fori_loop(0, TILES * halves, step, 0)
        run(G_D[-1], START)
        run(G_U[-1], START)
        hook(AFTER_TILES, 0)
        sums_ref[...] = jnp.zeros_like(sums_ref)
        for t in range(TILES):
            for s in range(TILE // 128):
                row, left = hidden_place(t, s)
                sums_ref[row : row + 1, left : left + 128] = bsum_ref[t, :, s * 128 : (s + 1) * 128]
        transpose_rows(o_ref, dyt_ref)
        hook(AFTER_TILES, 1)

        def finish(w, carry):
            rows = window_rows(w)
            x1 = x1_ref[rows, :]
            xhat, scale = norm_parts(x1)
            dn = dn_ref[rows, :]
            dy = dy_ref[rows, :].astype(full)
            dx1 = dy + norm_back(xhat, scale, dn, vec_ref[5:6, :])
            dr = dx1.astype(low)
            sums_ref[4:5, :] += jnp.sum(dr.astype(full), 0, keepdims=True)
            sums_ref[5:6, :] += jnp.sum(dn * xhat, 0, keepdims=True)
            sums_ref[6:7, :] += jnp.sum(dn, 0, keepdims=True)
            sums_ref[7:8, :] += jnp.sum(dy, 0, keepdims=True)
            dy_ref[rows, :] = ((x1 + y_ref[rows, :] + vec_ref[7:8, :]) * live(w)).astype(low)
            x1_ref[rows, :] = dx1
            n2_ref[rows, :] = dr
            return carry

        lax.fori_loop(0, windows, finish, 0)
        o_ref[...] = dot_nt(n2_ref[...], flat(wp[...])).astype(low)
        save = pltpu.make_async_copy(dy_ref.at[0:rows_all], out_hbm, local.at[0])
        save.start()
        hook(AFTER_TILES, 2)
        jobs[W_P].close()
        for g in range(GROUPS):
            cols = slice(g * GCOLS, (g + 1) * GCOLS)
            wp[:, :, cols] = blocks(dot(dyt_ref[...], n2_ref[:, cols]).astype(low), OWNERS)
        run(G_P, START)
        hook(AFTER_TILES, 3)
        save.wait()

    def both(dy_ref, dyt_ref):
        pl.run_scoped(functools.partial(forward, dy_ref, dyt_ref), V((rows_all, C), low), V((ROWS, C), low), V((C, ROWS), low),
                      V((2, 3, ROWS, GCOLS), low), V((2, TOK, PACK), low), V((GROUPS, TOK, PACK), full))
        pl.run_scoped(functools.partial(middle, dy_ref, dyt_ref), V((ROWS, C), low), V((C + 16, ROWS), low), V((ROWS, C), full), V((ROWS, C), full),
                      V((TILES, 1, TILE), full), V((TILES, 1, TILE), full))

    pl.run_scoped(both, V((ROWS, C), low), V((C, ROWS), low))

    def backward(x_ref, n1t_ref, qkv_ref, pt_ref, dproj_ref, dn_ref, bias_ref):
        loads = [pltpu.make_async_copy(x_hbm, x_ref, local.at[0]), pltpu.make_async_copy(n1t_hbm, n1t_ref, local.at[1])]
        fetch = [pltpu.make_async_copy(qkv_hbm.at[g], qkv_ref.at[g % 2], local.at[2 + g % 2]) for g in range(GROUPS)]
        fetch[0].start()
        pltpu.make_async_copy(pt_hbm.at[0], pt_ref.at[0], local.at[4]).start()
        fetch[1].start()
        for load in loads:
            load.start()
        bias_ref[...] = jnp.zeros_like(bias_ref)
        dn_ref[...] = jnp.zeros_like(dn_ref)
        for part in range(3):
            dproj_ref[part, rows_all:, :] = jnp.zeros((ROWS - rows_all, GCOLS), low)
        for g in range(GROUPS):
            cols = slice(g * GCOLS, (g + 1) * GCOLS)
            held = qkv_ref.at[g % 2]
            fetch[g].wait()

            def window(w, carry, g=g, cols=cols, held=held):
                hook_window(BACKWARD, g, w)
                rows = window_rows(w)
                n = g * windows + w
                slot = n % 2

                @pl.when(n + 1 < GROUPS * windows)
                def _():
                    pltpu.make_async_copy(pt_hbm.at[n + 1], pt_ref.at[1 - slot], local.at[5 - slot]).start()

                pltpu.make_async_copy(pt_hbm.at[n], pt_ref.at[slot], local.at[4 + slot]).wait()
                q = held[0, rows, :]
                k = held[1, rows, :]
                v = held[2, rows, :]
                p = pt_ref[slot]
                do = split_diag(o_ref[rows, cols], mask_ref)
                dp = against_heads(v, do)
                dv = over_queries(p, do).astype(low)
                pf = p.astype(full)
                ds = (pf * (dp - jnp.sum(pf * dp, 0, keepdims=True))).astype(low)
                bias_ref[g] += ds.astype(full)
                dproj_ref[1, rows, :] = over_queries(ds, split_diag(q, mask_ref)).astype(low)
                dq = (undiag(k.T, ds, mask_ref) * (HEAD_DIM**-0.5)).astype(low)
                dproj_ref[0, rows, :] = dq
                dproj_ref[2, rows, :] = dv
                sums_ref[2:3, cols] += jnp.sum(dq.astype(full), 0, keepdims=True)
                sums_ref[3:4, cols] += jnp.sum(dv.astype(full), 0, keepdims=True)
                return carry

            lax.fori_loop(0, windows, window, 0)
            if g + 2 < GROUPS:
                fetch[g + 2].start()
            if g == 0:
                for load in loads:
                    load.wait()
            jobs[W_Q[g]].close()
            if g == GROUPS - 1:
                jobs[W_U[-1]].close()
                for part in range(3):
                    up[TILES - 1, :, :, part * GCOLS : (part + 1) * GCOLS] = blocks(dot(n1t_ref[...], dproj_ref[part]).astype(low), OWNERS)
                    run(G_LAST[part], START)
                hook(LAST_STEPS, 0)
                for part in range(3):
                    dn_ref[...] += dot_nt(dproj_ref[part], flat(wq[g, part]))
            else:
                for part in range(3):
                    d = dproj_ref[part]
                    dn_ref[...] += dot_nt(d, flat(wq[g, part]))
                    wq[g, part] = blocks(dot(n1t_ref[...], d).astype(low), OWNERS)
                run(G_Q[g], START)

        def last_norm(grad_ref):
            def finish(w, carry):
                rows = window_rows(w)
                slot = w % 2
                xhat, scale = norm_parts(x_ref[rows, :].astype(full))
                dn = dn_ref[rows, :]
                save = pltpu.make_async_copy(grad_ref.at[slot], grad_hbm.at[rows], local.at[4 + slot])

                @pl.when(w >= 2)
                def _():
                    save.wait()

                grad_ref[slot] = x1_ref[rows, :] + norm_back(xhat, scale, dn, vec_ref[0:1, :])
                save.start()
                sums_ref[0:1, :] += jnp.sum(dn * xhat, 0, keepdims=True)
                sums_ref[1:2, :] += jnp.sum(dn, 0, keepdims=True)
                return carry

            lax.fori_loop(0, windows, finish, 0)
            hook(LAST_STEPS, 1)
            for slot in range(2):
                pltpu.make_async_copy(grad_ref.at[slot], grad_hbm.at[pl.ds(0, TOK)], local.at[4 + slot]).wait()

        pl.run_scoped(last_norm, V((2, TOK, C), full))
        hook(LAST_STEPS, 2)

        def table(tmp_ref):
            pack_small(sums_ref[...], table_grad(line_ref, tmp_ref, bias_ref), terms_ref)

        pl.run_scoped(table, V((2, TOK * HEADS, 128), full))
        run(G_S, START)
        hook(LAST_STEPS, 3)
        for stage in range(len(Reduce.STAGES)):
            for name in G_ALL:
                if stage < len(jobs[name].STAGES):
                    run(name, stage)

    pl.run_scoped(backward, V((rows_all, C), low), V((C, ROWS), low), V((2, 3, ROWS, GCOLS), low), V((2, TOK, PACK), low), V((3, ROWS, GCOLS), low),
                  V((ROWS, C), full), V((GROUPS, TOK, PACK), full))
    jobs[W_D[-1]].close()
    for i in range(1, OWNERS):
        await_bytes(small.at[mine], small_sems.at[i])
    for name in G_ALL:
        jobs[name].close()


def shape(dims, kind):
    return jax.ShapeDtypeStruct(dims, kind)


def adamw(weight, moment, second, gradient, step_rate):
    moment_new = beta_one * moment + (1.0 - beta_one) * gradient
    second_new = beta_two * second + (1.0 - beta_two) * gradient * gradient
    update = moment_new * (1.0 / (1.0 - beta_one**STEP)) / (jnp.sqrt(second_new * (1.0 / (1.0 - beta_two**STEP))) + adam_eps)
    weight_new = weight * (1.0 - step_rate * weight_decay) - step_rate * update
    return (weight_new, moment_new, second_new)


def update_kernel(*refs):
    gq, gp, gu, gd, gs = refs[:5]
    ins = [refs[5 + 3 * i : 8 + 3 * i] for i in range(6)]
    outs = [refs[25 + 4 * i : 29 + 4 * i] for i in range(4)] + [refs[41:44], refs[44:47]]
    for i in range(2):
        refs[47 + i][...] = refs[23 + i][...]

    def piece(which, place, gradient):
        new = adamw(*(ref[place] for ref in ins[which]), gradient, step_rates[which])
        for ref, value in zip(outs[which], new):
            ref[place] = value
        if which < 4:
            outs[which][3][place] = new[0].astype(low)

    for part in range(3):
        for g in range(GROUPS):
            left = part * C + g * GCOLS
            piece(0, (slice(None), slice(left, left + GCOLS)), gq[g, part].astype(full))
    piece(1, (slice(None), slice(None)), gp[...].astype(full))
    for t in range(TILES):
        for s in range(OWNERS):
            left = (MLP // OWNERS) * s + 128 * t
            piece(2, (slice(None), slice(left, left + 128)), gu[t, :, s * 128 : (s + 1) * 128].astype(full))
    piece(3, (slice(None), slice(None)), gd[0].astype(full))

    @pl.when(pl.program_id(0) == 0)
    def _():
        every = (slice(None), slice(None))
        piece(4, every, gs[0:12, 0:OWNED])
        piece(5, every, gs[16:40, 0 : ins[5][0].shape[1]])


def update(gq, gp, gu, gd, gs, states, results):
    steps = OWNED // 16

    def rows_of(array):
        tall = array.shape[0] // steps
        return pl.BlockSpec((tall, array.shape[1]), lambda i: (i, 0))

    def whole(array):
        return pl.BlockSpec(array.shape, lambda i: (0, 0))

    per_tile = 128 * TILES // steps
    specs = [
        pl.BlockSpec((GROUPS, 3, 16, GCOLS), lambda i: (0, 0, i, 0)),
        pl.BlockSpec((16, C), lambda i: (i, 0)),
        pl.BlockSpec((TILES, 16, TILE), lambda i: (0, i, 0)),
        pl.BlockSpec((1, per_tile, C), lambda i: (i // (128 // per_tile), i % (128 // per_tile), 0)),
        whole(gs),
    ]
    out_shapes, out_specs = [], []
    for i, group in enumerate(states):
        for array in group:
            specs.append(rows_of(array) if i < 4 else whole(array))
            out_shapes.append(shape(array.shape, full))
            out_specs.append(specs[-1])
        if i < 4:
            out_shapes.append(shape(group[0].shape, low))
            out_specs.append(rows_of(group[0]))
    results = [array.reshape(steps, -1, C) for array in results]
    for array in results:
        specs.append(pl.BlockSpec((1, *array.shape[1:]), lambda i: (i, 0, 0)))
        out_shapes.append(shape(array.shape, array.dtype))
        out_specs.append(specs[-1])
    return pl.pallas_call(
        update_kernel,
        grid=(steps,),
        in_specs=specs,
        out_specs=out_specs,
        out_shape=out_shapes,
        compiler_params=pltpu.CompilerParams(vmem_limit_bytes=63 * MIB),
        name="update",
    )(gq, gp, gu, gd, gs, *[array for group in states for array in group], *results)


def shards(
    tokens, out_grad, window_count,
    qkv_weight, qkv_first, qkv_second,
    output_weight, output_first, output_second,
    up_weight, up_first, up_second,
    down_weight, down_first, down_second,
    vectors, vector_first, vector_second,
    bias_table, table_first, table_second,
):
    windows = tokens.shape[0]
    rows = windows * TOK
    V = pltpu.VMEM
    D = pltpu.SemaphoreType.DMA
    hbm = pl.BlockSpec(memory_space=pl.ANY)
    vmem = pl.BlockSpec(memory_space=pltpu.VMEM)
    result = pl.pallas_call(
        functools.partial(layer_kernel, windows),
        out_shape=[
            shape((rows, C), low), shape((rows, C), full),
            shape((GROUPS, 3, OWNED, GCOLS), low), shape((OWNED, C), low), shape((TILES, OWNED, TILE), low), shape((TILES, 128, C), low),
            shape((40, 128), full),
            shape((GROUPS, 3, ROWS, GCOLS), low), shape((GROUPS * windows, TOK, PACK), low), shape((C, ROWS), low)],
        in_specs=[hbm, hbm, pl.BlockSpec(memory_space=pltpu.SMEM)] + [hbm] * 4 + [vmem] * 4,
        out_specs=[hbm, hbm] + [vmem] * 5 + [hbm] * 3,
        scratch_shapes=[
            V((GROUPS, 3, OWNERS, OWNED, GCOLS), low), V((OWNERS, OWNED, C), low), V((SLOTS, OWNERS, OWNED, TILE), low),
            V((SLOTS, OWNERS, 128, C), low), V((OWNERS, 48, 128), low), V((ROWS, C), low), V((rows, C), full), V((16, C), full), V((16, C), full),
            V((OWNERS, 40, 128), full)]
        + reduce_scratch()
        + [D((GATHERS, Gather.SEMS)), D((REDUCES, ReduceDirect.SEMS)), D((2 * OWNERS,)), D((ReduceSmall.SEMS,)), D((6,))],
        compiler_params=pltpu.CompilerParams(vmem_limit_bytes=63 * MIB, collective_id=0, has_side_effects=True),
        name="layer",
    )(tokens.reshape(rows, C), out_grad.reshape(rows, C), window_count, qkv_weight, output_weight, up_weight, down_weight, vectors, bias_table.T,
      jnp.asarray(line_matrix(), low), jnp.asarray(head_masks(), low))
    out, grad, gq, gp, gu, gd, gs = result[:7]
    new = update(gq, gp, gu, gd, gs, (
        (qkv_weight, qkv_first, qkv_second), (output_weight, output_first, output_second), (up_weight, up_first, up_second),
        (down_weight, down_first, down_second), (vectors, vector_first, vector_second), (bias_table.T, table_first.T, table_second.T)), (out, grad))
    *new, out, grad = new
    return (out.reshape(tokens.shape), grad.reshape(tokens.shape), *new[:-3], *(array.T for array in new[-3:]))


def vmem_call(body, outs, scratch, args, name, limit=60, **params):
    spec = pl.BlockSpec(memory_space=pltpu.VMEM)
    return pl.pallas_call(
        body,
        out_shape=outs,
        in_specs=[pl.BlockSpec(memory_space=pltpu.SMEM) if a.dtype == full and a.ndim == 1 else spec for a in args],
        out_specs=[spec] * len(outs),
        scratch_shapes=scratch,
        compiler_params=pltpu.CompilerParams(vmem_limit_bytes=limit * MIB, **params),
        name=name,
    )(*args)


def local_step(tokens, out_grad, window_count, small, wq, wp, up, down):
    windows = tokens.shape[0]
    rows = windows * TOK
    owned = C // OWNERS
    V = pltpu.VMEM
    x = tokens.reshape(rows, C)
    dy = out_grad.reshape(rows, C)
    live = (jnp.arange(windows) < window_count[0]).astype(full)
    line = jnp.asarray(line_matrix(), low)
    masks = jnp.asarray(head_masks(), low)
    qkv, pt, o, x1, n1t, vec = vmem_call(
        functools.partial(attention_forward, windows),
        [shape((9, ROWS, GCOLS), low), shape((GROUPS, windows, TOK, PACK), low), shape((ROWS, C), low), shape((rows, C), full), shape((C, ROWS), low),
         shape((16, C), full)],
        [V((ROWS, C), low), V((GROUPS, TOK, PACK), full), V((2, TOK * HEADS, 128), full)],
        (x, small, line, masks, wq, wp), "attention_forward")
    out, dx1, do, gup, gdown, gout, sums = vmem_call(
        functools.partial(feed_forward, windows),
        [shape((rows, C), low), shape((ROWS, C), full), shape((rows, C), low), shape((TILES, OWNERS, owned, TILE), low),
         shape((TILES, OWNERS, C, 128), low), shape((OWNERS, owned, C), low), shape((16, C), full)],
        [V((ROWS, C), low), V((C, ROWS), low), V((ROWS, C), low), V((C, ROWS), low), V((ROWS, C), full), V((ROWS, C), full),
         V((TILES, 1, TILE), full), V((TILES, 1, TILE), full)],
        (x1, dy, live, vec, up, down, wp, o), "feed_forward")
    gq, gsmall, grad = vmem_call(
        functools.partial(attention_backward, windows),
        [shape((GROUPS, 3, OWNERS, owned, GCOLS), low), shape((OWNERS, 40, 128), full), shape((rows, C), full)],
        [V((16, C), full), V((GROUPS, TOK, PACK), full), V((2, TOK * HEADS, 128), full), V((3, ROWS, GCOLS), low), V((ROWS, C), full)],
        (x, vec, line, masks, wq, qkv, pt, do, dx1, n1t, sums), "attention_backward")
    return out.reshape(tokens.shape), grad.reshape(tokens.shape), gq, gout, gup, gdown, gsmall


def shards_general(
    tokens, out_grad, window_count,
    qkv_weight, qkv_first, qkv_second,
    output_weight, output_first, output_second,
    up_weight, up_first, up_second,
    down_weight, down_first, down_second,
    vectors, vector_first, vector_second,
    bias_table, table_first, table_second,
):
    gather = functools.partial(lax.all_gather, axis_name="shard", tiled=True)
    scatter = functools.partial(lax.psum_scatter, axis_name="shard", tiled=True)
    owned = C // OWNERS
    wq = gather(qkv_weight.astype(low), axis=0).reshape(OWNERS, owned, 3, GROUPS, GCOLS).transpose(3, 2, 0, 1, 4)
    wp = gather(output_weight.astype(low), axis=0).reshape(OWNERS, owned, C)
    up = gather(up_weight.astype(low), axis=0).reshape(OWNERS, owned, OWNERS, TILES, 128).transpose(3, 0, 1, 2, 4)
    up = up.reshape(TILES, OWNERS, owned, TILE)
    down = gather(down_weight.astype(low), axis=0).reshape(OWNERS, TILES, 128, C).transpose(1, 0, 2, 3)
    vec = gather(vectors.astype(low), axis=1)
    tab = gather(bias_table.astype(low), axis=0)
    table_rows = tab.shape[0]
    count = TAB_ROWS // OWNERS
    vec = vec.reshape(12, OWNERS, owned).transpose(1, 0, 2)
    tab = tab[:TAB_ROWS].reshape(OWNERS, count, HEADS).transpose(0, 2, 1)
    small = jnp.concatenate([jnp.pad(vec, ((0, 0), (0, 4), (0, 128 - owned))), jnp.pad(tab, ((0, 0), (0, 8), (0, 128 - count)))], 1)
    out, grad, gq, gp, gu, gd, gs = local_step(tokens, out_grad, window_count, small, wq, wp, up, down)
    gq = gq.astype(full).transpose(2, 3, 1, 0, 4).reshape(C, 3 * C)
    gu = gu.astype(full).reshape(TILES, C, OWNERS, 128).transpose(1, 2, 0, 3).reshape(C, MLP)
    gd = gd.astype(full).transpose(1, 0, 3, 2).reshape(MLP, C)
    gv = gs[:, :12, :owned].transpose(1, 0, 2).reshape(12, C)
    gb = gs[:, 16:40, :count].transpose(0, 2, 1).reshape(TAB_ROWS, HEADS)
    gb = jnp.pad(gb, ((0, table_rows - TAB_ROWS), (0, 0)))
    totals = lax.psum(
        (scatter(gq, scatter_dimension=0), scatter(gp.astype(full).reshape(C, C), scatter_dimension=0), scatter(gu, scatter_dimension=0),
         scatter(gd, scatter_dimension=0), scatter(gv, scatter_dimension=1), scatter(gb, scatter_dimension=0)), "rep")
    states = (
        (qkv_weight, qkv_first, qkv_second), (output_weight, output_first, output_second), (up_weight, up_first, up_second),
        (down_weight, down_first, down_second), (vectors, vector_first, vector_second), (bias_table, table_first, table_second))
    results = [out, grad]
    for i, (state, total, rate) in enumerate(zip(states, totals, step_rates)):
        new = adamw(*state, total, rate)
        results += [*new, new[0].astype(low)] if i < 4 else [*new]
    return tuple(results)


def solution(mesh):
    wins = P(("rep", "shard"), None, None)
    rows = P("shard", None)
    cols = P(None, "shard")
    fits = mesh.shape["rep"] == REPS and mesh.shape["shard"] == OWNERS
    return jax.shard_map(
        shards if fits else shards_general,
        mesh=mesh,
        in_specs=(wins, wins, P(("rep", "shard"))) + (rows,) * 12 + (cols,) * 3 + (rows,) * 3,
        out_specs=(wins, wins) + (rows,) * 16 + (cols,) * 3 + (rows,) * 3,
        check_vma=False,
    )
```

```python
import functools
import math

import jax
import jax.numpy as jnp
import numpy as np
from jax import lax
from jax.experimental import pallas as pl
from jax.experimental.pallas import tpu as pltpu
from jax.sharding import PartitionSpec as P

C = 768
HEADS = 24
MLP = 3072
WIN = 12
STEP = 5
HEAD_DIM = 32
SPAN = 2 * WIN - 1
TOK = WIN * WIN
TAB_ROWS = 536
ROWS = 1024
GROUPS = 3
GCOLS = 256
GHEADS = 8
PACK = GHEADS * TOK
TAB_LANES = 640
TILES = 3
TILE = MLP // TILES
SUB = 512
LINE = 384
MIB = 1 << 20

beta_one = 0.5
beta_two = 0.6
weight_decay = 0.05
adam_eps = 1e-08
norm_eps = 1e-05
step_rates = (0.04, 0.15, 0.04, 0.02, 0.2, 1.0)
low = jnp.bfloat16
full = jnp.float32
NT = (((1,), (1,)), ((), ()))


def dot(a, b):
    return jnp.dot(a, b, preferred_element_type=full)


def dot_nt(a, b):
    return lax.dot_general(a, b, NT, preferred_element_type=full)


def line_matrix():
    out = np.zeros((TAB_LANES, LINE), np.float32)
    col = np.arange(SPAN * WIN)
    out[(col // WIN) * SPAN + col % WIN + WIN - 1, col] = 1.0
    return out


def head_masks():
    lane = np.arange(GCOLS) // HEAD_DIM
    one = (lane[None, :] == np.arange(GHEADS)[:, None]).astype(np.float32)
    return np.broadcast_to(one[:, None, :], (GHEADS, 16, GCOLS))


def norm_parts(z):
    mean = jnp.sum(z, -1, keepdims=True) * (1.0 / C)
    center = z - mean
    spread = jnp.sum(center * center, -1, keepdims=True) * (1.0 / C)
    scale = lax.rsqrt(spread + norm_eps)
    return center * scale, scale


def norm_back(xhat, scale, dn, gain):
    g = dn * gain
    m1 = jnp.sum(g, -1, keepdims=True) * (1.0 / C)
    m2 = jnp.sum(g * xhat, -1, keepdims=True) * (1.0 / C)
    return scale * (g - m1 - xhat * m2)


def diag(x, mask_ref):
    head = x[0:128].reshape(8, 16, GCOLS)
    tail = x[128:144]
    parts = []
    for h in range(GHEADS):
        parts.append((head * mask_ref[h][None]).reshape(128, GCOLS))
    for h in range(GHEADS):
        parts.append(tail * mask_ref[h])
    return jnp.concatenate(parts, 0)


def undiag(xt, m, mask_ref):
    main = []
    for h in range(0, GHEADS, 2):
        r = dot(xt[h * HEAD_DIM : (h + 2) * HEAD_DIM], m[:, h * 128 : (h + 2) * 128])
        main.append(r[0:HEAD_DIM, 0:128])
        main.append(r[HEAD_DIM : 2 * HEAD_DIM, 128:256])
    main = jnp.concatenate(main, 0)
    rest = dot(xt, m[:, GHEADS * 128 :])
    rest_t = rest.T.reshape(GHEADS, 16, GCOLS)
    keep = mask_ref[...].astype(full)
    return jnp.concatenate([main.T, jnp.sum(rest_t * keep, 0)], 0)


def flat(x):
    return x.reshape(x.shape[0] * x.shape[1], x.shape[2])


def blocks(x, owners):
    return x.reshape(owners, x.shape[0] // owners, x.shape[1])


def hidden_place(t, s):
    at = (MLP // GHEADS) * s + 128 * t
    return 8 + at // C, at % C


def unpack_small(small_ref, vec_ref):
    owners = small_ref.shape[0]
    width = C // owners
    count = TAB_ROWS // owners
    vec = jnp.zeros((16, C), full)
    tab = jnp.zeros((HEADS, TAB_LANES), full)
    lane = lax.broadcasted_iota(jnp.int32, (16, 128), 1)
    lane_tab = lax.broadcasted_iota(jnp.int32, (HEADS, 128), 1)
    for s in range(owners):
        piece = small_ref[s].astype(full)
        part = jnp.where(lane < width, piece[0:16], 0.0)
        part = jnp.concatenate([part, jnp.zeros((16, C - 128), full)], 1)
        vec = vec + (pltpu.roll(part, width * s, 1) if s else part)
        part = jnp.where(lane_tab < count, piece[16 : 16 + HEADS], 0.0)
        part = jnp.concatenate([part, jnp.zeros((HEADS, TAB_LANES - 128), full)], 1)
        tab = tab + (pltpu.roll(part, count * s, 1) if s else part)
    vec_ref[...] = vec
    return tab


def pack_small(vec, tab, out_ref):
    owners = out_ref.shape[0]
    width = C // owners
    count = TAB_ROWS // owners
    for s in range(owners):
        out_ref[s, 0:16, :] = (pltpu.roll(vec, C - width * s, 1) if s else vec)[:, 0:128]
        out_ref[s, 16:40, :] = (pltpu.roll(tab, TAB_LANES - count * s, 1) if s else tab)[:, 0:128]


def spread_table(tab, line_ref, tmp_ref):
    shifted = jnp.concatenate([pltpu.roll(tab, cj, 1) if cj else tab for cj in range(WIN)], 0)
    lines = dot(shifted.astype(low), line_ref[...])
    for cj in range(WIN):
        line = lines[cj * HEADS : (cj + 1) * HEADS]
        for rj in range(WIN):
            cut = (WIN - 1 - rj) * WIN
            part = pltpu.roll(line, LINE - cut, 1) if cut else line
            row = (rj * WIN + cj) * HEADS
            tmp_ref[0, row : row + HEADS, :] = part[:, 0:128]
            tmp_ref[1, row : row + HEADS, :] = part[:, 128:256]


def place_bias(tmp_ref, bias_ref):
    lane = lax.broadcasted_iota(jnp.int32, (TOK, 128), 1)
    for g in range(GROUPS):
        rest = jnp.zeros((TOK, 128), full)
        for h in range(GHEADS):
            at = pl.ds(g * GHEADS + h, TOK, stride=HEADS)
            bias_ref[g, :, h * 128 : (h + 1) * 128] = tmp_ref[0, at, :]
            piece = tmp_ref[1, at, :]
            piece = pltpu.roll(piece, 16 * h, 1) if h else piece
            rest = jnp.where((lane >= 16 * h) & (lane < 16 * h + 16), piece, rest)
        bias_ref[g, :, GHEADS * 128 :] = rest


def table_grad(line_ref, tmp_ref, bias_ref):
    lane = lax.broadcasted_iota(jnp.int32, (TOK, 128), 1)
    for g in range(GROUPS):
        rest = bias_ref[g, :, GHEADS * 128 :]
        for h in range(GHEADS):
            at = pl.ds(g * GHEADS + h, TOK, stride=HEADS)
            tmp_ref[0, at, :] = bias_ref[g, :, h * 128 : (h + 1) * 128]
            piece = pltpu.roll(rest, 128 - 16 * h, 1) if h else rest
            tmp_ref[1, at, :] = jnp.where(lane < 16, piece, 0.0)

    def column(cj, total):
        line = jnp.zeros((HEADS, LINE), full)
        for rj in range(WIN):
            cut = (WIN - 1 - rj) * WIN
            row = pl.multiple_of((rj * WIN + cj) * HEADS, 8)
            part = jnp.concatenate([tmp_ref[0, pl.ds(row, HEADS), :], tmp_ref[1, pl.ds(row, HEADS), :], jnp.zeros((HEADS, 128), full)], 1)
            line = line + (pltpu.roll(part, cut, 1) if cut else part)
        high = line.astype(low)
        rest = (line - high.astype(full)).astype(low)
        spread = dot_nt(high, line_ref[...]) + dot_nt(rest, line_ref[...])
        return total + pltpu.roll(spread, TAB_LANES - cj, 1)

    return lax.fori_loop(0, WIN, column, jnp.zeros((HEADS, TAB_LANES), full))


def transpose_rows(src_ref, dst_ref):
    def block(i, carry):
        at = pl.multiple_of(i * 128, 128)
        dst_ref[0 : src_ref.shape[1], pl.ds(at, 128)] = src_ref[pl.ds(at, 128), :].T
        return carry

    lax.fori_loop(0, ROWS // 128, block, 0)


def window_rows(w):
    return slice(w * TOK, (w + 1) * TOK) if isinstance(w, int) else pl.ds(pl.multiple_of(w * TOK, 16), TOK)


def zero_tail(ref, windows):
    at = windows * TOK
    ref[at:ROWS, :] = jnp.zeros((ROWS - at, ref.shape[1]), ref.dtype)


def half_diag(x, half, mask_ref):
    lanes = slice(half * 128, (half + 1) * 128)
    part = x[0:128, lanes].reshape(8, 16, 128)
    heads = range(half * GHEADS // 2, (half + 1) * GHEADS // 2)
    return jnp.concatenate([(part * mask_ref[h, :, lanes][None]).reshape(128, 128) for h in heads], 0)


def rest_diag(x, mask_ref):
    return jnp.concatenate([x[128:144] * mask_ref[h] for h in range(GHEADS)], 0)


def split_diag(x, mask_ref):
    return half_diag(x, 0, mask_ref), half_diag(x, 1, mask_ref), rest_diag(x, mask_ref)


def against_heads(x, split):
    first, second, rest = split
    return jnp.concatenate([dot_nt(x[:, 0:128], first), dot_nt(x[:, 128:256], second), dot_nt(x, rest)], 1)


def over_queries(m, split):
    first, second, rest = split
    return jnp.concatenate([dot(m[:, 0:512], first), dot(m[:, 512:1024], second)], 1) + dot(m[:, 1024:], rest)


def attention_forward(windows, x_ref, small_ref, line_ref, mask_ref, wq_ref, wp_ref,
                      qkv_ref, pt_ref, o_ref, x1_ref, n1t_ref, vec_ref, n1_ref, bias_ref, tmp_ref):
    tab = unpack_small(small_ref, vec_ref)
    spread_table(tab, line_ref, tmp_ref)
    place_bias(tmp_ref, bias_ref)
    zero_tail(n1_ref, windows)
    zero_tail(o_ref, windows)

    def first_norm(w, carry):
        xhat, _ = norm_parts(x_ref[window_rows(w), :].astype(full))
        n1_ref[window_rows(w), :] = (xhat * vec_ref[0:1, :] + vec_ref[1:2, :]).astype(low)
        return carry

    lax.fori_loop(0, windows, first_norm, 0)
    transpose_rows(n1_ref, n1t_ref)

    def group(g, carry):
        cols = pl.ds(pl.multiple_of(g * GCOLS, GCOLS), GCOLS)
        n1 = n1_ref[...]
        qkv_ref[g] = ((dot(n1, flat(wq_ref[g, 0])) + vec_ref[2:3, cols]) * (HEAD_DIM**-0.5)).astype(low)
        qkv_ref[GROUPS + g] = dot(n1, flat(wq_ref[g, 1])).astype(low)
        qkv_ref[2 * GROUPS + g] = (dot(n1, flat(wq_ref[g, 2])) + vec_ref[3:4, cols]).astype(low)

        def window(w, inner):
            rows = window_rows(w)
            q = qkv_ref[g, rows, :]
            k = qkv_ref[GROUPS + g, rows, :]
            v = qkv_ref[2 * GROUPS + g, rows, :]
            s = dot_nt(k, diag(q, mask_ref)) + bias_ref[g]
            e = jnp.exp(s - jnp.max(s, 0, keepdims=True))
            p = (e * (1.0 / jnp.sum(e, 0, keepdims=True))).astype(low)
            pt_ref[g, w] = p
            o_ref[rows, cols] = undiag(v.T, p, mask_ref).astype(low)
            return inner

        lax.fori_loop(0, windows, window, 0)
        return carry

    lax.fori_loop(0, GROUPS, group, 0)

    def output(w, carry):
        rows = window_rows(w)
        branch = dot(o_ref[rows, :], flat(wp_ref[...])) + vec_ref[4:5, :]
        x1_ref[rows, :] = x_ref[rows, :].astype(full) + branch
        return carry

    lax.fori_loop(0, windows, output, 0)


def gelu_both(h):
    c = math.sqrt(2.0 / math.pi)
    square = h * h
    t = jnp.tanh(h * (c + (c * 0.044715) * square))
    half = 0.5 + 0.5 * t
    act = h * half
    return act, half + act * (1.0 - half) * (2.0 * c + (6.0 * c * 0.044715) * square)


def feed_forward(windows, x1_ref, dy_ref, live_ref, vec_ref, up_ref, down_ref, wp_ref, o_ref,
                 out_ref, dx1_ref, do_ref, gup_ref, gdown_ref, gout_ref, sums_ref,
                 n2_ref, n2t_ref, dy2_ref, dyt_ref, y_ref, dn_ref, bu_ref, bsum_ref):
    zero_tail(n2_ref, windows)
    zero_tail(dy2_ref, windows)

    def second_norm(w, carry):
        rows = window_rows(w)
        xhat, _ = norm_parts(x1_ref[rows, :])
        n2_ref[rows, :] = (xhat * vec_ref[5:6, :] + vec_ref[6:7, :]).astype(low)
        dy2_ref[rows, :] = (dy_ref[rows, :].astype(full) * live_ref[w]).astype(low)
        return carry

    lax.fori_loop(0, windows, second_norm, 0)
    transpose_rows(n2_ref, n2t_ref)
    transpose_rows(dy2_ref, dyt_ref)
    y_ref[...] = jnp.zeros_like(y_ref)
    dn_ref[...] = jnp.zeros_like(dn_ref)
    owners = gup_ref.shape[1]
    for t in range(TILES):
        for s in range(TILE // 128):
            row, at = hidden_place(t, s)
            bu_ref[t, :, s * 128 : (s + 1) * 128] = vec_ref[row : row + 1, at : at + 128]

    def step(t, carry):
        for part in range(TILE // SUB):
            cols = slice(part * SUB, (part + 1) * SUB)
            up = flat(up_ref[t, :, :, cols])
            down = flat(down_ref[t, part * SUB // 128 : (part + 1) * SUB // 128])
            h = dot(n2_ref[...], up) + bu_ref[t, :, cols]
            da = dot_nt(dy2_ref[...], down)
            act, slope = gelu_both(h)
            a = act.astype(low)
            dh = (da * slope).astype(low)
            bsum_ref[t, :, cols] = jnp.sum(dh.astype(full), 0, keepdims=True)
            y_ref[...] += dot(a, down)
            dn_ref[...] += dot_nt(dh, up)
            gd = dot(dyt_ref[...], a).astype(low)
            for b in range(SUB // 128):
                gdown_ref[t, part * SUB // 128 + b] = gd[:, b * 128 : (b + 1) * 128]
            gup_ref[t, :, :, cols] = blocks(dot(n2t_ref[...], dh).astype(low), owners)
        return carry

    lax.fori_loop(0, TILES, step, 0)
    sums_ref[...] = jnp.zeros_like(sums_ref)
    for t in range(TILES):
        for s in range(TILE // 128):
            row, at = hidden_place(t, s)
            sums_ref[row : row + 1, at : at + 128] = bsum_ref[t, :, s * 128 : (s + 1) * 128]
    zero_tail(dx1_ref, windows)

    def finish(w, carry):
        rows = window_rows(w)
        x1 = x1_ref[rows, :]
        out_ref[rows, :] = ((x1 + y_ref[rows, :] + vec_ref[7:8, :]) * live_ref[w]).astype(low)
        xhat, scale = norm_parts(x1)
        dn = dn_ref[rows, :]
        dy = dy2_ref[rows, :].astype(full)
        dx1 = dy + norm_back(xhat, scale, dn, vec_ref[5:6, :])
        dx1_ref[rows, :] = dx1
        dr = dx1.astype(low)
        n2_ref[rows, :] = dr
        do_ref[rows, :] = dot_nt(dr, flat(wp_ref[...])).astype(low)
        sums_ref[4:5, :] += jnp.sum(dr.astype(full), 0, keepdims=True)
        sums_ref[5:6, :] += jnp.sum(dn * xhat, 0, keepdims=True)
        sums_ref[6:7, :] += jnp.sum(dn, 0, keepdims=True)
        sums_ref[7:8, :] += jnp.sum(dy, 0, keepdims=True)
        return carry

    lax.fori_loop(0, windows, finish, 0)
    transpose_rows(o_ref, dyt_ref)
    for g in range(GROUPS):
        at = pl.ds(g * GCOLS, GCOLS)
        gout_ref[:, :, at] = blocks(dot(dyt_ref[...], n2_ref[:, at]).astype(low), gout_ref.shape[0])


def attention_backward(windows, x_ref, vec_ref, line_ref, mask_ref, wq_ref, qkv_ref, pt_ref, do_ref, dx1_ref, n1t_ref, sums_in_ref,
                       gq_ref, gsmall_ref, grad_ref, sums_ref, bias_ref, tmp_ref, dproj_ref, dn_ref):
    bias_ref[...] = jnp.zeros_like(bias_ref)
    dn_ref[...] = jnp.zeros_like(dn_ref)
    sums_ref[...] = sums_in_ref[...]
    for part in range(3):
        dproj_ref[part, windows * TOK :, :] = jnp.zeros((ROWS - windows * TOK, GCOLS), low)

    def group(g, carry):
        cols = pl.ds(pl.multiple_of(g * GCOLS, GCOLS), GCOLS)

        def window(w, inner):
            rows = window_rows(w)
            q = qkv_ref[g, rows, :]
            k = qkv_ref[GROUPS + g, rows, :]
            v = qkv_ref[2 * GROUPS + g, rows, :]
            p = pt_ref[g, w]
            do = diag(do_ref[rows, cols], mask_ref)
            dp = dot_nt(v, do)
            dv = dot(p, do)
            pf = p.astype(full)
            ds = (pf * (dp - jnp.sum(pf * dp, 0, keepdims=True))).astype(low)
            bias_ref[g] += ds.astype(full)
            dk = dot(ds, diag(q, mask_ref))
            dq = undiag(k.T, ds, mask_ref) * (HEAD_DIM**-0.5)
            dq = dq.astype(low)
            dv = dv.astype(low)
            dproj_ref[0, rows, :] = dq
            dproj_ref[1, rows, :] = dk.astype(low)
            dproj_ref[2, rows, :] = dv
            sums_ref[2:3, cols] += jnp.sum(dq.astype(full), 0, keepdims=True)
            sums_ref[3:4, cols] += jnp.sum(dv.astype(full), 0, keepdims=True)
            return inner

        lax.fori_loop(0, windows, window, 0)
        for part in range(3):
            d = dproj_ref[part]
            gq_ref[g, part] = blocks(dot(n1t_ref[...], d).astype(low), gq_ref.shape[2])
            dn_ref[...] += dot_nt(d, flat(wq_ref[g, part]))
        return carry

    lax.fori_loop(0, GROUPS, group, 0)

    def finish(w, carry):
        rows = window_rows(w)
        xhat, scale = norm_parts(x_ref[rows, :].astype(full))
        dn = dn_ref[rows, :]
        grad_ref[rows, :] = dx1_ref[rows, :] + norm_back(xhat, scale, dn, vec_ref[0:1, :])
        sums_ref[0:1, :] += jnp.sum(dn * xhat, 0, keepdims=True)
        sums_ref[1:2, :] += jnp.sum(dn, 0, keepdims=True)
        return carry

    lax.fori_loop(0, windows, finish, 0)
    pack_small(sums_ref[...], table_grad(line_ref, tmp_ref, bias_ref), gsmall_ref)


MESH = pl.DeviceIdType.MESH
REPS = 4
OWNERS = 8
LINKS = OWNERS // 2


class Spot:
    def __init__(self):
        self.rep = lax.axis_index("rep")
        self.shard = lax.axis_index("shard")
        self.z = self.shard // 2
        self.core = self.shard % 2

    def sibling(self):
        return (self.rep, self.z * 2 + (1 - self.core))

    def along_z(self, step):
        return (self.rep, ((self.z + step) % LINKS) * 2 + self.core)

    def turned(self, axis):
        x, y = self.rep % 2, self.rep // 2
        return y * 2 + (1 - x) if axis == 0 else (1 - y) * 2 + x

    def beside(self, axis):
        return (self.turned(axis), self.shard)

    def across(self):
        return (REPS - 1 - self.rep, self.shard)


def greet(spot):
    barrier = pltpu.get_barrier_semaphore()
    peers = [(spot.rep, (spot.shard + i) % OWNERS) for i in range(1, OWNERS)]
    peers += [((spot.rep + i) % REPS, spot.shard) for i in range(1, REPS)]
    for peer in peers:
        pl.semaphore_signal(barrier, inc=1, device_id=peer, device_id_type=MESH)
    return barrier, len(peers)


def send(src, dst, send_sem, recv_sem, peer):
    pltpu.make_async_remote_copy(src_ref=src, dst_ref=dst, send_sem=send_sem, recv_sem=recv_sem, device_id=peer, device_id_type=MESH).start()


def await_bytes(ref, sem):
    pltpu.make_async_copy(ref, ref, sem).wait()


def quarter(ref, rep):
    rows, cols = ref.shape[-2:]
    lead = (slice(None),) * (len(ref.shape) - 2)
    top = pl.multiple_of((rep // 2) * (rows // 2), 16)
    left = pl.multiple_of((rep % 2) * (cols // 2), 128)
    return ref.at[lead + (pl.ds(top, rows // 2), pl.ds(left, cols // 2))]


def half(ref, rep, axis):
    rows, cols = ref.shape[-2:]
    lead = (slice(None),) * (len(ref.shape) - 2)
    if axis == 0:
        left = pl.multiple_of((rep % 2) * (cols // 2), 128)
        return ref.at[lead + (slice(None), pl.ds(left, cols // 2))]
    top = pl.multiple_of((rep // 2) * (rows // 2), 16)
    return ref.at[lead + (pl.ds(top, rows // 2), slice(None))]


class Gather:
    KINDS = (LINKS - 1, LINKS - 1, LINKS - 1, LINKS - 1, LINKS)
    SEMS = 2 * sum(KINDS)
    STAGES = ("start", "across", "relay", "beside", "finish")

    def __init__(self, spot, place, axis, sems, direct=False):
        self.spot, self.place, self.axis, self.sems, self.direct = spot, place, axis, sems, direct

    def sem(self, side, kind, i):
        return self.sems.at[side * (self.SEMS // 2) + sum(self.KINDS[:kind]) + i]

    def block(self, step):
        return self.place(((self.spot.z - step + LINKS) % LINKS) * 2 + self.spot.core)

    def other(self, step):
        return self.place(((self.spot.z - step + LINKS) % LINKS) * 2 + 1 - self.spot.core)

    def start(self):
        spot = self.spot
        mine = self.block(0)
        for i in range(1, LINKS):
            piece = quarter(mine, spot.rep)
            send(piece, piece, self.sem(0, 0, i - 1), self.sem(1, 0, i - 1), spot.along_z(i))
        send(mine, mine, self.sem(0, 4, 0), self.sem(1, 4, 0), spot.sibling())

    def across(self):
        spot = self.spot
        for i in range(1, LINKS):
            piece = quarter(self.block(i), spot.rep)
            await_bytes(piece, self.sem(1, 0, i - 1))
            for axis in (self.axis, 1 - self.axis):
                send(piece, piece, self.sem(0, 1 + axis, i - 1), self.sem(1, 1 + axis, i - 1), spot.beside(axis))
            if self.direct:
                send(piece, piece, self.sem(0, 3, i - 1), self.sem(1, 3, i - 1), spot.across())

    def relay(self):
        spot = self.spot
        if self.direct:
            return
        for i in range(1, LINKS):
            piece = quarter(self.block(i), spot.turned(self.axis))
            await_bytes(piece, self.sem(1, 1 + self.axis, i - 1))
            send(piece, piece, self.sem(0, 3, i - 1), self.sem(1, 3, i - 1), spot.beside(1 - self.axis))

    def beside(self):
        spot = self.spot
        for i in range(1, LINKS):
            block = self.block(i)
            piece = quarter(block, spot.rep)
            if self.direct:
                await_bytes(piece, self.sem(1, 1 + self.axis, i - 1))
            await_bytes(piece, self.sem(1, 2 - self.axis, i - 1))
            await_bytes(piece, self.sem(1, 3, i - 1))
            send(block, block, self.sem(0, 4, i), self.sem(1, 4, i), spot.sibling())

    def finish(self):
        for i in range(LINKS):
            await_bytes(self.other(i), self.sem(1, 4, i))

    def close(self):
        piece = quarter(self.block(0), self.spot.rep)
        for kind in range(4):
            for i in range(1, LINKS):
                await_bytes(piece, self.sem(0, kind, i - 1))
        for i in range(LINKS):
            await_bytes(self.block(i), self.sem(0, 4, i))


class Reduce:
    KINDS = (LINKS, 1, 1, LINKS - 1, REPS - 1)
    SEMS = 2 * sum(KINDS)
    STAGES = ("start", "first", "second", "along", "spread", "passed", "finish")

    def __init__(self, spot, place, out, core_sum, halves, quarters, links, axis, sems, direct):
        self.spot, self.place, self.out, self.axis, self.sems, self.direct = spot, place, out, axis, sems, direct
        self.core_sum, self.halves, self.quarters, self.links = core_sum, halves, quarters, links

    def sem(self, side, kind, i):
        return self.sems.at[side * (self.SEMS // 2) + sum(self.KINDS[:kind]) + i]

    def start(self):
        spot = self.spot
        for z in range(LINKS):
            send(self.place(z * 2 + (1 - spot.core)), self.core_sum.at[z], self.sem(0, 0, z), self.sem(1, 0, z), spot.sibling())

    def first(self):
        spot = self.spot
        for z in range(LINKS):
            total = self.core_sum.at[z]
            await_bytes(total, self.sem(1, 0, z))
            total[...] = (total[...].astype(full) + self.place(z * 2 + spot.core)[...].astype(full)).astype(low)
        theirs = half(self.core_sum, spot.turned(self.axis), self.axis)
        send(theirs, self.halves, self.sem(0, 1, 0), self.sem(1, 1, 0), spot.beside(self.axis))

    def second(self):
        spot = self.spot
        await_bytes(self.halves, self.sem(1, 1, 0))
        mine = half(self.core_sum, spot.rep, self.axis)
        self.halves[...] = (self.halves[...].astype(full) + mine[...].astype(full)).astype(low)
        theirs = half(self.halves, spot.turned(1 - self.axis), 1 - self.axis)
        send(theirs, self.quarters, self.sem(0, 2, 0), self.sem(1, 2, 0), spot.beside(1 - self.axis))

    def along(self):
        spot = self.spot
        await_bytes(self.quarters, self.sem(1, 2, 0))
        mine = half(self.halves, spot.rep, 1 - self.axis)
        self.quarters[...] = (self.quarters[...].astype(full) + mine[...].astype(full)).astype(low)
        for i in range(1, LINKS):
            send(self.quarters.at[(spot.z + i) % LINKS], self.links.at[i - 1], self.sem(0, 3, i - 1), self.sem(1, 3, i - 1), spot.along_z(i))

    def spread(self):
        spot = self.spot
        total = self.quarters[spot.z].astype(full)
        for i in range(1, LINKS):
            await_bytes(self.links.at[i - 1], self.sem(1, 3, i - 1))
            total = total + self.links[i - 1].astype(full)
        mine = quarter(self.out, spot.rep)
        mine[...] = total.astype(low)
        for axis in (self.axis, 1 - self.axis):
            send(mine, mine, self.sem(0, 4, axis), self.sem(1, 4, axis), spot.beside(axis))
        if self.direct:
            send(mine, mine, self.sem(0, 4, 2), self.sem(1, 4, 2), spot.across())

    def passed(self):
        spot = self.spot
        theirs = quarter(self.out, spot.turned(self.axis))
        await_bytes(theirs, self.sem(1, 4, self.axis))
        if not self.direct:
            send(theirs, theirs, self.sem(0, 4, 2), self.sem(1, 4, 2), spot.beside(1 - self.axis))

    def finish(self):
        spot = self.spot
        await_bytes(quarter(self.out, spot.turned(1 - self.axis)), self.sem(1, 4, 1 - self.axis))
        await_bytes(quarter(self.out, REPS - 1 - spot.rep), self.sem(1, 4, 2))

    def close(self):
        for z in range(LINKS):
            await_bytes(self.core_sum.at[z], self.sem(0, 0, z))
        await_bytes(self.halves, self.sem(0, 1, 0))
        await_bytes(self.quarters, self.sem(0, 2, 0))
        for i in range(1, LINKS):
            await_bytes(self.links.at[i - 1], self.sem(0, 3, i - 1))
        for j in range(1, REPS):
            await_bytes(quarter(self.out, self.spot.rep), self.sem(0, 4, j - 1))


class ReduceDirect(Reduce):
    KINDS = (LINKS, REPS - 1, 0, LINKS - 1, REPS - 1)
    SEMS = 2 * sum(KINDS)

    def peers(self):
        spot = self.spot
        return (spot.turned(0), spot.turned(1), REPS - 1 - spot.rep)

    def first(self):
        spot = self.spot
        for z in range(LINKS):
            total = self.core_sum.at[z]
            await_bytes(total, self.sem(1, 0, z))
            total[...] = (total[...].astype(full) + self.place(z * 2 + spot.core)[...].astype(full)).astype(low)
        for j, rep in enumerate(self.peers()):
            send(quarter(self.core_sum, rep), self.halves.at[j], self.sem(0, 1, j), self.sem(1, 1, j), (rep, spot.shard))

    def second(self):
        pass

    def along(self):
        spot = self.spot
        total = quarter(self.core_sum, spot.rep)[...].astype(full)
        for j in range(REPS - 1):
            await_bytes(self.halves.at[j], self.sem(1, 1, j))
            total = total + self.halves[j].astype(full)
        self.quarters[...] = total.astype(low)
        for i in range(1, LINKS):
            send(self.quarters.at[(spot.z + i) % LINKS], self.links.at[i - 1], self.sem(0, 3, i - 1), self.sem(1, 3, i - 1), spot.along_z(i))

    def close(self):
        for z in range(LINKS):
            await_bytes(self.core_sum.at[z], self.sem(0, 0, z))
        for j in range(REPS - 1):
            await_bytes(self.halves.at[j], self.sem(0, 1, j))
        for i in range(1, LINKS):
            await_bytes(self.links.at[i - 1], self.sem(0, 3, i - 1))
        for j in range(1, REPS):
            await_bytes(quarter(self.out, self.spot.rep), self.sem(0, 4, j - 1))


class ReduceSmall:
    KINDS = (LINKS, LINKS - 1, REPS - 1)
    SEMS = 2 * sum(KINDS)
    STAGES = ("start", "first", "second", "along")

    def __init__(self, spot, terms, out, core_sum, links, parts, sems):
        self.spot, self.terms, self.out, self.core_sum, self.links, self.parts, self.sems = spot, terms, out, core_sum, links, parts, sems

    sem = Reduce.sem

    def start(self):
        spot = self.spot
        for z in range(LINKS):
            send(self.terms.at[z * 2 + (1 - spot.core)], self.core_sum.at[z], self.sem(0, 0, z), self.sem(1, 0, z), spot.sibling())

    def first(self):
        spot = self.spot
        for z in range(LINKS):
            await_bytes(self.core_sum.at[z], self.sem(1, 0, z))
            self.core_sum[z] = self.core_sum[z] + self.terms[z * 2 + spot.core]
        for i in range(1, LINKS):
            send(self.core_sum.at[(spot.z + i) % LINKS], self.links.at[i - 1], self.sem(0, 1, i - 1), self.sem(1, 1, i - 1), spot.along_z(i))

    def second(self):
        spot = self.spot
        total = self.core_sum[spot.z]
        for i in range(1, LINKS):
            await_bytes(self.links.at[i - 1], self.sem(1, 1, i - 1))
            total = total + self.links[i - 1]
        self.parts[spot.rep] = total
        mine = self.parts.at[spot.rep]
        for j in range(1, REPS):
            send(mine, mine, self.sem(0, 2, j - 1), self.sem(1, 2, j - 1), ((spot.rep + j) % REPS, spot.shard))

    def along(self):
        for j in range(1, REPS):
            await_bytes(self.parts.at[(self.spot.rep - j + REPS) % REPS], self.sem(1, 2, j - 1))
        total = self.parts[0]
        for j in range(1, REPS):
            total = total + self.parts[j]
        self.out[...] = total

    def close(self):
        for z in range(LINKS):
            await_bytes(self.core_sum.at[z], self.sem(0, 0, z))
        for i in range(1, LINKS):
            await_bytes(self.links.at[i - 1], self.sem(0, 1, i - 1))
        for j in range(1, REPS):
            await_bytes(self.parts.at[self.spot.rep], self.sem(0, 2, j - 1))


OWNED = C // OWNERS
SLOTS = TILES + 1
GATHERS = 2 * TILES + 1 + GROUPS
REDUCES = 2 * TILES + 1 + (GROUPS - 1) + 3
W_Q0, W_Q1, W_Q2, W_P, W_U0, W_D0, W_U1, W_D1, W_U2, W_D2 = W_ALL = range(10)
G_D0, G_U0, G_D1, G_U1, G_D2, G_U2, G_P, G_Q0, G_Q1, G_Q2, G_K2, G_V2, G_S = G_ALL = range(10, 23)
W_Q, W_U, W_D = (W_Q0, W_Q1, W_Q2), (W_U0, W_U1, W_U2), (W_D0, W_D1, W_D2)
G_D, G_U, G_Q, G_LAST = (G_D0, G_D1, G_D2), (G_U0, G_U1, G_U2), (G_Q0, G_Q1), (G_Q2, G_K2, G_V2)
G_TWO = ()
START, ACROSS, RELAY, BESIDE, ARRIVED = range(5)
FIRST, SECOND, ALONG, SPREAD, PASSED, SUMMED = range(1, 7)
BEFORE = {
    2: ((W_Q0, ACROSS), (W_P, START),),
    3: ((W_Q2, START),),
    4: ((W_Q0, RELAY), (W_U0, START),),
    5: ((W_Q0, BESIDE), (W_Q1, ACROSS),),
}
FORWARD = {
    0: ((W_Q1, RELAY), (W_Q2, ACROSS), (W_P, ACROSS), (W_D0, START), (W_U1, START),),
    2: ((W_D1, START),),
    4: ((W_Q1, BESIDE),),
    5: ((W_U0, ACROSS),),
    6: ((W_Q2, RELAY),),
    7: ((W_P, RELAY),),
    8: ((W_D0, ACROSS),),
    11: ((W_Q2, BESIDE), (W_U0, RELAY),),
    12: ((W_U1, ACROSS),),
    14: ((W_D0, RELAY), (W_U2, START), (W_D2, START),),
    16: ((W_D1, ACROSS),),
    17: ((W_P, BESIDE), (W_U0, BESIDE),),
    18: ((W_U1, RELAY),),
}
MIDDLE = {
    0: ((W_D0, BESIDE), (W_U2, ACROSS),),
    1: ((W_D1, RELAY),),
    2: ((W_U1, BESIDE), (W_D2, ACROSS),),
}
TILE_STEP = {
    1: ((W_D1, BESIDE), (W_U2, RELAY), (W_D2, RELAY),),
    2: ((W_U2, BESIDE), (W_D2, BESIDE),),
    3: ((G_D0, FIRST), (G_U0, FIRST),),
    5: ((G_D0, SECOND), (G_U0, SECOND), (G_D1, FIRST), (G_U1, FIRST),),
}
AFTER_TILES = {
    0: ((G_D0, ALONG), (G_U0, ALONG),),
    2: ((G_D2, FIRST), (G_U2, FIRST),),
    3: ((G_U1, SECOND),),
}
BACKWARD = {
    2: ((G_D0, SPREAD), (G_U0, SPREAD),),
    3: ((G_D1, SECOND), (G_P, FIRST),),
    7: ((G_D2, SECOND),),
    8: ((G_U2, SECOND),),
    9: ((G_U1, ALONG),),
    10: ((G_Q0, FIRST),),
    11: ((G_U0, SUMMED), (G_D1, ALONG),),
    12: ((G_D0, SUMMED),),
    14: ((G_D2, ALONG), (G_P, SECOND),),
    16: ((G_U1, SPREAD), (G_Q0, SECOND),),
    17: ((G_D1, SPREAD), (G_U2, ALONG), (G_Q1, FIRST),),
    20: ((G_D2, SPREAD), (G_P, ALONG),),
}
LAST_STEPS = {
    0: ((G_Q2, FIRST), (G_Q2, SECOND), (G_K2, FIRST),),
    1: ((G_U2, SPREAD), (G_P, SPREAD), (G_Q0, ALONG), (G_V2, FIRST),),
    2: ((G_D1, SUMMED),),
    3: ((G_U1, SUMMED), (G_Q0, SPREAD), (G_Q1, SECOND), (G_K2, SECOND), (G_V2, SECOND),),
}


def chunk_shapes():
    out = []
    for _ in range(TILES):
        out += [(128, C), (OWNED, TILE)]
    return out + [(OWNED, C)] + [(3, OWNED, GCOLS)] * (GROUPS - 1) + [(OWNED, GCOLS)] * 3


def reduce_scratch():
    out = []
    for i, dims in enumerate(chunk_shapes()):
        *lead, rows, cols = dims
        near = (rows, cols // 2) if i % 2 == 0 else (rows // 2, cols)
        near = (LINKS, *lead, *near) if i < REDUCES - 3 else (REPS - 1, LINKS, *lead, rows // 2, cols // 2)
        out.append(pltpu.VMEM((LINKS, *dims), low))
        out.append(pltpu.VMEM(near, low))
        out.append(pltpu.VMEM((LINKS, *lead, rows // 2, cols // 2), low))
        out.append(pltpu.VMEM((LINKS - 1, *lead, rows // 2, cols // 2), low))
    out += [pltpu.VMEM((LINKS, 40, 128), full), pltpu.VMEM((LINKS - 1, 40, 128), full), pltpu.VMEM((REPS, 40, 128), full)]
    return out


def layer_kernel(windows, x_hbm, dy_hbm, count_ref, q32, p32, u32, d32, vec_in, tab_in, line_ref, mask_ref,
                 out_hbm, grad_hbm, gq_out, gp_out, gu_out, gd_out, gs_out, qkv_hbm, pt_hbm, n1_hbm, *scratch):
    wq, wp, up, down, small, o_ref, x1_ref, vec_ref, sums_ref, terms_ref = scratch[:10]
    gather_sems, reduce_sems, small_sems, small_reduce_sems, local = scratch[-5:]
    reduce_refs = scratch[10:-5]
    spot = Spot()
    rows_all = windows * TOK

    def live(w):
        return (w < count_ref[0]).astype(full)

    mine = spot.shard
    V = pltpu.VMEM

    jobs = {}
    places = [(W_Q[g], lambda s, g=g: wq.at[g, :, s]) for g in range(GROUPS)] + [(W_P, lambda s: wp.at[s])]
    for t in range(TILES):
        places += [(W_U[t], lambda s, t=t: up.at[t, s]), (W_D[t], lambda s, t=t: down.at[t, s])]
    for i, (name, place) in enumerate(places):
        jobs[name] = Gather(spot, place, i % 2, gather_sems.at[i], direct=name == W_Q0)
    places = []
    for t in range(TILES):
        slot = (t + SLOTS - 1) % SLOTS
        places.append((G_D[t], lambda s, slot=slot: down.at[slot, s], gd_out.at[t]))
        places.append((G_U[t], lambda s, slot=slot: up.at[slot, s], gu_out.at[t]))
    places.append((G_P, lambda s: wp.at[s], gp_out))
    for g in range(GROUPS - 1):
        places.append((G_Q[g], lambda s, g=g: wq.at[g, :, s], gq_out.at[g]))
    for part in range(3):
        places.append((G_LAST[part], lambda s, part=part: up.at[TILES - 1, s, :, pl.ds(part * GCOLS, GCOLS)], gq_out.at[GROUPS - 1, part]))
    for i, (name, place, out) in enumerate(places):
        kind = ReduceDirect if name in G_LAST else Reduce
        jobs[name] = kind(spot, place, out, *reduce_refs[4 * i : 4 * i + 4], i % 2, reduce_sems.at[i], name not in G_TWO)
    jobs[G_S] = ReduceSmall(spot, terms_ref, gs_out, *reduce_refs[-3:], small_reduce_sems)

    done = {}

    def run(name, upto):
        for stage in range(done.get(name, 0), upto + 1):
            getattr(jobs[name], jobs[name].STAGES[stage])()
        done[name] = max(done.get(name, 0), upto + 1)

    def hook(table, place):
        for item in table.get(place, ()):
            run(*item)

    def hook_window(table, g, w):
        for at in range(windows):
            place = g * windows + at
            if place in table:

                @pl.when(w == at)
                def _(place=place):
                    hook(table, place)

    barrier, peers = greet(spot)

    def cast(q_v, p_v, u_v, d_v):
        loads = [pltpu.make_async_copy(a, b, local.at[i]) for i, (a, b) in enumerate(((q32, q_v), (p32, p_v), (u32, u_v), (d32, d_v)))]
        for load in loads:
            load.start()
        small[mine] = jnp.zeros((48, 128), low)
        pad = jnp.zeros((16, 128), full)
        vec_ref[:, 0:128] = pad
        vec_ref[0:12, 0:OWNED] = vec_in[...]
        small[mine, 0:16, :] = vec_ref[:, 0:128].astype(low)
        x1_ref[0:32, 0:128] = jnp.zeros((32, 128), full)
        x1_ref[0:HEADS, 0 : tab_in.shape[1]] = tab_in[...]
        small[mine, 16:48, :] = x1_ref[0:32, 0:128].astype(low)
        loads[0].wait()
        for g in range(GROUPS):
            for part in range(3):
                wq[g, part, mine] = q_v[:, part * C + g * GCOLS : part * C + (g + 1) * GCOLS].astype(low)
        pl.semaphore_wait(barrier, peers)
        for i in range(1, OWNERS):
            send(small.at[mine], small.at[mine], small_sems.at[i], small_sems.at[OWNERS + i], (spot.rep, (mine + i) % OWNERS))
        run(W_Q0, START)
        run(W_Q1, START)
        loads[1].wait()
        wp[mine] = p_v[...].astype(low)
        loads[2].wait()
        loads[3].wait()
        for t in range(TILES):
            for s in range(OWNERS):
                src = (MLP // OWNERS) * s + 128 * t
                up[t, mine, :, s * 128 : (s + 1) * 128] = u_v[:, src : src + 128].astype(low)
            down[t, mine] = d_v[t * 128 : (t + 1) * 128, :].astype(low)

    pl.run_scoped(cast, V((OWNED, 3 * C), full), V((OWNED, C), full), V((OWNED, MLP), full), V((TILES * 128, C), full))

    def forward(dy_ref, dyt_ref, x_ref, n1_ref, qkv_ref, pt_ref, bias_ref):
        load = pltpu.make_async_copy(x_hbm, x_ref, local.at[0])
        load.start()
        load_dy = pltpu.make_async_copy(dy_hbm, dy_ref.at[0:rows_all], local.at[2])
        load_dy.start()
        zero_tail(n1_ref, windows)
        zero_tail(dy_ref, windows)
        zero_tail(o_ref, windows)
        for i in range(1, OWNERS):
            await_bytes(small.at[(mine - i + OWNERS) % OWNERS], small_sems.at[OWNERS + i])
        tab = unpack_small(small, vec_ref)
        hook(BEFORE, 0)
        load.wait()
        hook(BEFORE, 1)

        def first_norm(w, carry):
            xhat, _ = norm_parts(x_ref[window_rows(w), :].astype(full))
            n1_ref[window_rows(w), :] = (xhat * vec_ref[0:1, :] + vec_ref[1:2, :]).astype(low)
            return carry

        lax.fori_loop(0, windows, first_norm, 0)
        hook(BEFORE, 2)
        save = pltpu.make_async_copy(n1_ref, n1_hbm, local.at[1])
        save.start()
        hook(BEFORE, 3)
        load_dy.wait()

        def keep_live(w, carry):
            dy_ref[window_rows(w), :] = (dy_ref[window_rows(w), :].astype(full) * live(w)).astype(low)
            return carry

        lax.fori_loop(0, windows, keep_live, 0)
        transpose_rows(dy_ref, dyt_ref)
        hook(BEFORE, 4)

        def bias(tmp_ref):
            spread_table(tab, line_ref, tmp_ref)
            hook(BEFORE, 5)
            place_bias(tmp_ref, bias_ref)

        pl.run_scoped(bias, V((2, TOK * HEADS, 128), full))
        for g in range(GROUPS):
            cols = slice(g * GCOLS, (g + 1) * GCOLS)
            held = qkv_ref.at[g % 2]
            if g >= 2:
                pltpu.make_async_copy(held, qkv_hbm.at[g - 2], local.at[2 + g % 2]).wait()
            run(W_Q[g], ARRIVED)
            n1 = n1_ref[...]
            held[0] = ((dot(n1, flat(wq[g, 0])) + vec_ref[2:3, cols]) * (HEAD_DIM**-0.5)).astype(low)
            held[1] = dot(n1, flat(wq[g, 1])).astype(low)
            held[2] = (dot(n1, flat(wq[g, 2])) + vec_ref[3:4, cols]).astype(low)
            pltpu.make_async_copy(held, qkv_hbm.at[g], local.at[2 + g % 2]).start()

            def window(w, carry, g=g, cols=cols, held=held):
                hook_window(FORWARD, g, w)
                rows = window_rows(w)
                n = g * windows + w
                slot = n % 2
                s = against_heads(held[1, rows, :], split_diag(held[0, rows, :], mask_ref)) + bias_ref[g]
                e = jnp.exp(s - jnp.max(s, 0, keepdims=True))
                p = (e * (1.0 / jnp.sum(e, 0, keepdims=True))).astype(low)
                keep = pltpu.make_async_copy(pt_ref.at[slot], pt_hbm.at[n], local.at[4 + slot])

                @pl.when(n >= 2)
                def _():
                    keep.wait()

                pt_ref[slot] = p
                keep.start()
                o_ref[rows, cols] = undiag(held[2, rows, :].T, p, mask_ref).astype(low)
                return carry

            lax.fori_loop(0, windows, window, 0)

        run(W_P, ARRIVED)

        x1_ref[...] = x_ref[...].astype(full) + (dot(o_ref[0:rows_all], flat(wp[...])) + vec_ref[4:5, :])
        save.wait()
        for g in (GROUPS - 2, GROUPS - 1):
            pltpu.make_async_copy(qkv_ref.at[g % 2], qkv_hbm.at[g], local.at[2 + g % 2]).wait()
        for slot in range(2):
            pltpu.make_async_copy(pt_ref.at[slot], pt_hbm.at[0], local.at[4 + slot]).wait()

    def middle(dy_ref, dyt_ref, n2_ref, n2t_ref, y_ref, dn_ref, bu_ref, bsum_ref):
        zero_tail(n2_ref, windows)
        hook(MIDDLE, 0)

        def second_norm(w, carry):
            rows = window_rows(w)
            xhat, _ = norm_parts(x1_ref[rows, :])
            n2_ref[rows, :] = (xhat * vec_ref[5:6, :] + vec_ref[6:7, :]).astype(low)
            return carry

        lax.fori_loop(0, windows, second_norm, 0)
        transpose_rows(n2_ref, n2t_ref)
        hook(MIDDLE, 1)
        n2t_ref[C:, :] = jnp.ones((16, ROWS), low)
        y_ref[...] = jnp.zeros_like(y_ref)
        dn_ref[...] = jnp.zeros_like(dn_ref)
        for t in range(TILES):
            for s in range(TILE // 128):
                row, left = hidden_place(t, s)
                bu_ref[t, :, s * 128 : (s + 1) * 128] = vec_ref[row : row + 1, left : left + 128]
        hook(MIDDLE, 2)
        run(W_U0, ARRIVED)
        run(W_D0, ARRIVED)
        hook(TILE_STEP, 0)
        halves = TILE // SUB

        def step(i, carry):
            for k in range(1, TILES * halves):

                @pl.when(i == k)
                def _(k=k):
                    if k % halves == 0:
                        t = k // halves
                        for name in (W_U[t], W_D[t]):
                            run(name, ARRIVED)
                        for name in (W_U[t - 1], W_D[t - 1]):
                            jobs[name].close()
                        for name in (G_D[t - 1], G_U[t - 1]):
                            run(name, START)
                    hook(TILE_STEP, k)

            t, part = i // halves, i % halves
            cols = pl.ds(pl.multiple_of(part * SUB, SUB), SUB)
            wide = SUB // 128
            slot = (t + SLOTS - 1) % SLOTS
            u = flat(up[t, :, :, cols])
            d = flat(down[t, pl.ds(part * wide, wide)])
            h = dot(n2_ref[...], u) + bu_ref[t, :, cols]
            da = dot_nt(dy_ref[...], d)
            act, slope = gelu_both(h)
            a = act.astype(low)
            dh = (da * slope).astype(low)
            y_ref[...] += dot(a, d)
            dn_ref[...] += dot_nt(dh, u)
            gd = dot(dyt_ref[...], a).astype(low)
            down[slot, pl.ds(part * wide, wide)] = blocks(gd.T, wide)
            gu = dot(n2t_ref[...], dh)
            up[slot, :, :, cols] = blocks(gu[0:C].astype(low), OWNERS)
            bsum_ref[t, :, cols] = gu[C : C + 1]
            return carry

        lax.fori_loop(0, TILES * halves, step, 0)
        run(G_D[-1], START)
        run(G_U[-1], START)
        hook(AFTER_TILES, 0)
        sums_ref[...] = jnp.zeros_like(sums_ref)
        for t in range(TILES):
            for s in range(TILE // 128):
                row, left = hidden_place(t, s)
                sums_ref[row : row + 1, left : left + 128] = bsum_ref[t, :, s * 128 : (s + 1) * 128]
        transpose_rows(o_ref, dyt_ref)
        hook(AFTER_TILES, 1)

        def finish(w, carry):
            rows = window_rows(w)
            x1 = x1_ref[rows, :]
            xhat, scale = norm_parts(x1)
            dn = dn_ref[rows, :]
            dy = dy_ref[rows, :].astype(full)
            dx1 = dy + norm_back(xhat, scale, dn, vec_ref[5:6, :])
            dr = dx1.astype(low)
            sums_ref[4:5, :] += jnp.sum(dr.astype(full), 0, keepdims=True)
            sums_ref[5:6, :] += jnp.sum(dn * xhat, 0, keepdims=True)
            sums_ref[6:7, :] += jnp.sum(dn, 0, keepdims=True)
            sums_ref[7:8, :] += jnp.sum(dy, 0, keepdims=True)
            dy_ref[rows, :] = ((x1 + y_ref[rows, :] + vec_ref[7:8, :]) * live(w)).astype(low)
            x1_ref[rows, :] = dx1
            n2_ref[rows, :] = dr
            return carry

        lax.fori_loop(0, windows, finish, 0)
        o_ref[...] = dot_nt(n2_ref[...], flat(wp[...])).astype(low)
        save = pltpu.make_async_copy(dy_ref.at[0:rows_all], out_hbm, local.at[0])
        save.start()
        hook(AFTER_TILES, 2)
        jobs[W_P].close()
        for g in range(GROUPS):
            cols = slice(g * GCOLS, (g + 1) * GCOLS)
            wp[:, :, cols] = blocks(dot(dyt_ref[...], n2_ref[:, cols]).astype(low), OWNERS)
        run(G_P, START)
        hook(AFTER_TILES, 3)
        save.wait()

    def both(dy_ref, dyt_ref):
        pl.run_scoped(functools.partial(forward, dy_ref, dyt_ref), V((rows_all, C), low), V((ROWS, C), low),
                      V((2, 3, ROWS, GCOLS), low), V((2, TOK, PACK), low), V((GROUPS, TOK, PACK), full))
        pl.run_scoped(functools.partial(middle, dy_ref, dyt_ref), V((ROWS, C), low), V((C + 16, ROWS), low), V((ROWS, C), full), V((ROWS, C), full),
                      V((TILES, 1, TILE), full), V((TILES, 1, TILE), full))

    pl.run_scoped(both, V((ROWS, C), low), V((C, ROWS), low))

    def backward(x_ref, n1_ref, n1t_ref, qkv_ref, pt_ref, dproj_ref, dn_ref, bias_ref):
        loads = [pltpu.make_async_copy(x_hbm, x_ref, local.at[0]), pltpu.make_async_copy(n1_hbm, n1_ref, local.at[1])]
        fetch = [pltpu.make_async_copy(qkv_hbm.at[g], qkv_ref.at[g % 2], local.at[2 + g % 2]) for g in range(GROUPS)]
        fetch[0].start()
        pltpu.make_async_copy(pt_hbm.at[0], pt_ref.at[0], local.at[4]).start()
        fetch[1].start()
        for load in loads:
            load.start()
        bias_ref[...] = jnp.zeros_like(bias_ref)
        dn_ref[...] = jnp.zeros_like(dn_ref)
        for part in range(3):
            dproj_ref[part, rows_all:, :] = jnp.zeros((ROWS - rows_all, GCOLS), low)
        for g in range(GROUPS):
            cols = slice(g * GCOLS, (g + 1) * GCOLS)
            held = qkv_ref.at[g % 2]
            fetch[g].wait()

            def window(w, carry, g=g, cols=cols, held=held):
                hook_window(BACKWARD, g, w)
                rows = window_rows(w)
                n = g * windows + w
                slot = n % 2

                @pl.when(n + 1 < GROUPS * windows)
                def _():
                    pltpu.make_async_copy(pt_hbm.at[n + 1], pt_ref.at[1 - slot], local.at[5 - slot]).start()

                pltpu.make_async_copy(pt_hbm.at[n], pt_ref.at[slot], local.at[4 + slot]).wait()
                q = held[0, rows, :]
                k = held[1, rows, :]
                v = held[2, rows, :]
                p = pt_ref[slot]
                do = split_diag(o_ref[rows, cols], mask_ref)
                dp = against_heads(v, do)
                dv = over_queries(p, do).astype(low)
                pf = p.astype(full)
                ds = (pf * (dp - jnp.sum(pf * dp, 0, keepdims=True))).astype(low)
                bias_ref[g] += ds.astype(full)
                dproj_ref[1, rows, :] = over_queries(ds, split_diag(q, mask_ref)).astype(low)
                dq = (undiag(k.T, ds, mask_ref) * (HEAD_DIM**-0.5)).astype(low)
                dproj_ref[0, rows, :] = dq
                dproj_ref[2, rows, :] = dv
                sums_ref[2:3, cols] += jnp.sum(dq.astype(full), 0, keepdims=True)
                sums_ref[3:4, cols] += jnp.sum(dv.astype(full), 0, keepdims=True)
                return carry

            lax.fori_loop(0, windows, window, 0)
            if g + 2 < GROUPS:
                fetch[g + 2].start()
            if g == 0:
                for load in loads:
                    load.wait()
                transpose_rows(n1_ref, n1t_ref)
            jobs[W_Q[g]].close()
            if g == GROUPS - 1:
                jobs[W_U[-1]].close()
                for part in range(3):
                    up[TILES - 1, :, :, part * GCOLS : (part + 1) * GCOLS] = blocks(dot(n1t_ref[...], dproj_ref[part]).astype(low), OWNERS)
                    run(G_LAST[part], START)
                hook(LAST_STEPS, 0)
                for part in range(3):
                    dn_ref[...] += dot_nt(dproj_ref[part], flat(wq[g, part]))
            else:
                for part in range(3):
                    d = dproj_ref[part]
                    dn_ref[...] += dot_nt(d, flat(wq[g, part]))
                    wq[g, part] = blocks(dot(n1t_ref[...], d).astype(low), OWNERS)
                run(G_Q[g], START)

        def last_norm(grad_ref):
            def finish(w, carry):
                rows = window_rows(w)
                slot = w % 2
                xhat, scale = norm_parts(x_ref[rows, :].astype(full))
                dn = dn_ref[rows, :]
                save = pltpu.make_async_copy(grad_ref.at[slot], grad_hbm.at[rows], local.at[4 + slot])

                @pl.when(w >= 2)
                def _():
                    save.wait()

                grad_ref[slot] = x1_ref[rows, :] + norm_back(xhat, scale, dn, vec_ref[0:1, :])
                save.start()
                sums_ref[0:1, :] += jnp.sum(dn * xhat, 0, keepdims=True)
                sums_ref[1:2, :] += jnp.sum(dn, 0, keepdims=True)
                return carry

            lax.fori_loop(0, windows, finish, 0)
            hook(LAST_STEPS, 1)
            for slot in range(2):
                pltpu.make_async_copy(grad_ref.at[slot], grad_hbm.at[pl.ds(0, TOK)], local.at[4 + slot]).wait()

        pl.run_scoped(last_norm, V((2, TOK, C), full))
        hook(LAST_STEPS, 2)

        def table(tmp_ref):
            pack_small(sums_ref[...], table_grad(line_ref, tmp_ref, bias_ref), terms_ref)

        pl.run_scoped(table, V((2, TOK * HEADS, 128), full))
        run(G_S, START)
        hook(LAST_STEPS, 3)
        for stage in range(len(Reduce.STAGES)):
            for name in G_ALL:
                if stage < len(jobs[name].STAGES):
                    run(name, stage)

    pl.run_scoped(backward, V((rows_all, C), low), V((ROWS, C), low), V((C, ROWS), low), V((2, 3, ROWS, GCOLS), low), V((2, TOK, PACK), low), V((3, ROWS, GCOLS), low),
                  V((ROWS, C), full), V((GROUPS, TOK, PACK), full))
    jobs[W_D[-1]].close()
    for i in range(1, OWNERS):
        await_bytes(small.at[mine], small_sems.at[i])
    for name in G_ALL:
        jobs[name].close()


def shape(dims, kind):
    return jax.ShapeDtypeStruct(dims, kind)


def adamw(weight, moment, second, gradient, step_rate):
    moment_new = beta_one * moment + (1.0 - beta_one) * gradient
    second_new = beta_two * second + (1.0 - beta_two) * gradient * gradient
    update = moment_new * (1.0 / (1.0 - beta_one**STEP)) / (jnp.sqrt(second_new * (1.0 / (1.0 - beta_two**STEP))) + adam_eps)
    weight_new = weight * (1.0 - step_rate * weight_decay) - step_rate * update
    return (weight_new, moment_new, second_new)


def update_kernel(*refs):
    gq, gp, gu, gd, gs = refs[:5]
    ins = [refs[5 + 3 * i : 8 + 3 * i] for i in range(6)]
    outs = [refs[25 + 4 * i : 29 + 4 * i] for i in range(4)] + [refs[41:44], refs[44:47]]
    for i in range(2):
        refs[47 + i][...] = refs[23 + i][...]

    def piece(which, place, gradient):
        new = adamw(*(ref[place] for ref in ins[which]), gradient, step_rates[which])
        for ref, value in zip(outs[which], new):
            ref[place] = value
        if which < 4:
            outs[which][3][place] = new[0].astype(low)

    for part in range(3):
        for g in range(GROUPS):
            left = part * C + g * GCOLS
            piece(0, (slice(None), slice(left, left + GCOLS)), gq[g, part].astype(full))
    piece(1, (slice(None), slice(None)), gp[...].astype(full))
    for t in range(TILES):
        for s in range(OWNERS):
            left = (MLP // OWNERS) * s + 128 * t
            piece(2, (slice(None), slice(left, left + 128)), gu[t, :, s * 128 : (s + 1) * 128].astype(full))
    piece(3, (slice(None), slice(None)), gd[0].astype(full))

    @pl.when(pl.program_id(0) == 0)
    def _():
        every = (slice(None), slice(None))
        piece(4, every, gs[0:12, 0:OWNED])
        piece(5, every, gs[16:40, 0 : ins[5][0].shape[1]])


def update(gq, gp, gu, gd, gs, states, results):
    steps = OWNED // 16

    def rows_of(array):
        tall = array.shape[0] // steps
        return pl.BlockSpec((tall, array.shape[1]), lambda i: (i, 0))

    def whole(array):
        return pl.BlockSpec(array.shape, lambda i: (0, 0))

    per_tile = 128 * TILES // steps
    specs = [
        pl.BlockSpec((GROUPS, 3, 16, GCOLS), lambda i: (0, 0, i, 0)),
        pl.BlockSpec((16, C), lambda i: (i, 0)),
        pl.BlockSpec((TILES, 16, TILE), lambda i: (0, i, 0)),
        pl.BlockSpec((1, per_tile, C), lambda i: (i // (128 // per_tile), i % (128 // per_tile), 0)),
        whole(gs),
    ]
    out_shapes, out_specs = [], []
    for i, group in enumerate(states):
        for array in group:
            specs.append(rows_of(array) if i < 4 else whole(array))
            out_shapes.append(shape(array.shape, full))
            out_specs.append(specs[-1])
        if i < 4:
            out_shapes.append(shape(group[0].shape, low))
            out_specs.append(rows_of(group[0]))
    results = [array.reshape(steps, -1, C) for array in results]
    for array in results:
        specs.append(pl.BlockSpec((1, *array.shape[1:]), lambda i: (i, 0, 0)))
        out_shapes.append(shape(array.shape, array.dtype))
        out_specs.append(specs[-1])
    return pl.pallas_call(
        update_kernel,
        grid=(steps,),
        in_specs=specs,
        out_specs=out_specs,
        out_shape=out_shapes,
        compiler_params=pltpu.CompilerParams(vmem_limit_bytes=63 * MIB),
        name="update",
    )(gq, gp, gu, gd, gs, *[array for group in states for array in group], *results)


def shards(
    tokens, out_grad, window_count,
    qkv_weight, qkv_first, qkv_second,
    output_weight, output_first, output_second,
    up_weight, up_first, up_second,
    down_weight, down_first, down_second,
    vectors, vector_first, vector_second,
    bias_table, table_first, table_second,
):
    windows = tokens.shape[0]
    rows = windows * TOK
    V = pltpu.VMEM
    D = pltpu.SemaphoreType.DMA
    hbm = pl.BlockSpec(memory_space=pl.ANY)
    vmem = pl.BlockSpec(memory_space=pltpu.VMEM)
    result = pl.pallas_call(
        functools.partial(layer_kernel, windows),
        out_shape=[
            shape((rows, C), low), shape((rows, C), full),
            shape((GROUPS, 3, OWNED, GCOLS), low), shape((OWNED, C), low), shape((TILES, OWNED, TILE), low), shape((TILES, 128, C), low),
            shape((40, 128), full),
            shape((GROUPS, 3, ROWS, GCOLS), low), shape((GROUPS * windows, TOK, PACK), low), shape((ROWS, C), low)],
        in_specs=[hbm, hbm, pl.BlockSpec(memory_space=pltpu.SMEM)] + [hbm] * 4 + [vmem] * 4,
        out_specs=[hbm, hbm] + [vmem] * 5 + [hbm] * 3,
        scratch_shapes=[
            V((GROUPS, 3, OWNERS, OWNED, GCOLS), low), V((OWNERS, OWNED, C), low), V((SLOTS, OWNERS, OWNED, TILE), low),
            V((SLOTS, OWNERS, 128, C), low), V((OWNERS, 48, 128), low), V((ROWS, C), low), V((rows, C), full), V((16, C), full), V((16, C), full),
            V((OWNERS, 40, 128), full)]
        + reduce_scratch()
        + [D((GATHERS, Gather.SEMS)), D((REDUCES, ReduceDirect.SEMS)), D((2 * OWNERS,)), D((ReduceSmall.SEMS,)), D((6,))],
        compiler_params=pltpu.CompilerParams(vmem_limit_bytes=63 * MIB, collective_id=0, has_side_effects=True),
        name="layer",
    )(tokens.reshape(rows, C), out_grad.reshape(rows, C), window_count, qkv_weight, output_weight, up_weight, down_weight, vectors, bias_table.T,
      jnp.asarray(line_matrix(), low), jnp.asarray(head_masks(), low))
    out, grad, gq, gp, gu, gd, gs = result[:7]
    new = update(gq, gp, gu, gd, gs, (
        (qkv_weight, qkv_first, qkv_second), (output_weight, output_first, output_second), (up_weight, up_first, up_second),
        (down_weight, down_first, down_second), (vectors, vector_first, vector_second), (bias_table.T, table_first.T, table_second.T)), (out, grad))
    *new, out, grad = new
    return (out.reshape(tokens.shape), grad.reshape(tokens.shape), *new[:-3], *(array.T for array in new[-3:]))


def vmem_call(body, outs, scratch, args, name, limit=60, **params):
    spec = pl.BlockSpec(memory_space=pltpu.VMEM)
    return pl.pallas_call(
        body,
        out_shape=outs,
        in_specs=[pl.BlockSpec(memory_space=pltpu.SMEM) if a.dtype == full and a.ndim == 1 else spec for a in args],
        out_specs=[spec] * len(outs),
        scratch_shapes=scratch,
        compiler_params=pltpu.CompilerParams(vmem_limit_bytes=limit * MIB, **params),
        name=name,
    )(*args)


def local_step(tokens, out_grad, window_count, small, wq, wp, up, down):
    windows = tokens.shape[0]
    rows = windows * TOK
    owned = C // OWNERS
    V = pltpu.VMEM
    x = tokens.reshape(rows, C)
    dy = out_grad.reshape(rows, C)
    live = (jnp.arange(windows) < window_count[0]).astype(full)
    line = jnp.asarray(line_matrix(), low)
    masks = jnp.asarray(head_masks(), low)
    qkv, pt, o, x1, n1t, vec = vmem_call(
        functools.partial(attention_forward, windows),
        [shape((9, ROWS, GCOLS), low), shape((GROUPS, windows, TOK, PACK), low), shape((ROWS, C), low), shape((rows, C), full), shape((C, ROWS), low),
         shape((16, C), full)],
        [V((ROWS, C), low), V((GROUPS, TOK, PACK), full), V((2, TOK * HEADS, 128), full)],
        (x, small, line, masks, wq, wp), "attention_forward")
    out, dx1, do, gup, gdown, gout, sums = vmem_call(
        functools.partial(feed_forward, windows),
        [shape((rows, C), low), shape((ROWS, C), full), shape((rows, C), low), shape((TILES, OWNERS, owned, TILE), low),
         shape((TILES, OWNERS, C, 128), low), shape((OWNERS, owned, C), low), shape((16, C), full)],
        [V((ROWS, C), low), V((C, ROWS), low), V((ROWS, C), low), V((C, ROWS), low), V((ROWS, C), full), V((ROWS, C), full),
         V((TILES, 1, TILE), full), V((TILES, 1, TILE), full)],
        (x1, dy, live, vec, up, down, wp, o), "feed_forward")
    gq, gsmall, grad = vmem_call(
        functools.partial(attention_backward, windows),
        [shape((GROUPS, 3, OWNERS, owned, GCOLS), low), shape((OWNERS, 40, 128), full), shape((rows, C), full)],
        [V((16, C), full), V((GROUPS, TOK, PACK), full), V((2, TOK * HEADS, 128), full), V((3, ROWS, GCOLS), low), V((ROWS, C), full)],
        (x, vec, line, masks, wq, qkv, pt, do, dx1, n1t, sums), "attention_backward")
    return out.reshape(tokens.shape), grad.reshape(tokens.shape), gq, gout, gup, gdown, gsmall


def shards_general(
    tokens, out_grad, window_count,
    qkv_weight, qkv_first, qkv_second,
    output_weight, output_first, output_second,
    up_weight, up_first, up_second,
    down_weight, down_first, down_second,
    vectors, vector_first, vector_second,
    bias_table, table_first, table_second,
):
    gather = functools.partial(lax.all_gather, axis_name="shard", tiled=True)
    scatter = functools.partial(lax.psum_scatter, axis_name="shard", tiled=True)
    owned = C // OWNERS
    wq = gather(qkv_weight.astype(low), axis=0).reshape(OWNERS, owned, 3, GROUPS, GCOLS).transpose(3, 2, 0, 1, 4)
    wp = gather(output_weight.astype(low), axis=0).reshape(OWNERS, owned, C)
    up = gather(up_weight.astype(low), axis=0).reshape(OWNERS, owned, OWNERS, TILES, 128).transpose(3, 0, 1, 2, 4)
    up = up.reshape(TILES, OWNERS, owned, TILE)
    down = gather(down_weight.astype(low), axis=0).reshape(OWNERS, TILES, 128, C).transpose(1, 0, 2, 3)
    vec = gather(vectors.astype(low), axis=1)
    tab = gather(bias_table.astype(low), axis=0)
    table_rows = tab.shape[0]
    count = TAB_ROWS // OWNERS
    vec = vec.reshape(12, OWNERS, owned).transpose(1, 0, 2)
    tab = tab[:TAB_ROWS].reshape(OWNERS, count, HEADS).transpose(0, 2, 1)
    small = jnp.concatenate([jnp.pad(vec, ((0, 0), (0, 4), (0, 128 - owned))), jnp.pad(tab, ((0, 0), (0, 8), (0, 128 - count)))], 1)
    out, grad, gq, gp, gu, gd, gs = local_step(tokens, out_grad, window_count, small, wq, wp, up, down)
    gq = gq.astype(full).transpose(2, 3, 1, 0, 4).reshape(C, 3 * C)
    gu = gu.astype(full).reshape(TILES, C, OWNERS, 128).transpose(1, 2, 0, 3).reshape(C, MLP)
    gd = gd.astype(full).transpose(1, 0, 3, 2).reshape(MLP, C)
    gv = gs[:, :12, :owned].transpose(1, 0, 2).reshape(12, C)
    gb = gs[:, 16:40, :count].transpose(0, 2, 1).reshape(TAB_ROWS, HEADS)
    gb = jnp.pad(gb, ((0, table_rows - TAB_ROWS), (0, 0)))
    totals = lax.psum(
        (scatter(gq, scatter_dimension=0), scatter(gp.astype(full).reshape(C, C), scatter_dimension=0), scatter(gu, scatter_dimension=0),
         scatter(gd, scatter_dimension=0), scatter(gv, scatter_dimension=1), scatter(gb, scatter_dimension=0)), "rep")
    states = (
        (qkv_weight, qkv_first, qkv_second), (output_weight, output_first, output_second), (up_weight, up_first, up_second),
        (down_weight, down_first, down_second), (vectors, vector_first, vector_second), (bias_table, table_first, table_second))
    results = [out, grad]
    for i, (state, total, rate) in enumerate(zip(states, totals, step_rates)):
        new = adamw(*state, total, rate)
        results += [*new, new[0].astype(low)] if i < 4 else [*new]
    return tuple(results)


def solution(mesh):
    wins = P(("rep", "shard"), None, None)
    rows = P("shard", None)
    cols = P(None, "shard")
    fits = mesh.shape["rep"] == REPS and mesh.shape["shard"] == OWNERS
    return jax.shard_map(
        shards if fits else shards_general,
        mesh=mesh,
        in_specs=(wins, wins, P(("rep", "shard"))) + (rows,) * 12 + (cols,) * 3 + (rows,) * 3,
        out_specs=(wins, wins) + (rows,) * 16 + (cols,) * 3 + (rows,) * 3,
        check_vma=False,
    )
```

```python
import functools
import math

import jax
import jax.numpy as jnp
import numpy as np
from jax import lax
from jax.experimental import pallas as pl
from jax.experimental.pallas import tpu as pltpu
from jax.sharding import PartitionSpec as P

C = 768
HEADS = 24
MLP = 3072
WIN = 12
STEP = 5
HEAD_DIM = 32
SPAN = 2 * WIN - 1
TOK = WIN * WIN
TAB_ROWS = 536
ROWS = 1024
GROUPS = 3
GCOLS = 256
GHEADS = 8
PACK = GHEADS * TOK
TAB_LANES = 640
TILES = 3
TILE = MLP // TILES
SUB = 512
LINE = 384
MIB = 1 << 20

beta_one = 0.5
beta_two = 0.6
weight_decay = 0.05
adam_eps = 1e-08
norm_eps = 1e-05
step_rates = (0.04, 0.15, 0.04, 0.02, 0.2, 1.0)
low = jnp.bfloat16
full = jnp.float32
NT = (((1,), (1,)), ((), ()))


def dot(a, b):
    return jnp.dot(a, b, preferred_element_type=full)


def dot_nt(a, b):
    return lax.dot_general(a, b, NT, preferred_element_type=full)


def line_matrix():
    out = np.zeros((TAB_LANES, LINE), np.float32)
    col = np.arange(SPAN * WIN)
    out[(col // WIN) * SPAN + col % WIN + WIN - 1, col] = 1.0
    return out


def head_masks():
    lane = np.arange(GCOLS) // HEAD_DIM
    one = (lane[None, :] == np.arange(GHEADS)[:, None]).astype(np.float32)
    return np.broadcast_to(one[:, None, :], (GHEADS, 16, GCOLS))


def norm_parts(z):
    mean = jnp.sum(z, -1, keepdims=True) * (1.0 / C)
    center = z - mean
    spread = jnp.sum(center * center, -1, keepdims=True) * (1.0 / C)
    scale = lax.rsqrt(spread + norm_eps)
    return center * scale, scale


def norm_back(xhat, scale, dn, gain):
    g = dn * gain
    m1 = jnp.sum(g, -1, keepdims=True) * (1.0 / C)
    m2 = jnp.sum(g * xhat, -1, keepdims=True) * (1.0 / C)
    return scale * (g - m1 - xhat * m2)


def diag(x, mask_ref):
    head = x[0:128].reshape(8, 16, GCOLS)
    tail = x[128:144]
    parts = []
    for h in range(GHEADS):
        parts.append((head * mask_ref[h][None]).reshape(128, GCOLS))
    for h in range(GHEADS):
        parts.append(tail * mask_ref[h])
    return jnp.concatenate(parts, 0)


def undiag(xt, m, mask_ref):
    main = []
    for h in range(0, GHEADS, 2):
        r = dot(xt[h * HEAD_DIM : (h + 2) * HEAD_DIM], m[:, h * 128 : (h + 2) * 128])
        main.append(r[0:HEAD_DIM, 0:128])
        main.append(r[HEAD_DIM : 2 * HEAD_DIM, 128:256])
    main = jnp.concatenate(main, 0)
    rest = dot(xt, m[:, GHEADS * 128 :])
    rest_t = rest.T.reshape(GHEADS, 16, GCOLS)
    keep = mask_ref[...].astype(full)
    return jnp.concatenate([main.T, jnp.sum(rest_t * keep, 0)], 0)


def flat(x):
    return x.reshape(x.shape[0] * x.shape[1], x.shape[2])


def blocks(x, owners):
    return x.reshape(owners, x.shape[0] // owners, x.shape[1])


def hidden_place(t, s):
    at = (MLP // GHEADS) * s + 128 * t
    return 8 + at // C, at % C


def unpack_small(small_ref, vec_ref):
    owners = small_ref.shape[0]
    width = C // owners
    count = TAB_ROWS // owners
    vec = jnp.zeros((16, C), full)
    tab = jnp.zeros((HEADS, TAB_LANES), full)
    lane = lax.broadcasted_iota(jnp.int32, (16, 128), 1)
    lane_tab = lax.broadcasted_iota(jnp.int32, (HEADS, 128), 1)
    for s in range(owners):
        piece = small_ref[s].astype(full)
        part = jnp.where(lane < width, piece[0:16], 0.0)
        part = jnp.concatenate([part, jnp.zeros((16, C - 128), full)], 1)
        vec = vec + (pltpu.roll(part, width * s, 1) if s else part)
        part = jnp.where(lane_tab < count, piece[16 : 16 + HEADS], 0.0)
        part = jnp.concatenate([part, jnp.zeros((HEADS, TAB_LANES - 128), full)], 1)
        tab = tab + (pltpu.roll(part, count * s, 1) if s else part)
    vec_ref[...] = vec
    return tab


def pack_small(vec, tab, out_ref):
    owners = out_ref.shape[0]
    width = C // owners
    count = TAB_ROWS // owners
    for s in range(owners):
        out_ref[s, 0:16, :] = (pltpu.roll(vec, C - width * s, 1) if s else vec)[:, 0:128]
        out_ref[s, 16:40, :] = (pltpu.roll(tab, TAB_LANES - count * s, 1) if s else tab)[:, 0:128]


def spread_table(tab, line_ref, tmp_ref):
    shifted = jnp.concatenate([pltpu.roll(tab, cj, 1) if cj else tab for cj in range(WIN)], 0)
    lines = dot(shifted.astype(low), line_ref[...])
    for cj in range(WIN):
        line = lines[cj * HEADS : (cj + 1) * HEADS]
        for rj in range(WIN):
            cut = (WIN - 1 - rj) * WIN
            part = pltpu.roll(line, LINE - cut, 1) if cut else line
            row = (rj * WIN + cj) * HEADS
            tmp_ref[0, row : row + HEADS, :] = part[:, 0:128]
            tmp_ref[1, row : row + HEADS, :] = part[:, 128:256]


def place_bias(tmp_ref, bias_ref):
    lane = lax.broadcasted_iota(jnp.int32, (TOK, 128), 1)
    for g in range(GROUPS):
        rest = jnp.zeros((TOK, 128), full)
        for h in range(GHEADS):
            at = pl.ds(g * GHEADS + h, TOK, stride=HEADS)
            bias_ref[g, :, h * 128 : (h + 1) * 128] = tmp_ref[0, at, :]
            piece = tmp_ref[1, at, :]
            piece = pltpu.roll(piece, 16 * h, 1) if h else piece
            rest = jnp.where((lane >= 16 * h) & (lane < 16 * h + 16), piece, rest)
        bias_ref[g, :, GHEADS * 128 :] = rest


def table_grad(line_ref, tmp_ref, bias_ref):
    lane = lax.broadcasted_iota(jnp.int32, (TOK, 128), 1)
    for g in range(GROUPS):
        rest = bias_ref[g, :, GHEADS * 128 :]
        for h in range(GHEADS):
            at = pl.ds(g * GHEADS + h, TOK, stride=HEADS)
            tmp_ref[0, at, :] = bias_ref[g, :, h * 128 : (h + 1) * 128]
            piece = pltpu.roll(rest, 128 - 16 * h, 1) if h else rest
            tmp_ref[1, at, :] = jnp.where(lane < 16, piece, 0.0)

    def column(cj, total):
        line = jnp.zeros((HEADS, LINE), full)
        for rj in range(WIN):
            cut = (WIN - 1 - rj) * WIN
            row = pl.multiple_of((rj * WIN + cj) * HEADS, 8)
            part = jnp.concatenate([tmp_ref[0, pl.ds(row, HEADS), :], tmp_ref[1, pl.ds(row, HEADS), :], jnp.zeros((HEADS, 128), full)], 1)
            line = line + (pltpu.roll(part, cut, 1) if cut else part)
        high = line.astype(low)
        rest = (line - high.astype(full)).astype(low)
        spread = dot_nt(high, line_ref[...]) + dot_nt(rest, line_ref[...])
        return total + pltpu.roll(spread, TAB_LANES - cj, 1)

    return lax.fori_loop(0, WIN, column, jnp.zeros((HEADS, TAB_LANES), full))


def transpose_rows(src_ref, dst_ref):
    def block(i, carry):
        at = pl.multiple_of(i * 128, 128)
        dst_ref[0 : src_ref.shape[1], pl.ds(at, 128)] = src_ref[pl.ds(at, 128), :].T
        return carry

    lax.fori_loop(0, ROWS // 128, block, 0)


def window_rows(w):
    return slice(w * TOK, (w + 1) * TOK) if isinstance(w, int) else pl.ds(pl.multiple_of(w * TOK, 16), TOK)


def zero_tail(ref, windows):
    at = windows * TOK
    ref[at:ROWS, :] = jnp.zeros((ROWS - at, ref.shape[1]), ref.dtype)


def half_diag(x, half, mask_ref):
    lanes = slice(half * 128, (half + 1) * 128)
    part = x[0:128, lanes].reshape(8, 16, 128)
    heads = range(half * GHEADS // 2, (half + 1) * GHEADS // 2)
    return jnp.concatenate([(part * mask_ref[h, :, lanes][None]).reshape(128, 128) for h in heads], 0)


def rest_diag(x, mask_ref):
    return jnp.concatenate([x[128:144] * mask_ref[h] for h in range(GHEADS)], 0)


def split_diag(x, mask_ref):
    return half_diag(x, 0, mask_ref), half_diag(x, 1, mask_ref), rest_diag(x, mask_ref)


def against_heads(x, split):
    first, second, rest = split
    return jnp.concatenate([dot_nt(x[:, 0:128], first), dot_nt(x[:, 128:256], second), dot_nt(x, rest)], 1)


def over_queries(m, split):
    first, second, rest = split
    return jnp.concatenate([dot(m[:, 0:512], first), dot(m[:, 512:1024], second)], 1) + dot(m[:, 1024:], rest)


def attention_forward(windows, x_ref, small_ref, line_ref, mask_ref, wq_ref, wp_ref,
                      qkv_ref, pt_ref, o_ref, x1_ref, n1t_ref, vec_ref, n1_ref, bias_ref, tmp_ref):
    tab = unpack_small(small_ref, vec_ref)
    spread_table(tab, line_ref, tmp_ref)
    place_bias(tmp_ref, bias_ref)
    zero_tail(n1_ref, windows)
    zero_tail(o_ref, windows)

    def first_norm(w, carry):
        xhat, _ = norm_parts(x_ref[window_rows(w), :].astype(full))
        n1_ref[window_rows(w), :] = (xhat * vec_ref[0:1, :] + vec_ref[1:2, :]).astype(low)
        return carry

    lax.fori_loop(0, windows, first_norm, 0)
    transpose_rows(n1_ref, n1t_ref)

    def group(g, carry):
        cols = pl.ds(pl.multiple_of(g * GCOLS, GCOLS), GCOLS)
        n1 = n1_ref[...]
        qkv_ref[g] = ((dot(n1, flat(wq_ref[g, 0])) + vec_ref[2:3, cols]) * (HEAD_DIM**-0.5)).astype(low)
        qkv_ref[GROUPS + g] = dot(n1, flat(wq_ref[g, 1])).astype(low)
        qkv_ref[2 * GROUPS + g] = (dot(n1, flat(wq_ref[g, 2])) + vec_ref[3:4, cols]).astype(low)

        def window(w, inner):
            rows = window_rows(w)
            q = qkv_ref[g, rows, :]
            k = qkv_ref[GROUPS + g, rows, :]
            v = qkv_ref[2 * GROUPS + g, rows, :]
            s = dot_nt(k, diag(q, mask_ref)) + bias_ref[g]
            e = jnp.exp(s - jnp.max(s, 0, keepdims=True))
            p = (e * (1.0 / jnp.sum(e, 0, keepdims=True))).astype(low)
            pt_ref[g, w] = p
            o_ref[rows, cols] = undiag(v.T, p, mask_ref).astype(low)
            return inner

        lax.fori_loop(0, windows, window, 0)
        return carry

    lax.fori_loop(0, GROUPS, group, 0)

    def output(w, carry):
        rows = window_rows(w)
        branch = dot(o_ref[rows, :], flat(wp_ref[...])) + vec_ref[4:5, :]
        x1_ref[rows, :] = x_ref[rows, :].astype(full) + branch
        return carry

    lax.fori_loop(0, windows, output, 0)


def gelu_both(h):
    c = math.sqrt(2.0 / math.pi)
    square = h * h
    t = jnp.tanh(h * (c + (c * 0.044715) * square))
    half = 0.5 + 0.5 * t
    act = h * half
    return act, half + act * (1.0 - half) * (2.0 * c + (6.0 * c * 0.044715) * square)


def feed_forward(windows, x1_ref, dy_ref, live_ref, vec_ref, up_ref, down_ref, wp_ref, o_ref,
                 out_ref, dx1_ref, do_ref, gup_ref, gdown_ref, gout_ref, sums_ref,
                 n2_ref, n2t_ref, dy2_ref, dyt_ref, y_ref, dn_ref, bu_ref, bsum_ref):
    zero_tail(n2_ref, windows)
    zero_tail(dy2_ref, windows)

    def second_norm(w, carry):
        rows = window_rows(w)
        xhat, _ = norm_parts(x1_ref[rows, :])
        n2_ref[rows, :] = (xhat * vec_ref[5:6, :] + vec_ref[6:7, :]).astype(low)
        dy2_ref[rows, :] = (dy_ref[rows, :].astype(full) * live_ref[w]).astype(low)
        return carry

    lax.fori_loop(0, windows, second_norm, 0)
    transpose_rows(n2_ref, n2t_ref)
    transpose_rows(dy2_ref, dyt_ref)
    y_ref[...] = jnp.zeros_like(y_ref)
    dn_ref[...] = jnp.zeros_like(dn_ref)
    owners = gup_ref.shape[1]
    for t in range(TILES):
        for s in range(TILE // 128):
            row, at = hidden_place(t, s)
            bu_ref[t, :, s * 128 : (s + 1) * 128] = vec_ref[row : row + 1, at : at + 128]

    def step(t, carry):
        for part in range(TILE // SUB):
            cols = slice(part * SUB, (part + 1) * SUB)
            up = flat(up_ref[t, :, :, cols])
            down = flat(down_ref[t, part * SUB // 128 : (part + 1) * SUB // 128])
            h = dot(n2_ref[...], up) + bu_ref[t, :, cols]
            da = dot_nt(dy2_ref[...], down)
            act, slope = gelu_both(h)
            a = act.astype(low)
            dh = (da * slope).astype(low)
            bsum_ref[t, :, cols] = jnp.sum(dh.astype(full), 0, keepdims=True)
            y_ref[...] += dot(a, down)
            dn_ref[...] += dot_nt(dh, up)
            gd = dot(dyt_ref[...], a).astype(low)
            for b in range(SUB // 128):
                gdown_ref[t, part * SUB // 128 + b] = gd[:, b * 128 : (b + 1) * 128]
            gup_ref[t, :, :, cols] = blocks(dot(n2t_ref[...], dh).astype(low), owners)
        return carry

    lax.fori_loop(0, TILES, step, 0)
    sums_ref[...] = jnp.zeros_like(sums_ref)
    for t in range(TILES):
        for s in range(TILE // 128):
            row, at = hidden_place(t, s)
            sums_ref[row : row + 1, at : at + 128] = bsum_ref[t, :, s * 128 : (s + 1) * 128]
    zero_tail(dx1_ref, windows)

    def finish(w, carry):
        rows = window_rows(w)
        x1 = x1_ref[rows, :]
        out_ref[rows, :] = ((x1 + y_ref[rows, :] + vec_ref[7:8, :]) * live_ref[w]).astype(low)
        xhat, scale = norm_parts(x1)
        dn = dn_ref[rows, :]
        dy = dy2_ref[rows, :].astype(full)
        dx1 = dy + norm_back(xhat, scale, dn, vec_ref[5:6, :])
        dx1_ref[rows, :] = dx1
        dr = dx1.astype(low)
        n2_ref[rows, :] = dr
        do_ref[rows, :] = dot_nt(dr, flat(wp_ref[...])).astype(low)
        sums_ref[4:5, :] += jnp.sum(dr.astype(full), 0, keepdims=True)
        sums_ref[5:6, :] += jnp.sum(dn * xhat, 0, keepdims=True)
        sums_ref[6:7, :] += jnp.sum(dn, 0, keepdims=True)
        sums_ref[7:8, :] += jnp.sum(dy, 0, keepdims=True)
        return carry

    lax.fori_loop(0, windows, finish, 0)
    transpose_rows(o_ref, dyt_ref)
    for g in range(GROUPS):
        at = pl.ds(g * GCOLS, GCOLS)
        gout_ref[:, :, at] = blocks(dot(dyt_ref[...], n2_ref[:, at]).astype(low), gout_ref.shape[0])


def attention_backward(windows, x_ref, vec_ref, line_ref, mask_ref, wq_ref, qkv_ref, pt_ref, do_ref, dx1_ref, n1t_ref, sums_in_ref,
                       gq_ref, gsmall_ref, grad_ref, sums_ref, bias_ref, tmp_ref, dproj_ref, dn_ref):
    bias_ref[...] = jnp.zeros_like(bias_ref)
    dn_ref[...] = jnp.zeros_like(dn_ref)
    sums_ref[...] = sums_in_ref[...]
    for part in range(3):
        dproj_ref[part, windows * TOK :, :] = jnp.zeros((ROWS - windows * TOK, GCOLS), low)

    def group(g, carry):
        cols = pl.ds(pl.multiple_of(g * GCOLS, GCOLS), GCOLS)

        def window(w, inner):
            rows = window_rows(w)
            q = qkv_ref[g, rows, :]
            k = qkv_ref[GROUPS + g, rows, :]
            v = qkv_ref[2 * GROUPS + g, rows, :]
            p = pt_ref[g, w]
            do = diag(do_ref[rows, cols], mask_ref)
            dp = dot_nt(v, do)
            dv = dot(p, do)
            pf = p.astype(full)
            ds = (pf * (dp - jnp.sum(pf * dp, 0, keepdims=True))).astype(low)
            bias_ref[g] += ds.astype(full)
            dk = dot(ds, diag(q, mask_ref))
            dq = undiag(k.T, ds, mask_ref) * (HEAD_DIM**-0.5)
            dq = dq.astype(low)
            dv = dv.astype(low)
            dproj_ref[0, rows, :] = dq
            dproj_ref[1, rows, :] = dk.astype(low)
            dproj_ref[2, rows, :] = dv
            sums_ref[2:3, cols] += jnp.sum(dq.astype(full), 0, keepdims=True)
            sums_ref[3:4, cols] += jnp.sum(dv.astype(full), 0, keepdims=True)
            return inner

        lax.fori_loop(0, windows, window, 0)
        for part in range(3):
            d = dproj_ref[part]
            gq_ref[g, part] = blocks(dot(n1t_ref[...], d).astype(low), gq_ref.shape[2])
            dn_ref[...] += dot_nt(d, flat(wq_ref[g, part]))
        return carry

    lax.fori_loop(0, GROUPS, group, 0)

    def finish(w, carry):
        rows = window_rows(w)
        xhat, scale = norm_parts(x_ref[rows, :].astype(full))
        dn = dn_ref[rows, :]
        grad_ref[rows, :] = dx1_ref[rows, :] + norm_back(xhat, scale, dn, vec_ref[0:1, :])
        sums_ref[0:1, :] += jnp.sum(dn * xhat, 0, keepdims=True)
        sums_ref[1:2, :] += jnp.sum(dn, 0, keepdims=True)
        return carry

    lax.fori_loop(0, windows, finish, 0)
    pack_small(sums_ref[...], table_grad(line_ref, tmp_ref, bias_ref), gsmall_ref)


MESH = pl.DeviceIdType.MESH
REPS = 4
OWNERS = 8
LINKS = OWNERS // 2


class Spot:
    def __init__(self):
        self.rep = lax.axis_index("rep")
        self.shard = lax.axis_index("shard")
        self.z = self.shard // 2
        self.core = self.shard % 2

    def sibling(self):
        return (self.rep, self.z * 2 + (1 - self.core))

    def along_z(self, step):
        return (self.rep, ((self.z + step) % LINKS) * 2 + self.core)

    def turned(self, axis):
        x, y = self.rep % 2, self.rep // 2
        return y * 2 + (1 - x) if axis == 0 else (1 - y) * 2 + x

    def beside(self, axis):
        return (self.turned(axis), self.shard)

    def across(self):
        return (REPS - 1 - self.rep, self.shard)


def greet(spot):
    barrier = pltpu.get_barrier_semaphore()
    peers = [(spot.rep, (spot.shard + i) % OWNERS) for i in range(1, OWNERS)]
    peers += [((spot.rep + i) % REPS, spot.shard) for i in range(1, REPS)]
    for peer in peers:
        pl.semaphore_signal(barrier, inc=1, device_id=peer, device_id_type=MESH)
    return barrier, len(peers)


def send(src, dst, send_sem, recv_sem, peer):
    pltpu.make_async_remote_copy(src_ref=src, dst_ref=dst, send_sem=send_sem, recv_sem=recv_sem, device_id=peer, device_id_type=MESH).start()


def await_bytes(ref, sem):
    pltpu.make_async_copy(ref, ref, sem).wait()


def quarter(ref, rep):
    rows, cols = ref.shape[-2:]
    lead = (slice(None),) * (len(ref.shape) - 2)
    top = pl.multiple_of((rep // 2) * (rows // 2), 16)
    left = pl.multiple_of((rep % 2) * (cols // 2), 128)
    return ref.at[lead + (pl.ds(top, rows // 2), pl.ds(left, cols // 2))]


def half(ref, rep, axis):
    rows, cols = ref.shape[-2:]
    lead = (slice(None),) * (len(ref.shape) - 2)
    if axis == 0:
        left = pl.multiple_of((rep % 2) * (cols // 2), 128)
        return ref.at[lead + (slice(None), pl.ds(left, cols // 2))]
    top = pl.multiple_of((rep // 2) * (rows // 2), 16)
    return ref.at[lead + (pl.ds(top, rows // 2), slice(None))]


class Gather:
    KINDS = (LINKS - 1, LINKS - 1, LINKS - 1, LINKS - 1, LINKS)
    SEMS = 2 * sum(KINDS)
    STAGES = ("start", "across", "relay", "beside", "finish")

    def __init__(self, spot, place, axis, sems, direct=False):
        self.spot, self.place, self.axis, self.sems, self.direct = spot, place, axis, sems, direct

    def sem(self, side, kind, i):
        return self.sems.at[side * (self.SEMS // 2) + sum(self.KINDS[:kind]) + i]

    def block(self, step):
        return self.place(((self.spot.z - step + LINKS) % LINKS) * 2 + self.spot.core)

    def other(self, step):
        return self.place(((self.spot.z - step + LINKS) % LINKS) * 2 + 1 - self.spot.core)

    def start(self):
        spot = self.spot
        mine = self.block(0)
        for i in range(1, LINKS):
            piece = quarter(mine, spot.rep)
            send(piece, piece, self.sem(0, 0, i - 1), self.sem(1, 0, i - 1), spot.along_z(i))
        send(mine, mine, self.sem(0, 4, 0), self.sem(1, 4, 0), spot.sibling())

    def across(self):
        spot = self.spot
        for i in range(1, LINKS):
            piece = quarter(self.block(i), spot.rep)
            await_bytes(piece, self.sem(1, 0, i - 1))
            for axis in (self.axis, 1 - self.axis):
                send(piece, piece, self.sem(0, 1 + axis, i - 1), self.sem(1, 1 + axis, i - 1), spot.beside(axis))
            if self.direct:
                send(piece, piece, self.sem(0, 3, i - 1), self.sem(1, 3, i - 1), spot.across())

    def relay(self):
        spot = self.spot
        if self.direct:
            return
        for i in range(1, LINKS):
            piece = quarter(self.block(i), spot.turned(self.axis))
            await_bytes(piece, self.sem(1, 1 + self.axis, i - 1))
            send(piece, piece, self.sem(0, 3, i - 1), self.sem(1, 3, i - 1), spot.beside(1 - self.axis))

    def beside(self):
        spot = self.spot
        for i in range(1, LINKS):
            block = self.block(i)
            piece = quarter(block, spot.rep)
            if self.direct:
                await_bytes(piece, self.sem(1, 1 + self.axis, i - 1))
            await_bytes(piece, self.sem(1, 2 - self.axis, i - 1))
            await_bytes(piece, self.sem(1, 3, i - 1))
            send(block, block, self.sem(0, 4, i), self.sem(1, 4, i), spot.sibling())

    def finish(self):
        for i in range(LINKS):
            await_bytes(self.other(i), self.sem(1, 4, i))

    def close(self):
        piece = quarter(self.block(0), self.spot.rep)
        for kind in range(4):
            for i in range(1, LINKS):
                await_bytes(piece, self.sem(0, kind, i - 1))
        for i in range(LINKS):
            await_bytes(self.block(i), self.sem(0, 4, i))


class Reduce:
    KINDS = (LINKS, 1, 1, LINKS - 1, REPS - 1)
    SEMS = 2 * sum(KINDS)
    STAGES = ("start", "first", "second", "along", "spread", "passed", "finish")

    def __init__(self, spot, place, out, core_sum, halves, quarters, links, axis, sems, direct):
        self.spot, self.place, self.out, self.axis, self.sems, self.direct = spot, place, out, axis, sems, direct
        self.core_sum, self.halves, self.quarters, self.links = core_sum, halves, quarters, links

    def sem(self, side, kind, i):
        return self.sems.at[side * (self.SEMS // 2) + sum(self.KINDS[:kind]) + i]

    def start(self):
        spot = self.spot
        for z in range(LINKS):
            send(self.place(z * 2 + (1 - spot.core)), self.core_sum.at[z], self.sem(0, 0, z), self.sem(1, 0, z), spot.sibling())

    def first(self):
        spot = self.spot
        for z in range(LINKS):
            total = self.core_sum.at[z]
            await_bytes(total, self.sem(1, 0, z))
            total[...] = (total[...].astype(full) + self.place(z * 2 + spot.core)[...].astype(full)).astype(low)
        theirs = half(self.core_sum, spot.turned(self.axis), self.axis)
        send(theirs, self.halves, self.sem(0, 1, 0), self.sem(1, 1, 0), spot.beside(self.axis))

    def second(self):
        spot = self.spot
        await_bytes(self.halves, self.sem(1, 1, 0))
        mine = half(self.core_sum, spot.rep, self.axis)
        self.halves[...] = (self.halves[...].astype(full) + mine[...].astype(full)).astype(low)
        theirs = half(self.halves, spot.turned(1 - self.axis), 1 - self.axis)
        send(theirs, self.quarters, self.sem(0, 2, 0), self.sem(1, 2, 0), spot.beside(1 - self.axis))

    def along(self):
        spot = self.spot
        await_bytes(self.quarters, self.sem(1, 2, 0))
        mine = half(self.halves, spot.rep, 1 - self.axis)
        self.quarters[...] = (self.quarters[...].astype(full) + mine[...].astype(full)).astype(low)
        for i in range(1, LINKS):
            send(self.quarters.at[(spot.z + i) % LINKS], self.links.at[i - 1], self.sem(0, 3, i - 1), self.sem(1, 3, i - 1), spot.along_z(i))

    def spread(self):
        spot = self.spot
        total = self.quarters[spot.z].astype(full)
        for i in range(1, LINKS):
            await_bytes(self.links.at[i - 1], self.sem(1, 3, i - 1))
            total = total + self.links[i - 1].astype(full)
        mine = quarter(self.out, spot.rep)
        mine[...] = total.astype(low)
        for axis in (self.axis, 1 - self.axis):
            send(mine, mine, self.sem(0, 4, axis), self.sem(1, 4, axis), spot.beside(axis))
        if self.direct:
            send(mine, mine, self.sem(0, 4, 2), self.sem(1, 4, 2), spot.across())

    def passed(self):
        spot = self.spot
        theirs = quarter(self.out, spot.turned(self.axis))
        await_bytes(theirs, self.sem(1, 4, self.axis))
        if not self.direct:
            send(theirs, theirs, self.sem(0, 4, 2), self.sem(1, 4, 2), spot.beside(1 - self.axis))

    def finish(self):
        spot = self.spot
        await_bytes(quarter(self.out, spot.turned(1 - self.axis)), self.sem(1, 4, 1 - self.axis))
        await_bytes(quarter(self.out, REPS - 1 - spot.rep), self.sem(1, 4, 2))

    def close(self):
        for z in range(LINKS):
            await_bytes(self.core_sum.at[z], self.sem(0, 0, z))
        await_bytes(self.halves, self.sem(0, 1, 0))
        await_bytes(self.quarters, self.sem(0, 2, 0))
        for i in range(1, LINKS):
            await_bytes(self.links.at[i - 1], self.sem(0, 3, i - 1))
        for j in range(1, REPS):
            await_bytes(quarter(self.out, self.spot.rep), self.sem(0, 4, j - 1))


class ReduceDirect(Reduce):
    KINDS = (LINKS, REPS - 1, 0, LINKS - 1, REPS - 1)
    SEMS = 2 * sum(KINDS)

    def peers(self):
        spot = self.spot
        return (spot.turned(0), spot.turned(1), REPS - 1 - spot.rep)

    def first(self):
        spot = self.spot
        for z in range(LINKS):
            total = self.core_sum.at[z]
            await_bytes(total, self.sem(1, 0, z))
            total[...] = (total[...].astype(full) + self.place(z * 2 + spot.core)[...].astype(full)).astype(low)
        for j, rep in enumerate(self.peers()):
            send(quarter(self.core_sum, rep), self.halves.at[j], self.sem(0, 1, j), self.sem(1, 1, j), (rep, spot.shard))

    def second(self):
        pass

    def along(self):
        spot = self.spot
        total = quarter(self.core_sum, spot.rep)[...].astype(full)
        for j in range(REPS - 1):
            await_bytes(self.halves.at[j], self.sem(1, 1, j))
            total = total + self.halves[j].astype(full)
        self.quarters[...] = total.astype(low)
        for i in range(1, LINKS):
            send(self.quarters.at[(spot.z + i) % LINKS], self.links.at[i - 1], self.sem(0, 3, i - 1), self.sem(1, 3, i - 1), spot.along_z(i))

    def close(self):
        for z in range(LINKS):
            await_bytes(self.core_sum.at[z], self.sem(0, 0, z))
        for j in range(REPS - 1):
            await_bytes(self.halves.at[j], self.sem(0, 1, j))
        for i in range(1, LINKS):
            await_bytes(self.links.at[i - 1], self.sem(0, 3, i - 1))
        for j in range(1, REPS):
            await_bytes(quarter(self.out, self.spot.rep), self.sem(0, 4, j - 1))


class ReduceSmall:
    KINDS = (LINKS, LINKS - 1, REPS - 1)
    SEMS = 2 * sum(KINDS)
    STAGES = ("start", "first", "second", "along")

    def __init__(self, spot, terms, out, core_sum, links, parts, sems):
        self.spot, self.terms, self.out, self.core_sum, self.links, self.parts, self.sems = spot, terms, out, core_sum, links, parts, sems

    sem = Reduce.sem

    def start(self):
        spot = self.spot
        for z in range(LINKS):
            send(self.terms.at[z * 2 + (1 - spot.core)], self.core_sum.at[z], self.sem(0, 0, z), self.sem(1, 0, z), spot.sibling())

    def first(self):
        spot = self.spot
        for z in range(LINKS):
            await_bytes(self.core_sum.at[z], self.sem(1, 0, z))
            self.core_sum[z] = self.core_sum[z] + self.terms[z * 2 + spot.core]
        for i in range(1, LINKS):
            send(self.core_sum.at[(spot.z + i) % LINKS], self.links.at[i - 1], self.sem(0, 1, i - 1), self.sem(1, 1, i - 1), spot.along_z(i))

    def second(self):
        spot = self.spot
        total = self.core_sum[spot.z]
        for i in range(1, LINKS):
            await_bytes(self.links.at[i - 1], self.sem(1, 1, i - 1))
            total = total + self.links[i - 1]
        self.parts[spot.rep] = total
        mine = self.parts.at[spot.rep]
        for j in range(1, REPS):
            send(mine, mine, self.sem(0, 2, j - 1), self.sem(1, 2, j - 1), ((spot.rep + j) % REPS, spot.shard))

    def along(self):
        for j in range(1, REPS):
            await_bytes(self.parts.at[(self.spot.rep - j + REPS) % REPS], self.sem(1, 2, j - 1))
        total = self.parts[0]
        for j in range(1, REPS):
            total = total + self.parts[j]
        self.out[...] = total

    def close(self):
        for z in range(LINKS):
            await_bytes(self.core_sum.at[z], self.sem(0, 0, z))
        for i in range(1, LINKS):
            await_bytes(self.links.at[i - 1], self.sem(0, 1, i - 1))
        for j in range(1, REPS):
            await_bytes(self.parts.at[self.spot.rep], self.sem(0, 2, j - 1))


OWNED = C // OWNERS
SLOTS = TILES + 1
GATHERS = 2 * TILES + 1 + GROUPS
REDUCES = 2 * TILES + 1 + (GROUPS - 1) + 3
W_Q0, W_Q1, W_Q2, W_P, W_U0, W_D0, W_U1, W_D1, W_U2, W_D2 = W_ALL = range(10)
G_D0, G_U0, G_D1, G_U1, G_D2, G_U2, G_P, G_Q0, G_Q1, G_Q2, G_K2, G_V2, G_S = G_ALL = range(10, 23)
W_Q, W_U, W_D = (W_Q0, W_Q1, W_Q2), (W_U0, W_U1, W_U2), (W_D0, W_D1, W_D2)
G_D, G_U, G_Q, G_LAST = (G_D0, G_D1, G_D2), (G_U0, G_U1, G_U2), (G_Q0, G_Q1), (G_Q2, G_K2, G_V2)
G_TWO = ()
START, ACROSS, RELAY, BESIDE, ARRIVED = range(5)
FIRST, SECOND, ALONG, SPREAD, PASSED, SUMMED = range(1, 7)
BEFORE = {
    2: ((W_Q0, ACROSS), (W_P, START),),
    3: ((W_Q2, START),),
    4: ((W_Q0, RELAY), (W_U0, START),),
    5: ((W_Q0, BESIDE), (W_Q1, ACROSS),),
}
FORWARD = {
    0: ((W_Q1, RELAY), (W_Q2, ACROSS), (W_P, ACROSS), (W_D0, START), (W_U1, START),),
    2: ((W_D1, START),),
    4: ((W_Q1, BESIDE),),
    5: ((W_U0, ACROSS),),
    6: ((W_Q2, RELAY),),
    7: ((W_P, RELAY),),
    8: ((W_D0, ACROSS),),
    11: ((W_Q2, BESIDE), (W_U0, RELAY),),
    12: ((W_U1, ACROSS),),
    14: ((W_D0, RELAY), (W_U2, START), (W_D2, START),),
    16: ((W_D1, ACROSS),),
    17: ((W_P, BESIDE), (W_U0, BESIDE),),
    18: ((W_U1, RELAY),),
}
MIDDLE = {
    0: ((W_D0, BESIDE), (W_U2, ACROSS),),
    1: ((W_D1, RELAY),),
    2: ((W_U1, BESIDE), (W_D2, ACROSS),),
}
TILE_STEP = {
    1: ((W_D1, BESIDE), (W_U2, RELAY), (W_D2, RELAY),),
    2: ((W_U2, BESIDE), (W_D2, BESIDE),),
    3: ((G_D0, FIRST), (G_U0, FIRST),),
    5: ((G_D0, SECOND), (G_U0, SECOND), (G_D1, FIRST), (G_U1, FIRST),),
}
AFTER_TILES = {
    0: ((G_D0, ALONG), (G_U0, ALONG),),
    2: ((G_D2, FIRST), (G_U2, FIRST),),
    3: ((G_U1, SECOND),),
}
BACKWARD = {
    2: ((G_D0, SPREAD), (G_U0, SPREAD),),
    3: ((G_D1, SECOND), (G_P, FIRST),),
    7: ((G_D2, SECOND),),
    8: ((G_U2, SECOND),),
    9: ((G_U1, ALONG),),
    10: ((G_Q0, FIRST),),
    11: ((G_U0, SUMMED), (G_D1, ALONG),),
    12: ((G_D0, SUMMED),),
    14: ((G_D2, ALONG), (G_P, SECOND),),
    16: ((G_U1, SPREAD), (G_Q0, SECOND),),
    17: ((G_D1, SPREAD), (G_U2, ALONG), (G_Q1, FIRST),),
    20: ((G_D2, SPREAD), (G_P, ALONG),),
}
LAST_STEPS = {
    0: ((G_Q2, FIRST), (G_Q2, SECOND), (G_K2, FIRST),),
    1: ((G_U2, SPREAD), (G_P, SPREAD), (G_Q0, ALONG), (G_V2, FIRST),),
    2: ((G_D1, SUMMED),),
    3: ((G_U1, SUMMED), (G_Q0, SPREAD), (G_Q1, SECOND), (G_K2, SECOND), (G_V2, SECOND),),
}


def chunk_shapes():
    out = []
    for _ in range(TILES):
        out += [(128, C), (OWNED, TILE)]
    return out + [(OWNED, C)] + [(3, OWNED, GCOLS)] * (GROUPS - 1) + [(OWNED, GCOLS)] * 3


def reduce_scratch():
    out = []
    for i, dims in enumerate(chunk_shapes()):
        *lead, rows, cols = dims
        near = (rows, cols // 2) if i % 2 == 0 else (rows // 2, cols)
        near = (LINKS, *lead, *near) if i < REDUCES - 3 else (REPS - 1, LINKS, *lead, rows // 2, cols // 2)
        out.append(pltpu.VMEM((LINKS, *dims), low))
        out.append(pltpu.VMEM(near, low))
        out.append(pltpu.VMEM((LINKS, *lead, rows // 2, cols // 2), low))
        out.append(pltpu.VMEM((LINKS - 1, *lead, rows // 2, cols // 2), low))
    out += [pltpu.VMEM((LINKS, 40, 128), full), pltpu.VMEM((LINKS - 1, 40, 128), full), pltpu.VMEM((REPS, 40, 128), full)]
    return out


def layer_kernel(windows, x_hbm, dy_hbm, count_ref, q32, p32, u32, d32, vec_in, tab_in, line_ref, mask_ref,
                 out_hbm, grad_hbm, gq_out, gp_out, gu_out, gd_out, gs_out, qkv_hbm, pt_hbm, n1_hbm, *scratch):
    wq, wp, up, down, small, o_ref, x1_ref, vec_ref, sums_ref, terms_ref = scratch[:10]
    gather_sems, reduce_sems, small_sems, small_reduce_sems, local = scratch[-5:]
    reduce_refs = scratch[10:-5]
    spot = Spot()
    rows_all = windows * TOK

    def live(w):
        return (w < count_ref[0]).astype(full)

    mine = spot.shard
    V = pltpu.VMEM

    jobs = {}
    places = [(W_Q[g], lambda s, g=g: wq.at[g, :, s]) for g in range(GROUPS)] + [(W_P, lambda s: wp.at[s])]
    for t in range(TILES):
        places += [(W_U[t], lambda s, t=t: up.at[t, s]), (W_D[t], lambda s, t=t: down.at[t, s])]
    for i, (name, place) in enumerate(places):
        jobs[name] = Gather(spot, place, i % 2, gather_sems.at[i], direct=name == W_Q0)
    places = []
    for t in range(TILES):
        slot = (t + SLOTS - 1) % SLOTS
        places.append((G_D[t], lambda s, slot=slot: down.at[slot, s], gd_out.at[t]))
        places.append((G_U[t], lambda s, slot=slot: up.at[slot, s], gu_out.at[t]))
    places.append((G_P, lambda s: wp.at[s], gp_out))
    for g in range(GROUPS - 1):
        places.append((G_Q[g], lambda s, g=g: wq.at[g, :, s], gq_out.at[g]))
    for part in range(3):
        places.append((G_LAST[part], lambda s, part=part: up.at[TILES - 1, s, :, pl.ds(part * GCOLS, GCOLS)], gq_out.at[GROUPS - 1, part]))
    for i, (name, place, out) in enumerate(places):
        kind = ReduceDirect if name in G_LAST else Reduce
        jobs[name] = kind(spot, place, out, *reduce_refs[4 * i : 4 * i + 4], i % 2, reduce_sems.at[i], name not in G_TWO)
    jobs[G_S] = ReduceSmall(spot, terms_ref, gs_out, *reduce_refs[-3:], small_reduce_sems)

    done = {}

    def run(name, upto):
        for stage in range(done.get(name, 0), upto + 1):
            getattr(jobs[name], jobs[name].STAGES[stage])()
        done[name] = max(done.get(name, 0), upto + 1)

    def hook(table, place):
        for item in table.get(place, ()):
            run(*item)

    def hook_window(table, g, w):
        for at in range(windows):
            place = g * windows + at
            if place in table:

                @pl.when(w == at)
                def _(place=place):
                    hook(table, place)

    barrier, peers = greet(spot)

    def cast(q_v, p_v, u_v, d_v):
        loads = [pltpu.make_async_copy(a, b, local.at[i]) for i, (a, b) in enumerate(((q32, q_v), (p32, p_v), (u32, u_v), (d32, d_v)))]
        for load in loads:
            load.start()
        small[mine] = jnp.zeros((48, 128), low)
        pad = jnp.zeros((16, 128), full)
        vec_ref[:, 0:128] = pad
        vec_ref[0:12, 0:OWNED] = vec_in[...]
        small[mine, 0:16, :] = vec_ref[:, 0:128].astype(low)
        x1_ref[0:32, 0:128] = jnp.zeros((32, 128), full)
        x1_ref[0:HEADS, 0 : tab_in.shape[1]] = tab_in[...]
        small[mine, 16:48, :] = x1_ref[0:32, 0:128].astype(low)
        loads[0].wait()
        for g in range(GROUPS):
            for part in range(3):
                wq[g, part, mine] = q_v[:, part * C + g * GCOLS : part * C + (g + 1) * GCOLS].astype(low)
        pl.semaphore_wait(barrier, peers)
        for i in range(1, OWNERS):
            send(small.at[mine], small.at[mine], small_sems.at[i], small_sems.at[OWNERS + i], (spot.rep, (mine + i) % OWNERS))
        run(W_Q0, START)
        run(W_Q1, START)
        loads[1].wait()
        wp[mine] = p_v[...].astype(low)
        loads[2].wait()
        loads[3].wait()
        for t in range(TILES):
            for s in range(OWNERS):
                src = (MLP // OWNERS) * s + 128 * t
                up[t, mine, :, s * 128 : (s + 1) * 128] = u_v[:, src : src + 128].astype(low)
            down[t, mine] = d_v[t * 128 : (t + 1) * 128, :].astype(low)

    pl.run_scoped(cast, V((OWNED, 3 * C), full), V((OWNED, C), full), V((OWNED, MLP), full), V((TILES * 128, C), full))

    def forward(dy_ref, dyt_ref, x_ref, n1_ref, qkv_ref, pt_ref, bias_ref):
        load = pltpu.make_async_copy(x_hbm, x_ref, local.at[0])
        load.start()
        load_dy = pltpu.make_async_copy(dy_hbm, dy_ref.at[0:rows_all], local.at[2])
        load_dy.start()
        zero_tail(n1_ref, windows)
        zero_tail(dy_ref, windows)
        zero_tail(o_ref, windows)
        for i in range(1, OWNERS):
            await_bytes(small.at[(mine - i + OWNERS) % OWNERS], small_sems.at[OWNERS + i])
        tab = unpack_small(small, vec_ref)
        hook(BEFORE, 0)
        load.wait()
        hook(BEFORE, 1)

        def first_norm(w, carry):
            xhat, _ = norm_parts(x_ref[window_rows(w), :].astype(full))
            n1_ref[window_rows(w), :] = (xhat * vec_ref[0:1, :] + vec_ref[1:2, :]).astype(low)
            return carry

        lax.fori_loop(0, windows, first_norm, 0)
        hook(BEFORE, 2)
        save = pltpu.make_async_copy(n1_ref, n1_hbm, local.at[1])
        save.start()
        hook(BEFORE, 3)
        load_dy.wait()

        def keep_live(w, carry):
            dy_ref[window_rows(w), :] = (dy_ref[window_rows(w), :].astype(full) * live(w)).astype(low)
            return carry

        lax.fori_loop(0, windows, keep_live, 0)
        transpose_rows(dy_ref, dyt_ref)
        hook(BEFORE, 4)

        def bias(tmp_ref):
            spread_table(tab, line_ref, tmp_ref)
            hook(BEFORE, 5)
            place_bias(tmp_ref, bias_ref)

        pl.run_scoped(bias, V((2, TOK * HEADS, 128), full))
        for g in range(GROUPS):
            cols = slice(g * GCOLS, (g + 1) * GCOLS)
            held = qkv_ref.at[g % 2]
            if g >= 2:
                pltpu.make_async_copy(held, qkv_hbm.at[g - 2], local.at[2 + g % 2]).wait()
            run(W_Q[g], ARRIVED)
            n1 = n1_ref[...]
            held[0] = ((dot(n1, flat(wq[g, 0])) + vec_ref[2:3, cols]) * (HEAD_DIM**-0.5)).astype(low)
            held[1] = dot(n1, flat(wq[g, 1])).astype(low)
            held[2] = (dot(n1, flat(wq[g, 2])) + vec_ref[3:4, cols]).astype(low)
            pltpu.make_async_copy(held, qkv_hbm.at[g], local.at[2 + g % 2]).start()

            def window(w, carry, g=g, cols=cols, held=held):
                hook_window(FORWARD, g, w)
                rows = window_rows(w)
                n = g * windows + w
                slot = n % 2
                s = against_heads(held[1, rows, :], split_diag(held[0, rows, :], mask_ref)) + bias_ref[g]
                e = jnp.exp(s - jnp.max(s, 0, keepdims=True))
                p = (e * (1.0 / jnp.sum(e, 0, keepdims=True))).astype(low)
                keep = pltpu.make_async_copy(pt_ref.at[slot], pt_hbm.at[n], local.at[4 + slot])

                @pl.when(n >= 2)
                def _():
                    keep.wait()

                pt_ref[slot] = p
                keep.start()
                o_ref[rows, cols] = undiag(held[2, rows, :].T, p, mask_ref).astype(low)
                return carry

            lax.fori_loop(0, windows, window, 0)

        run(W_P, ARRIVED)

        x1_ref[...] = x_ref[...].astype(full) + (dot(o_ref[0:rows_all], flat(wp[...])) + vec_ref[4:5, :])
        save.wait()
        for g in (GROUPS - 2, GROUPS - 1):
            pltpu.make_async_copy(qkv_ref.at[g % 2], qkv_hbm.at[g], local.at[2 + g % 2]).wait()
        for slot in range(2):
            pltpu.make_async_copy(pt_ref.at[slot], pt_hbm.at[0], local.at[4 + slot]).wait()

    def middle(dy_ref, dyt_ref, n2_ref, n2t_ref, y_ref, dn_ref, bu_ref, bsum_ref):
        zero_tail(n2_ref, windows)
        hook(MIDDLE, 0)

        def second_norm(w, carry):
            rows = window_rows(w)
            xhat, _ = norm_parts(x1_ref[rows, :])
            n2_ref[rows, :] = (xhat * vec_ref[5:6, :] + vec_ref[6:7, :]).astype(low)
            return carry

        lax.fori_loop(0, windows, second_norm, 0)
        transpose_rows(n2_ref, n2t_ref)
        hook(MIDDLE, 1)
        n2t_ref[C:, :] = jnp.ones((16, ROWS), low)
        y_ref[...] = jnp.zeros_like(y_ref)
        dn_ref[...] = jnp.zeros_like(dn_ref)
        for t in range(TILES):
            for s in range(TILE // 128):
                row, left = hidden_place(t, s)
                bu_ref[t, :, s * 128 : (s + 1) * 128] = vec_ref[row : row + 1, left : left + 128]
        hook(MIDDLE, 2)
        run(W_U0, ARRIVED)
        run(W_D0, ARRIVED)
        hook(TILE_STEP, 0)
        halves = TILE // SUB

        def step(i, carry):
            for k in range(1, TILES * halves):

                @pl.when(i == k)
                def _(k=k):
                    if k % halves == 0:
                        t = k // halves
                        for name in (W_U[t], W_D[t]):
                            run(name, ARRIVED)
                        for name in (W_U[t - 1], W_D[t - 1]):
                            jobs[name].close()
                        for name in (G_D[t - 1], G_U[t - 1]):
                            run(name, START)
                    hook(TILE_STEP, k)

            t, part = i // halves, i % halves
            cols = pl.ds(pl.multiple_of(part * SUB, SUB), SUB)
            wide = SUB // 128
            slot = (t + SLOTS - 1) % SLOTS
            u = flat(up[t, :, :, cols])
            d = flat(down[t, pl.ds(part * wide, wide)])
            h = dot(n2_ref[...], u) + bu_ref[t, :, cols]
            da = dot_nt(dy_ref[...], d)
            act, slope = gelu_both(h)
            a = act.astype(low)
            dh = (da * slope).astype(low)
            y_ref[...] += dot(a, d)
            dn_ref[...] += dot_nt(dh, u)
            gd = dot(dyt_ref[...], a).astype(low)
            down[slot, pl.ds(part * wide, wide)] = blocks(gd.T, wide)
            gu = dot(n2t_ref[...], dh)
            up[slot, :, :, cols] = blocks(gu[0:C].astype(low), OWNERS)
            bsum_ref[t, :, cols] = gu[C : C + 1]
            return carry

        lax.fori_loop(0, TILES * halves, step, 0)
        run(G_D[-1], START)
        run(G_U[-1], START)
        hook(AFTER_TILES, 0)
        sums_ref[...] = jnp.zeros_like(sums_ref)
        for t in range(TILES):
            for s in range(TILE // 128):
                row, left = hidden_place(t, s)
                sums_ref[row : row + 1, left : left + 128] = bsum_ref[t, :, s * 128 : (s + 1) * 128]
        transpose_rows(o_ref, dyt_ref)
        hook(AFTER_TILES, 1)

        def finish(w, carry):
            rows = window_rows(w)
            x1 = x1_ref[rows, :]
            xhat, scale = norm_parts(x1)
            dn = dn_ref[rows, :]
            dy = dy_ref[rows, :].astype(full)
            dx1 = dy + norm_back(xhat, scale, dn, vec_ref[5:6, :])
            dr = dx1.astype(low)
            sums_ref[4:5, :] += jnp.sum(dr.astype(full), 0, keepdims=True)
            sums_ref[5:6, :] += jnp.sum(dn * xhat, 0, keepdims=True)
            sums_ref[6:7, :] += jnp.sum(dn, 0, keepdims=True)
            sums_ref[7:8, :] += jnp.sum(dy, 0, keepdims=True)
            dy_ref[rows, :] = ((x1 + y_ref[rows, :] + vec_ref[7:8, :]) * live(w)).astype(low)
            x1_ref[rows, :] = dx1
            n2_ref[rows, :] = dr
            return carry

        lax.fori_loop(0, windows, finish, 0)
        o_ref[...] = dot_nt(n2_ref[...], flat(wp[...])).astype(low)
        save = pltpu.make_async_copy(dy_ref.at[0:rows_all], out_hbm, local.at[0])
        save.start()
        hook(AFTER_TILES, 2)
        jobs[W_P].close()
        for g in range(GROUPS):
            cols = slice(g * GCOLS, (g + 1) * GCOLS)
            wp[:, :, cols] = blocks(dot(dyt_ref[...], n2_ref[:, cols]).astype(low), OWNERS)
        run(G_P, START)
        hook(AFTER_TILES, 3)
        save.wait()

    def both(dy_ref, dyt_ref):
        pl.run_scoped(functools.partial(forward, dy_ref, dyt_ref), V((rows_all, C), low), V((ROWS, C), low),
                      V((2, 3, ROWS, GCOLS), low), V((2, TOK, PACK), low), V((GROUPS, TOK, PACK), full))
        pl.run_scoped(functools.partial(middle, dy_ref, dyt_ref), V((ROWS, C), low), V((C + 16, ROWS), low), V((ROWS, C), full), V((ROWS, C), full),
                      V((TILES, 1, TILE), full), V((TILES, 1, TILE), full))

    pl.run_scoped(both, V((ROWS, C), low), V((C, ROWS), low))

    def backward(x_ref, n1_ref, n1t_ref, qkv_ref, pt_ref, dproj_ref, dn_ref, bias_ref):
        loads = [pltpu.make_async_copy(x_hbm, x_ref, local.at[0]), pltpu.make_async_copy(n1_hbm, n1_ref, local.at[1])]
        fetch = [pltpu.make_async_copy(qkv_hbm.at[g], qkv_ref.at[g % 2], local.at[2 + g % 2]) for g in range(GROUPS)]
        fetch[0].start()
        pltpu.make_async_copy(pt_hbm.at[0], pt_ref.at[0], local.at[4]).start()
        fetch[1].start()
        for load in loads:
            load.start()
        bias_ref[...] = jnp.zeros_like(bias_ref)
        dn_ref[...] = jnp.zeros_like(dn_ref)
        for part in range(3):
            dproj_ref[part, rows_all:, :] = jnp.zeros((ROWS - rows_all, GCOLS), low)
        for g in range(GROUPS):
            cols = slice(g * GCOLS, (g + 1) * GCOLS)
            held = qkv_ref.at[g % 2]
            fetch[g].wait()

            def window(w, carry, g=g, cols=cols, held=held):
                hook_window(BACKWARD, g, w)
                rows = window_rows(w)
                n = g * windows + w
                slot = n % 2

                @pl.when(n + 1 < GROUPS * windows)
                def _():
                    pltpu.make_async_copy(pt_hbm.at[n + 1], pt_ref.at[1 - slot], local.at[5 - slot]).start()

                pltpu.make_async_copy(pt_hbm.at[n], pt_ref.at[slot], local.at[4 + slot]).wait()
                q = held[0, rows, :]
                k = held[1, rows, :]
                v = held[2, rows, :]
                p = pt_ref[slot]
                do = split_diag(o_ref[rows, cols], mask_ref)
                dp = against_heads(v, do)
                dv = over_queries(p, do).astype(low)
                pf = p.astype(full)
                ds = (pf * (dp - jnp.sum(pf * dp, 0, keepdims=True))).astype(low)
                bias_ref[g] += ds.astype(full)
                dproj_ref[1, rows, :] = over_queries(ds, split_diag(q, mask_ref)).astype(low)
                dq = (undiag(k.T, ds, mask_ref) * (HEAD_DIM**-0.5)).astype(low)
                dproj_ref[0, rows, :] = dq
                dproj_ref[2, rows, :] = dv
                sums_ref[2:3, cols] += jnp.sum(dq.astype(full), 0, keepdims=True)
                sums_ref[3:4, cols] += jnp.sum(dv.astype(full), 0, keepdims=True)
                return carry

            lax.fori_loop(0, windows, window, 0)
            if g + 2 < GROUPS:
                fetch[g + 2].start()
            if g == 0:
                for load in loads:
                    load.wait()
                transpose_rows(n1_ref, n1t_ref)
            jobs[W_Q[g]].close()
            if g == GROUPS - 1:
                jobs[W_U[-1]].close()
                for part in range(3):
                    up[TILES - 1, :, :, part * GCOLS : (part + 1) * GCOLS] = blocks(dot(n1t_ref[...], dproj_ref[part]).astype(low), OWNERS)
                    run(G_LAST[part], START)
                hook(LAST_STEPS, 0)
                for part in range(3):
                    dn_ref[...] += dot_nt(dproj_ref[part], flat(wq[g, part]))
            else:
                for part in range(3):
                    d = dproj_ref[part]
                    dn_ref[...] += dot_nt(d, flat(wq[g, part]))
                    wq[g, part] = blocks(dot(n1t_ref[...], d).astype(low), OWNERS)
                run(G_Q[g], START)

        def last_norm(grad_ref):
            def finish(w, carry):
                rows = window_rows(w)
                slot = w % 2
                xhat, scale = norm_parts(x_ref[rows, :].astype(full))
                dn = dn_ref[rows, :]
                save = pltpu.make_async_copy(grad_ref.at[slot], grad_hbm.at[rows], local.at[4 + slot])

                @pl.when(w >= 2)
                def _():
                    save.wait()

                grad_ref[slot] = x1_ref[rows, :] + norm_back(xhat, scale, dn, vec_ref[0:1, :])
                save.start()
                sums_ref[0:1, :] += jnp.sum(dn * xhat, 0, keepdims=True)
                sums_ref[1:2, :] += jnp.sum(dn, 0, keepdims=True)
                return carry

            lax.fori_loop(0, windows, finish, 0)
            hook(LAST_STEPS, 1)
            for slot in range(2):
                pltpu.make_async_copy(grad_ref.at[slot], grad_hbm.at[pl.ds(0, TOK)], local.at[4 + slot]).wait()

        pl.run_scoped(last_norm, V((2, TOK, C), full))
        hook(LAST_STEPS, 2)

        def table(tmp_ref):
            pack_small(sums_ref[...], table_grad(line_ref, tmp_ref, bias_ref), terms_ref)

        pl.run_scoped(table, V((2, TOK * HEADS, 128), full))
        run(G_S, START)
        hook(LAST_STEPS, 3)
        for stage in range(len(Reduce.STAGES)):
            for name in G_ALL:
                if stage < len(jobs[name].STAGES):
                    run(name, stage)

    pl.run_scoped(backward, V((rows_all, C), low), V((ROWS, C), low), V((C, ROWS), low), V((2, 3, ROWS, GCOLS), low), V((2, TOK, PACK), low), V((3, ROWS, GCOLS), low),
                  V((ROWS, C), full), V((GROUPS, TOK, PACK), full))
    jobs[W_D[-1]].close()
    for i in range(1, OWNERS):
        await_bytes(small.at[mine], small_sems.at[i])
    for name in G_ALL:
        jobs[name].close()


def shape(dims, kind):
    return jax.ShapeDtypeStruct(dims, kind)


def adamw(weight, moment, second, gradient, step_rate):
    moment_new = beta_one * moment + (1.0 - beta_one) * gradient
    second_new = beta_two * second + (1.0 - beta_two) * gradient * gradient
    update = moment_new * (1.0 / (1.0 - beta_one**STEP)) / (jnp.sqrt(second_new * (1.0 / (1.0 - beta_two**STEP))) + adam_eps)
    weight_new = weight * (1.0 - step_rate * weight_decay) - step_rate * update
    return (weight_new, moment_new, second_new)


def update_kernel(*refs):
    gq, gp, gu, gd, gs = refs[:5]
    ins = [refs[5 + 3 * i : 8 + 3 * i] for i in range(6)]
    outs = [refs[25 + 4 * i : 29 + 4 * i] for i in range(4)] + [refs[41:44], refs[44:47]]
    for i in range(2):
        refs[47 + i][...] = refs[23 + i][...]

    def piece(which, place, gradient):
        new = adamw(*(ref[place] for ref in ins[which]), gradient, step_rates[which])
        for ref, value in zip(outs[which], new):
            ref[place] = value
        if which < 4:
            outs[which][3][place] = new[0].astype(low)

    every = (slice(None), slice(None))
    piece(0, every, jnp.concatenate([gq[g, part] for part in range(3) for g in range(GROUPS)], 1).astype(full))
    piece(1, every, gp[...].astype(full))
    piece(2, every, jnp.concatenate([gu[t, :, s * 128 : (s + 1) * 128] for s in range(OWNERS) for t in range(TILES)], 1).astype(full))
    piece(3, every, gd[0].astype(full))

    @pl.when(pl.program_id(0) == 0)
    def _():
        piece(4, every, gs[0:12, 0:OWNED])
        piece(5, every, gs[16:40, 0 : ins[5][0].shape[1]])


def update(gq, gp, gu, gd, gs, states, results):
    steps = OWNED // 16

    def rows_of(array):
        tall = array.shape[0] // steps
        return pl.BlockSpec((tall, array.shape[1]), lambda i: (i, 0))

    def whole(array):
        return pl.BlockSpec(array.shape, lambda i: (0, 0))

    per_tile = 128 * TILES // steps
    specs = [
        pl.BlockSpec((GROUPS, 3, 16, GCOLS), lambda i: (0, 0, i, 0)),
        pl.BlockSpec((16, C), lambda i: (i, 0)),
        pl.BlockSpec((TILES, 16, TILE), lambda i: (0, i, 0)),
        pl.BlockSpec((1, per_tile, C), lambda i: (i // (128 // per_tile), i % (128 // per_tile), 0)),
        whole(gs),
    ]
    out_shapes, out_specs = [], []
    for i, group in enumerate(states):
        for array in group:
            specs.append(rows_of(array) if i < 4 else whole(array))
            out_shapes.append(shape(array.shape, full))
            out_specs.append(specs[-1])
        if i < 4:
            out_shapes.append(shape(group[0].shape, low))
            out_specs.append(rows_of(group[0]))
    results = [array.reshape(steps, -1, C) for array in results]
    for array in results:
        specs.append(pl.BlockSpec((1, *array.shape[1:]), lambda i: (i, 0, 0)))
        out_shapes.append(shape(array.shape, array.dtype))
        out_specs.append(specs[-1])
    return pl.pallas_call(
        update_kernel,
        grid=(steps,),
        in_specs=specs,
        out_specs=out_specs,
        out_shape=out_shapes,
        compiler_params=pltpu.CompilerParams(vmem_limit_bytes=63 * MIB),
        name="update",
    )(gq, gp, gu, gd, gs, *[array for group in states for array in group], *results)


def shards(
    tokens, out_grad, window_count,
    qkv_weight, qkv_first, qkv_second,
    output_weight, output_first, output_second,
    up_weight, up_first, up_second,
    down_weight, down_first, down_second,
    vectors, vector_first, vector_second,
    bias_table, table_first, table_second,
):
    windows = tokens.shape[0]
    rows = windows * TOK
    V = pltpu.VMEM
    D = pltpu.SemaphoreType.DMA
    hbm = pl.BlockSpec(memory_space=pl.ANY)
    vmem = pl.BlockSpec(memory_space=pltpu.VMEM)
    result = pl.pallas_call(
        functools.partial(layer_kernel, windows),
        out_shape=[
            shape((rows, C), low), shape((rows, C), full),
            shape((GROUPS, 3, OWNED, GCOLS), low), shape((OWNED, C), low), shape((TILES, OWNED, TILE), low), shape((TILES, 128, C), low),
            shape((40, 128), full),
            shape((GROUPS, 3, ROWS, GCOLS), low), shape((GROUPS * windows, TOK, PACK), low), shape((ROWS, C), low)],
        in_specs=[hbm, hbm, pl.BlockSpec(memory_space=pltpu.SMEM)] + [hbm] * 4 + [vmem] * 4,
        out_specs=[hbm, hbm] + [vmem] * 5 + [hbm] * 3,
        scratch_shapes=[
            V((GROUPS, 3, OWNERS, OWNED, GCOLS), low), V((OWNERS, OWNED, C), low), V((SLOTS, OWNERS, OWNED, TILE), low),
            V((SLOTS, OWNERS, 128, C), low), V((OWNERS, 48, 128), low), V((ROWS, C), low), V((rows, C), full), V((16, C), full), V((16, C), full),
            V((OWNERS, 40, 128), full)]
        + reduce_scratch()
        + [D((GATHERS, Gather.SEMS)), D((REDUCES, ReduceDirect.SEMS)), D((2 * OWNERS,)), D((ReduceSmall.SEMS,)), D((6,))],
        compiler_params=pltpu.CompilerParams(vmem_limit_bytes=63 * MIB, collective_id=0, has_side_effects=True),
        name="layer",
    )(tokens.reshape(rows, C), out_grad.reshape(rows, C), window_count, qkv_weight, output_weight, up_weight, down_weight, vectors, bias_table.T,
      jnp.asarray(line_matrix(), low), jnp.asarray(head_masks(), low))
    out, grad, gq, gp, gu, gd, gs = result[:7]
    new = update(gq, gp, gu, gd, gs, (
        (qkv_weight, qkv_first, qkv_second), (output_weight, output_first, output_second), (up_weight, up_first, up_second),
        (down_weight, down_first, down_second), (vectors, vector_first, vector_second), (bias_table.T, table_first.T, table_second.T)), (out, grad))
    *new, out, grad = new
    return (out.reshape(tokens.shape), grad.reshape(tokens.shape), *new[:-3], *(array.T for array in new[-3:]))


def vmem_call(body, outs, scratch, args, name, limit=60, **params):
    spec = pl.BlockSpec(memory_space=pltpu.VMEM)
    return pl.pallas_call(
        body,
        out_shape=outs,
        in_specs=[pl.BlockSpec(memory_space=pltpu.SMEM) if a.dtype == full and a.ndim == 1 else spec for a in args],
        out_specs=[spec] * len(outs),
        scratch_shapes=scratch,
        compiler_params=pltpu.CompilerParams(vmem_limit_bytes=limit * MIB, **params),
        name=name,
    )(*args)


def local_step(tokens, out_grad, window_count, small, wq, wp, up, down):
    windows = tokens.shape[0]
    rows = windows * TOK
    owned = C // OWNERS
    V = pltpu.VMEM
    x = tokens.reshape(rows, C)
    dy = out_grad.reshape(rows, C)
    live = (jnp.arange(windows) < window_count[0]).astype(full)
    line = jnp.asarray(line_matrix(), low)
    masks = jnp.asarray(head_masks(), low)
    qkv, pt, o, x1, n1t, vec = vmem_call(
        functools.partial(attention_forward, windows),
        [shape((9, ROWS, GCOLS), low), shape((GROUPS, windows, TOK, PACK), low), shape((ROWS, C), low), shape((rows, C), full), shape((C, ROWS), low),
         shape((16, C), full)],
        [V((ROWS, C), low), V((GROUPS, TOK, PACK), full), V((2, TOK * HEADS, 128), full)],
        (x, small, line, masks, wq, wp), "attention_forward")
    out, dx1, do, gup, gdown, gout, sums = vmem_call(
        functools.partial(feed_forward, windows),
        [shape((rows, C), low), shape((ROWS, C), full), shape((rows, C), low), shape((TILES, OWNERS, owned, TILE), low),
         shape((TILES, OWNERS, C, 128), low), shape((OWNERS, owned, C), low), shape((16, C), full)],
        [V((ROWS, C), low), V((C, ROWS), low), V((ROWS, C), low), V((C, ROWS), low), V((ROWS, C), full), V((ROWS, C), full),
         V((TILES, 1, TILE), full), V((TILES, 1, TILE), full)],
        (x1, dy, live, vec, up, down, wp, o), "feed_forward")
    gq, gsmall, grad = vmem_call(
        functools.partial(attention_backward, windows),
        [shape((GROUPS, 3, OWNERS, owned, GCOLS), low), shape((OWNERS, 40, 128), full), shape((rows, C), full)],
        [V((16, C), full), V((GROUPS, TOK, PACK), full), V((2, TOK * HEADS, 128), full), V((3, ROWS, GCOLS), low), V((ROWS, C), full)],
        (x, vec, line, masks, wq, qkv, pt, do, dx1, n1t, sums), "attention_backward")
    return out.reshape(tokens.shape), grad.reshape(tokens.shape), gq, gout, gup, gdown, gsmall


def shards_general(
    tokens, out_grad, window_count,
    qkv_weight, qkv_first, qkv_second,
    output_weight, output_first, output_second,
    up_weight, up_first, up_second,
    down_weight, down_first, down_second,
    vectors, vector_first, vector_second,
    bias_table, table_first, table_second,
):
    gather = functools.partial(lax.all_gather, axis_name="shard", tiled=True)
    scatter = functools.partial(lax.psum_scatter, axis_name="shard", tiled=True)
    owned = C // OWNERS
    wq = gather(qkv_weight.astype(low), axis=0).reshape(OWNERS, owned, 3, GROUPS, GCOLS).transpose(3, 2, 0, 1, 4)
    wp = gather(output_weight.astype(low), axis=0).reshape(OWNERS, owned, C)
    up = gather(up_weight.astype(low), axis=0).reshape(OWNERS, owned, OWNERS, TILES, 128).transpose(3, 0, 1, 2, 4)
    up = up.reshape(TILES, OWNERS, owned, TILE)
    down = gather(down_weight.astype(low), axis=0).reshape(OWNERS, TILES, 128, C).transpose(1, 0, 2, 3)
    vec = gather(vectors.astype(low), axis=1)
    tab = gather(bias_table.astype(low), axis=0)
    table_rows = tab.shape[0]
    count = TAB_ROWS // OWNERS
    vec = vec.reshape(12, OWNERS, owned).transpose(1, 0, 2)
    tab = tab[:TAB_ROWS].reshape(OWNERS, count, HEADS).transpose(0, 2, 1)
    small = jnp.concatenate([jnp.pad(vec, ((0, 0), (0, 4), (0, 128 - owned))), jnp.pad(tab, ((0, 0), (0, 8), (0, 128 - count)))], 1)
    out, grad, gq, gp, gu, gd, gs = local_step(tokens, out_grad, window_count, small, wq, wp, up, down)
    gq = gq.astype(full).transpose(2, 3, 1, 0, 4).reshape(C, 3 * C)
    gu = gu.astype(full).reshape(TILES, C, OWNERS, 128).transpose(1, 2, 0, 3).reshape(C, MLP)
    gd = gd.astype(full).transpose(1, 0, 3, 2).reshape(MLP, C)
    gv = gs[:, :12, :owned].transpose(1, 0, 2).reshape(12, C)
    gb = gs[:, 16:40, :count].transpose(0, 2, 1).reshape(TAB_ROWS, HEADS)
    gb = jnp.pad(gb, ((0, table_rows - TAB_ROWS), (0, 0)))
    totals = lax.psum(
        (scatter(gq, scatter_dimension=0), scatter(gp.astype(full).reshape(C, C), scatter_dimension=0), scatter(gu, scatter_dimension=0),
         scatter(gd, scatter_dimension=0), scatter(gv, scatter_dimension=1), scatter(gb, scatter_dimension=0)), "rep")
    states = (
        (qkv_weight, qkv_first, qkv_second), (output_weight, output_first, output_second), (up_weight, up_first, up_second),
        (down_weight, down_first, down_second), (vectors, vector_first, vector_second), (bias_table, table_first, table_second))
    results = [out, grad]
    for i, (state, total, rate) in enumerate(zip(states, totals, step_rates)):
        new = adamw(*state, total, rate)
        results += [*new, new[0].astype(low)] if i < 4 else [*new]
    return tuple(results)


def solution(mesh):
    wins = P(("rep", "shard"), None, None)
    rows = P("shard", None)
    cols = P(None, "shard")
    fits = mesh.shape["rep"] == REPS and mesh.shape["shard"] == OWNERS
    return jax.shard_map(
        shards if fits else shards_general,
        mesh=mesh,
        in_specs=(wins, wins, P(("rep", "shard"))) + (rows,) * 12 + (cols,) * 3 + (rows,) * 3,
        out_specs=(wins, wins) + (rows,) * 16 + (cols,) * 3 + (rows,) * 3,
        check_vma=False,
    )
```

```python
import functools
import math

import jax
import jax.numpy as jnp
import numpy as np
from jax import lax
from jax.experimental import pallas as pl
from jax.experimental.pallas import tpu as pltpu
from jax.sharding import PartitionSpec as P

C = 768
HEADS = 24
MLP = 3072
WIN = 12
STEP = 5
HEAD_DIM = 32
SPAN = 2 * WIN - 1
TOK = WIN * WIN
TAB_ROWS = 536
ROWS = 1024
GROUPS = 3
GCOLS = 256
GHEADS = 8
PACK = GHEADS * TOK
TAB_LANES = 640
TILES = 3
TILE = MLP // TILES
SUB = 512
LINE = 384
MIB = 1 << 20

beta_one = 0.5
beta_two = 0.6
weight_decay = 0.05
adam_eps = 1e-08
norm_eps = 1e-05
step_rates = (0.04, 0.15, 0.04, 0.02, 0.2, 1.0)
low = jnp.bfloat16
full = jnp.float32
NT = (((1,), (1,)), ((), ()))


def dot(a, b):
    return jnp.dot(a, b, preferred_element_type=full)


def dot_nt(a, b):
    return lax.dot_general(a, b, NT, preferred_element_type=full)


def line_matrix():
    out = np.zeros((TAB_LANES, LINE), np.float32)
    col = np.arange(SPAN * WIN)
    out[(col // WIN) * SPAN + col % WIN + WIN - 1, col] = 1.0
    return out


def head_masks():
    lane = np.arange(GCOLS) // HEAD_DIM
    one = (lane[None, :] == np.arange(GHEADS)[:, None]).astype(np.float32)
    return np.broadcast_to(one[:, None, :], (GHEADS, 16, GCOLS))


def norm_parts(z):
    mean = jnp.sum(z, -1, keepdims=True) * (1.0 / C)
    center = z - mean
    spread = jnp.sum(center * center, -1, keepdims=True) * (1.0 / C)
    scale = lax.rsqrt(spread + norm_eps)
    return center * scale, scale


def norm_back(xhat, scale, dn, gain):
    g = dn * gain
    m1 = jnp.sum(g, -1, keepdims=True) * (1.0 / C)
    m2 = jnp.sum(g * xhat, -1, keepdims=True) * (1.0 / C)
    return scale * (g - m1 - xhat * m2)


def diag(x, mask_ref):
    head = x[0:128].reshape(8, 16, GCOLS)
    tail = x[128:144]
    parts = []
    for h in range(GHEADS):
        parts.append((head * mask_ref[h][None]).reshape(128, GCOLS))
    for h in range(GHEADS):
        parts.append(tail * mask_ref[h])
    return jnp.concatenate(parts, 0)


def undiag(xt, m, mask_ref):
    main = []
    for h in range(0, GHEADS, 2):
        r = dot(xt[h * HEAD_DIM : (h + 2) * HEAD_DIM], m[:, h * 128 : (h + 2) * 128])
        main.append(r[0:HEAD_DIM, 0:128])
        main.append(r[HEAD_DIM : 2 * HEAD_DIM, 128:256])
    main = jnp.concatenate(main, 0)
    rest = dot(xt, m[:, GHEADS * 128 :])
    rest_t = rest.T.reshape(GHEADS, 16, GCOLS)
    keep = mask_ref[...].astype(full)
    return jnp.concatenate([main.T, jnp.sum(rest_t * keep, 0)], 0)


def flat(x):
    return x.reshape(x.shape[0] * x.shape[1], x.shape[2])


def blocks(x, owners):
    return x.reshape(owners, x.shape[0] // owners, x.shape[1])


def hidden_place(t, s):
    at = (MLP // GHEADS) * s + 128 * t
    return 8 + at // C, at % C


def unpack_small(small_ref, vec_ref):
    owners = small_ref.shape[0]
    width = C // owners
    count = TAB_ROWS // owners
    vec = jnp.zeros((16, C), full)
    tab = jnp.zeros((HEADS, TAB_LANES), full)
    lane = lax.broadcasted_iota(jnp.int32, (16, 128), 1)
    lane_tab = lax.broadcasted_iota(jnp.int32, (HEADS, 128), 1)
    for s in range(owners):
        piece = small_ref[s].astype(full)
        part = jnp.where(lane < width, piece[0:16], 0.0)
        part = jnp.concatenate([part, jnp.zeros((16, C - 128), full)], 1)
        vec = vec + (pltpu.roll(part, width * s, 1) if s else part)
        part = jnp.where(lane_tab < count, piece[16 : 16 + HEADS], 0.0)
        part = jnp.concatenate([part, jnp.zeros((HEADS, TAB_LANES - 128), full)], 1)
        tab = tab + (pltpu.roll(part, count * s, 1) if s else part)
    vec_ref[...] = vec
    return tab


def pack_small(vec, tab, out_ref):
    owners = out_ref.shape[0]
    width = C // owners
    count = TAB_ROWS // owners
    for s in range(owners):
        out_ref[s, 0:16, :] = (pltpu.roll(vec, C - width * s, 1) if s else vec)[:, 0:128]
        out_ref[s, 16:40, :] = (pltpu.roll(tab, TAB_LANES - count * s, 1) if s else tab)[:, 0:128]


def spread_table(tab, line_ref, tmp_ref):
    def column(cj, carry):
        shifted = pltpu.roll(tab, cj, 1)
        line = dot(shifted.astype(low), line_ref[...])
        for rj in range(WIN):
            cut = (WIN - 1 - rj) * WIN
            part = pltpu.roll(line, LINE - cut, 1) if cut else line
            row = pl.multiple_of((rj * WIN + cj) * HEADS, 8)
            tmp_ref[0, pl.ds(row, HEADS), :] = part[:, 0:128]
            tmp_ref[1, pl.ds(row, HEADS), :] = part[:, 128:256]
        return carry

    lax.fori_loop(0, WIN, column, 0)


def place_bias(tmp_ref, bias_ref):
    lane = lax.broadcasted_iota(jnp.int32, (TOK, 128), 1)
    for g in range(GROUPS):
        rest = jnp.zeros((TOK, 128), full)
        for h in range(GHEADS):
            at = pl.ds(g * GHEADS + h, TOK, stride=HEADS)
            bias_ref[g, :, h * 128 : (h + 1) * 128] = tmp_ref[0, at, :]
            piece = tmp_ref[1, at, :]
            piece = pltpu.roll(piece, 16 * h, 1) if h else piece
            rest = jnp.where((lane >= 16 * h) & (lane < 16 * h + 16), piece, rest)
        bias_ref[g, :, GHEADS * 128 :] = rest


def table_grad(line_ref, tmp_ref, bias_ref):
    lane = lax.broadcasted_iota(jnp.int32, (TOK, 128), 1)
    for g in range(GROUPS):
        rest = bias_ref[g, :, GHEADS * 128 :]
        for h in range(GHEADS):
            at = pl.ds(g * GHEADS + h, TOK, stride=HEADS)
            tmp_ref[0, at, :] = bias_ref[g, :, h * 128 : (h + 1) * 128]
            piece = pltpu.roll(rest, 128 - 16 * h, 1) if h else rest
            tmp_ref[1, at, :] = jnp.where(lane < 16, piece, 0.0)

    def column(cj, total):
        line = jnp.zeros((HEADS, LINE), full)
        for rj in range(WIN):
            cut = (WIN - 1 - rj) * WIN
            row = pl.multiple_of((rj * WIN + cj) * HEADS, 8)
            part = jnp.concatenate([tmp_ref[0, pl.ds(row, HEADS), :], tmp_ref[1, pl.ds(row, HEADS), :], jnp.zeros((HEADS, 128), full)], 1)
            line = line + (pltpu.roll(part, cut, 1) if cut else part)
        high = line.astype(low)
        rest = (line - high.astype(full)).astype(low)
        spread = dot_nt(high, line_ref[...]) + dot_nt(rest, line_ref[...])
        return total + pltpu.roll(spread, TAB_LANES - cj, 1)

    return lax.fori_loop(0, WIN, column, jnp.zeros((HEADS, TAB_LANES), full))


def transpose_rows(src_ref, dst_ref):
    def block(i, carry):
        at = pl.multiple_of(i * 128, 128)
        dst_ref[0 : src_ref.shape[1], pl.ds(at, 128)] = src_ref[pl.ds(at, 128), :].T
        return carry

    lax.fori_loop(0, ROWS // 128, block, 0)


def window_rows(w):
    return slice(w * TOK, (w + 1) * TOK) if isinstance(w, int) else pl.ds(pl.multiple_of(w * TOK, 16), TOK)


def zero_tail(ref, windows):
    at = windows * TOK
    ref[at:ROWS, :] = jnp.zeros((ROWS - at, ref.shape[1]), ref.dtype)


def half_diag(x, half, mask_ref):
    lanes = slice(half * 128, (half + 1) * 128)
    part = x[0:128, lanes].reshape(8, 16, 128)
    heads = range(half * GHEADS // 2, (half + 1) * GHEADS // 2)
    return jnp.concatenate([(part * mask_ref[h, :, lanes][None]).reshape(128, 128) for h in heads], 0)


def rest_diag(x, mask_ref):
    return jnp.concatenate([x[128:144] * mask_ref[h] for h in range(GHEADS)], 0)


def split_diag(x, mask_ref):
    return half_diag(x, 0, mask_ref), half_diag(x, 1, mask_ref), rest_diag(x, mask_ref)


def against_heads(x, split):
    first, second, rest = split
    return jnp.concatenate([dot_nt(x[:, 0:128], first), dot_nt(x[:, 128:256], second), dot_nt(x, rest)], 1)


def over_queries(m, split):
    first, second, rest = split
    return jnp.concatenate([dot(m[:, 0:512], first), dot(m[:, 512:1024], second)], 1) + dot(m[:, 1024:], rest)


def attention_forward(windows, x_ref, small_ref, line_ref, mask_ref, wq_ref, wp_ref,
                      qkv_ref, pt_ref, o_ref, x1_ref, n1t_ref, vec_ref, n1_ref, bias_ref, tmp_ref):
    tab = unpack_small(small_ref, vec_ref)
    spread_table(tab, line_ref, tmp_ref)
    place_bias(tmp_ref, bias_ref)
    zero_tail(n1_ref, windows)
    zero_tail(o_ref, windows)

    def first_norm(w, carry):
        xhat, _ = norm_parts(x_ref[window_rows(w), :].astype(full))
        n1_ref[window_rows(w), :] = (xhat * vec_ref[0:1, :] + vec_ref[1:2, :]).astype(low)
        return carry

    lax.fori_loop(0, windows, first_norm, 0)
    transpose_rows(n1_ref, n1t_ref)

    def group(g, carry):
        cols = pl.ds(pl.multiple_of(g * GCOLS, GCOLS), GCOLS)
        n1 = n1_ref[...]
        qkv_ref[g] = ((dot(n1, flat(wq_ref[g, 0])) + vec_ref[2:3, cols]) * (HEAD_DIM**-0.5)).astype(low)
        qkv_ref[GROUPS + g] = dot(n1, flat(wq_ref[g, 1])).astype(low)
        qkv_ref[2 * GROUPS + g] = (dot(n1, flat(wq_ref[g, 2])) + vec_ref[3:4, cols]).astype(low)

        def window(w, inner):
            rows = window_rows(w)
            q = qkv_ref[g, rows, :]
            k = qkv_ref[GROUPS + g, rows, :]
            v = qkv_ref[2 * GROUPS + g, rows, :]
            s = dot_nt(k, diag(q, mask_ref)) + bias_ref[g]
            e = jnp.exp(s - jnp.max(s, 0, keepdims=True))
            p = (e * (1.0 / jnp.sum(e, 0, keepdims=True))).astype(low)
            pt_ref[g, w] = p
            o_ref[rows, cols] = undiag(v.T, p, mask_ref).astype(low)
            return inner

        lax.fori_loop(0, windows, window, 0)
        return carry

    lax.fori_loop(0, GROUPS, group, 0)

    def output(w, carry):
        rows = window_rows(w)
        branch = dot(o_ref[rows, :], flat(wp_ref[...])) + vec_ref[4:5, :]
        x1_ref[rows, :] = x_ref[rows, :].astype(full) + branch
        return carry

    lax.fori_loop(0, windows, output, 0)


def gelu_both(h):
    c = math.sqrt(2.0 / math.pi)
    square = h * h
    t = jnp.tanh(h * (c + (c * 0.044715) * square))
    half = 0.5 + 0.5 * t
    act = h * half
    return act, half + act * (1.0 - half) * (2.0 * c + (6.0 * c * 0.044715) * square)


def feed_forward(windows, x1_ref, dy_ref, live_ref, vec_ref, up_ref, down_ref, wp_ref, o_ref,
                 out_ref, dx1_ref, do_ref, gup_ref, gdown_ref, gout_ref, sums_ref,
                 n2_ref, n2t_ref, dy2_ref, dyt_ref, y_ref, dn_ref, bu_ref, bsum_ref):
    zero_tail(n2_ref, windows)
    zero_tail(dy2_ref, windows)

    def second_norm(w, carry):
        rows = window_rows(w)
        xhat, _ = norm_parts(x1_ref[rows, :])
        n2_ref[rows, :] = (xhat * vec_ref[5:6, :] + vec_ref[6:7, :]).astype(low)
        dy2_ref[rows, :] = (dy_ref[rows, :].astype(full) * live_ref[w]).astype(low)
        return carry

    lax.fori_loop(0, windows, second_norm, 0)
    transpose_rows(n2_ref, n2t_ref)
    transpose_rows(dy2_ref, dyt_ref)
    y_ref[...] = jnp.zeros_like(y_ref)
    dn_ref[...] = jnp.zeros_like(dn_ref)
    owners = gup_ref.shape[1]
    for t in range(TILES):
        for s in range(TILE // 128):
            row, at = hidden_place(t, s)
            bu_ref[t, :, s * 128 : (s + 1) * 128] = vec_ref[row : row + 1, at : at + 128]

    def step(t, carry):
        for part in range(TILE // SUB):
            cols = slice(part * SUB, (part + 1) * SUB)
            up = flat(up_ref[t, :, :, cols])
            down = flat(down_ref[t, part * SUB // 128 : (part + 1) * SUB // 128])
            h = dot(n2_ref[...], up) + bu_ref[t, :, cols]
            da = dot_nt(dy2_ref[...], down)
            act, slope = gelu_both(h)
            a = act.astype(low)
            dh = (da * slope).astype(low)
            bsum_ref[t, :, cols] = jnp.sum(dh.astype(full), 0, keepdims=True)
            y_ref[...] += dot(a, down)
            dn_ref[...] += dot_nt(dh, up)
            gd = dot(dyt_ref[...], a).astype(low)
            for b in range(SUB // 128):
                gdown_ref[t, part * SUB // 128 + b] = gd[:, b * 128 : (b + 1) * 128]
            gup_ref[t, :, :, cols] = blocks(dot(n2t_ref[...], dh).astype(low), owners)
        return carry

    lax.fori_loop(0, TILES, step, 0)
    sums_ref[...] = jnp.zeros_like(sums_ref)
    for t in range(TILES):
        for s in range(TILE // 128):
            row, at = hidden_place(t, s)
            sums_ref[row : row + 1, at : at + 128] = bsum_ref[t, :, s * 128 : (s + 1) * 128]
    zero_tail(dx1_ref, windows)

    def finish(w, carry):
        rows = window_rows(w)
        x1 = x1_ref[rows, :]
        out_ref[rows, :] = ((x1 + y_ref[rows, :] + vec_ref[7:8, :]) * live_ref[w]).astype(low)
        xhat, scale = norm_parts(x1)
        dn = dn_ref[rows, :]
        dy = dy2_ref[rows, :].astype(full)
        dx1 = dy + norm_back(xhat, scale, dn, vec_ref[5:6, :])
        dx1_ref[rows, :] = dx1
        dr = dx1.astype(low)
        n2_ref[rows, :] = dr
        do_ref[rows, :] = dot_nt(dr, flat(wp_ref[...])).astype(low)
        sums_ref[4:5, :] += jnp.sum(dr.astype(full), 0, keepdims=True)
        sums_ref[5:6, :] += jnp.sum(dn * xhat, 0, keepdims=True)
        sums_ref[6:7, :] += jnp.sum(dn, 0, keepdims=True)
        sums_ref[7:8, :] += jnp.sum(dy, 0, keepdims=True)
        return carry

    lax.fori_loop(0, windows, finish, 0)
    transpose_rows(o_ref, dyt_ref)
    for g in range(GROUPS):
        at = pl.ds(g * GCOLS, GCOLS)
        gout_ref[:, :, at] = blocks(dot(dyt_ref[...], n2_ref[:, at]).astype(low), gout_ref.shape[0])


def attention_backward(windows, x_ref, vec_ref, line_ref, mask_ref, wq_ref, qkv_ref, pt_ref, do_ref, dx1_ref, n1t_ref, sums_in_ref,
                       gq_ref, gsmall_ref, grad_ref, sums_ref, bias_ref, tmp_ref, dproj_ref, dn_ref):
    bias_ref[...] = jnp.zeros_like(bias_ref)
    dn_ref[...] = jnp.zeros_like(dn_ref)
    sums_ref[...] = sums_in_ref[...]
    for part in range(3):
        dproj_ref[part, windows * TOK :, :] = jnp.zeros((ROWS - windows * TOK, GCOLS), low)

    def group(g, carry):
        cols = pl.ds(pl.multiple_of(g * GCOLS, GCOLS), GCOLS)

        def window(w, inner):
            rows = window_rows(w)
            q = qkv_ref[g, rows, :]
            k = qkv_ref[GROUPS + g, rows, :]
            v = qkv_ref[2 * GROUPS + g, rows, :]
            p = pt_ref[g, w]
            do = diag(do_ref[rows, cols], mask_ref)
            dp = dot_nt(v, do)
            dv = dot(p, do)
            pf = p.astype(full)
            ds = (pf * (dp - jnp.sum(pf * dp, 0, keepdims=True))).astype(low)
            bias_ref[g] += ds.astype(full)
            dk = dot(ds, diag(q, mask_ref))
            dq = undiag(k.T, ds, mask_ref) * (HEAD_DIM**-0.5)
            dq = dq.astype(low)
            dv = dv.astype(low)
            dproj_ref[0, rows, :] = dq
            dproj_ref[1, rows, :] = dk.astype(low)
            dproj_ref[2, rows, :] = dv
            sums_ref[2:3, cols] += jnp.sum(dq.astype(full), 0, keepdims=True)
            sums_ref[3:4, cols] += jnp.sum(dv.astype(full), 0, keepdims=True)
            return inner

        lax.fori_loop(0, windows, window, 0)
        for part in range(3):
            d = dproj_ref[part]
            gq_ref[g, part] = blocks(dot(n1t_ref[...], d).astype(low), gq_ref.shape[2])
            dn_ref[...] += dot_nt(d, flat(wq_ref[g, part]))
        return carry

    lax.fori_loop(0, GROUPS, group, 0)

    def finish(w, carry):
        rows = window_rows(w)
        xhat, scale = norm_parts(x_ref[rows, :].astype(full))
        dn = dn_ref[rows, :]
        grad_ref[rows, :] = dx1_ref[rows, :] + norm_back(xhat, scale, dn, vec_ref[0:1, :])
        sums_ref[0:1, :] += jnp.sum(dn * xhat, 0, keepdims=True)
        sums_ref[1:2, :] += jnp.sum(dn, 0, keepdims=True)
        return carry

    lax.fori_loop(0, windows, finish, 0)
    pack_small(sums_ref[...], table_grad(line_ref, tmp_ref, bias_ref), gsmall_ref)


MESH = pl.DeviceIdType.MESH
REPS = 4
OWNERS = 8
LINKS = OWNERS // 2


class Spot:
    def __init__(self):
        self.rep = lax.axis_index("rep")
        self.shard = lax.axis_index("shard")
        self.z = self.shard // 2
        self.core = self.shard % 2

    def sibling(self):
        return (self.rep, self.z * 2 + (1 - self.core))

    def along_z(self, step):
        return (self.rep, ((self.z + step) % LINKS) * 2 + self.core)

    def turned(self, axis):
        x, y = self.rep % 2, self.rep // 2
        return y * 2 + (1 - x) if axis == 0 else (1 - y) * 2 + x

    def beside(self, axis):
        return (self.turned(axis), self.shard)

    def across(self):
        return (REPS - 1 - self.rep, self.shard)


def greet(spot):
    barrier = pltpu.get_barrier_semaphore()
    peers = [(spot.rep, (spot.shard + i) % OWNERS) for i in range(1, OWNERS)]
    peers += [((spot.rep + i) % REPS, spot.shard) for i in range(1, REPS)]
    for peer in peers:
        pl.semaphore_signal(barrier, inc=1, device_id=peer, device_id_type=MESH)
    return barrier, len(peers)


def send(src, dst, send_sem, recv_sem, peer):
    pltpu.make_async_remote_copy(src_ref=src, dst_ref=dst, send_sem=send_sem, recv_sem=recv_sem, device_id=peer, device_id_type=MESH).start()


def await_bytes(ref, sem):
    pltpu.make_async_copy(ref, ref, sem).wait()


def quarter(ref, rep):
    rows, cols = ref.shape[-2:]
    lead = (slice(None),) * (len(ref.shape) - 2)
    top = pl.multiple_of((rep // 2) * (rows // 2), 16)
    left = pl.multiple_of((rep % 2) * (cols // 2), 128)
    return ref.at[lead + (pl.ds(top, rows // 2), pl.ds(left, cols // 2))]


def half(ref, rep, axis):
    rows, cols = ref.shape[-2:]
    lead = (slice(None),) * (len(ref.shape) - 2)
    if axis == 0:
        left = pl.multiple_of((rep % 2) * (cols // 2), 128)
        return ref.at[lead + (slice(None), pl.ds(left, cols // 2))]
    top = pl.multiple_of((rep // 2) * (rows // 2), 16)
    return ref.at[lead + (pl.ds(top, rows // 2), slice(None))]


class Gather:
    KINDS = (LINKS - 1, LINKS - 1, LINKS - 1, LINKS - 1, LINKS)
    SEMS = 2 * sum(KINDS)
    STAGES = ("start", "across", "relay", "beside", "finish")

    def __init__(self, spot, place, axis, sems, direct=False):
        self.spot, self.place, self.axis, self.sems, self.direct = spot, place, axis, sems, direct

    def sem(self, side, kind, i):
        return self.sems.at[side * (self.SEMS // 2) + sum(self.KINDS[:kind]) + i]

    def block(self, step):
        return self.place(((self.spot.z - step + LINKS) % LINKS) * 2 + self.spot.core)

    def other(self, step):
        return self.place(((self.spot.z - step + LINKS) % LINKS) * 2 + 1 - self.spot.core)

    def start(self):
        spot = self.spot
        mine = self.block(0)
        for i in range(1, LINKS):
            piece = quarter(mine, spot.rep)
            send(piece, piece, self.sem(0, 0, i - 1), self.sem(1, 0, i - 1), spot.along_z(i))
        send(mine, mine, self.sem(0, 4, 0), self.sem(1, 4, 0), spot.sibling())

    def across(self):
        spot = self.spot
        for i in range(1, LINKS):
            piece = quarter(self.block(i), spot.rep)
            await_bytes(piece, self.sem(1, 0, i - 1))
            for axis in (self.axis, 1 - self.axis):
                send(piece, piece, self.sem(0, 1 + axis, i - 1), self.sem(1, 1 + axis, i - 1), spot.beside(axis))
            if self.direct:
                send(piece, piece, self.sem(0, 3, i - 1), self.sem(1, 3, i - 1), spot.across())

    def relay(self):
        spot = self.spot
        if self.direct:
            return
        for i in range(1, LINKS):
            piece = quarter(self.block(i), spot.turned(self.axis))
            await_bytes(piece, self.sem(1, 1 + self.axis, i - 1))
            send(piece, piece, self.sem(0, 3, i - 1), self.sem(1, 3, i - 1), spot.beside(1 - self.axis))

    def beside(self):
        spot = self.spot
        for i in range(1, LINKS):
            block = self.block(i)
            piece = quarter(block, spot.rep)
            if self.direct:
                await_bytes(piece, self.sem(1, 1 + self.axis, i - 1))
            await_bytes(piece, self.sem(1, 2 - self.axis, i - 1))
            await_bytes(piece, self.sem(1, 3, i - 1))
            send(block, block, self.sem(0, 4, i), self.sem(1, 4, i), spot.sibling())

    def finish(self):
        for i in range(LINKS):
            await_bytes(self.other(i), self.sem(1, 4, i))

    def close(self):
        piece = quarter(self.block(0), self.spot.rep)
        for kind in range(4):
            for i in range(1, LINKS):
                await_bytes(piece, self.sem(0, kind, i - 1))
        for i in range(LINKS):
            await_bytes(self.block(i), self.sem(0, 4, i))


class Reduce:
    KINDS = (LINKS, 1, 1, LINKS - 1, REPS - 1)
    SEMS = 2 * sum(KINDS)
    STAGES = ("start", "first", "second", "along", "spread", "passed", "finish")

    def __init__(self, spot, place, out, core_sum, halves, quarters, links, axis, sems, direct):
        self.spot, self.place, self.out, self.axis, self.sems, self.direct = spot, place, out, axis, sems, direct
        self.core_sum, self.halves, self.quarters, self.links = core_sum, halves, quarters, links

    def sem(self, side, kind, i):
        return self.sems.at[side * (self.SEMS // 2) + sum(self.KINDS[:kind]) + i]

    def start(self):
        spot = self.spot
        for z in range(LINKS):
            send(self.place(z * 2 + (1 - spot.core)), self.core_sum.at[z], self.sem(0, 0, z), self.sem(1, 0, z), spot.sibling())

    def first(self):
        spot = self.spot
        for z in range(LINKS):
            total = self.core_sum.at[z]
            await_bytes(total, self.sem(1, 0, z))
            total[...] = (total[...].astype(full) + self.place(z * 2 + spot.core)[...].astype(full)).astype(low)
        theirs = half(self.core_sum, spot.turned(self.axis), self.axis)
        send(theirs, self.halves, self.sem(0, 1, 0), self.sem(1, 1, 0), spot.beside(self.axis))

    def second(self):
        spot = self.spot
        await_bytes(self.halves, self.sem(1, 1, 0))
        mine = half(self.core_sum, spot.rep, self.axis)
        self.halves[...] = (self.halves[...].astype(full) + mine[...].astype(full)).astype(low)
        theirs = half(self.halves, spot.turned(1 - self.axis), 1 - self.axis)
        send(theirs, self.quarters, self.sem(0, 2, 0), self.sem(1, 2, 0), spot.beside(1 - self.axis))

    def along(self):
        spot = self.spot
        await_bytes(self.quarters, self.sem(1, 2, 0))
        mine = half(self.halves, spot.rep, 1 - self.axis)
        self.quarters[...] = (self.quarters[...].astype(full) + mine[...].astype(full)).astype(low)
        for i in range(1, LINKS):
            send(self.quarters.at[(spot.z + i) % LINKS], self.links.at[i - 1], self.sem(0, 3, i - 1), self.sem(1, 3, i - 1), spot.along_z(i))

    def spread(self):
        spot = self.spot
        total = self.quarters[spot.z].astype(full)
        for i in range(1, LINKS):
            await_bytes(self.links.at[i - 1], self.sem(1, 3, i - 1))
            total = total + self.links[i - 1].astype(full)
        mine = quarter(self.out, spot.rep)
        mine[...] = total.astype(low)
        for axis in (self.axis, 1 - self.axis):
            send(mine, mine, self.sem(0, 4, axis), self.sem(1, 4, axis), spot.beside(axis))
        if self.direct:
            send(mine, mine, self.sem(0, 4, 2), self.sem(1, 4, 2), spot.across())

    def passed(self):
        spot = self.spot
        theirs = quarter(self.out, spot.turned(self.axis))
        await_bytes(theirs, self.sem(1, 4, self.axis))
        if not self.direct:
            send(theirs, theirs, self.sem(0, 4, 2), self.sem(1, 4, 2), spot.beside(1 - self.axis))

    def finish(self):
        spot = self.spot
        await_bytes(quarter(self.out, spot.turned(1 - self.axis)), self.sem(1, 4, 1 - self.axis))
        await_bytes(quarter(self.out, REPS - 1 - spot.rep), self.sem(1, 4, 2))

    def close(self):
        for z in range(LINKS):
            await_bytes(self.core_sum.at[z], self.sem(0, 0, z))
        await_bytes(self.halves, self.sem(0, 1, 0))
        await_bytes(self.quarters, self.sem(0, 2, 0))
        for i in range(1, LINKS):
            await_bytes(self.links.at[i - 1], self.sem(0, 3, i - 1))
        for j in range(1, REPS):
            await_bytes(quarter(self.out, self.spot.rep), self.sem(0, 4, j - 1))


class ReduceDirect(Reduce):
    KINDS = (LINKS, REPS - 1, 0, LINKS - 1, REPS - 1)
    SEMS = 2 * sum(KINDS)

    def peers(self):
        spot = self.spot
        return (spot.turned(0), spot.turned(1), REPS - 1 - spot.rep)

    def first(self):
        spot = self.spot
        for z in range(LINKS):
            total = self.core_sum.at[z]
            await_bytes(total, self.sem(1, 0, z))
            total[...] = (total[...].astype(full) + self.place(z * 2 + spot.core)[...].astype(full)).astype(low)
        for j, rep in enumerate(self.peers()):
            send(quarter(self.core_sum, rep), self.halves.at[j], self.sem(0, 1, j), self.sem(1, 1, j), (rep, spot.shard))

    def second(self):
        pass

    def along(self):
        spot = self.spot
        total = quarter(self.core_sum, spot.rep)[...].astype(full)
        for j in range(REPS - 1):
            await_bytes(self.halves.at[j], self.sem(1, 1, j))
            total = total + self.halves[j].astype(full)
        self.quarters[...] = total.astype(low)
        for i in range(1, LINKS):
            send(self.quarters.at[(spot.z + i) % LINKS], self.links.at[i - 1], self.sem(0, 3, i - 1), self.sem(1, 3, i - 1), spot.along_z(i))

    def close(self):
        for z in range(LINKS):
            await_bytes(self.core_sum.at[z], self.sem(0, 0, z))
        for j in range(REPS - 1):
            await_bytes(self.halves.at[j], self.sem(0, 1, j))
        for i in range(1, LINKS):
            await_bytes(self.links.at[i - 1], self.sem(0, 3, i - 1))
        for j in range(1, REPS):
            await_bytes(quarter(self.out, self.spot.rep), self.sem(0, 4, j - 1))


class ReduceSmall:
    KINDS = (LINKS, LINKS - 1, REPS - 1)
    SEMS = 2 * sum(KINDS)
    STAGES = ("start", "first", "second", "along")

    def __init__(self, spot, terms, out, core_sum, links, parts, sems):
        self.spot, self.terms, self.out, self.core_sum, self.links, self.parts, self.sems = spot, terms, out, core_sum, links, parts, sems

    sem = Reduce.sem

    def start(self):
        spot = self.spot
        for z in range(LINKS):
            send(self.terms.at[z * 2 + (1 - spot.core)], self.core_sum.at[z], self.sem(0, 0, z), self.sem(1, 0, z), spot.sibling())

    def first(self):
        spot = self.spot
        for z in range(LINKS):
            await_bytes(self.core_sum.at[z], self.sem(1, 0, z))
            self.core_sum[z] = self.core_sum[z] + self.terms[z * 2 + spot.core]
        for i in range(1, LINKS):
            send(self.core_sum.at[(spot.z + i) % LINKS], self.links.at[i - 1], self.sem(0, 1, i - 1), self.sem(1, 1, i - 1), spot.along_z(i))

    def second(self):
        spot = self.spot
        total = self.core_sum[spot.z]
        for i in range(1, LINKS):
            await_bytes(self.links.at[i - 1], self.sem(1, 1, i - 1))
            total = total + self.links[i - 1]
        self.parts[spot.rep] = total
        mine = self.parts.at[spot.rep]
        for j in range(1, REPS):
            send(mine, mine, self.sem(0, 2, j - 1), self.sem(1, 2, j - 1), ((spot.rep + j) % REPS, spot.shard))

    def along(self):
        for j in range(1, REPS):
            await_bytes(self.parts.at[(self.spot.rep - j + REPS) % REPS], self.sem(1, 2, j - 1))
        total = self.parts[0]
        for j in range(1, REPS):
            total = total + self.parts[j]
        self.out[...] = total

    def close(self):
        for z in range(LINKS):
            await_bytes(self.core_sum.at[z], self.sem(0, 0, z))
        for i in range(1, LINKS):
            await_bytes(self.links.at[i - 1], self.sem(0, 1, i - 1))
        for j in range(1, REPS):
            await_bytes(self.parts.at[self.spot.rep], self.sem(0, 2, j - 1))


OWNED = C // OWNERS
SLOTS = TILES + 1
GATHERS = 2 * TILES + 1 + GROUPS
REDUCES = 2 * TILES + 1 + (GROUPS - 1) + 3
W_Q0, W_Q1, W_Q2, W_P, W_U0, W_D0, W_U1, W_D1, W_U2, W_D2 = W_ALL = range(10)
G_D0, G_U0, G_D1, G_U1, G_D2, G_U2, G_P, G_Q0, G_Q1, G_Q2, G_K2, G_V2, G_S = G_ALL = range(10, 23)
W_Q, W_U, W_D = (W_Q0, W_Q1, W_Q2), (W_U0, W_U1, W_U2), (W_D0, W_D1, W_D2)
G_D, G_U, G_Q, G_LAST = (G_D0, G_D1, G_D2), (G_U0, G_U1, G_U2), (G_Q0, G_Q1), (G_Q2, G_K2, G_V2)
G_TWO = ()
START, ACROSS, RELAY, BESIDE, ARRIVED = range(5)
FIRST, SECOND, ALONG, SPREAD, PASSED, SUMMED = range(1, 7)
BEFORE = {
    2: ((W_Q0, ACROSS), (W_P, START),),
    3: ((W_Q0, RELAY), (W_Q2, START), (W_U0, START),),
    5: ((W_Q0, BESIDE), (W_Q1, ACROSS),),
}
FORWARD = {
    0: ((W_Q1, RELAY), (W_Q2, ACROSS), (W_P, ACROSS), (W_D0, START), (W_U1, START),),
    4: ((W_Q1, BESIDE), (W_U0, ACROSS),),
    6: ((W_Q2, RELAY), (W_P, RELAY),),
    8: ((W_D0, ACROSS), (W_D1, START),),
    9: ((W_D2, START),),
    11: ((W_Q2, BESIDE), (W_U0, RELAY),),
    13: ((W_U1, ACROSS),),
    14: ((W_U2, START),),
    15: ((W_P, BESIDE), (W_D0, RELAY),),
    17: ((W_D1, ACROSS),),
    19: ((W_U0, BESIDE), (W_U1, RELAY),),
}
MIDDLE = {
    0: ((W_D0, BESIDE),),
    1: ((W_D1, RELAY), (W_U2, ACROSS), (W_D2, ACROSS),),
}
TILE_STEP = {
    0: ((W_U1, BESIDE),),
    1: ((W_D1, BESIDE), (W_U2, RELAY), (W_D2, RELAY),),
    2: ((W_U2, BESIDE), (W_D2, BESIDE),),
    3: ((G_D0, FIRST), (G_U0, FIRST),),
    5: ((G_D0, SECOND), (G_U0, SECOND), (G_D1, FIRST), (G_U1, FIRST),),
}
AFTER_TILES = {
    1: ((G_D0, ALONG),),
    2: ((G_D2, FIRST), (G_U2, FIRST),),
}
BACKWARD = {
    1: ((G_D1, SECOND), (G_U1, SECOND),),
    2: ((G_D0, SPREAD), (G_U0, ALONG),),
    4: ((G_P, FIRST),),
    7: ((G_D0, PASSED), (G_D2, SECOND),),
    8: ((G_D1, ALONG), (G_U2, SECOND),),
    9: ((G_U1, ALONG),),
    10: ((G_Q0, FIRST),),
    11: ((G_U0, SPREAD),),
    14: ((G_D2, ALONG), (G_P, SECOND),),
    15: ((G_Q0, SECOND),),
    17: ((G_U0, PASSED), (G_D1, SPREAD), (G_D1, PASSED), (G_U1, SPREAD), (G_U1, PASSED), (G_Q1, FIRST),),
    19: ((G_U2, ALONG),),
    20: ((G_D0, SUMMED), (G_P, ALONG),),
}
LAST_STEPS = {
    0: ((G_Q2, FIRST), (G_K2, FIRST), (G_V2, FIRST),),
    1: ((G_D2, SPREAD), (G_Q2, SECOND),),
    2: ((G_D2, PASSED), (G_P, SPREAD), (G_Q0, ALONG),),
    3: ((G_U1, SUMMED), (G_Q1, SECOND),),
}


def chunk_shapes():
    out = []
    for _ in range(TILES):
        out += [(128, C), (OWNED, TILE)]
    return out + [(OWNED, C)] + [(3, OWNED, GCOLS)] * (GROUPS - 1) + [(OWNED, GCOLS)] * 3


def reduce_scratch():
    out = []
    for i, dims in enumerate(chunk_shapes()):
        *lead, rows, cols = dims
        near = (rows, cols // 2) if i % 2 == 0 else (rows // 2, cols)
        near = (LINKS, *lead, *near) if i < REDUCES - 3 else (REPS - 1, LINKS, *lead, rows // 2, cols // 2)
        out.append(pltpu.VMEM((LINKS, *dims), low))
        out.append(pltpu.VMEM(near, low))
        out.append(pltpu.VMEM((LINKS, *lead, rows // 2, cols // 2), low))
        out.append(pltpu.VMEM((LINKS - 1, *lead, rows // 2, cols // 2), low))
    out += [pltpu.VMEM((LINKS, 40, 128), full), pltpu.VMEM((LINKS - 1, 40, 128), full), pltpu.VMEM((REPS, 40, 128), full)]
    return out


def layer_kernel(windows, x_hbm, dy_hbm, count_ref, q32, p32, u32, d32, vec_in, tab_in, line_ref, mask_ref,
                 out_hbm, grad_hbm, gq_out, gp_out, gu_out, gd_out, gs_out, qkv_hbm, pt_hbm, n1_hbm, *scratch):
    wq, wp, up, down, small, o_ref, x1_ref, vec_ref, sums_ref, terms_ref = scratch[:10]
    gather_sems, reduce_sems, small_sems, small_reduce_sems, local = scratch[-5:]
    reduce_refs = scratch[10:-5]
    spot = Spot()
    rows_all = windows * TOK

    def live(w):
        return (w < count_ref[0]).astype(full)

    mine = spot.shard
    V = pltpu.VMEM

    jobs = {}
    places = [(W_Q[g], lambda s, g=g: wq.at[g, :, s]) for g in range(GROUPS)] + [(W_P, lambda s: wp.at[s])]
    for t in range(TILES):
        places += [(W_U[t], lambda s, t=t: up.at[t, s]), (W_D[t], lambda s, t=t: down.at[t, s])]
    for i, (name, place) in enumerate(places):
        jobs[name] = Gather(spot, place, i % 2, gather_sems.at[i], direct=name == W_Q0)
    places = []
    for t in range(TILES):
        slot = (t + SLOTS - 1) % SLOTS
        places.append((G_D[t], lambda s, slot=slot: down.at[slot, s], gd_out.at[t]))
        places.append((G_U[t], lambda s, slot=slot: up.at[slot, s], gu_out.at[t]))
    places.append((G_P, lambda s: wp.at[s], gp_out))
    for g in range(GROUPS - 1):
        places.append((G_Q[g], lambda s, g=g: wq.at[g, :, s], gq_out.at[g]))
    for part in range(3):
        places.append((G_LAST[part], lambda s, part=part: up.at[TILES - 1, s, :, pl.ds(part * GCOLS, GCOLS)], gq_out.at[GROUPS - 1, part]))
    for i, (name, place, out) in enumerate(places):
        kind = ReduceDirect if name in G_LAST else Reduce
        jobs[name] = kind(spot, place, out, *reduce_refs[4 * i : 4 * i + 4], i % 2, reduce_sems.at[i], name not in G_TWO)
    jobs[G_S] = ReduceSmall(spot, terms_ref, gs_out, *reduce_refs[-3:], small_reduce_sems)

    done = {}

    def run(name, upto):
        for stage in range(done.get(name, 0), upto + 1):
            getattr(jobs[name], jobs[name].STAGES[stage])()
        done[name] = max(done.get(name, 0), upto + 1)

    def hook(table, place):
        for item in table.get(place, ()):
            run(*item)

    def hook_window(table, g, w):
        for at in range(windows):
            place = g * windows + at
            if place in table:

                @pl.when(w == at)
                def _(place=place):
                    hook(table, place)

    barrier, peers = greet(spot)

    def cast(q_v, p_v, u_v, d_v):
        loads = [pltpu.make_async_copy(a, b, local.at[i]) for i, (a, b) in enumerate(((q32, q_v), (p32, p_v), (u32, u_v), (d32, d_v)))]
        for load in loads:
            load.start()
        small[mine] = jnp.zeros((48, 128), low)
        pad = jnp.zeros((16, 128), full)
        vec_ref[:, 0:128] = pad
        vec_ref[0:12, 0:OWNED] = vec_in[...]
        small[mine, 0:16, :] = vec_ref[:, 0:128].astype(low)
        x1_ref[0:32, 0:128] = jnp.zeros((32, 128), full)
        x1_ref[0:HEADS, 0 : tab_in.shape[1]] = tab_in[...]
        small[mine, 16:48, :] = x1_ref[0:32, 0:128].astype(low)
        loads[0].wait()
        for g in range(GROUPS):
            for part in range(3):
                wq[g, part, mine] = q_v[:, part * C + g * GCOLS : part * C + (g + 1) * GCOLS].astype(low)
        pl.semaphore_wait(barrier, peers)
        for i in range(1, OWNERS):
            send(small.at[mine], small.at[mine], small_sems.at[i], small_sems.at[OWNERS + i], (spot.rep, (mine + i) % OWNERS))
        run(W_Q0, START)
        run(W_Q1, START)
        loads[1].wait()
        wp[mine] = p_v[...].astype(low)
        loads[2].wait()
        loads[3].wait()
        for t in range(TILES):
            for s in range(OWNERS):
                src = (MLP // OWNERS) * s + 128 * t
                up[t, mine, :, s * 128 : (s + 1) * 128] = u_v[:, src : src + 128].astype(low)
            down[t, mine] = d_v[t * 128 : (t + 1) * 128, :].astype(low)

    pl.run_scoped(cast, V((OWNED, 3 * C), full), V((OWNED, C), full), V((OWNED, MLP), full), V((TILES * 128, C), full))

    def forward(dy_ref, dyt_ref, x_ref, n1_ref, qkv_ref, pt_ref, bias_ref):
        load = pltpu.make_async_copy(x_hbm, x_ref, local.at[0])
        load.start()
        load_dy = pltpu.make_async_copy(dy_hbm, dy_ref.at[0:rows_all], local.at[2])
        load_dy.start()
        zero_tail(n1_ref, windows)
        zero_tail(dy_ref, windows)
        zero_tail(o_ref, windows)
        for i in range(1, OWNERS):
            await_bytes(small.at[(mine - i + OWNERS) % OWNERS], small_sems.at[OWNERS + i])
        tab = unpack_small(small, vec_ref)
        hook(BEFORE, 0)
        load.wait()
        hook(BEFORE, 1)

        def first_norm(w, carry):
            xhat, _ = norm_parts(x_ref[window_rows(w), :].astype(full))
            n1_ref[window_rows(w), :] = (xhat * vec_ref[0:1, :] + vec_ref[1:2, :]).astype(low)
            return carry

        lax.fori_loop(0, windows, first_norm, 0)
        hook(BEFORE, 2)
        save = pltpu.make_async_copy(n1_ref, n1_hbm, local.at[1])
        save.start()
        hook(BEFORE, 3)
        load_dy.wait()

        def keep_live(w, carry):
            dy_ref[window_rows(w), :] = (dy_ref[window_rows(w), :].astype(full) * live(w)).astype(low)
            return carry

        lax.fori_loop(0, windows, keep_live, 0)
        transpose_rows(dy_ref, dyt_ref)
        hook(BEFORE, 4)

        def bias(tmp_ref):
            spread_table(tab, line_ref, tmp_ref)
            hook(BEFORE, 5)
            place_bias(tmp_ref, bias_ref)

        pl.run_scoped(bias, V((2, TOK * HEADS, 128), full))
        for g in range(GROUPS):
            cols = slice(g * GCOLS, (g + 1) * GCOLS)
            held = qkv_ref.at[g % 2]
            if g >= 2:
                pltpu.make_async_copy(held, qkv_hbm.at[g - 2], local.at[2 + g % 2]).wait()
            run(W_Q[g], ARRIVED)
            n1 = n1_ref[...]
            held[0] = ((dot(n1, flat(wq[g, 0])) + vec_ref[2:3, cols]) * (HEAD_DIM**-0.5)).astype(low)
            held[1] = dot(n1, flat(wq[g, 1])).astype(low)
            held[2] = (dot(n1, flat(wq[g, 2])) + vec_ref[3:4, cols]).astype(low)
            pltpu.make_async_copy(held, qkv_hbm.at[g], local.at[2 + g % 2]).start()

            def window(w, carry, g=g, cols=cols, held=held):
                hook_window(FORWARD, g, w)
                rows = window_rows(w)
                n = g * windows + w
                slot = n % 2
                s = against_heads(held[1, rows, :], split_diag(held[0, rows, :], mask_ref)) + bias_ref[g]
                e = jnp.exp(s - jnp.max(s, 0, keepdims=True))
                p = (e * (1.0 / jnp.sum(e, 0, keepdims=True))).astype(low)
                keep = pltpu.make_async_copy(pt_ref.at[slot], pt_hbm.at[n], local.at[4 + slot])

                @pl.when(n >= 2)
                def _():
                    keep.wait()

                pt_ref[slot] = p
                keep.start()
                o_ref[rows, cols] = undiag(held[2, rows, :].T, p, mask_ref).astype(low)
                return carry

            lax.fori_loop(0, windows, window, 0)

        run(W_P, ARRIVED)

        x1_ref[...] = x_ref[...].astype(full) + (dot(o_ref[0:rows_all], flat(wp[...])) + vec_ref[4:5, :])
        save.wait()
        for g in (GROUPS - 2, GROUPS - 1):
            pltpu.make_async_copy(qkv_ref.at[g % 2], qkv_hbm.at[g], local.at[2 + g % 2]).wait()
        for slot in range(2):
            pltpu.make_async_copy(pt_ref.at[slot], pt_hbm.at[0], local.at[4 + slot]).wait()

    def middle(dy_ref, dyt_ref, n2_ref, n2t_ref, y_ref, dn_ref, bu_ref, bsum_ref):
        zero_tail(n2_ref, windows)
        hook(MIDDLE, 0)

        def second_norm(w, carry):
            rows = window_rows(w)
            xhat, _ = norm_parts(x1_ref[rows, :])
            n2_ref[rows, :] = (xhat * vec_ref[5:6, :] + vec_ref[6:7, :]).astype(low)
            return carry

        lax.fori_loop(0, windows, second_norm, 0)
        transpose_rows(n2_ref, n2t_ref)
        hook(MIDDLE, 1)
        n2t_ref[C:, :] = jnp.ones((16, ROWS), low)
        y_ref[...] = jnp.zeros_like(y_ref)
        dn_ref[...] = jnp.zeros_like(dn_ref)
        for t in range(TILES):
            for s in range(TILE // 128):
                row, left = hidden_place(t, s)
                bu_ref[t, :, s * 128 : (s + 1) * 128] = vec_ref[row : row + 1, left : left + 128]
        hook(MIDDLE, 2)
        run(W_U0, ARRIVED)
        run(W_D0, ARRIVED)
        hook(TILE_STEP, 0)
        halves = TILE // SUB

        def step(i, carry):
            for k in range(1, TILES * halves):

                @pl.when(i == k)
                def _(k=k):
                    if k % halves == 0:
                        t = k // halves
                        for name in (W_U[t], W_D[t]):
                            run(name, ARRIVED)
                        for name in (W_U[t - 1], W_D[t - 1]):
                            jobs[name].close()
                        for name in (G_D[t - 1], G_U[t - 1]):
                            run(name, START)
                    hook(TILE_STEP, k)

            t, part = i // halves, i % halves
            cols = pl.ds(pl.multiple_of(part * SUB, SUB), SUB)
            wide = SUB // 128
            slot = (t + SLOTS - 1) % SLOTS
            u = flat(up[t, :, :, cols])
            d = flat(down[t, pl.ds(part * wide, wide)])
            h = dot(n2_ref[...], u) + bu_ref[t, :, cols]
            da = dot_nt(dy_ref[...], d)
            act, slope = gelu_both(h)
            a = act.astype(low)
            dh = (da * slope).astype(low)
            y_ref[...] += dot(a, d)
            dn_ref[...] += dot_nt(dh, u)
            gd = dot(dyt_ref[...], a).astype(low)
            down[slot, pl.ds(part * wide, wide)] = blocks(gd.T, wide)
            gu = dot(n2t_ref[...], dh)
            up[slot, :, :, cols] = blocks(gu[0:C].astype(low), OWNERS)
            bsum_ref[t, :, cols] = gu[C : C + 1]
            return carry

        lax.fori_loop(0, TILES * halves, step, 0)
        run(G_D[-1], START)
        run(G_U[-1], START)
        hook(AFTER_TILES, 0)
        sums_ref[...] = jnp.zeros_like(sums_ref)
        for t in range(TILES):
            for s in range(TILE // 128):
                row, left = hidden_place(t, s)
                sums_ref[row : row + 1, left : left + 128] = bsum_ref[t, :, s * 128 : (s + 1) * 128]
        transpose_rows(o_ref, dyt_ref)
        hook(AFTER_TILES, 1)

        def finish(w, carry):
            rows = window_rows(w)
            x1 = x1_ref[rows, :]
            xhat, scale = norm_parts(x1)
            dn = dn_ref[rows, :]
            dy = dy_ref[rows, :].astype(full)
            dx1 = dy + norm_back(xhat, scale, dn, vec_ref[5:6, :])
            dr = dx1.astype(low)
            sums_ref[4:5, :] += jnp.sum(dr.astype(full), 0, keepdims=True)
            sums_ref[5:6, :] += jnp.sum(dn * xhat, 0, keepdims=True)
            sums_ref[6:7, :] += jnp.sum(dn, 0, keepdims=True)
            sums_ref[7:8, :] += jnp.sum(dy, 0, keepdims=True)
            dy_ref[rows, :] = ((x1 + y_ref[rows, :] + vec_ref[7:8, :]) * live(w)).astype(low)
            x1_ref[rows, :] = dx1
            n2_ref[rows, :] = dr
            return carry

        lax.fori_loop(0, windows, finish, 0)
        o_ref[...] = dot_nt(n2_ref[...], flat(wp[...])).astype(low)
        save = pltpu.make_async_copy(dy_ref.at[0:rows_all], out_hbm, local.at[0])
        save.start()
        hook(AFTER_TILES, 2)
        jobs[W_P].close()
        for g in range(GROUPS):
            cols = slice(g * GCOLS, (g + 1) * GCOLS)
            wp[:, :, cols] = blocks(dot(dyt_ref[...], n2_ref[:, cols]).astype(low), OWNERS)
        run(G_P, START)
        hook(AFTER_TILES, 3)
        save.wait()

    def both(dy_ref, dyt_ref):
        pl.run_scoped(functools.partial(forward, dy_ref, dyt_ref), V((rows_all, C), low), V((ROWS, C), low),
                      V((2, 3, ROWS, GCOLS), low), V((2, TOK, PACK), low), V((GROUPS, TOK, PACK), full))
        pl.run_scoped(functools.partial(middle, dy_ref, dyt_ref), V((ROWS, C), low), V((C + 16, ROWS), low), V((ROWS, C), full), V((ROWS, C), full),
                      V((TILES, 1, TILE), full), V((TILES, 1, TILE), full))

    pl.run_scoped(both, V((ROWS, C), low), V((C, ROWS), low))

    def backward(x_ref, n1_ref, n1t_ref, qkv_ref, pt_ref, dproj_ref, dn_ref, bias_ref):
        loads = [pltpu.make_async_copy(x_hbm, x_ref, local.at[0]), pltpu.make_async_copy(n1_hbm, n1_ref, local.at[1])]
        fetch = [pltpu.make_async_copy(qkv_hbm.at[g], qkv_ref.at[g % 2], local.at[2 + g % 2]) for g in range(GROUPS)]
        fetch[0].start()
        pltpu.make_async_copy(pt_hbm.at[0], pt_ref.at[0], local.at[4]).start()
        fetch[1].start()
        for load in loads:
            load.start()
        bias_ref[...] = jnp.zeros_like(bias_ref)
        dn_ref[...] = jnp.zeros_like(dn_ref)
        for part in range(3):
            dproj_ref[part, rows_all:, :] = jnp.zeros((ROWS - rows_all, GCOLS), low)
        for g in range(GROUPS):
            cols = slice(g * GCOLS, (g + 1) * GCOLS)
            held = qkv_ref.at[g % 2]
            fetch[g].wait()

            def window(w, carry, g=g, cols=cols, held=held):
                hook_window(BACKWARD, g, w)
                rows = window_rows(w)
                n = g * windows + w
                slot = n % 2

                @pl.when(n + 1 < GROUPS * windows)
                def _():
                    pltpu.make_async_copy(pt_hbm.at[n + 1], pt_ref.at[1 - slot], local.at[5 - slot]).start()

                pltpu.make_async_copy(pt_hbm.at[n], pt_ref.at[slot], local.at[4 + slot]).wait()
                q = held[0, rows, :]
                k = held[1, rows, :]
                v = held[2, rows, :]
                p = pt_ref[slot]
                do = split_diag(o_ref[rows, cols], mask_ref)
                dp = against_heads(v, do)
                dv = over_queries(p, do).astype(low)
                pf = p.astype(full)
                ds = (pf * (dp - jnp.sum(pf * dp, 0, keepdims=True))).astype(low)
                bias_ref[g] += ds.astype(full)
                dproj_ref[1, rows, :] = over_queries(ds, split_diag(q, mask_ref)).astype(low)
                dq = (undiag(k.T, ds, mask_ref) * (HEAD_DIM**-0.5)).astype(low)
                dproj_ref[0, rows, :] = dq
                dproj_ref[2, rows, :] = dv
                sums_ref[2:3, cols] += jnp.sum(dq.astype(full), 0, keepdims=True)
                sums_ref[3:4, cols] += jnp.sum(dv.astype(full), 0, keepdims=True)
                return carry

            lax.fori_loop(0, windows, window, 0)
            if g + 2 < GROUPS:
                fetch[g + 2].start()
            if g == 0:
                for load in loads:
                    load.wait()
                transpose_rows(n1_ref, n1t_ref)
            jobs[W_Q[g]].close()
            if g == GROUPS - 1:
                jobs[W_U[-1]].close()
                for part in range(3):
                    up[TILES - 1, :, :, part * GCOLS : (part + 1) * GCOLS] = blocks(dot(n1t_ref[...], dproj_ref[part]).astype(low), OWNERS)
                    run(G_LAST[part], START)
                hook(LAST_STEPS, 0)
                for part in range(3):
                    dn_ref[...] += dot_nt(dproj_ref[part], flat(wq[g, part]))
            else:
                for part in range(3):
                    d = dproj_ref[part]
                    dn_ref[...] += dot_nt(d, flat(wq[g, part]))
                    wq[g, part] = blocks(dot(n1t_ref[...], d).astype(low), OWNERS)
                run(G_Q[g], START)

        def last_norm(grad_ref):
            def finish(w, carry):
                rows = window_rows(w)
                slot = w % 2
                xhat, scale = norm_parts(x_ref[rows, :].astype(full))
                dn = dn_ref[rows, :]
                save = pltpu.make_async_copy(grad_ref.at[slot], grad_hbm.at[rows], local.at[4 + slot])

                @pl.when(w >= 2)
                def _():
                    save.wait()

                grad_ref[slot] = x1_ref[rows, :] + norm_back(xhat, scale, dn, vec_ref[0:1, :])
                save.start()
                sums_ref[0:1, :] += jnp.sum(dn * xhat, 0, keepdims=True)
                sums_ref[1:2, :] += jnp.sum(dn, 0, keepdims=True)
                return carry

            lax.fori_loop(0, windows, finish, 0)
            hook(LAST_STEPS, 1)
            for slot in range(2):
                pltpu.make_async_copy(grad_ref.at[slot], grad_hbm.at[pl.ds(0, TOK)], local.at[4 + slot]).wait()

        pl.run_scoped(last_norm, V((2, TOK, C), full))
        hook(LAST_STEPS, 2)

        def table(tmp_ref):
            pack_small(sums_ref[...], table_grad(line_ref, tmp_ref, bias_ref), terms_ref)

        pl.run_scoped(table, V((2, TOK * HEADS, 128), full))
        run(G_S, START)
        hook(LAST_STEPS, 3)
        for stage in range(len(Reduce.STAGES)):
            for name in G_ALL:
                if stage < len(jobs[name].STAGES):
                    run(name, stage)

    pl.run_scoped(backward, V((rows_all, C), low), V((ROWS, C), low), V((C, ROWS), low), V((2, 3, ROWS, GCOLS), low), V((2, TOK, PACK), low), V((3, ROWS, GCOLS), low),
                  V((ROWS, C), full), V((GROUPS, TOK, PACK), full))
    jobs[W_D[-1]].close()
    for i in range(1, OWNERS):
        await_bytes(small.at[mine], small_sems.at[i])
    for name in G_ALL:
        jobs[name].close()


def shape(dims, kind):
    return jax.ShapeDtypeStruct(dims, kind)


def adamw(weight, moment, second, gradient, step_rate):
    moment_new = beta_one * moment + (1.0 - beta_one) * gradient
    second_new = beta_two * second + (1.0 - beta_two) * gradient * gradient
    update = moment_new * (1.0 / (1.0 - beta_one**STEP)) / (jnp.sqrt(second_new * (1.0 / (1.0 - beta_two**STEP))) + adam_eps)
    weight_new = weight * (1.0 - step_rate * weight_decay) - step_rate * update
    return (weight_new, moment_new, second_new)


def update_kernel(*refs):
    gq, gp, gu, gd, gs = refs[:5]
    ins = [refs[5 + 3 * i : 8 + 3 * i] for i in range(6)]
    outs = [refs[25 + 4 * i : 29 + 4 * i] for i in range(4)] + [refs[41:44], refs[44:47]]
    for i in range(2):
        refs[47 + i][...] = refs[23 + i][...]

    def piece(which, place, gradient):
        new = adamw(*(ref[place] for ref in ins[which]), gradient, step_rates[which])
        for ref, value in zip(outs[which], new):
            ref[place] = value
        if which < 4:
            outs[which][3][place] = new[0].astype(low)

    every = (slice(None), slice(None))
    piece(0, every, jnp.concatenate([gq[g, part] for part in range(3) for g in range(GROUPS)], 1).astype(full))
    piece(1, every, gp[...].astype(full))
    piece(2, every, jnp.concatenate([gu[t, :, s * 128 : (s + 1) * 128] for s in range(OWNERS) for t in range(TILES)], 1).astype(full))
    piece(3, every, gd[0].astype(full))

    @pl.when(pl.program_id(0) == 0)
    def _():
        piece(4, every, gs[0:12, 0:OWNED])
        piece(5, every, gs[16:40, 0 : ins[5][0].shape[1]])


def update(gq, gp, gu, gd, gs, states, results):
    steps = OWNED // 16

    def rows_of(array):
        tall = array.shape[0] // steps
        return pl.BlockSpec((tall, array.shape[1]), lambda i: (i, 0))

    def whole(array):
        return pl.BlockSpec(array.shape, lambda i: (0, 0))

    per_tile = 128 * TILES // steps
    specs = [
        pl.BlockSpec((GROUPS, 3, 16, GCOLS), lambda i: (0, 0, i, 0)),
        pl.BlockSpec((16, C), lambda i: (i, 0)),
        pl.BlockSpec((TILES, 16, TILE), lambda i: (0, i, 0)),
        pl.BlockSpec((1, per_tile, C), lambda i: (i // (128 // per_tile), i % (128 // per_tile), 0)),
        whole(gs),
    ]
    out_shapes, out_specs = [], []
    for i, group in enumerate(states):
        for array in group:
            specs.append(rows_of(array) if i < 4 else whole(array))
            out_shapes.append(shape(array.shape, full))
            out_specs.append(specs[-1])
        if i < 4:
            out_shapes.append(shape(group[0].shape, low))
            out_specs.append(rows_of(group[0]))
    results = [array.reshape(steps, -1, C) for array in results]
    for array in results:
        specs.append(pl.BlockSpec((1, *array.shape[1:]), lambda i: (i, 0, 0)))
        out_shapes.append(shape(array.shape, array.dtype))
        out_specs.append(specs[-1])
    return pl.pallas_call(
        update_kernel,
        grid=(steps,),
        in_specs=specs,
        out_specs=out_specs,
        out_shape=out_shapes,
        compiler_params=pltpu.CompilerParams(vmem_limit_bytes=63 * MIB),
        name="update",
    )(gq, gp, gu, gd, gs, *[array for group in states for array in group], *results)


def shards(
    tokens, out_grad, window_count,
    qkv_weight, qkv_first, qkv_second,
    output_weight, output_first, output_second,
    up_weight, up_first, up_second,
    down_weight, down_first, down_second,
    vectors, vector_first, vector_second,
    bias_table, table_first, table_second,
):
    windows = tokens.shape[0]
    rows = windows * TOK
    V = pltpu.VMEM
    D = pltpu.SemaphoreType.DMA
    hbm = pl.BlockSpec(memory_space=pl.ANY)
    vmem = pl.BlockSpec(memory_space=pltpu.VMEM)
    result = pl.pallas_call(
        functools.partial(layer_kernel, windows),
        out_shape=[
            shape((rows, C), low), shape((rows, C), full),
            shape((GROUPS, 3, OWNED, GCOLS), low), shape((OWNED, C), low), shape((TILES, OWNED, TILE), low), shape((TILES, 128, C), low),
            shape((40, 128), full),
            shape((GROUPS, 3, ROWS, GCOLS), low), shape((GROUPS * windows, TOK, PACK), low), shape((ROWS, C), low)],
        in_specs=[hbm, hbm, pl.BlockSpec(memory_space=pltpu.SMEM)] + [hbm] * 4 + [vmem] * 4,
        out_specs=[hbm, hbm] + [vmem] * 5 + [hbm] * 3,
        scratch_shapes=[
            V((GROUPS, 3, OWNERS, OWNED, GCOLS), low), V((OWNERS, OWNED, C), low), V((SLOTS, OWNERS, OWNED, TILE), low),
            V((SLOTS, OWNERS, 128, C), low), V((OWNERS, 48, 128), low), V((ROWS, C), low), V((rows, C), full), V((16, C), full), V((16, C), full),
            V((OWNERS, 40, 128), full)]
        + reduce_scratch()
        + [D((GATHERS, Gather.SEMS)), D((REDUCES, ReduceDirect.SEMS)), D((2 * OWNERS,)), D((ReduceSmall.SEMS,)), D((6,))],
        compiler_params=pltpu.CompilerParams(vmem_limit_bytes=63 * MIB, collective_id=0, has_side_effects=True),
        name="layer",
    )(tokens.reshape(rows, C), out_grad.reshape(rows, C), window_count, qkv_weight, output_weight, up_weight, down_weight, vectors, bias_table.T,
      jnp.asarray(line_matrix(), low), jnp.asarray(head_masks(), low))
    out, grad, gq, gp, gu, gd, gs = result[:7]
    new = update(gq, gp, gu, gd, gs, (
        (qkv_weight, qkv_first, qkv_second), (output_weight, output_first, output_second), (up_weight, up_first, up_second),
        (down_weight, down_first, down_second), (vectors, vector_first, vector_second), (bias_table.T, table_first.T, table_second.T)), (out, grad))
    *new, out, grad = new
    return (out.reshape(tokens.shape), grad.reshape(tokens.shape), *new[:-3], *(array.T for array in new[-3:]))


def vmem_call(body, outs, scratch, args, name, limit=60, **params):
    spec = pl.BlockSpec(memory_space=pltpu.VMEM)
    return pl.pallas_call(
        body,
        out_shape=outs,
        in_specs=[pl.BlockSpec(memory_space=pltpu.SMEM) if a.dtype == full and a.ndim == 1 else spec for a in args],
        out_specs=[spec] * len(outs),
        scratch_shapes=scratch,
        compiler_params=pltpu.CompilerParams(vmem_limit_bytes=limit * MIB, **params),
        name=name,
    )(*args)


def local_step(tokens, out_grad, window_count, small, wq, wp, up, down):
    windows = tokens.shape[0]
    rows = windows * TOK
    owned = C // OWNERS
    V = pltpu.VMEM
    x = tokens.reshape(rows, C)
    dy = out_grad.reshape(rows, C)
    live = (jnp.arange(windows) < window_count[0]).astype(full)
    line = jnp.asarray(line_matrix(), low)
    masks = jnp.asarray(head_masks(), low)
    qkv, pt, o, x1, n1t, vec = vmem_call(
        functools.partial(attention_forward, windows),
        [shape((9, ROWS, GCOLS), low), shape((GROUPS, windows, TOK, PACK), low), shape((ROWS, C), low), shape((rows, C), full), shape((C, ROWS), low),
         shape((16, C), full)],
        [V((ROWS, C), low), V((GROUPS, TOK, PACK), full), V((2, TOK * HEADS, 128), full)],
        (x, small, line, masks, wq, wp), "attention_forward")
    out, dx1, do, gup, gdown, gout, sums = vmem_call(
        functools.partial(feed_forward, windows),
        [shape((rows, C), low), shape((ROWS, C), full), shape((rows, C), low), shape((TILES, OWNERS, owned, TILE), low),
         shape((TILES, OWNERS, C, 128), low), shape((OWNERS, owned, C), low), shape((16, C), full)],
        [V((ROWS, C), low), V((C, ROWS), low), V((ROWS, C), low), V((C, ROWS), low), V((ROWS, C), full), V((ROWS, C), full),
         V((TILES, 1, TILE), full), V((TILES, 1, TILE), full)],
        (x1, dy, live, vec, up, down, wp, o), "feed_forward")
    gq, gsmall, grad = vmem_call(
        functools.partial(attention_backward, windows),
        [shape((GROUPS, 3, OWNERS, owned, GCOLS), low), shape((OWNERS, 40, 128), full), shape((rows, C), full)],
        [V((16, C), full), V((GROUPS, TOK, PACK), full), V((2, TOK * HEADS, 128), full), V((3, ROWS, GCOLS), low), V((ROWS, C), full)],
        (x, vec, line, masks, wq, qkv, pt, do, dx1, n1t, sums), "attention_backward")
    return out.reshape(tokens.shape), grad.reshape(tokens.shape), gq, gout, gup, gdown, gsmall


def shards_general(
    tokens, out_grad, window_count,
    qkv_weight, qkv_first, qkv_second,
    output_weight, output_first, output_second,
    up_weight, up_first, up_second,
    down_weight, down_first, down_second,
    vectors, vector_first, vector_second,
    bias_table, table_first, table_second,
):
    gather = functools.partial(lax.all_gather, axis_name="shard", tiled=True)
    scatter = functools.partial(lax.psum_scatter, axis_name="shard", tiled=True)
    owned = C // OWNERS
    wq = gather(qkv_weight.astype(low), axis=0).reshape(OWNERS, owned, 3, GROUPS, GCOLS).transpose(3, 2, 0, 1, 4)
    wp = gather(output_weight.astype(low), axis=0).reshape(OWNERS, owned, C)
    up = gather(up_weight.astype(low), axis=0).reshape(OWNERS, owned, OWNERS, TILES, 128).transpose(3, 0, 1, 2, 4)
    up = up.reshape(TILES, OWNERS, owned, TILE)
    down = gather(down_weight.astype(low), axis=0).reshape(OWNERS, TILES, 128, C).transpose(1, 0, 2, 3)
    vec = gather(vectors.astype(low), axis=1)
    tab = gather(bias_table.astype(low), axis=0)
    table_rows = tab.shape[0]
    count = TAB_ROWS // OWNERS
    vec = vec.reshape(12, OWNERS, owned).transpose(1, 0, 2)
    tab = tab[:TAB_ROWS].reshape(OWNERS, count, HEADS).transpose(0, 2, 1)
    small = jnp.concatenate([jnp.pad(vec, ((0, 0), (0, 4), (0, 128 - owned))), jnp.pad(tab, ((0, 0), (0, 8), (0, 128 - count)))], 1)
    out, grad, gq, gp, gu, gd, gs = local_step(tokens, out_grad, window_count, small, wq, wp, up, down)
    gq = gq.astype(full).transpose(2, 3, 1, 0, 4).reshape(C, 3 * C)
    gu = gu.astype(full).reshape(TILES, C, OWNERS, 128).transpose(1, 2, 0, 3).reshape(C, MLP)
    gd = gd.astype(full).transpose(1, 0, 3, 2).reshape(MLP, C)
    gv = gs[:, :12, :owned].transpose(1, 0, 2).reshape(12, C)
    gb = gs[:, 16:40, :count].transpose(0, 2, 1).reshape(TAB_ROWS, HEADS)
    gb = jnp.pad(gb, ((0, table_rows - TAB_ROWS), (0, 0)))
    totals = lax.psum(
        (scatter(gq, scatter_dimension=0), scatter(gp.astype(full).reshape(C, C), scatter_dimension=0), scatter(gu, scatter_dimension=0),
         scatter(gd, scatter_dimension=0), scatter(gv, scatter_dimension=1), scatter(gb, scatter_dimension=0)), "rep")
    states = (
        (qkv_weight, qkv_first, qkv_second), (output_weight, output_first, output_second), (up_weight, up_first, up_second),
        (down_weight, down_first, down_second), (vectors, vector_first, vector_second), (bias_table, table_first, table_second))
    results = [out, grad]
    for i, (state, total, rate) in enumerate(zip(states, totals, step_rates)):
        new = adamw(*state, total, rate)
        results += [*new, new[0].astype(low)] if i < 4 else [*new]
    return tuple(results)


def solution(mesh):
    wins = P(("rep", "shard"), None, None)
    rows = P("shard", None)
    cols = P(None, "shard")
    fits = mesh.shape["rep"] == REPS and mesh.shape["shard"] == OWNERS
    return jax.shard_map(
        shards if fits else shards_general,
        mesh=mesh,
        in_specs=(wins, wins, P(("rep", "shard"))) + (rows,) * 12 + (cols,) * 3 + (rows,) * 3,
        out_specs=(wins, wins) + (rows,) * 16 + (cols,) * 3 + (rows,) * 3,
        check_vma=False,
    )
```

```python
import functools
import math

import jax
import jax.numpy as jnp
import numpy as np
from jax import lax
from jax.experimental import pallas as pl
from jax.experimental.pallas import tpu as pltpu
from jax.sharding import PartitionSpec as P

C = 768
HEADS = 24
MLP = 3072
WIN = 12
STEP = 5
HEAD_DIM = 32
SPAN = 2 * WIN - 1
TOK = WIN * WIN
TAB_ROWS = 536
ROWS = 1024
GROUPS = 3
GCOLS = 256
GHEADS = 8
PACK = GHEADS * TOK
TAB_LANES = 640
TILES = 3
TILE = MLP // TILES
SUB = 512
LINE = 384
MIB = 1 << 20

beta_one = 0.5
beta_two = 0.6
weight_decay = 0.05
adam_eps = 1e-08
norm_eps = 1e-05
step_rates = (0.04, 0.15, 0.04, 0.02, 0.2, 1.0)
low = jnp.bfloat16
full = jnp.float32
NT = (((1,), (1,)), ((), ()))


def dot(a, b):
    return jnp.dot(a, b, preferred_element_type=full)


def dot_nt(a, b):
    return lax.dot_general(a, b, NT, preferred_element_type=full)


def line_matrix():
    out = np.zeros((TAB_LANES, LINE), np.float32)
    col = np.arange(SPAN * WIN)
    out[(col // WIN) * SPAN + col % WIN + WIN - 1, col] = 1.0
    return out


def head_masks():
    lane = np.arange(GCOLS) // HEAD_DIM
    one = (lane[None, :] == np.arange(GHEADS)[:, None]).astype(np.float32)
    return np.broadcast_to(one[:, None, :], (GHEADS, 16, GCOLS))


def norm_parts(z):
    mean = jnp.sum(z, -1, keepdims=True) * (1.0 / C)
    center = z - mean
    spread = jnp.sum(center * center, -1, keepdims=True) * (1.0 / C)
    scale = lax.rsqrt(spread + norm_eps)
    return center * scale, scale


def norm_back(xhat, scale, dn, gain):
    g = dn * gain
    m1 = jnp.sum(g, -1, keepdims=True) * (1.0 / C)
    m2 = jnp.sum(g * xhat, -1, keepdims=True) * (1.0 / C)
    return scale * (g - m1 - xhat * m2)


def diag(x, mask_ref):
    head = x[0:128].reshape(8, 16, GCOLS)
    tail = x[128:144]
    parts = []
    for h in range(GHEADS):
        parts.append((head * mask_ref[h][None]).reshape(128, GCOLS))
    for h in range(GHEADS):
        parts.append(tail * mask_ref[h])
    return jnp.concatenate(parts, 0)


def undiag(xt, m, mask_ref):
    main = []
    for h in range(0, GHEADS, 2):
        r = dot(xt[h * HEAD_DIM : (h + 2) * HEAD_DIM], m[:, h * 128 : (h + 2) * 128])
        main.append(r[0:HEAD_DIM, 0:128])
        main.append(r[HEAD_DIM : 2 * HEAD_DIM, 128:256])
    main = jnp.concatenate(main, 0)
    rest = dot(xt, m[:, GHEADS * 128 :])
    rest_t = rest.T.reshape(GHEADS, 16, GCOLS)
    keep = mask_ref[...].astype(full)
    return jnp.concatenate([main.T, jnp.sum(rest_t * keep, 0)], 0)


def flat(x):
    return x.reshape(x.shape[0] * x.shape[1], x.shape[2])


def blocks(x, owners):
    return x.reshape(owners, x.shape[0] // owners, x.shape[1])


def hidden_place(t, s):
    at = (MLP // GHEADS) * s + 128 * t
    return 8 + at // C, at % C


def unpack_small(small_ref, vec_ref):
    owners = small_ref.shape[0]
    width = C // owners
    count = TAB_ROWS // owners
    vec = jnp.zeros((16, C), full)
    tab = jnp.zeros((HEADS, TAB_LANES), full)
    lane = lax.broadcasted_iota(jnp.int32, (16, 128), 1)
    lane_tab = lax.broadcasted_iota(jnp.int32, (HEADS, 128), 1)
    for s in range(owners):
        piece = small_ref[s].astype(full)
        part = jnp.where(lane < width, piece[0:16], 0.0)
        part = jnp.concatenate([part, jnp.zeros((16, C - 128), full)], 1)
        vec = vec + (pltpu.roll(part, width * s, 1) if s else part)
        part = jnp.where(lane_tab < count, piece[16 : 16 + HEADS], 0.0)
        part = jnp.concatenate([part, jnp.zeros((HEADS, TAB_LANES - 128), full)], 1)
        tab = tab + (pltpu.roll(part, count * s, 1) if s else part)
    vec_ref[...] = vec
    return tab


def pack_small(vec, tab, out_ref):
    owners = out_ref.shape[0]
    width = C // owners
    count = TAB_ROWS // owners
    for s in range(owners):
        out_ref[s, 0:16, :] = (pltpu.roll(vec, C - width * s, 1) if s else vec)[:, 0:128]
        out_ref[s, 16:40, :] = (pltpu.roll(tab, TAB_LANES - count * s, 1) if s else tab)[:, 0:128]


def spread_table(tab, line_ref, tmp_ref):
    def column(cj, carry):
        shifted = pltpu.roll(tab, cj, 1)
        line = dot(shifted.astype(low), line_ref[...])
        for rj in range(WIN):
            cut = (WIN - 1 - rj) * WIN
            part = pltpu.roll(line, LINE - cut, 1) if cut else line
            row = pl.multiple_of((rj * WIN + cj) * HEADS, 8)
            tmp_ref[0, pl.ds(row, HEADS), :] = part[:, 0:128]
            tmp_ref[1, pl.ds(row, HEADS), :] = part[:, 128:256]
        return carry

    lax.fori_loop(0, WIN, column, 0)


def place_bias(tmp_ref, bias_ref):
    lane = lax.broadcasted_iota(jnp.int32, (TOK, 128), 1)
    for g in range(GROUPS):
        rest = jnp.zeros((TOK, 128), full)
        for h in range(GHEADS):
            at = pl.ds(g * GHEADS + h, TOK, stride=HEADS)
            bias_ref[g, :, h * 128 : (h + 1) * 128] = tmp_ref[0, at, :]
            piece = tmp_ref[1, at, :]
            piece = pltpu.roll(piece, 16 * h, 1) if h else piece
            rest = jnp.where((lane >= 16 * h) & (lane < 16 * h + 16), piece, rest)
        bias_ref[g, :, GHEADS * 128 :] = rest


def table_grad(line_ref, tmp_ref, bias_ref):
    lane = lax.broadcasted_iota(jnp.int32, (TOK, 128), 1)
    for g in range(GROUPS):
        rest = bias_ref[g, :, GHEADS * 128 :]
        for h in range(GHEADS):
            at = pl.ds(g * GHEADS + h, TOK, stride=HEADS)
            tmp_ref[0, at, :] = bias_ref[g, :, h * 128 : (h + 1) * 128]
            piece = pltpu.roll(rest, 128 - 16 * h, 1) if h else rest
            tmp_ref[1, at, :] = jnp.where(lane < 16, piece, 0.0)

    def column(cj, total):
        line = jnp.zeros((HEADS, LINE), full)
        for rj in range(WIN):
            cut = (WIN - 1 - rj) * WIN
            row = pl.multiple_of((rj * WIN + cj) * HEADS, 8)
            part = jnp.concatenate([tmp_ref[0, pl.ds(row, HEADS), :], tmp_ref[1, pl.ds(row, HEADS), :], jnp.zeros((HEADS, 128), full)], 1)
            line = line + (pltpu.roll(part, cut, 1) if cut else part)
        high = line.astype(low)
        rest = (line - high.astype(full)).astype(low)
        spread = dot_nt(high, line_ref[...]) + dot_nt(rest, line_ref[...])
        return total + pltpu.roll(spread, TAB_LANES - cj, 1)

    return lax.fori_loop(0, WIN, column, jnp.zeros((HEADS, TAB_LANES), full))


def transpose_rows(src_ref, dst_ref):
    def block(i, carry):
        at = pl.multiple_of(i * 128, 128)
        dst_ref[0 : src_ref.shape[1], pl.ds(at, 128)] = src_ref[pl.ds(at, 128), :].T
        return carry

    lax.fori_loop(0, ROWS // 128, block, 0)


def window_rows(w):
    return slice(w * TOK, (w + 1) * TOK) if isinstance(w, int) else pl.ds(pl.multiple_of(w * TOK, 16), TOK)


def zero_tail(ref, windows):
    at = windows * TOK
    ref[at:ROWS, :] = jnp.zeros((ROWS - at, ref.shape[1]), ref.dtype)


def half_diag(x, half, mask_ref):
    lanes = slice(half * 128, (half + 1) * 128)
    part = x[0:128, lanes].reshape(8, 16, 128)
    heads = range(half * GHEADS // 2, (half + 1) * GHEADS // 2)
    return jnp.concatenate([(part * mask_ref[h, :, lanes][None]).reshape(128, 128) for h in heads], 0)


def rest_diag(x, mask_ref):
    return jnp.concatenate([x[128:144] * mask_ref[h] for h in range(GHEADS)], 0)


def split_diag(x, mask_ref):
    return half_diag(x, 0, mask_ref), half_diag(x, 1, mask_ref), rest_diag(x, mask_ref)


def against_heads(x, split):
    first, second, rest = split
    return jnp.concatenate([dot_nt(x[:, 0:128], first), dot_nt(x[:, 128:256], second), dot_nt(x, rest)], 1)


def over_queries(m, split):
    first, second, rest = split
    return jnp.concatenate([dot(m[:, 0:512], first), dot(m[:, 512:1024], second)], 1) + dot(m[:, 1024:], rest)


def attention_forward(windows, x_ref, small_ref, line_ref, mask_ref, wq_ref, wp_ref,
                      qkv_ref, pt_ref, o_ref, x1_ref, n1t_ref, vec_ref, n1_ref, bias_ref, tmp_ref):
    tab = unpack_small(small_ref, vec_ref)
    spread_table(tab, line_ref, tmp_ref)
    place_bias(tmp_ref, bias_ref)
    zero_tail(n1_ref, windows)
    zero_tail(o_ref, windows)

    def first_norm(w, carry):
        xhat, _ = norm_parts(x_ref[window_rows(w), :].astype(full))
        n1_ref[window_rows(w), :] = (xhat * vec_ref[0:1, :] + vec_ref[1:2, :]).astype(low)
        return carry

    lax.fori_loop(0, windows, first_norm, 0)
    transpose_rows(n1_ref, n1t_ref)

    def group(g, carry):
        cols = pl.ds(pl.multiple_of(g * GCOLS, GCOLS), GCOLS)
        n1 = n1_ref[...]
        qkv_ref[g] = ((dot(n1, flat(wq_ref[g, 0])) + vec_ref[2:3, cols]) * (HEAD_DIM**-0.5)).astype(low)
        qkv_ref[GROUPS + g] = dot(n1, flat(wq_ref[g, 1])).astype(low)
        qkv_ref[2 * GROUPS + g] = (dot(n1, flat(wq_ref[g, 2])) + vec_ref[3:4, cols]).astype(low)

        def window(w, inner):
            rows = window_rows(w)
            q = qkv_ref[g, rows, :]
            k = qkv_ref[GROUPS + g, rows, :]
            v = qkv_ref[2 * GROUPS + g, rows, :]
            s = dot_nt(k, diag(q, mask_ref)) + bias_ref[g]
            e = jnp.exp(s - jnp.max(s, 0, keepdims=True))
            p = (e * (1.0 / jnp.sum(e, 0, keepdims=True))).astype(low)
            pt_ref[g, w] = p
            o_ref[rows, cols] = undiag(v.T, p, mask_ref).astype(low)
            return inner

        lax.fori_loop(0, windows, window, 0)
        return carry

    lax.fori_loop(0, GROUPS, group, 0)

    def output(w, carry):
        rows = window_rows(w)
        branch = dot(o_ref[rows, :], flat(wp_ref[...])) + vec_ref[4:5, :]
        x1_ref[rows, :] = x_ref[rows, :].astype(full) + branch
        return carry

    lax.fori_loop(0, windows, output, 0)


def gelu_both(h):
    c = math.sqrt(2.0 / math.pi)
    square = h * h
    t = jnp.tanh(h * (c + (c * 0.044715) * square))
    half = 0.5 + 0.5 * t
    act = h * half
    return act, half + act * (1.0 - half) * (2.0 * c + (6.0 * c * 0.044715) * square)


def feed_forward(windows, x1_ref, dy_ref, live_ref, vec_ref, up_ref, down_ref, wp_ref, o_ref,
                 out_ref, dx1_ref, do_ref, gup_ref, gdown_ref, gout_ref, sums_ref,
                 n2_ref, n2t_ref, dy2_ref, dyt_ref, y_ref, dn_ref, bu_ref, bsum_ref):
    zero_tail(n2_ref, windows)
    zero_tail(dy2_ref, windows)

    def second_norm(w, carry):
        rows = window_rows(w)
        xhat, _ = norm_parts(x1_ref[rows, :])
        n2_ref[rows, :] = (xhat * vec_ref[5:6, :] + vec_ref[6:7, :]).astype(low)
        dy2_ref[rows, :] = (dy_ref[rows, :].astype(full) * live_ref[w]).astype(low)
        return carry

    lax.fori_loop(0, windows, second_norm, 0)
    transpose_rows(n2_ref, n2t_ref)
    transpose_rows(dy2_ref, dyt_ref)
    y_ref[...] = jnp.zeros_like(y_ref)
    dn_ref[...] = jnp.zeros_like(dn_ref)
    owners = gup_ref.shape[1]
    for t in range(TILES):
        for s in range(TILE // 128):
            row, at = hidden_place(t, s)
            bu_ref[t, :, s * 128 : (s + 1) * 128] = vec_ref[row : row + 1, at : at + 128]

    def step(t, carry):
        for part in range(TILE // SUB):
            cols = slice(part * SUB, (part + 1) * SUB)
            up = flat(up_ref[t, :, :, cols])
            down = flat(down_ref[t, part * SUB // 128 : (part + 1) * SUB // 128])
            h = dot(n2_ref[...], up) + bu_ref[t, :, cols]
            da = dot_nt(dy2_ref[...], down)
            act, slope = gelu_both(h)
            a = act.astype(low)
            dh = (da * slope).astype(low)
            bsum_ref[t, :, cols] = jnp.sum(dh.astype(full), 0, keepdims=True)
            y_ref[...] += dot(a, down)
            dn_ref[...] += dot_nt(dh, up)
            gd = dot(dyt_ref[...], a).astype(low)
            for b in range(SUB // 128):
                gdown_ref[t, part * SUB // 128 + b] = gd[:, b * 128 : (b + 1) * 128]
            gup_ref[t, :, :, cols] = blocks(dot(n2t_ref[...], dh).astype(low), owners)
        return carry

    lax.fori_loop(0, TILES, step, 0)
    sums_ref[...] = jnp.zeros_like(sums_ref)
    for t in range(TILES):
        for s in range(TILE // 128):
            row, at = hidden_place(t, s)
            sums_ref[row : row + 1, at : at + 128] = bsum_ref[t, :, s * 128 : (s + 1) * 128]
    zero_tail(dx1_ref, windows)

    def finish(w, carry):
        rows = window_rows(w)
        x1 = x1_ref[rows, :]
        out_ref[rows, :] = ((x1 + y_ref[rows, :] + vec_ref[7:8, :]) * live_ref[w]).astype(low)
        xhat, scale = norm_parts(x1)
        dn = dn_ref[rows, :]
        dy = dy2_ref[rows, :].astype(full)
        dx1 = dy + norm_back(xhat, scale, dn, vec_ref[5:6, :])
        dx1_ref[rows, :] = dx1
        dr = dx1.astype(low)
        n2_ref[rows, :] = dr
        do_ref[rows, :] = dot_nt(dr, flat(wp_ref[...])).astype(low)
        sums_ref[4:5, :] += jnp.sum(dr.astype(full), 0, keepdims=True)
        sums_ref[5:6, :] += jnp.sum(dn * xhat, 0, keepdims=True)
        sums_ref[6:7, :] += jnp.sum(dn, 0, keepdims=True)
        sums_ref[7:8, :] += jnp.sum(dy, 0, keepdims=True)
        return carry

    lax.fori_loop(0, windows, finish, 0)
    transpose_rows(o_ref, dyt_ref)
    for g in range(GROUPS):
        at = pl.ds(g * GCOLS, GCOLS)
        gout_ref[:, :, at] = blocks(dot(dyt_ref[...], n2_ref[:, at]).astype(low), gout_ref.shape[0])


def attention_backward(windows, x_ref, vec_ref, line_ref, mask_ref, wq_ref, qkv_ref, pt_ref, do_ref, dx1_ref, n1t_ref, sums_in_ref,
                       gq_ref, gsmall_ref, grad_ref, sums_ref, bias_ref, tmp_ref, dproj_ref, dn_ref):
    bias_ref[...] = jnp.zeros_like(bias_ref)
    dn_ref[...] = jnp.zeros_like(dn_ref)
    sums_ref[...] = sums_in_ref[...]
    for part in range(3):
        dproj_ref[part, windows * TOK :, :] = jnp.zeros((ROWS - windows * TOK, GCOLS), low)

    def group(g, carry):
        cols = pl.ds(pl.multiple_of(g * GCOLS, GCOLS), GCOLS)

        def window(w, inner):
            rows = window_rows(w)
            q = qkv_ref[g, rows, :]
            k = qkv_ref[GROUPS + g, rows, :]
            v = qkv_ref[2 * GROUPS + g, rows, :]
            p = pt_ref[g, w]
            do = diag(do_ref[rows, cols], mask_ref)
            dp = dot_nt(v, do)
            dv = dot(p, do)
            pf = p.astype(full)
            ds = (pf * (dp - jnp.sum(pf * dp, 0, keepdims=True))).astype(low)
            bias_ref[g] += ds.astype(full)
            dk = dot(ds, diag(q, mask_ref))
            dq = undiag(k.T, ds, mask_ref) * (HEAD_DIM**-0.5)
            dq = dq.astype(low)
            dv = dv.astype(low)
            dproj_ref[0, rows, :] = dq
            dproj_ref[1, rows, :] = dk.astype(low)
            dproj_ref[2, rows, :] = dv
            sums_ref[2:3, cols] += jnp.sum(dq.astype(full), 0, keepdims=True)
            sums_ref[3:4, cols] += jnp.sum(dv.astype(full), 0, keepdims=True)
            return inner

        lax.fori_loop(0, windows, window, 0)
        for part in range(3):
            d = dproj_ref[part]
            gq_ref[g, part] = blocks(dot(n1t_ref[...], d).astype(low), gq_ref.shape[2])
            dn_ref[...] += dot_nt(d, flat(wq_ref[g, part]))
        return carry

    lax.fori_loop(0, GROUPS, group, 0)

    def finish(w, carry):
        rows = window_rows(w)
        xhat, scale = norm_parts(x_ref[rows, :].astype(full))
        dn = dn_ref[rows, :]
        grad_ref[rows, :] = dx1_ref[rows, :] + norm_back(xhat, scale, dn, vec_ref[0:1, :])
        sums_ref[0:1, :] += jnp.sum(dn * xhat, 0, keepdims=True)
        sums_ref[1:2, :] += jnp.sum(dn, 0, keepdims=True)
        return carry

    lax.fori_loop(0, windows, finish, 0)
    pack_small(sums_ref[...], table_grad(line_ref, tmp_ref, bias_ref), gsmall_ref)


MESH = pl.DeviceIdType.MESH
REPS = 4
OWNERS = 8
LINKS = OWNERS // 2


class Spot:
    def __init__(self):
        self.rep = lax.axis_index("rep")
        self.shard = lax.axis_index("shard")
        self.z = self.shard // 2
        self.core = self.shard % 2

    def sibling(self):
        return (self.rep, self.z * 2 + (1 - self.core))

    def along_z(self, step):
        return (self.rep, ((self.z + step) % LINKS) * 2 + self.core)

    def turned(self, axis):
        x, y = self.rep % 2, self.rep // 2
        return y * 2 + (1 - x) if axis == 0 else (1 - y) * 2 + x

    def beside(self, axis):
        return (self.turned(axis), self.shard)

    def across(self):
        return (REPS - 1 - self.rep, self.shard)


def greet(spot):
    barrier = pltpu.get_barrier_semaphore()
    peers = [(spot.rep, (spot.shard + i) % OWNERS) for i in range(1, OWNERS)]
    peers += [((spot.rep + i) % REPS, spot.shard) for i in range(1, REPS)]
    for peer in peers:
        pl.semaphore_signal(barrier, inc=1, device_id=peer, device_id_type=MESH)
    return barrier, len(peers)


def send(src, dst, send_sem, recv_sem, peer):
    pltpu.make_async_remote_copy(src_ref=src, dst_ref=dst, send_sem=send_sem, recv_sem=recv_sem, device_id=peer, device_id_type=MESH).start()


def await_bytes(ref, sem):
    pltpu.make_async_copy(ref, ref, sem).wait()


def quarter(ref, rep):
    rows, cols = ref.shape[-2:]
    lead = (slice(None),) * (len(ref.shape) - 2)
    top = pl.multiple_of((rep // 2) * (rows // 2), 16)
    left = pl.multiple_of((rep % 2) * (cols // 2), 128)
    return ref.at[lead + (pl.ds(top, rows // 2), pl.ds(left, cols // 2))]


def half(ref, rep, axis):
    rows, cols = ref.shape[-2:]
    lead = (slice(None),) * (len(ref.shape) - 2)
    if axis == 0:
        left = pl.multiple_of((rep % 2) * (cols // 2), 128)
        return ref.at[lead + (slice(None), pl.ds(left, cols // 2))]
    top = pl.multiple_of((rep // 2) * (rows // 2), 16)
    return ref.at[lead + (pl.ds(top, rows // 2), slice(None))]


class Gather:
    KINDS = (LINKS - 1, LINKS - 1, LINKS - 1, LINKS - 1, LINKS)
    SEMS = 2 * sum(KINDS)
    STAGES = ("start", "across", "relay", "beside", "finish")

    def __init__(self, spot, place, axis, sems, direct=False):
        self.spot, self.place, self.axis, self.sems, self.direct = spot, place, axis, sems, direct

    def sem(self, side, kind, i):
        return self.sems.at[side * (self.SEMS // 2) + sum(self.KINDS[:kind]) + i]

    def block(self, step):
        return self.place(((self.spot.z - step + LINKS) % LINKS) * 2 + self.spot.core)

    def other(self, step):
        return self.place(((self.spot.z - step + LINKS) % LINKS) * 2 + 1 - self.spot.core)

    def start(self):
        spot = self.spot
        mine = self.block(0)
        for i in range(1, LINKS):
            piece = quarter(mine, spot.rep)
            send(piece, piece, self.sem(0, 0, i - 1), self.sem(1, 0, i - 1), spot.along_z(i))
        send(mine, mine, self.sem(0, 4, 0), self.sem(1, 4, 0), spot.sibling())

    def across(self):
        spot = self.spot
        for i in range(1, LINKS):
            piece = quarter(self.block(i), spot.rep)
            await_bytes(piece, self.sem(1, 0, i - 1))
            for axis in (self.axis, 1 - self.axis):
                send(piece, piece, self.sem(0, 1 + axis, i - 1), self.sem(1, 1 + axis, i - 1), spot.beside(axis))
            if self.direct:
                send(piece, piece, self.sem(0, 3, i - 1), self.sem(1, 3, i - 1), spot.across())

    def relay(self):
        spot = self.spot
        if self.direct:
            return
        for i in range(1, LINKS):
            piece = quarter(self.block(i), spot.turned(self.axis))
            await_bytes(piece, self.sem(1, 1 + self.axis, i - 1))
            send(piece, piece, self.sem(0, 3, i - 1), self.sem(1, 3, i - 1), spot.beside(1 - self.axis))

    def beside(self):
        spot = self.spot
        for i in range(1, LINKS):
            block = self.block(i)
            piece = quarter(block, spot.rep)
            if self.direct:
                await_bytes(piece, self.sem(1, 1 + self.axis, i - 1))
            await_bytes(piece, self.sem(1, 2 - self.axis, i - 1))
            await_bytes(piece, self.sem(1, 3, i - 1))
            send(block, block, self.sem(0, 4, i), self.sem(1, 4, i), spot.sibling())

    def finish(self):
        for i in range(LINKS):
            await_bytes(self.other(i), self.sem(1, 4, i))

    def close(self):
        piece = quarter(self.block(0), self.spot.rep)
        for kind in range(4):
            for i in range(1, LINKS):
                await_bytes(piece, self.sem(0, kind, i - 1))
        for i in range(LINKS):
            await_bytes(self.block(i), self.sem(0, 4, i))


class Reduce:
    KINDS = (LINKS, 1, 1, LINKS - 1, REPS - 1)
    SEMS = 2 * sum(KINDS)
    STAGES = ("start", "first", "second", "along", "spread", "passed", "finish")

    def __init__(self, spot, place, out, core_sum, halves, quarters, links, axis, sems, direct):
        self.spot, self.place, self.out, self.axis, self.sems, self.direct = spot, place, out, axis, sems, direct
        self.core_sum, self.halves, self.quarters, self.links = core_sum, halves, quarters, links

    def sem(self, side, kind, i):
        return self.sems.at[side * (self.SEMS // 2) + sum(self.KINDS[:kind]) + i]

    def start(self):
        spot = self.spot
        for z in range(LINKS):
            send(self.place(z * 2 + (1 - spot.core)), self.core_sum.at[z], self.sem(0, 0, z), self.sem(1, 0, z), spot.sibling())

    def first(self):
        spot = self.spot
        for z in range(LINKS):
            total = self.core_sum.at[z]
            await_bytes(total, self.sem(1, 0, z))
            total[...] = (total[...].astype(full) + self.place(z * 2 + spot.core)[...].astype(full)).astype(low)
        theirs = half(self.core_sum, spot.turned(self.axis), self.axis)
        send(theirs, self.halves, self.sem(0, 1, 0), self.sem(1, 1, 0), spot.beside(self.axis))

    def second(self):
        spot = self.spot
        await_bytes(self.halves, self.sem(1, 1, 0))
        mine = half(self.core_sum, spot.rep, self.axis)
        self.halves[...] = (self.halves[...].astype(full) + mine[...].astype(full)).astype(low)
        theirs = half(self.halves, spot.turned(1 - self.axis), 1 - self.axis)
        send(theirs, self.quarters, self.sem(0, 2, 0), self.sem(1, 2, 0), spot.beside(1 - self.axis))

    def along(self):
        spot = self.spot
        await_bytes(self.quarters, self.sem(1, 2, 0))
        mine = half(self.halves, spot.rep, 1 - self.axis)
        self.quarters[...] = (self.quarters[...].astype(full) + mine[...].astype(full)).astype(low)
        for i in range(1, LINKS):
            send(self.quarters.at[(spot.z + i) % LINKS], self.links.at[i - 1], self.sem(0, 3, i - 1), self.sem(1, 3, i - 1), spot.along_z(i))

    def spread(self):
        spot = self.spot
        total = self.quarters[spot.z].astype(full)
        for i in range(1, LINKS):
            await_bytes(self.links.at[i - 1], self.sem(1, 3, i - 1))
            total = total + self.links[i - 1].astype(full)
        mine = quarter(self.out, spot.rep)
        mine[...] = total.astype(low)
        for axis in (self.axis, 1 - self.axis):
            send(mine, mine, self.sem(0, 4, axis), self.sem(1, 4, axis), spot.beside(axis))
        if self.direct:
            send(mine, mine, self.sem(0, 4, 2), self.sem(1, 4, 2), spot.across())

    def passed(self):
        spot = self.spot
        theirs = quarter(self.out, spot.turned(self.axis))
        await_bytes(theirs, self.sem(1, 4, self.axis))
        if not self.direct:
            send(theirs, theirs, self.sem(0, 4, 2), self.sem(1, 4, 2), spot.beside(1 - self.axis))

    def finish(self):
        spot = self.spot
        await_bytes(quarter(self.out, spot.turned(1 - self.axis)), self.sem(1, 4, 1 - self.axis))
        await_bytes(quarter(self.out, REPS - 1 - spot.rep), self.sem(1, 4, 2))

    def close(self):
        for z in range(LINKS):
            await_bytes(self.core_sum.at[z], self.sem(0, 0, z))
        await_bytes(self.halves, self.sem(0, 1, 0))
        await_bytes(self.quarters, self.sem(0, 2, 0))
        for i in range(1, LINKS):
            await_bytes(self.links.at[i - 1], self.sem(0, 3, i - 1))
        for j in range(1, REPS):
            await_bytes(quarter(self.out, self.spot.rep), self.sem(0, 4, j - 1))


class ReduceDirect(Reduce):
    KINDS = (LINKS, REPS - 1, 0, LINKS - 1, REPS - 1)
    SEMS = 2 * sum(KINDS)

    def peers(self):
        spot = self.spot
        return (spot.turned(0), spot.turned(1), REPS - 1 - spot.rep)

    def first(self):
        spot = self.spot
        for z in range(LINKS):
            total = self.core_sum.at[z]
            await_bytes(total, self.sem(1, 0, z))
            total[...] = (total[...].astype(full) + self.place(z * 2 + spot.core)[...].astype(full)).astype(low)
        for j, rep in enumerate(self.peers()):
            send(quarter(self.core_sum, rep), self.halves.at[j], self.sem(0, 1, j), self.sem(1, 1, j), (rep, spot.shard))

    def second(self):
        pass

    def along(self):
        spot = self.spot
        total = quarter(self.core_sum, spot.rep)[...].astype(full)
        for j in range(REPS - 1):
            await_bytes(self.halves.at[j], self.sem(1, 1, j))
            total = total + self.halves[j].astype(full)
        self.quarters[...] = total.astype(low)
        for i in range(1, LINKS):
            send(self.quarters.at[(spot.z + i) % LINKS], self.links.at[i - 1], self.sem(0, 3, i - 1), self.sem(1, 3, i - 1), spot.along_z(i))

    def close(self):
        for z in range(LINKS):
            await_bytes(self.core_sum.at[z], self.sem(0, 0, z))
        for j in range(REPS - 1):
            await_bytes(self.halves.at[j], self.sem(0, 1, j))
        for i in range(1, LINKS):
            await_bytes(self.links.at[i - 1], self.sem(0, 3, i - 1))
        for j in range(1, REPS):
            await_bytes(quarter(self.out, self.spot.rep), self.sem(0, 4, j - 1))


class ReduceSmall:
    KINDS = (LINKS, LINKS - 1, REPS - 1)
    SEMS = 2 * sum(KINDS)
    STAGES = ("start", "first", "second", "along")

    def __init__(self, spot, terms, out, core_sum, links, parts, sems):
        self.spot, self.terms, self.out, self.core_sum, self.links, self.parts, self.sems = spot, terms, out, core_sum, links, parts, sems

    sem = Reduce.sem

    def start(self):
        spot = self.spot
        for z in range(LINKS):
            send(self.terms.at[z * 2 + (1 - spot.core)], self.core_sum.at[z], self.sem(0, 0, z), self.sem(1, 0, z), spot.sibling())

    def first(self):
        spot = self.spot
        for z in range(LINKS):
            await_bytes(self.core_sum.at[z], self.sem(1, 0, z))
            self.core_sum[z] = self.core_sum[z] + self.terms[z * 2 + spot.core]
        for i in range(1, LINKS):
            send(self.core_sum.at[(spot.z + i) % LINKS], self.links.at[i - 1], self.sem(0, 1, i - 1), self.sem(1, 1, i - 1), spot.along_z(i))

    def second(self):
        spot = self.spot
        total = self.core_sum[spot.z]
        for i in range(1, LINKS):
            await_bytes(self.links.at[i - 1], self.sem(1, 1, i - 1))
            total = total + self.links[i - 1]
        self.parts[spot.rep] = total
        mine = self.parts.at[spot.rep]
        for j in range(1, REPS):
            send(mine, mine, self.sem(0, 2, j - 1), self.sem(1, 2, j - 1), ((spot.rep + j) % REPS, spot.shard))

    def along(self):
        for j in range(1, REPS):
            await_bytes(self.parts.at[(self.spot.rep - j + REPS) % REPS], self.sem(1, 2, j - 1))
        total = self.parts[0]
        for j in range(1, REPS):
            total = total + self.parts[j]
        self.out[...] = total

    def close(self):
        for z in range(LINKS):
            await_bytes(self.core_sum.at[z], self.sem(0, 0, z))
        for i in range(1, LINKS):
            await_bytes(self.links.at[i - 1], self.sem(0, 1, i - 1))
        for j in range(1, REPS):
            await_bytes(self.parts.at[self.spot.rep], self.sem(0, 2, j - 1))


OWNED = C // OWNERS
SLOTS = TILES + 1
GATHERS = 2 * TILES + 1 + GROUPS
REDUCES = 2 * TILES + 1 + (GROUPS - 1) + 3
W_Q0, W_Q1, W_Q2, W_P, W_U0, W_D0, W_U1, W_D1, W_U2, W_D2 = W_ALL = range(10)
G_D0, G_U0, G_D1, G_U1, G_D2, G_U2, G_P, G_Q0, G_Q1, G_Q2, G_K2, G_V2, G_S = G_ALL = range(10, 23)
W_Q, W_U, W_D = (W_Q0, W_Q1, W_Q2), (W_U0, W_U1, W_U2), (W_D0, W_D1, W_D2)
G_D, G_U, G_Q, G_LAST = (G_D0, G_D1, G_D2), (G_U0, G_U1, G_U2), (G_Q0, G_Q1), (G_Q2, G_K2, G_V2)
G_TWO = ()
START, ACROSS, RELAY, BESIDE, ARRIVED = range(5)
FIRST, SECOND, ALONG, SPREAD, PASSED, SUMMED = range(1, 7)
BEFORE = {
    2: ((W_Q0, ACROSS), (W_Q0, RELAY),),
    3: ((W_Q2, START), (W_P, START), (W_U0, START),),
    5: ((W_Q0, BESIDE), (W_Q1, ACROSS),),
}
FORWARD = {
    0: ((W_Q1, RELAY), (W_Q2, ACROSS), (W_P, ACROSS), (W_D0, START),),
    4: ((W_Q1, BESIDE),),
    5: ((W_U0, ACROSS),),
    6: ((W_Q2, RELAY), (W_D1, START),),
    7: ((W_P, RELAY),),
    8: ((W_U1, START),),
    9: ((W_D0, ACROSS),),
    10: ((W_U0, RELAY),),
    11: ((W_Q2, BESIDE),),
    14: ((W_D0, RELAY), (W_U2, START),),
    15: ((W_D1, ACROSS),),
    16: ((W_P, BESIDE), (W_D2, START),),
    19: ((W_U1, ACROSS),),
    20: ((W_U0, BESIDE), (W_D0, BESIDE),),
}
MIDDLE = {
    0: ((W_U2, ACROSS),),
    1: ((W_D1, RELAY),),
    2: ((W_U1, RELAY), (W_D2, ACROSS),),
}
TILE_STEP = {
    1: ((W_U1, BESIDE), (W_D1, BESIDE), (W_U2, RELAY),),
    2: ((W_D2, RELAY),),
    3: ((G_D0, FIRST), (G_U0, FIRST), (W_U2, BESIDE), (W_D2, BESIDE),),
    5: ((G_D0, SECOND), (G_U0, SECOND), (G_D1, FIRST), (G_U1, FIRST),),
}
AFTER_TILES = {
    0: ((G_D0, ALONG),),
    2: ((G_U0, ALONG), (G_D2, FIRST), (G_U2, FIRST),),
}
BACKWARD = {
    1: ((G_U1, SECOND),),
    3: ((G_D0, SPREAD), (G_D1, SECOND), (G_P, FIRST),),
    5: ((G_D2, SECOND),),
    7: ((G_U0, SPREAD), (G_U0, PASSED),),
    9: ((G_D0, PASSED), (G_U1, ALONG), (G_Q0, FIRST),),
    11: ((G_D1, ALONG),),
    12: ((G_U2, SECOND),),
    14: ((G_D2, ALONG), (G_P, SECOND),),
    16: ((G_U1, SPREAD), (G_Q0, SECOND),),
    17: ((G_U0, SUMMED), (G_U2, ALONG),),
    19: ((G_D1, SPREAD), (G_D1, PASSED), (G_Q1, FIRST),),
    20: ((G_D2, SPREAD), (G_P, ALONG),),
}
LAST_STEPS = {
    0: ((G_D0, SUMMED), (G_U2, SPREAD), (G_Q2, FIRST), (G_Q2, SECOND), (G_K2, FIRST),),
    1: ((G_P, SPREAD), (G_Q0, ALONG), (G_V2, FIRST),),
    3: ((G_U2, PASSED), (G_Q0, SPREAD),),
}


def chunk_shapes():
    out = []
    for _ in range(TILES):
        out += [(128, C), (OWNED, TILE)]
    return out + [(OWNED, C)] + [(3, OWNED, GCOLS)] * (GROUPS - 1) + [(OWNED, GCOLS)] * 3


def reduce_scratch():
    out = []
    for i, dims in enumerate(chunk_shapes()):
        *lead, rows, cols = dims
        near = (rows, cols // 2) if i % 2 == 0 else (rows // 2, cols)
        near = (LINKS, *lead, *near) if i < REDUCES - 3 else (REPS - 1, LINKS, *lead, rows // 2, cols // 2)
        out.append(pltpu.VMEM((LINKS, *dims), low))
        out.append(pltpu.VMEM(near, low))
        out.append(pltpu.VMEM((LINKS, *lead, rows // 2, cols // 2), low))
        out.append(pltpu.VMEM((LINKS - 1, *lead, rows // 2, cols // 2), low))
    out += [pltpu.VMEM((LINKS, 40, 128), full), pltpu.VMEM((LINKS - 1, 40, 128), full), pltpu.VMEM((REPS, 40, 128), full)]
    return out


def layer_kernel(windows, x_hbm, dy_hbm, count_ref, q32, p32, u32, d32, vec_in, tab_in, line_ref, mask_ref,
                 out_hbm, grad_hbm, gq_out, gp_out, gu_out, gd_out, gs_out, qkv_hbm, pt_hbm, n1_hbm, *scratch):
    wq, wp, up, down, small, o_ref, x1_ref, vec_ref, sums_ref, terms_ref = scratch[:10]
    gather_sems, reduce_sems, small_sems, small_reduce_sems, local = scratch[-5:]
    reduce_refs = scratch[10:-5]
    spot = Spot()
    rows_all = windows * TOK

    def live(w):
        return (w < count_ref[0]).astype(full)

    mine = spot.shard
    V = pltpu.VMEM

    jobs = {}
    places = [(W_Q[g], lambda s, g=g: wq.at[g, :, s]) for g in range(GROUPS)] + [(W_P, lambda s: wp.at[s])]
    for t in range(TILES):
        places += [(W_U[t], lambda s, t=t: up.at[t, s]), (W_D[t], lambda s, t=t: down.at[t, s])]
    for i, (name, place) in enumerate(places):
        jobs[name] = Gather(spot, place, i % 2, gather_sems.at[i], direct=name == W_Q0)
    places = []
    for t in range(TILES):
        slot = (t + SLOTS - 1) % SLOTS
        places.append((G_D[t], lambda s, slot=slot: down.at[slot, s], gd_out.at[t]))
        places.append((G_U[t], lambda s, slot=slot: up.at[slot, s], gu_out.at[t]))
    places.append((G_P, lambda s: wp.at[s], gp_out))
    for g in range(GROUPS - 1):
        places.append((G_Q[g], lambda s, g=g: wq.at[g, :, s], gq_out.at[g]))
    for part in range(3):
        places.append((G_LAST[part], lambda s, part=part: up.at[TILES - 1, s, :, pl.ds(part * GCOLS, GCOLS)], gq_out.at[GROUPS - 1, part]))
    for i, (name, place, out) in enumerate(places):
        kind = ReduceDirect if name in G_LAST else Reduce
        jobs[name] = kind(spot, place, out, *reduce_refs[4 * i : 4 * i + 4], i % 2, reduce_sems.at[i], name not in G_TWO)
    jobs[G_S] = ReduceSmall(spot, terms_ref, gs_out, *reduce_refs[-3:], small_reduce_sems)

    done = {}

    def run(name, upto):
        for stage in range(done.get(name, 0), upto + 1):
            getattr(jobs[name], jobs[name].STAGES[stage])()
        done[name] = max(done.get(name, 0), upto + 1)

    def hook(table, place):
        for item in table.get(place, ()):
            run(*item)

    def hook_window(table, g, w):
        for at in range(windows):
            place = g * windows + at
            if place in table:

                @pl.when(w == at)
                def _(place=place):
                    hook(table, place)

    barrier, peers = greet(spot)

    def cast(q_v, p_v, u_v, d_v):
        loads = [pltpu.make_async_copy(a, b, local.at[i]) for i, (a, b) in enumerate(((q32, q_v), (p32, p_v), (u32, u_v), (d32, d_v)))]
        for load in loads:
            load.start()
        small[mine] = jnp.zeros((48, 128), low)
        pad = jnp.zeros((16, 128), full)
        vec_ref[:, 0:128] = pad
        vec_ref[0:12, 0:OWNED] = vec_in[...]
        small[mine, 0:16, :] = vec_ref[:, 0:128].astype(low)
        x1_ref[0:32, 0:128] = jnp.zeros((32, 128), full)
        x1_ref[0:HEADS, 0 : tab_in.shape[1]] = tab_in[...]
        small[mine, 16:48, :] = x1_ref[0:32, 0:128].astype(low)
        loads[0].wait()
        for g in range(GROUPS):
            for part in range(3):
                wq[g, part, mine] = q_v[:, part * C + g * GCOLS : part * C + (g + 1) * GCOLS].astype(low)
        pl.semaphore_wait(barrier, peers)
        for i in range(1, OWNERS):
            send(small.at[mine], small.at[mine], small_sems.at[i], small_sems.at[OWNERS + i], (spot.rep, (mine + i) % OWNERS))
        run(W_Q0, START)
        run(W_Q1, START)
        loads[1].wait()
        wp[mine] = p_v[...].astype(low)
        loads[2].wait()
        loads[3].wait()
        for t in range(TILES):
            for s in range(OWNERS):
                src = (MLP // OWNERS) * s + 128 * t
                up[t, mine, :, s * 128 : (s + 1) * 128] = u_v[:, src : src + 128].astype(low)
            down[t, mine] = d_v[t * 128 : (t + 1) * 128, :].astype(low)

    pl.run_scoped(cast, V((OWNED, 3 * C), full), V((OWNED, C), full), V((OWNED, MLP), full), V((TILES * 128, C), full))

    def forward(dy_ref, dyt_ref, x_ref, n1_ref, qkv_ref, pt_ref, bias_ref):
        load = pltpu.make_async_copy(x_hbm, x_ref, local.at[0])
        load.start()
        load_dy = pltpu.make_async_copy(dy_hbm, dy_ref.at[0:rows_all], local.at[2])
        load_dy.start()
        zero_tail(n1_ref, windows)
        zero_tail(dy_ref, windows)
        zero_tail(o_ref, windows)
        for i in range(1, OWNERS):
            await_bytes(small.at[(mine - i + OWNERS) % OWNERS], small_sems.at[OWNERS + i])
        tab = unpack_small(small, vec_ref)
        hook(BEFORE, 0)
        load.wait()
        hook(BEFORE, 1)

        def first_norm(w, carry):
            xhat, _ = norm_parts(x_ref[window_rows(w), :].astype(full))
            n1_ref[window_rows(w), :] = (xhat * vec_ref[0:1, :] + vec_ref[1:2, :]).astype(low)
            return carry

        lax.fori_loop(0, windows, first_norm, 0)
        hook(BEFORE, 2)
        save = pltpu.make_async_copy(n1_ref, n1_hbm, local.at[1])
        save.start()
        hook(BEFORE, 3)
        load_dy.wait()

        def keep_live(w, carry):
            dy_ref[window_rows(w), :] = (dy_ref[window_rows(w), :].astype(full) * live(w)).astype(low)
            return carry

        lax.fori_loop(0, windows, keep_live, 0)
        transpose_rows(dy_ref, dyt_ref)
        hook(BEFORE, 4)

        def bias(tmp_ref):
            spread_table(tab, line_ref, tmp_ref)
            hook(BEFORE, 5)
            place_bias(tmp_ref, bias_ref)

        pl.run_scoped(bias, V((2, TOK * HEADS, 128), full))
        for g in range(GROUPS):
            cols = slice(g * GCOLS, (g + 1) * GCOLS)
            held = qkv_ref.at[g % 2]
            if g >= 2:
                pltpu.make_async_copy(held, qkv_hbm.at[g - 2], local.at[2 + g % 2]).wait()
            run(W_Q[g], ARRIVED)
            n1 = n1_ref[...]
            held[0] = ((dot(n1, flat(wq[g, 0])) + vec_ref[2:3, cols]) * (HEAD_DIM**-0.5)).astype(low)
            held[1] = dot(n1, flat(wq[g, 1])).astype(low)
            held[2] = (dot(n1, flat(wq[g, 2])) + vec_ref[3:4, cols]).astype(low)
            pltpu.make_async_copy(held, qkv_hbm.at[g], local.at[2 + g % 2]).start()

            def window(w, carry, g=g, cols=cols, held=held):
                hook_window(FORWARD, g, w)
                rows = window_rows(w)
                n = g * windows + w
                slot = n % 2
                s = against_heads(held[1, rows, :], split_diag(held[0, rows, :], mask_ref)) + bias_ref[g]
                e = jnp.exp(s - jnp.max(s, 0, keepdims=True))
                p = (e * (1.0 / jnp.sum(e, 0, keepdims=True))).astype(low)
                keep = pltpu.make_async_copy(pt_ref.at[slot], pt_hbm.at[n], local.at[4 + slot])

                @pl.when(n >= 2)
                def _():
                    keep.wait()

                pt_ref[slot] = p
                keep.start()
                o_ref[rows, cols] = undiag(held[2, rows, :].T, p, mask_ref).astype(low)
                return carry

            lax.fori_loop(0, windows, window, 0)

        run(W_P, ARRIVED)

        x1_ref[...] = x_ref[...].astype(full) + (dot(o_ref[0:rows_all], flat(wp[...])) + vec_ref[4:5, :])
        save.wait()
        for g in (GROUPS - 2, GROUPS - 1):
            pltpu.make_async_copy(qkv_ref.at[g % 2], qkv_hbm.at[g], local.at[2 + g % 2]).wait()
        for slot in range(2):
            pltpu.make_async_copy(pt_ref.at[slot], pt_hbm.at[0], local.at[4 + slot]).wait()

    def middle(dy_ref, dyt_ref, n2_ref, n2t_ref, y_ref, dn_ref, bu_ref, bsum_ref):
        zero_tail(n2_ref, windows)
        hook(MIDDLE, 0)

        def second_norm(w, carry):
            rows = window_rows(w)
            xhat, _ = norm_parts(x1_ref[rows, :])
            n2_ref[rows, :] = (xhat * vec_ref[5:6, :] + vec_ref[6:7, :]).astype(low)
            return carry

        lax.fori_loop(0, windows, second_norm, 0)
        transpose_rows(n2_ref, n2t_ref)
        hook(MIDDLE, 1)
        n2t_ref[C:, :] = jnp.ones((16, ROWS), low)
        y_ref[...] = jnp.zeros_like(y_ref)
        dn_ref[...] = jnp.zeros_like(dn_ref)
        for t in range(TILES):
            for s in range(TILE // 128):
                row, left = hidden_place(t, s)
                bu_ref[t, :, s * 128 : (s + 1) * 128] = vec_ref[row : row + 1, left : left + 128]
        hook(MIDDLE, 2)
        run(W_U0, ARRIVED)
        run(W_D0, ARRIVED)
        hook(TILE_STEP, 0)
        halves = TILE // SUB

        def step(i, carry):
            for k in range(1, TILES * halves):

                @pl.when(i == k)
                def _(k=k):
                    if k % halves == 0:
                        t = k // halves
                        for name in (W_U[t], W_D[t]):
                            run(name, ARRIVED)
                        for name in (W_U[t - 1], W_D[t - 1]):
                            jobs[name].close()
                        for name in (G_D[t - 1], G_U[t - 1]):
                            run(name, START)
                    hook(TILE_STEP, k)

            t, part = i // halves, i % halves
            cols = pl.ds(pl.multiple_of(part * SUB, SUB), SUB)
            wide = SUB // 128
            slot = (t + SLOTS - 1) % SLOTS
            u = flat(up[t, :, :, cols])
            d = flat(down[t, pl.ds(part * wide, wide)])
            h = dot(n2_ref[...], u) + bu_ref[t, :, cols]
            da = dot_nt(dy_ref[...], d)
            act, slope = gelu_both(h)
            a = act.astype(low)
            dh = (da * slope).astype(low)
            y_ref[...] += dot(a, d)
            dn_ref[...] += dot_nt(dh, u)
            gd = dot(dyt_ref[...], a).astype(low)
            down[slot, pl.ds(part * wide, wide)] = blocks(gd.T, wide)
            gu = dot(n2t_ref[...], dh)
            up[slot, :, :, cols] = blocks(gu[0:C].astype(low), OWNERS)
            bsum_ref[t, :, cols] = gu[C : C + 1]
            return carry

        lax.fori_loop(0, TILES * halves, step, 0)
        run(G_D[-1], START)
        run(G_U[-1], START)
        hook(AFTER_TILES, 0)
        sums_ref[...] = jnp.zeros_like(sums_ref)
        for t in range(TILES):
            for s in range(TILE // 128):
                row, left = hidden_place(t, s)
                sums_ref[row : row + 1, left : left + 128] = bsum_ref[t, :, s * 128 : (s + 1) * 128]
        transpose_rows(o_ref, dyt_ref)
        hook(AFTER_TILES, 1)

        def finish(w, carry):
            rows = window_rows(w)
            x1 = x1_ref[rows, :]
            xhat, scale = norm_parts(x1)
            dn = dn_ref[rows, :]
            dy = dy_ref[rows, :].astype(full)
            dx1 = dy + norm_back(xhat, scale, dn, vec_ref[5:6, :])
            dr = dx1.astype(low)
            sums_ref[4:5, :] += jnp.sum(dr.astype(full), 0, keepdims=True)
            sums_ref[5:6, :] += jnp.sum(dn * xhat, 0, keepdims=True)
            sums_ref[6:7, :] += jnp.sum(dn, 0, keepdims=True)
            sums_ref[7:8, :] += jnp.sum(dy, 0, keepdims=True)
            dy_ref[rows, :] = ((x1 + y_ref[rows, :] + vec_ref[7:8, :]) * live(w)).astype(low)
            x1_ref[rows, :] = dx1
            n2_ref[rows, :] = dr
            return carry

        lax.fori_loop(0, windows, finish, 0)
        o_ref[...] = dot_nt(n2_ref[...], flat(wp[...])).astype(low)
        save = pltpu.make_async_copy(dy_ref.at[0:rows_all], out_hbm, local.at[0])
        save.start()
        hook(AFTER_TILES, 2)
        jobs[W_P].close()
        for g in range(GROUPS):
            cols = slice(g * GCOLS, (g + 1) * GCOLS)
            wp[:, :, cols] = blocks(dot(dyt_ref[...], n2_ref[:, cols]).astype(low), OWNERS)
        run(G_P, START)
        hook(AFTER_TILES, 3)
        save.wait()

    def both(dy_ref, dyt_ref):
        pl.run_scoped(functools.partial(forward, dy_ref, dyt_ref), V((rows_all, C), low), V((ROWS, C), low),
                      V((2, 3, ROWS, GCOLS), low), V((2, TOK, PACK), low), V((GROUPS, TOK, PACK), full))
        pl.run_scoped(functools.partial(middle, dy_ref, dyt_ref), V((ROWS, C), low), V((C + 16, ROWS), low), V((ROWS, C), full), V((ROWS, C), full),
                      V((TILES, 1, TILE), full), V((TILES, 1, TILE), full))

    pl.run_scoped(both, V((ROWS, C), low), V((C, ROWS), low))

    def backward(x_ref, n1_ref, n1t_ref, qkv_ref, pt_ref, dproj_ref, dn_ref, bias_ref):
        loads = [pltpu.make_async_copy(x_hbm, x_ref, local.at[0]), pltpu.make_async_copy(n1_hbm, n1_ref, local.at[1])]
        fetch = [pltpu.make_async_copy(qkv_hbm.at[g], qkv_ref.at[g % 2], local.at[2 + g % 2]) for g in range(GROUPS)]
        fetch[0].start()
        pltpu.make_async_copy(pt_hbm.at[0], pt_ref.at[0], local.at[4]).start()
        fetch[1].start()
        for load in loads:
            load.start()
        bias_ref[...] = jnp.zeros_like(bias_ref)
        dn_ref[...] = jnp.zeros_like(dn_ref)
        for part in range(3):
            dproj_ref[part, rows_all:, :] = jnp.zeros((ROWS - rows_all, GCOLS), low)
        for g in range(GROUPS):
            cols = slice(g * GCOLS, (g + 1) * GCOLS)
            held = qkv_ref.at[g % 2]
            fetch[g].wait()

            def window(w, carry, g=g, cols=cols, held=held):
                hook_window(BACKWARD, g, w)
                rows = window_rows(w)
                n = g * windows + w
                slot = n % 2

                @pl.when(n + 1 < GROUPS * windows)
                def _():
                    pltpu.make_async_copy(pt_hbm.at[n + 1], pt_ref.at[1 - slot], local.at[5 - slot]).start()

                pltpu.make_async_copy(pt_hbm.at[n], pt_ref.at[slot], local.at[4 + slot]).wait()
                q = held[0, rows, :]
                k = held[1, rows, :]
                v = held[2, rows, :]
                p = pt_ref[slot]
                do = split_diag(o_ref[rows, cols], mask_ref)
                dp = against_heads(v, do)
                dv = over_queries(p, do).astype(low)
                pf = p.astype(full)
                ds = (pf * (dp - jnp.sum(pf * dp, 0, keepdims=True))).astype(low)
                bias_ref[g] += ds.astype(full)
                dproj_ref[1, rows, :] = over_queries(ds, split_diag(q, mask_ref)).astype(low)
                dq = (undiag(k.T, ds, mask_ref) * (HEAD_DIM**-0.5)).astype(low)
                dproj_ref[0, rows, :] = dq
                dproj_ref[2, rows, :] = dv
                sums_ref[2:3, cols] += jnp.sum(dq.astype(full), 0, keepdims=True)
                sums_ref[3:4, cols] += jnp.sum(dv.astype(full), 0, keepdims=True)
                return carry

            lax.fori_loop(0, windows, window, 0)
            if g + 2 < GROUPS:
                fetch[g + 2].start()
            if g == 0:
                for load in loads:
                    load.wait()
                transpose_rows(n1_ref, n1t_ref)
            jobs[W_Q[g]].close()
            if g == GROUPS - 1:
                jobs[W_U[-1]].close()
                for part in range(3):
                    up[TILES - 1, :, :, part * GCOLS : (part + 1) * GCOLS] = blocks(dot(n1t_ref[...], dproj_ref[part]).astype(low), OWNERS)
                    run(G_LAST[part], START)
                hook(LAST_STEPS, 0)
                for part in range(3):
                    dn_ref[...] += dot_nt(dproj_ref[part], flat(wq[g, part]))
            else:
                for part in range(3):
                    d = dproj_ref[part]
                    dn_ref[...] += dot_nt(d, flat(wq[g, part]))
                    wq[g, part] = blocks(dot(n1t_ref[...], d).astype(low), OWNERS)
                run(G_Q[g], START)

        def last_norm(grad_ref):
            def finish(w, carry):
                rows = window_rows(w)
                slot = w % 2
                xhat, scale = norm_parts(x_ref[rows, :].astype(full))
                dn = dn_ref[rows, :]
                save = pltpu.make_async_copy(grad_ref.at[slot], grad_hbm.at[rows], local.at[4 + slot])

                @pl.when(w >= 2)
                def _():
                    save.wait()

                grad_ref[slot] = x1_ref[rows, :] + norm_back(xhat, scale, dn, vec_ref[0:1, :])
                save.start()
                sums_ref[0:1, :] += jnp.sum(dn * xhat, 0, keepdims=True)
                sums_ref[1:2, :] += jnp.sum(dn, 0, keepdims=True)
                return carry

            lax.fori_loop(0, windows, finish, 0)
            hook(LAST_STEPS, 1)
            for slot in range(2):
                pltpu.make_async_copy(grad_ref.at[slot], grad_hbm.at[pl.ds(0, TOK)], local.at[4 + slot]).wait()

        pl.run_scoped(last_norm, V((2, TOK, C), full))
        hook(LAST_STEPS, 2)

        def table(tmp_ref):
            pack_small(sums_ref[...], table_grad(line_ref, tmp_ref, bias_ref), terms_ref)

        pl.run_scoped(table, V((2, TOK * HEADS, 128), full))
        run(G_S, START)
        hook(LAST_STEPS, 3)
        for stage in range(len(Reduce.STAGES)):
            for name in G_ALL:
                if stage < len(jobs[name].STAGES):
                    run(name, stage)

    pl.run_scoped(backward, V((rows_all, C), low), V((ROWS, C), low), V((C, ROWS), low), V((2, 3, ROWS, GCOLS), low), V((2, TOK, PACK), low), V((3, ROWS, GCOLS), low),
                  V((ROWS, C), full), V((GROUPS, TOK, PACK), full))
    jobs[W_D[-1]].close()
    for i in range(1, OWNERS):
        await_bytes(small.at[mine], small_sems.at[i])
    for name in G_ALL:
        jobs[name].close()


def shape(dims, kind):
    return jax.ShapeDtypeStruct(dims, kind)


def adamw(weight, moment, second, gradient, step_rate):
    moment_new = beta_one * moment + (1.0 - beta_one) * gradient
    second_new = beta_two * second + (1.0 - beta_two) * gradient * gradient
    update = moment_new * (1.0 / (1.0 - beta_one**STEP)) / (jnp.sqrt(second_new * (1.0 / (1.0 - beta_two**STEP))) + adam_eps)
    weight_new = weight * (1.0 - step_rate * weight_decay) - step_rate * update
    return (weight_new, moment_new, second_new)


def update_kernel(*refs):
    gq, gp, gu, gd, gs = refs[:5]
    ins = [refs[5 + 3 * i : 8 + 3 * i] for i in range(6)]
    outs = [refs[25 + 4 * i : 29 + 4 * i] for i in range(4)] + [refs[41:44], refs[44:47]]
    for i in range(2):
        refs[47 + i][...] = refs[23 + i][...]

    def piece(which, place, gradient):
        new = adamw(*(ref[place] for ref in ins[which]), gradient, step_rates[which])
        for ref, value in zip(outs[which], new):
            ref[place] = value
        if which < 4:
            outs[which][3][place] = new[0].astype(low)

    every = (slice(None), slice(None))
    piece(0, every, jnp.concatenate([gq[g, part] for part in range(3) for g in range(GROUPS)], 1).astype(full))
    piece(1, every, gp[...].astype(full))
    piece(2, every, jnp.concatenate([gu[t, :, s * 128 : (s + 1) * 128] for s in range(OWNERS) for t in range(TILES)], 1).astype(full))
    piece(3, every, gd[0].astype(full))

    @pl.when(pl.program_id(0) == 0)
    def _():
        piece(4, every, gs[0:12, 0:OWNED])
        piece(5, every, gs[16:40, 0 : ins[5][0].shape[1]])


def update(gq, gp, gu, gd, gs, states, results):
    steps = OWNED // 16

    def rows_of(array):
        tall = array.shape[0] // steps
        return pl.BlockSpec((tall, array.shape[1]), lambda i: (i, 0))

    def whole(array):
        return pl.BlockSpec(array.shape, lambda i: (0, 0))

    per_tile = 128 * TILES // steps
    specs = [
        pl.BlockSpec((GROUPS, 3, 16, GCOLS), lambda i: (0, 0, i, 0)),
        pl.BlockSpec((16, C), lambda i: (i, 0)),
        pl.BlockSpec((TILES, 16, TILE), lambda i: (0, i, 0)),
        pl.BlockSpec((1, per_tile, C), lambda i: (i // (128 // per_tile), i % (128 // per_tile), 0)),
        whole(gs),
    ]
    out_shapes, out_specs = [], []
    for i, group in enumerate(states):
        for array in group:
            specs.append(rows_of(array) if i < 4 else whole(array))
            out_shapes.append(shape(array.shape, full))
            out_specs.append(specs[-1])
        if i < 4:
            out_shapes.append(shape(group[0].shape, low))
            out_specs.append(rows_of(group[0]))
    results = [array.reshape(steps, -1, C) for array in results]
    for array in results:
        specs.append(pl.BlockSpec((1, *array.shape[1:]), lambda i: (i, 0, 0)))
        out_shapes.append(shape(array.shape, array.dtype))
        out_specs.append(specs[-1])
    return pl.pallas_call(
        update_kernel,
        grid=(steps,),
        in_specs=specs,
        out_specs=out_specs,
        out_shape=out_shapes,
        compiler_params=pltpu.CompilerParams(vmem_limit_bytes=63 * MIB),
        name="update",
    )(gq, gp, gu, gd, gs, *[array for group in states for array in group], *results)


def shards(
    tokens, out_grad, window_count,
    qkv_weight, qkv_first, qkv_second,
    output_weight, output_first, output_second,
    up_weight, up_first, up_second,
    down_weight, down_first, down_second,
    vectors, vector_first, vector_second,
    bias_table, table_first, table_second,
):
    windows = tokens.shape[0]
    rows = windows * TOK
    V = pltpu.VMEM
    D = pltpu.SemaphoreType.DMA
    hbm = pl.BlockSpec(memory_space=pl.ANY)
    vmem = pl.BlockSpec(memory_space=pltpu.VMEM)
    result = pl.pallas_call(
        functools.partial(layer_kernel, windows),
        out_shape=[
            shape((rows, C), low), shape((rows, C), full),
            shape((GROUPS, 3, OWNED, GCOLS), low), shape((OWNED, C), low), shape((TILES, OWNED, TILE), low), shape((TILES, 128, C), low),
            shape((40, 128), full),
            shape((GROUPS, 3, ROWS, GCOLS), low), shape((GROUPS * windows, TOK, PACK), low), shape((ROWS, C), low)],
        in_specs=[hbm, hbm, pl.BlockSpec(memory_space=pltpu.SMEM)] + [hbm] * 4 + [vmem] * 4,
        out_specs=[hbm, hbm] + [vmem] * 5 + [hbm] * 3,
        scratch_shapes=[
            V((GROUPS, 3, OWNERS, OWNED, GCOLS), low), V((OWNERS, OWNED, C), low), V((SLOTS, OWNERS, OWNED, TILE), low),
            V((SLOTS, OWNERS, 128, C), low), V((OWNERS, 48, 128), low), V((ROWS, C), low), V((rows, C), full), V((16, C), full), V((16, C), full),
            V((OWNERS, 40, 128), full)]
        + reduce_scratch()
        + [D((GATHERS, Gather.SEMS)), D((REDUCES, ReduceDirect.SEMS)), D((2 * OWNERS,)), D((ReduceSmall.SEMS,)), D((6,))],
        compiler_params=pltpu.CompilerParams(vmem_limit_bytes=63 * MIB, collective_id=0, has_side_effects=True),
        name="layer",
    )(tokens.reshape(rows, C), out_grad.reshape(rows, C), window_count, qkv_weight, output_weight, up_weight, down_weight, vectors, bias_table.T,
      jnp.asarray(line_matrix(), low), jnp.asarray(head_masks(), low))
    out, grad, gq, gp, gu, gd, gs = result[:7]
    new = update(gq, gp, gu, gd, gs, (
        (qkv_weight, qkv_first, qkv_second), (output_weight, output_first, output_second), (up_weight, up_first, up_second),
        (down_weight, down_first, down_second), (vectors, vector_first, vector_second), (bias_table.T, table_first.T, table_second.T)), (out, grad))
    *new, out, grad = new
    return (out.reshape(tokens.shape), grad.reshape(tokens.shape), *new[:-3], *(array.T for array in new[-3:]))


def vmem_call(body, outs, scratch, args, name, limit=60, **params):
    spec = pl.BlockSpec(memory_space=pltpu.VMEM)
    return pl.pallas_call(
        body,
        out_shape=outs,
        in_specs=[pl.BlockSpec(memory_space=pltpu.SMEM) if a.dtype == full and a.ndim == 1 else spec for a in args],
        out_specs=[spec] * len(outs),
        scratch_shapes=scratch,
        compiler_params=pltpu.CompilerParams(vmem_limit_bytes=limit * MIB, **params),
        name=name,
    )(*args)


def local_step(tokens, out_grad, window_count, small, wq, wp, up, down):
    windows = tokens.shape[0]
    rows = windows * TOK
    owned = C // OWNERS
    V = pltpu.VMEM
    x = tokens.reshape(rows, C)
    dy = out_grad.reshape(rows, C)
    live = (jnp.arange(windows) < window_count[0]).astype(full)
    line = jnp.asarray(line_matrix(), low)
    masks = jnp.asarray(head_masks(), low)
    qkv, pt, o, x1, n1t, vec = vmem_call(
        functools.partial(attention_forward, windows),
        [shape((9, ROWS, GCOLS), low), shape((GROUPS, windows, TOK, PACK), low), shape((ROWS, C), low), shape((rows, C), full), shape((C, ROWS), low),
         shape((16, C), full)],
        [V((ROWS, C), low), V((GROUPS, TOK, PACK), full), V((2, TOK * HEADS, 128), full)],
        (x, small, line, masks, wq, wp), "attention_forward")
    out, dx1, do, gup, gdown, gout, sums = vmem_call(
        functools.partial(feed_forward, windows),
        [shape((rows, C), low), shape((ROWS, C), full), shape((rows, C), low), shape((TILES, OWNERS, owned, TILE), low),
         shape((TILES, OWNERS, C, 128), low), shape((OWNERS, owned, C), low), shape((16, C), full)],
        [V((ROWS, C), low), V((C, ROWS), low), V((ROWS, C), low), V((C, ROWS), low), V((ROWS, C), full), V((ROWS, C), full),
         V((TILES, 1, TILE), full), V((TILES, 1, TILE), full)],
        (x1, dy, live, vec, up, down, wp, o), "feed_forward")
    gq, gsmall, grad = vmem_call(
        functools.partial(attention_backward, windows),
        [shape((GROUPS, 3, OWNERS, owned, GCOLS), low), shape((OWNERS, 40, 128), full), shape((rows, C), full)],
        [V((16, C), full), V((GROUPS, TOK, PACK), full), V((2, TOK * HEADS, 128), full), V((3, ROWS, GCOLS), low), V((ROWS, C), full)],
        (x, vec, line, masks, wq, qkv, pt, do, dx1, n1t, sums), "attention_backward")
    return out.reshape(tokens.shape), grad.reshape(tokens.shape), gq, gout, gup, gdown, gsmall


def shards_general(
    tokens, out_grad, window_count,
    qkv_weight, qkv_first, qkv_second,
    output_weight, output_first, output_second,
    up_weight, up_first, up_second,
    down_weight, down_first, down_second,
    vectors, vector_first, vector_second,
    bias_table, table_first, table_second,
):
    gather = functools.partial(lax.all_gather, axis_name="shard", tiled=True)
    scatter = functools.partial(lax.psum_scatter, axis_name="shard", tiled=True)
    owned = C // OWNERS
    wq = gather(qkv_weight.astype(low), axis=0).reshape(OWNERS, owned, 3, GROUPS, GCOLS).transpose(3, 2, 0, 1, 4)
    wp = gather(output_weight.astype(low), axis=0).reshape(OWNERS, owned, C)
    up = gather(up_weight.astype(low), axis=0).reshape(OWNERS, owned, OWNERS, TILES, 128).transpose(3, 0, 1, 2, 4)
    up = up.reshape(TILES, OWNERS, owned, TILE)
    down = gather(down_weight.astype(low), axis=0).reshape(OWNERS, TILES, 128, C).transpose(1, 0, 2, 3)
    vec = gather(vectors.astype(low), axis=1)
    tab = gather(bias_table.astype(low), axis=0)
    table_rows = tab.shape[0]
    count = TAB_ROWS // OWNERS
    vec = vec.reshape(12, OWNERS, owned).transpose(1, 0, 2)
    tab = tab[:TAB_ROWS].reshape(OWNERS, count, HEADS).transpose(0, 2, 1)
    small = jnp.concatenate([jnp.pad(vec, ((0, 0), (0, 4), (0, 128 - owned))), jnp.pad(tab, ((0, 0), (0, 8), (0, 128 - count)))], 1)
    out, grad, gq, gp, gu, gd, gs = local_step(tokens, out_grad, window_count, small, wq, wp, up, down)
    gq = gq.astype(full).transpose(2, 3, 1, 0, 4).reshape(C, 3 * C)
    gu = gu.astype(full).reshape(TILES, C, OWNERS, 128).transpose(1, 2, 0, 3).reshape(C, MLP)
    gd = gd.astype(full).transpose(1, 0, 3, 2).reshape(MLP, C)
    gv = gs[:, :12, :owned].transpose(1, 0, 2).reshape(12, C)
    gb = gs[:, 16:40, :count].transpose(0, 2, 1).reshape(TAB_ROWS, HEADS)
    gb = jnp.pad(gb, ((0, table_rows - TAB_ROWS), (0, 0)))
    totals = lax.psum(
        (scatter(gq, scatter_dimension=0), scatter(gp.astype(full).reshape(C, C), scatter_dimension=0), scatter(gu, scatter_dimension=0),
         scatter(gd, scatter_dimension=0), scatter(gv, scatter_dimension=1), scatter(gb, scatter_dimension=0)), "rep")
    states = (
        (qkv_weight, qkv_first, qkv_second), (output_weight, output_first, output_second), (up_weight, up_first, up_second),
        (down_weight, down_first, down_second), (vectors, vector_first, vector_second), (bias_table, table_first, table_second))
    results = [out, grad]
    for i, (state, total, rate) in enumerate(zip(states, totals, step_rates)):
        new = adamw(*state, total, rate)
        results += [*new, new[0].astype(low)] if i < 4 else [*new]
    return tuple(results)


def solution(mesh):
    wins = P(("rep", "shard"), None, None)
    rows = P("shard", None)
    cols = P(None, "shard")
    fits = mesh.shape["rep"] == REPS and mesh.shape["shard"] == OWNERS
    return jax.shard_map(
        shards if fits else shards_general,
        mesh=mesh,
        in_specs=(wins, wins, P(("rep", "shard"))) + (rows,) * 12 + (cols,) * 3 + (rows,) * 3,
        out_specs=(wins, wins) + (rows,) * 16 + (cols,) * 3 + (rows,) * 3,
        check_vma=False,
    )
```
